32 devices in a mesh: dp: 4 (over y, x), fsdp: 8 (over z, core).
Axes of the slice: x: 2, y: 2, z: 4, core: 2. Of those that a mesh axis runs over, the one named last changes fastest.
Arguments:
- pixels: bfloat16 [32768, 3072], P(('dp', 'fsdp')), may hold values from -6 to 6
- segment: int32 [32768], P(('dp', 'fsdp')), may hold values from 0 to 8, as said below
- patch_size: int32 [32, 8], P(('dp', 'fsdp')), may hold values from 8 to 48, as said below
- labels: int32 [32, 8], P(('dp', 'fsdp')), may hold values from 0 to 999
- patch_kernel: float32 [3072, 768], P('fsdp'), may hold values from -0.109375 to 0.109375
- head_weight: float32 [768, 1000], P('fsdp'), may hold values from -0.21875 to 0.21875
- input_proj: float32 [2, 768, 5376], P(None, 'fsdp'), may hold values from -0.21875 to 0.21875
- output_proj: float32 [2, 3840, 768], P(None, 'fsdp')
- layer_vector: float32 [2, 9984], P(None, 'fsdp')
- position_table: float32 [49, 768], replicated, may hold values from -0.625 to 0.625
- global_vector: float32 [3304], replicated
- patch_moment: float32 [3072, 768], P('fsdp')
- head_moment: float32 [768, 1000], P('fsdp')
- input_moment: float32 [2, 768, 5376], P(None, 'fsdp')
- output_moment: float32 [2, 3840, 768], P(None, 'fsdp')
- layer_moment: float32 [2, 9984], P(None, 'fsdp')
- position_moment: float32 [49, 768], replicated
- global_moment: float32 [3304], replicated
- patch_square: float32 [3072, 768], P('fsdp')
- head_square: float32 [768, 1000], P('fsdp')
- input_square: float32 [2, 768, 5376], P(None, 'fsdp')
- output_square: float32 [2, 3840, 768], P(None, 'fsdp')
- layer_square: float32 [2, 9984], P(None, 'fsdp')
- position_square: float32 [49, 768], replicated
- global_square: float32 [3304], replicated
Outputs:
- loss_sum: float32 [], replicated
- token_total: float32 [], replicated
- grad_norm: float32 [], replicated
- next_patch_moment: float32 [3072, 768], P('fsdp')
- next_head_moment: float32 [768, 1000], P('fsdp')
- next_input_moment: float32 [2, 768, 5376], P(None, 'fsdp')
- next_output_moment: float32 [2, 3840, 768], P(None, 'fsdp')
- next_layer_moment: float32 [2, 9984], P(None, 'fsdp')
- next_position_moment: float32 [49, 768], replicated
- next_global_moment: float32 [3304], replicated
- next_patch_square: float32 [3072, 768], P('fsdp')
- next_head_square: float32 [768, 1000], P('fsdp')
- next_input_square: float32 [2, 768, 5376], P(None, 'fsdp')
- next_output_square: float32 [2, 3840, 768], P(None, 'fsdp')
- next_layer_square: float32 [2, 9984], P(None, 'fsdp')
- next_position_square: float32 [49, 768], replicated
- next_global_square: float32 [3304], replicated
- next_patch_kernel: float32 [3072, 768], P('fsdp')
- next_head_weight: float32 [768, 1000], P('fsdp')
- next_input_proj: float32 [2, 768, 5376], P(None, 'fsdp')
- next_output_proj: float32 [2, 3840, 768], P(None, 'fsdp')
- next_layer_vector: float32 [2, 9984], P(None, 'fsdp')
- next_position_table: float32 [49, 768], replicated
- next_global_vector: float32 [3304], replicated
The draws below stay inside these ranges and needn't reach their ends.
Inputs may be any that keep to these rules, and one draw needn't show every extreme that they name: `patch_size`: each entry is one of 8, 10, 12, 15, 16, 20, 24, 30, 40, 48, all divisors of 240. `segment`: within each row of 1024 tokens (the tokens of one device), the slots that the row holds come in increasing order from the row's first token, each as one run of (240 / its patch size)^2 tokens; slot 0 is always held; the tokens after the last run have the value 8.
All inputs are finite; a program needn't handle non-finite values.
Results may differ from the reference program's by a relative error of at most 0.035.
Values may be sent and summed in bfloat16 or wider, within the bound.
A program may use at most 384 MiB of HBM per device.

```python
import math
import jax
import jax.numpy as jnp
from jax import lax

D = 768
HEADS = 12
HD = 64
FF = 3072
CLS = 1000
PIX = 3072
GRID = 7
IMG = 240
IMGS = 8
LAYERS = 2
ROW = 1024
STEP = 3
ROWS = 32
TOKENS = 32768
N_DP = 4
N_FSDP = 8


def packing(key):
    sizes_table = jnp.array([8, 10, 12, 15, 16, 20, 24, 30, 40, 48], jnp.int32)
    image_tokens = IMG // sizes_table * (IMG // sizes_table)
    row_total = N_DP * N_FSDP
    row_index = jnp.arange(row_total, dtype=jnp.int32)
    outer = row_index // N_FSDP
    inner = row_index % N_FSDP
    capacity = ROW * (N_FSDP - 1 + 2 * inner) * (N_DP - 1 + 2 * outer) // (9 * (N_FSDP - 1) * (N_DP - 1))
    capacity = jnp.maximum(capacity, 36)
    first_key, other_key = jax.random.split(key)
    too_large = jnp.sum((image_tokens[None, :] > capacity[:, None]).astype(jnp.int32), 1)
    leading = too_large + jax.random.randint(first_key, (row_total,), 0, 100000) % (10 - too_large)
    picks = jax.random.randint(other_key, (row_total, IMGS), 0, 10)
    picks = picks.at[:, 0].set(leading)
    wanted = image_tokens[picks]

    def place(used, column):
        taken = jnp.where(used + column <= capacity, column, 0)
        return (used + taken, taken)
    _, counts = lax.scan(place, jnp.zeros((row_total,), jnp.int32), wanted.T)
    counts = counts.T
    starts = jnp.cumsum(counts, 1) - counts
    position = jnp.arange(ROW, dtype=jnp.int32)[None, :, None]
    inside = (position >= starts[:, None, :]) & (position < (starts + counts)[:, None, :])
    slots = jnp.arange(IMGS, dtype=jnp.int32)[None, None, :]
    padding = 1 - jnp.any(inside, 2).astype(jnp.int32)
    segment = jnp.sum(jnp.where(inside, slots, 0), 2) + IMGS * padding
    return (sizes_table[picks], segment.reshape(row_total * ROW))


def draw_patch_size(key, part):
    picked, _ = packing(key)
    return picked


def draw_segment(key, part):
    _, segment = packing(key)
    return segment


def ramp_gain(key, count, low_end):
    line = low_end + jnp.arange(count, dtype=jnp.float32) / (count - 1)
    return line * jax.random.uniform(key, (count,), jnp.float32, 0.8, 1.25)


def small_normal(key, count):
    return 0.1 * jax.random.normal(key, (count,), jnp.float32)


def draw_layer_vector(key, part):
    key = jax.random.fold_in(key, 3)
    low_end = 0.5
    layers_out = []
    for depth_index in range(LAYERS):
        keys = jax.random.split(jax.random.fold_in(key, depth_index), 4)
        layers_out.append(jnp.concatenate([ramp_gain(keys[0], D, low_end), small_normal(keys[1], D), ramp_gain(keys[2], D, low_end), small_normal(keys[3], 6 * D + FF)]))
    return jnp.stack(layers_out)


def draw_global_vector(key, part):
    key = jax.random.fold_in(key, 5)
    low_end = 0.5
    keys = jax.random.split(key, 3)
    return jnp.concatenate([small_normal(keys[0], D), ramp_gain(keys[1], D, low_end), small_normal(keys[2], D + CLS)])


def draw_output_proj(key, part):
    key = jax.random.fold_in(key, 7)
    raw = jax.random.truncated_normal(key, -4.0, 4.0, (LAYERS, D + FF, D), jnp.float32)
    rows = jnp.arange(D + FF, dtype=jnp.int32)
    scale = jnp.where(rows < D, 4.0 / math.sqrt(D), 1.0 / math.sqrt(FF))
    return raw * scale[None, :, None]


def state_scale():
    count = PIX * D + D * CLS + LAYERS * (D * (4 * D + 2 * FF) + 9 * D + FF) + GRID * GRID * D + 3 * D + CLS
    return 0.01 / math.sqrt(count)


def moment_like(key, shape, factor):
    return jax.random.normal(key, shape, jnp.float32) * (state_scale() * factor)


def square_like(key, shape, factor):
    scale = state_scale()
    return jnp.exp(jax.random.uniform(key, shape, jnp.float32, math.log(0.5), math.log(8.0))) * (scale * scale * factor)


def draw_patch_moment(key, part):
    return moment_like(jax.random.fold_in(key, 11), (PIX, D), 1.0)


def draw_head_moment(key, part):
    return moment_like(jax.random.fold_in(key, 12), (D, CLS), 1.0)


def draw_input_moment(key, part):
    return moment_like(jax.random.fold_in(key, 13), (LAYERS, D, 3 * D + FF), 1.0)


def draw_output_moment(key, part):
    return moment_like(jax.random.fold_in(key, 14), (LAYERS, D + FF, D), 1.0)


def draw_layer_moment(key, part):
    return moment_like(jax.random.fold_in(key, 15), (LAYERS, 9 * D + FF), 1.0)


def draw_position_moment(key, part):
    return moment_like(jax.random.fold_in(key, 16), (GRID * GRID, D), 0.3)


def draw_global_moment(key, part):
    return moment_like(jax.random.fold_in(key, 17), (3 * D + CLS,), 1.0)


def draw_patch_square(key, part):
    return square_like(jax.random.fold_in(key, 21), (PIX, D), 1.0)


def draw_head_square(key, part):
    return square_like(jax.random.fold_in(key, 22), (D, CLS), 1.0)


def draw_input_square(key, part):
    return square_like(jax.random.fold_in(key, 23), (LAYERS, D, 3 * D + FF), 1.0)


def draw_output_square(key, part):
    return square_like(jax.random.fold_in(key, 24), (LAYERS, D + FF, D), 1.0)


def draw_layer_square(key, part):
    return square_like(jax.random.fold_in(key, 25), (LAYERS, 9 * D + FF), 1.0)


def draw_position_square(key, part):
    return square_like(jax.random.fold_in(key, 26), (GRID * GRID, D), 0.1)


def draw_global_square(key, part):
    return square_like(jax.random.fold_in(key, 27), (3 * D + CLS,), 1.0)


def touch_ends(drawn, key, least, high):
    extent = drawn.shape
    index_at = [jax.random.randint(jax.random.fold_in(key, axis), (), 0, extent[axis]) for axis in range(len(extent))]
    drawn = drawn.at[tuple(index_at)].set(least)
    longest = extent.index(max(extent))
    index_at[longest] = (index_at[longest] + 1) % extent[longest]
    return drawn.at[tuple(index_at)].set(high)


def block_levels(stream_key, extent, cuts, least, high):
    factor_of, own = 1.0, jax.random.fold_in(stream_key, 6)
    for axis_at, blocks in cuts:
        steps = jnp.exp(jax.random.uniform(jax.random.fold_in(own, axis_at), (blocks,), jnp.float32, least / len(cuts), high / len(cuts)))
        factor_of = factor_of * jnp.repeat(steps, extent[axis_at] // blocks).reshape([-1 if axis == axis_at else 1 for axis in range(len(extent))])
    return factor_of


def noise(key, shape, width, limit, cuts=(), kind=jnp.bfloat16):
    result = width * jax.random.normal(key, shape, jnp.float32)
    if cuts:
        result = result * block_levels(key, shape, cuts, -0.22, 0.18)
    return jnp.clip(result, -limit, limit).astype(kind)


def setup_inputs(seed: int = 0) -> dict:
    key_of = jax.random.split(jax.random.key(seed), 26)
    return {
        "pixels": noise(key_of[0], (TOKENS, PIX), 1.0, 6.0, ((0, 32),)),
        "segment": draw_segment(jax.random.fold_in(key_of[25], 71), 0),
        "patch_size": draw_patch_size(jax.random.fold_in(key_of[25], 71), 0),
        "labels": touch_ends(jax.random.randint(key_of[3], (ROWS, IMGS), 0, CLS), jax.random.fold_in(key_of[3], 1), 0, CLS - 1).astype(jnp.int32),
        "patch_kernel": noise(key_of[4], (PIX, D), PIX ** -0.5, 0.109375, ((0, 8),), jnp.float32),
        "head_weight": noise(key_of[5], (D, CLS), D ** -0.5, 0.21875, ((0, 8),), jnp.float32),
        "input_proj": noise(key_of[6], (LAYERS, D, 3 * D + FF), D ** -0.5, 0.21875, ((1, 8),), jnp.float32),
        "output_proj": draw_output_proj(jax.random.fold_in(key_of[25], 71), 0),
        "layer_vector": draw_layer_vector(jax.random.fold_in(key_of[25], 71), 0),
        "position_table": noise(key_of[9], (GRID * GRID, D), 0.1, 0.625, (), jnp.float32),
        "global_vector": draw_global_vector(jax.random.fold_in(key_of[25], 71), 0),
        "patch_moment": draw_patch_moment(jax.random.fold_in(key_of[25], 71), 0),
        "head_moment": draw_head_moment(jax.random.fold_in(key_of[25], 71), 0),
        "input_moment": draw_input_moment(jax.random.fold_in(key_of[25], 71), 0),
        "output_moment": draw_output_moment(jax.random.fold_in(key_of[25], 71), 0),
        "layer_moment": draw_layer_moment(jax.random.fold_in(key_of[25], 71), 0),
        "position_moment": draw_position_moment(jax.random.fold_in(key_of[25], 71), 0),
        "global_moment": draw_global_moment(jax.random.fold_in(key_of[25], 71), 0),
        "patch_square": draw_patch_square(jax.random.fold_in(key_of[25], 71), 0),
        "head_square": draw_head_square(jax.random.fold_in(key_of[25], 71), 0),
        "input_square": draw_input_square(jax.random.fold_in(key_of[25], 71), 0),
        "output_square": draw_output_square(jax.random.fold_in(key_of[25], 71), 0),
        "layer_square": draw_layer_square(jax.random.fold_in(key_of[25], 71), 0),
        "position_square": draw_position_square(jax.random.fold_in(key_of[25], 71), 0),
        "global_square": draw_global_square(jax.random.fold_in(key_of[25], 71), 0),
    }


@jax.custom_vjp
def low(v):
    return lax.optimization_barrier(v.astype(jnp.bfloat16)).astype(jnp.float32)

@jax.custom_vjp
def low_back(v):
    return v

def low_keep(v):
    return (low(v), None)

def low_pass(kept, grad):
    return (grad,)

def back_keep(v):
    return (v, None)

def back_low(kept, grad):
    return (low(grad),)
low.defvjp(low_keep, low_pass)
low_back.defvjp(back_keep, back_low)
NORM_EPS = 1e-06
CLIP_NORM = 0.01
LEARN_RATE = 0.05
VECTOR_RATE = 0.25
BETA_ONE = 0.5
BETA_TWO = 0.5
ADAM_EPS = 1e-08
WEIGHT_DECAY = 0.05

def precise(left, right):
    return jnp.dot(left, right, precision=lax.Precision.HIGHEST)

def layer_norm(values, gain, shift):
    center = values - lax.optimization_barrier(jnp.mean(values, -1, keepdims=True))
    spread = lax.optimization_barrier(jnp.mean(center * center, -1, keepdims=True))
    return center * lax.rsqrt(spread + NORM_EPS) * gain + shift

def row_layout(seg_row, patch_row):
    slots = jnp.arange(IMGS, dtype=jnp.int32)
    member = seg_row[:, None] == slots[None, :]
    counts = lax.optimization_barrier(jnp.sum(member.astype(jnp.int32), 0, dtype=jnp.int32))
    starts = jnp.cumsum(counts, dtype=jnp.int32) - counts
    inside = jnp.any(member, 1)
    offset = jnp.arange(ROW, dtype=jnp.int32) - lax.optimization_barrier(jnp.sum(jnp.where(member, starts[None, :], 0), 1, dtype=jnp.int32))
    offset = jnp.where(inside, offset, 0)
    patch_tok = lax.optimization_barrier(jnp.sum(jnp.where(member, patch_row[None, :], 0), 1, dtype=jnp.int32)) + jnp.where(inside, 0, IMG)
    side = IMG // patch_tok
    nodes = jnp.arange(GRID, dtype=jnp.int32).astype(jnp.float32)

    def hat(coord):
        place = ((2 * coord + 1) * GRID).astype(jnp.float32) / (2 * side).astype(jnp.float32) - 0.5
        place = jnp.clip(place, 0.0, GRID - 1.0)
        return jnp.maximum(1.0 - jnp.abs(place[:, None] - nodes[None, :]), 0.0)
    weights = (hat(offset // side)[:, :, None] * hat(offset % side)[:, None, :]).reshape(ROW, GRID * GRID)
    return (weights, member.astype(jnp.float32), counts.astype(jnp.float32))

def block(stream, proj_in, proj_out, vector, same_image):
    normed = low(layer_norm(stream, vector[0:D], vector[D:2 * D]))
    qkv_rows = low_back(low(precise(normed, proj_in[:, :3 * D]) + vector[4 * D:7 * D]))
    queries = qkv_rows[:, :D].reshape(ROW, HEADS, HD)
    key_rows = qkv_rows[:, D:2 * D].reshape(ROW, HEADS, HD)
    values = qkv_rows[:, 2 * D:].reshape(ROW, HEADS, HD)
    scores = low_back(jnp.einsum('qhd,khd->hqk', queries, key_rows, precision=lax.Precision.HIGHEST) * HD ** (-0.5))
    scores = jnp.where(same_image[None], scores, -1e+30)
    highest = lax.optimization_barrier(jnp.max(scores, -1, keepdims=True))
    exponent = jnp.exp(scores - highest)
    probabilities = exponent / lax.optimization_barrier(jnp.sum(exponent, -1, keepdims=True))
    attended = jnp.einsum('hqk,khd->qhd', low(probabilities), values, precision=lax.Precision.HIGHEST).reshape(ROW, D)
    attended = low_back(low(attended))
    residual = stream + low_back(precise(attended, proj_out[:D]) + vector[7 * D:8 * D])
    normed_second = low(layer_norm(residual, vector[2 * D:3 * D], vector[3 * D:4 * D]))
    hidden = low_back(precise(normed_second, proj_in[:, 3 * D:]) + vector[9 * D:])
    active = low(jax.nn.gelu(hidden))
    return residual + low_back(precise(active, proj_out[D:]) + vector[8 * D:9 * D])

def row_loss(params, pixel_row, seg_row, patch_row, label_row):
    patch_kernel, head_weight, input_proj, output_proj, layer_vector, position_table, global_vector = [low(item) for item in params]
    pos_weights, member, counts = row_layout(seg_row, patch_row)
    stream = low_back(precise(pixel_row, patch_kernel) + global_vector[:D]) + precise(pos_weights, position_table)
    same_image = seg_row[:, None] == seg_row[None, :]
    for depth_index in range(LAYERS):
        stream = block(stream, input_proj[depth_index], output_proj[depth_index], layer_vector[depth_index], same_image)
    final_norm = layer_norm(stream, global_vector[D:2 * D], global_vector[2 * D:3 * D])
    pooled = low(precise(member.T, final_norm) / jnp.maximum(counts, 1.0)[:, None])
    logits = low_back(precise(pooled, head_weight) + global_vector[3 * D:])
    highest = lax.optimization_barrier(jnp.max(logits, -1))
    logsum = highest + jnp.log(lax.optimization_barrier(jnp.sum(jnp.exp(logits - highest[:, None]), -1)))
    onehot = label_row[:, None] == jnp.arange(CLS, dtype=jnp.int32)[None, :]
    picked = lax.optimization_barrier(jnp.sum(jnp.where(onehot, logits, 0.0), 1))
    return jnp.sum(counts * (logsum - picked))

def reference(pixels, segment, patch_size, labels, patch_kernel, head_weight, input_proj, output_proj, layer_vector, position_table, global_vector, patch_moment, head_moment, input_moment, output_moment, layer_moment, position_moment, global_moment, patch_square, head_square, input_square, output_square, layer_square, position_square, global_square):
    row_total = N_DP * N_FSDP
    params = (patch_kernel, head_weight, input_proj, output_proj, layer_vector, position_table, global_vector)
    token_total = jnp.sum((segment < IMGS).astype(jnp.float32))
    pixel_rows = pixels.astype(jnp.float32).reshape(row_total, ROW, PIX)
    segment_rows = segment.reshape(row_total, ROW)

    def loss_fn(weights):

        def accumulate(running, item):
            return (running + jax.checkpoint(row_loss)(weights, *item), None)
        loss_sum, _ = lax.scan(accumulate, jnp.zeros((), jnp.float32), (pixel_rows, segment_rows, patch_size, labels))
        return (loss_sum / token_total, loss_sum)
    _, pullback, loss_sum = jax.vjp(loss_fn, params, has_aux=True)
    gradients = pullback(jnp.ones((), jnp.float32))[0]
    grad_norm = jnp.sqrt(sum((jnp.sum(item * item) for item in gradients)))
    factor = jnp.minimum(1.0, CLIP_NORM / grad_norm)
    moments = (patch_moment, head_moment, input_moment, output_moment, layer_moment, position_moment, global_moment)
    squares = (patch_square, head_square, input_square, output_square, layer_square, position_square, global_square)
    rates = (LEARN_RATE, LEARN_RATE, LEARN_RATE, LEARN_RATE, VECTOR_RATE, LEARN_RATE, VECTOR_RATE)
    fixed_one = 1.0 - BETA_ONE ** STEP
    fixed_two = 1.0 - BETA_TWO ** STEP
    new_moments = []
    new_squares = []
    new_weights = []
    for gradient, moment, square, weight, learn_rate in zip(gradients, moments, squares, params, rates):
        clipped = gradient * factor
        moment = BETA_ONE * moment + (1.0 - BETA_ONE) * clipped
        square = BETA_TWO * square + (1.0 - BETA_TWO) * clipped * clipped
        step_dir = moment / fixed_one / (jnp.sqrt(square / fixed_two) + ADAM_EPS) + WEIGHT_DECAY * weight
        new_moments.append(moment)
        new_squares.append(square)
        new_weights.append(weight - learn_rate * step_dir)
    return (loss_sum, token_total, grad_norm, new_moments[0], new_moments[1], new_moments[2], new_moments[3], new_moments[4], new_moments[5], new_moments[6], new_squares[0], new_squares[1], new_squares[2], new_squares[3], new_squares[4], new_squares[5], new_squares[6], new_weights[0], new_weights[1], new_weights[2], new_weights[3], new_weights[4], new_weights[5], new_weights[6])
```

```python
import functools

import jax
import jax.numpy as jnp
from jax import lax
from jax.experimental import pallas as pl
from jax.experimental.pallas import tpu as pltpu
from jax.sharding import PartitionSpec as P

D = 768
HEADS = 12
HD = 64
CLS = 1000
GRID = 7
IMG = 240
IMGS = 8
LAYERS = 2
STEP = 3


NORM_EPS = 1e-06
CLIP_NORM = 0.01
LEARN_RATE = 0.05
VECTOR_RATE = 0.25
BETA_ONE = 0.5
BETA_TWO = 0.5
ADAM_EPS = 1e-08
WEIGHT_DECAY = 0.05
HIGHEST = lax.Precision.HIGHEST

PAIR = 2 * HD
MASKED = -1e30
VMEM_LIMIT = 56 * 1024 * 1024
AXES = ("fsdp", "dp")
LANES = 128


def layer_norm(values, gain, shift):
    center = values - jnp.mean(values, -1, keepdims=True)
    spread = jnp.mean(center * center, -1, keepdims=True)
    return center * lax.rsqrt(spread + NORM_EPS) * gain + shift


def rounded(values):
    return lax.optimization_barrier(values.astype(jnp.bfloat16)).astype(jnp.float32)


def column_total(rows):
    return jnp.sum(rows.astype(jnp.float32), 0)


def matmul(left, right):
    return jnp.dot(left, right, preferred_element_type=jnp.float32)


def gather_rows(shard):
    share = shard.shape[0] // lax.axis_size("dp")
    mine = lax.dynamic_slice_in_dim(shard, lax.axis_index("dp") * share, share, 0)
    return lax.all_gather(mine.astype(jnp.bfloat16), AXES, axis=0, tiled=True)


def scatter_rows(partial_sum):
    return lax.psum_scatter(
        partial_sum.astype(jnp.bfloat16), AXES, scatter_dimension=0, tiled=True
    )


def regather(shares):
    return lax.all_gather(shares, "dp", axis=0, tiled=True).astype(jnp.float32)


def padded_rows(flat, multiple):
    extra = -flat.shape[0] % (multiple * LANES)
    return jnp.pad(flat, (0, extra)).reshape(-1, LANES)


def gather_vectors(shard):
    size = shard.size
    full = lax.all_gather(
        padded_rows(shard.astype(jnp.bfloat16).reshape(-1), 16), "fsdp", axis=0, tiled=True
    )
    owners = lax.axis_size("fsdp")
    full = full.reshape(owners, -1)[:, :size].reshape(owners, *shard.shape)
    return jnp.swapaxes(full, 0, 1).reshape(shard.shape[0], -1)


def total_flat(flat):
    rows = padded_rows(flat, 16 * lax.axis_size("dp") * lax.axis_size("fsdp"))
    share = lax.psum_scatter(rows, AXES, scatter_dimension=0, tiled=True)
    return lax.all_gather(share, AXES, axis=0, tiled=True).reshape(-1)[: flat.shape[0]]


def row_layout(seg_row, patch_row):
    row_count = seg_row.shape[0]
    slots = jnp.arange(IMGS, dtype=jnp.int32)
    member = seg_row[:, None] == slots[None, :]
    counts = jnp.sum(member.astype(jnp.int32), 0, dtype=jnp.int32)
    starts = jnp.cumsum(counts, dtype=jnp.int32) - counts
    inside = jnp.any(member, 1)
    offset = jnp.arange(row_count, dtype=jnp.int32) - jnp.sum(
        jnp.where(member, starts[None, :], 0), 1, dtype=jnp.int32
    )
    offset = jnp.where(inside, offset, 0)
    patch_tok = jnp.sum(jnp.where(member, patch_row[None, :], 0), 1, dtype=jnp.int32) + jnp.where(
        inside, 0, IMG
    )
    side = IMG // patch_tok
    nodes = jnp.arange(GRID, dtype=jnp.int32).astype(jnp.float32)

    def hat(coord):
        place = ((2 * coord + 1) * GRID).astype(jnp.float32) / (2 * side).astype(jnp.float32) - 0.5
        place = jnp.clip(place, 0.0, GRID - 1.0)
        return jnp.maximum(1.0 - jnp.abs(place[:, None] - nodes[None, :]), 0.0)

    weights = (hat(offset // side)[:, :, None] * hat(offset % side)[:, None, :]).reshape(
        row_count, GRID * GRID
    )
    return (weights, member.astype(jnp.float32), counts.astype(jnp.float32))


def attention_forward_kernel(q_ref, k_ref, v_ref, seg_col_ref, seg_row_ref, out_ref, expo_ref, inv_ref, *, block):
    rows = q_ref.shape[0]
    lower = lax.broadcasted_iota(jnp.int32, (block, PAIR), 1) < HD
    keys = k_ref[...]
    values = v_ref[...]
    seg_row = seg_row_ref[...]

    def one_block(step, carry):
        at = pl.ds(pl.multiple_of(step * block, block), block)
        query = q_ref[at, :] * jnp.bfloat16(HD**-0.5)
        same = seg_col_ref[at, :] == seg_row
        outs, invs = [], []
        for head in range(2):
            keep = lower if head == 0 else jnp.logical_not(lower)
            mine = jnp.where(keep, query, jnp.bfloat16(0))
            scores = lax.dot_general(
                mine, keys, (((1,), (1,)), ((), ())), preferred_element_type=jnp.float32
            )
            scores = jnp.where(same, scores, MASKED)
            highest = jnp.max(scores, -1, keepdims=True)
            exponent = jnp.exp(scores - highest)
            total = jnp.sum(exponent, -1, keepdims=True)
            low = exponent.astype(jnp.bfloat16)
            expo_ref[head, at, :] = low
            outs.append(jnp.dot(low, values, preferred_element_type=jnp.float32))
            invs.append(1.0 / total)
        inverse = jnp.where(lower, invs[0], invs[1])
        out_ref[at, :] = (jnp.where(lower, outs[0], outs[1]) * inverse).astype(jnp.bfloat16)
        inv_ref[at, :] = inverse
        return carry

    lax.fori_loop(0, rows // block, one_block, 0, unroll=True)


def attention_forward(qkv_rows, segment):
    rows = qkv_rows.shape[0]
    pairs = HEADS // 2
    block = min(256, rows)
    wide = lambda base: pl.BlockSpec((rows, PAIR), lambda j, base=base: (0, base + j))
    return pl.pallas_call(
        functools.partial(attention_forward_kernel, block=block),
        grid=(pairs,),
        in_specs=[
            wide(0),
            wide(pairs),
            wide(2 * pairs),
            pl.BlockSpec((rows, 1), lambda j: (0, 0)),
            pl.BlockSpec((1, rows), lambda j: (0, 0)),
        ],
        out_specs=[
            wide(0),
            pl.BlockSpec((2, rows, rows), lambda j: (j, 0, 0)),
            wide(0),
        ],
        out_shape=[
            jax.ShapeDtypeStruct((rows, D), jnp.bfloat16),
            jax.ShapeDtypeStruct((HEADS, rows, rows), jnp.bfloat16),
            jax.ShapeDtypeStruct((rows, D), jnp.float32),
        ],
        compiler_params=pltpu.CompilerParams(vmem_limit_bytes=VMEM_LIMIT),
        cost_estimate=pl.CostEstimate(
            flops=4 * HEADS * rows * rows * HD * 4,
            bytes_accessed=2 * HEADS * rows * rows + 12 * rows * D,
            transcendentals=HEADS * rows * rows,
        ),
        name="attention_forward",
    )(qkv_rows, qkv_rows, qkv_rows, segment[:, None], segment[None, :])


def attention_backward_kernel(q_ref, k_ref, v_ref, expo_ref, inv_ref, out_ref, grad_ref, dqkv_ref, *, block):
    rows = q_ref.shape[0]
    pair = pl.program_id(0)
    lower = lax.broadcasted_iota(jnp.int32, (block, PAIR), 1) < HD
    keys = k_ref[...]
    values = v_ref[...]
    scale = HD**-0.5
    scaled_grad = (grad_ref[...].astype(jnp.float32) * inv_ref[...]).astype(jnp.bfloat16)
    query = q_ref[...]
    query_t = query.T
    grad_t = scaled_grad.T
    product = scaled_grad.astype(jnp.float32) * out_ref[...].astype(jnp.float32)
    key_t = [None, None]
    value_t = [None, None]
    for step in range(rows // block):
        at = slice(step * block, (step + 1) * block)
        query_parts = []
        for head in range(2):
            lanes = slice(head * HD, (head + 1) * HD)
            keep = lower if head == 0 else jnp.logical_not(lower)
            mine = jnp.where(keep, scaled_grad[at], jnp.bfloat16(0))
            inner = jnp.sum(jnp.where(keep, product[at], 0.0), -1, keepdims=True)
            low = expo_ref[head, at, :]
            probs_grad = lax.dot_general(
                mine, values, (((1,), (1,)), ((), ())), preferred_element_type=jnp.float32
            )
            scores_grad = (low.astype(jnp.float32) * (probs_grad - inner)).astype(jnp.bfloat16)
            query_parts.append(jnp.dot(scores_grad, keys, preferred_element_type=jnp.float32))
            key_part = jnp.dot(query_t[lanes, at], scores_grad, preferred_element_type=jnp.float32)
            value_part = jnp.dot(grad_t[lanes, at], low, preferred_element_type=jnp.float32)
            key_t[head] = key_part if step == 0 else key_t[head] + key_part
            value_t[head] = value_part if step == 0 else value_t[head] + value_part
        query_grad = jnp.where(lower, query_parts[0], query_parts[1]) * scale
        dqkv_ref[at, pl.ds(pl.multiple_of(pair * PAIR, PAIR), PAIR)] = query_grad.astype(jnp.bfloat16)
    key_grad = (jnp.concatenate(key_t, 0) * scale).T
    value_grad = jnp.concatenate(value_t, 0).T
    dqkv_ref[:, pl.ds(pl.multiple_of(D + pair * PAIR, PAIR), PAIR)] = key_grad.astype(jnp.bfloat16)
    dqkv_ref[:, pl.ds(pl.multiple_of(2 * D + pair * PAIR, PAIR), PAIR)] = value_grad.astype(jnp.bfloat16)


def attention_backward(qkv_rows, expo, inverse, attended, attended_grad):
    rows = qkv_rows.shape[0]
    pairs = HEADS // 2
    block = min(256, rows)
    wide = lambda base: pl.BlockSpec((rows, PAIR), lambda j, base=base: (0, base + j))
    return pl.pallas_call(
        functools.partial(attention_backward_kernel, block=block),
        grid=(pairs,),
        in_specs=[
            wide(0),
            wide(pairs),
            wide(2 * pairs),
            pl.BlockSpec((2, rows, rows), lambda j: (j, 0, 0)),
            wide(0),
            wide(0),
            wide(0),
        ],
        out_specs=pl.BlockSpec((rows, 3 * D), lambda j: (0, 0)),
        out_shape=jax.ShapeDtypeStruct((rows, 3 * D), jnp.bfloat16),
        compiler_params=pltpu.CompilerParams(vmem_limit_bytes=VMEM_LIMIT),
        cost_estimate=pl.CostEstimate(
            flops=8 * HEADS * rows * rows * HD * 4,
            bytes_accessed=2 * HEADS * rows * rows + 20 * rows * D,
            transcendentals=0,
        ),
        name="attention_backward",
    )(qkv_rows, qkv_rows, qkv_rows, expo, inverse, attended, attended_grad)


def layer_forward(stream, weights, seg_row):
    proj_in, proj_out, vector_low = weights
    vector = vector_low.astype(jnp.float32)
    normed = layer_norm(stream, vector[0:D], vector[D : 2 * D]).astype(jnp.bfloat16)
    qkv_rows = (matmul(normed, proj_in[:, : 3 * D]) + vector[4 * D : 7 * D]).astype(jnp.bfloat16)
    attended, expo, inverse = attention_forward(qkv_rows, seg_row)
    residual = stream + matmul(attended, proj_out[:D]) + vector[7 * D : 8 * D]
    normed_second = layer_norm(residual, vector[2 * D : 3 * D], vector[3 * D : 4 * D]).astype(
        jnp.bfloat16
    )
    hidden = matmul(normed_second, proj_in[:, 3 * D :]) + vector[9 * D :]
    active = jax.nn.gelu(hidden).astype(jnp.bfloat16)
    output = residual + matmul(active, proj_out[D:]) + vector[8 * D : 9 * D]
    return (output, (stream, qkv_rows, attended, expo, inverse, residual, hidden))


def layer_backward(grad_stream, weights, layer_saved):
    proj_in, proj_out, vector_low = weights
    vector = vector_low.astype(jnp.float32)
    stream, qkv_rows, attended, expo, inverse, residual, hidden = layer_saved
    grad_low = grad_stream.astype(jnp.bfloat16)
    normed_second, second_back = jax.vjp(
        layer_norm, residual, vector[2 * D : 3 * D], vector[3 * D : 4 * D]
    )
    normed_second = normed_second.astype(jnp.bfloat16)
    active, gelu_back = jax.vjp(jax.nn.gelu, hidden)
    active = active.astype(jnp.bfloat16)
    down_grad = matmul(active.T, grad_low)
    active_grad = matmul(grad_low, proj_out[D:].T)
    hidden_grad = gelu_back(active_grad)[0].astype(jnp.bfloat16)
    up_grad = matmul(normed_second.T, hidden_grad)
    second_grad = matmul(hidden_grad, proj_in[:, 3 * D :].T)
    residual_grad, gain_second, shift_second = second_back(second_grad)
    residual_grad = residual_grad + grad_stream
    residual_low = residual_grad.astype(jnp.bfloat16)
    mixing_grad = matmul(attended.T, residual_low)
    attended_grad = matmul(residual_low, proj_out[:D].T).astype(jnp.bfloat16)
    qkv_grad = attention_backward(qkv_rows, expo, inverse, attended, attended_grad)
    normed, first_back = jax.vjp(layer_norm, stream, vector[0:D], vector[D : 2 * D])
    project_grad = matmul(normed.astype(jnp.bfloat16).T, qkv_grad)
    normed_grad = matmul(qkv_grad, proj_in[:, : 3 * D].T)
    stream_grad, gain_first, shift_first = first_back(normed_grad)
    vector_grad = jnp.concatenate(
        [
            gain_first,
            shift_first,
            gain_second,
            shift_second,
            column_total(qkv_grad),
            column_total(residual_low),
            column_total(grad_low),
            column_total(hidden_grad),
        ]
    )
    return (
        residual_grad + stream_grad,
        (
            jnp.concatenate([project_grad, up_grad], 1),
            jnp.concatenate([mixing_grad, down_grad], 0),
            vector_grad,
        ),
    )


def adam_update(gradient, moment, square, weight, factor, learn_rate):
    clipped = gradient * factor
    moment = BETA_ONE * moment + (1.0 - BETA_ONE) * clipped
    square = BETA_TWO * square + (1.0 - BETA_TWO) * clipped * clipped
    fixed_one = 1.0 - BETA_ONE**STEP
    fixed_two = 1.0 - BETA_TWO**STEP
    step_dir = (
        moment / fixed_one / (jnp.sqrt(square / fixed_two) + ADAM_EPS) + WEIGHT_DECAY * weight
    )
    return (moment, square, weight - learn_rate * step_dir)


def body(
    pixels,
    segment,
    patch_size,
    labels,
    patch_kernel,
    head_weight,
    input_proj,
    output_proj,
    layer_vector,
    position_table,
    global_vector,
    patch_moment,
    head_moment,
    input_moment,
    output_moment,
    layer_moment,
    position_moment,
    global_moment,
    patch_square,
    head_square,
    input_square,
    output_square,
    layer_square,
    position_square,
    global_square,
):
    pos_weights, member, counts = row_layout(segment, patch_size[0])
    kernel_full = gather_rows(patch_kernel)
    vectors = gather_vectors(layer_vector)
    layer_weights = [
        (gather_rows(input_proj[index]), gather_rows(output_proj[index]), vectors[index])
        for index in range(LAYERS)
    ]
    head_full = gather_rows(head_weight)
    global_low = rounded(global_vector)
    position_low = rounded(position_table)
    embed_pre = matmul(pixels, kernel_full) + global_low[:D]
    stream = embed_pre + jnp.dot(pos_weights, position_low, precision=HIGHEST)
    saved_layers = []
    for weights in layer_weights:
        stream, layer_saved = layer_forward(stream, weights, segment)
        saved_layers.append(layer_saved)
    final_norm, final_back = jax.vjp(
        layer_norm, stream, global_low[D : 2 * D], global_low[2 * D : 3 * D]
    )
    image_sizes = jnp.maximum(counts, 1.0)
    pooled = (jnp.dot(member.T, final_norm, precision=HIGHEST) / image_sizes[:, None]).astype(
        jnp.bfloat16
    )
    logits = matmul(pooled, head_full) + global_low[3 * D :]
    highest = jnp.max(logits, -1, keepdims=True)
    exponent = jnp.exp(logits - highest)
    totals = jnp.sum(exponent, -1, keepdims=True)
    logsum = (highest + jnp.log(totals))[:, 0]
    onehot = labels[0][:, None] == jnp.arange(CLS, dtype=jnp.int32)[None, :]
    picked = jnp.sum(jnp.where(onehot, logits, 0.0), 1)
    loss_local = jnp.sum(counts * (logsum - picked))
    logits_grad = ((exponent / totals - onehot.astype(jnp.float32)) * counts[:, None]).astype(
        jnp.bfloat16
    )
    head_share = scatter_rows(matmul(pooled.T, logits_grad))
    pooled_grad = matmul(logits_grad, head_full.T)
    final_grad = jnp.dot(member, pooled_grad / image_sizes[:, None], precision=HIGHEST)
    stream_grad, final_gain, final_shift = final_back(final_grad)
    layer_shares = [None] * LAYERS
    vector_grads = [None] * LAYERS
    for index in reversed(range(LAYERS)):
        stream_grad, grads = layer_backward(stream_grad, layer_weights[index], saved_layers[index])
        layer_shares[index] = (scatter_rows(grads[0]), scatter_rows(grads[1]))
        vector_grads[index] = grads[2]
    embed_low = stream_grad.astype(jnp.bfloat16)
    kernel_share = scatter_rows(matmul(pixels.T, embed_low))
    position_grad = jnp.dot(pos_weights.T, stream_grad, precision=HIGHEST)
    pieces = [
        position_grad.reshape(-1),
        column_total(embed_low),
        final_gain,
        final_shift,
        column_total(logits_grad),
        *vector_grads,
        loss_local[None],
        jnp.sum(counts)[None],
    ]
    small = total_flat(jnp.concatenate(pieces))
    position_sum = small[: position_grad.size].reshape(position_grad.shape)
    global_sum = small[position_grad.size :][: global_vector.shape[0]]
    vector_total = small[position_grad.size + global_vector.shape[0] :][
        : LAYERS * vectors.shape[1]
    ].reshape(vectors.shape)
    loss_sum = small[-2]
    token_total = small[-1]
    shares = [kernel_share, head_share]
    for pair in layer_shares:
        shares.extend(pair)
    local_squares = sum(jnp.sum(jnp.square(item.astype(jnp.float32))) for item in shares)
    share_squares = lax.psum(local_squares, ("dp", "fsdp"))
    kernel_sum = regather(kernel_share)
    head_sum = regather(head_share)
    input_sum = jnp.stack([regather(pair[0]) for pair in layer_shares])
    output_sum = jnp.stack([regather(pair[1]) for pair in layer_shares])
    vector_sum = lax.dynamic_slice_in_dim(
        vector_total, lax.axis_index("fsdp") * layer_vector.shape[1], layer_vector.shape[1], 1
    )
    grad_norm = (
        jnp.sqrt(
            share_squares
            + jnp.sum(vector_total * vector_total)
            + jnp.sum(position_sum * position_sum)
            + jnp.sum(global_sum * global_sum)
        )
        / token_total
    )
    factor = jnp.minimum(1.0, CLIP_NORM / grad_norm) / token_total
    patch_next = adam_update(
        kernel_sum, patch_moment, patch_square, patch_kernel, factor, LEARN_RATE
    )
    head_next = adam_update(head_sum, head_moment, head_square, head_weight, factor, LEARN_RATE)
    input_next = adam_update(input_sum, input_moment, input_square, input_proj, factor, LEARN_RATE)
    output_next = adam_update(
        output_sum, output_moment, output_square, output_proj, factor, LEARN_RATE
    )
    layer_next = adam_update(
        vector_sum, layer_moment, layer_square, layer_vector, factor, VECTOR_RATE
    )
    position_next = adam_update(
        position_sum, position_moment, position_square, position_table, factor, LEARN_RATE
    )
    global_next = adam_update(
        global_sum, global_moment, global_square, global_vector, factor, VECTOR_RATE
    )
    return (
        loss_sum,
        token_total,
        grad_norm,
        patch_next[0],
        head_next[0],
        input_next[0],
        output_next[0],
        layer_next[0],
        position_next[0],
        global_next[0],
        patch_next[1],
        head_next[1],
        input_next[1],
        output_next[1],
        layer_next[1],
        position_next[1],
        global_next[1],
        patch_next[2],
        head_next[2],
        input_next[2],
        output_next[2],
        layer_next[2],
        position_next[2],
        global_next[2],
    )


def solution(mesh):
    in_specs = (
        P(("dp", "fsdp"), None),
        P(("dp", "fsdp")),
        P(("dp", "fsdp"), None),
        P(("dp", "fsdp"), None),
        P("fsdp", None),
        P("fsdp", None),
        P(None, "fsdp", None),
        P(None, "fsdp", None),
        P(None, "fsdp"),
        P(),
        P(),
        P("fsdp", None),
        P("fsdp", None),
        P(None, "fsdp", None),
        P(None, "fsdp", None),
        P(None, "fsdp"),
        P(),
        P(),
        P("fsdp", None),
        P("fsdp", None),
        P(None, "fsdp", None),
        P(None, "fsdp", None),
        P(None, "fsdp"),
        P(),
        P(),
    )
    out_specs = (
        P(),
        P(),
        P(),
        P("fsdp", None),
        P("fsdp", None),
        P(None, "fsdp", None),
        P(None, "fsdp", None),
        P(None, "fsdp"),
        P(),
        P(),
        P("fsdp", None),
        P("fsdp", None),
        P(None, "fsdp", None),
        P(None, "fsdp", None),
        P(None, "fsdp"),
        P(),
        P(),
        P("fsdp", None),
        P("fsdp", None),
        P(None, "fsdp", None),
        P(None, "fsdp", None),
        P(None, "fsdp"),
        P(),
        P(),
    )
    return jax.shard_map(body, mesh=mesh, in_specs=in_specs, out_specs=out_specs, check_vma=False)
```

```python
import functools

import jax
import jax.numpy as jnp
from jax import lax
from jax.experimental import pallas as pl
from jax.experimental.pallas import tpu as pltpu
from jax.sharding import PartitionSpec as P

D = 768
HEADS = 12
HD = 64
CLS = 1000
GRID = 7
IMG = 240
IMGS = 8
LAYERS = 2
STEP = 3


NORM_EPS = 1e-06
CLIP_NORM = 0.01
LEARN_RATE = 0.05
VECTOR_RATE = 0.25
BETA_ONE = 0.5
BETA_TWO = 0.5
ADAM_EPS = 1e-08
WEIGHT_DECAY = 0.05
HIGHEST = lax.Precision.HIGHEST

PAIR = 2 * HD
MASKED = -1e30
VMEM_LIMIT = 56 * 1024 * 1024
MESH = pl.DeviceIdType.MESH
LANES = 128


def layer_norm(values, gain, shift):
    center = values - jnp.mean(values, -1, keepdims=True)
    spread = jnp.mean(center * center, -1, keepdims=True)
    return center * lax.rsqrt(spread + NORM_EPS) * gain + shift


def rounded(values):
    return lax.optimization_barrier(values.astype(jnp.bfloat16)).astype(jnp.float32)


def column_total(rows):
    return jnp.sum(rows.astype(jnp.float32), 0)


def matmul(left, right):
    return jnp.dot(left, right, preferred_element_type=jnp.float32)


def padded_rows(flat, multiple):
    extra = -flat.shape[0] % (multiple * LANES)
    return jnp.pad(flat, (0, extra)).reshape(-1, LANES)


def row_layout(seg_row, patch_row):
    row_count = seg_row.shape[0]
    slots = jnp.arange(IMGS, dtype=jnp.int32)
    member = seg_row[:, None] == slots[None, :]
    counts = jnp.sum(member.astype(jnp.int32), 0, dtype=jnp.int32)
    starts = jnp.cumsum(counts, dtype=jnp.int32) - counts
    inside = jnp.any(member, 1)
    offset = jnp.arange(row_count, dtype=jnp.int32) - jnp.sum(
        jnp.where(member, starts[None, :], 0), 1, dtype=jnp.int32
    )
    offset = jnp.where(inside, offset, 0)
    patch_tok = jnp.sum(jnp.where(member, patch_row[None, :], 0), 1, dtype=jnp.int32) + jnp.where(
        inside, 0, IMG
    )
    side = IMG // patch_tok
    nodes = jnp.arange(GRID, dtype=jnp.int32).astype(jnp.float32)

    def hat(coord):
        place = ((2 * coord + 1) * GRID).astype(jnp.float32) / (2 * side).astype(jnp.float32) - 0.5
        place = jnp.clip(place, 0.0, GRID - 1.0)
        return jnp.maximum(1.0 - jnp.abs(place[:, None] - nodes[None, :]), 0.0)

    weights = (hat(offset // side)[:, :, None] * hat(offset % side)[:, None, :]).reshape(
        row_count, GRID * GRID
    )
    return (weights, member.astype(jnp.float32), counts.astype(jnp.float32))


TURNS = (1, 2, 3)


def place():
    slot = lax.axis_index("fsdp")
    return lax.axis_index("dp"), lax.div(slot, 2), lax.rem(slot, 2)


def partner(index, turn):
    if turn == 0:
        return index
    if turn == 1:
        return index + 1 - 2 * lax.rem(index, 2)
    if turn == 2:
        return lax.rem(index + 2, 4)
    return 3 - index


def greet():
    group, level, core = place()
    barrier = pltpu.get_barrier_semaphore()
    peers = [(group, 2 * level + 1 - core)]
    for turn in TURNS:
        peers.append((group, 2 * partner(level, turn) + core))
        peers.append((partner(group, turn), 2 * level + core))
    for peer in peers:
        pl.semaphore_signal(barrier, inc=1, device_id=peer, device_id_type=MESH)
    pl.semaphore_wait(barrier, len(peers))


def quarter_shape(rows, columns):
    if columns % (2 * LANES) == 0:
        return rows // 2, columns // 2
    return rows // 4, columns


def quarter(index, rows, columns):
    high, wide = quarter_shape(rows, columns)
    if wide == columns:
        return pl.ds(pl.multiple_of(index * high, high), high), pl.ds(0, columns)
    return (
        pl.ds(pl.multiple_of(lax.div(index, 2) * high, high), high),
        pl.ds(pl.multiple_of(lax.rem(index, 2) * wide, wide), wide),
    )


def remote(source, target, send, receive, device):
    return pltpu.make_async_remote_copy(
        src_ref=source,
        dst_ref=target,
        send_sem=send,
        recv_sem=receive,
        device_id=device,
        device_id_type=MESH,
    )


GATHER_SEMS = 33


class Gather:
    def __init__(self, shard, out, sems, split):
        self.shard, self.out, self.sems, self.split = shard, out, sems, split
        self.rows, self.columns = shard.shape

    def level_copy(self, turn):
        group, level, core = place()
        block = self.out.at[2 * level + core]
        source = self.shard
        if self.split:
            part = quarter(group, self.rows, self.columns)
            source, block = source.at[part], block.at[part]
        sems = self.sems
        peer = (group, 2 * partner(level, turn) + core)
        return remote(source, block, sems.at[turn], sems.at[3 + turn], peer)

    def group_copy(self, turn, other):
        group, level, core = place()
        part = quarter(group, self.rows, self.columns)
        block = self.out.at[2 * partner(level, turn) + core].at[part]
        index = 3 * (turn - 1) + other - 1
        peer = (partner(group, other), 2 * level + core)
        return remote(block, block, self.sems.at[7 + index], self.sems.at[16 + index], peer)

    def core_copy(self, turn):
        group, level, core = place()
        slot = 2 * partner(level, turn) + core
        source = self.shard if turn == 0 else self.out.at[slot]
        peer = (group, 2 * level + 1 - core)
        return remote(source, self.out.at[slot], self.sems.at[25 + turn], self.sems.at[29 + turn], peer)

    def own_copy(self):
        _, level, core = place()
        return pltpu.make_async_copy(self.shard, self.out.at[2 * level + core], self.sems.at[0])

    def first(self):
        for turn in TURNS:
            self.level_copy(turn).start()
        self.core_copy(0).start()
        self.own_copy().start()

    def second(self):
        for turn in TURNS:
            self.level_copy(turn).wait_recv()
            if self.split:
                for other in TURNS:
                    self.group_copy(turn, other).start()
            else:
                self.core_copy(turn).start()

    def third(self):
        if not self.split:
            return
        for turn in TURNS:
            for other in TURNS:
                self.group_copy(turn, other).wait_recv()
            self.core_copy(turn).start()

    def fourth(self):
        for turn in (0, *TURNS):
            self.core_copy(turn).wait_recv()
        for turn in TURNS:
            self.level_copy(turn).wait_send()
            if self.split:
                for other in TURNS:
                    self.group_copy(turn, other).wait_send()
        for turn in (0, *TURNS):
            self.core_copy(turn).wait_send()
        self.own_copy().wait()


def gather_kernel(*refs, split):
    count = len(split)
    sems = refs[2 * count]
    jobs = [
        Gather(refs[i], refs[count + i], sems.at[i], split[i]) for i in range(count)
    ]
    greet()
    for stage in ("first", "second", "third", "fourth"):
        for job in jobs:
            getattr(job, stage)()


def gather_call(shards, split, collective_id):
    count = len(shards)
    owners = lax.axis_size("fsdp")
    anywhere = pl.BlockSpec(memory_space=pl.ANY)
    full = pl.pallas_call(
        functools.partial(gather_kernel, split=split),
        in_specs=[anywhere] * count,
        out_specs=[anywhere] * count,
        out_shape=[jax.ShapeDtypeStruct((owners, *s.shape), s.dtype) for s in shards],
        scratch_shapes=[pltpu.SemaphoreType.DMA((count, GATHER_SEMS))],
        compiler_params=pltpu.CompilerParams(
            collective_id=collective_id, has_side_effects=True, vmem_limit_bytes=VMEM_LIMIT
        ),
        name="gather_weights",
    )(*shards)
    return [f.reshape(owners * f.shape[1], f.shape[2]) for f in full]


REDUCE_SEMS = 48


class Reduce:
    def __init__(self, grad, out, scratch, sems):
        self.grad, self.out, self.sems = grad, out, sems
        self.own, self.got_core, self.got_group, self.part, self.got_level = scratch
        self.rows, self.columns = out.shape
        self.chunk = 16

    def load(self, level):
        _, _, core = place()
        return pltpu.make_async_copy(
            self.grad.at[2 * level + core], self.own.at[level], self.sems.at[level]
        )

    def core_copy(self, target_level):
        group, level, core = place()
        return remote(
            self.grad.at[2 * target_level + 1 - core],
            self.got_core.at[target_level],
            self.sems.at[4 + target_level],
            self.sems.at[8 + target_level],
            (group, 2 * level + 1 - core),
        )

    def group_copy(self, turn, other):
        group, level, core = place()
        target = partner(level, turn)
        peer = partner(group, other)
        part = quarter(peer, self.rows, self.columns)
        index = 3 * turn + other - 1
        return remote(
            self.own.at[target].at[part],
            self.got_group.at[other - 1, target],
            self.sems.at[12 + index],
            self.sems.at[24 + index],
            (peer, 2 * level + core),
        )

    def level_copy(self, turn):
        group, level, core = place()
        target = partner(level, turn)
        return remote(
            self.part.at[target],
            self.got_level.at[turn - 1],
            self.sems.at[35 + turn],
            self.sems.at[38 + turn],
            (group, 2 * target + core),
        )

    def share_copy(self, other):
        group, level, core = place()
        mine = self.out.at[quarter(group, self.rows, self.columns)]
        return remote(
            mine,
            mine,
            self.sems.at[41 + other],
            self.sems.at[44 + other],
            (partner(group, other), 2 * level + core),
        )

    def first(self):
        _, level, _ = place()
        for turn in (*TURNS, 0):
            self.core_copy(partner(level, turn)).start()
            self.load(partner(level, turn)).start()

    def second(self):
        _, level, _ = place()
        for turn in (*TURNS, 0):
            target = partner(level, turn)
            self.load(target).wait()
            self.core_copy(target).wait_recv()

            def add(step, carry):
                rows = pl.ds(pl.multiple_of(step * self.chunk, self.chunk), self.chunk)
                total = self.own[target, rows, :].astype(jnp.float32)
                total = total + self.got_core[target, rows, :].astype(jnp.float32)
                self.own[target, rows, :] = total.astype(self.own.dtype)
                return carry

            lax.fori_loop(0, self.rows // self.chunk, add, 0)
            for other in TURNS:
                self.group_copy(turn, other).start()

    def third(self):
        group, level, _ = place()
        high, wide = quarter_shape(self.rows, self.columns)
        row_part, column_part = quarter(group, self.rows, self.columns)
        for turn in (*TURNS, 0):
            target = partner(level, turn)
            for other in TURNS:
                self.group_copy(turn, other).wait_recv()

            def add(step, carry):
                at = pl.multiple_of(step * self.chunk, self.chunk)
                rows = pl.ds(at, self.chunk)
                mine = pl.ds(pl.multiple_of(row_part.start + at, self.chunk), self.chunk)
                total = self.own[target, mine, column_part].astype(jnp.float32)
                for slot in range(3):
                    total = total + self.got_group[slot, target, rows, :].astype(jnp.float32)
                self.part[target, rows, :] = total.astype(self.part.dtype)
                return carry

            lax.fori_loop(0, high // self.chunk, add, 0)
            if turn:
                self.level_copy(turn).start()

    def fourth(self):
        group, level, _ = place()
        high, wide = quarter_shape(self.rows, self.columns)
        row_part, column_part = quarter(group, self.rows, self.columns)
        for turn in TURNS:
            self.level_copy(turn).wait_recv()

        def add(step, carry):
            at = pl.multiple_of(step * self.chunk, self.chunk)
            rows = pl.ds(at, self.chunk)
            mine = pl.ds(pl.multiple_of(row_part.start + at, self.chunk), self.chunk)
            total = self.part[level, rows, :].astype(jnp.float32)
            for slot in range(3):
                total = total + self.got_level[slot, rows, :].astype(jnp.float32)
            self.out[mine, column_part] = total.astype(self.out.dtype)
            return carry

        lax.fori_loop(0, high // self.chunk, add, 0)
        for other in TURNS:
            self.share_copy(other).start()

    def fifth(self):
        for other in TURNS:
            self.share_copy(other).wait_recv()

    def sixth(self):
        _, level, _ = place()
        for turn in (*TURNS, 0):
            self.core_copy(partner(level, turn)).wait_send()
            for other in TURNS:
                self.group_copy(turn, other).wait_send()
            if turn:
                self.level_copy(turn).wait_send()
                self.share_copy(turn).wait_send()


class Spread:
    def __init__(self, full, sems):
        self.full, self.sems = full, sems

    def level_copy(self, turn):
        group, level, core = place()
        block = self.full.at[2 * level + core]
        peer = (group, 2 * partner(level, turn) + core)
        return remote(block, block, self.sems.at[turn - 1], self.sems.at[2 + turn], peer)

    def core_copy(self, turn):
        group, level, core = place()
        block = self.full.at[2 * partner(level, turn) + core]
        peer = (group, 2 * level + 1 - core)
        return remote(block, block, self.sems.at[6 + turn], self.sems.at[10 + turn], peer)

    def run(self):
        for turn in TURNS:
            self.level_copy(turn).start()
        self.core_copy(0).start()
        for turn in TURNS:
            self.level_copy(turn).wait_recv()
            self.core_copy(turn).start()
        for turn in (0, *TURNS):
            self.core_copy(turn).wait_recv()
        for turn in (0, *TURNS):
            self.core_copy(turn).wait_send()
            if turn:
                self.level_copy(turn).wait_send()


def reduce_kernel(*refs, count, spread):
    grads, refs = refs[:count], refs[count:]
    squares = None
    if spread:
        squares, refs = refs[0], refs[1:]
    outs, refs = refs[:count], refs[count:]
    if spread:
        full, refs = refs[0], refs[1:]
    sems, refs = refs[0], refs[1:]
    if spread:
        spread_sems, refs = refs[0], refs[1:]
    jobs = [
        Reduce(grads[i], outs[i], refs[5 * i : 5 * i + 5], sems.at[i]) for i in range(count)
    ]
    greet()
    for stage in ("first", "second", "third", "fourth", "fifth"):
        for job in jobs:
            getattr(job, stage)()
    if spread:
        _, level, core = place()
        total = squares[...]
        for out in outs[:-1]:
            for step in range(out.shape[0] // 16):
                piece = out[step * 16 : step * 16 + 16, :].astype(jnp.float32)
                piece = jnp.sum(piece * piece, 0, keepdims=True)
                for lane in range(0, out.shape[1], LANES):
                    total = total + piece[:, lane : lane + LANES]
        mine = 2 * level + core
        last = outs[-1].shape[0] - 1
        full[mine] = outs[-1][...]
        full[mine, last : last + 1, :] = total
        Spread(full, spread_sems).run()
    for job in jobs:
        job.sixth()


def reduce_call(grads, collective_id, squares=None):
    count = len(grads)
    spread = squares is not None
    anywhere = pl.BlockSpec(memory_space=pl.ANY)
    in_vmem = pl.BlockSpec(memory_space=pltpu.VMEM)
    scratch = [pltpu.SemaphoreType.DMA((count, REDUCE_SEMS))]
    if spread:
        scratch.append(pltpu.SemaphoreType.DMA((14,)))
    for grad in grads:
        _, rows, columns = grad.shape
        high, wide = quarter_shape(rows, columns)
        for shape in ((4, rows, columns), (4, rows, columns), (3, 4, high, wide), (4, high, wide), (3, high, wide)):
            scratch.append(pltpu.VMEM(shape, grad.dtype))
    out_shape = [jax.ShapeDtypeStruct(g.shape[1:], g.dtype) for g in grads]
    operands = list(grads)
    if spread:
        out_shape.append(jax.ShapeDtypeStruct(grads[-1].shape, grads[-1].dtype))
        operands.append(squares)
    return pl.pallas_call(
        functools.partial(reduce_kernel, count=count, spread=spread),
        in_specs=[anywhere] * count + [in_vmem] * spread,
        out_specs=[in_vmem] * len(out_shape),
        out_shape=out_shape,
        scratch_shapes=scratch,
        compiler_params=pltpu.CompilerParams(
            collective_id=collective_id, has_side_effects=True, vmem_limit_bytes=VMEM_LIMIT
        ),
        name="reduce_gradients",
    )(*operands)


def with_kernels():
    return lax.axis_size("dp") == 4 and lax.axis_size("fsdp") == 8


def gather_all(shards, split, collective_id):
    if with_kernels():
        return gather_call(shards, split, collective_id)
    return [lax.all_gather(shard, "fsdp", axis=0, tiled=True) for shard in shards]


def reduce_all(grads, collective_id, squares=None):
    if with_kernels():
        return reduce_call(grads, collective_id, squares)
    outs = [
        lax.psum(lax.psum_scatter(grad, "fsdp", scatter_dimension=0), "dp") for grad in grads
    ]
    if squares is not None:
        for out in outs[:-1]:
            squares = squares + squares_of(out)
        outs.append(lax.all_gather(outs[-1].at[-1:].set(squares), "fsdp", axis=0))
    return outs


def squares_of(item):
    total = jnp.sum(jnp.square(item.astype(jnp.float32)))
    return jnp.full((1, LANES), 1.0 / LANES, jnp.float32) * total


def by_owner(grad, low=jnp.bfloat16):
    owners = lax.axis_size("fsdp")
    return grad.astype(low).reshape(owners, grad.shape[0] // owners, grad.shape[1])


def attention_forward_kernel(q_ref, k_ref, v_ref, seg_col_ref, seg_row_ref, out_ref, expo_ref, inv_ref, *, block):
    rows = q_ref.shape[0]
    lower = lax.broadcasted_iota(jnp.int32, (block, PAIR), 1) < HD
    keys = k_ref[...]
    values = v_ref[...]
    seg_row = seg_row_ref[...]

    def one_block(step, carry):
        at = pl.ds(pl.multiple_of(step * block, block), block)
        query = q_ref[at, :] * jnp.bfloat16(HD**-0.5)
        same = seg_col_ref[at, :] == seg_row
        outs, invs = [], []
        for head in range(2):
            keep = lower if head == 0 else jnp.logical_not(lower)
            mine = jnp.where(keep, query, jnp.bfloat16(0))
            scores = lax.dot_general(
                mine, keys, (((1,), (1,)), ((), ())), preferred_element_type=jnp.float32
            )
            scores = jnp.where(same, scores, MASKED)
            highest = jnp.max(scores, -1, keepdims=True)
            exponent = jnp.exp(scores - highest)
            total = jnp.sum(exponent, -1, keepdims=True)
            low = exponent.astype(jnp.bfloat16)
            expo_ref[head, at, :] = low
            outs.append(jnp.dot(low, values, preferred_element_type=jnp.float32))
            invs.append(1.0 / total)
        inverse = jnp.where(lower, invs[0], invs[1])
        out_ref[at, :] = (jnp.where(lower, outs[0], outs[1]) * inverse).astype(jnp.bfloat16)
        inv_ref[at, :] = inverse
        return carry

    lax.fori_loop(0, rows // block, one_block, 0, unroll=True)


def attention_forward(qkv_rows, segment):
    rows = qkv_rows.shape[0]
    pairs = HEADS // 2
    block = min(256, rows)
    wide = lambda base: pl.BlockSpec((rows, PAIR), lambda j, base=base: (0, base + j))
    return pl.pallas_call(
        functools.partial(attention_forward_kernel, block=block),
        grid=(pairs,),
        in_specs=[
            wide(0),
            wide(pairs),
            wide(2 * pairs),
            pl.BlockSpec((rows, 1), lambda j: (0, 0)),
            pl.BlockSpec((1, rows), lambda j: (0, 0)),
        ],
        out_specs=[
            wide(0),
            pl.BlockSpec((2, rows, rows), lambda j: (j, 0, 0)),
            wide(0),
        ],
        out_shape=[
            jax.ShapeDtypeStruct((rows, D), jnp.bfloat16),
            jax.ShapeDtypeStruct((HEADS, rows, rows), jnp.bfloat16),
            jax.ShapeDtypeStruct((rows, D), jnp.float32),
        ],
        compiler_params=pltpu.CompilerParams(vmem_limit_bytes=VMEM_LIMIT),
        cost_estimate=pl.CostEstimate(
            flops=4 * HEADS * rows * rows * HD * 4,
            bytes_accessed=2 * HEADS * rows * rows + 12 * rows * D,
            transcendentals=HEADS * rows * rows,
        ),
        name="attention_forward",
    )(qkv_rows, qkv_rows, qkv_rows, segment[:, None], segment[None, :])


def attention_backward_kernel(q_ref, k_ref, v_ref, expo_ref, inv_ref, out_ref, grad_ref, dqkv_ref, *, block):
    rows = q_ref.shape[0]
    pair = pl.program_id(0)
    lower = lax.broadcasted_iota(jnp.int32, (block, PAIR), 1) < HD
    keys = k_ref[...]
    values = v_ref[...]
    scale = HD**-0.5
    scaled_grad = (grad_ref[...].astype(jnp.float32) * inv_ref[...]).astype(jnp.bfloat16)
    query = q_ref[...]
    query_t = query.T
    grad_t = scaled_grad.T
    product = scaled_grad.astype(jnp.float32) * out_ref[...].astype(jnp.float32)
    key_t = [None, None]
    value_t = [None, None]
    for step in range(rows // block):
        at = slice(step * block, (step + 1) * block)
        query_parts = []
        for head in range(2):
            lanes = slice(head * HD, (head + 1) * HD)
            keep = lower if head == 0 else jnp.logical_not(lower)
            mine = jnp.where(keep, scaled_grad[at], jnp.bfloat16(0))
            inner = jnp.sum(jnp.where(keep, product[at], 0.0), -1, keepdims=True)
            low = expo_ref[head, at, :]
            probs_grad = lax.dot_general(
                mine, values, (((1,), (1,)), ((), ())), preferred_element_type=jnp.float32
            )
            scores_grad = (low.astype(jnp.float32) * (probs_grad - inner)).astype(jnp.bfloat16)
            query_parts.append(jnp.dot(scores_grad, keys, preferred_element_type=jnp.float32))
            key_part = jnp.dot(query_t[lanes, at], scores_grad, preferred_element_type=jnp.float32)
            value_part = jnp.dot(grad_t[lanes, at], low, preferred_element_type=jnp.float32)
            key_t[head] = key_part if step == 0 else key_t[head] + key_part
            value_t[head] = value_part if step == 0 else value_t[head] + value_part
        query_grad = jnp.where(lower, query_parts[0], query_parts[1]) * scale
        dqkv_ref[at, pl.ds(pl.multiple_of(pair * PAIR, PAIR), PAIR)] = query_grad.astype(jnp.bfloat16)
    key_grad = (jnp.concatenate(key_t, 0) * scale).T
    value_grad = jnp.concatenate(value_t, 0).T
    dqkv_ref[:, pl.ds(pl.multiple_of(D + pair * PAIR, PAIR), PAIR)] = key_grad.astype(jnp.bfloat16)
    dqkv_ref[:, pl.ds(pl.multiple_of(2 * D + pair * PAIR, PAIR), PAIR)] = value_grad.astype(jnp.bfloat16)


def attention_backward(qkv_rows, expo, inverse, attended, attended_grad):
    rows = qkv_rows.shape[0]
    pairs = HEADS // 2
    block = min(256, rows)
    wide = lambda base: pl.BlockSpec((rows, PAIR), lambda j, base=base: (0, base + j))
    return pl.pallas_call(
        functools.partial(attention_backward_kernel, block=block),
        grid=(pairs,),
        in_specs=[
            wide(0),
            wide(pairs),
            wide(2 * pairs),
            pl.BlockSpec((2, rows, rows), lambda j: (j, 0, 0)),
            wide(0),
            wide(0),
            wide(0),
        ],
        out_specs=pl.BlockSpec((rows, 3 * D), lambda j: (0, 0)),
        out_shape=jax.ShapeDtypeStruct((rows, 3 * D), jnp.bfloat16),
        compiler_params=pltpu.CompilerParams(vmem_limit_bytes=VMEM_LIMIT),
        cost_estimate=pl.CostEstimate(
            flops=8 * HEADS * rows * rows * HD * 4,
            bytes_accessed=2 * HEADS * rows * rows + 20 * rows * D,
            transcendentals=0,
        ),
        name="attention_backward",
    )(qkv_rows, qkv_rows, qkv_rows, expo, inverse, attended, attended_grad)


def layer_forward(stream, weights, seg_row):
    proj_in, proj_out, vector_low = weights
    vector = vector_low.astype(jnp.float32)
    normed = layer_norm(stream, vector[0:D], vector[D : 2 * D]).astype(jnp.bfloat16)
    qkv_rows = (matmul(normed, proj_in[:, : 3 * D]) + vector[4 * D : 7 * D]).astype(jnp.bfloat16)
    attended, expo, inverse = attention_forward(qkv_rows, seg_row)
    residual = stream + matmul(attended, proj_out[:D]) + vector[7 * D : 8 * D]
    normed_second = layer_norm(residual, vector[2 * D : 3 * D], vector[3 * D : 4 * D]).astype(
        jnp.bfloat16
    )
    hidden = matmul(normed_second, proj_in[:, 3 * D :]) + vector[9 * D :]
    active = jax.nn.gelu(hidden).astype(jnp.bfloat16)
    output = residual + matmul(active, proj_out[D:]) + vector[8 * D : 9 * D]
    return (output, (stream, qkv_rows, attended, expo, inverse, residual, hidden))


def layer_backward(grad_stream, weights, layer_saved):
    proj_in, proj_out, vector_low = weights
    vector = vector_low.astype(jnp.float32)
    stream, qkv_rows, attended, expo, inverse, residual, hidden = layer_saved
    grad_low = grad_stream.astype(jnp.bfloat16)
    normed_second, second_back = jax.vjp(
        layer_norm, residual, vector[2 * D : 3 * D], vector[3 * D : 4 * D]
    )
    normed_second = normed_second.astype(jnp.bfloat16)
    active, gelu_back = jax.vjp(jax.nn.gelu, hidden)
    active = active.astype(jnp.bfloat16)
    down_grad = matmul(active.T, grad_low)
    active_grad = matmul(grad_low, proj_out[D:].T)
    hidden_grad = gelu_back(active_grad)[0].astype(jnp.bfloat16)
    up_grad = matmul(normed_second.T, hidden_grad)
    second_grad = matmul(hidden_grad, proj_in[:, 3 * D :].T)
    residual_grad, gain_second, shift_second = second_back(second_grad)
    residual_grad = residual_grad + grad_stream
    residual_low = residual_grad.astype(jnp.bfloat16)
    mixing_grad = matmul(attended.T, residual_low)
    attended_grad = matmul(residual_low, proj_out[:D].T).astype(jnp.bfloat16)
    qkv_grad = attention_backward(qkv_rows, expo, inverse, attended, attended_grad)
    normed, first_back = jax.vjp(layer_norm, stream, vector[0:D], vector[D : 2 * D])
    project_grad = matmul(normed.astype(jnp.bfloat16).T, qkv_grad)
    normed_grad = matmul(qkv_grad, proj_in[:, : 3 * D].T)
    stream_grad, gain_first, shift_first = first_back(normed_grad)
    vector_grad = jnp.concatenate(
        [
            gain_first,
            shift_first,
            gain_second,
            shift_second,
            column_total(qkv_grad),
            column_total(residual_low),
            column_total(grad_low),
            column_total(hidden_grad),
        ]
    )
    return (
        residual_grad + stream_grad,
        (
            project_grad,
            up_grad,
            jnp.concatenate([mixing_grad, down_grad], 0),
            vector_grad,
        ),
    )


def adam_update(gradient, moment, square, weight, factor, learn_rate):
    clipped = gradient * factor
    moment = BETA_ONE * moment + (1.0 - BETA_ONE) * clipped
    square = BETA_TWO * square + (1.0 - BETA_TWO) * clipped * clipped
    fixed_one = 1.0 - BETA_ONE**STEP
    fixed_two = 1.0 - BETA_TWO**STEP
    step_dir = (
        moment / fixed_one / (jnp.sqrt(square / fixed_two) + ADAM_EPS) + WEIGHT_DECAY * weight
    )
    return (moment, square, weight - learn_rate * step_dir)


def body(
    pixels,
    segment,
    patch_size,
    labels,
    patch_kernel,
    head_weight,
    input_proj,
    output_proj,
    layer_vector,
    position_table,
    global_vector,
    patch_moment,
    head_moment,
    input_moment,
    output_moment,
    layer_moment,
    position_moment,
    global_moment,
    patch_square,
    head_square,
    input_square,
    output_square,
    layer_square,
    position_square,
    global_square,
):
    pos_weights, member, counts = row_layout(segment, patch_size[0])
    owners = lax.axis_size("fsdp")
    low = jnp.bfloat16
    vector_size = layer_vector.size
    kernel_full, vectors = gather_all(
        [patch_kernel.astype(low), padded_rows(layer_vector.astype(low).reshape(-1), 32)],
        (True, False),
        1,
    )
    vectors = vectors.reshape(owners, -1)[:, :vector_size].reshape(owners, *layer_vector.shape)
    vectors = jnp.swapaxes(vectors, 0, 1).reshape(LAYERS, -1)
    head_shard = jnp.pad(head_weight.astype(low), ((0, 0), (0, -CLS % LANES)))
    full_zero = gather_all(
        [input_proj[0].astype(low), output_proj[0].astype(low)], (True, True), 2
    )
    full_one = gather_all(
        [input_proj[1].astype(low), output_proj[1].astype(low), head_shard], (True,) * 3, 3
    )
    layer_weights = [(*full_zero, vectors[0]), (*full_one[:2], vectors[1])]
    head_full = full_one[2][:, :CLS]
    global_low = rounded(global_vector)
    position_low = rounded(position_table)
    embed_pre = matmul(pixels, kernel_full) + global_low[:D]
    stream = embed_pre + jnp.dot(pos_weights, position_low, precision=HIGHEST)
    saved_layers = []
    for weights in layer_weights:
        stream, layer_saved = layer_forward(stream, weights, segment)
        saved_layers.append(layer_saved)
    final_norm, final_back = jax.vjp(
        layer_norm, stream, global_low[D : 2 * D], global_low[2 * D : 3 * D]
    )
    image_sizes = jnp.maximum(counts, 1.0)
    pooled = (jnp.dot(member.T, final_norm, precision=HIGHEST) / image_sizes[:, None]).astype(
        jnp.bfloat16
    )
    logits = matmul(pooled, head_full) + global_low[3 * D :]
    highest = jnp.max(logits, -1, keepdims=True)
    exponent = jnp.exp(logits - highest)
    totals = jnp.sum(exponent, -1, keepdims=True)
    logsum = (highest + jnp.log(totals))[:, 0]
    onehot = labels[0][:, None] == jnp.arange(CLS, dtype=jnp.int32)[None, :]
    picked = jnp.sum(jnp.where(onehot, logits, 0.0), 1)
    loss_local = jnp.sum(counts * (logsum - picked))
    logits_grad = ((exponent / totals - onehot.astype(jnp.float32)) * counts[:, None]).astype(
        jnp.bfloat16
    )
    head_grad = jnp.pad(matmul(pooled.T, logits_grad), ((0, 0), (0, -CLS % LANES)))
    pooled_grad = matmul(logits_grad, head_full.T)
    final_grad = jnp.dot(member, pooled_grad / image_sizes[:, None], precision=HIGHEST)
    stream_grad, final_gain, final_shift = final_back(final_grad)
    stream_grad, grads_one = layer_backward(stream_grad, layer_weights[1], saved_layers[1])
    shares_one = reduce_all([by_owner(grad) for grad in (*grads_one[:3], head_grad)], 4)
    stream_grad, grads_zero = layer_backward(stream_grad, layer_weights[0], saved_layers[0])
    shares_zero = reduce_all([by_owner(grad) for grad in grads_zero[:3]], 5)
    embed_low = stream_grad.astype(jnp.bfloat16)
    position_grad = jnp.dot(pos_weights.T, stream_grad, precision=HIGHEST)
    vector_part = jnp.stack([grads_zero[3], grads_one[3]]).reshape(LAYERS, owners, -1)
    vector_part = jnp.swapaxes(vector_part, 0, 1).reshape(owners, vector_size)
    vector_rows = -(-vector_size // LANES)
    vector_part = jnp.pad(vector_part, ((0, 0), (0, vector_rows * LANES - vector_size)))
    rest = jnp.concatenate(
        [
            position_grad.reshape(-1),
            column_total(embed_low),
            final_gain,
            final_shift,
            column_total(logits_grad),
            loss_local[None],
            jnp.sum(counts)[None],
        ]
    )
    rest_rows = -(-rest.shape[0] // (owners * LANES))
    rest_part = jnp.pad(rest, (0, rest_rows * owners * LANES - rest.shape[0]))
    small = jnp.concatenate([vector_part, rest_part.reshape(owners, -1)], 1)
    used = vector_rows + rest_rows
    block_rows = (used // 64 + 1) * 64
    small = jnp.pad(small.reshape(owners, used, LANES), ((0, 0), (0, block_rows - used), (0, 0)))
    squares = sum(squares_of(item) for item in (*shares_zero, *shares_one))
    kernel_sum, small_share, small_full = reduce_all(
        [by_owner(matmul(pixels.T, embed_low)), small], 6, squares
    )
    rest_sum = small_full[:, vector_rows:used].reshape(-1)
    position_sum = rest_sum[: position_grad.size].reshape(position_grad.shape)
    global_sum = rest_sum[position_grad.size :][: global_vector.shape[0]]
    loss_sum = rest_sum[rest.shape[0] - 2]
    token_total = rest_sum[rest.shape[0] - 1]
    kernel_sum = kernel_sum.astype(jnp.float32)
    head_sum = shares_one[3][:, :CLS].astype(jnp.float32)
    input_sum = jnp.stack(
        [jnp.concatenate(pair[:2], 1) for pair in (shares_zero, shares_one)]
    ).astype(jnp.float32)
    output_sum = jnp.stack([shares_zero[2], shares_one[2]]).astype(jnp.float32)
    vector_sum = small_share[:vector_rows].reshape(-1)[:vector_size].reshape(layer_vector.shape)
    grad_norm = (
        jnp.sqrt(
            jnp.sum(small_full[:, -1])
            + jnp.sum(jnp.square(small_full[:, :vector_rows]))
            + jnp.sum(position_sum * position_sum)
            + jnp.sum(global_sum * global_sum)
        )
        / token_total
    )
    factor = jnp.minimum(1.0, CLIP_NORM / grad_norm) / token_total
    patch_next = adam_update(
        kernel_sum, patch_moment, patch_square, patch_kernel, factor, LEARN_RATE
    )
    head_next = adam_update(head_sum, head_moment, head_square, head_weight, factor, LEARN_RATE)
    input_next = adam_update(input_sum, input_moment, input_square, input_proj, factor, LEARN_RATE)
    output_next = adam_update(
        output_sum, output_moment, output_square, output_proj, factor, LEARN_RATE
    )
    layer_next = adam_update(
        vector_sum, layer_moment, layer_square, layer_vector, factor, VECTOR_RATE
    )
    position_next = adam_update(
        position_sum, position_moment, position_square, position_table, factor, LEARN_RATE
    )
    global_next = adam_update(
        global_sum, global_moment, global_square, global_vector, factor, VECTOR_RATE
    )
    return (
        loss_sum,
        token_total,
        grad_norm,
        patch_next[0],
        head_next[0],
        input_next[0],
        output_next[0],
        layer_next[0],
        position_next[0],
        global_next[0],
        patch_next[1],
        head_next[1],
        input_next[1],
        output_next[1],
        layer_next[1],
        position_next[1],
        global_next[1],
        patch_next[2],
        head_next[2],
        input_next[2],
        output_next[2],
        layer_next[2],
        position_next[2],
        global_next[2],
    )


def solution(mesh):
    in_specs = (
        P(("dp", "fsdp"), None),
        P(("dp", "fsdp")),
        P(("dp", "fsdp"), None),
        P(("dp", "fsdp"), None),
        P("fsdp", None),
        P("fsdp", None),
        P(None, "fsdp", None),
        P(None, "fsdp", None),
        P(None, "fsdp"),
        P(),
        P(),
        P("fsdp", None),
        P("fsdp", None),
        P(None, "fsdp", None),
        P(None, "fsdp", None),
        P(None, "fsdp"),
        P(),
        P(),
        P("fsdp", None),
        P("fsdp", None),
        P(None, "fsdp", None),
        P(None, "fsdp", None),
        P(None, "fsdp"),
        P(),
        P(),
    )
    out_specs = (
        P(),
        P(),
        P(),
        P("fsdp", None),
        P("fsdp", None),
        P(None, "fsdp", None),
        P(None, "fsdp", None),
        P(None, "fsdp"),
        P(),
        P(),
        P("fsdp", None),
        P("fsdp", None),
        P(None, "fsdp", None),
        P(None, "fsdp", None),
        P(None, "fsdp"),
        P(),
        P(),
        P("fsdp", None),
        P("fsdp", None),
        P(None, "fsdp", None),
        P(None, "fsdp", None),
        P(None, "fsdp"),
        P(),
        P(),
    )
    return jax.shard_map(body, mesh=mesh, in_specs=in_specs, out_specs=out_specs, check_vma=False)
```

```python
import functools

import jax
import jax.numpy as jnp
from jax import lax
from jax.experimental import pallas as pl
from jax.experimental.pallas import tpu as pltpu
from jax.sharding import PartitionSpec as P

D = 768
HEADS = 12
HD = 64
CLS = 1000
GRID = 7
IMG = 240
IMGS = 8
LAYERS = 2
STEP = 3


NORM_EPS = 1e-06
CLIP_NORM = 0.01
LEARN_RATE = 0.05
VECTOR_RATE = 0.25
BETA_ONE = 0.5
BETA_TWO = 0.5
ADAM_EPS = 1e-08
WEIGHT_DECAY = 0.05
HIGHEST = lax.Precision.HIGHEST

PAIR = 2 * HD
MASKED = -1e30
VMEM_LIMIT = 56 * 1024 * 1024
MESH = pl.DeviceIdType.MESH
LANES = 128


def layer_norm(values, gain, shift):
    center = values - jnp.mean(values, -1, keepdims=True)
    spread = jnp.mean(center * center, -1, keepdims=True)
    return center * lax.rsqrt(spread + NORM_EPS) * gain + shift


def rounded(values):
    return lax.optimization_barrier(values.astype(jnp.bfloat16)).astype(jnp.float32)


def column_total(rows):
    return jnp.sum(rows.astype(jnp.float32), 0)


def matmul(left, right):
    return jnp.dot(left, right, preferred_element_type=jnp.float32)


def padded_rows(flat, multiple):
    extra = -flat.shape[0] % (multiple * LANES)
    return jnp.pad(flat, (0, extra)).reshape(-1, LANES)


def row_layout(seg_row, patch_row):
    row_count = seg_row.shape[0]
    slots = jnp.arange(IMGS, dtype=jnp.int32)
    member = seg_row[:, None] == slots[None, :]
    counts = jnp.sum(member.astype(jnp.int32), 0, dtype=jnp.int32)
    starts = jnp.cumsum(counts, dtype=jnp.int32) - counts
    inside = jnp.any(member, 1)
    offset = jnp.arange(row_count, dtype=jnp.int32) - jnp.sum(
        jnp.where(member, starts[None, :], 0), 1, dtype=jnp.int32
    )
    offset = jnp.where(inside, offset, 0)
    patch_tok = jnp.sum(jnp.where(member, patch_row[None, :], 0), 1, dtype=jnp.int32) + jnp.where(
        inside, 0, IMG
    )
    side = IMG // patch_tok
    nodes = jnp.arange(GRID, dtype=jnp.int32).astype(jnp.float32)

    def hat(coord):
        place = ((2 * coord + 1) * GRID).astype(jnp.float32) / (2 * side).astype(jnp.float32) - 0.5
        place = jnp.clip(place, 0.0, GRID - 1.0)
        return jnp.maximum(1.0 - jnp.abs(place[:, None] - nodes[None, :]), 0.0)

    weights = (hat(offset // side)[:, :, None] * hat(offset % side)[:, None, :]).reshape(
        row_count, GRID * GRID
    )
    return (weights, member.astype(jnp.float32), counts.astype(jnp.float32))


TURNS = (1, 2, 3)


def place():
    slot = lax.axis_index("fsdp")
    return lax.axis_index("dp"), lax.div(slot, 2), lax.rem(slot, 2)


def partner(index, turn):
    if turn == 0:
        return index
    if turn == 1:
        return index + 1 - 2 * lax.rem(index, 2)
    if turn == 2:
        return lax.rem(index + 2, 4)
    return 3 - index


def greet():
    group, level, core = place()
    barrier = pltpu.get_barrier_semaphore()
    peers = [(group, 2 * level + 1 - core)]
    for turn in TURNS:
        peers.append((group, 2 * partner(level, turn) + core))
        peers.append((partner(group, turn), 2 * level + core))
    for peer in peers:
        pl.semaphore_signal(barrier, inc=1, device_id=peer, device_id_type=MESH)
    pl.semaphore_wait(barrier, len(peers))


def quarter_shape(rows, columns):
    if columns % (2 * LANES) == 0:
        return rows // 2, columns // 2
    return rows // 4, columns


def quarter(index, rows, columns):
    high, wide = quarter_shape(rows, columns)
    if wide == columns:
        return pl.ds(pl.multiple_of(index * high, high), high), pl.ds(0, columns)
    return (
        pl.ds(pl.multiple_of(lax.div(index, 2) * high, high), high),
        pl.ds(pl.multiple_of(lax.rem(index, 2) * wide, wide), wide),
    )


def remote(source, target, send, receive, device):
    return pltpu.make_async_remote_copy(
        src_ref=source,
        dst_ref=target,
        send_sem=send,
        recv_sem=receive,
        device_id=device,
        device_id_type=MESH,
    )


GATHER_SEMS = 33


class Gather:
    def __init__(self, shard, out, sems, split):
        self.shard, self.out, self.sems, self.split = shard, out, sems, split
        self.rows, self.columns = shard.shape

    def level_copy(self, turn):
        group, level, core = place()
        block = self.out.at[2 * level + core]
        source = self.shard
        if self.split:
            part = quarter(group, self.rows, self.columns)
            source, block = source.at[part], block.at[part]
        sems = self.sems
        peer = (group, 2 * partner(level, turn) + core)
        return remote(source, block, sems.at[turn], sems.at[3 + turn], peer)

    def group_copy(self, turn, other):
        group, level, core = place()
        part = quarter(group, self.rows, self.columns)
        block = self.out.at[2 * partner(level, turn) + core].at[part]
        index = 3 * (turn - 1) + other - 1
        peer = (partner(group, other), 2 * level + core)
        return remote(block, block, self.sems.at[7 + index], self.sems.at[16 + index], peer)

    def core_copy(self, turn):
        group, level, core = place()
        slot = 2 * partner(level, turn) + core
        source = self.shard if turn == 0 else self.out.at[slot]
        peer = (group, 2 * level + 1 - core)
        return remote(source, self.out.at[slot], self.sems.at[25 + turn], self.sems.at[29 + turn], peer)

    def own_copy(self):
        _, level, core = place()
        return pltpu.make_async_copy(self.shard, self.out.at[2 * level + core], self.sems.at[0])

    def first(self):
        for turn in TURNS:
            self.level_copy(turn).start()
        self.core_copy(0).start()
        self.own_copy().start()

    def second(self):
        for turn in TURNS:
            self.level_copy(turn).wait_recv()
            if self.split:
                for other in TURNS:
                    self.group_copy(turn, other).start()
            else:
                self.core_copy(turn).start()

    def third(self):
        if not self.split:
            return
        for turn in TURNS:
            for other in TURNS:
                self.group_copy(turn, other).wait_recv()
            self.core_copy(turn).start()

    def fourth(self):
        for turn in (0, *TURNS):
            self.core_copy(turn).wait_recv()
        for turn in TURNS:
            self.level_copy(turn).wait_send()
            if self.split:
                for other in TURNS:
                    self.group_copy(turn, other).wait_send()
        for turn in (0, *TURNS):
            self.core_copy(turn).wait_send()
        self.own_copy().wait()


def gather_kernel(*refs, split):
    count = len(split)
    sems = refs[2 * count]
    jobs = [
        Gather(refs[i], refs[count + i], sems.at[i], split[i]) for i in range(count)
    ]
    greet()
    for stage in ("first", "second", "third", "fourth"):
        for job in jobs:
            getattr(job, stage)()


def gather_call(shards, split, collective_id):
    count = len(shards)
    owners = lax.axis_size("fsdp")
    anywhere = pl.BlockSpec(memory_space=pl.ANY)
    full = pl.pallas_call(
        functools.partial(gather_kernel, split=split),
        in_specs=[anywhere] * count,
        out_specs=[anywhere] * count,
        out_shape=[jax.ShapeDtypeStruct((owners, *s.shape), s.dtype) for s in shards],
        scratch_shapes=[pltpu.SemaphoreType.DMA((count, GATHER_SEMS))],
        cost_estimate=transfer_cost(sum(shard.size for shard in shards) * owners),
        compiler_params=pltpu.CompilerParams(
            collective_id=collective_id, has_side_effects=True, vmem_limit_bytes=VMEM_LIMIT
        ),
        name="gather_weights",
    )(*shards)
    return [f.reshape(owners * f.shape[1], f.shape[2]) for f in full]


REDUCE_SEMS = 48


class Reduce:
    def __init__(self, grad, out, scratch, sems):
        self.grad, self.out, self.sems = grad, out, sems
        self.own, self.got_core, self.got_group, self.part, self.got_level = scratch
        self.rows, self.columns = out.shape
        self.chunk = 16

    def load(self, level):
        _, _, core = place()
        return pltpu.make_async_copy(
            self.grad.at[2 * level + core], self.own.at[level], self.sems.at[level]
        )

    def core_copy(self, target_level):
        group, level, core = place()
        return remote(
            self.grad.at[2 * target_level + 1 - core],
            self.got_core.at[target_level],
            self.sems.at[4 + target_level],
            self.sems.at[8 + target_level],
            (group, 2 * level + 1 - core),
        )

    def group_copy(self, turn, other):
        group, level, core = place()
        target = partner(level, turn)
        peer = partner(group, other)
        part = quarter(peer, self.rows, self.columns)
        index = 3 * turn + other - 1
        return remote(
            self.own.at[target].at[part],
            self.got_group.at[other - 1, target],
            self.sems.at[12 + index],
            self.sems.at[24 + index],
            (peer, 2 * level + core),
        )

    def level_copy(self, turn):
        group, level, core = place()
        target = partner(level, turn)
        return remote(
            self.part.at[target],
            self.got_level.at[turn - 1],
            self.sems.at[35 + turn],
            self.sems.at[38 + turn],
            (group, 2 * target + core),
        )

    def share_copy(self, other):
        group, level, core = place()
        mine = self.out.at[quarter(group, self.rows, self.columns)]
        return remote(
            mine,
            mine,
            self.sems.at[41 + other],
            self.sems.at[44 + other],
            (partner(group, other), 2 * level + core),
        )

    def first(self):
        _, level, _ = place()
        for turn in (*TURNS, 0):
            self.core_copy(partner(level, turn)).start()
            self.load(partner(level, turn)).start()

    def second(self):
        _, level, _ = place()
        for turn in (*TURNS, 0):
            target = partner(level, turn)
            self.load(target).wait()
            self.core_copy(target).wait_recv()

            def add(step, carry):
                rows = pl.ds(pl.multiple_of(step * self.chunk, self.chunk), self.chunk)
                total = self.own[target, rows, :].astype(jnp.float32)
                total = total + self.got_core[target, rows, :].astype(jnp.float32)
                self.own[target, rows, :] = total.astype(self.own.dtype)
                return carry

            lax.fori_loop(0, self.rows // self.chunk, add, 0)
            for other in TURNS:
                self.group_copy(turn, other).start()

    def third(self):
        group, level, _ = place()
        high, wide = quarter_shape(self.rows, self.columns)
        row_part, column_part = quarter(group, self.rows, self.columns)
        for turn in (*TURNS, 0):
            target = partner(level, turn)
            for other in TURNS:
                self.group_copy(turn, other).wait_recv()

            def add(step, carry):
                at = pl.multiple_of(step * self.chunk, self.chunk)
                rows = pl.ds(at, self.chunk)
                mine = pl.ds(pl.multiple_of(row_part.start + at, self.chunk), self.chunk)
                total = self.own[target, mine, column_part].astype(jnp.float32)
                for slot in range(3):
                    total = total + self.got_group[slot, target, rows, :].astype(jnp.float32)
                self.part[target, rows, :] = total.astype(self.part.dtype)
                return carry

            lax.fori_loop(0, high // self.chunk, add, 0)
            if turn:
                self.level_copy(turn).start()

    def fourth(self):
        group, level, _ = place()
        high, wide = quarter_shape(self.rows, self.columns)
        row_part, column_part = quarter(group, self.rows, self.columns)
        for turn in TURNS:
            self.level_copy(turn).wait_recv()

        def add(step, carry):
            at = pl.multiple_of(step * self.chunk, self.chunk)
            rows = pl.ds(at, self.chunk)
            mine = pl.ds(pl.multiple_of(row_part.start + at, self.chunk), self.chunk)
            total = self.part[level, rows, :].astype(jnp.float32)
            for slot in range(3):
                total = total + self.got_level[slot, rows, :].astype(jnp.float32)
            self.out[mine, column_part] = total.astype(self.out.dtype)
            return carry

        lax.fori_loop(0, high // self.chunk, add, 0)
        for other in TURNS:
            self.share_copy(other).start()

    def fifth(self):
        for other in TURNS:
            self.share_copy(other).wait_recv()

    def sixth(self):
        _, level, _ = place()
        for turn in (*TURNS, 0):
            self.core_copy(partner(level, turn)).wait_send()
            for other in TURNS:
                self.group_copy(turn, other).wait_send()
            if turn:
                self.level_copy(turn).wait_send()
                self.share_copy(turn).wait_send()


GROUP_SEMS = 13


class GroupReduce:
    def __init__(self, share, out, scratch, sems):
        self.share, self.out, self.sems = share, out, sems
        self.own, self.got = scratch
        self.rows, self.columns = out.shape
        self.chunk = 16

    def load(self):
        return pltpu.make_async_copy(self.share, self.own, self.sems.at[0])

    def group_copy(self, other):
        group, level, core = place()
        peer = partner(group, other)
        return remote(
            self.own.at[quarter(peer, self.rows, self.columns)],
            self.got.at[other - 1],
            self.sems.at[other],
            self.sems.at[3 + other],
            (peer, 2 * level + core),
        )

    def share_copy(self, other):
        group, level, core = place()
        mine = self.out.at[quarter(group, self.rows, self.columns)]
        return remote(
            mine,
            mine,
            self.sems.at[6 + other],
            self.sems.at[9 + other],
            (partner(group, other), 2 * level + core),
        )

    def first(self):
        self.load().start()

    def second(self):
        self.load().wait()
        for other in TURNS:
            self.group_copy(other).start()

    def third(self):
        group, _, _ = place()
        high, wide = quarter_shape(self.rows, self.columns)
        row_part, column_part = quarter(group, self.rows, self.columns)
        for other in TURNS:
            self.group_copy(other).wait_recv()

        def add(step, carry):
            at = pl.multiple_of(step * self.chunk, self.chunk)
            rows = pl.ds(at, self.chunk)
            mine = pl.ds(pl.multiple_of(row_part.start + at, self.chunk), self.chunk)
            total = self.own[mine, column_part].astype(jnp.float32)
            for slot in range(3):
                total = total + self.got[slot, rows, :].astype(jnp.float32)
            self.out[mine, column_part] = total.astype(self.out.dtype)
            return carry

        lax.fori_loop(0, high // self.chunk, add, 0)
        for other in TURNS:
            self.share_copy(other).start()

    def fourth(self):
        pass

    def fifth(self):
        for other in TURNS:
            self.share_copy(other).wait_recv()

    def sixth(self):
        for other in TURNS:
            self.group_copy(other).wait_send()
            self.share_copy(other).wait_send()


class Spread:
    def __init__(self, full, sems):
        self.full, self.sems = full, sems

    def level_copy(self, turn):
        group, level, core = place()
        block = self.full.at[2 * level + core]
        peer = (group, 2 * partner(level, turn) + core)
        return remote(block, block, self.sems.at[turn - 1], self.sems.at[2 + turn], peer)

    def core_copy(self, turn):
        group, level, core = place()
        block = self.full.at[2 * partner(level, turn) + core]
        peer = (group, 2 * level + 1 - core)
        return remote(block, block, self.sems.at[6 + turn], self.sems.at[10 + turn], peer)

    def run(self):
        for turn in TURNS:
            self.level_copy(turn).start()
        self.core_copy(0).start()
        for turn in TURNS:
            self.level_copy(turn).wait_recv()
            self.core_copy(turn).start()
        for turn in (0, *TURNS):
            self.core_copy(turn).wait_recv()
        for turn in (0, *TURNS):
            self.core_copy(turn).wait_send()
            if turn:
                self.level_copy(turn).wait_send()


def squares_in(out):
    def add(step, total):
        piece = out[pl.ds(pl.multiple_of(step * 16, 16), 16), :].astype(jnp.float32)
        piece = piece * piece
        for lane in range(0, out.shape[1], LANES):
            total = total + piece[:, lane : lane + LANES]
        return total

    total = lax.fori_loop(0, out.shape[0] // 16, add, jnp.zeros((16, LANES), jnp.float32))
    return jnp.sum(total, 0, keepdims=True)


def run_stages(jobs, stages):
    for stage in stages:
        for job in jobs:
            getattr(job, stage)()


STAGES = ("first", "second", "third", "fourth", "fifth", "sixth")


def whole_scratch(grad):
    _, rows, columns = grad.shape
    high, wide = quarter_shape(rows, columns)
    shapes = ((4, rows, columns), (4, rows, columns), (3, 4, high, wide), (4, high, wide))
    return [pltpu.VMEM(shape, grad.dtype) for shape in (*shapes, (3, high, wide))]


def reduce_kernel(*refs):
    count = (len(refs) - 1) // 7
    grads, outs, sems, refs = refs[:count], refs[count : 2 * count], refs[2 * count], refs[2 * count + 1 :]
    jobs = [
        Reduce(grads[i], outs[i], refs[5 * i : 5 * i + 5], sems.at[i]) for i in range(count)
    ]
    greet()
    run_stages(jobs, STAGES)


def transfer_cost(size):
    return pl.CostEstimate(flops=4000 * size, bytes_accessed=2 * size, transcendentals=0)


def reduce_call(grads, collective_id):
    in_vmem = pl.BlockSpec(memory_space=pltpu.VMEM)
    scratch = [pltpu.SemaphoreType.DMA((len(grads), REDUCE_SEMS))]
    for grad in grads:
        scratch.extend(whole_scratch(grad))
    return pl.pallas_call(
        reduce_kernel,
        in_specs=[pl.BlockSpec(memory_space=pl.ANY)] * len(grads),
        out_specs=[in_vmem] * len(grads),
        out_shape=[jax.ShapeDtypeStruct(g.shape[1:], g.dtype) for g in grads],
        scratch_shapes=scratch,
        compiler_params=pltpu.CompilerParams(
            collective_id=collective_id, has_side_effects=True, vmem_limit_bytes=VMEM_LIMIT
        ),
        cost_estimate=pl.CostEstimate(flops=0, bytes_accessed=0, transcendentals=0),
        name="reduce_gradients",
    )(*grads)


def finish_kernel(*refs, done, partly):
    finished, refs = refs[:done], refs[done:]
    shares, small, refs = refs[:partly], refs[partly], refs[partly + 1 :]
    outs, small_out, full, refs = refs[:partly], refs[partly], refs[partly + 1], refs[partly + 2 :]
    sems, group_sems, spread_sems, refs = refs[0], refs[1], refs[2], refs[3:]
    job = Reduce(small, small_out, refs[:5], sems)
    refs = refs[5:]
    jobs = [
        GroupReduce(shares[i], outs[i], refs[2 * i : 2 * i + 2], group_sems.at[i])
        for i in range(partly)
    ]
    greet()
    run_stages([job, *jobs], STAGES[:2])
    total = sum(squares_in(out) for out in finished)
    run_stages([*jobs, job], STAGES[2:5])
    total = total + sum(squares_in(out) for out in outs)
    _, level, core = place()
    mine = 2 * level + core
    last = small_out.shape[0] - 1
    full[mine] = small_out[...]
    full[mine, last : last + 1, :] = total
    Spread(full, spread_sems).run()
    run_stages([job, *jobs], STAGES[5:])


def finish_call(finished, shares, small, collective_id):
    done, partly = len(finished), len(shares)
    anywhere = pl.BlockSpec(memory_space=pl.ANY)
    in_vmem = pl.BlockSpec(memory_space=pltpu.VMEM)
    scratch = [
        pltpu.SemaphoreType.DMA((REDUCE_SEMS,)),
        pltpu.SemaphoreType.DMA((partly, GROUP_SEMS)),
        pltpu.SemaphoreType.DMA((14,)),
        *whole_scratch(small),
    ]
    for share in shares:
        scratch.append(pltpu.VMEM(share.shape, share.dtype))
        scratch.append(pltpu.VMEM((3, *quarter_shape(*share.shape)), share.dtype))
    out_shape = [jax.ShapeDtypeStruct(s.shape, s.dtype) for s in shares]
    out_shape.append(jax.ShapeDtypeStruct(small.shape[1:], small.dtype))
    out_shape.append(jax.ShapeDtypeStruct(small.shape, small.dtype))
    return pl.pallas_call(
        functools.partial(finish_kernel, done=done, partly=partly),
        in_specs=[in_vmem] * done + [anywhere] * (partly + 1),
        out_specs=[in_vmem] * len(out_shape),
        out_shape=out_shape,
        scratch_shapes=scratch,
        compiler_params=pltpu.CompilerParams(
            collective_id=collective_id, has_side_effects=True, vmem_limit_bytes=VMEM_LIMIT
        ),
        name="finish_gradients",
    )(*finished, *shares, small)


def with_kernels():
    return lax.axis_size("dp") == 4 and lax.axis_size("fsdp") == 8


def gather_all(shards, split, collective_id):
    if with_kernels():
        return gather_call(shards, split, collective_id)
    return [lax.all_gather(shard, "fsdp", axis=0, tiled=True) for shard in shards]


def reduce_all(grads, collective_id):
    if with_kernels():
        return reduce_call(grads, collective_id)
    return [lax.psum(scatter(grad), "dp") for grad in grads]


def finish_all(finished, shares, small, collective_id):
    if with_kernels():
        return finish_call(finished, shares, small, collective_id)
    outs = [lax.psum(share, "dp") for share in shares]
    own = lax.psum(scatter(small), "dp")
    total = sum(jnp.sum(jnp.square(out.astype(jnp.float32))) for out in (*finished, *outs))
    row = jnp.full((1, LANES), 1.0 / LANES, jnp.float32) * total
    return [*outs, own, lax.all_gather(own.at[-1:].set(row), "fsdp", axis=0)]


def scatter(grad):
    return lax.psum_scatter(grad, "fsdp", scatter_dimension=0)


def by_owner(grad, low=jnp.bfloat16):
    owners = lax.axis_size("fsdp")
    return grad.astype(low).reshape(owners, grad.shape[0] // owners, grad.shape[1])


def attention_forward_kernel(q_ref, k_ref, v_ref, seg_col_ref, seg_row_ref, out_ref, expo_ref, inv_ref, *, block):
    rows = q_ref.shape[0]
    lower = lax.broadcasted_iota(jnp.int32, (block, PAIR), 1) < HD
    keys = k_ref[...]
    values = v_ref[...]
    seg_row = seg_row_ref[...]

    def one_block(step, carry):
        at = pl.ds(pl.multiple_of(step * block, block), block)
        query = q_ref[at, :] * jnp.bfloat16(HD**-0.5)
        same = seg_col_ref[at, :] == seg_row
        outs, invs = [], []
        for head in range(2):
            keep = lower if head == 0 else jnp.logical_not(lower)
            mine = jnp.where(keep, query, jnp.bfloat16(0))
            scores = lax.dot_general(
                mine, keys, (((1,), (1,)), ((), ())), preferred_element_type=jnp.float32
            )
            scores = jnp.where(same, scores, MASKED)
            highest = jnp.max(scores, -1, keepdims=True)
            exponent = jnp.exp(scores - highest)
            total = jnp.sum(exponent, -1, keepdims=True)
            low = exponent.astype(jnp.bfloat16)
            expo_ref[head, at, :] = low
            outs.append(jnp.dot(low, values, preferred_element_type=jnp.float32))
            invs.append(1.0 / total)
        inverse = jnp.where(lower, invs[0], invs[1])
        out_ref[at, :] = (jnp.where(lower, outs[0], outs[1]) * inverse).astype(jnp.bfloat16)
        inv_ref[at, :] = inverse
        return carry

    lax.fori_loop(0, rows // block, one_block, 0, unroll=True)


def attention_forward(qkv_rows, segment):
    rows = qkv_rows.shape[0]
    pairs = HEADS // 2
    block = min(256, rows)
    wide = lambda base: pl.BlockSpec((rows, PAIR), lambda j, base=base: (0, base + j))
    return pl.pallas_call(
        functools.partial(attention_forward_kernel, block=block),
        grid=(pairs,),
        in_specs=[
            wide(0),
            wide(pairs),
            wide(2 * pairs),
            pl.BlockSpec((rows, 1), lambda j: (0, 0)),
            pl.BlockSpec((1, rows), lambda j: (0, 0)),
        ],
        out_specs=[
            wide(0),
            pl.BlockSpec((2, rows, rows), lambda j: (j, 0, 0)),
            wide(0),
        ],
        out_shape=[
            jax.ShapeDtypeStruct((rows, D), jnp.bfloat16),
            jax.ShapeDtypeStruct((HEADS, rows, rows), jnp.bfloat16),
            jax.ShapeDtypeStruct((rows, D), jnp.float32),
        ],
        compiler_params=pltpu.CompilerParams(vmem_limit_bytes=VMEM_LIMIT),
        cost_estimate=pl.CostEstimate(
            flops=4 * HEADS * rows * rows * HD * 4,
            bytes_accessed=2 * HEADS * rows * rows + 12 * rows * D,
            transcendentals=HEADS * rows * rows,
        ),
        name="attention_forward",
    )(qkv_rows, qkv_rows, qkv_rows, segment[:, None], segment[None, :])


def attention_backward_kernel(q_ref, k_ref, v_ref, expo_ref, inv_ref, out_ref, grad_ref, dqkv_ref, *, block):
    rows = q_ref.shape[0]
    pair = pl.program_id(0)
    lower = lax.broadcasted_iota(jnp.int32, (block, PAIR), 1) < HD
    keys = k_ref[...]
    values = v_ref[...]
    scale = HD**-0.5
    scaled_grad = (grad_ref[...].astype(jnp.float32) * inv_ref[...]).astype(jnp.bfloat16)
    query = q_ref[...]
    query_t = query.T
    grad_t = scaled_grad.T
    product = scaled_grad.astype(jnp.float32) * out_ref[...].astype(jnp.float32)
    key_t = [None, None]
    value_t = [None, None]
    for step in range(rows // block):
        at = slice(step * block, (step + 1) * block)
        query_parts = []
        for head in range(2):
            lanes = slice(head * HD, (head + 1) * HD)
            keep = lower if head == 0 else jnp.logical_not(lower)
            mine = jnp.where(keep, scaled_grad[at], jnp.bfloat16(0))
            inner = jnp.sum(jnp.where(keep, product[at], 0.0), -1, keepdims=True)
            low = expo_ref[head, at, :]
            probs_grad = lax.dot_general(
                mine, values, (((1,), (1,)), ((), ())), preferred_element_type=jnp.float32
            )
            scores_grad = (low.astype(jnp.float32) * (probs_grad - inner)).astype(jnp.bfloat16)
            query_parts.append(jnp.dot(scores_grad, keys, preferred_element_type=jnp.float32))
            key_part = jnp.dot(query_t[lanes, at], scores_grad, preferred_element_type=jnp.float32)
            value_part = jnp.dot(grad_t[lanes, at], low, preferred_element_type=jnp.float32)
            key_t[head] = key_part if step == 0 else key_t[head] + key_part
            value_t[head] = value_part if step == 0 else value_t[head] + value_part
        query_grad = jnp.where(lower, query_parts[0], query_parts[1]) * scale
        dqkv_ref[at, pl.ds(pl.multiple_of(pair * PAIR, PAIR), PAIR)] = query_grad.astype(jnp.bfloat16)
    key_grad = (jnp.concatenate(key_t, 0) * scale).T
    value_grad = jnp.concatenate(value_t, 0).T
    dqkv_ref[:, pl.ds(pl.multiple_of(D + pair * PAIR, PAIR), PAIR)] = key_grad.astype(jnp.bfloat16)
    dqkv_ref[:, pl.ds(pl.multiple_of(2 * D + pair * PAIR, PAIR), PAIR)] = value_grad.astype(jnp.bfloat16)


def attention_backward(qkv_rows, expo, inverse, attended, attended_grad):
    rows = qkv_rows.shape[0]
    pairs = HEADS // 2
    block = min(256, rows)
    wide = lambda base: pl.BlockSpec((rows, PAIR), lambda j, base=base: (0, base + j))
    return pl.pallas_call(
        functools.partial(attention_backward_kernel, block=block),
        grid=(pairs,),
        in_specs=[
            wide(0),
            wide(pairs),
            wide(2 * pairs),
            pl.BlockSpec((2, rows, rows), lambda j: (j, 0, 0)),
            wide(0),
            wide(0),
            wide(0),
        ],
        out_specs=pl.BlockSpec((rows, 3 * D), lambda j: (0, 0)),
        out_shape=jax.ShapeDtypeStruct((rows, 3 * D), jnp.bfloat16),
        compiler_params=pltpu.CompilerParams(vmem_limit_bytes=VMEM_LIMIT),
        cost_estimate=pl.CostEstimate(
            flops=8 * HEADS * rows * rows * HD * 4,
            bytes_accessed=2 * HEADS * rows * rows + 20 * rows * D,
            transcendentals=0,
        ),
        name="attention_backward",
    )(qkv_rows, qkv_rows, qkv_rows, expo, inverse, attended, attended_grad)


def layer_forward(stream, weights, seg_row):
    proj_in, proj_out, vector_low = weights
    vector = vector_low.astype(jnp.float32)
    normed = layer_norm(stream, vector[0:D], vector[D : 2 * D]).astype(jnp.bfloat16)
    qkv_rows = (matmul(normed, proj_in[:, : 3 * D]) + vector[4 * D : 7 * D]).astype(jnp.bfloat16)
    attended, expo, inverse = attention_forward(qkv_rows, seg_row)
    residual = stream + matmul(attended, proj_out[:D]) + vector[7 * D : 8 * D]
    normed_second = layer_norm(residual, vector[2 * D : 3 * D], vector[3 * D : 4 * D]).astype(
        jnp.bfloat16
    )
    hidden = matmul(normed_second, proj_in[:, 3 * D :]) + vector[9 * D :]
    active = jax.nn.gelu(hidden).astype(jnp.bfloat16)
    output = residual + matmul(active, proj_out[D:]) + vector[8 * D : 9 * D]
    return (output, (stream, qkv_rows, attended, expo, inverse, residual, hidden))


def layer_backward(grad_stream, weights, layer_saved):
    proj_in, proj_out, vector_low = weights
    vector = vector_low.astype(jnp.float32)
    stream, qkv_rows, attended, expo, inverse, residual, hidden = layer_saved
    grad_low = grad_stream.astype(jnp.bfloat16)
    normed_second, second_back = jax.vjp(
        layer_norm, residual, vector[2 * D : 3 * D], vector[3 * D : 4 * D]
    )
    normed_second = normed_second.astype(jnp.bfloat16)
    active, gelu_back = jax.vjp(jax.nn.gelu, hidden)
    active = active.astype(jnp.bfloat16)
    down_grad = matmul(active.T, grad_low)
    active_grad = matmul(grad_low, proj_out[D:].T)
    hidden_grad = gelu_back(active_grad)[0].astype(jnp.bfloat16)
    up_grad = matmul(normed_second.T, hidden_grad)
    second_grad = matmul(hidden_grad, proj_in[:, 3 * D :].T)
    residual_grad, gain_second, shift_second = second_back(second_grad)
    residual_grad = residual_grad + grad_stream
    residual_low = residual_grad.astype(jnp.bfloat16)
    mixing_grad = matmul(attended.T, residual_low)
    attended_grad = matmul(residual_low, proj_out[:D].T).astype(jnp.bfloat16)
    qkv_grad = attention_backward(qkv_rows, expo, inverse, attended, attended_grad)
    normed, first_back = jax.vjp(layer_norm, stream, vector[0:D], vector[D : 2 * D])
    project_grad = matmul(normed.astype(jnp.bfloat16).T, qkv_grad)
    normed_grad = matmul(qkv_grad, proj_in[:, : 3 * D].T)
    stream_grad, gain_first, shift_first = first_back(normed_grad)
    vector_grad = jnp.concatenate(
        [
            gain_first,
            shift_first,
            gain_second,
            shift_second,
            column_total(qkv_grad),
            column_total(residual_low),
            column_total(grad_low),
            column_total(hidden_grad),
        ]
    )
    return (
        residual_grad + stream_grad,
        (
            project_grad,
            up_grad,
            jnp.concatenate([mixing_grad, down_grad], 0),
            vector_grad,
        ),
    )


def adam_update(gradient, moment, square, weight, factor, learn_rate):
    clipped = gradient * factor
    moment = BETA_ONE * moment + (1.0 - BETA_ONE) * clipped
    square = BETA_TWO * square + (1.0 - BETA_TWO) * clipped * clipped
    fixed_one = 1.0 - BETA_ONE**STEP
    fixed_two = 1.0 - BETA_TWO**STEP
    step_dir = (
        moment / fixed_one / (jnp.sqrt(square / fixed_two) + ADAM_EPS) + WEIGHT_DECAY * weight
    )
    return (moment, square, weight - learn_rate * step_dir)


def body(
    pixels,
    segment,
    patch_size,
    labels,
    patch_kernel,
    head_weight,
    input_proj,
    output_proj,
    layer_vector,
    position_table,
    global_vector,
    patch_moment,
    head_moment,
    input_moment,
    output_moment,
    layer_moment,
    position_moment,
    global_moment,
    patch_square,
    head_square,
    input_square,
    output_square,
    layer_square,
    position_square,
    global_square,
):
    pos_weights, member, counts = row_layout(segment, patch_size[0])
    owners = lax.axis_size("fsdp")
    low = jnp.bfloat16
    vector_size = layer_vector.size
    kernel_full, vectors, input_zero = gather_all(
        [
            patch_kernel.astype(low),
            padded_rows(layer_vector.astype(low).reshape(-1), 32),
            input_proj[0].astype(low),
        ],
        (True, False, True),
        1,
    )
    vectors = vectors.reshape(owners, -1)[:, :vector_size].reshape(owners, *layer_vector.shape)
    vectors = jnp.swapaxes(vectors, 0, 1).reshape(LAYERS, -1)
    output_zero, input_one, output_one, head_full = (
        lax.all_gather(shard.astype(low), "fsdp", axis=0, tiled=True)
        for shard in (output_proj[0], input_proj[1], output_proj[1], head_weight)
    )
    layer_weights = [(input_zero, output_zero, vectors[0]), (input_one, output_one, vectors[1])]
    global_low = rounded(global_vector)
    position_low = rounded(position_table)
    embed_pre = matmul(pixels, kernel_full) + global_low[:D]
    stream = embed_pre + jnp.dot(pos_weights, position_low, precision=HIGHEST)
    saved_layers = []
    for weights in layer_weights:
        stream, layer_saved = layer_forward(stream, weights, segment)
        saved_layers.append(layer_saved)
    final_norm, final_back = jax.vjp(
        layer_norm, stream, global_low[D : 2 * D], global_low[2 * D : 3 * D]
    )
    image_sizes = jnp.maximum(counts, 1.0)
    pooled = (jnp.dot(member.T, final_norm, precision=HIGHEST) / image_sizes[:, None]).astype(
        jnp.bfloat16
    )
    logits = matmul(pooled, head_full) + global_low[3 * D :]
    highest = jnp.max(logits, -1, keepdims=True)
    exponent = jnp.exp(logits - highest)
    totals = jnp.sum(exponent, -1, keepdims=True)
    logsum = (highest + jnp.log(totals))[:, 0]
    onehot = labels[0][:, None] == jnp.arange(CLS, dtype=jnp.int32)[None, :]
    picked = jnp.sum(jnp.where(onehot, logits, 0.0), 1)
    loss_local = jnp.sum(counts * (logsum - picked))
    logits_grad = ((exponent / totals - onehot.astype(jnp.float32)) * counts[:, None]).astype(
        jnp.bfloat16
    )
    head_grad = jnp.pad(matmul(pooled.T, logits_grad), ((0, 0), (0, -CLS % LANES)))
    pooled_grad = matmul(logits_grad, head_full.T)
    final_grad = jnp.dot(member, pooled_grad / image_sizes[:, None], precision=HIGHEST)
    stream_grad, final_gain, final_shift = final_back(final_grad)
    stream_grad, grads_one = layer_backward(stream_grad, layer_weights[1], saved_layers[1])
    stream_grad, *parts_one = lax.optimization_barrier(
        (stream_grad, *(by_owner(grad) for grad in (*grads_one[:3], head_grad)))
    )
    parts_one = [scatter(part) for part in parts_one]
    stream_grad, grads_zero = layer_backward(stream_grad, layer_weights[0], saved_layers[0])
    embed_low = stream_grad.astype(jnp.bfloat16)
    position_grad = jnp.dot(pos_weights.T, stream_grad, precision=HIGHEST)
    vector_part = jnp.stack([grads_zero[3], grads_one[3]]).reshape(LAYERS, owners, -1)
    vector_part = jnp.swapaxes(vector_part, 0, 1).reshape(owners, vector_size)
    vector_rows = -(-vector_size // LANES)
    vector_part = jnp.pad(vector_part, ((0, 0), (0, vector_rows * LANES - vector_size)))
    rest = jnp.concatenate(
        [
            position_grad.reshape(-1),
            column_total(embed_low),
            final_gain,
            final_shift,
            column_total(logits_grad),
            loss_local[None],
            jnp.sum(counts)[None],
        ]
    )
    rest_rows = -(-rest.shape[0] // (owners * LANES))
    rest_part = jnp.pad(rest, (0, rest_rows * owners * LANES - rest.shape[0]))
    small = jnp.concatenate([vector_part, rest_part.reshape(owners, -1)], 1)
    used = vector_rows + rest_rows
    block_rows = (used // 64 + 1) * 64
    small = jnp.pad(small.reshape(owners, used, LANES), ((0, 0), (0, block_rows - used), (0, 0)))
    summed = reduce_all(
        [by_owner(grad) for grad in (*grads_zero[:3], matmul(pixels.T, embed_low))], 2
    )
    shares_zero, kernel_sum = summed[:3], summed[3]
    *shares_one, small_share, small_full = finish_all(summed, parts_one, small, 3)
    rest_sum = small_full[:, vector_rows:used].reshape(-1)
    position_sum = rest_sum[: position_grad.size].reshape(position_grad.shape)
    global_sum = rest_sum[position_grad.size :][: global_vector.shape[0]]
    loss_sum = rest_sum[rest.shape[0] - 2]
    token_total = rest_sum[rest.shape[0] - 1]
    kernel_sum = kernel_sum.astype(jnp.float32)
    head_sum = shares_one[3][:, :CLS].astype(jnp.float32)
    input_sum = jnp.stack(
        [jnp.concatenate(pair[:2], 1) for pair in (shares_zero, shares_one)]
    ).astype(jnp.float32)
    output_sum = jnp.stack([shares_zero[2], shares_one[2]]).astype(jnp.float32)
    vector_sum = small_share[:vector_rows].reshape(-1)[:vector_size].reshape(layer_vector.shape)
    grad_norm = (
        jnp.sqrt(
            jnp.sum(small_full[:, -1])
            + jnp.sum(jnp.square(small_full[:, :vector_rows]))
            + jnp.sum(position_sum * position_sum)
            + jnp.sum(global_sum * global_sum)
        )
        / token_total
    )
    factor = jnp.minimum(1.0, CLIP_NORM / grad_norm) / token_total
    patch_next = adam_update(
        kernel_sum, patch_moment, patch_square, patch_kernel, factor, LEARN_RATE
    )
    head_next = adam_update(head_sum, head_moment, head_square, head_weight, factor, LEARN_RATE)
    input_next = adam_update(input_sum, input_moment, input_square, input_proj, factor, LEARN_RATE)
    output_next = adam_update(
        output_sum, output_moment, output_square, output_proj, factor, LEARN_RATE
    )
    layer_next = adam_update(
        vector_sum, layer_moment, layer_square, layer_vector, factor, VECTOR_RATE
    )
    position_next = adam_update(
        position_sum, position_moment, position_square, position_table, factor, LEARN_RATE
    )
    global_next = adam_update(
        global_sum, global_moment, global_square, global_vector, factor, VECTOR_RATE
    )
    return (
        loss_sum,
        token_total,
        grad_norm,
        patch_next[0],
        head_next[0],
        input_next[0],
        output_next[0],
        layer_next[0],
        position_next[0],
        global_next[0],
        patch_next[1],
        head_next[1],
        input_next[1],
        output_next[1],
        layer_next[1],
        position_next[1],
        global_next[1],
        patch_next[2],
        head_next[2],
        input_next[2],
        output_next[2],
        layer_next[2],
        position_next[2],
        global_next[2],
    )


def solution(mesh):
    in_specs = (
        P(("dp", "fsdp"), None),
        P(("dp", "fsdp")),
        P(("dp", "fsdp"), None),
        P(("dp", "fsdp"), None),
        P("fsdp", None),
        P("fsdp", None),
        P(None, "fsdp", None),
        P(None, "fsdp", None),
        P(None, "fsdp"),
        P(),
        P(),
        P("fsdp", None),
        P("fsdp", None),
        P(None, "fsdp", None),
        P(None, "fsdp", None),
        P(None, "fsdp"),
        P(),
        P(),
        P("fsdp", None),
        P("fsdp", None),
        P(None, "fsdp", None),
        P(None, "fsdp", None),
        P(None, "fsdp"),
        P(),
        P(),
    )
    out_specs = (
        P(),
        P(),
        P(),
        P("fsdp", None),
        P("fsdp", None),
        P(None, "fsdp", None),
        P(None, "fsdp", None),
        P(None, "fsdp"),
        P(),
        P(),
        P("fsdp", None),
        P("fsdp", None),
        P(None, "fsdp", None),
        P(None, "fsdp", None),
        P(None, "fsdp"),
        P(),
        P(),
        P("fsdp", None),
        P("fsdp", None),
        P(None, "fsdp", None),
        P(None, "fsdp", None),
        P(None, "fsdp"),
        P(),
        P(),
    )
    return jax.shard_map(body, mesh=mesh, in_specs=in_specs, out_specs=out_specs, check_vma=False)
```

```python
import functools

import jax
import jax.numpy as jnp
from jax import lax
from jax.experimental import pallas as pl
from jax.experimental.pallas import tpu as pltpu
from jax.sharding import PartitionSpec as P

D = 768
HEADS = 12
HD = 64
CLS = 1000
GRID = 7
IMG = 240
IMGS = 8
LAYERS = 2
STEP = 3


NORM_EPS = 1e-06
CLIP_NORM = 0.01
LEARN_RATE = 0.05
VECTOR_RATE = 0.25
BETA_ONE = 0.5
BETA_TWO = 0.5
ADAM_EPS = 1e-08
WEIGHT_DECAY = 0.05
HIGHEST = lax.Precision.HIGHEST

PAIR = 2 * HD
MASKED = -1e30
VMEM_LIMIT = 56 * 1024 * 1024
MESH = pl.DeviceIdType.MESH
LANES = 128
LOW = jnp.bfloat16
ANYWHERE = pl.BlockSpec(memory_space=pl.ANY)
NO_COST = pl.CostEstimate(flops=0, bytes_accessed=0, transcendentals=0)
ROOT = 0.7978845608028654
CUBE = 0.044715
NT = (((1,), (1,)), ((), ()))


def layer_norm(values, gain, shift):
    center = values - jnp.mean(values, -1, keepdims=True)
    spread = jnp.mean(center * center, -1, keepdims=True)
    return center * lax.rsqrt(spread + NORM_EPS) * gain + shift


def rounded(values):
    return lax.optimization_barrier(values.astype(jnp.bfloat16)).astype(jnp.float32)


def matmul(left, right):
    return jnp.dot(left, right, preferred_element_type=jnp.float32)


def padded_rows(flat, multiple):
    extra = -flat.shape[0] % (multiple * LANES)
    return jnp.pad(flat, (0, extra)).reshape(-1, LANES)


def row_layout(seg_row, patch_row):
    row_count = seg_row.shape[0]
    slots = jnp.arange(IMGS, dtype=jnp.int32)
    member = seg_row[:, None] == slots[None, :]
    counts = jnp.sum(member.astype(jnp.int32), 0, dtype=jnp.int32)
    starts = jnp.cumsum(counts, dtype=jnp.int32) - counts
    inside = jnp.any(member, 1)
    offset = jnp.arange(row_count, dtype=jnp.int32) - jnp.sum(
        jnp.where(member, starts[None, :], 0), 1, dtype=jnp.int32
    )
    offset = jnp.where(inside, offset, 0)
    patch_tok = jnp.sum(jnp.where(member, patch_row[None, :], 0), 1, dtype=jnp.int32) + jnp.where(
        inside, 0, IMG
    )
    side = IMG // patch_tok
    nodes = jnp.arange(GRID, dtype=jnp.int32).astype(jnp.float32)

    def hat(coord):
        place = ((2 * coord + 1) * GRID).astype(jnp.float32) / (2 * side).astype(jnp.float32) - 0.5
        place = jnp.clip(place, 0.0, GRID - 1.0)
        return jnp.maximum(1.0 - jnp.abs(place[:, None] - nodes[None, :]), 0.0)

    weights = (hat(offset // side)[:, :, None] * hat(offset % side)[:, None, :]).reshape(
        row_count, GRID * GRID
    )
    return (weights, member.astype(jnp.float32), counts.astype(jnp.float32))


TURNS = (1, 2, 3)


def place():
    slot = lax.axis_index("fsdp")
    return lax.axis_index("dp"), lax.div(slot, 2), lax.rem(slot, 2)


def partner(index, turn):
    if turn == 0:
        return index
    if turn == 1:
        return index + 1 - 2 * lax.rem(index, 2)
    if turn == 2:
        return lax.rem(index + 2, 4)
    return 3 - index


def greet():
    group, level, core = place()
    barrier = pltpu.get_barrier_semaphore()
    peers = [(group, 2 * level + 1 - core)]
    for turn in TURNS:
        peers.append((group, 2 * partner(level, turn) + core))
        peers.append((partner(group, turn), 2 * level + core))
    for peer in peers:
        pl.semaphore_signal(barrier, inc=1, device_id=peer, device_id_type=MESH)
    pl.semaphore_wait(barrier, len(peers))


def quarter_shape(rows, columns):
    if columns % (2 * LANES) == 0:
        return rows // 2, columns // 2
    return rows // 4, columns


def quarter(index, rows, columns):
    high, wide = quarter_shape(rows, columns)
    if wide == columns:
        return pl.ds(pl.multiple_of(index * high, high), high), pl.ds(0, columns)
    return (
        pl.ds(pl.multiple_of(lax.div(index, 2) * high, high), high),
        pl.ds(pl.multiple_of(lax.rem(index, 2) * wide, wide), wide),
    )


def remote(source, target, send, receive, device):
    return pltpu.make_async_remote_copy(
        src_ref=source,
        dst_ref=target,
        send_sem=send,
        recv_sem=receive,
        device_id=device,
        device_id_type=MESH,
    )


GATHER_SEMS = 33


class Gather:
    def __init__(self, shard, out, sems, split):
        self.shard, self.out, self.sems, self.split = shard, out, sems, split
        self.rows, self.columns = shard.shape

    def level_copy(self, turn):
        group, level, core = place()
        block = self.out.at[2 * level + core]
        source = self.shard
        if self.split:
            part = quarter(group, self.rows, self.columns)
            source, block = source.at[part], block.at[part]
        sems = self.sems
        peer = (group, 2 * partner(level, turn) + core)
        return remote(source, block, sems.at[turn], sems.at[3 + turn], peer)

    def group_copy(self, turn, other):
        group, level, core = place()
        part = quarter(group, self.rows, self.columns)
        block = self.out.at[2 * partner(level, turn) + core].at[part]
        index = 3 * (turn - 1) + other - 1
        peer = (partner(group, other), 2 * level + core)
        return remote(block, block, self.sems.at[7 + index], self.sems.at[16 + index], peer)

    def core_copy(self, turn):
        group, level, core = place()
        slot = 2 * partner(level, turn) + core
        source = self.shard if turn == 0 else self.out.at[slot]
        peer = (group, 2 * level + 1 - core)
        return remote(source, self.out.at[slot], self.sems.at[25 + turn], self.sems.at[29 + turn], peer)

    def own_copy(self):
        _, level, core = place()
        return pltpu.make_async_copy(self.shard, self.out.at[2 * level + core], self.sems.at[0])

    def first(self):
        for turn in TURNS:
            self.level_copy(turn).start()
        self.core_copy(0).start()
        self.own_copy().start()

    def second(self):
        for turn in TURNS:
            self.level_copy(turn).wait_recv()
            if self.split:
                for other in TURNS:
                    self.group_copy(turn, other).start()
            else:
                self.core_copy(turn).start()

    def third(self):
        if not self.split:
            return
        for turn in TURNS:
            for other in TURNS:
                self.group_copy(turn, other).wait_recv()
            self.core_copy(turn).start()

    def fourth(self):
        for turn in (0, *TURNS):
            self.core_copy(turn).wait_recv()
        for turn in TURNS:
            self.level_copy(turn).wait_send()
            if self.split:
                for other in TURNS:
                    self.group_copy(turn, other).wait_send()
        for turn in (0, *TURNS):
            self.core_copy(turn).wait_send()
        self.own_copy().wait()


def beside(jobs, plan):
    for step, stages in plan.items():

        @pl.when(pl.program_id(0) == step)
        def _(stages=stages):
            for stage in stages:
                if stage == "greet":
                    greet()
                else:
                    run_stages(jobs, (stage,))


def gather_kernel(*refs, split):
    count = len(split)
    sems = refs[2 * count]
    jobs = [
        Gather(refs[i], refs[count + i], sems.at[i], split[i]) for i in range(count)
    ]
    greet()
    for stage in ("first", "second", "third", "fourth"):
        for job in jobs:
            getattr(job, stage)()


def gather_call(shards, split, collective_id):
    count = len(shards)
    owners = lax.axis_size("fsdp")
    full = pl.pallas_call(
        functools.partial(gather_kernel, split=split),
        in_specs=[ANYWHERE] * count,
        out_specs=[ANYWHERE] * count,
        out_shape=[jax.ShapeDtypeStruct((owners, *s.shape), s.dtype) for s in shards],
        scratch_shapes=[pltpu.SemaphoreType.DMA((count, GATHER_SEMS))],
        cost_estimate=transfer_cost(sum(shard.size for shard in shards) * owners),
        compiler_params=pltpu.CompilerParams(
            collective_id=collective_id, has_side_effects=True, vmem_limit_bytes=VMEM_LIMIT
        ),
        name="gather_weights",
    )(*shards)
    return [f.reshape(owners * f.shape[1], f.shape[2]) for f in full]


REDUCE_SEMS = 48


class Reduce:
    def __init__(self, grad, out, scratch, sems):
        self.grad, self.out, self.sems = grad, out, sems
        self.own, self.got_core, self.got_group, self.part, self.got_level = scratch
        self.rows, self.columns = out.shape
        self.chunk = 16

    def load(self, level):
        _, _, core = place()
        return pltpu.make_async_copy(
            self.grad.at[2 * level + core], self.own.at[level], self.sems.at[level]
        )

    def core_copy(self, target_level):
        group, level, core = place()
        return remote(
            self.grad.at[2 * target_level + 1 - core],
            self.got_core.at[target_level],
            self.sems.at[4 + target_level],
            self.sems.at[8 + target_level],
            (group, 2 * level + 1 - core),
        )

    def group_copy(self, turn, other):
        group, level, core = place()
        target = partner(level, turn)
        peer = partner(group, other)
        part = quarter(peer, self.rows, self.columns)
        index = 3 * turn + other - 1
        return remote(
            self.own.at[target].at[part],
            self.got_group.at[other - 1, target],
            self.sems.at[12 + index],
            self.sems.at[24 + index],
            (peer, 2 * level + core),
        )

    def level_copy(self, turn):
        group, level, core = place()
        target = partner(level, turn)
        return remote(
            self.part.at[target],
            self.got_level.at[turn - 1],
            self.sems.at[35 + turn],
            self.sems.at[38 + turn],
            (group, 2 * target + core),
        )

    def share_copy(self, other):
        group, level, core = place()
        mine = self.out.at[quarter(group, self.rows, self.columns)]
        return remote(
            mine,
            mine,
            self.sems.at[41 + other],
            self.sems.at[44 + other],
            (partner(group, other), 2 * level + core),
        )

    def first(self):
        _, level, _ = place()
        for turn in (*TURNS, 0):
            self.core_copy(partner(level, turn)).start()
            self.load(partner(level, turn)).start()

    def second(self):
        _, level, _ = place()
        for turn in (*TURNS, 0):
            target = partner(level, turn)
            self.load(target).wait()
            self.core_copy(target).wait_recv()

            def add(step, carry):
                rows = pl.ds(pl.multiple_of(step * self.chunk, self.chunk), self.chunk)
                total = self.own[target, rows, :].astype(jnp.float32)
                total = total + self.got_core[target, rows, :].astype(jnp.float32)
                self.own[target, rows, :] = total.astype(self.own.dtype)
                return carry

            lax.fori_loop(0, self.rows // self.chunk, add, 0)
            for other in TURNS:
                self.group_copy(turn, other).start()

    def third(self):
        group, level, _ = place()
        high, wide = quarter_shape(self.rows, self.columns)
        row_part, column_part = quarter(group, self.rows, self.columns)
        for turn in (*TURNS, 0):
            target = partner(level, turn)
            for other in TURNS:
                self.group_copy(turn, other).wait_recv()

            def add(step, carry):
                at = pl.multiple_of(step * self.chunk, self.chunk)
                rows = pl.ds(at, self.chunk)
                mine = pl.ds(pl.multiple_of(row_part.start + at, self.chunk), self.chunk)
                total = self.own[target, mine, column_part].astype(jnp.float32)
                for slot in range(3):
                    total = total + self.got_group[slot, target, rows, :].astype(jnp.float32)
                self.part[target, rows, :] = total.astype(self.part.dtype)
                return carry

            lax.fori_loop(0, high // self.chunk, add, 0)
            if turn:
                self.level_copy(turn).start()

    def fourth(self):
        group, level, _ = place()
        high, wide = quarter_shape(self.rows, self.columns)
        row_part, column_part = quarter(group, self.rows, self.columns)
        for turn in TURNS:
            self.level_copy(turn).wait_recv()

        def add(step, carry):
            at = pl.multiple_of(step * self.chunk, self.chunk)
            rows = pl.ds(at, self.chunk)
            mine = pl.ds(pl.multiple_of(row_part.start + at, self.chunk), self.chunk)
            total = self.part[level, rows, :].astype(jnp.float32)
            for slot in range(3):
                total = total + self.got_level[slot, rows, :].astype(jnp.float32)
            self.out[mine, column_part] = total.astype(self.out.dtype)
            return carry

        lax.fori_loop(0, high // self.chunk, add, 0)
        for other in TURNS:
            self.share_copy(other).start()

    def fifth(self):
        for other in TURNS:
            self.share_copy(other).wait_recv()

    def sixth(self):
        _, level, _ = place()
        for turn in (*TURNS, 0):
            self.core_copy(partner(level, turn)).wait_send()
            for other in TURNS:
                self.group_copy(turn, other).wait_send()
            if turn:
                self.level_copy(turn).wait_send()
                self.share_copy(turn).wait_send()


GROUP_SEMS = 13


class GroupReduce:
    def __init__(self, share, out, scratch, sems):
        self.share, self.out, self.sems = share, out, sems
        self.own, self.got = scratch
        self.rows, self.columns = out.shape
        self.chunk = 16

    def load(self):
        return pltpu.make_async_copy(self.share, self.own, self.sems.at[0])

    def group_copy(self, other):
        group, level, core = place()
        peer = partner(group, other)
        return remote(
            self.own.at[quarter(peer, self.rows, self.columns)],
            self.got.at[other - 1],
            self.sems.at[other],
            self.sems.at[3 + other],
            (peer, 2 * level + core),
        )

    def share_copy(self, other):
        group, level, core = place()
        mine = self.out.at[quarter(group, self.rows, self.columns)]
        return remote(
            mine,
            mine,
            self.sems.at[6 + other],
            self.sems.at[9 + other],
            (partner(group, other), 2 * level + core),
        )

    def first(self):
        self.load().start()

    def second(self):
        self.load().wait()
        for other in TURNS:
            self.group_copy(other).start()

    def third(self):
        group, _, _ = place()
        high, wide = quarter_shape(self.rows, self.columns)
        row_part, column_part = quarter(group, self.rows, self.columns)
        for other in TURNS:
            self.group_copy(other).wait_recv()

        def add(step, carry):
            at = pl.multiple_of(step * self.chunk, self.chunk)
            rows = pl.ds(at, self.chunk)
            mine = pl.ds(pl.multiple_of(row_part.start + at, self.chunk), self.chunk)
            total = self.own[mine, column_part].astype(jnp.float32)
            for slot in range(3):
                total = total + self.got[slot, rows, :].astype(jnp.float32)
            self.out[mine, column_part] = total.astype(self.out.dtype)
            return carry

        lax.fori_loop(0, high // self.chunk, add, 0)
        for other in TURNS:
            self.share_copy(other).start()

    def fourth(self):
        pass

    def fifth(self):
        for other in TURNS:
            self.share_copy(other).wait_recv()

    def sixth(self):
        for other in TURNS:
            self.group_copy(other).wait_send()
            self.share_copy(other).wait_send()


class Spread:
    def __init__(self, full, sems):
        self.full, self.sems = full, sems

    def level_copy(self, turn):
        group, level, core = place()
        block = self.full.at[2 * level + core]
        peer = (group, 2 * partner(level, turn) + core)
        return remote(block, block, self.sems.at[turn - 1], self.sems.at[2 + turn], peer)

    def core_copy(self, turn):
        group, level, core = place()
        block = self.full.at[2 * partner(level, turn) + core]
        peer = (group, 2 * level + 1 - core)
        return remote(block, block, self.sems.at[6 + turn], self.sems.at[10 + turn], peer)

    def run(self):
        for turn in TURNS:
            self.level_copy(turn).start()
        self.core_copy(0).start()
        for turn in TURNS:
            self.level_copy(turn).wait_recv()
            self.core_copy(turn).start()
        for turn in (0, *TURNS):
            self.core_copy(turn).wait_recv()
        for turn in (0, *TURNS):
            self.core_copy(turn).wait_send()
            if turn:
                self.level_copy(turn).wait_send()


def squares_in(out):
    def add(step, total):
        piece = out[pl.ds(pl.multiple_of(step * 16, 16), 16), :].astype(jnp.float32)
        piece = piece * piece
        for lane in range(0, out.shape[1], LANES):
            total = total + piece[:, lane : lane + LANES]
        return total

    total = lax.fori_loop(0, out.shape[0] // 16, add, jnp.zeros((16, LANES), jnp.float32))
    return jnp.sum(total, 0, keepdims=True)


def run_stages(jobs, stages):
    for stage in stages:
        for job in jobs:
            getattr(job, stage)()


STAGES = ("first", "second", "third", "fourth", "fifth", "sixth")


def whole_scratch(grad):
    _, rows, columns = grad.shape
    high, wide = quarter_shape(rows, columns)
    shapes = ((4, rows, columns), (4, rows, columns), (3, 4, high, wide), (4, high, wide))
    return [pltpu.VMEM(shape, grad.dtype) for shape in (*shapes, (3, high, wide))]


def reduce_kernel(*refs):
    count = (len(refs) - 1) // 7
    grads, outs, sems, refs = refs[:count], refs[count : 2 * count], refs[2 * count], refs[2 * count + 1 :]
    jobs = [
        Reduce(grads[i], outs[i], refs[5 * i : 5 * i + 5], sems.at[i]) for i in range(count)
    ]
    greet()
    run_stages(jobs, STAGES)


def transfer_cost(size):
    return pl.CostEstimate(flops=4000 * size, bytes_accessed=2 * size, transcendentals=0)


def reduce_call(grads, collective_id):
    in_vmem = pl.BlockSpec(memory_space=pltpu.VMEM)
    scratch = [pltpu.SemaphoreType.DMA((len(grads), REDUCE_SEMS))]
    for grad in grads:
        scratch.extend(whole_scratch(grad))
    return pl.pallas_call(
        reduce_kernel,
        in_specs=[ANYWHERE] * len(grads),
        out_specs=[in_vmem] * len(grads),
        out_shape=[jax.ShapeDtypeStruct(g.shape[1:], g.dtype) for g in grads],
        scratch_shapes=scratch,
        compiler_params=pltpu.CompilerParams(
            collective_id=collective_id, has_side_effects=True, vmem_limit_bytes=VMEM_LIMIT
        ),
        cost_estimate=NO_COST,
        name="reduce_gradients",
    )(*grads)


def finish_kernel(*refs, done, partly):
    finished, refs = refs[:done], refs[done:]
    shares, small, refs = refs[:partly], refs[partly], refs[partly + 1 :]
    outs, small_out, full, refs = refs[:partly], refs[partly], refs[partly + 1], refs[partly + 2 :]
    sems, group_sems, spread_sems, refs = refs[0], refs[1], refs[2], refs[3:]
    job = Reduce(small, small_out, refs[:5], sems)
    refs = refs[5:]
    jobs = [
        GroupReduce(shares[i], outs[i], refs[2 * i : 2 * i + 2], group_sems.at[i])
        for i in range(partly)
    ]
    greet()
    run_stages([job, *jobs], STAGES[:2])
    total = sum(squares_in(out) for out in finished)
    run_stages([*jobs, job], STAGES[2:5])
    total = total + sum(squares_in(out) for out in outs)
    _, level, core = place()
    mine = 2 * level + core
    last = small_out.shape[0] - 1
    full[mine] = small_out[...]
    full[mine, last : last + 1, :] = total
    Spread(full, spread_sems).run()
    run_stages([job, *jobs], STAGES[5:])


def finish_call(finished, shares, small, collective_id):
    done, partly = len(finished), len(shares)
    in_vmem = pl.BlockSpec(memory_space=pltpu.VMEM)
    scratch = [
        pltpu.SemaphoreType.DMA((REDUCE_SEMS,)),
        pltpu.SemaphoreType.DMA((partly, GROUP_SEMS)),
        pltpu.SemaphoreType.DMA((14,)),
        *whole_scratch(small),
    ]
    for share in shares:
        scratch.append(pltpu.VMEM(share.shape, share.dtype))
        scratch.append(pltpu.VMEM((3, *quarter_shape(*share.shape)), share.dtype))
    out_shape = [jax.ShapeDtypeStruct(s.shape, s.dtype) for s in shares]
    out_shape.append(jax.ShapeDtypeStruct(small.shape[1:], small.dtype))
    out_shape.append(jax.ShapeDtypeStruct(small.shape, small.dtype))
    return pl.pallas_call(
        functools.partial(finish_kernel, done=done, partly=partly),
        in_specs=[in_vmem] * done + [ANYWHERE] * (partly + 1),
        out_specs=[in_vmem] * len(out_shape),
        out_shape=out_shape,
        scratch_shapes=scratch,
        compiler_params=pltpu.CompilerParams(
            collective_id=collective_id, has_side_effects=True, vmem_limit_bytes=VMEM_LIMIT
        ),
        name="finish_gradients",
    )(*finished, *shares, small)


def with_kernels():
    return lax.axis_size("dp") == 4 and lax.axis_size("fsdp") == 8


def gather_all(shards, split, collective_id):
    if with_kernels():
        return gather_call(shards, split, collective_id)
    return [lax.all_gather(shard, "fsdp", axis=0, tiled=True) for shard in shards]


def reduce_all(grads, collective_id):
    if with_kernels():
        return reduce_call(grads, collective_id)
    return [lax.psum(scatter(grad), "dp") for grad in grads]


def finish_all(finished, shares, small, collective_id):
    if with_kernels():
        return finish_call(finished, shares, small, collective_id)
    outs = [lax.psum(share, "dp") for share in shares]
    own = lax.psum(scatter(small), "dp")
    total = sum(jnp.sum(jnp.square(out.astype(jnp.float32))) for out in (*finished, *outs))
    row = jnp.full((1, LANES), 1.0 / LANES, jnp.float32) * total
    return [*outs, own, lax.all_gather(own.at[-1:].set(row), "fsdp", axis=0)]


def scatter(grad):
    return lax.psum_scatter(grad, "fsdp", scatter_dimension=0)


def by_owner(grad, low=jnp.bfloat16):
    owners = lax.axis_size("fsdp")
    return grad.astype(low).reshape(owners, grad.shape[0] // owners, grad.shape[1])


def attention_forward_kernel(*refs, block, fetched):
    q_ref, k_ref, v_ref, seg_col_ref, seg_row_ref = refs[:5]
    shards, refs = refs[5 : 5 + fetched], refs[5 + fetched :]
    out_ref, expo_ref, inv_ref = refs[:3]
    fulls, refs = refs[3 : 3 + fetched], refs[3 + fetched :]
    jobs = [Gather(shards[i], fulls[i], refs[0].at[i], True) for i in range(fetched)]
    if jobs:
        beside(jobs, {0: ("greet", "first"), 1: ("second",), 3: ("third",)})
    rows = q_ref.shape[0]
    lower = lax.broadcasted_iota(jnp.int32, (block, PAIR), 1) < HD
    keys = k_ref[...]
    values = v_ref[...]
    seg_row = seg_row_ref[...]

    def one_block(step, carry):
        at = pl.ds(pl.multiple_of(step * block, block), block)
        query = q_ref[at, :] * jnp.bfloat16(HD**-0.5)
        same = seg_col_ref[at, :] == seg_row
        outs, invs = [], []
        for head in range(2):
            keep = lower if head == 0 else jnp.logical_not(lower)
            mine = jnp.where(keep, query, jnp.bfloat16(0))
            scores = lax.dot_general(
                mine, keys, (((1,), (1,)), ((), ())), preferred_element_type=jnp.float32
            )
            scores = jnp.where(same, scores, MASKED)
            highest = jnp.max(scores, -1, keepdims=True)
            exponent = jnp.exp(scores - highest)
            total = jnp.sum(exponent, -1, keepdims=True)
            low = exponent.astype(jnp.bfloat16)
            expo_ref[head, at, :] = low
            outs.append(jnp.dot(low, values, preferred_element_type=jnp.float32))
            invs.append(1.0 / total)
        inverse = jnp.where(lower, invs[0], invs[1])
        out_ref[at, :] = (jnp.where(lower, outs[0], outs[1]) * inverse).astype(jnp.bfloat16)
        inv_ref[at, :] = inverse
        return carry

    lax.fori_loop(0, rows // block, one_block, 0, unroll=True)
    if jobs:
        beside(jobs, {pl.num_programs(0) - 1: ("fourth",)})


def attention_forward(qkv_rows, segment, shards, collective_id):
    gathered = []
    if not with_kernels():
        gathered, shards = gather_all(shards, (True,) * len(shards), collective_id), []
    rows = qkv_rows.shape[0]
    fetched = len(shards)
    owners = lax.axis_size("fsdp")
    transfer = {}
    if fetched:
        transfer = {"collective_id": collective_id, "has_side_effects": True}
    pairs = HEADS // 2
    block = min(256, rows)
    wide = lambda base: pl.BlockSpec((rows, PAIR), lambda j, base=base: (0, base + j))
    attended, expo, inverse, *full = pl.pallas_call(
        functools.partial(attention_forward_kernel, block=block, fetched=fetched),
        grid=(pairs,),
        in_specs=[
            wide(0),
            wide(pairs),
            wide(2 * pairs),
            pl.BlockSpec((rows, 1), lambda j: (0, 0)),
            pl.BlockSpec((1, rows), lambda j: (0, 0)),
            *[ANYWHERE] * fetched,
        ],
        out_specs=[
            wide(0),
            pl.BlockSpec((2, rows, rows), lambda j: (j, 0, 0)),
            wide(0),
            *[ANYWHERE] * fetched,
        ],
        out_shape=[
            jax.ShapeDtypeStruct((rows, D), jnp.bfloat16),
            jax.ShapeDtypeStruct((HEADS, rows, rows), jnp.bfloat16),
            jax.ShapeDtypeStruct((rows, D), jnp.float32),
            *[jax.ShapeDtypeStruct((owners, *s.shape), s.dtype) for s in shards],
        ],
        scratch_shapes=[pltpu.SemaphoreType.DMA((fetched, GATHER_SEMS))] * (fetched > 0),
        compiler_params=pltpu.CompilerParams(vmem_limit_bytes=VMEM_LIMIT, **transfer),
        cost_estimate=pl.CostEstimate(
            flops=4 * HEADS * rows * rows * HD * 4,
            bytes_accessed=2 * HEADS * rows * rows + 12 * rows * D,
            transcendentals=HEADS * rows * rows,
        ),
        name="attention_forward",
    )(qkv_rows, qkv_rows, qkv_rows, segment[:, None], segment[None, :], *shards)
    gathered += [f.reshape(owners * f.shape[1], f.shape[2]) for f in full]
    return attended, expo, inverse, gathered


def attention_backward_kernel(*refs, block, reduced):
    q_ref, k_ref, v_ref, expo_ref, inv_ref, out_ref, grad_ref = refs[:7]
    sources, refs = refs[7 : 7 + reduced], refs[7 + reduced :]
    dqkv_ref, sums, refs = refs[0], refs[1 : 1 + reduced], refs[1 + reduced :]
    jobs = [
        Reduce(sources[i], refs[6 * i + 1], refs[6 * i + 2 : 6 * i + 7], refs[0].at[i])
        for i in range(reduced)
    ]
    if jobs:
        beside(jobs, {0: ("greet", "first"), 1: ("second",)})
    rows = q_ref.shape[0]
    pair = pl.program_id(0)
    lower = lax.broadcasted_iota(jnp.int32, (block, PAIR), 1) < HD
    keys = k_ref[...]
    values = v_ref[...]
    scale = HD**-0.5
    scaled_grad = (grad_ref[...].astype(jnp.float32) * inv_ref[...]).astype(jnp.bfloat16)
    query = q_ref[...]
    query_t = query.T
    grad_t = scaled_grad.T
    product = scaled_grad.astype(jnp.float32) * out_ref[...].astype(jnp.float32)
    key_t = [None, None]
    value_t = [None, None]
    for step in range(rows // block):
        at = slice(step * block, (step + 1) * block)
        query_parts = []
        for head in range(2):
            lanes = slice(head * HD, (head + 1) * HD)
            keep = lower if head == 0 else jnp.logical_not(lower)
            mine = jnp.where(keep, scaled_grad[at], jnp.bfloat16(0))
            inner = jnp.sum(jnp.where(keep, product[at], 0.0), -1, keepdims=True)
            low = expo_ref[head, at, :]
            probs_grad = lax.dot_general(
                mine, values, (((1,), (1,)), ((), ())), preferred_element_type=jnp.float32
            )
            scores_grad = (low.astype(jnp.float32) * (probs_grad - inner)).astype(jnp.bfloat16)
            query_parts.append(jnp.dot(scores_grad, keys, preferred_element_type=jnp.float32))
            key_part = jnp.dot(query_t[lanes, at], scores_grad, preferred_element_type=jnp.float32)
            value_part = jnp.dot(grad_t[lanes, at], low, preferred_element_type=jnp.float32)
            key_t[head] = key_part if step == 0 else key_t[head] + key_part
            value_t[head] = value_part if step == 0 else value_t[head] + value_part
        query_grad = jnp.where(lower, query_parts[0], query_parts[1]) * scale
        dqkv_ref[at, pl.ds(pl.multiple_of(pair * PAIR, PAIR), PAIR)] = query_grad.astype(jnp.bfloat16)
    key_grad = (jnp.concatenate(key_t, 0) * scale).T
    value_grad = jnp.concatenate(value_t, 0).T
    dqkv_ref[:, pl.ds(pl.multiple_of(D + pair * PAIR, PAIR), PAIR)] = key_grad.astype(jnp.bfloat16)
    dqkv_ref[:, pl.ds(pl.multiple_of(2 * D + pair * PAIR, PAIR), PAIR)] = value_grad.astype(jnp.bfloat16)
    if jobs:
        beside(jobs, {pl.num_programs(0) - 1: STAGES[2:]})

        @pl.when(pair == pl.num_programs(0) - 1)
        def _():
            for job, total in zip(jobs, sums):
                total[...] = job.out[...]


def attention_backward(qkv_rows, expo, inverse, attended, attended_grad, grads, collective_id):
    plain = []
    if not with_kernels():
        plain, grads = reduce_all(grads, collective_id), []
    reduced = len(grads)
    transfer, scratch = {}, []
    if reduced:
        transfer = {"collective_id": collective_id, "has_side_effects": True}
        scratch.append(pltpu.SemaphoreType.DMA((reduced, REDUCE_SEMS)))
    for grad in grads:
        scratch.append(pltpu.VMEM(grad.shape[1:], grad.dtype))
        scratch.extend(whole_scratch(grad))
    rows = qkv_rows.shape[0]
    pairs = HEADS // 2
    block = min(256, rows)
    wide = lambda base: pl.BlockSpec((rows, PAIR), lambda j, base=base: (0, base + j))
    qkv_grad, *sums = pl.pallas_call(
        functools.partial(attention_backward_kernel, block=block, reduced=reduced),
        grid=(pairs,),
        in_specs=[
            wide(0),
            wide(pairs),
            wide(2 * pairs),
            pl.BlockSpec((2, rows, rows), lambda j: (j, 0, 0)),
            wide(0),
            wide(0),
            wide(0),
            *[ANYWHERE] * reduced,
        ],
        out_specs=[fixed(rows, 3 * D), *[fixed(*g.shape[1:]) for g in grads]],
        out_shape=[
            jax.ShapeDtypeStruct((rows, 3 * D), jnp.bfloat16),
            *[jax.ShapeDtypeStruct(g.shape[1:], g.dtype) for g in grads],
        ],
        scratch_shapes=scratch,
        compiler_params=pltpu.CompilerParams(vmem_limit_bytes=VMEM_LIMIT, **transfer),
        cost_estimate=NO_COST,
        name="attention_backward",
    )(qkv_rows, qkv_rows, qkv_rows, expo, inverse, attended, attended_grad, *grads)
    return qkv_grad, plain + sums


def mul(left, right):
    return jnp.dot(left, right, preferred_element_type=jnp.float32)


def mul_nt(left, right):
    return lax.dot_general(left, right, NT, preferred_element_type=jnp.float32)


def normalized(values):
    center = values - jnp.mean(values, -1, keepdims=True)
    inverse = lax.rsqrt(jnp.mean(center * center, -1, keepdims=True) + NORM_EPS)
    return center * inverse, inverse


def norm_backward(grad, values, gain):
    unit, inverse = normalized(values)
    inner = grad * gain
    mean_inner = jnp.mean(inner, -1, keepdims=True)
    mean_cross = jnp.mean(inner * unit, -1, keepdims=True)
    value_grad = inverse * (inner - mean_inner - unit * mean_cross)
    return value_grad, column_sum(grad * unit), column_sum(grad)


def column_sum(rows):
    return jnp.sum(rows.astype(jnp.float32), 0, keepdims=True)


def at_first(action):
    pl.when(pl.program_id(0) == 0)(action)


def accumulate(out_ref, parts):
    value = jnp.concatenate(parts, 1)

    @pl.when(pl.program_id(0) == 0)
    def _():
        out_ref[...] = value

    @pl.when(pl.program_id(0) > 0)
    def _():
        out_ref[...] += value


def rows_of(block, columns):
    return pl.BlockSpec((block, columns), lambda i: (i, 0))


def fixed(*shape):
    return pl.BlockSpec(shape, lambda i: (0,) * len(shape))


def loads(sources, targets, sems):
    return [
        pltpu.make_async_copy(source, target, sems.at[index])
        for index, (source, target) in enumerate(zip(sources, targets))
    ]


def shape_of(*shape, dtype=jnp.float32):
    return jax.ShapeDtypeStruct(shape, dtype)


def block_call(body, grid, in_specs, out_specs, out_shape, scratch, flops, size, name, early=False):
    return pl.pallas_call(
        body,
        grid=(grid,),
        in_specs=in_specs,
        out_specs=out_specs,
        out_shape=out_shape,
        scratch_shapes=scratch,
        compiler_params=pltpu.CompilerParams(vmem_limit_bytes=VMEM_LIMIT),
        cost_estimate=NO_COST if early else pl.CostEstimate(flops=flops, bytes_accessed=size, transcendentals=0),
        name=name,
    )


def embed_kernel(pixel_ref, weight_ref, pos_ref, table_ref, bias_ref, out_ref):
    position = jnp.dot(
        pos_ref[...], table_ref[...], precision=HIGHEST, preferred_element_type=jnp.float32
    )
    out_ref[...] = mul(pixel_ref[...], weight_ref[...]) + bias_ref[...] + position


def embed(pixels, weight, pos_weights, table, bias):
    rows, depth = pixels.shape
    block = 256
    nodes = pos_weights.shape[1]
    return block_call(
        embed_kernel,
        rows // block,
        [rows_of(block, depth), fixed(depth, D), rows_of(block, nodes), fixed(nodes, D), fixed(1, D)],
        rows_of(block, D),
        shape_of(rows, D),
        [],
        2 * rows * depth * D,
        2 * rows * depth + 2 * depth * D + 4 * rows * D,
        "embed",
    )(pixels, weight, pos_weights, table, bias)


def qkv_kernel(stream_ref, weight_ref, vector_ref, normed_ref, qkv_ref):
    unit, _ = normalized(stream_ref[...])
    normed = (unit * vector_ref[:, :D] + vector_ref[:, D : 2 * D]).astype(jnp.bfloat16)
    normed_ref[...] = normed
    bias = vector_ref[:, 4 * D : 7 * D]
    qkv_ref[...] = (mul(normed, weight_ref[...]) + bias).astype(jnp.bfloat16)


def qkv_forward(stream, weight, vector):
    rows = stream.shape[0]
    block = 256
    low = jnp.bfloat16
    return block_call(
        qkv_kernel,
        rows // block,
        [rows_of(block, D), fixed(D, 3 * D), fixed(1, vector.shape[1])],
        [rows_of(block, D), rows_of(block, 3 * D)],
        [shape_of(rows, D, dtype=low), shape_of(rows, 3 * D, dtype=low)],
        [],
        6 * rows * D * D,
        14 * rows * D + 6 * D * D,
        "qkv_forward",
    )(stream, weight, vector)


def mlp_kernel(
    stream_ref, attended_ref, up_full, proj_out, vector_ref,
    residual_ref, normed_ref, active_ref, slope_ref, out_ref,
    mix_ref, up_ref, down_ref, sems,
):
    width = up_ref.shape[1]
    copies = loads(
        (proj_out.at[pl.ds(0, D)], up_full, proj_out.at[pl.ds(D, width)]),
        (mix_ref, up_ref, down_ref),
        sems,
    )

    @at_first
    def _():
        for copy in copies:
            copy.start()
        copies[0].wait()

    residual = stream_ref[...] + mul(attended_ref[...], mix_ref[...]) + vector_ref[:, 7 * D : 8 * D]
    residual_ref[...] = residual
    unit, _ = normalized(residual)
    normed = (unit * vector_ref[:, 2 * D : 3 * D] + vector_ref[:, 3 * D : 4 * D]).astype(jnp.bfloat16)
    normed_ref[...] = normed
    at_first(copies[1].wait)
    part = 768
    for base in range(0, width, part):
        columns = slice(base, base + part)
        bias = vector_ref[:, 9 * D + base : 9 * D + base + part]
        hidden = mul(normed, up_ref[:, columns]) + bias
        square = hidden * hidden
        bend = jnp.tanh(hidden * (ROOT + (ROOT * CUBE) * square))
        half = 0.5 * (1.0 + bend)
        active_ref[:, columns] = (hidden * half).astype(jnp.bfloat16)
        rise = (0.5 * ROOT) + (1.5 * ROOT * CUBE) * square
        slope_ref[:, columns] = (half + hidden * (1.0 - bend * bend) * rise).astype(jnp.bfloat16)
    at_first(copies[2].wait)
    out_ref[...] = residual + mul(active_ref[...], down_ref[...]) + vector_ref[:, 8 * D : 9 * D]


def mlp_forward(stream, attended, up, proj_out, vector):
    rows = stream.shape[0]
    width = up.shape[1]
    block = 256
    low = jnp.bfloat16
    return block_call(
        mlp_kernel,
        rows // block,
        [rows_of(block, D), rows_of(block, D), ANYWHERE, ANYWHERE, fixed(1, vector.shape[1])],
        [rows_of(block, D), rows_of(block, D), rows_of(block, width), rows_of(block, width), rows_of(block, D)],
        [
            shape_of(rows, D),
            shape_of(rows, D, dtype=low),
            shape_of(rows, width, dtype=low),
            shape_of(rows, width, dtype=low),
            shape_of(rows, D),
        ],
        [
            pltpu.VMEM((D, D), low),
            pltpu.VMEM((D, width), low),
            pltpu.VMEM((width, D), low),
            pltpu.SemaphoreType.DMA((3,)),
        ],
        2 * rows * D * (D + 2 * width),
        rows * (16 * D + 4 * width) + 2 * D * (D + 2 * width),
        "mlp_forward",
    )(stream, attended, up, proj_out, vector)


def mlp_back_kernel(
    grad_ref, slope_ref, residual_ref, up_full, proj_out, vector_ref,
    low_ref, hidden_ref, out_ref, out_low_ref, attended_ref, sums_ref,
    mix_ref, up_ref, down_ref, sems,
):
    width = up_ref.shape[1]
    copies = loads(
        (proj_out.at[pl.ds(D, width)], up_full, proj_out.at[pl.ds(0, D)]),
        (down_ref, up_ref, mix_ref),
        sems,
    )

    @at_first
    def _():
        for copy in copies:
            copy.start()
        copies[0].wait()

    grad = grad_ref[...]
    grad_low = grad.astype(jnp.bfloat16)
    low_ref[...] = grad_low
    part = 768
    hidden_sums = []
    for base in range(0, width, part):
        columns = slice(base, base + part)
        active_grad = mul_nt(grad_low, down_ref[columns, :])
        hidden_grad = (active_grad * slope_ref[:, columns].astype(jnp.float32)).astype(jnp.bfloat16)
        hidden_ref[:, columns] = hidden_grad
        hidden_sums.append(column_sum(hidden_grad))
    at_first(copies[1].wait)
    second_grad = mul_nt(hidden_ref[...], up_ref[...])
    value_grad, gain_grad, shift_grad = norm_backward(
        second_grad, residual_ref[...], vector_ref[:, 2 * D : 3 * D]
    )
    total = value_grad + grad
    out_ref[...] = total
    total_low = total.astype(jnp.bfloat16)
    out_low_ref[...] = total_low
    at_first(copies[2].wait)
    attended_ref[...] = mul_nt(total_low, mix_ref[...]).astype(jnp.bfloat16)
    accumulate(
        sums_ref,
        [gain_grad, shift_grad, column_sum(total_low), column_sum(grad_low), *hidden_sums],
    )


def mlp_backward(grad, slope, residual, up, proj_out, vector):
    rows = grad.shape[0]
    width = up.shape[1]
    block = 256
    low = jnp.bfloat16
    narrow = rows_of(block, D)
    return block_call(
        mlp_back_kernel,
        rows // block,
        [narrow, rows_of(block, width), narrow, ANYWHERE, ANYWHERE, fixed(1, vector.shape[1])],
        [narrow, rows_of(block, width), narrow, narrow, narrow, fixed(1, 4 * D + width)],
        [
            shape_of(rows, D, dtype=low),
            shape_of(rows, width, dtype=low),
            shape_of(rows, D),
            shape_of(rows, D, dtype=low),
            shape_of(rows, D, dtype=low),
            shape_of(1, 4 * D + width),
        ],
        [
            pltpu.VMEM((D, D), low),
            pltpu.VMEM((D, width), low),
            pltpu.VMEM((width, D), low),
            pltpu.SemaphoreType.DMA((3,)),
        ],
        2 * rows * D * (D + 2 * width),
        rows * (18 * D + 4 * width) + 2 * D * (D + 2 * width),
        "mlp_backward",
        early=True,
    )(grad, slope, residual, up, proj_out, vector)


def qkv_back_kernel(grad_ref, residual_ref, stream_ref, weight_ref, vector_ref, out_ref, sums_ref):
    grad = grad_ref[...]
    normed_grad = mul_nt(grad, weight_ref[...])
    value_grad, gain_grad, shift_grad = norm_backward(normed_grad, stream_ref[...], vector_ref[:, :D])
    out_ref[...] = residual_ref[...] + value_grad
    accumulate(sums_ref, [gain_grad, shift_grad, column_sum(grad)])


def qkv_backward(grad, residual_grad, stream, weight, vector):
    rows = stream.shape[0]
    block = 256
    narrow = rows_of(block, D)
    return block_call(
        qkv_back_kernel,
        rows // block,
        [rows_of(block, 3 * D), narrow, narrow, fixed(D, 3 * D), fixed(1, vector.shape[1])],
        [narrow, fixed(1, 5 * D)],
        [shape_of(rows, D), shape_of(1, 5 * D)],
        [],
        6 * rows * D * D,
        18 * rows * D + 6 * D * D,
        "qkv_backward",
        early=True,
    )(grad, residual_grad, stream, weight, vector)


def input_grad_kernel(first_ref, second_ref, qkv_ref, hidden_ref, out_ref, left_ref, *, cut):
    step = pl.program_id(0)

    @pl.when(step == 0)
    def _():
        left_ref[...] = first_ref[...].T

    @pl.when(step == cut)
    def _():
        left_ref[...] = second_ref[...].T

    @pl.when(step < cut)
    def _():
        out_ref[...] = mul(left_ref[...], qkv_ref[...]).astype(jnp.bfloat16)

    @pl.when(step >= cut)
    def _():
        out_ref[...] = mul(left_ref[...], hidden_ref[...]).astype(jnp.bfloat16)


def input_weight_grad(first, second, qkv_grad, hidden_grad):
    rows = first.shape[0]
    cut = qkv_grad.shape[1] // D
    steps = cut + hidden_grad.shape[1] // D
    return block_call(
        functools.partial(input_grad_kernel, cut=cut),
        steps,
        [
            fixed(rows, D),
            fixed(rows, D),
            pl.BlockSpec((rows, D), lambda i: (0, jnp.minimum(i, cut - 1))),
            pl.BlockSpec((rows, D), lambda i: (0, jnp.maximum(i - cut, 0))),
        ],
        pl.BlockSpec((D, D), lambda i: (0, i)),
        shape_of(D, steps * D, dtype=jnp.bfloat16),
        [pltpu.VMEM((D, rows), jnp.bfloat16)],
        2 * rows * D * D * steps,
        2 * rows * D * (steps + 2) + 2 * D * D * steps,
        "input_weight_grad",
        early=True,
    )(first, second, qkv_grad, hidden_grad)


def output_grad_kernel(attended_ref, active_ref, residual_ref, grad_ref, out_ref, *, cut):
    step = pl.program_id(0)

    @pl.when(step < cut)
    def _():
        out_ref[...] = mul(attended_ref[...].T, residual_ref[...]).astype(jnp.bfloat16)

    @pl.when(step >= cut)
    def _():
        out_ref[...] = mul(active_ref[...].T, grad_ref[...]).astype(jnp.bfloat16)


def output_weight_grad(attended, active, residual_low, grad_low):
    rows = attended.shape[0]
    block = 768
    cut = attended.shape[1] // block
    steps = cut + active.shape[1] // block
    return block_call(
        functools.partial(output_grad_kernel, cut=cut),
        steps,
        [
            pl.BlockSpec((rows, block), lambda i: (0, jnp.minimum(i, cut - 1))),
            pl.BlockSpec((rows, block), lambda i: (0, jnp.maximum(i - cut, 0))),
            fixed(rows, D),
            fixed(rows, D),
        ],
        rows_of(block, D),
        shape_of(steps * block, D, dtype=jnp.bfloat16),
        [],
        2 * rows * D * block * steps,
        2 * rows * (block * steps + 2 * D) + 2 * D * block * steps,
        "output_weight_grad",
        early=True,
    )(attended, active, residual_low, grad_low)


def embed_back_kernel(pixel_ref, grad_ref, pos_ref, out_ref, table_ref, bias_ref, low_ref):
    @at_first
    def _():
        grad = grad_ref[...]
        low = grad.astype(jnp.bfloat16)
        low_ref[...] = low
        bias_ref[...] = column_sum(low)
        table_ref[...] = jnp.dot(
            pos_ref[...], grad, precision=HIGHEST, preferred_element_type=jnp.float32
        )

    out_ref[...] = mul(pixel_ref[...].T, low_ref[...]).astype(jnp.bfloat16)


def embed_backward(pixels, grad, pos_weights_t):
    rows, depth = pixels.shape
    block = 768
    nodes = pos_weights_t.shape[0]
    return block_call(
        embed_back_kernel,
        depth // block,
        [pl.BlockSpec((rows, block), lambda i: (0, i)), fixed(rows, D), fixed(nodes, rows)],
        [rows_of(block, D), fixed(nodes, D), fixed(1, D)],
        [shape_of(depth, D, dtype=jnp.bfloat16), shape_of(nodes, D), shape_of(1, D)],
        [pltpu.VMEM((rows, D), jnp.bfloat16)],
        2 * rows * depth * D,
        2 * rows * depth + 2 * depth * D + 4 * rows * D,
        "embed_backward",
        early=True,
    )(pixels, grad, pos_weights_t)


def adam_update(gradient, moment, square, weight, factor, learn_rate):
    clipped = gradient * factor
    moment = BETA_ONE * moment + (1.0 - BETA_ONE) * clipped
    square = BETA_TWO * square + (1.0 - BETA_TWO) * clipped * clipped
    fixed_one = 1.0 - BETA_ONE**STEP
    fixed_two = 1.0 - BETA_TWO**STEP
    step_dir = (
        moment / fixed_one / (jnp.sqrt(square / fixed_two) + ADAM_EPS) + WEIGHT_DECAY * weight
    )
    return (moment, square, weight - learn_rate * step_dir)


def body(
    pixels,
    segment,
    patch_size,
    labels,
    patch_kernel,
    head_weight,
    input_proj,
    output_proj,
    layer_vector,
    position_table,
    global_vector,
    patch_moment,
    head_moment,
    input_moment,
    output_moment,
    layer_moment,
    position_moment,
    global_moment,
    patch_square,
    head_square,
    input_square,
    output_square,
    layer_square,
    position_square,
    global_square,
):
    pos_weights, member, counts = row_layout(segment, patch_size[0])
    owners = lax.axis_size("fsdp")
    nodes = pos_weights.shape[1]
    pos_weights = jnp.pad(pos_weights, ((0, 0), (0, -nodes % 64)))
    vector_size = layer_vector.size
    inputs = [
        (input_proj[index, :, : 3 * D].astype(LOW), input_proj[index, :, 3 * D :].astype(LOW))
        for index in range(LAYERS)
    ]
    outputs = [output_proj[index].astype(LOW) for index in range(LAYERS)]
    kernel_full, vectors, qkv_zero = gather_all(
        [
            patch_kernel.astype(LOW),
            padded_rows(layer_vector.astype(LOW).reshape(-1), 32),
            inputs[0][0],
        ],
        (True, False, True),
        1,
    )
    vectors = vectors.reshape(owners, -1)[:, :vector_size].reshape(owners, *layer_vector.shape)
    vectors = jnp.swapaxes(vectors, 0, 1).reshape(LAYERS, 1, -1).astype(jnp.float32)
    output_zero, qkv_one, up_one, head_full = (
        lax.all_gather(shard, "fsdp", axis=0, tiled=True)
        for shard in (outputs[0], *inputs[1], head_weight.astype(LOW))
    )
    global_low = rounded(global_vector)
    position_low = jnp.pad(rounded(position_table), ((0, -nodes % 64), (0, 0)))
    stream = embed(pixels, kernel_full, pos_weights, position_low, global_low[None, :D])
    saved_layers = []
    for index, qkv_weight in enumerate((qkv_zero, qkv_one)):
        vector = vectors[index]
        normed, qkv_rows = qkv_forward(stream, qkv_weight, vector)
        fetch = inputs[0][1] if index == 0 else outputs[1]
        attended, expo, inverse, (fetched,) = attention_forward(
            qkv_rows, segment, [fetch], 4 + index
        )
        up, output = (fetched, output_zero) if index == 0 else (up_one, fetched)
        residual, normed_second, active, slope, following = mlp_forward(
            stream, attended, up, output, vector
        )
        saved_layers.append(
            (
                (qkv_weight, up, output, vector),
                (stream, normed, qkv_rows, attended, expo, inverse),
                (residual, normed_second, active, slope),
            )
        )
        stream = following
    final_norm, final_back = jax.vjp(
        layer_norm, stream, global_low[D : 2 * D], global_low[2 * D : 3 * D]
    )
    image_sizes = jnp.maximum(counts, 1.0)
    pooled = (jnp.dot(member.T, final_norm, precision=HIGHEST) / image_sizes[:, None]).astype(
        jnp.bfloat16
    )
    logits = matmul(pooled, head_full) + global_low[3 * D :]
    highest = jnp.max(logits, -1, keepdims=True)
    exponent = jnp.exp(logits - highest)
    totals = jnp.sum(exponent, -1, keepdims=True)
    logsum = (highest + jnp.log(totals))[:, 0]
    onehot = labels[0][:, None] == jnp.arange(CLS, dtype=jnp.int32)[None, :]
    picked = jnp.sum(jnp.where(onehot, logits, 0.0), 1)
    loss_local = jnp.sum(counts * (logsum - picked))
    logits_grad = ((exponent / totals - onehot.astype(jnp.float32)) * counts[:, None]).astype(
        jnp.bfloat16
    )
    head_grad = matmul(pooled.T, logits_grad).astype(LOW)
    head_part = scatter(by_owner(jnp.pad(head_grad, ((0, 0), (0, -CLS % LANES)))))
    pooled_grad = matmul(logits_grad, head_full.T)
    final_grad = jnp.dot(member, pooled_grad / image_sizes[:, None], precision=HIGHEST)
    stream_grad, final_gain, final_shift = final_back(final_grad)
    vector_grads = [None] * LAYERS
    parts = [head_part]
    for index in reversed(range(LAYERS)):
        (qkv_weight, up, output, vector), first, second = saved_layers[index]
        entering, normed, qkv_rows, attended, expo, inverse = first
        residual, normed_second, active, slope = second
        grad_low, hidden_grad, residual_grad, residual_low, attended_grad, mlp_sums = mlp_backward(
            stream_grad, slope, residual, up, output, vector
        )
        output_grad = output_weight_grad(attended, active, residual_low, grad_low)
        attended_grad, output_grad = lax.optimization_barrier((attended_grad, output_grad))
        beside_attention = []
        if index:
            parts.append(scatter(by_owner(output_grad)))
        else:
            beside_attention.append(by_owner(output_grad))
        qkv_grad, output_sums = attention_backward(
            qkv_rows, expo, inverse, attended, attended_grad, beside_attention, 6
        )
        stream_grad, qkv_sums = qkv_backward(qkv_grad, residual_grad, entering, qkv_weight, vector)
        input_grad = input_weight_grad(normed, normed_second, qkv_grad, hidden_grad)
        if index:
            stream_grad, input_grad = lax.optimization_barrier((stream_grad, input_grad))
            parts.append(scatter(by_owner(input_grad)))
        vector_grads[index] = jnp.concatenate(
            [
                qkv_sums[0, : 2 * D],
                mlp_sums[0, : 2 * D],
                qkv_sums[0, 2 * D :],
                mlp_sums[0, 2 * D :],
            ]
        )
    kernel_grad, position_grad, bias_grad = embed_backward(pixels, stream_grad, pos_weights.T)
    position_grad = position_grad[:nodes]
    vector_part = jnp.stack(vector_grads).reshape(LAYERS, owners, -1)
    vector_part = jnp.swapaxes(vector_part, 0, 1).reshape(owners, vector_size)
    vector_rows = -(-vector_size // LANES)
    vector_part = jnp.pad(vector_part, ((0, 0), (0, vector_rows * LANES - vector_size)))
    rest = jnp.concatenate(
        [
            position_grad.reshape(-1),
            bias_grad[0],
            final_gain,
            final_shift,
            jnp.sum(logits_grad.astype(jnp.float32), 0),
            loss_local[None],
            jnp.sum(counts)[None],
        ]
    )
    rest_rows = -(-rest.shape[0] // (owners * LANES))
    rest_part = jnp.pad(rest, (0, rest_rows * owners * LANES - rest.shape[0]))
    small = jnp.concatenate([vector_part, rest_part.reshape(owners, -1)], 1)
    used = vector_rows + rest_rows
    block_rows = (used // 64 + 1) * 64
    small = jnp.pad(small.reshape(owners, used, LANES), ((0, 0), (0, block_rows - used), (0, 0)))
    summed = reduce_all([by_owner(input_grad), by_owner(kernel_grad)], 2)
    (output_zero_sum,) = output_sums
    head_sum, output_one_sum, input_one_sum, small_share, small_full = finish_all(
        [*summed, output_zero_sum], parts, small, 3
    )
    rest_sum = small_full[:, vector_rows:used].reshape(-1)
    position_sum = rest_sum[: position_grad.size].reshape(position_grad.shape)
    global_sum = rest_sum[position_grad.size :][: global_vector.shape[0]]
    loss_sum = rest_sum[rest.shape[0] - 2]
    token_total = rest_sum[rest.shape[0] - 1]
    kernel_sum = summed[1].astype(jnp.float32)
    head_sum = head_sum[:, :CLS].astype(jnp.float32)
    input_sum = jnp.stack([summed[0], input_one_sum]).astype(jnp.float32)
    output_sum = jnp.stack([output_zero_sum, output_one_sum]).astype(jnp.float32)
    vector_sum = small_share[:vector_rows].reshape(-1)[:vector_size].reshape(layer_vector.shape)
    grad_norm = (
        jnp.sqrt(
            jnp.sum(small_full[:, -1])
            + jnp.sum(jnp.square(small_full[:, :vector_rows]))
            + jnp.sum(position_sum * position_sum)
            + jnp.sum(global_sum * global_sum)
        )
        / token_total
    )
    factor = jnp.minimum(1.0, CLIP_NORM / grad_norm) / token_total
    patch_next = adam_update(
        kernel_sum, patch_moment, patch_square, patch_kernel, factor, LEARN_RATE
    )
    head_next = adam_update(head_sum, head_moment, head_square, head_weight, factor, LEARN_RATE)
    input_next = adam_update(input_sum, input_moment, input_square, input_proj, factor, LEARN_RATE)
    output_next = adam_update(
        output_sum, output_moment, output_square, output_proj, factor, LEARN_RATE
    )
    layer_next = adam_update(
        vector_sum, layer_moment, layer_square, layer_vector, factor, VECTOR_RATE
    )
    position_next = adam_update(
        position_sum, position_moment, position_square, position_table, factor, LEARN_RATE
    )
    global_next = adam_update(
        global_sum, global_moment, global_square, global_vector, factor, VECTOR_RATE
    )
    return (
        loss_sum,
        token_total,
        grad_norm,
        patch_next[0],
        head_next[0],
        input_next[0],
        output_next[0],
        layer_next[0],
        position_next[0],
        global_next[0],
        patch_next[1],
        head_next[1],
        input_next[1],
        output_next[1],
        layer_next[1],
        position_next[1],
        global_next[1],
        patch_next[2],
        head_next[2],
        input_next[2],
        output_next[2],
        layer_next[2],
        position_next[2],
        global_next[2],
    )


def solution(mesh):
    in_specs = (
        P(("dp", "fsdp"), None),
        P(("dp", "fsdp")),
        P(("dp", "fsdp"), None),
        P(("dp", "fsdp"), None),
        P("fsdp", None),
        P("fsdp", None),
        P(None, "fsdp", None),
        P(None, "fsdp", None),
        P(None, "fsdp"),
        P(),
        P(),
        P("fsdp", None),
        P("fsdp", None),
        P(None, "fsdp", None),
        P(None, "fsdp", None),
        P(None, "fsdp"),
        P(),
        P(),
        P("fsdp", None),
        P("fsdp", None),
        P(None, "fsdp", None),
        P(None, "fsdp", None),
        P(None, "fsdp"),
        P(),
        P(),
    )
    out_specs = (
        P(),
        P(),
        P(),
        P("fsdp", None),
        P("fsdp", None),
        P(None, "fsdp", None),
        P(None, "fsdp", None),
        P(None, "fsdp"),
        P(),
        P(),
        P("fsdp", None),
        P("fsdp", None),
        P(None, "fsdp", None),
        P(None, "fsdp", None),
        P(None, "fsdp"),
        P(),
        P(),
        P("fsdp", None),
        P("fsdp", None),
        P(None, "fsdp", None),
        P(None, "fsdp", None),
        P(None, "fsdp"),
        P(),
        P(),
    )
    return jax.shard_map(body, mesh=mesh, in_specs=in_specs, out_specs=out_specs, check_vma=False)
```

```python
import functools

import jax
import jax.numpy as jnp
from jax import lax
from jax.experimental import pallas as pl
from jax.experimental.pallas import tpu as pltpu
from jax.sharding import PartitionSpec as P

D = 768
HEADS = 12
HD = 64
CLS = 1000
GRID = 7
IMG = 240
IMGS = 8
LAYERS = 2
STEP = 3


NORM_EPS = 1e-06
CLIP_NORM = 0.01
LEARN_RATE = 0.05
VECTOR_RATE = 0.25
BETA_ONE = 0.5
BETA_TWO = 0.5
ADAM_EPS = 1e-08
WEIGHT_DECAY = 0.05
HIGHEST = lax.Precision.HIGHEST

PAIR = 2 * HD
MASKED = -1e30
VMEM_LIMIT = 56 * 1024 * 1024
MESH = pl.DeviceIdType.MESH
LANES = 128
LOW = jnp.bfloat16
ANYWHERE = pl.BlockSpec(memory_space=pl.ANY)
NO_COST = pl.CostEstimate(flops=0, bytes_accessed=0, transcendentals=0)
ROOT = 0.7978845608028654
CUBE = 0.044715
NT = (((1,), (1,)), ((), ()))


def layer_norm(values, gain, shift):
    center = values - jnp.mean(values, -1, keepdims=True)
    spread = jnp.mean(center * center, -1, keepdims=True)
    return center * lax.rsqrt(spread + NORM_EPS) * gain + shift


def rounded(values):
    return lax.optimization_barrier(values.astype(jnp.bfloat16)).astype(jnp.float32)


def matmul(left, right):
    return jnp.dot(left, right, preferred_element_type=jnp.float32)


def padded_rows(flat, multiple):
    extra = -flat.shape[0] % (multiple * LANES)
    return jnp.pad(flat, (0, extra)).reshape(-1, LANES)


def row_layout(seg_row, patch_row):
    row_count = seg_row.shape[0]
    slots = jnp.arange(IMGS, dtype=jnp.int32)
    member = seg_row[:, None] == slots[None, :]
    counts = jnp.sum(member.astype(jnp.int32), 0, dtype=jnp.int32)
    starts = jnp.cumsum(counts, dtype=jnp.int32) - counts
    inside = jnp.any(member, 1)
    offset = jnp.arange(row_count, dtype=jnp.int32) - jnp.sum(
        jnp.where(member, starts[None, :], 0), 1, dtype=jnp.int32
    )
    offset = jnp.where(inside, offset, 0)
    patch_tok = jnp.sum(jnp.where(member, patch_row[None, :], 0), 1, dtype=jnp.int32) + jnp.where(
        inside, 0, IMG
    )
    side = IMG // patch_tok
    nodes = jnp.arange(GRID, dtype=jnp.int32).astype(jnp.float32)

    def hat(coord):
        place = ((2 * coord + 1) * GRID).astype(jnp.float32) / (2 * side).astype(jnp.float32) - 0.5
        place = jnp.clip(place, 0.0, GRID - 1.0)
        return jnp.maximum(1.0 - jnp.abs(place[:, None] - nodes[None, :]), 0.0)

    weights = (hat(offset // side)[:, :, None] * hat(offset % side)[:, None, :]).reshape(
        row_count, GRID * GRID
    )
    return (weights, member.astype(jnp.float32), counts.astype(jnp.float32))


TURNS = (1, 2, 3)


def place():
    slot = lax.axis_index("fsdp")
    return lax.axis_index("dp"), lax.div(slot, 2), lax.rem(slot, 2)


def partner(index, turn):
    if turn == 0:
        return index
    if turn == 1:
        return index + 1 - 2 * lax.rem(index, 2)
    if turn == 2:
        return lax.rem(index + 2, 4)
    return 3 - index


def greet():
    group, level, core = place()
    barrier = pltpu.get_barrier_semaphore()
    peers = [(group, 2 * level + 1 - core)]
    for turn in TURNS:
        peers.append((group, 2 * partner(level, turn) + core))
        peers.append((partner(group, turn), 2 * level + core))
    for peer in peers:
        pl.semaphore_signal(barrier, inc=1, device_id=peer, device_id_type=MESH)
    pl.semaphore_wait(barrier, len(peers))


def quarter_shape(rows, columns):
    if columns % (2 * LANES) == 0:
        return rows // 2, columns // 2
    return rows // 4, columns


def quarter(index, rows, columns):
    high, wide = quarter_shape(rows, columns)
    if wide == columns:
        return pl.ds(pl.multiple_of(index * high, high), high), pl.ds(0, columns)
    return (
        pl.ds(pl.multiple_of(lax.div(index, 2) * high, high), high),
        pl.ds(pl.multiple_of(lax.rem(index, 2) * wide, wide), wide),
    )


def remote(source, target, send, receive, device):
    return pltpu.make_async_remote_copy(
        src_ref=source,
        dst_ref=target,
        send_sem=send,
        recv_sem=receive,
        device_id=device,
        device_id_type=MESH,
    )


GATHER_SEMS = 33


class Gather:
    def __init__(self, shard, out, sems, split):
        self.shard, self.out, self.sems, self.split = shard, out, sems, split
        self.rows, self.columns = shard.shape

    def level_copy(self, turn):
        group, level, core = place()
        block = self.out.at[2 * level + core]
        source = self.shard
        if self.split:
            part = quarter(group, self.rows, self.columns)
            source, block = source.at[part], block.at[part]
        sems = self.sems
        peer = (group, 2 * partner(level, turn) + core)
        return remote(source, block, sems.at[turn], sems.at[3 + turn], peer)

    def group_copy(self, turn, other):
        group, level, core = place()
        part = quarter(group, self.rows, self.columns)
        block = self.out.at[2 * partner(level, turn) + core].at[part]
        index = 3 * (turn - 1) + other - 1
        peer = (partner(group, other), 2 * level + core)
        return remote(block, block, self.sems.at[7 + index], self.sems.at[16 + index], peer)

    def core_copy(self, turn):
        group, level, core = place()
        slot = 2 * partner(level, turn) + core
        source = self.shard if turn == 0 else self.out.at[slot]
        peer = (group, 2 * level + 1 - core)
        return remote(source, self.out.at[slot], self.sems.at[25 + turn], self.sems.at[29 + turn], peer)

    def own_copy(self):
        _, level, core = place()
        return pltpu.make_async_copy(self.shard, self.out.at[2 * level + core], self.sems.at[0])

    def first(self):
        for turn in TURNS:
            self.level_copy(turn).start()
        self.core_copy(0).start()
        self.own_copy().start()

    def second(self):
        for turn in TURNS:
            self.level_copy(turn).wait_recv()
            if self.split:
                for other in TURNS:
                    self.group_copy(turn, other).start()
            else:
                self.core_copy(turn).start()

    def third(self):
        if not self.split:
            return
        for turn in TURNS:
            for other in TURNS:
                self.group_copy(turn, other).wait_recv()
            self.core_copy(turn).start()

    def fourth(self):
        for turn in (0, *TURNS):
            self.core_copy(turn).wait_recv()
        for turn in TURNS:
            self.level_copy(turn).wait_send()
            if self.split:
                for other in TURNS:
                    self.group_copy(turn, other).wait_send()
        for turn in (0, *TURNS):
            self.core_copy(turn).wait_send()
        self.own_copy().wait()


def beside(jobs, plan):
    for step, stages in plan.items():

        @pl.when(pl.program_id(0) == step)
        def _(stages=stages):
            for stage in stages:
                if stage == "greet":
                    greet()
                else:
                    run_stages(jobs, (stage,))


def gather_kernel(*refs, split):
    count = len(split)
    sems = refs[2 * count]
    jobs = [
        Gather(refs[i], refs[count + i], sems.at[i], split[i]) for i in range(count)
    ]
    greet()
    for stage in ("first", "second", "third", "fourth"):
        for job in jobs:
            getattr(job, stage)()


def gather_call(shards, split, collective_id):
    count = len(shards)
    owners = lax.axis_size("fsdp")
    full = pl.pallas_call(
        functools.partial(gather_kernel, split=split),
        in_specs=[ANYWHERE] * count,
        out_specs=[ANYWHERE] * count,
        out_shape=[jax.ShapeDtypeStruct((owners, *s.shape), s.dtype) for s in shards],
        scratch_shapes=[pltpu.SemaphoreType.DMA((count, GATHER_SEMS))],
        cost_estimate=transfer_cost(sum(shard.size for shard in shards) * owners),
        compiler_params=pltpu.CompilerParams(
            collective_id=collective_id, has_side_effects=True, vmem_limit_bytes=VMEM_LIMIT
        ),
        name="gather_weights",
    )(*shards)
    return [f.reshape(owners * f.shape[1], f.shape[2]) for f in full]


REDUCE_SEMS = 48


class Reduce:
    def __init__(self, grad, out, scratch, sems):
        self.grad, self.out, self.sems = grad, out, sems
        self.own, self.got_core, self.got_group, self.part, self.got_level = scratch
        self.rows, self.columns = out.shape
        self.chunk = 16

    def load(self, level):
        _, _, core = place()
        return pltpu.make_async_copy(
            self.grad.at[2 * level + core], self.own.at[level], self.sems.at[level]
        )

    def core_copy(self, target_level):
        group, level, core = place()
        return remote(
            self.grad.at[2 * target_level + 1 - core],
            self.got_core.at[target_level],
            self.sems.at[4 + target_level],
            self.sems.at[8 + target_level],
            (group, 2 * level + 1 - core),
        )

    def group_copy(self, turn, other):
        group, level, core = place()
        target = partner(level, turn)
        peer = partner(group, other)
        part = quarter(peer, self.rows, self.columns)
        index = 3 * turn + other - 1
        return remote(
            self.own.at[target].at[part],
            self.got_group.at[other - 1, target],
            self.sems.at[12 + index],
            self.sems.at[24 + index],
            (peer, 2 * level + core),
        )

    def level_copy(self, turn):
        group, level, core = place()
        target = partner(level, turn)
        return remote(
            self.part.at[target],
            self.got_level.at[turn - 1],
            self.sems.at[35 + turn],
            self.sems.at[38 + turn],
            (group, 2 * target + core),
        )

    def share_copy(self, other):
        group, level, core = place()
        mine = self.out.at[quarter(group, self.rows, self.columns)]
        return remote(
            mine,
            mine,
            self.sems.at[41 + other],
            self.sems.at[44 + other],
            (partner(group, other), 2 * level + core),
        )

    def first(self):
        _, level, _ = place()
        for turn in (*TURNS, 0):
            self.core_copy(partner(level, turn)).start()
            self.load(partner(level, turn)).start()

    def second(self):
        _, level, _ = place()
        for turn in (*TURNS, 0):
            target = partner(level, turn)
            self.load(target).wait()
            self.core_copy(target).wait_recv()

            def add(step, carry):
                rows = pl.ds(pl.multiple_of(step * self.chunk, self.chunk), self.chunk)
                total = self.own[target, rows, :].astype(jnp.float32)
                total = total + self.got_core[target, rows, :].astype(jnp.float32)
                self.own[target, rows, :] = total.astype(self.own.dtype)
                return carry

            lax.fori_loop(0, self.rows // self.chunk, add, 0)
            for other in TURNS:
                self.group_copy(turn, other).start()

    def between(self):
        pass

    def third(self):
        group, level, _ = place()
        high, wide = quarter_shape(self.rows, self.columns)
        row_part, column_part = quarter(group, self.rows, self.columns)
        for turn in (*TURNS, 0):
            target = partner(level, turn)
            for other in TURNS:
                self.group_copy(turn, other).wait_recv()

            def add(step, carry):
                at = pl.multiple_of(step * self.chunk, self.chunk)
                rows = pl.ds(at, self.chunk)
                mine = pl.ds(pl.multiple_of(row_part.start + at, self.chunk), self.chunk)
                total = self.own[target, mine, column_part].astype(jnp.float32)
                for slot in range(3):
                    total = total + self.got_group[slot, target, rows, :].astype(jnp.float32)
                self.part[target, rows, :] = total.astype(self.part.dtype)
                return carry

            lax.fori_loop(0, high // self.chunk, add, 0)
            if turn:
                self.level_copy(turn).start()

    def fourth(self):
        group, level, _ = place()
        high, wide = quarter_shape(self.rows, self.columns)
        row_part, column_part = quarter(group, self.rows, self.columns)
        for turn in TURNS:
            self.level_copy(turn).wait_recv()

        def add(step, carry):
            at = pl.multiple_of(step * self.chunk, self.chunk)
            rows = pl.ds(at, self.chunk)
            mine = pl.ds(pl.multiple_of(row_part.start + at, self.chunk), self.chunk)
            total = self.part[level, rows, :].astype(jnp.float32)
            for slot in range(3):
                total = total + self.got_level[slot, rows, :].astype(jnp.float32)
            self.out[mine, column_part] = total.astype(self.out.dtype)
            return carry

        lax.fori_loop(0, high // self.chunk, add, 0)
        for other in TURNS:
            self.share_copy(other).start()

    def fifth(self):
        for other in TURNS:
            self.share_copy(other).wait_recv()

    def sixth(self):
        _, level, _ = place()
        for turn in (*TURNS, 0):
            self.core_copy(partner(level, turn)).wait_send()
            for other in TURNS:
                self.group_copy(turn, other).wait_send()
            if turn:
                self.level_copy(turn).wait_send()
                self.share_copy(turn).wait_send()


WHOLE_SEMS = 40


def add_rows(target, row, columns, source, count, wide):
    chunk = 16 if wide > 1536 else 48

    def add(step, carry):
        at = pl.multiple_of(step * chunk, chunk)
        mine = pl.ds(pl.multiple_of(row + at, 16), chunk)
        total = target[mine, columns].astype(jnp.float32)
        total = total + source[pl.ds(at, chunk), :].astype(jnp.float32)
        target[mine, columns] = total.astype(target.dtype)
        return carry

    lax.fori_loop(0, count // chunk, add, 0)


class Whole:
    FIRST_X = (1, 0)

    def __init__(self, grad, out, scratch, sems):
        self.grad, self.out, self.sems = grad, out, sems
        self.own, self.got_core, self.got_x, self.got_y, self.got_last, self.part, self.got_level = scratch
        self.rows, self.columns = out.shape
        self.high, self.wide = self.rows // 2, self.columns // 2

    def row_half(self, index):
        return pl.ds(pl.multiple_of(lax.div(index, 2) * self.high, self.high), self.high)

    def column_half(self, index):
        return pl.ds(pl.multiple_of(lax.rem(index, 2) * self.wide, self.wide), self.wide)

    def load(self, level):
        _, _, core = place()
        return pltpu.make_async_copy(
            self.grad.at[2 * level + core], self.own.at[level], self.sems.at[level]
        )

    def core_copy(self, target_level):
        group, level, core = place()
        return remote(
            self.grad.at[2 * target_level + 1 - core],
            self.got_core.at[target_level],
            self.sems.at[4 + target_level],
            self.sems.at[8 + target_level],
            (group, 2 * level + 1 - core),
        )

    def step_copy(self, turn):
        group, level, core = place()
        block = self.own.at[partner(level, turn)]
        if turn in self.FIRST_X:
            peer = partner(group, 1)
            source = block.at[:, self.column_half(peer)]
            target = self.got_x.at[self.FIRST_X.index(turn)]
        else:
            peer = partner(group, 2)
            source = block.at[self.row_half(peer), :]
            target = self.got_y.at[turn - 2]
        return remote(
            source, target, self.sems.at[12 + turn], self.sems.at[16 + turn], (peer, 2 * level + core)
        )

    def last_copy(self, turn):
        group, level, core = place()
        block = self.own.at[partner(level, turn)]
        peer = partner(group, 2 if turn in self.FIRST_X else 1)
        rows = self.row_half(peer)
        columns = self.column_half(peer)
        return remote(
            block.at[rows, columns],
            self.got_last.at[turn],
            self.sems.at[20 + turn],
            self.sems.at[24 + turn],
            (peer, 2 * level + core),
        )

    def level_copy(self, turn):
        group, level, core = place()
        target = partner(level, turn)
        return remote(
            self.part.at[target],
            self.got_level.at[turn - 1],
            self.sems.at[27 + turn],
            self.sems.at[30 + turn],
            (group, 2 * target + core),
        )

    def share_copy(self, other):
        group, level, core = place()
        mine = self.out.at[self.row_half(group), self.column_half(group)]
        return remote(
            mine,
            mine,
            self.sems.at[33 + other],
            self.sems.at[36 + other],
            (partner(group, other), 2 * level + core),
        )

    def first(self):
        _, level, _ = place()
        for turn in (*TURNS, 0):
            self.core_copy(partner(level, turn)).start()
            self.load(partner(level, turn)).start()

    def second(self):
        _, level, _ = place()
        for turn in (*TURNS, 0):
            target = partner(level, turn)
            self.load(target).wait()
            self.core_copy(target).wait_recv()
            add_rows(
                self.own.at[target], 0, slice(None), self.got_core.at[target], self.rows, self.columns
            )
            self.step_copy(turn).start()

    def between(self):
        group, level, _ = place()
        for turn in (*TURNS, 0):
            block = self.own.at[partner(level, turn)]
            self.step_copy(turn).wait_recv()
            if turn in self.FIRST_X:
                source = self.got_x.at[self.FIRST_X.index(turn)]
                add_rows(block, 0, self.column_half(group), source, self.rows, self.wide)
            else:
                source = self.got_y.at[turn - 2]
                start = lax.div(group, 2) * self.high
                add_rows(block, start, slice(None), source, self.high, self.columns)
            self.last_copy(turn).start()

    def third(self):
        group, level, _ = place()
        start = lax.div(group, 2) * self.high
        columns = self.column_half(group)
        chunk = 16 if self.wide > 1536 else 48
        for turn in (*TURNS, 0):
            target = partner(level, turn)
            self.last_copy(turn).wait_recv()

            def add(step, carry):
                at = pl.multiple_of(step * chunk, chunk)
                rows = pl.ds(at, chunk)
                mine = pl.ds(pl.multiple_of(start + at, 16), chunk)
                total = self.own[target, mine, columns].astype(jnp.float32)
                total = total + self.got_last[turn, rows, :].astype(jnp.float32)
                self.part[target, rows, :] = total.astype(self.part.dtype)
                return carry

            lax.fori_loop(0, self.high // chunk, add, 0)
            if turn:
                self.level_copy(turn).start()

    def fourth(self):
        group, level, _ = place()
        start = lax.div(group, 2) * self.high
        columns = self.column_half(group)
        chunk = 16 if self.wide > 1536 else 48
        for turn in TURNS:
            self.level_copy(turn).wait_recv()

        def add(step, carry):
            at = pl.multiple_of(step * chunk, chunk)
            rows = pl.ds(at, chunk)
            mine = pl.ds(pl.multiple_of(start + at, 16), chunk)
            total = self.part[level, rows, :].astype(jnp.float32)
            for slot in range(3):
                total = total + self.got_level[slot, rows, :].astype(jnp.float32)
            self.out[mine, columns] = total.astype(self.out.dtype)
            return carry

        lax.fori_loop(0, self.high // chunk, add, 0)
        for other in TURNS:
            self.share_copy(other).start()

    def fifth(self):
        for other in TURNS:
            self.share_copy(other).wait_recv()

    def sixth(self):
        _, level, _ = place()
        for turn in (*TURNS, 0):
            self.core_copy(partner(level, turn)).wait_send()
            self.step_copy(turn).wait_send()
            self.last_copy(turn).wait_send()
            if turn:
                self.level_copy(turn).wait_send()
                self.share_copy(turn).wait_send()


GROUP_SEMS = 13


class GroupReduce:
    def __init__(self, share, out, scratch, sems):
        self.share, self.out, self.sems = share, out, sems
        self.own, self.got = scratch
        self.rows, self.columns = out.shape
        self.chunk = 16

    def load(self):
        return pltpu.make_async_copy(self.share, self.own, self.sems.at[0])

    def group_copy(self, other):
        group, level, core = place()
        peer = partner(group, other)
        return remote(
            self.own.at[quarter(peer, self.rows, self.columns)],
            self.got.at[other - 1],
            self.sems.at[other],
            self.sems.at[3 + other],
            (peer, 2 * level + core),
        )

    def share_copy(self, other):
        group, level, core = place()
        mine = self.out.at[quarter(group, self.rows, self.columns)]
        return remote(
            mine,
            mine,
            self.sems.at[6 + other],
            self.sems.at[9 + other],
            (partner(group, other), 2 * level + core),
        )

    def first(self):
        self.load().start()

    def second(self):
        self.load().wait()
        for other in TURNS:
            self.group_copy(other).start()

    def between(self):
        pass

    def third(self):
        group, _, _ = place()
        high, wide = quarter_shape(self.rows, self.columns)
        row_part, column_part = quarter(group, self.rows, self.columns)
        for other in TURNS:
            self.group_copy(other).wait_recv()

        def add(step, carry):
            at = pl.multiple_of(step * self.chunk, self.chunk)
            rows = pl.ds(at, self.chunk)
            mine = pl.ds(pl.multiple_of(row_part.start + at, self.chunk), self.chunk)
            total = self.own[mine, column_part].astype(jnp.float32)
            for slot in range(3):
                total = total + self.got[slot, rows, :].astype(jnp.float32)
            self.out[mine, column_part] = total.astype(self.out.dtype)
            return carry

        lax.fori_loop(0, high // self.chunk, add, 0)
        for other in TURNS:
            self.share_copy(other).start()

    def fourth(self):
        pass

    def fifth(self):
        for other in TURNS:
            self.share_copy(other).wait_recv()

    def sixth(self):
        for other in TURNS:
            self.group_copy(other).wait_send()
            self.share_copy(other).wait_send()


class Spread:
    def __init__(self, full, sems):
        self.full, self.sems = full, sems

    def level_copy(self, turn):
        group, level, core = place()
        block = self.full.at[2 * level + core]
        peer = (group, 2 * partner(level, turn) + core)
        return remote(block, block, self.sems.at[turn - 1], self.sems.at[2 + turn], peer)

    def core_copy(self, turn):
        group, level, core = place()
        block = self.full.at[2 * partner(level, turn) + core]
        peer = (group, 2 * level + 1 - core)
        return remote(block, block, self.sems.at[6 + turn], self.sems.at[10 + turn], peer)

    def run(self):
        for turn in TURNS:
            self.level_copy(turn).start()
        self.core_copy(0).start()
        for turn in TURNS:
            self.level_copy(turn).wait_recv()
            self.core_copy(turn).start()
        for turn in (0, *TURNS):
            self.core_copy(turn).wait_recv()
        for turn in (0, *TURNS):
            self.core_copy(turn).wait_send()
            if turn:
                self.level_copy(turn).wait_send()


def squares_in(out):
    def add(step, total):
        piece = out[pl.ds(pl.multiple_of(step * 16, 16), 16), :].astype(jnp.float32)
        piece = piece * piece
        for lane in range(0, out.shape[1], LANES):
            total = total + piece[:, lane : lane + LANES]
        return total

    total = lax.fori_loop(0, out.shape[0] // 16, add, jnp.zeros((16, LANES), jnp.float32))
    return jnp.sum(total, 0, keepdims=True)


def run_stages(jobs, stages):
    for stage in stages:
        for job in jobs:
            getattr(job, stage)()


STAGES = ("first", "second", "between", "third", "fourth", "fifth", "sixth")


def whole_scratch(grad):
    _, rows, columns = grad.shape
    high, wide = quarter_shape(rows, columns)
    shapes = ((4, rows, columns), (4, rows, columns), (3, 4, high, wide), (4, high, wide))
    return [pltpu.VMEM(shape, grad.dtype) for shape in (*shapes, (3, high, wide))]


def stepped_scratch(grad):
    _, rows, columns = grad.shape
    high, wide = rows // 2, columns // 2
    shapes = (
        (4, rows, columns),
        (4, rows, columns),
        (2, rows, wide),
        (2, high, columns),
        (4, high, wide),
        (4, high, wide),
        (3, high, wide),
    )
    return [pltpu.VMEM(shape, grad.dtype) for shape in shapes]


def share_scratch(share):
    return [
        pltpu.VMEM(share.shape, share.dtype),
        pltpu.VMEM((3, *quarter_shape(*share.shape)), share.dtype),
    ]


def reduce_kernel(*refs, whole, partly):
    count = whole + partly
    grads, outs, refs = refs[:count], refs[count : 2 * count], refs[2 * count :]
    sems, group_sems, refs = refs[0], refs[1], refs[2:]
    jobs = [
        Whole(grads[i], outs[i], refs[7 * i : 7 * i + 7], sems.at[i]) for i in range(whole)
    ]
    refs = refs[7 * whole :]
    shares = [
        GroupReduce(grads[whole + i], outs[whole + i], refs[2 * i : 2 * i + 2], group_sems.at[i])
        for i in range(partly)
    ]
    greet()
    run_stages([*jobs, *shares], STAGES[:1])
    run_stages(shares, STAGES[1:2])
    run_stages(jobs, STAGES[1:3])
    run_stages(shares, STAGES[3:4])
    run_stages(jobs, STAGES[3:5])
    run_stages([*shares, *jobs], STAGES[5:])


def transfer_cost(size):
    return pl.CostEstimate(flops=4000 * size, bytes_accessed=2 * size, transcendentals=0)


def reduce_call(grads, shares, collective_id):
    in_vmem = pl.BlockSpec(memory_space=pltpu.VMEM)
    whole, partly = len(grads), len(shares)
    scratch = [
        pltpu.SemaphoreType.DMA((whole, WHOLE_SEMS)),
        pltpu.SemaphoreType.DMA((partly, GROUP_SEMS)),
    ]
    for grad in grads:
        scratch.extend(stepped_scratch(grad))
    for share in shares:
        scratch.extend(share_scratch(share))
    out_shape = [jax.ShapeDtypeStruct(g.shape[1:], g.dtype) for g in grads]
    out_shape += [jax.ShapeDtypeStruct(s.shape, s.dtype) for s in shares]
    return pl.pallas_call(
        functools.partial(reduce_kernel, whole=whole, partly=partly),
        in_specs=[ANYWHERE] * (whole + partly),
        out_specs=[in_vmem] * (whole + partly),
        out_shape=out_shape,
        scratch_shapes=scratch,
        compiler_params=pltpu.CompilerParams(
            collective_id=collective_id, has_side_effects=True, vmem_limit_bytes=VMEM_LIMIT
        ),
        cost_estimate=NO_COST,
        name="reduce_gradients",
    )(*grads, *shares)


def finish_kernel(*refs, done, partly):
    finished, refs = refs[:done], refs[done:]
    shares, small, refs = refs[:partly], refs[partly], refs[partly + 1 :]
    outs, small_out, full, refs = refs[:partly], refs[partly], refs[partly + 1], refs[partly + 2 :]
    sems, group_sems, spread_sems, refs = refs[0], refs[1], refs[2], refs[3:]
    job = Reduce(small, small_out, refs[:5], sems)
    refs = refs[5:]
    jobs = [
        GroupReduce(shares[i], outs[i], refs[2 * i : 2 * i + 2], group_sems.at[i])
        for i in range(partly)
    ]
    greet()
    run_stages([job, *jobs], STAGES[:3])
    total = sum(squares_in(out) for out in finished)
    run_stages([*jobs, job], STAGES[3:6])
    total = total + sum(squares_in(out) for out in outs)
    _, level, core = place()
    mine = 2 * level + core
    last = small_out.shape[0] - 1
    full[mine] = small_out[...]
    full[mine, last : last + 1, :] = total
    Spread(full, spread_sems).run()
    run_stages([job, *jobs], STAGES[6:])


def finish_call(finished, shares, small, collective_id):
    done, partly = len(finished), len(shares)
    in_vmem = pl.BlockSpec(memory_space=pltpu.VMEM)
    scratch = [
        pltpu.SemaphoreType.DMA((REDUCE_SEMS,)),
        pltpu.SemaphoreType.DMA((partly, GROUP_SEMS)),
        pltpu.SemaphoreType.DMA((14,)),
        *whole_scratch(small),
    ]
    for share in shares:
        scratch.extend(share_scratch(share))
    out_shape = [jax.ShapeDtypeStruct(s.shape, s.dtype) for s in shares]
    out_shape.append(jax.ShapeDtypeStruct(small.shape[1:], small.dtype))
    out_shape.append(jax.ShapeDtypeStruct(small.shape, small.dtype))
    return pl.pallas_call(
        functools.partial(finish_kernel, done=done, partly=partly),
        in_specs=[in_vmem] * done + [ANYWHERE] * (partly + 1),
        out_specs=[in_vmem] * len(out_shape),
        out_shape=out_shape,
        scratch_shapes=scratch,
        compiler_params=pltpu.CompilerParams(
            collective_id=collective_id, has_side_effects=True, vmem_limit_bytes=VMEM_LIMIT
        ),
        name="finish_gradients",
    )(*finished, *shares, small)


def with_kernels():
    return lax.axis_size("dp") == 4 and lax.axis_size("fsdp") == 8


def gather_all(shards, split, collective_id):
    if with_kernels():
        return gather_call(shards, split, collective_id)
    return [lax.all_gather(shard, "fsdp", axis=0, tiled=True) for shard in shards]


def reduce_all(grads, shares, collective_id):
    if with_kernels():
        return reduce_call(grads, shares, collective_id)
    return [lax.psum(scatter(grad), "dp") for grad in grads] + sum_shares(shares)


def sum_shares(shares):
    return [lax.psum(share, "dp") for share in shares]


def finish_all(finished, shares, small, collective_id):
    if with_kernels():
        return finish_call(finished, shares, small, collective_id)
    outs = [lax.psum(share, "dp") for share in shares]
    own = lax.psum(scatter(small), "dp")
    total = sum(jnp.sum(jnp.square(out.astype(jnp.float32))) for out in (*finished, *outs))
    row = jnp.full((1, LANES), 1.0 / LANES, jnp.float32) * total
    return [*outs, own, lax.all_gather(own.at[-1:].set(row), "fsdp", axis=0)]


def take(items, *counts):
    cut = []
    for count in counts:
        cut.append(items[:count])
        items = items[count:]
    return cut


def scatter(grad):
    return lax.psum_scatter(grad, "fsdp", scatter_dimension=0)


def by_owner(grad, low=jnp.bfloat16):
    owners = lax.axis_size("fsdp")
    return grad.astype(low).reshape(owners, grad.shape[0] // owners, grad.shape[1])


def attention_forward_kernel(*refs, block, fetched):
    q_ref, k_ref, v_ref, seg_col_ref, seg_row_ref = refs[:5]
    shards, refs = refs[5 : 5 + fetched], refs[5 + fetched :]
    out_ref, expo_ref, inv_ref = refs[:3]
    fulls, refs = refs[3 : 3 + fetched], refs[3 + fetched :]
    jobs = [Gather(shards[i], fulls[i], refs[0].at[i], True) for i in range(fetched)]
    if jobs:
        beside(jobs, {0: ("greet", "first"), 1: ("second",), 3: ("third",)})
    rows = q_ref.shape[0]
    lower = lax.broadcasted_iota(jnp.int32, (block, PAIR), 1) < HD
    keys = k_ref[...]
    values = jnp.concatenate([v_ref[...], jnp.ones((rows, PAIR), v_ref.dtype)], 1)
    seg_row = seg_row_ref[...]
    tasks = [(step, head) for step in range(rows // block) for head in range(2)]

    def scores_of(step, head):
        query = q_ref[step * block : (step + 1) * block, :] * jnp.bfloat16(HD**-0.5)
        keep = lower if head == 0 else jnp.logical_not(lower)
        return mul_nt(jnp.where(keep, query, jnp.bfloat16(0)), keys)

    scores = scores_of(*tasks[0])
    outs = []
    for index, (step, head) in enumerate(tasks):
        following = scores_of(*tasks[index + 1]) if index + 1 < len(tasks) else None
        at = slice(step * block, (step + 1) * block)
        scores = jnp.where(seg_col_ref[at, :] == seg_row, scores, MASKED)
        highest = jnp.max(scores, -1, keepdims=True)
        low = jnp.exp(scores - highest).astype(jnp.bfloat16)
        expo_ref[head, at, :] = low
        outs.append(mul(low, values))
        if head:
            inverse = 1.0 / jnp.where(lower, outs[0][:, PAIR:], outs[1][:, PAIR:])
            sums = jnp.where(lower, outs[0][:, :PAIR], outs[1][:, :PAIR])
            out_ref[at, :] = (sums * inverse).astype(jnp.bfloat16)
            inv_ref[at, :] = inverse
            outs = []
        scores = following
    if jobs:
        beside(jobs, {pl.num_programs(0) - 1: ("fourth",)})


def attention_forward(qkv_rows, segment, shards, collective_id):
    gathered = []
    if not with_kernels():
        gathered, shards = gather_all(shards, (True,) * len(shards), collective_id), []
    rows = qkv_rows.shape[0]
    fetched = len(shards)
    owners = lax.axis_size("fsdp")
    transfer = {}
    if fetched:
        transfer = {"collective_id": collective_id, "has_side_effects": True}
    pairs = HEADS // 2
    block = min(256, rows)
    wide = lambda base: pl.BlockSpec((rows, PAIR), lambda j, base=base: (0, base + j))
    attended, expo, inverse, *full = pl.pallas_call(
        functools.partial(attention_forward_kernel, block=block, fetched=fetched),
        grid=(pairs,),
        in_specs=[
            wide(0),
            wide(pairs),
            wide(2 * pairs),
            pl.BlockSpec((rows, 1), lambda j: (0, 0)),
            pl.BlockSpec((1, rows), lambda j: (0, 0)),
            *[ANYWHERE] * fetched,
        ],
        out_specs=[
            wide(0),
            pl.BlockSpec((2, rows, rows), lambda j: (j, 0, 0)),
            wide(0),
            *[ANYWHERE] * fetched,
        ],
        out_shape=[
            jax.ShapeDtypeStruct((rows, D), jnp.bfloat16),
            jax.ShapeDtypeStruct((HEADS, rows, rows), jnp.bfloat16),
            jax.ShapeDtypeStruct((rows, D), jnp.float32),
            *[jax.ShapeDtypeStruct((owners, *s.shape), s.dtype) for s in shards],
        ],
        scratch_shapes=[pltpu.SemaphoreType.DMA((fetched, GATHER_SEMS))] * (fetched > 0),
        compiler_params=pltpu.CompilerParams(vmem_limit_bytes=VMEM_LIMIT, **transfer),
        cost_estimate=pl.CostEstimate(
            flops=4 * HEADS * rows * rows * HD * 4,
            bytes_accessed=2 * HEADS * rows * rows + 12 * rows * D,
            transcendentals=HEADS * rows * rows,
        ),
        name="attention_forward",
    )(qkv_rows, qkv_rows, qkv_rows, segment[:, None], segment[None, :], *shards)
    gathered += [f.reshape(owners * f.shape[1], f.shape[2]) for f in full]
    return attended, expo, inverse, gathered


def attention_backward_kernel(*refs, block, reduced):
    q_ref, k_ref, v_ref, expo_ref, inv_ref, out_ref, grad_ref = refs[:7]
    sources, refs = refs[7 : 7 + reduced], refs[7 + reduced :]
    dqkv_ref, sums, refs = refs[0], refs[1 : 1 + reduced], refs[1 + reduced :]
    jobs = [
        GroupReduce(sources[i], refs[3 * i + 1], refs[3 * i + 2 : 3 * i + 4], refs[0].at[i])
        for i in range(reduced)
    ]
    if jobs:
        beside(jobs, {0: ("greet", "first", "second"), 3: ("third",)})
    rows = q_ref.shape[0]
    pair = pl.program_id(0)
    lower = lax.broadcasted_iota(jnp.int32, (block, PAIR), 1) < HD
    keys = k_ref[...]
    values = v_ref[...]
    scale = HD**-0.5
    scaled_grad = (grad_ref[...].astype(jnp.float32) * inv_ref[...]).astype(jnp.bfloat16)
    query = q_ref[...]
    query_t = query.T
    grad_t = scaled_grad.T
    product = scaled_grad.astype(jnp.float32) * out_ref[...].astype(jnp.float32)
    key_t = [None, None]
    value_t = [None, None]
    tasks = [(step, head) for step in range(rows // block) for head in range(2)]

    def probs_grad_of(step, head):
        keep = lower if head == 0 else jnp.logical_not(lower)
        mine = scaled_grad[step * block : (step + 1) * block]
        return mul_nt(jnp.where(keep, mine, jnp.bfloat16(0)), values)

    probs_grad = probs_grad_of(*tasks[0])
    query_parts = []
    for index, (step, head) in enumerate(tasks):
        following = probs_grad_of(*tasks[index + 1]) if index + 1 < len(tasks) else None
        at = slice(step * block, (step + 1) * block)
        lanes = slice(head * HD, (head + 1) * HD)
        keep = lower if head == 0 else jnp.logical_not(lower)
        inner = jnp.sum(jnp.where(keep, product[at], 0.0), -1, keepdims=True)
        low = expo_ref[head, at, :]
        value_part = mul(grad_t[lanes, at], low)
        scores_grad = (low.astype(jnp.float32) * (probs_grad - inner)).astype(jnp.bfloat16)
        query_parts.append(mul(scores_grad, keys))
        key_part = mul(query_t[lanes, at], scores_grad)
        key_t[head] = key_part if step == 0 else key_t[head] + key_part
        value_t[head] = value_part if step == 0 else value_t[head] + value_part
        if head:
            query_grad = jnp.where(lower, query_parts[0], query_parts[1]) * scale
            dqkv_ref[at, pl.ds(pl.multiple_of(pair * PAIR, PAIR), PAIR)] = query_grad.astype(
                jnp.bfloat16
            )
            query_parts = []
        probs_grad = following
    key_grad = (jnp.concatenate(key_t, 0) * scale).T
    value_grad = jnp.concatenate(value_t, 0).T
    dqkv_ref[:, pl.ds(pl.multiple_of(D + pair * PAIR, PAIR), PAIR)] = key_grad.astype(jnp.bfloat16)
    dqkv_ref[:, pl.ds(pl.multiple_of(2 * D + pair * PAIR, PAIR), PAIR)] = value_grad.astype(jnp.bfloat16)
    if jobs:
        beside(jobs, {pl.num_programs(0) - 1: STAGES[5:]})

        @pl.when(pair == pl.num_programs(0) - 1)
        def _():
            for job, total in zip(jobs, sums):
                total[...] = job.out[...]


def attention_backward(qkv_rows, expo, inverse, attended, attended_grad, shares, collective_id):
    plain = []
    if not with_kernels():
        plain, shares = sum_shares(shares), []
    reduced = len(shares)
    transfer, scratch = {}, []
    if reduced:
        transfer = {"collective_id": collective_id, "has_side_effects": True}
        scratch.append(pltpu.SemaphoreType.DMA((reduced, GROUP_SEMS)))
    for share in shares:
        scratch.append(pltpu.VMEM(share.shape, share.dtype))
        scratch.extend(share_scratch(share))
    rows = qkv_rows.shape[0]
    pairs = HEADS // 2
    block = min(256, rows)
    wide = lambda base: pl.BlockSpec((rows, PAIR), lambda j, base=base: (0, base + j))
    qkv_grad, *sums = pl.pallas_call(
        functools.partial(attention_backward_kernel, block=block, reduced=reduced),
        grid=(pairs,),
        in_specs=[
            wide(0),
            wide(pairs),
            wide(2 * pairs),
            pl.BlockSpec((2, rows, rows), lambda j: (j, 0, 0)),
            wide(0),
            wide(0),
            wide(0),
            *[ANYWHERE] * reduced,
        ],
        out_specs=[fixed(rows, 3 * D), *[fixed(*s.shape) for s in shares]],
        out_shape=[
            jax.ShapeDtypeStruct((rows, 3 * D), jnp.bfloat16),
            *[jax.ShapeDtypeStruct(s.shape, s.dtype) for s in shares],
        ],
        scratch_shapes=scratch,
        compiler_params=pltpu.CompilerParams(vmem_limit_bytes=VMEM_LIMIT, **transfer),
        cost_estimate=NO_COST,
        name="attention_backward",
    )(qkv_rows, qkv_rows, qkv_rows, expo, inverse, attended, attended_grad, *shares)
    return qkv_grad, plain + sums


def mul(left, right):
    return jnp.dot(left, right, preferred_element_type=jnp.float32)


def mul_nt(left, right):
    return lax.dot_general(left, right, NT, preferred_element_type=jnp.float32)


def normalized(values):
    center = values - jnp.mean(values, -1, keepdims=True)
    inverse = lax.rsqrt(jnp.mean(center * center, -1, keepdims=True) + NORM_EPS)
    return center * inverse, inverse


def norm_backward(grad, values, gain):
    unit, inverse = normalized(values)
    inner = grad * gain
    mean_inner = jnp.mean(inner, -1, keepdims=True)
    mean_cross = jnp.mean(inner * unit, -1, keepdims=True)
    value_grad = inverse * (inner - mean_inner - unit * mean_cross)
    return value_grad, column_sum(grad * unit), column_sum(grad)


def column_sum(rows):
    return jnp.sum(rows.astype(jnp.float32), 0, keepdims=True)


def at_first(action):
    pl.when(pl.program_id(0) == 0)(action)


def accumulate(out_ref, parts):
    value = jnp.concatenate(parts, 1)

    @pl.when(pl.program_id(0) == 0)
    def _():
        out_ref[...] = value

    @pl.when(pl.program_id(0) > 0)
    def _():
        out_ref[...] += value


def rows_of(block, columns):
    return pl.BlockSpec((block, columns), lambda i: (i, 0))


def fixed(*shape):
    return pl.BlockSpec(shape, lambda i: (0,) * len(shape))


def loads(sources, targets, sems):
    return [
        pltpu.make_async_copy(source, target, sems.at[index])
        for index, (source, target) in enumerate(zip(sources, targets))
    ]


def shape_of(*shape, dtype=jnp.float32):
    return jax.ShapeDtypeStruct(shape, dtype)


def block_call(body, grid, in_specs, out_specs, out_shape, scratch, flops, size, name, early=False):
    return pl.pallas_call(
        body,
        grid=(grid,),
        in_specs=in_specs,
        out_specs=out_specs,
        out_shape=out_shape,
        scratch_shapes=scratch,
        compiler_params=pltpu.CompilerParams(vmem_limit_bytes=VMEM_LIMIT),
        cost_estimate=NO_COST if early else pl.CostEstimate(flops=flops, bytes_accessed=size, transcendentals=0),
        name=name,
    )


def embed_kernel(pixel_ref, weight_ref, pos_ref, table_ref, bias_ref, out_ref):
    position = jnp.dot(
        pos_ref[...], table_ref[...], precision=HIGHEST, preferred_element_type=jnp.float32
    )
    out_ref[...] = mul(pixel_ref[...], weight_ref[...]) + bias_ref[...] + position


def embed(pixels, weight, pos_weights, table, bias):
    rows, depth = pixels.shape
    block = 256
    nodes = pos_weights.shape[1]
    return block_call(
        embed_kernel,
        rows // block,
        [rows_of(block, depth), fixed(depth, D), rows_of(block, nodes), fixed(nodes, D), fixed(1, D)],
        rows_of(block, D),
        shape_of(rows, D),
        [],
        2 * rows * depth * D,
        2 * rows * depth + 2 * depth * D + 4 * rows * D,
        "embed",
    )(pixels, weight, pos_weights, table, bias)


def qkv_kernel(stream_ref, weight_ref, vector_ref, normed_ref, qkv_ref):
    unit, _ = normalized(stream_ref[...])
    normed = (unit * vector_ref[:, :D] + vector_ref[:, D : 2 * D]).astype(jnp.bfloat16)
    normed_ref[...] = normed
    bias = vector_ref[:, 4 * D : 7 * D]
    qkv_ref[...] = (mul(normed, weight_ref[...]) + bias).astype(jnp.bfloat16)


def qkv_forward(stream, weight, vector):
    rows = stream.shape[0]
    block = 256
    low = jnp.bfloat16
    return block_call(
        qkv_kernel,
        rows // block,
        [rows_of(block, D), fixed(D, 3 * D), fixed(1, vector.shape[1])],
        [rows_of(block, D), rows_of(block, 3 * D)],
        [shape_of(rows, D, dtype=low), shape_of(rows, 3 * D, dtype=low)],
        [],
        6 * rows * D * D,
        14 * rows * D + 6 * D * D,
        "qkv_forward",
    )(stream, weight, vector)


def mlp_kernel(
    stream_ref, attended_ref, up_full, proj_out, vector_ref,
    residual_ref, normed_ref, active_ref, slope_ref, out_ref,
    mix_ref, up_ref, down_ref, sems,
):
    width = up_ref.shape[1]
    copies = loads(
        (proj_out.at[pl.ds(0, D)], up_full, proj_out.at[pl.ds(D, width)]),
        (mix_ref, up_ref, down_ref),
        sems,
    )

    @at_first
    def _():
        for copy in copies:
            copy.start()
        copies[0].wait()

    residual = stream_ref[...] + mul(attended_ref[...], mix_ref[...]) + vector_ref[:, 7 * D : 8 * D]
    residual_ref[...] = residual
    unit, _ = normalized(residual)
    normed = (unit * vector_ref[:, 2 * D : 3 * D] + vector_ref[:, 3 * D : 4 * D]).astype(jnp.bfloat16)
    normed_ref[...] = normed
    at_first(copies[1].wait)
    part = 512

    def hidden_of(base):
        bias = vector_ref[:, 9 * D + base : 9 * D + base + part]
        return mul(normed, up_ref[:, base : base + part]) + bias

    hidden = hidden_of(0)
    for base in range(0, width, part):
        following = hidden_of(base + part) if base + part < width else None
        columns = slice(base, base + part)
        square = hidden * hidden
        half = 0.5 + 0.5 * jnp.tanh(hidden * (ROOT + (ROOT * CUBE) * square))
        active = hidden * half
        active_ref[:, columns] = active.astype(jnp.bfloat16)
        rise = (2.0 * ROOT) + (6.0 * ROOT * CUBE) * square
        slope_ref[:, columns] = (half + active * (1.0 - half) * rise).astype(jnp.bfloat16)
        hidden = following
    at_first(copies[2].wait)
    out_ref[...] = residual + mul(active_ref[...], down_ref[...]) + vector_ref[:, 8 * D : 9 * D]


def mlp_forward(stream, attended, up, proj_out, vector):
    rows = stream.shape[0]
    width = up.shape[1]
    block = 256
    low = jnp.bfloat16
    return block_call(
        mlp_kernel,
        rows // block,
        [rows_of(block, D), rows_of(block, D), ANYWHERE, ANYWHERE, fixed(1, vector.shape[1])],
        [rows_of(block, D), rows_of(block, D), rows_of(block, width), rows_of(block, width), rows_of(block, D)],
        [
            shape_of(rows, D),
            shape_of(rows, D, dtype=low),
            shape_of(rows, width, dtype=low),
            shape_of(rows, width, dtype=low),
            shape_of(rows, D),
        ],
        [
            pltpu.VMEM((D, D), low),
            pltpu.VMEM((D, width), low),
            pltpu.VMEM((width, D), low),
            pltpu.SemaphoreType.DMA((3,)),
        ],
        2 * rows * D * (D + 2 * width),
        rows * (16 * D + 4 * width) + 2 * D * (D + 2 * width),
        "mlp_forward",
    )(stream, attended, up, proj_out, vector)


def mlp_back_kernel(
    grad_ref, slope_ref, residual_ref, up_full, proj_out, vector_ref,
    low_ref, hidden_ref, out_ref, out_low_ref, attended_ref, sums_ref,
    mix_ref, up_ref, down_ref, sems,
):
    width = up_ref.shape[1]
    copies = loads(
        (proj_out.at[pl.ds(D, width)], up_full, proj_out.at[pl.ds(0, D)]),
        (down_ref, up_ref, mix_ref),
        sems,
    )

    @at_first
    def _():
        for copy in copies:
            copy.start()
        copies[0].wait()

    grad = grad_ref[...]
    grad_low = grad.astype(jnp.bfloat16)
    low_ref[...] = grad_low
    part = 512
    hidden_sums = []
    active_grad = mul_nt(grad_low, down_ref[:part, :])
    for base in range(0, width, part):
        following = None
        if base + part < width:
            following = mul_nt(grad_low, down_ref[base + part : base + 2 * part, :])
        columns = slice(base, base + part)
        hidden_grad = (active_grad * slope_ref[:, columns].astype(jnp.float32)).astype(jnp.bfloat16)
        hidden_ref[:, columns] = hidden_grad
        hidden_sums.append(column_sum(hidden_grad))
        active_grad = following
    at_first(copies[1].wait)
    second_grad = mul_nt(hidden_ref[...], up_ref[...])
    value_grad, gain_grad, shift_grad = norm_backward(
        second_grad, residual_ref[...], vector_ref[:, 2 * D : 3 * D]
    )
    total = value_grad + grad
    out_ref[...] = total
    total_low = total.astype(jnp.bfloat16)
    out_low_ref[...] = total_low
    at_first(copies[2].wait)
    attended_ref[...] = mul_nt(total_low, mix_ref[...]).astype(jnp.bfloat16)
    accumulate(
        sums_ref,
        [gain_grad, shift_grad, column_sum(total_low), column_sum(grad_low), *hidden_sums],
    )


def mlp_backward(grad, slope, residual, up, proj_out, vector):
    rows = grad.shape[0]
    width = up.shape[1]
    block = 256
    low = jnp.bfloat16
    narrow = rows_of(block, D)
    return block_call(
        mlp_back_kernel,
        rows // block,
        [narrow, rows_of(block, width), narrow, ANYWHERE, ANYWHERE, fixed(1, vector.shape[1])],
        [narrow, rows_of(block, width), narrow, narrow, narrow, fixed(1, 4 * D + width)],
        [
            shape_of(rows, D, dtype=low),
            shape_of(rows, width, dtype=low),
            shape_of(rows, D),
            shape_of(rows, D, dtype=low),
            shape_of(rows, D, dtype=low),
            shape_of(1, 4 * D + width),
        ],
        [
            pltpu.VMEM((D, D), low),
            pltpu.VMEM((D, width), low),
            pltpu.VMEM((width, D), low),
            pltpu.SemaphoreType.DMA((3,)),
        ],
        2 * rows * D * (D + 2 * width),
        rows * (18 * D + 4 * width) + 2 * D * (D + 2 * width),
        "mlp_backward",
        early=True,
    )(grad, slope, residual, up, proj_out, vector)


def qkv_back_kernel(grad_ref, residual_ref, stream_ref, weight_ref, vector_ref, out_ref, sums_ref):
    grad = grad_ref[...]
    normed_grad = mul_nt(grad, weight_ref[...])
    value_grad, gain_grad, shift_grad = norm_backward(normed_grad, stream_ref[...], vector_ref[:, :D])
    out_ref[...] = residual_ref[...] + value_grad
    accumulate(sums_ref, [gain_grad, shift_grad, column_sum(grad)])


def qkv_backward(grad, residual_grad, stream, weight, vector):
    rows = stream.shape[0]
    block = 256
    narrow = rows_of(block, D)
    return block_call(
        qkv_back_kernel,
        rows // block,
        [rows_of(block, 3 * D), narrow, narrow, fixed(D, 3 * D), fixed(1, vector.shape[1])],
        [narrow, fixed(1, 5 * D)],
        [shape_of(rows, D), shape_of(1, 5 * D)],
        [],
        6 * rows * D * D,
        18 * rows * D + 6 * D * D,
        "qkv_backward",
        early=True,
    )(grad, residual_grad, stream, weight, vector)


def input_grad_kernel(first_ref, second_ref, qkv_ref, hidden_ref, qkv_out, up_out, left_ref, *, cut):
    step = pl.program_id(0)

    @pl.when(step == 0)
    def _():
        left_ref[...] = first_ref[...].T

    @pl.when(step == cut)
    def _():
        left_ref[...] = second_ref[...].T

    @pl.when(step < cut)
    def _():
        qkv_out[...] = mul(left_ref[...], qkv_ref[...]).astype(jnp.bfloat16)

    @pl.when(step >= cut)
    def _():
        up_out[...] = mul(left_ref[...], hidden_ref[...]).astype(jnp.bfloat16)


def input_weight_grad(first, second, qkv_grad, hidden_grad):
    rows = first.shape[0]
    cut = qkv_grad.shape[1] // D
    steps = cut + hidden_grad.shape[1] // D
    before = lambda i: (0, jnp.minimum(i, cut - 1))
    after = lambda i: (0, jnp.maximum(i - cut, 0))
    return block_call(
        functools.partial(input_grad_kernel, cut=cut),
        steps,
        [
            fixed(rows, D),
            fixed(rows, D),
            pl.BlockSpec((rows, D), before),
            pl.BlockSpec((rows, D), after),
        ],
        [pl.BlockSpec((D, D), before), pl.BlockSpec((D, D), after)],
        [
            shape_of(D, qkv_grad.shape[1], dtype=jnp.bfloat16),
            shape_of(D, hidden_grad.shape[1], dtype=jnp.bfloat16),
        ],
        [pltpu.VMEM((D, rows), jnp.bfloat16)],
        2 * rows * D * D * steps,
        2 * rows * D * (steps + 2) + 2 * D * D * steps,
        "input_weight_grad",
        early=True,
    )(first, second, qkv_grad, hidden_grad)


def output_grad_kernel(attended_ref, active_ref, residual_ref, grad_ref, out_ref, *, cut):
    step = pl.program_id(0)

    @pl.when(step < cut)
    def _():
        out_ref[...] = mul(attended_ref[...].T, residual_ref[...]).astype(jnp.bfloat16)

    @pl.when(step >= cut)
    def _():
        out_ref[...] = mul(active_ref[...].T, grad_ref[...]).astype(jnp.bfloat16)


def output_weight_grad(attended, active, residual_low, grad_low):
    rows = attended.shape[0]
    block = 768
    cut = attended.shape[1] // block
    steps = cut + active.shape[1] // block
    return block_call(
        functools.partial(output_grad_kernel, cut=cut),
        steps,
        [
            pl.BlockSpec((rows, block), lambda i: (0, jnp.minimum(i, cut - 1))),
            pl.BlockSpec((rows, block), lambda i: (0, jnp.maximum(i - cut, 0))),
            fixed(rows, D),
            fixed(rows, D),
        ],
        rows_of(block, D),
        shape_of(steps * block, D, dtype=jnp.bfloat16),
        [],
        2 * rows * D * block * steps,
        2 * rows * (block * steps + 2 * D) + 2 * D * block * steps,
        "output_weight_grad",
        early=True,
    )(attended, active, residual_low, grad_low)


def embed_back_kernel(pixel_ref, grad_ref, pos_ref, out_ref, table_ref, bias_ref, low_ref):
    @at_first
    def _():
        grad = grad_ref[...]
        low = grad.astype(jnp.bfloat16)
        low_ref[...] = low
        bias_ref[...] = column_sum(low)
        table_ref[...] = jnp.dot(
            pos_ref[...], grad, precision=HIGHEST, preferred_element_type=jnp.float32
        )

    out_ref[...] = mul(pixel_ref[...].T, low_ref[...]).astype(jnp.bfloat16)


def embed_backward(pixels, grad, pos_weights_t):
    rows, depth = pixels.shape
    block = 768
    nodes = pos_weights_t.shape[0]
    return block_call(
        embed_back_kernel,
        depth // block,
        [pl.BlockSpec((rows, block), lambda i: (0, i)), fixed(rows, D), fixed(nodes, rows)],
        [rows_of(block, D), fixed(nodes, D), fixed(1, D)],
        [shape_of(depth, D, dtype=jnp.bfloat16), shape_of(nodes, D), shape_of(1, D)],
        [pltpu.VMEM((rows, D), jnp.bfloat16)],
        2 * rows * depth * D,
        2 * rows * depth + 2 * depth * D + 4 * rows * D,
        "embed_backward",
        early=True,
    )(pixels, grad, pos_weights_t)


def adam_update(gradient, moment, square, weight, factor, learn_rate):
    clipped = gradient * factor
    moment = BETA_ONE * moment + (1.0 - BETA_ONE) * clipped
    square = BETA_TWO * square + (1.0 - BETA_TWO) * clipped * clipped
    fixed_one = 1.0 - BETA_ONE**STEP
    fixed_two = 1.0 - BETA_TWO**STEP
    step_dir = (
        moment / fixed_one / (jnp.sqrt(square / fixed_two) + ADAM_EPS) + WEIGHT_DECAY * weight
    )
    return (moment, square, weight - learn_rate * step_dir)


def body(
    pixels,
    segment,
    patch_size,
    labels,
    patch_kernel,
    head_weight,
    input_proj,
    output_proj,
    layer_vector,
    position_table,
    global_vector,
    patch_moment,
    head_moment,
    input_moment,
    output_moment,
    layer_moment,
    position_moment,
    global_moment,
    patch_square,
    head_square,
    input_square,
    output_square,
    layer_square,
    position_square,
    global_square,
):
    pos_weights, member, counts = row_layout(segment, patch_size[0])
    owners = lax.axis_size("fsdp")
    nodes = pos_weights.shape[1]
    pos_weights = jnp.pad(pos_weights, ((0, 0), (0, -nodes % 64)))
    vector_size = layer_vector.size
    inputs = [
        (input_proj[index, :, : 3 * D].astype(LOW), input_proj[index, :, 3 * D :].astype(LOW))
        for index in range(LAYERS)
    ]
    outputs = [output_proj[index].astype(LOW) for index in range(LAYERS)]
    kernel_full, vectors, qkv_zero = gather_all(
        [
            patch_kernel.astype(LOW),
            padded_rows(layer_vector.astype(LOW).reshape(-1), 32),
            inputs[0][0],
        ],
        (True, False, True),
        1,
    )
    vectors = vectors.reshape(owners, -1)[:, :vector_size].reshape(owners, *layer_vector.shape)
    vectors = jnp.swapaxes(vectors, 0, 1).reshape(LAYERS, 1, -1).astype(jnp.float32)
    output_zero, qkv_one, up_one, head_full = (
        lax.all_gather(shard, "fsdp", axis=0, tiled=True)
        for shard in (outputs[0], *inputs[1], head_weight.astype(LOW))
    )
    global_low = rounded(global_vector)
    position_low = jnp.pad(rounded(position_table), ((0, -nodes % 64), (0, 0)))
    stream = embed(pixels, kernel_full, pos_weights, position_low, global_low[None, :D])
    saved_layers = []
    for index, qkv_weight in enumerate((qkv_zero, qkv_one)):
        vector = vectors[index]
        normed, qkv_rows = qkv_forward(stream, qkv_weight, vector)
        fetch = inputs[0][1] if index == 0 else outputs[1]
        attended, expo, inverse, (fetched,) = attention_forward(
            qkv_rows, segment, [fetch], 4 + index
        )
        up, output = (fetched, output_zero) if index == 0 else (up_one, fetched)
        residual, normed_second, active, slope, following = mlp_forward(
            stream, attended, up, output, vector
        )
        saved_layers.append(
            (
                (qkv_weight, up, output, vector),
                (stream, normed, qkv_rows, attended, expo, inverse),
                (residual, normed_second, active, slope),
            )
        )
        stream = following
    final_norm, final_back = jax.vjp(
        layer_norm, stream, global_low[D : 2 * D], global_low[2 * D : 3 * D]
    )
    image_sizes = jnp.maximum(counts, 1.0)
    pooled = (jnp.dot(member.T, final_norm, precision=HIGHEST) / image_sizes[:, None]).astype(
        jnp.bfloat16
    )
    logits = matmul(pooled, head_full) + global_low[3 * D :]
    highest = jnp.max(logits, -1, keepdims=True)
    exponent = jnp.exp(logits - highest)
    totals = jnp.sum(exponent, -1, keepdims=True)
    logsum = (highest + jnp.log(totals))[:, 0]
    onehot = labels[0][:, None] == jnp.arange(CLS, dtype=jnp.int32)[None, :]
    picked = jnp.sum(jnp.where(onehot, logits, 0.0), 1)
    loss_local = jnp.sum(counts * (logsum - picked))
    logits_grad = ((exponent / totals - onehot.astype(jnp.float32)) * counts[:, None]).astype(
        jnp.bfloat16
    )
    head_grad = matmul(pooled.T, logits_grad).astype(LOW)
    head_part = scatter(by_owner(jnp.pad(head_grad, ((0, 0), (0, -CLS % LANES)))))
    pooled_grad = matmul(logits_grad, head_full.T)
    final_grad = jnp.dot(member, pooled_grad / image_sizes[:, None], precision=HIGHEST)
    stream_grad, final_gain, final_shift = final_back(final_grad)
    vector_grads = [None] * LAYERS
    early_parts, late_parts = [head_part], []
    for index in reversed(range(LAYERS)):
        (qkv_weight, up, output, vector), first, second = saved_layers[index]
        entering, normed, qkv_rows, attended, expo, inverse = first
        residual, normed_second, active, slope = second
        grad_low, hidden_grad, residual_grad, residual_low, attended_grad, mlp_sums = mlp_backward(
            stream_grad, slope, residual, up, output, vector
        )
        output_grad = output_weight_grad(attended, active, residual_low, grad_low)
        attended_grad, output_grad = lax.optimization_barrier((attended_grad, output_grad))
        output_grad = by_owner(output_grad)
        half = -(-output_grad.shape[1] // 64) * 32
        if index:
            early_parts.append(scatter(output_grad[:, :half]))
            early_parts.append(scatter(output_grad[:, half:]))
        else:
            last_part = scatter(output_grad)
        qkv_grad, early_sums = attention_backward(
            qkv_rows, expo, inverse, attended, attended_grad, [] if index else early_parts, 6
        )
        stream_grad, qkv_sums = qkv_backward(qkv_grad, residual_grad, entering, qkv_weight, vector)
        input_grads = input_weight_grad(normed, normed_second, qkv_grad, hidden_grad)
        if index:
            stream_grad, *input_grads = lax.optimization_barrier((stream_grad, *input_grads))
            late_parts.extend(scatter(by_owner(grad)) for grad in input_grads)
        vector_grads[index] = jnp.concatenate(
            [
                qkv_sums[0, : 2 * D],
                mlp_sums[0, : 2 * D],
                qkv_sums[0, 2 * D :],
                mlp_sums[0, 2 * D :],
            ]
        )
    kernel_grad, position_grad, bias_grad = embed_backward(pixels, stream_grad, pos_weights.T)
    position_grad = position_grad[:nodes]
    vector_part = jnp.stack(vector_grads).reshape(LAYERS, owners, -1)
    vector_part = jnp.swapaxes(vector_part, 0, 1).reshape(owners, vector_size)
    vector_rows = -(-vector_size // LANES)
    vector_part = jnp.pad(vector_part, ((0, 0), (0, vector_rows * LANES - vector_size)))
    rest = jnp.concatenate(
        [
            position_grad.reshape(-1),
            bias_grad[0],
            final_gain,
            final_shift,
            jnp.sum(logits_grad.astype(jnp.float32), 0),
            loss_local[None],
            jnp.sum(counts)[None],
        ]
    )
    rest_rows = -(-rest.shape[0] // (owners * LANES))
    rest_part = jnp.pad(rest, (0, rest_rows * owners * LANES - rest.shape[0]))
    small = jnp.concatenate([vector_part, rest_part.reshape(owners, -1)], 1)
    used = vector_rows + rest_rows
    block_rows = (used // 64 + 1) * 64
    small = jnp.pad(small.reshape(owners, used, LANES), ((0, 0), (0, block_rows - used), (0, 0)))
    input_zero_sums, kernel_sum, input_one_sums = take(
        reduce_all([by_owner(grad) for grad in (*input_grads, kernel_grad)], late_parts, 2), 2, 1, 2
    )
    output_zero_sum, small_share, small_full = finish_all(
        [*early_sums, *input_zero_sums, *kernel_sum, *input_one_sums], [last_part], small, 3
    )
    head_sum, output_one_sums = early_sums[0], early_sums[1:]
    rest_sum = small_full[:, vector_rows:used].reshape(-1)
    position_sum = rest_sum[: position_grad.size].reshape(position_grad.shape)
    global_sum = rest_sum[position_grad.size :][: global_vector.shape[0]]
    loss_sum = rest_sum[rest.shape[0] - 2]
    token_total = rest_sum[rest.shape[0] - 1]
    kernel_sum = kernel_sum[0].astype(jnp.float32)
    head_sum = head_sum[:, :CLS].astype(jnp.float32)
    input_sum = jnp.stack(
        [jnp.concatenate(pair, 1) for pair in (input_zero_sums, input_one_sums)]
    ).astype(jnp.float32)
    output_sum = jnp.stack([output_zero_sum, jnp.concatenate(output_one_sums, 0)]).astype(
        jnp.float32
    )
    vector_sum = small_share[:vector_rows].reshape(-1)[:vector_size].reshape(layer_vector.shape)
    grad_norm = (
        jnp.sqrt(
            jnp.sum(small_full[:, -1])
            + jnp.sum(jnp.square(small_full[:, :vector_rows]))
            + jnp.sum(position_sum * position_sum)
            + jnp.sum(global_sum * global_sum)
        )
        / token_total
    )
    factor = jnp.minimum(1.0, CLIP_NORM / grad_norm) / token_total
    patch_next = adam_update(
        kernel_sum, patch_moment, patch_square, patch_kernel, factor, LEARN_RATE
    )
    head_next = adam_update(head_sum, head_moment, head_square, head_weight, factor, LEARN_RATE)
    input_next = adam_update(input_sum, input_moment, input_square, input_proj, factor, LEARN_RATE)
    output_next = adam_update(
        output_sum, output_moment, output_square, output_proj, factor, LEARN_RATE
    )
    layer_next = adam_update(
        vector_sum, layer_moment, layer_square, layer_vector, factor, VECTOR_RATE
    )
    position_next = adam_update(
        position_sum, position_moment, position_square, position_table, factor, LEARN_RATE
    )
    global_next = adam_update(
        global_sum, global_moment, global_square, global_vector, factor, VECTOR_RATE
    )
    return (
        loss_sum,
        token_total,
        grad_norm,
        patch_next[0],
        head_next[0],
        input_next[0],
        output_next[0],
        layer_next[0],
        position_next[0],
        global_next[0],
        patch_next[1],
        head_next[1],
        input_next[1],
        output_next[1],
        layer_next[1],
        position_next[1],
        global_next[1],
        patch_next[2],
        head_next[2],
        input_next[2],
        output_next[2],
        layer_next[2],
        position_next[2],
        global_next[2],
    )


def solution(mesh):
    in_specs = (
        P(("dp", "fsdp"), None),
        P(("dp", "fsdp")),
        P(("dp", "fsdp"), None),
        P(("dp", "fsdp"), None),
        P("fsdp", None),
        P("fsdp", None),
        P(None, "fsdp", None),
        P(None, "fsdp", None),
        P(None, "fsdp"),
        P(),
        P(),
        P("fsdp", None),
        P("fsdp", None),
        P(None, "fsdp", None),
        P(None, "fsdp", None),
        P(None, "fsdp"),
        P(),
        P(),
        P("fsdp", None),
        P("fsdp", None),
        P(None, "fsdp", None),
        P(None, "fsdp", None),
        P(None, "fsdp"),
        P(),
        P(),
    )
    out_specs = (
        P(),
        P(),
        P(),
        P("fsdp", None),
        P("fsdp", None),
        P(None, "fsdp", None),
        P(None, "fsdp", None),
        P(None, "fsdp"),
        P(),
        P(),
        P("fsdp", None),
        P("fsdp", None),
        P(None, "fsdp", None),
        P(None, "fsdp", None),
        P(None, "fsdp"),
        P(),
        P(),
        P("fsdp", None),
        P("fsdp", None),
        P(None, "fsdp", None),
        P(None, "fsdp", None),
        P(None, "fsdp"),
        P(),
        P(),
    )
    return jax.shard_map(body, mesh=mesh, in_specs=in_specs, out_specs=out_specs, check_vma=False)
```

```python
import functools

import jax
import jax.numpy as jnp
from jax import lax
from jax.experimental import pallas as pl
from jax.experimental.pallas import tpu as pltpu
from jax.sharding import PartitionSpec as P

D = 768
HEADS = 12
HD = 64
CLS = 1000
GRID = 7
IMG = 240
IMGS = 8
LAYERS = 2
STEP = 3


NORM_EPS = 1e-06
CLIP_NORM = 0.01
LEARN_RATE = 0.05
VECTOR_RATE = 0.25
BETA_ONE = 0.5
BETA_TWO = 0.5
ADAM_EPS = 1e-08
WEIGHT_DECAY = 0.05
HIGHEST = lax.Precision.HIGHEST

PAIR = 2 * HD
MASKED = -1e30
MIB = 1024 * 1024
VMEM_LIMIT = 56 * MIB
MESH = pl.DeviceIdType.MESH
LANES = 128
LOW = jnp.bfloat16
ANYWHERE = pl.BlockSpec(memory_space=pl.ANY)
NO_COST = pl.CostEstimate(flops=0, bytes_accessed=0, transcendentals=0)
ROOT = 0.7978845608028654
CUBE = 0.044715
NT = (((1,), (1,)), ((), ()))


def layer_norm(values, gain, shift):
    center = values - jnp.mean(values, -1, keepdims=True)
    spread = jnp.mean(center * center, -1, keepdims=True)
    return center * lax.rsqrt(spread + NORM_EPS) * gain + shift


def rounded(values):
    return lax.optimization_barrier(values.astype(jnp.bfloat16)).astype(jnp.float32)


def matmul(left, right):
    return jnp.dot(left, right, preferred_element_type=jnp.float32)


def padded_rows(flat, multiple):
    extra = -flat.shape[0] % (multiple * LANES)
    return jnp.pad(flat, (0, extra)).reshape(-1, LANES)


def row_layout(seg_row, patch_row):
    row_count = seg_row.shape[0]
    slots = jnp.arange(IMGS, dtype=jnp.int32)
    member = seg_row[:, None] == slots[None, :]
    counts = jnp.sum(member.astype(jnp.int32), 0, dtype=jnp.int32)
    starts = jnp.cumsum(counts, dtype=jnp.int32) - counts
    inside = jnp.any(member, 1)
    offset = jnp.arange(row_count, dtype=jnp.int32) - jnp.sum(
        jnp.where(member, starts[None, :], 0), 1, dtype=jnp.int32
    )
    offset = jnp.where(inside, offset, 0)
    patch_tok = jnp.sum(jnp.where(member, patch_row[None, :], 0), 1, dtype=jnp.int32) + jnp.where(
        inside, 0, IMG
    )
    side = IMG // patch_tok
    nodes = jnp.arange(GRID, dtype=jnp.int32).astype(jnp.float32)

    def hat(coord):
        place = ((2 * coord + 1) * GRID).astype(jnp.float32) / (2 * side).astype(jnp.float32) - 0.5
        place = jnp.clip(place, 0.0, GRID - 1.0)
        return jnp.maximum(1.0 - jnp.abs(place[:, None] - nodes[None, :]), 0.0)

    weights = (hat(offset // side)[:, :, None] * hat(offset % side)[:, None, :]).reshape(
        row_count, GRID * GRID
    )
    return (weights, member.astype(jnp.float32), counts.astype(jnp.float32))


TURNS = (1, 2, 3)


def place():
    slot = lax.axis_index("fsdp")
    return lax.axis_index("dp"), lax.div(slot, 2), lax.rem(slot, 2)


def partner(index, turn):
    if turn == 0:
        return index
    if turn == 1:
        return index + 1 - 2 * lax.rem(index, 2)
    if turn == 2:
        return lax.rem(index + 2, 4)
    return 3 - index


def greet():
    group, level, core = place()
    barrier = pltpu.get_barrier_semaphore()
    peers = [(group, 2 * level + 1 - core)]
    for turn in TURNS:
        peers.append((group, 2 * partner(level, turn) + core))
        peers.append((partner(group, turn), 2 * level + core))
    for peer in peers:
        pl.semaphore_signal(barrier, inc=1, device_id=peer, device_id_type=MESH)
    pl.semaphore_wait(barrier, len(peers))


def quarter_shape(rows, columns):
    if columns % (2 * LANES) == 0:
        return rows // 2, columns // 2
    return rows // 4, columns


def quarter(index, rows, columns):
    high, wide = quarter_shape(rows, columns)
    if wide == columns:
        return pl.ds(pl.multiple_of(index * high, high), high), pl.ds(0, columns)
    return (
        pl.ds(pl.multiple_of(lax.div(index, 2) * high, high), high),
        pl.ds(pl.multiple_of(lax.rem(index, 2) * wide, wide), wide),
    )


def remote(source, target, send, receive, device):
    return pltpu.make_async_remote_copy(
        src_ref=source,
        dst_ref=target,
        send_sem=send,
        recv_sem=receive,
        device_id=device,
        device_id_type=MESH,
    )


GATHER_SEMS = 33


class Gather:
    def __init__(self, shard, out, sems, split):
        self.shard, self.out, self.sems, self.split = shard, out, sems, split
        self.rows, self.columns = shard.shape

    def level_copy(self, turn):
        group, level, core = place()
        block = self.out.at[2 * level + core]
        source = self.shard
        if self.split:
            part = quarter(group, self.rows, self.columns)
            source, block = source.at[part], block.at[part]
        sems = self.sems
        peer = (group, 2 * partner(level, turn) + core)
        return remote(source, block, sems.at[turn], sems.at[3 + turn], peer)

    def group_copy(self, turn, other):
        group, level, core = place()
        part = quarter(group, self.rows, self.columns)
        block = self.out.at[2 * partner(level, turn) + core].at[part]
        index = 3 * (turn - 1) + other - 1
        peer = (partner(group, other), 2 * level + core)
        return remote(block, block, self.sems.at[7 + index], self.sems.at[16 + index], peer)

    def core_copy(self, turn):
        group, level, core = place()
        slot = 2 * partner(level, turn) + core
        source = self.shard if turn == 0 else self.out.at[slot]
        peer = (group, 2 * level + 1 - core)
        return remote(source, self.out.at[slot], self.sems.at[25 + turn], self.sems.at[29 + turn], peer)

    def own_copy(self):
        _, level, core = place()
        return pltpu.make_async_copy(self.shard, self.out.at[2 * level + core], self.sems.at[0])

    def first(self):
        for turn in TURNS:
            self.level_copy(turn).start()
        self.core_copy(0).start()
        self.own_copy().start()

    def second(self):
        for turn in TURNS:
            self.level_copy(turn).wait_recv()
            if self.split:
                for other in TURNS:
                    self.group_copy(turn, other).start()
            else:
                self.core_copy(turn).start()

    def third(self):
        if not self.split:
            return
        for turn in TURNS:
            for other in TURNS:
                self.group_copy(turn, other).wait_recv()
            self.core_copy(turn).start()

    def fourth(self):
        for turn in (0, *TURNS):
            self.core_copy(turn).wait_recv()
        for turn in TURNS:
            self.level_copy(turn).wait_send()
            if self.split:
                for other in TURNS:
                    self.group_copy(turn, other).wait_send()
        for turn in (0, *TURNS):
            self.core_copy(turn).wait_send()
        self.own_copy().wait()


class LevelGather:
    def __init__(self, shard, out, sems):
        self.shard, self.out, self.sems = shard, out, sems

    def level_copy(self, turn):
        group, level, core = place()
        return remote(
            self.shard.at[quarter(group, *self.shard.shape)],
            self.out.at[level],
            self.sems.at[turn],
            self.sems.at[3 + turn],
            (group, 2 * partner(level, turn) + core),
        )

    def first(self):
        for turn in TURNS:
            self.level_copy(turn).start()

    def second(self):
        pass

    def third(self):
        pass

    def fourth(self):
        for turn in TURNS:
            self.level_copy(turn).wait_recv()
            self.level_copy(turn).wait_send()


GROUP_GATHER_SEMS = 30


class GroupGather:
    def __init__(self, shard, quarters, out, sems):
        self.shard, self.quarters, self.out, self.sems = shard, quarters, out, sems

    def part(self, turn):
        group, level, core = place()
        block = self.out.at[2 * partner(level, turn) + core]
        return block.at[quarter(group, *self.shard.shape)]

    def own_copy(self, turn):
        _, level, core = place()
        if turn == 0:
            source, target = self.shard, self.out.at[2 * level + core]
        else:
            source, target = self.quarters.at[partner(level, turn)], self.part(turn)
        return pltpu.make_async_copy(source, target, self.sems.at[turn])

    def group_copy(self, turn, other):
        group, level, core = place()
        index = 3 * (turn - 1) + other - 1
        return remote(
            self.quarters.at[partner(level, turn)],
            self.part(turn),
            self.sems.at[4 + index],
            self.sems.at[13 + index],
            (partner(group, other), 2 * level + core),
        )

    def core_copy(self, turn):
        group, level, core = place()
        slot = 2 * partner(level, turn) + core
        source = self.shard if turn == 0 else self.out.at[slot]
        peer = (group, 2 * level + 1 - core)
        return remote(source, self.out.at[slot], self.sems.at[22 + turn], self.sems.at[26 + turn], peer)

    def first(self):
        for turn in TURNS:
            for other in TURNS:
                self.group_copy(turn, other).start()
        for turn in (0, *TURNS):
            self.own_copy(turn).start()
        self.core_copy(0).start()

    def second(self):
        for turn in TURNS:
            for other in TURNS:
                self.group_copy(turn, other).wait_recv()
            self.own_copy(turn).wait()
            self.core_copy(turn).start()

    def third(self):
        for turn in (0, *TURNS):
            self.core_copy(turn).wait_recv()
            self.core_copy(turn).wait_send()
        for turn in TURNS:
            for other in TURNS:
                self.group_copy(turn, other).wait_send()
        self.own_copy(0).wait()


class GatherRide:
    def __init__(self, shard, quarters):
        owners = lax.axis_size("fsdp")
        self.operands = [shard, quarters]
        self.out_specs = [ANYWHERE]
        self.out_shapes = [jax.ShapeDtypeStruct((owners, *shard.shape), shard.dtype)]
        self.scratch = [pltpu.SemaphoreType.DMA((GROUP_GATHER_SEMS,))]

    def job(self, sources, targets, scratch):
        return GroupGather(*sources, *targets, *scratch)

    def before(self, steps):
        return {0: ("first",), max(1, 2 * steps // 3): ("second",)}

    after = ("third",)

    def result(self, outs):
        return outs[0].reshape(-1, outs[0].shape[2])

    def plain(self):
        return lax.all_gather(self.operands[0], "fsdp", axis=0, tiled=True)


class ShareRide:
    def __init__(self, share):
        self.operands = [share]
        self.out_specs = [fixed(*share.shape)]
        self.out_shapes = [jax.ShapeDtypeStruct(share.shape, share.dtype)]
        self.scratch = [
            pltpu.VMEM(share.shape, share.dtype),
            *share_scratch(share),
            pltpu.SemaphoreType.DMA((GROUP_SEMS,)),
        ]

    def job(self, sources, targets, scratch):
        job = GroupReduce(sources[0], scratch[0], scratch[1:3], scratch[3])
        job.target = targets[0]
        return job

    def before(self, steps):
        return {0: ("first", "second"), max(1, steps // 2): ("third",)}

    after = ("fifth", "sixth", "store")

    def result(self, outs):
        return outs[0]

    def plain(self):
        return lax.psum(self.operands[0], "dp")


def riding(body, counts, rides, steps):
    def kernel(*refs):
        refs = list(refs)

        def pop(count):
            taken = refs[:count]
            del refs[:count]
            return taken

        own = pop(counts[0])
        sources = [pop(len(ride.operands)) for ride in rides]
        own += pop(counts[1])
        targets = [pop(len(ride.out_shapes)) for ride in rides]
        own += pop(counts[2])
        jobs = [
            ride.job(source, target, pop(len(ride.scratch)))
            for ride, source, target in zip(rides, sources, targets)
        ]
        for step in range(steps):
            planned = [
                (job, stages)
                for ride, job in zip(rides, jobs)
                for at, stages in ride.before(steps).items()
                if at == step
            ]
            if planned:

                @pl.when(pl.program_id(0) == step)
                def _(planned=planned, step=step):
                    if step == 0:
                        greet()
                    for job, stages in planned:
                        run_stages([job], stages)

        body(*own)

        @pl.when(pl.program_id(0) == steps - 1)
        def _():
            for ride, job in zip(rides, jobs):
                run_stages([job], ride.after)

    return kernel


def block_call(
    body, grid, in_specs, operands, out_specs, out_shape, scratch, room, name,
    cost=None, rides=(), collective_id=None,
):
    plain = []
    if rides and not with_kernels():
        plain, rides = [ride.plain() for ride in rides], ()
    transfer = {}
    kernel = body
    if rides:
        transfer = {"collective_id": collective_id, "has_side_effects": True}
        kernel = riding(body, (len(operands), len(out_shape), len(scratch)), rides, grid)
    count = len(out_shape)
    for ride in rides:
        operands, in_specs = [*operands, *ride.operands], [*in_specs, *[ANYWHERE] * len(ride.operands)]
        out_specs, out_shape = [*out_specs, *ride.out_specs], [*out_shape, *ride.out_shapes]
        scratch = [*scratch, *ride.scratch]
    outs = pl.pallas_call(
        kernel,
        grid=(grid,),
        in_specs=in_specs,
        out_specs=out_specs,
        out_shape=out_shape,
        scratch_shapes=scratch,
        compiler_params=pltpu.CompilerParams(vmem_limit_bytes=room * MIB, **transfer),
        cost_estimate=cost or NO_COST,
        name=name,
    )(*operands)
    brought, outs = list(outs[count:]), list(outs[:count])
    for ride in rides:
        plain.append(ride.result(brought[: len(ride.out_shapes)]))
        brought = brought[len(ride.out_shapes) :]
    return outs + plain


def work(flops, size):
    return pl.CostEstimate(flops=flops, bytes_accessed=size, transcendentals=0)


def gather_kernel(*refs):
    kernel, vectors, inputs, outputs, head = refs[:5]
    kernel_full, vectors_full, qkv_full, up_level, qkv_level, output_level = refs[5:11]
    up_zero, output_zero, qkv_one, up_one, output_one, head_low = refs[11:17]
    wide_kernel, wide_inputs, wide_outputs, wide_head, kernel_low, qkv_zero = refs[17:23]
    load_sems, sems = refs[23:]
    pairs = [
        (kernel, wide_kernel),
        (inputs.at[0], wide_inputs.at[0]),
        (outputs.at[1], wide_outputs.at[1]),
        (inputs.at[1], wide_inputs.at[1]),
        (outputs.at[0], wide_outputs.at[0]),
        (head, wide_head),
    ]
    copies = [
        pltpu.make_async_copy(source, target, load_sems.at[index])
        for index, (source, target) in enumerate(pairs)
    ]
    for copy in copies:
        copy.start()
    jobs = [
        Gather(kernel_low, kernel_full, sems.at[0], True),
        Gather(vectors, vectors_full, sems.at[1], False),
        Gather(qkv_zero, qkv_full, sems.at[2], True),
        LevelGather(up_zero, up_level, sems.at[3]),
        LevelGather(qkv_one, qkv_level, sems.at[4]),
        LevelGather(output_one, output_level, sems.at[5]),
    ]
    greet()
    jobs[1].first()
    copies[0].wait()
    kernel_low[...] = wide_kernel[...].astype(LOW)
    jobs[0].first()
    copies[1].wait()
    qkv_zero[...] = wide_inputs[0, :, : 3 * D].astype(LOW)
    jobs[2].first()
    up_zero[...] = wide_inputs[0, :, 3 * D :].astype(LOW)
    jobs[3].first()
    copies[3].wait()
    qkv_one[...] = wide_inputs[1, :, : 3 * D].astype(LOW)
    jobs[4].first()
    copies[2].wait()
    output_one[...] = wide_outputs[1].astype(LOW)
    jobs[5].first()
    run_stages(jobs[:3], ("second",))
    up_one[...] = wide_inputs[1, :, 3 * D :].astype(LOW)
    copies[4].wait()
    output_zero[...] = wide_outputs[0].astype(LOW)
    copies[5].wait()
    head_low[...] = wide_head[...].astype(LOW)
    run_stages(jobs[:3], ("third",))
    run_stages(jobs, ("fourth",))


def gather_first(patch_kernel, vectors, input_proj, output_proj, head_weight):
    if not with_kernels():
        inputs = [
            (input_proj[index, :, : 3 * D].astype(LOW), input_proj[index, :, 3 * D :].astype(LOW))
            for index in range(LAYERS)
        ]
        outputs = [output_proj[index].astype(LOW) for index in range(LAYERS)]
        whole = [patch_kernel.astype(LOW), vectors, inputs[0][0]]
        return (
            [lax.all_gather(shard, "fsdp", axis=0, tiled=True) for shard in whole],
            [GatherRide(shard, shard) for shard in (inputs[0][1], inputs[1][0], outputs[1])],
            [outputs[0], inputs[1][1], head_weight.astype(LOW)],
        )
    owners = lax.axis_size("fsdp")
    depth = input_proj.shape[1]
    up_shape = (depth, input_proj.shape[2] - 3 * D)
    qkv_shape, out_shape = (depth, 3 * D), output_proj.shape[1:]
    low = lambda *shape: jax.ShapeDtypeStruct(shape, LOW)
    levels = lambda shape: low(4, *quarter_shape(*shape))
    shapes = [
        low(owners, *patch_kernel.shape),
        low(owners, *vectors.shape),
        low(owners, *qkv_shape),
        levels(up_shape),
        levels(qkv_shape),
        levels(out_shape),
        low(*up_shape),
        low(*out_shape),
        low(*qkv_shape),
        low(*up_shape),
        low(*out_shape),
        low(*head_weight.shape),
    ]
    wide = (patch_kernel, input_proj, output_proj, head_weight)
    results = pl.pallas_call(
        gather_kernel,
        in_specs=[ANYWHERE] * 5,
        out_specs=[ANYWHERE] * 6 + [pl.BlockSpec(memory_space=pltpu.VMEM)] * 6,
        out_shape=shapes,
        scratch_shapes=[
            *[pltpu.VMEM(array.shape, array.dtype) for array in wide],
            pltpu.VMEM(patch_kernel.shape, LOW),
            pltpu.VMEM(qkv_shape, LOW),
            pltpu.SemaphoreType.DMA((6,)),
            pltpu.SemaphoreType.DMA((6, GATHER_SEMS)),
        ],
        compiler_params=pltpu.CompilerParams(
            collective_id=1, has_side_effects=True, vmem_limit_bytes=32 * MIB
        ),
        cost_estimate=NO_COST,
        name="gather_weights",
    )(patch_kernel, vectors, input_proj, output_proj, head_weight)
    up_zero, output_zero, qkv_one, up_one, output_one, head_low = results[6:]
    return (
        [full.reshape(owners * full.shape[1], full.shape[2]) for full in results[:3]],
        [
            GatherRide(up_zero, results[3]),
            GatherRide(qkv_one, results[4]),
            GatherRide(output_one, results[5]),
        ],
        [output_zero, up_one, head_low],
    )


REDUCE_SEMS = 48


class Reduce:
    def __init__(self, grad, out, scratch, sems):
        self.grad, self.out, self.sems = grad, out, sems
        self.own, self.got_core, self.got_group, self.part, self.got_level = scratch
        self.rows, self.columns = out.shape
        self.chunk = 16

    def load(self, level):
        _, _, core = place()
        return pltpu.make_async_copy(
            self.grad.at[2 * level + core], self.own.at[level], self.sems.at[level]
        )

    def core_copy(self, target_level):
        group, level, core = place()
        return remote(
            self.grad.at[2 * target_level + 1 - core],
            self.got_core.at[target_level],
            self.sems.at[4 + target_level],
            self.sems.at[8 + target_level],
            (group, 2 * level + 1 - core),
        )

    def group_copy(self, turn, other):
        group, level, core = place()
        target = partner(level, turn)
        peer = partner(group, other)
        part = quarter(peer, self.rows, self.columns)
        index = 3 * turn + other - 1
        return remote(
            self.own.at[target].at[part],
            self.got_group.at[other - 1, target],
            self.sems.at[12 + index],
            self.sems.at[24 + index],
            (peer, 2 * level + core),
        )

    def level_copy(self, turn):
        group, level, core = place()
        target = partner(level, turn)
        return remote(
            self.part.at[target],
            self.got_level.at[turn - 1],
            self.sems.at[35 + turn],
            self.sems.at[38 + turn],
            (group, 2 * target + core),
        )

    def share_copy(self, other):
        group, level, core = place()
        mine = self.out.at[quarter(group, self.rows, self.columns)]
        return remote(
            mine,
            mine,
            self.sems.at[41 + other],
            self.sems.at[44 + other],
            (partner(group, other), 2 * level + core),
        )

    def first(self):
        _, level, _ = place()
        for turn in (*TURNS, 0):
            self.core_copy(partner(level, turn)).start()
            self.load(partner(level, turn)).start()

    def second(self):
        _, level, _ = place()
        for turn in (*TURNS, 0):
            target = partner(level, turn)
            self.load(target).wait()
            self.core_copy(target).wait_recv()

            def add(step, carry):
                rows = pl.ds(pl.multiple_of(step * self.chunk, self.chunk), self.chunk)
                total = self.own[target, rows, :].astype(jnp.float32)
                total = total + self.got_core[target, rows, :].astype(jnp.float32)
                self.own[target, rows, :] = total.astype(self.own.dtype)
                return carry

            lax.fori_loop(0, self.rows // self.chunk, add, 0)
            for other in TURNS:
                self.group_copy(turn, other).start()

    def between(self):
        pass

    def third(self):
        group, level, _ = place()
        high, wide = quarter_shape(self.rows, self.columns)
        row_part, column_part = quarter(group, self.rows, self.columns)
        for turn in (*TURNS, 0):
            target = partner(level, turn)
            for other in TURNS:
                self.group_copy(turn, other).wait_recv()

            def add(step, carry):
                at = pl.multiple_of(step * self.chunk, self.chunk)
                rows = pl.ds(at, self.chunk)
                mine = pl.ds(pl.multiple_of(row_part.start + at, self.chunk), self.chunk)
                total = self.own[target, mine, column_part].astype(jnp.float32)
                for slot in range(3):
                    total = total + self.got_group[slot, target, rows, :].astype(jnp.float32)
                self.part[target, rows, :] = total.astype(self.part.dtype)
                return carry

            lax.fori_loop(0, high // self.chunk, add, 0)
            if turn:
                self.level_copy(turn).start()

    def fourth(self):
        group, level, _ = place()
        high, wide = quarter_shape(self.rows, self.columns)
        row_part, column_part = quarter(group, self.rows, self.columns)
        for turn in TURNS:
            self.level_copy(turn).wait_recv()

        def add(step, carry):
            at = pl.multiple_of(step * self.chunk, self.chunk)
            rows = pl.ds(at, self.chunk)
            mine = pl.ds(pl.multiple_of(row_part.start + at, self.chunk), self.chunk)
            total = self.part[level, rows, :].astype(jnp.float32)
            for slot in range(3):
                total = total + self.got_level[slot, rows, :].astype(jnp.float32)
            self.out[mine, column_part] = total.astype(self.out.dtype)
            return carry

        lax.fori_loop(0, high // self.chunk, add, 0)
        for other in TURNS:
            self.share_copy(other).start()

    def fifth(self):
        for other in TURNS:
            self.share_copy(other).wait_recv()

    def sixth(self):
        _, level, _ = place()
        for turn in (*TURNS, 0):
            self.core_copy(partner(level, turn)).wait_send()
            for other in TURNS:
                self.group_copy(turn, other).wait_send()
            if turn:
                self.level_copy(turn).wait_send()
                self.share_copy(turn).wait_send()


WHOLE_SEMS = 40


def add_rows(target, row, columns, source, count, wide):
    chunk = 16 if wide > 1536 else 48

    def add(step, carry):
        at = pl.multiple_of(step * chunk, chunk)
        mine = pl.ds(pl.multiple_of(row + at, 16), chunk)
        total = target[mine, columns].astype(jnp.float32)
        total = total + source[pl.ds(at, chunk), :].astype(jnp.float32)
        target[mine, columns] = total.astype(target.dtype)
        return carry

    lax.fori_loop(0, count // chunk, add, 0)


class Whole:
    FIRST_X = (1, 0)

    def __init__(self, grad, out, scratch, sems):
        self.grad, self.out, self.sems = grad, out, sems
        self.own, self.got_core, self.got_x, self.got_y, self.got_last, self.part, self.got_level = scratch
        self.rows, self.columns = out.shape
        self.high, self.wide = self.rows // 2, self.columns // 2

    def row_half(self, index):
        return pl.ds(pl.multiple_of(lax.div(index, 2) * self.high, self.high), self.high)

    def column_half(self, index):
        return pl.ds(pl.multiple_of(lax.rem(index, 2) * self.wide, self.wide), self.wide)

    def load(self, level):
        _, _, core = place()
        return pltpu.make_async_copy(
            self.grad.at[2 * level + core], self.own.at[level], self.sems.at[level]
        )

    def core_copy(self, target_level):
        group, level, core = place()
        return remote(
            self.grad.at[2 * target_level + 1 - core],
            self.got_core.at[target_level],
            self.sems.at[4 + target_level],
            self.sems.at[8 + target_level],
            (group, 2 * level + 1 - core),
        )

    def step_copy(self, turn):
        group, level, core = place()
        block = self.own.at[partner(level, turn)]
        if turn in self.FIRST_X:
            peer = partner(group, 1)
            source = block.at[:, self.column_half(peer)]
            target = self.got_x.at[self.FIRST_X.index(turn)]
        else:
            peer = partner(group, 2)
            source = block.at[self.row_half(peer), :]
            target = self.got_y.at[turn - 2]
        return remote(
            source, target, self.sems.at[12 + turn], self.sems.at[16 + turn], (peer, 2 * level + core)
        )

    def last_copy(self, turn):
        group, level, core = place()
        block = self.own.at[partner(level, turn)]
        peer = partner(group, 2 if turn in self.FIRST_X else 1)
        rows = self.row_half(peer)
        columns = self.column_half(peer)
        return remote(
            block.at[rows, columns],
            self.got_last.at[turn],
            self.sems.at[20 + turn],
            self.sems.at[24 + turn],
            (peer, 2 * level + core),
        )

    def level_copy(self, turn):
        group, level, core = place()
        target = partner(level, turn)
        return remote(
            self.part.at[target],
            self.got_level.at[turn - 1],
            self.sems.at[27 + turn],
            self.sems.at[30 + turn],
            (group, 2 * target + core),
        )

    def share_copy(self, other):
        group, level, core = place()
        mine = self.out.at[self.row_half(group), self.column_half(group)]
        return remote(
            mine,
            mine,
            self.sems.at[33 + other],
            self.sems.at[36 + other],
            (partner(group, other), 2 * level + core),
        )

    def first(self):
        _, level, _ = place()
        for turn in (*TURNS, 0):
            self.core_copy(partner(level, turn)).start()
            self.load(partner(level, turn)).start()

    def second(self):
        _, level, _ = place()
        for turn in (*TURNS, 0):
            target = partner(level, turn)
            self.load(target).wait()
            self.core_copy(target).wait_recv()
            add_rows(
                self.own.at[target], 0, slice(None), self.got_core.at[target], self.rows, self.columns
            )
            self.step_copy(turn).start()

    def between(self):
        group, level, _ = place()
        for turn in (*TURNS, 0):
            block = self.own.at[partner(level, turn)]
            self.step_copy(turn).wait_recv()
            if turn in self.FIRST_X:
                source = self.got_x.at[self.FIRST_X.index(turn)]
                add_rows(block, 0, self.column_half(group), source, self.rows, self.wide)
            else:
                source = self.got_y.at[turn - 2]
                start = lax.div(group, 2) * self.high
                add_rows(block, start, slice(None), source, self.high, self.columns)
            self.last_copy(turn).start()

    def third(self):
        group, level, _ = place()
        start = lax.div(group, 2) * self.high
        columns = self.column_half(group)
        chunk = 16 if self.wide > 1536 else 48
        for turn in (*TURNS, 0):
            target = partner(level, turn)
            self.last_copy(turn).wait_recv()

            def add(step, carry):
                at = pl.multiple_of(step * chunk, chunk)
                rows = pl.ds(at, chunk)
                mine = pl.ds(pl.multiple_of(start + at, 16), chunk)
                total = self.own[target, mine, columns].astype(jnp.float32)
                total = total + self.got_last[turn, rows, :].astype(jnp.float32)
                self.part[target, rows, :] = total.astype(self.part.dtype)
                return carry

            lax.fori_loop(0, self.high // chunk, add, 0)
            if turn:
                self.level_copy(turn).start()

    def fourth(self):
        group, level, _ = place()
        start = lax.div(group, 2) * self.high
        columns = self.column_half(group)
        chunk = 16 if self.wide > 1536 else 48
        for turn in TURNS:
            self.level_copy(turn).wait_recv()

        def add(step, carry):
            at = pl.multiple_of(step * chunk, chunk)
            rows = pl.ds(at, chunk)
            mine = pl.ds(pl.multiple_of(start + at, 16), chunk)
            total = self.part[level, rows, :].astype(jnp.float32)
            for slot in range(3):
                total = total + self.got_level[slot, rows, :].astype(jnp.float32)
            self.out[mine, columns] = total.astype(self.out.dtype)
            return carry

        lax.fori_loop(0, self.high // chunk, add, 0)
        for other in TURNS:
            self.share_copy(other).start()

    def fifth(self):
        for other in TURNS:
            self.share_copy(other).wait_recv()

    def sixth(self):
        _, level, _ = place()
        for turn in (*TURNS, 0):
            self.core_copy(partner(level, turn)).wait_send()
            self.step_copy(turn).wait_send()
            self.last_copy(turn).wait_send()
            if turn:
                self.level_copy(turn).wait_send()
                self.share_copy(turn).wait_send()


GROUP_SEMS = 13


class GroupReduce:
    def __init__(self, share, out, scratch, sems):
        self.share, self.out, self.sems = share, out, sems
        self.own, self.got = scratch
        self.rows, self.columns = out.shape
        self.chunk = 16

    def load(self):
        return pltpu.make_async_copy(self.share, self.own, self.sems.at[0])

    def group_copy(self, other):
        group, level, core = place()
        peer = partner(group, other)
        return remote(
            self.own.at[quarter(peer, self.rows, self.columns)],
            self.got.at[other - 1],
            self.sems.at[other],
            self.sems.at[3 + other],
            (peer, 2 * level + core),
        )

    def share_copy(self, other):
        group, level, core = place()
        mine = self.out.at[quarter(group, self.rows, self.columns)]
        return remote(
            mine,
            mine,
            self.sems.at[6 + other],
            self.sems.at[9 + other],
            (partner(group, other), 2 * level + core),
        )

    def first(self):
        self.load().start()

    def second(self):
        self.load().wait()
        for other in TURNS:
            self.group_copy(other).start()

    def between(self):
        pass

    def third(self):
        group, _, _ = place()
        high, wide = quarter_shape(self.rows, self.columns)
        row_part, column_part = quarter(group, self.rows, self.columns)
        for other in TURNS:
            self.group_copy(other).wait_recv()

        def add(step, carry):
            at = pl.multiple_of(step * self.chunk, self.chunk)
            rows = pl.ds(at, self.chunk)
            mine = pl.ds(pl.multiple_of(row_part.start + at, self.chunk), self.chunk)
            total = self.own[mine, column_part].astype(jnp.float32)
            for slot in range(3):
                total = total + self.got[slot, rows, :].astype(jnp.float32)
            self.out[mine, column_part] = total.astype(self.out.dtype)
            return carry

        lax.fori_loop(0, high // self.chunk, add, 0)
        for other in TURNS:
            self.share_copy(other).start()

    def fourth(self):
        pass

    def fifth(self):
        for other in TURNS:
            self.share_copy(other).wait_recv()

    def store(self):
        self.target[...] = self.out[...]

    def sixth(self):
        for other in TURNS:
            self.group_copy(other).wait_send()
            self.share_copy(other).wait_send()


class Spread:
    def __init__(self, full, sems):
        self.full, self.sems = full, sems

    def level_copy(self, turn):
        group, level, core = place()
        block = self.full.at[2 * level + core]
        peer = (group, 2 * partner(level, turn) + core)
        return remote(block, block, self.sems.at[turn - 1], self.sems.at[2 + turn], peer)

    def core_copy(self, turn):
        group, level, core = place()
        block = self.full.at[2 * partner(level, turn) + core]
        peer = (group, 2 * level + 1 - core)
        return remote(block, block, self.sems.at[6 + turn], self.sems.at[10 + turn], peer)

    def run(self):
        for turn in TURNS:
            self.level_copy(turn).start()
        self.core_copy(0).start()
        for turn in TURNS:
            self.level_copy(turn).wait_recv()
            self.core_copy(turn).start()
        for turn in (0, *TURNS):
            self.core_copy(turn).wait_recv()
        for turn in (0, *TURNS):
            self.core_copy(turn).wait_send()
            if turn:
                self.level_copy(turn).wait_send()


def squares_in(out):
    def add(step, total):
        piece = out[pl.ds(pl.multiple_of(step * 16, 16), 16), :].astype(jnp.float32)
        piece = piece * piece
        for lane in range(0, out.shape[1], LANES):
            total = total + piece[:, lane : lane + LANES]
        return total

    total = lax.fori_loop(0, out.shape[0] // 16, add, jnp.zeros((16, LANES), jnp.float32))
    return jnp.sum(total, 0, keepdims=True)


def run_stages(jobs, stages):
    for stage in stages:
        for job in jobs:
            getattr(job, stage)()


STAGES = ("first", "second", "between", "third", "fourth", "fifth", "sixth")


def whole_scratch(grad):
    _, rows, columns = grad.shape
    high, wide = quarter_shape(rows, columns)
    shapes = ((4, rows, columns), (4, rows, columns), (3, 4, high, wide), (4, high, wide))
    return [pltpu.VMEM(shape, grad.dtype) for shape in (*shapes, (3, high, wide))]


def stepped_scratch(grad):
    _, rows, columns = grad.shape
    high, wide = rows // 2, columns // 2
    shapes = (
        (4, rows, columns),
        (4, rows, columns),
        (2, rows, wide),
        (2, high, columns),
        (4, high, wide),
        (4, high, wide),
        (3, high, wide),
    )
    return [pltpu.VMEM(shape, grad.dtype) for shape in shapes]


def share_scratch(share):
    return [
        pltpu.VMEM(share.shape, share.dtype),
        pltpu.VMEM((3, *quarter_shape(*share.shape)), share.dtype),
    ]


def reduce_kernel(*refs, whole, partly):
    count = whole + partly
    grads, outs, refs = refs[:count], refs[count : 2 * count], refs[2 * count :]
    sems, group_sems, refs = refs[0], refs[1], refs[2:]
    jobs = [
        Whole(grads[i], outs[i], refs[7 * i : 7 * i + 7], sems.at[i]) for i in range(whole)
    ]
    refs = refs[7 * whole :]
    shares = [
        GroupReduce(grads[whole + i], outs[whole + i], refs[2 * i : 2 * i + 2], group_sems.at[i])
        for i in range(partly)
    ]
    greet()
    run_stages([*jobs, *shares], STAGES[:1])
    run_stages(shares, STAGES[1:2])
    run_stages(jobs, STAGES[1:3])
    run_stages(shares, STAGES[3:4])
    run_stages(jobs, STAGES[3:5])
    run_stages([*shares, *jobs], STAGES[5:])


def transfer_cost(size):
    return pl.CostEstimate(flops=4000 * size, bytes_accessed=2 * size, transcendentals=0)


def reduce_call(grads, shares, collective_id):
    in_vmem = pl.BlockSpec(memory_space=pltpu.VMEM)
    whole, partly = len(grads), len(shares)
    scratch = [
        pltpu.SemaphoreType.DMA((whole, WHOLE_SEMS)),
        pltpu.SemaphoreType.DMA((partly, GROUP_SEMS)),
    ]
    for grad in grads:
        scratch.extend(stepped_scratch(grad))
    for share in shares:
        scratch.extend(share_scratch(share))
    out_shape = [jax.ShapeDtypeStruct(g.shape[1:], g.dtype) for g in grads]
    out_shape += [jax.ShapeDtypeStruct(s.shape, s.dtype) for s in shares]
    return pl.pallas_call(
        functools.partial(reduce_kernel, whole=whole, partly=partly),
        in_specs=[ANYWHERE] * (whole + partly),
        out_specs=[in_vmem] * (whole + partly),
        out_shape=out_shape,
        scratch_shapes=scratch,
        compiler_params=pltpu.CompilerParams(
            collective_id=collective_id, has_side_effects=True, vmem_limit_bytes=VMEM_LIMIT
        ),
        cost_estimate=NO_COST,
        name="reduce_gradients",
    )(*grads, *shares)


def finish_kernel(*refs, done, partly):
    finished, refs = refs[:done], refs[done:]
    shares, small, refs = refs[:partly], refs[partly], refs[partly + 1 :]
    outs, small_out, full, refs = refs[:partly], refs[partly], refs[partly + 1], refs[partly + 2 :]
    sems, group_sems, spread_sems, refs = refs[0], refs[1], refs[2], refs[3:]
    job = Reduce(small, small_out, refs[:5], sems)
    refs = refs[5:]
    jobs = [
        GroupReduce(shares[i], outs[i], refs[2 * i : 2 * i + 2], group_sems.at[i])
        for i in range(partly)
    ]
    greet()
    run_stages([job, *jobs], STAGES[:3])
    total = sum(squares_in(out) for out in finished)
    run_stages([*jobs, job], STAGES[3:6])
    total = total + sum(squares_in(out) for out in outs)
    _, level, core = place()
    mine = 2 * level + core
    last = small_out.shape[0] - 1
    full[mine] = small_out[...]
    full[mine, last : last + 1, :] = total
    Spread(full, spread_sems).run()
    run_stages([job, *jobs], STAGES[6:])


def finish_call(finished, shares, small, collective_id):
    done, partly = len(finished), len(shares)
    in_vmem = pl.BlockSpec(memory_space=pltpu.VMEM)
    scratch = [
        pltpu.SemaphoreType.DMA((REDUCE_SEMS,)),
        pltpu.SemaphoreType.DMA((partly, GROUP_SEMS)),
        pltpu.SemaphoreType.DMA((14,)),
        *whole_scratch(small),
    ]
    for share in shares:
        scratch.extend(share_scratch(share))
    out_shape = [jax.ShapeDtypeStruct(s.shape, s.dtype) for s in shares]
    out_shape.append(jax.ShapeDtypeStruct(small.shape[1:], small.dtype))
    out_shape.append(jax.ShapeDtypeStruct(small.shape, small.dtype))
    return pl.pallas_call(
        functools.partial(finish_kernel, done=done, partly=partly),
        in_specs=[in_vmem] * done + [ANYWHERE] * (partly + 1),
        out_specs=[in_vmem] * len(out_shape),
        out_shape=out_shape,
        scratch_shapes=scratch,
        compiler_params=pltpu.CompilerParams(
            collective_id=collective_id, has_side_effects=True, vmem_limit_bytes=VMEM_LIMIT
        ),
        name="finish_gradients",
    )(*finished, *shares, small)


def with_kernels():
    return lax.axis_size("dp") == 4 and lax.axis_size("fsdp") == 8


def reduce_all(grads, shares, collective_id):
    if with_kernels():
        return reduce_call(grads, shares, collective_id)
    return [lax.psum(scatter(grad), "dp") for grad in grads] + sum_shares(shares)


def sum_shares(shares):
    return [lax.psum(share, "dp") for share in shares]


def finish_all(finished, shares, small, collective_id):
    if with_kernels():
        return finish_call(finished, shares, small, collective_id)
    outs = [lax.psum(share, "dp") for share in shares]
    own = lax.psum(scatter(small), "dp")
    total = sum(jnp.sum(jnp.square(out.astype(jnp.float32))) for out in (*finished, *outs))
    row = jnp.full((1, LANES), 1.0 / LANES, jnp.float32) * total
    return [*outs, own, lax.all_gather(own.at[-1:].set(row), "fsdp", axis=0)]


def take(items, *counts):
    cut = []
    for count in counts:
        cut.append(items[:count])
        items = items[count:]
    return cut


def scatter(grad):
    return lax.psum_scatter(grad, "fsdp", scatter_dimension=0)


def by_owner(grad, low=jnp.bfloat16):
    owners = lax.axis_size("fsdp")
    return grad.astype(low).reshape(owners, grad.shape[0] // owners, grad.shape[1])


def attention_forward_kernel(
    q_ref, k_ref, v_ref, seg_col_ref, seg_row_ref, out_ref, expo_ref, inv_ref, *, block
):
    rows = q_ref.shape[0]
    lower = lax.broadcasted_iota(jnp.int32, (block, PAIR), 1) < HD
    keys = k_ref[...]
    values = jnp.concatenate([v_ref[...], jnp.ones((rows, PAIR), v_ref.dtype)], 1)
    seg_row = seg_row_ref[...]
    tasks = [(step, head) for step in range(rows // block) for head in range(2)]

    def scores_of(step, head):
        query = q_ref[step * block : (step + 1) * block, :] * jnp.bfloat16(HD**-0.5)
        keep = lower if head == 0 else jnp.logical_not(lower)
        return mul_nt(jnp.where(keep, query, jnp.bfloat16(0)), keys)

    scores = scores_of(*tasks[0])
    outs = []
    for index, (step, head) in enumerate(tasks):
        following = scores_of(*tasks[index + 1]) if index + 1 < len(tasks) else None
        at = slice(step * block, (step + 1) * block)
        scores = jnp.where(seg_col_ref[at, :] == seg_row, scores, MASKED)
        highest = jnp.max(scores, -1, keepdims=True)
        low = jnp.exp(scores - highest).astype(jnp.bfloat16)
        expo_ref[head, at, :] = low
        outs.append(mul(low, values))
        if head:
            inverse = 1.0 / jnp.where(lower, outs[0][:, PAIR:], outs[1][:, PAIR:])
            sums = jnp.where(lower, outs[0][:, :PAIR], outs[1][:, :PAIR])
            out_ref[at, :] = (sums * inverse).astype(jnp.bfloat16)
            inv_ref[at, :] = inverse
            outs = []
        scores = following


def attention_forward(qkv_rows, segment, rides, collective_id):
    rows = qkv_rows.shape[0]
    pairs = HEADS // 2
    wide = lambda base: pl.BlockSpec((rows, PAIR), lambda j, base=base: (0, base + j))
    return block_call(
        functools.partial(attention_forward_kernel, block=min(256, rows)),
        pairs,
        [wide(0), wide(pairs), wide(2 * pairs), fixed(rows, 1), fixed(1, rows)],
        [qkv_rows, qkv_rows, qkv_rows, segment[:, None], segment[None, :]],
        [wide(0), pl.BlockSpec((2, rows, rows), lambda j: (j, 0, 0)), wide(0)],
        [
            shape_of(rows, D, dtype=LOW),
            shape_of(HEADS, rows, rows, dtype=LOW),
            shape_of(rows, D),
        ],
        [],
        26,
        "attention_forward",
        work(16 * HEADS * rows * rows * HD, 2 * HEADS * rows * rows + 12 * rows * D),
        rides,
        collective_id,
    )


def attention_backward_kernel(
    q_ref, k_ref, v_ref, expo_ref, inv_ref, out_ref, grad_ref, dqkv_ref, *, block
):
    rows = q_ref.shape[0]
    pair = pl.program_id(0)
    lower = lax.broadcasted_iota(jnp.int32, (block, PAIR), 1) < HD
    keys = k_ref[...]
    values = v_ref[...]
    scale = HD**-0.5
    scaled_grad = (grad_ref[...].astype(jnp.float32) * inv_ref[...]).astype(jnp.bfloat16)
    query = q_ref[...]
    query_t = query.T
    grad_t = scaled_grad.T
    product = scaled_grad.astype(jnp.float32) * out_ref[...].astype(jnp.float32)
    key_t = [None, None]
    value_t = [None, None]
    tasks = [(step, head) for step in range(rows // block) for head in range(2)]

    def probs_grad_of(step, head):
        keep = lower if head == 0 else jnp.logical_not(lower)
        mine = scaled_grad[step * block : (step + 1) * block]
        return mul_nt(jnp.where(keep, mine, jnp.bfloat16(0)), values)

    probs_grad = probs_grad_of(*tasks[0])
    query_parts = []
    for index, (step, head) in enumerate(tasks):
        following = probs_grad_of(*tasks[index + 1]) if index + 1 < len(tasks) else None
        at = slice(step * block, (step + 1) * block)
        lanes = slice(head * HD, (head + 1) * HD)
        keep = lower if head == 0 else jnp.logical_not(lower)
        inner = jnp.sum(jnp.where(keep, product[at], 0.0), -1, keepdims=True)
        low = expo_ref[head, at, :]
        value_part = mul(grad_t[lanes, at], low)
        scores_grad = (low.astype(jnp.float32) * (probs_grad - inner)).astype(jnp.bfloat16)
        query_parts.append(mul(scores_grad, keys))
        key_part = mul(query_t[lanes, at], scores_grad)
        key_t[head] = key_part if step == 0 else key_t[head] + key_part
        value_t[head] = value_part if step == 0 else value_t[head] + value_part
        if head:
            query_grad = jnp.where(lower, query_parts[0], query_parts[1]) * scale
            dqkv_ref[at, pl.ds(pl.multiple_of(pair * PAIR, PAIR), PAIR)] = query_grad.astype(
                jnp.bfloat16
            )
            query_parts = []
        probs_grad = following
    key_grad = (jnp.concatenate(key_t, 0) * scale).T
    value_grad = jnp.concatenate(value_t, 0).T
    dqkv_ref[:, pl.ds(pl.multiple_of(D + pair * PAIR, PAIR), PAIR)] = key_grad.astype(jnp.bfloat16)
    dqkv_ref[:, pl.ds(pl.multiple_of(2 * D + pair * PAIR, PAIR), PAIR)] = value_grad.astype(jnp.bfloat16)


def attention_backward(qkv_rows, expo, inverse, attended, attended_grad, rides, collective_id):
    rows = qkv_rows.shape[0]
    pairs = HEADS // 2
    wide = lambda base: pl.BlockSpec((rows, PAIR), lambda j, base=base: (0, base + j))
    return block_call(
        functools.partial(attention_backward_kernel, block=min(256, rows)),
        pairs,
        [
            wide(0),
            wide(pairs),
            wide(2 * pairs),
            pl.BlockSpec((2, rows, rows), lambda j: (j, 0, 0)),
            wide(0),
            wide(0),
            wide(0),
        ],
        [qkv_rows, qkv_rows, qkv_rows, expo, inverse, attended, attended_grad],
        [fixed(rows, 3 * D)],
        [shape_of(rows, 3 * D, dtype=LOW)],
        [],
        34,
        "attention_backward",
        None,
        rides,
        collective_id,
    )


def mul(left, right):
    return jnp.dot(left, right, preferred_element_type=jnp.float32)


def mul_nt(left, right):
    return lax.dot_general(left, right, NT, preferred_element_type=jnp.float32)


def normalized(values):
    center = values - jnp.mean(values, -1, keepdims=True)
    inverse = lax.rsqrt(jnp.mean(center * center, -1, keepdims=True) + NORM_EPS)
    return center * inverse, inverse


def norm_backward(grad, values, gain):
    unit, inverse = normalized(values)
    inner = grad * gain
    mean_inner = jnp.mean(inner, -1, keepdims=True)
    mean_cross = jnp.mean(inner * unit, -1, keepdims=True)
    value_grad = inverse * (inner - mean_inner - unit * mean_cross)
    return value_grad, column_sum(grad * unit), column_sum(grad)


def column_sum(rows):
    return jnp.sum(rows.astype(jnp.float32), 0, keepdims=True)


def at_first(action):
    pl.when(pl.program_id(0) == 0)(action)


def accumulate(out_ref, parts):
    value = jnp.concatenate(parts, 1)

    @pl.when(pl.program_id(0) == 0)
    def _():
        out_ref[...] = value

    @pl.when(pl.program_id(0) > 0)
    def _():
        out_ref[...] += value


def rows_of(block, columns):
    return pl.BlockSpec((block, columns), lambda i: (i, 0))


def fixed(*shape):
    return pl.BlockSpec(shape, lambda i: (0,) * len(shape), pipeline_mode=pl.Buffered(1))


def loads(sources, targets, sems):
    return [
        pltpu.make_async_copy(source, target, sems.at[index])
        for index, (source, target) in enumerate(zip(sources, targets))
    ]


def shape_of(*shape, dtype=jnp.float32):
    return jax.ShapeDtypeStruct(shape, dtype)


def embed_kernel(pixel_ref, weight_ref, pos_ref, table_ref, bias_ref, out_ref):
    position = jnp.dot(
        pos_ref[...], table_ref[...], precision=HIGHEST, preferred_element_type=jnp.float32
    )
    out_ref[...] = mul(pixel_ref[...], weight_ref[...]) + bias_ref[...] + position


def embed(pixels, weight, pos_weights, table, bias):
    rows, depth = pixels.shape
    block = 256
    nodes = pos_weights.shape[1]
    return block_call(
        embed_kernel,
        rows // block,
        [rows_of(block, depth), fixed(depth, D), rows_of(block, nodes), fixed(nodes, D), fixed(1, D)],
        [pixels, weight, pos_weights, table, bias],
        [rows_of(block, D)],
        [shape_of(rows, D)],
        [],
        18,
        "embed",
        work(2 * rows * depth * D, 2 * rows * depth + 2 * depth * D + 4 * rows * D),
    )[0]


def qkv_kernel(stream_ref, weight_ref, vector_ref, normed_ref, qkv_ref):
    unit, _ = normalized(stream_ref[...])
    normed = (unit * vector_ref[:, :D] + vector_ref[:, D : 2 * D]).astype(jnp.bfloat16)
    normed_ref[...] = normed
    bias = vector_ref[:, 4 * D : 7 * D]
    qkv_ref[...] = (mul(normed, weight_ref[...]) + bias).astype(jnp.bfloat16)


def qkv_forward(stream, weight, vector):
    rows = stream.shape[0]
    block = 256
    low = jnp.bfloat16
    return block_call(
        qkv_kernel,
        rows // block,
        [rows_of(block, D), fixed(D, 3 * D), fixed(1, vector.shape[1])],
        [stream, weight, vector],
        [rows_of(block, D), rows_of(block, 3 * D)],
        [shape_of(rows, D, dtype=low), shape_of(rows, 3 * D, dtype=low)],
        [],
        16,
        "qkv_forward",
        work(6 * rows * D * D, 14 * rows * D + 6 * D * D),
    )


def mlp_kernel(
    stream_ref, attended_ref, up_full, proj_out, vector_ref,
    residual_ref, normed_ref, active_ref, slope_ref, out_ref,
    mix_ref, up_ref, down_ref, sems,
):
    width = up_ref.shape[1]
    copies = loads(
        (proj_out.at[pl.ds(0, D)], up_full, proj_out.at[pl.ds(D, width)]),
        (mix_ref, up_ref, down_ref),
        sems,
    )

    @at_first
    def _():
        for copy in copies:
            copy.start()
        copies[0].wait()

    residual = stream_ref[...] + mul(attended_ref[...], mix_ref[...]) + vector_ref[:, 7 * D : 8 * D]
    residual_ref[...] = residual
    unit, _ = normalized(residual)
    normed = (unit * vector_ref[:, 2 * D : 3 * D] + vector_ref[:, 3 * D : 4 * D]).astype(jnp.bfloat16)
    normed_ref[...] = normed
    at_first(copies[1].wait)
    part = 512

    def hidden_of(base):
        bias = vector_ref[:, 9 * D + base : 9 * D + base + part]
        return mul(normed, up_ref[:, base : base + part]) + bias

    hidden = hidden_of(0)
    for base in range(0, width, part):
        following = hidden_of(base + part) if base + part < width else None
        columns = slice(base, base + part)
        square = hidden * hidden
        half = 0.5 + 0.5 * jnp.tanh(hidden * (ROOT + (ROOT * CUBE) * square))
        active = hidden * half
        active_ref[:, columns] = active.astype(jnp.bfloat16)
        rise = (2.0 * ROOT) + (6.0 * ROOT * CUBE) * square
        slope_ref[:, columns] = (half + active * (1.0 - half) * rise).astype(jnp.bfloat16)
        hidden = following
    at_first(copies[2].wait)
    out_ref[...] = residual + mul(active_ref[...], down_ref[...]) + vector_ref[:, 8 * D : 9 * D]


def mlp_forward(stream, attended, up, proj_out, vector, rides, collective_id):
    rows = stream.shape[0]
    width = up.shape[1]
    block = 256
    low = jnp.bfloat16
    return block_call(
        mlp_kernel,
        rows // block,
        [rows_of(block, D), rows_of(block, D), ANYWHERE, ANYWHERE, fixed(1, vector.shape[1])],
        [stream, attended, up, proj_out, vector],
        [rows_of(block, D), rows_of(block, D), rows_of(block, width), rows_of(block, width), rows_of(block, D)],
        [
            shape_of(rows, D),
            shape_of(rows, D, dtype=low),
            shape_of(rows, width, dtype=low),
            shape_of(rows, width, dtype=low),
            shape_of(rows, D),
        ],
        [
            pltpu.VMEM((D, D), low),
            pltpu.VMEM((D, width), low),
            pltpu.VMEM((width, D), low),
            pltpu.SemaphoreType.DMA((3,)),
        ],
        30,
        "mlp_forward",
        work(2 * rows * D * (D + 2 * width), rows * (16 * D + 4 * width) + 2 * D * (D + 2 * width)),
        rides,
        collective_id,
    )


def mlp_back_kernel(
    grad_ref, slope_ref, residual_ref, up_full, proj_out, vector_ref,
    low_ref, hidden_ref, out_ref, out_low_ref, attended_ref, sums_ref,
    mix_ref, up_ref, down_ref, sems,
):
    width = up_ref.shape[1]
    copies = loads(
        (proj_out.at[pl.ds(D, width)], up_full, proj_out.at[pl.ds(0, D)]),
        (down_ref, up_ref, mix_ref),
        sems,
    )

    @at_first
    def _():
        for copy in copies:
            copy.start()
        copies[0].wait()

    grad = grad_ref[...]
    grad_low = grad.astype(jnp.bfloat16)
    low_ref[...] = grad_low
    part = 512
    hidden_sums = []
    active_grad = mul_nt(grad_low, down_ref[:part, :])
    for base in range(0, width, part):
        following = None
        if base + part < width:
            following = mul_nt(grad_low, down_ref[base + part : base + 2 * part, :])
        columns = slice(base, base + part)
        hidden_grad = (active_grad * slope_ref[:, columns].astype(jnp.float32)).astype(jnp.bfloat16)
        hidden_ref[:, columns] = hidden_grad
        hidden_sums.append(column_sum(hidden_grad))
        active_grad = following
    at_first(copies[1].wait)
    second_grad = mul_nt(hidden_ref[...], up_ref[...])
    value_grad, gain_grad, shift_grad = norm_backward(
        second_grad, residual_ref[...], vector_ref[:, 2 * D : 3 * D]
    )
    total = value_grad + grad
    out_ref[...] = total
    total_low = total.astype(jnp.bfloat16)
    out_low_ref[...] = total_low
    at_first(copies[2].wait)
    attended_ref[...] = mul_nt(total_low, mix_ref[...]).astype(jnp.bfloat16)
    accumulate(
        sums_ref,
        [gain_grad, shift_grad, column_sum(total_low), column_sum(grad_low), *hidden_sums],
    )


def mlp_backward(grad, slope, residual, up, proj_out, vector):
    rows = grad.shape[0]
    width = up.shape[1]
    block = 256
    low = jnp.bfloat16
    narrow = rows_of(block, D)
    return block_call(
        mlp_back_kernel,
        rows // block,
        [narrow, rows_of(block, width), narrow, ANYWHERE, ANYWHERE, fixed(1, vector.shape[1])],
        [grad, slope, residual, up, proj_out, vector],
        [narrow, rows_of(block, width), narrow, narrow, narrow, fixed(1, 4 * D + width)],
        [
            shape_of(rows, D, dtype=low),
            shape_of(rows, width, dtype=low),
            shape_of(rows, D),
            shape_of(rows, D, dtype=low),
            shape_of(rows, D, dtype=low),
            shape_of(1, 4 * D + width),
        ],
        [
            pltpu.VMEM((D, D), low),
            pltpu.VMEM((D, width), low),
            pltpu.VMEM((width, D), low),
            pltpu.SemaphoreType.DMA((3,)),
        ],
        30,
        "mlp_backward",
        None,
    )


def qkv_back_kernel(grad_ref, residual_ref, stream_ref, weight_ref, vector_ref, out_ref, sums_ref):
    grad = grad_ref[...]
    normed_grad = mul_nt(grad, weight_ref[...])
    value_grad, gain_grad, shift_grad = norm_backward(normed_grad, stream_ref[...], vector_ref[:, :D])
    out_ref[...] = residual_ref[...] + value_grad
    accumulate(sums_ref, [gain_grad, shift_grad, column_sum(grad)])


def qkv_backward(grad, residual_grad, stream, weight, vector):
    rows = stream.shape[0]
    block = 256
    narrow = rows_of(block, D)
    return block_call(
        qkv_back_kernel,
        rows // block,
        [rows_of(block, 3 * D), narrow, narrow, fixed(D, 3 * D), fixed(1, vector.shape[1])],
        [grad, residual_grad, stream, weight, vector],
        [narrow, fixed(1, 5 * D)],
        [shape_of(rows, D), shape_of(1, 5 * D)],
        [],
        16,
        "qkv_backward",
        None,
    )


def input_grad_kernel(first_ref, second_ref, qkv_ref, hidden_ref, qkv_out, up_out, left_ref, *, cut):
    step = pl.program_id(0)

    @pl.when(step == 0)
    def _():
        left_ref[...] = first_ref[...].T

    @pl.when(step == cut)
    def _():
        left_ref[...] = second_ref[...].T

    @pl.when(step < cut)
    def _():
        qkv_out[...] = mul(left_ref[...], qkv_ref[...]).astype(jnp.bfloat16)

    @pl.when(step >= cut)
    def _():
        up_out[...] = mul(left_ref[...], hidden_ref[...]).astype(jnp.bfloat16)


def input_weight_grad(first, second, qkv_grad, hidden_grad):
    rows = first.shape[0]
    cut = qkv_grad.shape[1] // D
    steps = cut + hidden_grad.shape[1] // D
    before = lambda i: (0, jnp.minimum(i, cut - 1))
    after = lambda i: (0, jnp.maximum(i - cut, 0))
    return block_call(
        functools.partial(input_grad_kernel, cut=cut),
        steps,
        [
            fixed(rows, D),
            fixed(rows, D),
            pl.BlockSpec((rows, D), before),
            pl.BlockSpec((rows, D), after),
        ],
        [first, second, qkv_grad, hidden_grad],
        [pl.BlockSpec((D, D), before), pl.BlockSpec((D, D), after)],
        [
            shape_of(D, qkv_grad.shape[1], dtype=jnp.bfloat16),
            shape_of(D, hidden_grad.shape[1], dtype=jnp.bfloat16),
        ],
        [pltpu.VMEM((D, rows), jnp.bfloat16)],
        24,
        "input_weight_grad",
        None,
    )


def output_grad_kernel(attended_ref, active_ref, residual_ref, grad_ref, *outs, cut):
    step = pl.program_id(0)

    def store(product):
        base = 0
        for out in outs:
            out[...] = product[:, base : base + out.shape[1]].astype(jnp.bfloat16)
            base += out.shape[1]

    @pl.when(step < cut)
    def _():
        store(mul(attended_ref[...].T, residual_ref[...]))

    @pl.when(step >= cut)
    def _():
        store(mul(active_ref[...].T, grad_ref[...]))


def output_weight_grad(attended, active, residual_low, grad_low, parts):
    rows = attended.shape[0]
    block = 768
    cut = attended.shape[1] // block
    steps = cut + active.shape[1] // block
    return block_call(
        functools.partial(output_grad_kernel, cut=cut),
        steps,
        [
            pl.BlockSpec((rows, block), lambda i: (0, jnp.minimum(i, cut - 1))),
            pl.BlockSpec((rows, block), lambda i: (0, jnp.maximum(i - cut, 0))),
            fixed(rows, D),
            fixed(rows, D),
        ],
        [attended, active, residual_low, grad_low],
        [rows_of(block, part) for part in parts],
        [shape_of(steps * block, part, dtype=LOW) for part in parts],
        [],
        24,
        "output_weight_grad",
    )


def embed_back_kernel(pixel_ref, grad_ref, pos_ref, out_ref, table_ref, bias_ref, low_ref):
    @at_first
    def _():
        grad = grad_ref[...]
        low = grad.astype(jnp.bfloat16)
        low_ref[...] = low
        bias_ref[...] = column_sum(low)
        table_ref[...] = jnp.dot(
            pos_ref[...], grad, precision=HIGHEST, preferred_element_type=jnp.float32
        )

    out_ref[...] = mul(pixel_ref[...].T, low_ref[...]).astype(jnp.bfloat16)


def embed_backward(pixels, grad, pos_weights_t):
    rows, depth = pixels.shape
    block = 768
    nodes = pos_weights_t.shape[0]
    return block_call(
        embed_back_kernel,
        depth // block,
        [pl.BlockSpec((rows, block), lambda i: (0, i)), fixed(rows, D), fixed(nodes, rows)],
        [pixels, grad, pos_weights_t],
        [rows_of(block, D), fixed(nodes, D), fixed(1, D)],
        [shape_of(depth, D, dtype=jnp.bfloat16), shape_of(nodes, D), shape_of(1, D)],
        [pltpu.VMEM((rows, D), jnp.bfloat16)],
        20,
        "embed_backward",
        None,
    )


def adam_update(gradient, moment, square, weight, factor, learn_rate):
    clipped = gradient * factor
    moment = BETA_ONE * moment + (1.0 - BETA_ONE) * clipped
    square = BETA_TWO * square + (1.0 - BETA_TWO) * clipped * clipped
    fixed_one = 1.0 - BETA_ONE**STEP
    fixed_two = 1.0 - BETA_TWO**STEP
    step_dir = (
        moment / fixed_one / (jnp.sqrt(square / fixed_two) + ADAM_EPS) + WEIGHT_DECAY * weight
    )
    return (moment, square, weight - learn_rate * step_dir)


def body(
    pixels,
    segment,
    patch_size,
    labels,
    patch_kernel,
    head_weight,
    input_proj,
    output_proj,
    layer_vector,
    position_table,
    global_vector,
    patch_moment,
    head_moment,
    input_moment,
    output_moment,
    layer_moment,
    position_moment,
    global_moment,
    patch_square,
    head_square,
    input_square,
    output_square,
    layer_square,
    position_square,
    global_square,
):
    pos_weights, member, counts = row_layout(segment, patch_size[0])
    owners = lax.axis_size("fsdp")
    nodes = pos_weights.shape[1]
    pos_weights = jnp.pad(pos_weights, ((0, 0), (0, -nodes % 64)))
    vector_size = layer_vector.size
    (kernel_full, vectors, qkv_zero), rides, rest_shards = gather_first(
        patch_kernel,
        padded_rows(layer_vector.astype(LOW).reshape(-1), 32),
        input_proj,
        output_proj,
        head_weight,
    )
    vectors = vectors.reshape(owners, -1)[:, :vector_size].reshape(owners, *layer_vector.shape)
    vectors = jnp.swapaxes(vectors, 0, 1).reshape(LAYERS, 1, -1).astype(jnp.float32)
    output_zero, up_one, head_full = (
        lax.all_gather(shard, "fsdp", axis=0, tiled=True) for shard in rest_shards
    )
    global_low = rounded(global_vector)
    position_low = jnp.pad(rounded(position_table), ((0, -nodes % 64), (0, 0)))
    stream = embed(pixels, kernel_full, pos_weights, position_low, global_low[None, :D])
    saved_layers = []
    qkv_weight = qkv_zero
    for index in range(LAYERS):
        vector = vectors[index]
        normed, qkv_rows = qkv_forward(stream, qkv_weight, vector)
        attended, expo, inverse, fetched = attention_forward(
            qkv_rows, segment, [rides[0] if index == 0 else rides[2]], 4 + index
        )
        up, output = (fetched, output_zero) if index == 0 else (up_one, fetched)
        residual, normed_second, active, slope, following, *fetched = mlp_forward(
            stream, attended, up, output, vector, rides[1:2] if index == 0 else (), 7
        )
        saved_layers.append(
            (
                (qkv_weight, up, output, vector),
                (stream, normed, qkv_rows, attended, expo, inverse),
                (residual, normed_second, active, slope),
            )
        )
        stream = following
        if fetched:
            (qkv_weight,) = fetched
    final_norm, final_back = jax.vjp(
        layer_norm, stream, global_low[D : 2 * D], global_low[2 * D : 3 * D]
    )
    image_sizes = jnp.maximum(counts, 1.0)
    pooled = (jnp.dot(member.T, final_norm, precision=HIGHEST) / image_sizes[:, None]).astype(
        jnp.bfloat16
    )
    logits = matmul(pooled, head_full) + global_low[3 * D :]
    highest = jnp.max(logits, -1, keepdims=True)
    exponent = jnp.exp(logits - highest)
    totals = jnp.sum(exponent, -1, keepdims=True)
    logsum = (highest + jnp.log(totals))[:, 0]
    onehot = labels[0][:, None] == jnp.arange(CLS, dtype=jnp.int32)[None, :]
    picked = jnp.sum(jnp.where(onehot, logits, 0.0), 1)
    loss_local = jnp.sum(counts * (logsum - picked))
    logits_grad = ((exponent / totals - onehot.astype(jnp.float32)) * counts[:, None]).astype(
        jnp.bfloat16
    )
    head_grad = matmul(pooled.T, logits_grad).astype(LOW)
    head_part = scatter(by_owner(jnp.pad(head_grad, ((0, 0), (0, -CLS % LANES)))))
    pooled_grad = matmul(logits_grad, head_full.T)
    final_grad = jnp.dot(member, pooled_grad / image_sizes[:, None], precision=HIGHEST)
    stream_grad, final_gain, final_shift = final_back(final_grad)
    vector_grads = [None] * LAYERS
    early_parts, late_parts = [head_part], []
    for index in reversed(range(LAYERS)):
        (qkv_weight, up, output, vector), first, second = saved_layers[index]
        entering, normed, qkv_rows, attended, expo, inverse = first
        residual, normed_second, active, slope = second
        grad_low, hidden_grad, residual_grad, residual_low, attended_grad, mlp_sums = mlp_backward(
            stream_grad, slope, residual, up, output, vector
        )
        output_grads = output_weight_grad(
            attended, active, residual_low, grad_low, (D // 3,) * 3 if index else (D,)
        )
        attended_grad, *output_grads = lax.optimization_barrier((attended_grad, *output_grads))
        output_parts = [scatter(by_owner(grad)) for grad in output_grads]
        if index:
            early_parts.extend(output_parts)
        else:
            (last_part,) = output_parts
        qkv_grad, *early_sums = attention_backward(
            qkv_rows,
            expo,
            inverse,
            attended,
            attended_grad,
            () if index else [ShareRide(part) for part in early_parts],
            6,
        )
        stream_grad, qkv_sums = qkv_backward(qkv_grad, residual_grad, entering, qkv_weight, vector)
        input_grads = input_weight_grad(normed, normed_second, qkv_grad, hidden_grad)
        if index:
            stream_grad, *input_grads = lax.optimization_barrier((stream_grad, *input_grads))
            late_parts.extend(scatter(by_owner(grad)) for grad in input_grads)
        vector_grads[index] = jnp.concatenate(
            [
                qkv_sums[0, : 2 * D],
                mlp_sums[0, : 2 * D],
                qkv_sums[0, 2 * D :],
                mlp_sums[0, 2 * D :],
            ]
        )
    kernel_grad, position_grad, bias_grad = embed_backward(pixels, stream_grad, pos_weights.T)
    position_grad = position_grad[:nodes]
    vector_part = jnp.stack(vector_grads).reshape(LAYERS, owners, -1)
    vector_part = jnp.swapaxes(vector_part, 0, 1).reshape(owners, vector_size)
    vector_rows = -(-vector_size // LANES)
    vector_part = jnp.pad(vector_part, ((0, 0), (0, vector_rows * LANES - vector_size)))
    rest = jnp.concatenate(
        [
            position_grad.reshape(-1),
            bias_grad[0],
            final_gain,
            final_shift,
            jnp.sum(logits_grad.astype(jnp.float32), 0),
            loss_local[None],
            jnp.sum(counts)[None],
        ]
    )
    rest_rows = -(-rest.shape[0] // (owners * LANES))
    rest_part = jnp.pad(rest, (0, rest_rows * owners * LANES - rest.shape[0]))
    small = jnp.concatenate([vector_part, rest_part.reshape(owners, -1)], 1)
    used = vector_rows + rest_rows
    block_rows = (used // 64 + 1) * 64
    small = jnp.pad(small.reshape(owners, used, LANES), ((0, 0), (0, block_rows - used), (0, 0)))
    input_zero_sums, kernel_sum, input_one_sums = take(
        reduce_all([by_owner(grad) for grad in (*input_grads, kernel_grad)], late_parts, 2), 2, 1, 2
    )
    output_zero_sum, small_share, small_full = finish_all(
        [*early_sums, *input_zero_sums, *kernel_sum, *input_one_sums], [last_part], small, 3
    )
    head_sum, output_one_sums = early_sums[0], early_sums[1:]
    rest_sum = small_full[:, vector_rows:used].reshape(-1)
    position_sum = rest_sum[: position_grad.size].reshape(position_grad.shape)
    global_sum = rest_sum[position_grad.size :][: global_vector.shape[0]]
    loss_sum = rest_sum[rest.shape[0] - 2]
    token_total = rest_sum[rest.shape[0] - 1]
    kernel_sum = kernel_sum[0].astype(jnp.float32)
    head_sum = head_sum[:, :CLS].astype(jnp.float32)
    input_sum = jnp.stack(
        [jnp.concatenate(pair, 1) for pair in (input_zero_sums, input_one_sums)]
    ).astype(jnp.float32)
    output_sum = jnp.stack([output_zero_sum, jnp.concatenate(output_one_sums, 1)]).astype(
        jnp.float32
    )
    vector_sum = small_share[:vector_rows].reshape(-1)[:vector_size].reshape(layer_vector.shape)
    grad_norm = (
        jnp.sqrt(
            jnp.sum(small_full[:, -1])
            + jnp.sum(jnp.square(small_full[:, :vector_rows]))
            + jnp.sum(position_sum * position_sum)
            + jnp.sum(global_sum * global_sum)
        )
        / token_total
    )
    factor = jnp.minimum(1.0, CLIP_NORM / grad_norm) / token_total
    patch_next = adam_update(
        kernel_sum, patch_moment, patch_square, patch_kernel, factor, LEARN_RATE
    )
    head_next = adam_update(head_sum, head_moment, head_square, head_weight, factor, LEARN_RATE)
    input_next = adam_update(input_sum, input_moment, input_square, input_proj, factor, LEARN_RATE)
    output_next = adam_update(
        output_sum, output_moment, output_square, output_proj, factor, LEARN_RATE
    )
    layer_next = adam_update(
        vector_sum, layer_moment, layer_square, layer_vector, factor, VECTOR_RATE
    )
    position_next = adam_update(
        position_sum, position_moment, position_square, position_table, factor, LEARN_RATE
    )
    global_next = adam_update(
        global_sum, global_moment, global_square, global_vector, factor, VECTOR_RATE
    )
    return (
        loss_sum,
        token_total,
        grad_norm,
        patch_next[0],
        head_next[0],
        input_next[0],
        output_next[0],
        layer_next[0],
        position_next[0],
        global_next[0],
        patch_next[1],
        head_next[1],
        input_next[1],
        output_next[1],
        layer_next[1],
        position_next[1],
        global_next[1],
        patch_next[2],
        head_next[2],
        input_next[2],
        output_next[2],
        layer_next[2],
        position_next[2],
        global_next[2],
    )


def solution(mesh):
    in_specs = (
        P(("dp", "fsdp"), None),
        P(("dp", "fsdp")),
        P(("dp", "fsdp"), None),
        P(("dp", "fsdp"), None),
        P("fsdp", None),
        P("fsdp", None),
        P(None, "fsdp", None),
        P(None, "fsdp", None),
        P(None, "fsdp"),
        P(),
        P(),
        P("fsdp", None),
        P("fsdp", None),
        P(None, "fsdp", None),
        P(None, "fsdp", None),
        P(None, "fsdp"),
        P(),
        P(),
        P("fsdp", None),
        P("fsdp", None),
        P(None, "fsdp", None),
        P(None, "fsdp", None),
        P(None, "fsdp"),
        P(),
        P(),
    )
    out_specs = (
        P(),
        P(),
        P(),
        P("fsdp", None),
        P("fsdp", None),
        P(None, "fsdp", None),
        P(None, "fsdp", None),
        P(None, "fsdp"),
        P(),
        P(),
        P("fsdp", None),
        P("fsdp", None),
        P(None, "fsdp", None),
        P(None, "fsdp", None),
        P(None, "fsdp"),
        P(),
        P(),
        P("fsdp", None),
        P("fsdp", None),
        P(None, "fsdp", None),
        P(None, "fsdp", None),
        P(None, "fsdp"),
        P(),
        P(),
    )
    return jax.shard_map(body, mesh=mesh, in_specs=in_specs, out_specs=out_specs, check_vma=False)
```

```python
import functools

import jax
import jax.numpy as jnp
from jax import lax
from jax.experimental import pallas as pl
from jax.experimental.pallas import tpu as pltpu
from jax.sharding import PartitionSpec as P

D = 768
HEADS = 12
HD = 64
CLS = 1000
GRID = 7
IMG = 240
IMGS = 8
LAYERS = 2
STEP = 3


NORM_EPS = 1e-06
CLIP_NORM = 0.01
LEARN_RATE = 0.05
VECTOR_RATE = 0.25
BETA_ONE = 0.5
BETA_TWO = 0.5
ADAM_EPS = 1e-08
WEIGHT_DECAY = 0.05
HIGHEST = lax.Precision.HIGHEST

PAIR = 2 * HD
MASKED = -1e30
MIB = 1024 * 1024
VMEM_LIMIT = 56 * MIB
MESH = pl.DeviceIdType.MESH
LANES = 128
LOW = jnp.bfloat16
ANYWHERE = pl.BlockSpec(memory_space=pl.ANY)
NO_COST = pl.CostEstimate(flops=0, bytes_accessed=0, transcendentals=0)
ROOT = 0.7978845608028654
CUBE = 0.044715
NT = (((1,), (1,)), ((), ()))


def layer_norm(values, gain, shift):
    center = values - jnp.mean(values, -1, keepdims=True)
    spread = jnp.mean(center * center, -1, keepdims=True)
    return center * lax.rsqrt(spread + NORM_EPS) * gain + shift


def rounded(values):
    return lax.optimization_barrier(values.astype(jnp.bfloat16)).astype(jnp.float32)


def matmul(left, right):
    return jnp.dot(left, right, preferred_element_type=jnp.float32)


def padded_rows(flat, multiple):
    extra = -flat.shape[0] % (multiple * LANES)
    return jnp.pad(flat, (0, extra)).reshape(-1, LANES)


def row_layout(seg_row, patch_row):
    row_count = seg_row.shape[0]
    slots = jnp.arange(IMGS, dtype=jnp.int32)
    member = seg_row[:, None] == slots[None, :]
    counts = jnp.sum(member.astype(jnp.int32), 0, dtype=jnp.int32)
    starts = jnp.cumsum(counts, dtype=jnp.int32) - counts
    inside = jnp.any(member, 1)
    offset = jnp.arange(row_count, dtype=jnp.int32) - jnp.sum(
        jnp.where(member, starts[None, :], 0), 1, dtype=jnp.int32
    )
    offset = jnp.where(inside, offset, 0)
    patch_tok = jnp.sum(jnp.where(member, patch_row[None, :], 0), 1, dtype=jnp.int32) + jnp.where(
        inside, 0, IMG
    )
    side = IMG // patch_tok
    nodes = jnp.arange(GRID, dtype=jnp.int32).astype(jnp.float32)

    def hat(coord):
        place = ((2 * coord + 1) * GRID).astype(jnp.float32) / (2 * side).astype(jnp.float32) - 0.5
        place = jnp.clip(place, 0.0, GRID - 1.0)
        return jnp.maximum(1.0 - jnp.abs(place[:, None] - nodes[None, :]), 0.0)

    weights = (hat(offset // side)[:, :, None] * hat(offset % side)[:, None, :]).reshape(
        row_count, GRID * GRID
    )
    return (weights, member.astype(jnp.float32), counts.astype(jnp.float32))


TURNS = (1, 2, 3)


def place():
    slot = lax.axis_index("fsdp")
    return lax.axis_index("dp"), lax.div(slot, 2), lax.rem(slot, 2)


def partner(index, turn):
    if turn == 0:
        return index
    if turn == 1:
        return index + 1 - 2 * lax.rem(index, 2)
    if turn == 2:
        return lax.rem(index + 2, 4)
    return 3 - index


def greet():
    group, level, core = place()
    barrier = pltpu.get_barrier_semaphore()
    peers = [(group, 2 * level + 1 - core)]
    for turn in TURNS:
        peers.append((group, 2 * partner(level, turn) + core))
        peers.append((partner(group, turn), 2 * level + core))
    for peer in peers:
        pl.semaphore_signal(barrier, inc=1, device_id=peer, device_id_type=MESH)
    pl.semaphore_wait(barrier, len(peers))


def quarter_shape(rows, columns):
    if columns % (2 * LANES) == 0:
        return rows // 2, columns // 2
    return rows // 4, columns


def quarter(index, rows, columns):
    high, wide = quarter_shape(rows, columns)
    if wide == columns:
        return pl.ds(pl.multiple_of(index * high, high), high), pl.ds(0, columns)
    return (
        pl.ds(pl.multiple_of(lax.div(index, 2) * high, high), high),
        pl.ds(pl.multiple_of(lax.rem(index, 2) * wide, wide), wide),
    )


def remote(source, target, send, receive, device):
    return pltpu.make_async_remote_copy(
        src_ref=source,
        dst_ref=target,
        send_sem=send,
        recv_sem=receive,
        device_id=device,
        device_id_type=MESH,
    )


GATHER_SEMS = 33


class Gather:
    def __init__(self, shard, out, sems, split, in_place=False):
        self.shard, self.out, self.sems, self.split = shard, out, sems, split
        self.in_place = in_place
        self.rows, self.columns = shard.shape

    def level_copy(self, turn):
        group, level, core = place()
        block = self.out.at[2 * level + core]
        source = self.shard
        if self.split:
            part = quarter(group, self.rows, self.columns)
            source, block = source.at[part], block.at[part]
        sems = self.sems
        peer = (group, 2 * partner(level, turn) + core)
        return remote(source, block, sems.at[turn], sems.at[3 + turn], peer)

    def group_copy(self, turn, other):
        group, level, core = place()
        part = quarter(group, self.rows, self.columns)
        block = self.out.at[2 * partner(level, turn) + core].at[part]
        index = 3 * (turn - 1) + other - 1
        peer = (partner(group, other), 2 * level + core)
        return remote(block, block, self.sems.at[7 + index], self.sems.at[16 + index], peer)

    def core_copy(self, turn):
        group, level, core = place()
        slot = 2 * partner(level, turn) + core
        source = self.shard if turn == 0 else self.out.at[slot]
        peer = (group, 2 * level + 1 - core)
        return remote(source, self.out.at[slot], self.sems.at[25 + turn], self.sems.at[29 + turn], peer)

    def own_copy(self):
        _, level, core = place()
        return pltpu.make_async_copy(self.shard, self.out.at[2 * level + core], self.sems.at[0])

    def first(self):
        for turn in TURNS:
            self.level_copy(turn).start()
        self.core_copy(0).start()
        if not self.in_place:
            self.own_copy().start()

    def second(self):
        for turn in TURNS:
            self.level_copy(turn).wait_recv()
            if self.split:
                for other in TURNS:
                    self.group_copy(turn, other).start()
            else:
                self.core_copy(turn).start()

    def third(self, use=None):
        for turn in TURNS if self.split else ():
            for other in TURNS:
                self.group_copy(turn, other).wait_recv()
            self.core_copy(turn).start()
            if use is not None:
                use(turn, True)

    def fourth(self, use=None):
        for turn in TURNS if use is not None else (0, *TURNS):
            self.core_copy(turn).wait_recv()
            if use is not None:
                use(turn, False)
        for turn in TURNS:
            self.level_copy(turn).wait_send()
            if self.split:
                for other in TURNS:
                    self.group_copy(turn, other).wait_send()
        for turn in (0, *TURNS):
            self.core_copy(turn).wait_send()
        if not self.in_place:
            self.own_copy().wait()


class LevelGather:
    def __init__(self, shard, out, sems):
        self.shard, self.out, self.sems = shard, out, sems

    def level_copy(self, turn):
        group, level, core = place()
        return remote(
            self.shard.at[quarter(group, *self.shard.shape)],
            self.out.at[level],
            self.sems.at[turn],
            self.sems.at[3 + turn],
            (group, 2 * partner(level, turn) + core),
        )

    def first(self):
        for turn in TURNS:
            self.level_copy(turn).start()

    def second(self):
        pass

    def third(self):
        pass

    def fourth(self):
        for turn in TURNS:
            self.level_copy(turn).wait_recv()
            self.level_copy(turn).wait_send()


GROUP_GATHER_SEMS = 30


class GroupGather:
    def __init__(self, shard, quarters, out, sems):
        self.shard, self.quarters, self.out, self.sems = shard, quarters, out, sems

    def part(self, turn):
        group, level, core = place()
        block = self.out.at[2 * partner(level, turn) + core]
        return block.at[quarter(group, *self.shard.shape)]

    def own_copy(self, turn):
        _, level, core = place()
        if turn == 0:
            source, target = self.shard, self.out.at[2 * level + core]
        else:
            source, target = self.quarters.at[partner(level, turn)], self.part(turn)
        return pltpu.make_async_copy(source, target, self.sems.at[turn])

    def group_copy(self, turn, other):
        group, level, core = place()
        index = 3 * (turn - 1) + other - 1
        return remote(
            self.quarters.at[partner(level, turn)],
            self.part(turn),
            self.sems.at[4 + index],
            self.sems.at[13 + index],
            (partner(group, other), 2 * level + core),
        )

    def core_copy(self, turn):
        group, level, core = place()
        slot = 2 * partner(level, turn) + core
        source = self.shard if turn == 0 else self.out.at[slot]
        peer = (group, 2 * level + 1 - core)
        return remote(source, self.out.at[slot], self.sems.at[22 + turn], self.sems.at[26 + turn], peer)

    def first(self):
        for turn in TURNS:
            for other in TURNS:
                self.group_copy(turn, other).start()
        for turn in (0, *TURNS):
            self.own_copy(turn).start()
        self.core_copy(0).start()

    def second(self):
        for turn in TURNS:
            for other in TURNS:
                self.group_copy(turn, other).wait_recv()
            self.own_copy(turn).wait()
            self.core_copy(turn).start()

    def third(self):
        for turn in (0, *TURNS):
            self.core_copy(turn).wait_recv()
            self.core_copy(turn).wait_send()
        for turn in TURNS:
            for other in TURNS:
                self.group_copy(turn, other).wait_send()
        self.own_copy(0).wait()


class GatherRide:
    def __init__(self, shard, quarters):
        owners = lax.axis_size("fsdp")
        self.operands = [shard, quarters]
        self.out_specs = [ANYWHERE]
        self.out_shapes = [jax.ShapeDtypeStruct((owners, *shard.shape), shard.dtype)]
        self.scratch = [pltpu.SemaphoreType.DMA((GROUP_GATHER_SEMS,))]

    def job(self, sources, targets, scratch):
        return GroupGather(*sources, *targets, *scratch)

    def before(self, steps):
        return {0: ("first",), max(1, 2 * steps // 3): ("second",)}

    after = ("third",)

    def result(self, outs):
        return outs[0].reshape(-1, outs[0].shape[2])

    def plain(self):
        return lax.all_gather(self.operands[0], "fsdp", axis=0, tiled=True)


class ShareRide:
    def __init__(self, share):
        self.operands = [share]
        self.out_specs = [fixed(*share.shape)]
        self.out_shapes = [jax.ShapeDtypeStruct(share.shape, share.dtype)]
        self.scratch = [
            pltpu.VMEM(share.shape, share.dtype),
            *share_scratch(share),
            pltpu.SemaphoreType.DMA((GROUP_SEMS,)),
        ]

    def job(self, sources, targets, scratch):
        job = GroupReduce(sources[0], scratch[0], scratch[1:3], scratch[3])
        job.target = targets[0]
        return job

    def before(self, steps):
        return {0: ("first", "second"), max(1, steps // 2): ("third",)}

    after = ("fifth", "sixth", "store")

    def result(self, outs):
        return outs[0]

    def plain(self):
        return lax.psum(self.operands[0], "dp")


def riding(body, counts, rides, steps):
    def kernel(*refs):
        refs = list(refs)

        def pop(count):
            taken = refs[:count]
            del refs[:count]
            return taken

        own = pop(counts[0])
        sources = [pop(len(ride.operands)) for ride in rides]
        own += pop(counts[1])
        targets = [pop(len(ride.out_shapes)) for ride in rides]
        own += pop(counts[2])
        jobs = [
            ride.job(source, target, pop(len(ride.scratch)))
            for ride, source, target in zip(rides, sources, targets)
        ]
        for step in range(steps):
            planned = [
                (job, stages)
                for ride, job in zip(rides, jobs)
                for at, stages in ride.before(steps).items()
                if at == step
            ]
            if planned:

                @pl.when(pl.program_id(0) == step)
                def _(planned=planned, step=step):
                    if step == 0:
                        greet()
                    for job, stages in planned:
                        run_stages([job], stages)

        body(*own)

        @pl.when(pl.program_id(0) == steps - 1)
        def _():
            for ride, job in zip(rides, jobs):
                run_stages([job], ride.after)

    return kernel


def block_call(
    body, grid, in_specs, operands, out_specs, out_shape, scratch, name,
    cost=None, rides=(), collective_id=None,
):
    plain = []
    if rides and not with_kernels():
        plain, rides = [ride.plain() for ride in rides], ()
    transfer = {}
    kernel = body
    if rides:
        transfer = {"collective_id": collective_id, "has_side_effects": True}
        kernel = riding(body, (len(operands), len(out_shape), len(scratch)), rides, grid)
    count = len(out_shape)
    for ride in rides:
        operands, in_specs = [*operands, *ride.operands], [*in_specs, *[ANYWHERE] * len(ride.operands)]
        out_specs, out_shape = [*out_specs, *ride.out_specs], [*out_shape, *ride.out_shapes]
        scratch = [*scratch, *ride.scratch]
    outs = pl.pallas_call(
        kernel,
        grid=(grid,),
        in_specs=in_specs,
        out_specs=out_specs,
        out_shape=out_shape,
        scratch_shapes=scratch,
        compiler_params=pltpu.CompilerParams(vmem_limit_bytes=VMEM_LIMIT, **transfer),
        cost_estimate=cost or NO_COST,
        name=name,
    )(*operands)
    brought, outs = list(outs[count:]), list(outs[:count])
    for ride in rides:
        plain.append(ride.result(brought[: len(ride.out_shapes)]))
        brought = brought[len(ride.out_shapes) :]
    return outs + plain


def work(flops, size):
    return pl.CostEstimate(flops=flops, bytes_accessed=size, transcendentals=0)


def position_weights(seg_col, patch_row, nodes):
    rows = seg_col.shape[0]
    slot = lax.broadcasted_iota(jnp.int32, (rows, IMGS), 1)
    member = seg_col == slot
    counts = jnp.sum(member.astype(jnp.float32), 0, keepdims=True)
    start = jnp.sum(jnp.where(slot < seg_col, counts, 0.0), 1, keepdims=True)
    token = lax.broadcasted_iota(jnp.int32, (rows, 1), 0).astype(jnp.float32)
    inside = seg_col < IMGS
    offset = jnp.where(inside, token - start, 0.0)
    patch = jnp.sum(jnp.where(member, patch_row.astype(jnp.float32), 0.0), 1, keepdims=True)
    side = jnp.where(inside, jnp.floor(IMG / jnp.where(inside, patch, 1.0) + 0.5), 1.0)
    line = jnp.floor((offset + 0.5) / side)
    column = offset - line * side

    def spot(coord):
        return jnp.clip((2.0 * coord + 1.0) * GRID / (2.0 * side) - 0.5, 0.0, GRID - 1.0)

    node = lax.broadcasted_iota(jnp.int32, (rows, LANES), 1).astype(jnp.float32)
    across = jnp.floor((node + 0.5) / GRID)
    along = node - across * GRID
    weights = jnp.maximum(1.0 - jnp.abs(spot(line) - across), 0.0)
    weights = weights * jnp.maximum(1.0 - jnp.abs(spot(column) - along), 0.0)
    return jnp.where(node < nodes, weights, 0.0)


def first_kernel(*refs, spots):
    kernel, vectors, inputs, outputs, head, pixels, seg_col, patch_row, table, biases = refs[:10]
    stream, pos_t, vector_zero, vector_one = refs[10:14]
    qkv_full, up_level, qkv_level, output_level = refs[14:18]
    up_zero, output_zero, qkv_one, up_one, output_one, head_low = refs[18:24]
    wide_kernel, wide_inputs, wide_outputs, wide_head, pixel_rows, table_low = refs[24:30]
    kernel_full, qkv_zero, vectors_full, load_sems, sems = refs[30:]
    _, level, core = place()
    mine = 2 * level + core
    pairs = [
        (kernel, wide_kernel),
        (inputs.at[0], wide_inputs.at[0]),
        (outputs.at[1], wide_outputs.at[1]),
        (inputs.at[1], wide_inputs.at[1]),
        (pixels, pixel_rows),
        (outputs.at[0], wide_outputs.at[0]),
        (head, wide_head),
    ]
    copies = [
        pltpu.make_async_copy(source, target, load_sems.at[index])
        for index, (source, target) in enumerate(pairs)
    ]
    for copy in copies:
        copy.start()
    patch_job = Gather(kernel_full.at[mine], kernel_full, sems.at[0], True, in_place=True)
    vector_job = Gather(vectors, vectors_full, sems.at[1], False)
    qkv_job = Gather(qkv_zero, qkv_full, sems.at[2], True)
    level_jobs = [
        LevelGather(up_zero, up_level, sems.at[3]),
        LevelGather(qkv_one, qkv_level, sems.at[4]),
        LevelGather(output_one, output_level, sems.at[5]),
    ]
    copies[0].wait()
    kernel_full[mine] = wide_kernel[...].astype(LOW)
    greet()
    patch_job.first()
    vector_job.first()
    copies[1].wait()
    qkv_zero[...] = wide_inputs[0, :, : 3 * D].astype(LOW)
    qkv_job.first()
    up_zero[...] = wide_inputs[0, :, 3 * D :].astype(LOW)
    level_jobs[0].first()
    copies[3].wait()
    qkv_one[...] = wide_inputs[1, :, : 3 * D].astype(LOW)
    level_jobs[1].first()
    copies[2].wait()
    output_one[...] = wide_outputs[1].astype(LOW)
    level_jobs[2].first()

    weights = position_weights(seg_col[...], patch_row[...], table.shape[0])
    pos_t[...] = weights.T[: pos_t.shape[0], :]
    table_low[...] = jnp.zeros_like(table_low)
    table_low[: table.shape[0], :] = table[...].astype(LOW).astype(jnp.float32)
    bias = biases[:, :D].astype(LOW).astype(jnp.float32)
    stream[...] = bias + jnp.dot(
        weights, table_low[...], precision=HIGHEST, preferred_element_type=jnp.float32
    )
    copies[4].wait()
    depth = wide_kernel.shape[0]

    def add_block(slot):
        columns = pl.ds(pl.multiple_of(slot * depth, depth), depth)

        def add(step, carry):
            rows = pl.ds(pl.multiple_of(step * 256, 256), 256)
            stream[rows, :] += mul(pixel_rows[rows, columns], kernel_full[slot])
            return carry

        lax.fori_loop(0, stream.shape[0] // 256, add, 0)

    def use(turn, own_core):
        add_block(2 * partner(level, turn) + (core if own_core else 1 - core))

    add_block(mine)
    patch_job.second()
    vector_job.second()
    qkv_job.second()
    patch_job.core_copy(0).wait_recv()
    use(0, False)
    up_one[...] = wide_inputs[1, :, 3 * D :].astype(LOW)
    copies[5].wait()
    output_zero[...] = wide_outputs[0].astype(LOW)
    copies[6].wait()
    head_low[...] = jnp.zeros_like(head_low)
    head_low[:, : head.shape[1]] = wide_head[...].astype(LOW)
    patch_job.third(use)
    qkv_job.third()
    patch_job.fourth(use)
    vector_job.third()
    vector_job.fourth()
    blocks = [vectors_full[slot].astype(jnp.float32) for slot in range(vectors_full.shape[0])]
    span = vectors.shape[0] // LAYERS
    for layer, out in enumerate((vector_zero, vector_one)):
        for row in range(out.shape[1] // LANES):
            parts = [
                block[layer * span + row - spot : layer * span + row - spot + 1, :]
                for block, spot in zip(blocks, spots)
                if 0 <= row - spot < span
            ]
            out[:, row * LANES : (row + 1) * LANES] = sum(parts)
    run_stages([qkv_job, *level_jobs], ("fourth",))


def padded_vectors(shard):
    layers, width = shard.shape
    owners = lax.axis_size("fsdp")
    spots = [owner * width // LANES for owner in range(owners)]
    span = max(-(-(owner + 1) * width // LANES) - spot for owner, spot in enumerate(spots))
    span += -span % 16
    shift = lax.rem(lax.axis_index("fsdp") * width, LANES)
    padded = jnp.zeros((layers, span * LANES), LOW)
    padded = lax.dynamic_update_slice(padded, shard.astype(LOW), (0, shift))
    return padded.reshape(layers * span, LANES), spots


def begin(
    pixels, segment, patch_size, patch_kernel, layer_vector, input_proj, output_proj, head_weight,
    position_table, global_vector,
):
    classes = head_weight.shape[1] + -head_weight.shape[1] % LANES
    nodes = position_table.shape[0] + -position_table.shape[0] % 64
    if not with_kernels():
        inputs = [
            (input_proj[index, :, : 3 * D].astype(LOW), input_proj[index, :, 3 * D :].astype(LOW))
            for index in range(LAYERS)
        ]
        outputs = [output_proj[index].astype(LOW) for index in range(LAYERS)]
        gather = lambda shard, axis: lax.all_gather(shard, "fsdp", axis=axis, tiled=True)
        weights, _, _ = row_layout(segment, patch_size[0])
        weights = jnp.pad(weights, ((0, 0), (0, nodes - weights.shape[1])))
        table = jnp.pad(rounded(position_table), ((0, nodes - position_table.shape[0]), (0, 0)))
        bias = rounded(global_vector)[None, :D]
        stream = embed(pixels, gather(patch_kernel.astype(LOW), 0), weights, table, bias)
        vectors = gather(layer_vector.astype(LOW), 1).astype(jnp.float32)
        head = jnp.pad(head_weight.astype(LOW), ((0, 0), (0, classes - head_weight.shape[1])))
        return (
            stream,
            weights.T,
            [vectors[index : index + 1] for index in range(LAYERS)],
            gather(inputs[0][0], 0),
            [GatherRide(shard, shard) for shard in (inputs[0][1], inputs[1][0], outputs[1])],
            [outputs[0], inputs[1][1], head],
        )
    rows = pixels.shape[0]
    owners = lax.axis_size("fsdp")
    vectors, spots = padded_vectors(layer_vector)
    depth = input_proj.shape[1]
    up_shape = (depth, input_proj.shape[2] - 3 * D)
    qkv_shape, out_shape = (depth, 3 * D), output_proj.shape[1:]
    low = lambda *shape: jax.ShapeDtypeStruct(shape, LOW)
    levels = lambda shape: low(4, *quarter_shape(*shape))
    width = layer_vector.shape[1] * owners
    shapes = [
        shape_of(rows, D),
        shape_of(nodes, rows),
        shape_of(1, width),
        shape_of(1, width),
        low(owners, *qkv_shape),
        levels(up_shape),
        levels(qkv_shape),
        levels(out_shape),
        low(*up_shape),
        low(*out_shape),
        low(*qkv_shape),
        low(*up_shape),
        low(*out_shape),
        low(head_weight.shape[0], classes),
    ]
    wide = (patch_kernel, input_proj, output_proj, head_weight, pixels)
    in_vmem = pl.BlockSpec(memory_space=pltpu.VMEM)
    results = pl.pallas_call(
        functools.partial(first_kernel, spots=spots),
        in_specs=[ANYWHERE] * 6 + [in_vmem] * 4,
        out_specs=[in_vmem] * 4 + [ANYWHERE] * 4 + [in_vmem] * 6,
        out_shape=shapes,
        scratch_shapes=[
            *[pltpu.VMEM(array.shape, array.dtype) for array in wide],
            pltpu.VMEM((LANES, D), jnp.float32),
            pltpu.VMEM((owners, *patch_kernel.shape), LOW),
            pltpu.VMEM(qkv_shape, LOW),
            pltpu.VMEM((owners, *vectors.shape), LOW),
            pltpu.SemaphoreType.DMA((7,)),
            pltpu.SemaphoreType.DMA((6, GATHER_SEMS)),
        ],
        compiler_params=pltpu.CompilerParams(
            collective_id=1, has_side_effects=True, vmem_limit_bytes=VMEM_LIMIT
        ),
        cost_estimate=NO_COST,
        name="begin",
    )(
        patch_kernel,
        vectors,
        input_proj,
        output_proj,
        head_weight,
        pixels,
        segment[:, None],
        patch_size,
        position_table,
        global_vector[None, :],
    )
    up_zero, output_zero, qkv_one, up_one, output_one, head_low = results[8:]
    return (
        results[0],
        results[1],
        results[2:4],
        results[4].reshape(owners * depth, 3 * D),
        [
            GatherRide(up_zero, results[5]),
            GatherRide(qkv_one, results[6]),
            GatherRide(output_one, results[7]),
        ],
        [output_zero, up_one, head_low],
    )


REDUCE_SEMS = 48


class Reduce:
    def __init__(self, grad, out, scratch, sems):
        self.grad, self.out, self.sems = grad, out, sems
        self.own, self.got_core, self.got_group, self.part, self.got_level = scratch
        self.rows, self.columns = out.shape
        self.chunk = 16

    def load(self, level):
        _, _, core = place()
        return pltpu.make_async_copy(
            self.grad.at[2 * level + core], self.own.at[level], self.sems.at[level]
        )

    def core_copy(self, target_level):
        group, level, core = place()
        return remote(
            self.grad.at[2 * target_level + 1 - core],
            self.got_core.at[target_level],
            self.sems.at[4 + target_level],
            self.sems.at[8 + target_level],
            (group, 2 * level + 1 - core),
        )

    def group_copy(self, turn, other):
        group, level, core = place()
        target = partner(level, turn)
        peer = partner(group, other)
        part = quarter(peer, self.rows, self.columns)
        index = 3 * turn + other - 1
        return remote(
            self.own.at[target].at[part],
            self.got_group.at[other - 1, target],
            self.sems.at[12 + index],
            self.sems.at[24 + index],
            (peer, 2 * level + core),
        )

    def level_copy(self, turn):
        group, level, core = place()
        target = partner(level, turn)
        return remote(
            self.part.at[target],
            self.got_level.at[turn - 1],
            self.sems.at[35 + turn],
            self.sems.at[38 + turn],
            (group, 2 * target + core),
        )

    def share_copy(self, other):
        group, level, core = place()
        mine = self.out.at[quarter(group, self.rows, self.columns)]
        return remote(
            mine,
            mine,
            self.sems.at[41 + other],
            self.sems.at[44 + other],
            (partner(group, other), 2 * level + core),
        )

    def first(self):
        _, level, _ = place()
        for turn in (*TURNS, 0):
            self.core_copy(partner(level, turn)).start()
            self.load(partner(level, turn)).start()

    def second(self):
        _, level, _ = place()
        for turn in (*TURNS, 0):
            target = partner(level, turn)
            self.load(target).wait()
            self.core_copy(target).wait_recv()

            def add(step, carry):
                rows = pl.ds(pl.multiple_of(step * self.chunk, self.chunk), self.chunk)
                total = self.own[target, rows, :].astype(jnp.float32)
                total = total + self.got_core[target, rows, :].astype(jnp.float32)
                self.own[target, rows, :] = total.astype(self.own.dtype)
                return carry

            lax.fori_loop(0, self.rows // self.chunk, add, 0)
            for other in TURNS:
                self.group_copy(turn, other).start()

    def between(self):
        pass

    def third(self):
        group, level, _ = place()
        high, wide = quarter_shape(self.rows, self.columns)
        row_part, column_part = quarter(group, self.rows, self.columns)
        for turn in (*TURNS, 0):
            target = partner(level, turn)
            for other in TURNS:
                self.group_copy(turn, other).wait_recv()

            def add(step, carry):
                at = pl.multiple_of(step * self.chunk, self.chunk)
                rows = pl.ds(at, self.chunk)
                mine = pl.ds(pl.multiple_of(row_part.start + at, self.chunk), self.chunk)
                total = self.own[target, mine, column_part].astype(jnp.float32)
                for slot in range(3):
                    total = total + self.got_group[slot, target, rows, :].astype(jnp.float32)
                self.part[target, rows, :] = total.astype(self.part.dtype)
                return carry

            lax.fori_loop(0, high // self.chunk, add, 0)
            if turn:
                self.level_copy(turn).start()

    def fourth(self):
        group, level, _ = place()
        high, wide = quarter_shape(self.rows, self.columns)
        row_part, column_part = quarter(group, self.rows, self.columns)
        for turn in TURNS:
            self.level_copy(turn).wait_recv()

        def add(step, carry):
            at = pl.multiple_of(step * self.chunk, self.chunk)
            rows = pl.ds(at, self.chunk)
            mine = pl.ds(pl.multiple_of(row_part.start + at, self.chunk), self.chunk)
            total = self.part[level, rows, :].astype(jnp.float32)
            for slot in range(3):
                total = total + self.got_level[slot, rows, :].astype(jnp.float32)
            self.out[mine, column_part] = total.astype(self.out.dtype)
            return carry

        lax.fori_loop(0, high // self.chunk, add, 0)
        for other in TURNS:
            self.share_copy(other).start()

    def fifth(self):
        for other in TURNS:
            self.share_copy(other).wait_recv()

    def sixth(self):
        _, level, _ = place()
        for turn in (*TURNS, 0):
            self.core_copy(partner(level, turn)).wait_send()
            for other in TURNS:
                self.group_copy(turn, other).wait_send()
            if turn:
                self.level_copy(turn).wait_send()
                self.share_copy(turn).wait_send()


WHOLE_SEMS = 40


def add_rows(target, row, columns, source, count, wide):
    chunk = 16 if wide > 1536 else 48

    def add(step, carry):
        at = pl.multiple_of(step * chunk, chunk)
        mine = pl.ds(pl.multiple_of(row + at, 16), chunk)
        total = target[mine, columns].astype(jnp.float32)
        total = total + source[pl.ds(at, chunk), :].astype(jnp.float32)
        target[mine, columns] = total.astype(target.dtype)
        return carry

    lax.fori_loop(0, count // chunk, add, 0)


class Whole:
    FIRST_X = (1, 0)

    def __init__(self, grad, out, scratch, sems):
        self.grad, self.out, self.sems = grad, out, sems
        self.own, self.got_core, self.got_x, self.got_y, self.got_last, self.part, self.got_level = scratch
        self.rows, self.columns = out.shape
        self.high, self.wide = self.rows // 2, self.columns // 2

    def row_half(self, index):
        return pl.ds(pl.multiple_of(lax.div(index, 2) * self.high, self.high), self.high)

    def column_half(self, index):
        return pl.ds(pl.multiple_of(lax.rem(index, 2) * self.wide, self.wide), self.wide)

    def load(self, level):
        _, _, core = place()
        return pltpu.make_async_copy(
            self.grad.at[2 * level + core], self.own.at[level], self.sems.at[level]
        )

    def core_copy(self, target_level):
        group, level, core = place()
        return remote(
            self.grad.at[2 * target_level + 1 - core],
            self.got_core.at[target_level],
            self.sems.at[4 + target_level],
            self.sems.at[8 + target_level],
            (group, 2 * level + 1 - core),
        )

    def step_copy(self, turn):
        group, level, core = place()
        block = self.own.at[partner(level, turn)]
        if turn in self.FIRST_X:
            peer = partner(group, 1)
            source = block.at[:, self.column_half(peer)]
            target = self.got_x.at[self.FIRST_X.index(turn)]
        else:
            peer = partner(group, 2)
            source = block.at[self.row_half(peer), :]
            target = self.got_y.at[turn - 2]
        return remote(
            source, target, self.sems.at[12 + turn], self.sems.at[16 + turn], (peer, 2 * level + core)
        )

    def last_copy(self, turn):
        group, level, core = place()
        block = self.own.at[partner(level, turn)]
        peer = partner(group, 2 if turn in self.FIRST_X else 1)
        rows = self.row_half(peer)
        columns = self.column_half(peer)
        return remote(
            block.at[rows, columns],
            self.got_last.at[turn],
            self.sems.at[20 + turn],
            self.sems.at[24 + turn],
            (peer, 2 * level + core),
        )

    def level_copy(self, turn):
        group, level, core = place()
        target = partner(level, turn)
        return remote(
            self.part.at[target],
            self.got_level.at[turn - 1],
            self.sems.at[27 + turn],
            self.sems.at[30 + turn],
            (group, 2 * target + core),
        )

    def share_copy(self, other):
        group, level, core = place()
        mine = self.out.at[self.row_half(group), self.column_half(group)]
        return remote(
            mine,
            mine,
            self.sems.at[33 + other],
            self.sems.at[36 + other],
            (partner(group, other), 2 * level + core),
        )

    def first(self):
        _, level, _ = place()
        for turn in (*TURNS, 0):
            self.core_copy(partner(level, turn)).start()
            self.load(partner(level, turn)).start()

    def second(self):
        _, level, _ = place()
        for turn in (*TURNS, 0):
            target = partner(level, turn)
            self.load(target).wait()
            self.core_copy(target).wait_recv()
            add_rows(
                self.own.at[target], 0, slice(None), self.got_core.at[target], self.rows, self.columns
            )
            self.step_copy(turn).start()

    def between(self):
        group, level, _ = place()
        for turn in (*TURNS, 0):
            block = self.own.at[partner(level, turn)]
            self.step_copy(turn).wait_recv()
            if turn in self.FIRST_X:
                source = self.got_x.at[self.FIRST_X.index(turn)]
                add_rows(block, 0, self.column_half(group), source, self.rows, self.wide)
            else:
                source = self.got_y.at[turn - 2]
                start = lax.div(group, 2) * self.high
                add_rows(block, start, slice(None), source, self.high, self.columns)
            self.last_copy(turn).start()

    def third(self):
        group, level, _ = place()
        start = lax.div(group, 2) * self.high
        columns = self.column_half(group)
        chunk = 16 if self.wide > 1536 else 48
        for turn in (*TURNS, 0):
            target = partner(level, turn)
            self.last_copy(turn).wait_recv()

            def add(step, carry):
                at = pl.multiple_of(step * chunk, chunk)
                rows = pl.ds(at, chunk)
                mine = pl.ds(pl.multiple_of(start + at, 16), chunk)
                total = self.own[target, mine, columns].astype(jnp.float32)
                total = total + self.got_last[turn, rows, :].astype(jnp.float32)
                self.part[target, rows, :] = total.astype(self.part.dtype)
                return carry

            lax.fori_loop(0, self.high // chunk, add, 0)
            if turn:
                self.level_copy(turn).start()

    def fourth(self):
        group, level, _ = place()
        start = lax.div(group, 2) * self.high
        columns = self.column_half(group)
        chunk = 16 if self.wide > 1536 else 48
        for turn in TURNS:
            self.level_copy(turn).wait_recv()

        def add(step, carry):
            at = pl.multiple_of(step * chunk, chunk)
            rows = pl.ds(at, chunk)
            mine = pl.ds(pl.multiple_of(start + at, 16), chunk)
            total = self.part[level, rows, :].astype(jnp.float32)
            for slot in range(3):
                total = total + self.got_level[slot, rows, :].astype(jnp.float32)
            self.out[mine, columns] = total.astype(self.out.dtype)
            return carry

        lax.fori_loop(0, self.high // chunk, add, 0)
        for other in TURNS:
            self.share_copy(other).start()

    def fifth(self):
        for other in TURNS:
            self.share_copy(other).wait_recv()

    def sixth(self):
        _, level, _ = place()
        for turn in (*TURNS, 0):
            self.core_copy(partner(level, turn)).wait_send()
            self.step_copy(turn).wait_send()
            self.last_copy(turn).wait_send()
            if turn:
                self.level_copy(turn).wait_send()
                self.share_copy(turn).wait_send()


GROUP_SEMS = 13


class GroupReduce:
    def __init__(self, share, out, scratch, sems):
        self.share, self.out, self.sems = share, out, sems
        self.own, self.got = scratch
        self.rows, self.columns = out.shape
        self.chunk = 16

    def load(self):
        return pltpu.make_async_copy(self.share, self.own, self.sems.at[0])

    def group_copy(self, other):
        group, level, core = place()
        peer = partner(group, other)
        return remote(
            self.own.at[quarter(peer, self.rows, self.columns)],
            self.got.at[other - 1],
            self.sems.at[other],
            self.sems.at[3 + other],
            (peer, 2 * level + core),
        )

    def share_copy(self, other):
        group, level, core = place()
        mine = self.out.at[quarter(group, self.rows, self.columns)]
        return remote(
            mine,
            mine,
            self.sems.at[6 + other],
            self.sems.at[9 + other],
            (partner(group, other), 2 * level + core),
        )

    def first(self):
        self.load().start()

    def second(self):
        self.load().wait()
        for other in TURNS:
            self.group_copy(other).start()

    def between(self):
        pass

    def third(self):
        group, _, _ = place()
        high, wide = quarter_shape(self.rows, self.columns)
        row_part, column_part = quarter(group, self.rows, self.columns)
        for other in TURNS:
            self.group_copy(other).wait_recv()

        def add(step, carry):
            at = pl.multiple_of(step * self.chunk, self.chunk)
            rows = pl.ds(at, self.chunk)
            mine = pl.ds(pl.multiple_of(row_part.start + at, self.chunk), self.chunk)
            total = self.own[mine, column_part].astype(jnp.float32)
            for slot in range(3):
                total = total + self.got[slot, rows, :].astype(jnp.float32)
            self.out[mine, column_part] = total.astype(self.out.dtype)
            return carry

        lax.fori_loop(0, high // self.chunk, add, 0)
        for other in TURNS:
            self.share_copy(other).start()

    def fourth(self):
        pass

    def fifth(self):
        for other in TURNS:
            self.share_copy(other).wait_recv()

    def store(self):
        self.target[...] = self.out[...]

    def sixth(self):
        for other in TURNS:
            self.group_copy(other).wait_send()
            self.share_copy(other).wait_send()


class Spread:
    def __init__(self, full, sems):
        self.full, self.sems = full, sems

    def level_copy(self, turn):
        group, level, core = place()
        block = self.full.at[2 * level + core]
        peer = (group, 2 * partner(level, turn) + core)
        return remote(block, block, self.sems.at[turn - 1], self.sems.at[2 + turn], peer)

    def core_copy(self, turn):
        group, level, core = place()
        block = self.full.at[2 * partner(level, turn) + core]
        peer = (group, 2 * level + 1 - core)
        return remote(block, block, self.sems.at[6 + turn], self.sems.at[10 + turn], peer)

    def run(self):
        for turn in TURNS:
            self.level_copy(turn).start()
        self.core_copy(0).start()
        for turn in TURNS:
            self.level_copy(turn).wait_recv()
            self.core_copy(turn).start()
        for turn in (0, *TURNS):
            self.core_copy(turn).wait_recv()
        for turn in (0, *TURNS):
            self.core_copy(turn).wait_send()
            if turn:
                self.level_copy(turn).wait_send()


def squares_in(out):
    def add(step, total):
        piece = out[pl.ds(pl.multiple_of(step * 16, 16), 16), :].astype(jnp.float32)
        piece = piece * piece
        for lane in range(0, out.shape[1], LANES):
            total = total + piece[:, lane : lane + LANES]
        return total

    total = lax.fori_loop(0, out.shape[0] // 16, add, jnp.zeros((16, LANES), jnp.float32))
    return jnp.sum(total, 0, keepdims=True)


def run_stages(jobs, stages):
    for stage in stages:
        for job in jobs:
            getattr(job, stage)()


STAGES = ("first", "second", "between", "third", "fourth", "fifth", "sixth")


def whole_scratch(grad):
    _, rows, columns = grad.shape
    high, wide = quarter_shape(rows, columns)
    shapes = ((4, rows, columns), (4, rows, columns), (3, 4, high, wide), (4, high, wide))
    return [pltpu.VMEM(shape, grad.dtype) for shape in (*shapes, (3, high, wide))]


def stepped_scratch(grad):
    _, rows, columns = grad.shape
    high, wide = rows // 2, columns // 2
    shapes = (
        (4, rows, columns),
        (4, rows, columns),
        (2, rows, wide),
        (2, high, columns),
        (4, high, wide),
        (4, high, wide),
        (3, high, wide),
    )
    return [pltpu.VMEM(shape, grad.dtype) for shape in shapes]


def share_scratch(share):
    return [
        pltpu.VMEM(share.shape, share.dtype),
        pltpu.VMEM((3, *quarter_shape(*share.shape)), share.dtype),
    ]


def reduce_kernel(*refs, whole, partly):
    count = whole + partly
    grads, outs, refs = refs[:count], refs[count : 2 * count], refs[2 * count :]
    sems, group_sems, refs = refs[0], refs[1], refs[2:]
    jobs = [
        Whole(grads[i], outs[i], refs[7 * i : 7 * i + 7], sems.at[i]) for i in range(whole)
    ]
    refs = refs[7 * whole :]
    shares = [
        GroupReduce(grads[whole + i], outs[whole + i], refs[2 * i : 2 * i + 2], group_sems.at[i])
        for i in range(partly)
    ]
    greet()
    run_stages([*jobs, *shares], STAGES[:1])
    run_stages(shares, STAGES[1:2])
    run_stages(jobs, STAGES[1:3])
    run_stages(shares, STAGES[3:4])
    run_stages(jobs, STAGES[3:5])
    run_stages([*shares, *jobs], STAGES[5:])


def transfer_cost(size):
    return pl.CostEstimate(flops=4000 * size, bytes_accessed=2 * size, transcendentals=0)


def reduce_call(grads, shares, collective_id):
    in_vmem = pl.BlockSpec(memory_space=pltpu.VMEM)
    whole, partly = len(grads), len(shares)
    scratch = [
        pltpu.SemaphoreType.DMA((whole, WHOLE_SEMS)),
        pltpu.SemaphoreType.DMA((partly, GROUP_SEMS)),
    ]
    for grad in grads:
        scratch.extend(stepped_scratch(grad))
    for share in shares:
        scratch.extend(share_scratch(share))
    out_shape = [jax.ShapeDtypeStruct(g.shape[1:], g.dtype) for g in grads]
    out_shape += [jax.ShapeDtypeStruct(s.shape, s.dtype) for s in shares]
    return pl.pallas_call(
        functools.partial(reduce_kernel, whole=whole, partly=partly),
        in_specs=[ANYWHERE] * (whole + partly),
        out_specs=[in_vmem] * (whole + partly),
        out_shape=out_shape,
        scratch_shapes=scratch,
        compiler_params=pltpu.CompilerParams(
            collective_id=collective_id, has_side_effects=True, vmem_limit_bytes=VMEM_LIMIT
        ),
        cost_estimate=NO_COST,
        name="reduce_gradients",
    )(*grads, *shares)


def finish_kernel(*refs, done, partly):
    finished, refs = refs[:done], refs[done:]
    shares, small, refs = refs[:partly], refs[partly], refs[partly + 1 :]
    outs, small_out, full, refs = refs[:partly], refs[partly], refs[partly + 1], refs[partly + 2 :]
    sems, group_sems, spread_sems, refs = refs[0], refs[1], refs[2], refs[3:]
    job = Reduce(small, small_out, refs[:5], sems)
    refs = refs[5:]
    jobs = [
        GroupReduce(shares[i], outs[i], refs[2 * i : 2 * i + 2], group_sems.at[i])
        for i in range(partly)
    ]
    greet()
    run_stages([job, *jobs], STAGES[:3])
    total = sum(squares_in(out) for out in finished)
    run_stages([*jobs, job], STAGES[3:6])
    total = total + sum(squares_in(out) for out in outs)
    _, level, core = place()
    mine = 2 * level + core
    last = small_out.shape[0] - 1
    full[mine] = small_out[...]
    full[mine, last : last + 1, :] = total
    Spread(full, spread_sems).run()
    run_stages([job, *jobs], STAGES[6:])


def finish_call(finished, shares, small, collective_id):
    done, partly = len(finished), len(shares)
    in_vmem = pl.BlockSpec(memory_space=pltpu.VMEM)
    scratch = [
        pltpu.SemaphoreType.DMA((REDUCE_SEMS,)),
        pltpu.SemaphoreType.DMA((partly, GROUP_SEMS)),
        pltpu.SemaphoreType.DMA((14,)),
        *whole_scratch(small),
    ]
    for share in shares:
        scratch.extend(share_scratch(share))
    out_shape = [jax.ShapeDtypeStruct(s.shape, s.dtype) for s in shares]
    out_shape.append(jax.ShapeDtypeStruct(small.shape[1:], small.dtype))
    out_shape.append(jax.ShapeDtypeStruct(small.shape, small.dtype))
    return pl.pallas_call(
        functools.partial(finish_kernel, done=done, partly=partly),
        in_specs=[in_vmem] * done + [ANYWHERE] * (partly + 1),
        out_specs=[in_vmem] * len(out_shape),
        out_shape=out_shape,
        scratch_shapes=scratch,
        compiler_params=pltpu.CompilerParams(
            collective_id=collective_id, has_side_effects=True, vmem_limit_bytes=VMEM_LIMIT
        ),
        name="finish_gradients",
    )(*finished, *shares, small)


def with_kernels():
    return lax.axis_size("dp") == 4 and lax.axis_size("fsdp") == 8


def reduce_all(grads, shares, collective_id):
    if with_kernels():
        return reduce_call(grads, shares, collective_id)
    return [lax.psum(scatter(grad), "dp") for grad in grads] + sum_shares(shares)


def sum_shares(shares):
    return [lax.psum(share, "dp") for share in shares]


def finish_all(finished, shares, small, collective_id):
    if with_kernels():
        return finish_call(finished, shares, small, collective_id)
    outs = [lax.psum(share, "dp") for share in shares]
    own = lax.psum(scatter(small), "dp")
    total = sum(jnp.sum(jnp.square(out.astype(jnp.float32))) for out in (*finished, *outs))
    row = jnp.full((1, LANES), 1.0 / LANES, jnp.float32) * total
    return [*outs, own, lax.all_gather(own.at[-1:].set(row), "fsdp", axis=0)]


def take(items, *counts):
    cut = []
    for count in counts:
        cut.append(items[:count])
        items = items[count:]
    return cut


def scatter(grad):
    return lax.psum_scatter(grad, "fsdp", scatter_dimension=0)


def by_owner(grad, low=jnp.bfloat16):
    owners = lax.axis_size("fsdp")
    return grad.astype(low).reshape(owners, grad.shape[0] // owners, grad.shape[1])


def attention_forward_kernel(
    q_ref, k_ref, v_ref, seg_col_ref, seg_row_ref, out_ref, expo_ref, inv_ref, *, block
):
    rows = q_ref.shape[0]
    lower = lax.broadcasted_iota(jnp.int32, (block, PAIR), 1) < HD
    keys = k_ref[...]
    values = jnp.concatenate([v_ref[...], jnp.ones((rows, PAIR), v_ref.dtype)], 1)
    seg_row = seg_row_ref[...]
    tasks = [(step, head) for step in range(rows // block) for head in range(2)]

    def scores_of(step, head):
        query = q_ref[step * block : (step + 1) * block, :] * jnp.bfloat16(HD**-0.5)
        keep = lower if head == 0 else jnp.logical_not(lower)
        return mul_nt(jnp.where(keep, query, jnp.bfloat16(0)), keys)

    scores = scores_of(*tasks[0])
    outs = []
    for index, (step, head) in enumerate(tasks):
        following = scores_of(*tasks[index + 1]) if index + 1 < len(tasks) else None
        at = slice(step * block, (step + 1) * block)
        scores = jnp.where(seg_col_ref[at, :] == seg_row, scores, MASKED)
        highest = jnp.max(scores, -1, keepdims=True)
        low = jnp.exp(scores - highest).astype(jnp.bfloat16)
        expo_ref[head, at, :] = low
        outs.append(mul(low, values))
        if head:
            inverse = 1.0 / jnp.where(lower, outs[0][:, PAIR:], outs[1][:, PAIR:])
            sums = jnp.where(lower, outs[0][:, :PAIR], outs[1][:, :PAIR])
            out_ref[at, :] = (sums * inverse).astype(jnp.bfloat16)
            inv_ref[at, :] = inverse
            outs = []
        scores = following


def attention_forward(qkv_rows, segment, rides, collective_id):
    rows = qkv_rows.shape[0]
    pairs = HEADS // 2
    wide = lambda base: pl.BlockSpec((rows, PAIR), lambda j, base=base: (0, base + j))
    return block_call(
        functools.partial(attention_forward_kernel, block=min(256, rows)),
        pairs,
        [wide(0), wide(pairs), wide(2 * pairs), fixed(rows, 1), fixed(1, rows)],
        [qkv_rows, qkv_rows, qkv_rows, segment[:, None], segment[None, :]],
        [wide(0), pl.BlockSpec((2, rows, rows), lambda j: (j, 0, 0)), wide(0)],
        [
            shape_of(rows, D, dtype=LOW),
            shape_of(HEADS, rows, rows, dtype=LOW),
            shape_of(rows, D),
        ],
        [],
        "attention_forward",
        work(16 * HEADS * rows * rows * HD, 2 * HEADS * rows * rows + 12 * rows * D),
        rides,
        collective_id,
    )


def attention_backward_kernel(
    q_ref, k_ref, v_ref, expo_ref, inv_ref, out_ref, grad_ref, dqkv_ref, *, block
):
    rows = q_ref.shape[0]
    pair = pl.program_id(0)
    lower = lax.broadcasted_iota(jnp.int32, (block, PAIR), 1) < HD
    keys = k_ref[...]
    values = v_ref[...]
    scale = HD**-0.5
    scaled_grad = (grad_ref[...].astype(jnp.float32) * inv_ref[...]).astype(jnp.bfloat16)
    query = q_ref[...]
    query_t = query.T
    grad_t = scaled_grad.T
    product = scaled_grad.astype(jnp.float32) * out_ref[...].astype(jnp.float32)
    key_t = [None, None]
    value_t = [None, None]
    tasks = [(step, head) for step in range(rows // block) for head in range(2)]

    def probs_grad_of(step, head):
        keep = lower if head == 0 else jnp.logical_not(lower)
        mine = scaled_grad[step * block : (step + 1) * block]
        return mul_nt(jnp.where(keep, mine, jnp.bfloat16(0)), values)

    probs_grad = probs_grad_of(*tasks[0])
    query_parts = []
    for index, (step, head) in enumerate(tasks):
        following = probs_grad_of(*tasks[index + 1]) if index + 1 < len(tasks) else None
        at = slice(step * block, (step + 1) * block)
        lanes = slice(head * HD, (head + 1) * HD)
        keep = lower if head == 0 else jnp.logical_not(lower)
        inner = jnp.sum(jnp.where(keep, product[at], 0.0), -1, keepdims=True)
        low = expo_ref[head, at, :]
        value_part = mul(grad_t[lanes, at], low)
        scores_grad = (low.astype(jnp.float32) * (probs_grad - inner)).astype(jnp.bfloat16)
        query_parts.append(mul(scores_grad, keys))
        key_part = mul(query_t[lanes, at], scores_grad)
        key_t[head] = key_part if step == 0 else key_t[head] + key_part
        value_t[head] = value_part if step == 0 else value_t[head] + value_part
        if head:
            query_grad = jnp.where(lower, query_parts[0], query_parts[1]) * scale
            dqkv_ref[at, pl.ds(pl.multiple_of(pair * PAIR, PAIR), PAIR)] = query_grad.astype(
                jnp.bfloat16
            )
            query_parts = []
        probs_grad = following
    key_grad = (jnp.concatenate(key_t, 0) * scale).T
    value_grad = jnp.concatenate(value_t, 0).T
    dqkv_ref[:, pl.ds(pl.multiple_of(D + pair * PAIR, PAIR), PAIR)] = key_grad.astype(jnp.bfloat16)
    dqkv_ref[:, pl.ds(pl.multiple_of(2 * D + pair * PAIR, PAIR), PAIR)] = value_grad.astype(jnp.bfloat16)


def attention_backward(qkv_rows, expo, inverse, attended, attended_grad, rides, collective_id):
    rows = qkv_rows.shape[0]
    pairs = HEADS // 2
    wide = lambda base: pl.BlockSpec((rows, PAIR), lambda j, base=base: (0, base + j))
    return block_call(
        functools.partial(attention_backward_kernel, block=min(256, rows)),
        pairs,
        [
            wide(0),
            wide(pairs),
            wide(2 * pairs),
            pl.BlockSpec((2, rows, rows), lambda j: (j, 0, 0)),
            wide(0),
            wide(0),
            wide(0),
        ],
        [qkv_rows, qkv_rows, qkv_rows, expo, inverse, attended, attended_grad],
        [fixed(rows, 3 * D)],
        [shape_of(rows, 3 * D, dtype=LOW)],
        [],
        "attention_backward",
        None,
        rides,
        collective_id,
    )


def mul(left, right):
    return jnp.dot(left, right, preferred_element_type=jnp.float32)


def mul_nt(left, right):
    return lax.dot_general(left, right, NT, preferred_element_type=jnp.float32)


def normalized(values):
    center = values - jnp.mean(values, -1, keepdims=True)
    inverse = lax.rsqrt(jnp.mean(center * center, -1, keepdims=True) + NORM_EPS)
    return center * inverse, inverse


def norm_backward(grad, values, gain):
    unit, inverse = normalized(values)
    inner = grad * gain
    mean_inner = jnp.mean(inner, -1, keepdims=True)
    mean_cross = jnp.mean(inner * unit, -1, keepdims=True)
    value_grad = inverse * (inner - mean_inner - unit * mean_cross)
    return value_grad, column_sum(grad * unit), column_sum(grad)


def column_sum(rows):
    return jnp.sum(rows.astype(jnp.float32), 0, keepdims=True)


def at_first(action):
    pl.when(pl.program_id(0) == 0)(action)


def accumulate(out_ref, parts):
    value = jnp.concatenate(parts, 1)

    @pl.when(pl.program_id(0) == 0)
    def _():
        out_ref[...] = value

    @pl.when(pl.program_id(0) > 0)
    def _():
        out_ref[...] += value


def rows_of(block, columns):
    return pl.BlockSpec((block, columns), lambda i: (i, 0))


def fixed(*shape):
    return pl.BlockSpec(shape, lambda i: (0,) * len(shape), pipeline_mode=pl.Buffered(1))


def loads(sources, targets, sems):
    return [
        pltpu.make_async_copy(source, target, sems.at[index])
        for index, (source, target) in enumerate(zip(sources, targets))
    ]


def shape_of(*shape, dtype=jnp.float32):
    return jax.ShapeDtypeStruct(shape, dtype)


def embed_kernel(pixel_ref, weight_ref, pos_ref, table_ref, bias_ref, out_ref):
    position = jnp.dot(
        pos_ref[...], table_ref[...], precision=HIGHEST, preferred_element_type=jnp.float32
    )
    out_ref[...] = mul(pixel_ref[...], weight_ref[...]) + bias_ref[...] + position


def embed(pixels, weight, pos_weights, table, bias):
    rows, depth = pixels.shape
    block = 256
    nodes = pos_weights.shape[1]
    return block_call(
        embed_kernel,
        rows // block,
        [rows_of(block, depth), fixed(depth, D), rows_of(block, nodes), fixed(nodes, D), fixed(1, D)],
        [pixels, weight, pos_weights, table, bias],
        [rows_of(block, D)],
        [shape_of(rows, D)],
        [],
        "embed",
        work(2 * rows * depth * D, 2 * rows * depth + 2 * depth * D + 4 * rows * D),
    )[0]


def qkv_kernel(stream_ref, weight_ref, vector_ref, normed_ref, qkv_ref):
    unit, _ = normalized(stream_ref[...])
    normed = (unit * vector_ref[:, :D] + vector_ref[:, D : 2 * D]).astype(jnp.bfloat16)
    normed_ref[...] = normed
    bias = vector_ref[:, 4 * D : 7 * D]
    qkv_ref[...] = (mul(normed, weight_ref[...]) + bias).astype(jnp.bfloat16)


def qkv_forward(stream, weight, vector):
    rows = stream.shape[0]
    block = 256
    low = jnp.bfloat16
    return block_call(
        qkv_kernel,
        rows // block,
        [rows_of(block, D), fixed(D, 3 * D), fixed(1, vector.shape[1])],
        [stream, weight, vector],
        [rows_of(block, D), rows_of(block, 3 * D)],
        [shape_of(rows, D, dtype=low), shape_of(rows, 3 * D, dtype=low)],
        [],
        "qkv_forward",
        work(6 * rows * D * D, 14 * rows * D + 6 * D * D),
    )


def mlp_kernel(
    stream_ref, attended_ref, up_full, proj_out, vector_ref,
    residual_ref, normed_ref, active_ref, slope_ref, out_ref,
    mix_ref, up_ref, down_ref, sems,
):
    width = up_ref.shape[1]
    copies = loads(
        (proj_out.at[pl.ds(0, D)], up_full, proj_out.at[pl.ds(D, width)]),
        (mix_ref, up_ref, down_ref),
        sems,
    )

    @at_first
    def _():
        for copy in copies:
            copy.start()
        copies[0].wait()

    residual = stream_ref[...] + mul(attended_ref[...], mix_ref[...]) + vector_ref[:, 7 * D : 8 * D]
    residual_ref[...] = residual
    unit, _ = normalized(residual)
    normed = (unit * vector_ref[:, 2 * D : 3 * D] + vector_ref[:, 3 * D : 4 * D]).astype(jnp.bfloat16)
    normed_ref[...] = normed
    at_first(copies[1].wait)
    part = 512

    def hidden_of(base):
        bias = vector_ref[:, 9 * D + base : 9 * D + base + part]
        return mul(normed, up_ref[:, base : base + part]) + bias

    hidden = hidden_of(0)
    for base in range(0, width, part):
        following = hidden_of(base + part) if base + part < width else None
        columns = slice(base, base + part)
        square = hidden * hidden
        half = 0.5 + 0.5 * jnp.tanh(hidden * (ROOT + (ROOT * CUBE) * square))
        active = hidden * half
        active_ref[:, columns] = active.astype(jnp.bfloat16)
        rise = (2.0 * ROOT) + (6.0 * ROOT * CUBE) * square
        slope_ref[:, columns] = (half + active * (1.0 - half) * rise).astype(jnp.bfloat16)
        hidden = following
    at_first(copies[2].wait)
    out_ref[...] = residual + mul(active_ref[...], down_ref[...]) + vector_ref[:, 8 * D : 9 * D]


def mlp_forward(stream, attended, up, proj_out, vector, rides, collective_id):
    rows = stream.shape[0]
    width = up.shape[1]
    block = 256
    low = jnp.bfloat16
    return block_call(
        mlp_kernel,
        rows // block,
        [rows_of(block, D), rows_of(block, D), ANYWHERE, ANYWHERE, fixed(1, vector.shape[1])],
        [stream, attended, up, proj_out, vector],
        [rows_of(block, D), rows_of(block, D), rows_of(block, width), rows_of(block, width), rows_of(block, D)],
        [
            shape_of(rows, D),
            shape_of(rows, D, dtype=low),
            shape_of(rows, width, dtype=low),
            shape_of(rows, width, dtype=low),
            shape_of(rows, D),
        ],
        [
            pltpu.VMEM((D, D), low),
            pltpu.VMEM((D, width), low),
            pltpu.VMEM((width, D), low),
            pltpu.SemaphoreType.DMA((3,)),
        ],
        "mlp_forward",
        work(2 * rows * D * (D + 2 * width), rows * (16 * D + 4 * width) + 2 * D * (D + 2 * width)),
        rides,
        collective_id,
    )


def mlp_back_kernel(
    grad_ref, slope_ref, residual_ref, up_full, proj_out, vector_ref,
    low_ref, hidden_ref, out_ref, out_low_ref, attended_ref, sums_ref,
    mix_ref, up_ref, down_ref, sems,
):
    width = up_ref.shape[1]
    copies = loads(
        (proj_out.at[pl.ds(D, width)], up_full, proj_out.at[pl.ds(0, D)]),
        (down_ref, up_ref, mix_ref),
        sems,
    )

    @at_first
    def _():
        for copy in copies:
            copy.start()
        copies[0].wait()

    grad = grad_ref[...]
    grad_low = grad.astype(jnp.bfloat16)
    low_ref[...] = grad_low
    part = 512
    hidden_sums = []
    active_grad = mul_nt(grad_low, down_ref[:part, :])
    for base in range(0, width, part):
        following = None
        if base + part < width:
            following = mul_nt(grad_low, down_ref[base + part : base + 2 * part, :])
        columns = slice(base, base + part)
        hidden_grad = (active_grad * slope_ref[:, columns].astype(jnp.float32)).astype(jnp.bfloat16)
        hidden_ref[:, columns] = hidden_grad
        hidden_sums.append(column_sum(hidden_grad))
        active_grad = following
    at_first(copies[1].wait)
    second_grad = mul_nt(hidden_ref[...], up_ref[...])
    value_grad, gain_grad, shift_grad = norm_backward(
        second_grad, residual_ref[...], vector_ref[:, 2 * D : 3 * D]
    )
    total = value_grad + grad
    out_ref[...] = total
    total_low = total.astype(jnp.bfloat16)
    out_low_ref[...] = total_low
    at_first(copies[2].wait)
    attended_ref[...] = mul_nt(total_low, mix_ref[...]).astype(jnp.bfloat16)
    accumulate(
        sums_ref,
        [gain_grad, shift_grad, column_sum(total_low), column_sum(grad_low), *hidden_sums],
    )


def mlp_backward(grad, slope, residual, up, proj_out, vector):
    rows = grad.shape[0]
    width = up.shape[1]
    block = 256
    low = jnp.bfloat16
    narrow = rows_of(block, D)
    return block_call(
        mlp_back_kernel,
        rows // block,
        [narrow, rows_of(block, width), narrow, ANYWHERE, ANYWHERE, fixed(1, vector.shape[1])],
        [grad, slope, residual, up, proj_out, vector],
        [narrow, rows_of(block, width), narrow, narrow, narrow, fixed(1, 4 * D + width)],
        [
            shape_of(rows, D, dtype=low),
            shape_of(rows, width, dtype=low),
            shape_of(rows, D),
            shape_of(rows, D, dtype=low),
            shape_of(rows, D, dtype=low),
            shape_of(1, 4 * D + width),
        ],
        [
            pltpu.VMEM((D, D), low),
            pltpu.VMEM((D, width), low),
            pltpu.VMEM((width, D), low),
            pltpu.SemaphoreType.DMA((3,)),
        ],
        "mlp_backward",
        None,
    )


def qkv_back_kernel(grad_ref, residual_ref, stream_ref, weight_ref, vector_ref, out_ref, sums_ref):
    grad = grad_ref[...]
    normed_grad = mul_nt(grad, weight_ref[...])
    value_grad, gain_grad, shift_grad = norm_backward(normed_grad, stream_ref[...], vector_ref[:, :D])
    out_ref[...] = residual_ref[...] + value_grad
    accumulate(sums_ref, [gain_grad, shift_grad, column_sum(grad)])


def qkv_backward(grad, residual_grad, stream, weight, vector):
    rows = stream.shape[0]
    block = 256
    narrow = rows_of(block, D)
    return block_call(
        qkv_back_kernel,
        rows // block,
        [rows_of(block, 3 * D), narrow, narrow, fixed(D, 3 * D), fixed(1, vector.shape[1])],
        [grad, residual_grad, stream, weight, vector],
        [narrow, fixed(1, 5 * D)],
        [shape_of(rows, D), shape_of(1, 5 * D)],
        [],
        "qkv_backward",
        None,
    )


def input_grad_kernel(first_ref, second_ref, qkv_ref, hidden_ref, qkv_out, up_out, left_ref, *, cut):
    step = pl.program_id(0)

    @pl.when(step == 0)
    def _():
        left_ref[...] = first_ref[...].T

    @pl.when(step == cut)
    def _():
        left_ref[...] = second_ref[...].T

    @pl.when(step < cut)
    def _():
        qkv_out[...] = mul(left_ref[...], qkv_ref[...]).astype(jnp.bfloat16)

    @pl.when(step >= cut)
    def _():
        up_out[...] = mul(left_ref[...], hidden_ref[...]).astype(jnp.bfloat16)


def input_weight_grad(first, second, qkv_grad, hidden_grad):
    rows = first.shape[0]
    cut = qkv_grad.shape[1] // D
    steps = cut + hidden_grad.shape[1] // D
    before = lambda i: (0, jnp.minimum(i, cut - 1))
    after = lambda i: (0, jnp.maximum(i - cut, 0))
    return block_call(
        functools.partial(input_grad_kernel, cut=cut),
        steps,
        [
            fixed(rows, D),
            fixed(rows, D),
            pl.BlockSpec((rows, D), before),
            pl.BlockSpec((rows, D), after),
        ],
        [first, second, qkv_grad, hidden_grad],
        [pl.BlockSpec((D, D), before), pl.BlockSpec((D, D), after)],
        [
            shape_of(D, qkv_grad.shape[1], dtype=jnp.bfloat16),
            shape_of(D, hidden_grad.shape[1], dtype=jnp.bfloat16),
        ],
        [pltpu.VMEM((D, rows), jnp.bfloat16)],
        "input_weight_grad",
        None,
    )


def output_grad_kernel(attended_ref, active_ref, residual_ref, grad_ref, *outs, cut):
    step = pl.program_id(0)

    def store(product):
        base = 0
        for out in outs:
            out[...] = product[:, base : base + out.shape[1]].astype(jnp.bfloat16)
            base += out.shape[1]

    @pl.when(step < cut)
    def _():
        store(mul(attended_ref[...].T, residual_ref[...]))

    @pl.when(step >= cut)
    def _():
        store(mul(active_ref[...].T, grad_ref[...]))


def output_weight_grad(attended, active, residual_low, grad_low, parts):
    rows = attended.shape[0]
    block = 768
    cut = attended.shape[1] // block
    steps = cut + active.shape[1] // block
    return block_call(
        functools.partial(output_grad_kernel, cut=cut),
        steps,
        [
            pl.BlockSpec((rows, block), lambda i: (0, jnp.minimum(i, cut - 1))),
            pl.BlockSpec((rows, block), lambda i: (0, jnp.maximum(i - cut, 0))),
            fixed(rows, D),
            fixed(rows, D),
        ],
        [attended, active, residual_low, grad_low],
        [rows_of(block, part) for part in parts],
        [shape_of(steps * block, part, dtype=LOW) for part in parts],
        [],
        "output_weight_grad",
    )


def embed_back_kernel(pixel_ref, grad_ref, pos_ref, out_ref, table_ref, bias_ref, low_ref):
    @at_first
    def _():
        grad = grad_ref[...]
        low = grad.astype(jnp.bfloat16)
        low_ref[...] = low
        bias_ref[...] = column_sum(low)
        table_ref[...] = jnp.dot(
            pos_ref[...], grad, precision=HIGHEST, preferred_element_type=jnp.float32
        )

    out_ref[...] = mul(pixel_ref[...].T, low_ref[...]).astype(jnp.bfloat16)


def embed_backward(pixels, grad, pos_weights_t):
    rows, depth = pixels.shape
    block = 768
    nodes = pos_weights_t.shape[0]
    return block_call(
        embed_back_kernel,
        depth // block,
        [pl.BlockSpec((rows, block), lambda i: (0, i)), fixed(rows, D), fixed(nodes, rows)],
        [pixels, grad, pos_weights_t],
        [rows_of(block, D), fixed(nodes, D), fixed(1, D)],
        [shape_of(depth, D, dtype=jnp.bfloat16), shape_of(nodes, D), shape_of(1, D)],
        [pltpu.VMEM((rows, D), jnp.bfloat16)],
        "embed_backward",
        None,
    )


def head_kernel(
    stream_ref, seg_col_ref, seg_row_ref, label_ref, weight_ref, vector_ref,
    grad_ref, weight_grad_ref, sums_ref, bias_grad_ref, numbers_ref, *, classes,
):
    padded = weight_ref.shape[1]
    vector = vector_ref[...].astype(LOW).astype(jnp.float32)
    gain, shift = vector[:, D : 2 * D], vector[:, 2 * D : 3 * D]
    slots = lax.broadcasted_iota(jnp.int32, (IMGS, 1), 0)
    member = (seg_row_ref[...] == slots).astype(jnp.float32)
    counts = jnp.sum(member, 1, keepdims=True)
    sizes = jnp.maximum(counts, 1.0)
    unit, inverse = normalized(stream_ref[...])
    final = unit * gain + shift
    pooled = jnp.dot(member, final, precision=HIGHEST, preferred_element_type=jnp.float32)
    pooled = (pooled / sizes).astype(LOW)
    class_at = lax.broadcasted_iota(jnp.int32, (IMGS, padded), 1)
    logits = mul(pooled, weight_ref[...]) + vector[:, 3 * D :]
    logits = jnp.where(class_at < classes, logits, MASKED)
    highest = jnp.max(logits, -1, keepdims=True)
    exponent = jnp.exp(logits - highest)
    totals = jnp.sum(exponent, -1, keepdims=True)
    onehot = class_at == label_ref[...]
    picked = jnp.sum(jnp.where(onehot, logits, 0.0), 1, keepdims=True)
    loss = jnp.sum(counts * (highest + jnp.log(totals) - picked), 0, keepdims=True)
    numbers_ref[...] = jnp.concatenate([loss, jnp.sum(counts, 0, keepdims=True)], 1)
    logits_grad = ((exponent / totals - onehot.astype(jnp.float32)) * counts).astype(LOW)
    bias_grad_ref[...] = column_sum(logits_grad)
    weight_grad_ref[...] = lax.dot_general(
        pooled, logits_grad, (((0,), (0,)), ((), ())), preferred_element_type=jnp.float32
    ).astype(LOW)
    pooled_grad = mul_nt(logits_grad, weight_ref[...]) / sizes
    own = (seg_col_ref[...] == lax.broadcasted_iota(jnp.int32, (1, IMGS), 1)).astype(jnp.float32)
    final_grad = jnp.dot(own, pooled_grad, precision=HIGHEST, preferred_element_type=jnp.float32)
    inner = final_grad * gain
    mean_inner = jnp.mean(inner, -1, keepdims=True)
    mean_cross = jnp.mean(inner * unit, -1, keepdims=True)
    grad_ref[...] = inverse * (inner - mean_inner - unit * mean_cross)
    sums_ref[...] = jnp.concatenate([column_sum(final_grad * unit), column_sum(final_grad)], 1)


def head(stream, segment, labels, weight, global_vector, classes):
    rows = stream.shape[0]
    padded = weight.shape[1]
    vector = jnp.pad(global_vector, (0, padded - classes))[None, :]
    return pl.pallas_call(
        functools.partial(head_kernel, classes=classes),
        out_shape=[
            shape_of(rows, D),
            shape_of(D, padded, dtype=LOW),
            shape_of(1, 2 * D),
            shape_of(1, padded),
            shape_of(1, 2),
        ],
        compiler_params=pltpu.CompilerParams(vmem_limit_bytes=VMEM_LIMIT),
        cost_estimate=NO_COST,
        name="head",
    )(stream, segment[:, None], segment[None, :], labels.reshape(IMGS, 1), weight, vector)


def adam_update(gradient, moment, square, weight, factor, learn_rate):
    clipped = gradient * factor
    moment = BETA_ONE * moment + (1.0 - BETA_ONE) * clipped
    square = BETA_TWO * square + (1.0 - BETA_TWO) * clipped * clipped
    fixed_one = 1.0 - BETA_ONE**STEP
    fixed_two = 1.0 - BETA_TWO**STEP
    step_dir = (
        moment / fixed_one / (jnp.sqrt(square / fixed_two) + ADAM_EPS) + WEIGHT_DECAY * weight
    )
    return (moment, square, weight - learn_rate * step_dir)


def body(
    pixels,
    segment,
    patch_size,
    labels,
    patch_kernel,
    head_weight,
    input_proj,
    output_proj,
    layer_vector,
    position_table,
    global_vector,
    patch_moment,
    head_moment,
    input_moment,
    output_moment,
    layer_moment,
    position_moment,
    global_moment,
    patch_square,
    head_square,
    input_square,
    output_square,
    layer_square,
    position_square,
    global_square,
):
    owners = lax.axis_size("fsdp")
    nodes = position_table.shape[0]
    vector_size = layer_vector.size
    stream, pos_weights_t, vectors, qkv_weight, rides, rest_shards = begin(
        pixels,
        segment,
        patch_size,
        patch_kernel,
        layer_vector,
        input_proj,
        output_proj,
        head_weight,
        position_table,
        global_vector,
    )
    output_zero, up_one, head_full = (
        lax.all_gather(shard, "fsdp", axis=0, tiled=True) for shard in rest_shards
    )
    saved_layers = []
    for index in range(LAYERS):
        vector = vectors[index]
        normed, qkv_rows = qkv_forward(stream, qkv_weight, vector)
        attended, expo, inverse, fetched = attention_forward(
            qkv_rows, segment, [rides[0] if index == 0 else rides[2]], 4 + index
        )
        up, output = (fetched, output_zero) if index == 0 else (up_one, fetched)
        residual, normed_second, active, slope, following, *fetched = mlp_forward(
            stream, attended, up, output, vector, rides[1:2] if index == 0 else (), 7
        )
        saved_layers.append(
            (
                (qkv_weight, up, output, vector),
                (stream, normed, qkv_rows, attended, expo, inverse),
                (residual, normed_second, active, slope),
            )
        )
        stream = following
        if fetched:
            (qkv_weight,) = fetched
    stream_grad, head_grad, final_sums, head_bias_grad, numbers = head(
        stream, segment, labels, head_full, global_vector, head_weight.shape[1]
    )
    head_part = scatter(by_owner(head_grad))
    vector_grads = [None] * LAYERS
    early_parts, late_parts = [head_part], []
    for index in reversed(range(LAYERS)):
        (qkv_weight, up, output, vector), first, second = saved_layers[index]
        entering, normed, qkv_rows, attended, expo, inverse = first
        residual, normed_second, active, slope = second
        grad_low, hidden_grad, residual_grad, residual_low, attended_grad, mlp_sums = mlp_backward(
            stream_grad, slope, residual, up, output, vector
        )
        output_grads = output_weight_grad(
            attended, active, residual_low, grad_low, (D // 3,) * 3 if index else (D,)
        )
        attended_grad, *output_grads = lax.optimization_barrier((attended_grad, *output_grads))
        output_parts = [scatter(by_owner(grad)) for grad in output_grads]
        if index:
            early_parts.extend(output_parts)
        else:
            (last_part,) = output_parts
        qkv_grad, *early_sums = attention_backward(
            qkv_rows,
            expo,
            inverse,
            attended,
            attended_grad,
            () if index else [ShareRide(part) for part in early_parts],
            6,
        )
        stream_grad, qkv_sums = qkv_backward(qkv_grad, residual_grad, entering, qkv_weight, vector)
        input_grads = input_weight_grad(normed, normed_second, qkv_grad, hidden_grad)
        if index:
            stream_grad, *input_grads = lax.optimization_barrier((stream_grad, *input_grads))
            late_parts.extend(scatter(by_owner(grad)) for grad in input_grads)
        vector_grads[index] = jnp.concatenate(
            [
                qkv_sums[0, : 2 * D],
                mlp_sums[0, : 2 * D],
                qkv_sums[0, 2 * D :],
                mlp_sums[0, 2 * D :],
            ]
        )
    kernel_grad, position_grad, bias_grad = embed_backward(pixels, stream_grad, pos_weights_t)
    position_grad = position_grad[:nodes]
    vector_part = jnp.stack(vector_grads).reshape(LAYERS, owners, -1)
    vector_part = jnp.swapaxes(vector_part, 0, 1).reshape(owners, vector_size)
    vector_rows = -(-vector_size // LANES)
    vector_part = jnp.pad(vector_part, ((0, 0), (0, vector_rows * LANES - vector_size)))
    rest = jnp.concatenate(
        [
            position_grad.reshape(-1),
            bias_grad[0],
            final_sums[0],
            head_bias_grad[0, :CLS],
            numbers[0],
        ]
    )
    rest_rows = -(-rest.shape[0] // (owners * LANES))
    rest_part = jnp.pad(rest, (0, rest_rows * owners * LANES - rest.shape[0]))
    small = jnp.concatenate([vector_part, rest_part.reshape(owners, -1)], 1)
    used = vector_rows + rest_rows
    block_rows = (used // 64 + 1) * 64
    small = jnp.pad(small.reshape(owners, used, LANES), ((0, 0), (0, block_rows - used), (0, 0)))
    input_zero_sums, kernel_sum, input_one_sums = take(
        reduce_all([by_owner(grad) for grad in (*input_grads, kernel_grad)], late_parts, 2), 2, 1, 2
    )
    output_zero_sum, small_share, small_full = finish_all(
        [*early_sums, *input_zero_sums, *kernel_sum, *input_one_sums], [last_part], small, 3
    )
    head_sum, output_one_sums = early_sums[0], early_sums[1:]
    rest_sum = small_full[:, vector_rows:used].reshape(-1)
    position_sum = rest_sum[: position_grad.size].reshape(position_grad.shape)
    global_sum = rest_sum[position_grad.size :][: global_vector.shape[0]]
    loss_sum = rest_sum[rest.shape[0] - 2]
    token_total = rest_sum[rest.shape[0] - 1]
    kernel_sum = kernel_sum[0].astype(jnp.float32)
    head_sum = head_sum[:, :CLS].astype(jnp.float32)
    input_sum = jnp.stack(
        [jnp.concatenate(pair, 1) for pair in (input_zero_sums, input_one_sums)]
    ).astype(jnp.float32)
    output_sum = jnp.stack([output_zero_sum, jnp.concatenate(output_one_sums, 1)]).astype(
        jnp.float32
    )
    vector_sum = small_share[:vector_rows].reshape(-1)[:vector_size].reshape(layer_vector.shape)
    grad_norm = (
        jnp.sqrt(
            jnp.sum(small_full[:, -1])
            + jnp.sum(jnp.square(small_full[:, :vector_rows]))
            + jnp.sum(position_sum * position_sum)
            + jnp.sum(global_sum * global_sum)
        )
        / token_total
    )
    factor = jnp.minimum(1.0, CLIP_NORM / grad_norm) / token_total
    patch_next = adam_update(
        kernel_sum, patch_moment, patch_square, patch_kernel, factor, LEARN_RATE
    )
    head_next = adam_update(head_sum, head_moment, head_square, head_weight, factor, LEARN_RATE)
    input_next = adam_update(input_sum, input_moment, input_square, input_proj, factor, LEARN_RATE)
    output_next = adam_update(
        output_sum, output_moment, output_square, output_proj, factor, LEARN_RATE
    )
    layer_next = adam_update(
        vector_sum, layer_moment, layer_square, layer_vector, factor, VECTOR_RATE
    )
    position_next = adam_update(
        position_sum, position_moment, position_square, position_table, factor, LEARN_RATE
    )
    global_next = adam_update(
        global_sum, global_moment, global_square, global_vector, factor, VECTOR_RATE
    )
    return (
        loss_sum,
        token_total,
        grad_norm,
        patch_next[0],
        head_next[0],
        input_next[0],
        output_next[0],
        layer_next[0],
        position_next[0],
        global_next[0],
        patch_next[1],
        head_next[1],
        input_next[1],
        output_next[1],
        layer_next[1],
        position_next[1],
        global_next[1],
        patch_next[2],
        head_next[2],
        input_next[2],
        output_next[2],
        layer_next[2],
        position_next[2],
        global_next[2],
    )


def solution(mesh):
    in_specs = (
        P(("dp", "fsdp"), None),
        P(("dp", "fsdp")),
        P(("dp", "fsdp"), None),
        P(("dp", "fsdp"), None),
        P("fsdp", None),
        P("fsdp", None),
        P(None, "fsdp", None),
        P(None, "fsdp", None),
        P(None, "fsdp"),
        P(),
        P(),
        P("fsdp", None),
        P("fsdp", None),
        P(None, "fsdp", None),
        P(None, "fsdp", None),
        P(None, "fsdp"),
        P(),
        P(),
        P("fsdp", None),
        P("fsdp", None),
        P(None, "fsdp", None),
        P(None, "fsdp", None),
        P(None, "fsdp"),
        P(),
        P(),
    )
    out_specs = (
        P(),
        P(),
        P(),
        P("fsdp", None),
        P("fsdp", None),
        P(None, "fsdp", None),
        P(None, "fsdp", None),
        P(None, "fsdp"),
        P(),
        P(),
        P("fsdp", None),
        P("fsdp", None),
        P(None, "fsdp", None),
        P(None, "fsdp", None),
        P(None, "fsdp"),
        P(),
        P(),
        P("fsdp", None),
        P("fsdp", None),
        P(None, "fsdp", None),
        P(None, "fsdp", None),
        P(None, "fsdp"),
        P(),
        P(),
    )
    return jax.shard_map(body, mesh=mesh, in_specs=in_specs, out_specs=out_specs, check_vma=False)
```

```python
import functools

import jax
import jax.numpy as jnp
from jax import lax
from jax.experimental import pallas as pl
from jax.experimental.pallas import tpu as pltpu
from jax.sharding import PartitionSpec as P

D = 768
HEADS = 12
HD = 64
CLS = 1000
GRID = 7
IMG = 240
IMGS = 8
LAYERS = 2
STEP = 3


NORM_EPS = 1e-06
CLIP_NORM = 0.01
LEARN_RATE = 0.05
VECTOR_RATE = 0.25
BETA_ONE = 0.5
BETA_TWO = 0.5
ADAM_EPS = 1e-08
WEIGHT_DECAY = 0.05
HIGHEST = lax.Precision.HIGHEST

PAIR = 2 * HD
MASKED = -1e30
MIB = 1024 * 1024
VMEM_LIMIT = 56 * MIB
MESH = pl.DeviceIdType.MESH
LANES = 128
LOW = jnp.bfloat16
ANYWHERE = pl.BlockSpec(memory_space=pl.ANY)
NO_COST = pl.CostEstimate(flops=0, bytes_accessed=0, transcendentals=0)
ROOT = 0.7978845608028654
CUBE = 0.044715
NT = (((1,), (1,)), ((), ()))


def layer_norm(values, gain, shift):
    center = values - jnp.mean(values, -1, keepdims=True)
    spread = jnp.mean(center * center, -1, keepdims=True)
    return center * lax.rsqrt(spread + NORM_EPS) * gain + shift


def rounded(values):
    return lax.optimization_barrier(values.astype(jnp.bfloat16)).astype(jnp.float32)


def matmul(left, right):
    return jnp.dot(left, right, preferred_element_type=jnp.float32)


def padded_rows(flat, multiple):
    extra = -flat.shape[0] % (multiple * LANES)
    return jnp.pad(flat, (0, extra)).reshape(-1, LANES)


def row_layout(seg_row, patch_row):
    row_count = seg_row.shape[0]
    slots = jnp.arange(IMGS, dtype=jnp.int32)
    member = seg_row[:, None] == slots[None, :]
    counts = jnp.sum(member.astype(jnp.int32), 0, dtype=jnp.int32)
    starts = jnp.cumsum(counts, dtype=jnp.int32) - counts
    inside = jnp.any(member, 1)
    offset = jnp.arange(row_count, dtype=jnp.int32) - jnp.sum(
        jnp.where(member, starts[None, :], 0), 1, dtype=jnp.int32
    )
    offset = jnp.where(inside, offset, 0)
    patch_tok = jnp.sum(jnp.where(member, patch_row[None, :], 0), 1, dtype=jnp.int32) + jnp.where(
        inside, 0, IMG
    )
    side = IMG // patch_tok
    nodes = jnp.arange(GRID, dtype=jnp.int32).astype(jnp.float32)

    def hat(coord):
        place = ((2 * coord + 1) * GRID).astype(jnp.float32) / (2 * side).astype(jnp.float32) - 0.5
        place = jnp.clip(place, 0.0, GRID - 1.0)
        return jnp.maximum(1.0 - jnp.abs(place[:, None] - nodes[None, :]), 0.0)

    weights = (hat(offset // side)[:, :, None] * hat(offset % side)[:, None, :]).reshape(
        row_count, GRID * GRID
    )
    return (weights, member.astype(jnp.float32), counts.astype(jnp.float32))


TURNS = (1, 2, 3)


def place():
    slot = lax.axis_index("fsdp")
    return lax.axis_index("dp"), lax.div(slot, 2), lax.rem(slot, 2)


def partner(index, turn):
    if turn == 0:
        return index
    if turn == 1:
        return index + 1 - 2 * lax.rem(index, 2)
    if turn == 2:
        return lax.rem(index + 2, 4)
    return 3 - index


def greet():
    group, level, core = place()
    barrier = pltpu.get_barrier_semaphore()
    peers = [(group, 2 * level + 1 - core)]
    for turn in TURNS:
        peers.append((group, 2 * partner(level, turn) + core))
        peers.append((partner(group, turn), 2 * level + core))
    for peer in peers:
        pl.semaphore_signal(barrier, inc=1, device_id=peer, device_id_type=MESH)
    pl.semaphore_wait(barrier, len(peers))


def quarter_shape(rows, columns):
    if columns % (2 * LANES) == 0:
        return rows // 2, columns // 2
    return rows // 4, columns


def quarter(index, rows, columns):
    high, wide = quarter_shape(rows, columns)
    if wide == columns:
        return pl.ds(pl.multiple_of(index * high, high), high), pl.ds(0, columns)
    return (
        pl.ds(pl.multiple_of(lax.div(index, 2) * high, high), high),
        pl.ds(pl.multiple_of(lax.rem(index, 2) * wide, wide), wide),
    )


def remote(source, target, send, receive, device):
    return pltpu.make_async_remote_copy(
        src_ref=source,
        dst_ref=target,
        send_sem=send,
        recv_sem=receive,
        device_id=device,
        device_id_type=MESH,
    )


GATHER_SEMS = 33


class Gather:
    def __init__(self, shard, out, sems, split, in_place=False):
        self.shard, self.out, self.sems, self.split = shard, out, sems, split
        self.in_place = in_place
        self.rows, self.columns = shard.shape

    def level_copy(self, turn):
        group, level, core = place()
        block = self.out.at[2 * level + core]
        source = self.shard
        if self.split:
            part = quarter(group, self.rows, self.columns)
            source, block = source.at[part], block.at[part]
        sems = self.sems
        peer = (group, 2 * partner(level, turn) + core)
        return remote(source, block, sems.at[turn], sems.at[3 + turn], peer)

    def group_copy(self, turn, other):
        group, level, core = place()
        part = quarter(group, self.rows, self.columns)
        block = self.out.at[2 * partner(level, turn) + core].at[part]
        index = 3 * (turn - 1) + other - 1
        peer = (partner(group, other), 2 * level + core)
        return remote(block, block, self.sems.at[7 + index], self.sems.at[16 + index], peer)

    def core_copy(self, turn):
        group, level, core = place()
        slot = 2 * partner(level, turn) + core
        source = self.shard if turn == 0 else self.out.at[slot]
        peer = (group, 2 * level + 1 - core)
        return remote(source, self.out.at[slot], self.sems.at[25 + turn], self.sems.at[29 + turn], peer)

    def own_copy(self):
        _, level, core = place()
        return pltpu.make_async_copy(self.shard, self.out.at[2 * level + core], self.sems.at[0])

    def first(self):
        for turn in TURNS:
            self.level_copy(turn).start()
        self.core_copy(0).start()
        if not self.in_place:
            self.own_copy().start()

    def second(self):
        for turn in TURNS:
            self.level_copy(turn).wait_recv()
            if self.split:
                for other in TURNS:
                    self.group_copy(turn, other).start()
            else:
                self.core_copy(turn).start()

    def third(self, use=None):
        for turn in TURNS if self.split else ():
            for other in TURNS:
                self.group_copy(turn, other).wait_recv()
            self.core_copy(turn).start()
            if use is not None:
                use(turn, True)

    def fourth(self, use=None):
        for turn in TURNS if use is not None else (0, *TURNS):
            self.core_copy(turn).wait_recv()
            if use is not None:
                use(turn, False)
        for turn in TURNS:
            self.level_copy(turn).wait_send()
            if self.split:
                for other in TURNS:
                    self.group_copy(turn, other).wait_send()
        for turn in (0, *TURNS):
            self.core_copy(turn).wait_send()
        if not self.in_place:
            self.own_copy().wait()


class LevelGather:
    def __init__(self, shard, out, sems):
        self.shard, self.out, self.sems = shard, out, sems

    def level_copy(self, turn):
        group, level, core = place()
        return remote(
            self.shard.at[quarter(group, *self.shard.shape)],
            self.out.at[level],
            self.sems.at[turn],
            self.sems.at[3 + turn],
            (group, 2 * partner(level, turn) + core),
        )

    def first(self):
        for turn in TURNS:
            self.level_copy(turn).start()

    def second(self):
        pass

    def third(self):
        pass

    def fourth(self):
        for turn in TURNS:
            self.level_copy(turn).wait_recv()
            self.level_copy(turn).wait_send()

    def store(self):
        _, level, _ = place()
        self.out[level] = jnp.zeros(self.out.shape[1:], self.out.dtype)
        self.target[...] = self.out[...]


GROUP_GATHER_SEMS = 30


class GroupGather:
    def __init__(self, shard, quarters, out, sems):
        self.shard, self.quarters, self.out, self.sems = shard, quarters, out, sems

    def part(self, turn):
        group, level, core = place()
        block = self.out.at[2 * partner(level, turn) + core]
        return block.at[quarter(group, *self.shard.shape)]

    def own_copy(self, turn):
        _, level, core = place()
        if turn == 0:
            source, target = self.shard, self.out.at[2 * level + core]
        else:
            source, target = self.quarters.at[partner(level, turn)], self.part(turn)
        return pltpu.make_async_copy(source, target, self.sems.at[turn])

    def group_copy(self, turn, other):
        group, level, core = place()
        index = 3 * (turn - 1) + other - 1
        return remote(
            self.quarters.at[partner(level, turn)],
            self.part(turn),
            self.sems.at[4 + index],
            self.sems.at[13 + index],
            (partner(group, other), 2 * level + core),
        )

    def core_copy(self, turn):
        group, level, core = place()
        slot = 2 * partner(level, turn) + core
        source = self.shard if turn == 0 else self.out.at[slot]
        peer = (group, 2 * level + 1 - core)
        return remote(source, self.out.at[slot], self.sems.at[22 + turn], self.sems.at[26 + turn], peer)

    def first(self):
        for turn in TURNS:
            for other in TURNS:
                self.group_copy(turn, other).start()
        for turn in (0, *TURNS):
            self.own_copy(turn).start()
        self.core_copy(0).start()

    def second(self):
        for turn in TURNS:
            for other in TURNS:
                self.group_copy(turn, other).wait_recv()
            self.own_copy(turn).wait()
            self.core_copy(turn).start()

    def third(self):
        for turn in (0, *TURNS):
            self.core_copy(turn).wait_recv()
            self.core_copy(turn).wait_send()
        for turn in TURNS:
            for other in TURNS:
                self.group_copy(turn, other).wait_send()
        self.own_copy(0).wait()

    def store(self):
        copy = pltpu.make_async_copy(self.out, self.target, self.sems.at[0])
        copy.start()
        copy.wait()


class LevelRide:
    def __init__(self, shard):
        self.operands = [shard]
        shape = (4, *quarter_shape(*shard.shape))
        self.out_specs = [fixed(*shape)]
        self.out_shapes = [jax.ShapeDtypeStruct(shape, shard.dtype)]
        self.scratch = [pltpu.VMEM(shape, shard.dtype), pltpu.SemaphoreType.DMA((7,))]

    def job(self, sources, targets, scratch):
        job = LevelGather(sources[0], *scratch)
        job.target = targets[0]
        return job

    def before(self, steps):
        return {0: ("first",)}

    after = ("fourth", "store")

    def result(self, outs):
        return GatherRide(self.operands[0], outs[0])

    def plain(self):
        return GatherRide(self.operands[0], self.operands[0])


class GatherRide:
    def __init__(self, shard, quarters):
        owners = lax.axis_size("fsdp")
        full = (owners, *shard.shape)
        self.operands = [shard, quarters]
        self.out_specs = [ANYWHERE]
        self.out_shapes = [jax.ShapeDtypeStruct(full, shard.dtype)]
        self.scratch = [
            pltpu.VMEM(full, shard.dtype),
            pltpu.SemaphoreType.DMA((GROUP_GATHER_SEMS,)),
        ]

    def job(self, sources, targets, scratch):
        job = GroupGather(*sources, *scratch)
        job.target = targets[0]
        return job

    def before(self, steps):
        return {0: ("first",), max(1, 2 * steps // 3): ("second",)}

    after = ("third", "store")

    def result(self, outs):
        return outs[0].reshape(-1, outs[0].shape[2])

    def plain(self):
        return lax.all_gather(self.operands[0], "fsdp", axis=0, tiled=True)


class ShareRide:
    def __init__(self, share):
        self.operands = [share]
        self.out_specs = [fixed(*share.shape)]
        self.out_shapes = [jax.ShapeDtypeStruct(share.shape, share.dtype)]
        self.scratch = [
            pltpu.VMEM(share.shape, share.dtype),
            *share_scratch(share),
            pltpu.SemaphoreType.DMA((GROUP_SEMS,)),
        ]

    def job(self, sources, targets, scratch):
        job = GroupReduce(sources[0], scratch[0], scratch[1:3], scratch[3])
        job.target = targets[0]
        return job

    def before(self, steps):
        return {0: ("first", "second"), max(1, steps // 2): ("third",)}

    after = ("fifth", "sixth", "store")

    def result(self, outs):
        return outs[0]

    def plain(self):
        return lax.psum(self.operands[0], "dp")


def riding(body, counts, rides, steps):
    def kernel(*refs):
        refs = list(refs)

        def pop(count):
            taken = refs[:count]
            del refs[:count]
            return taken

        own = pop(counts[0])
        sources = [pop(len(ride.operands)) for ride in rides]
        own += pop(counts[1])
        targets = [pop(len(ride.out_shapes)) for ride in rides]
        own += pop(counts[2])
        jobs = [
            ride.job(source, target, pop(len(ride.scratch)))
            for ride, source, target in zip(rides, sources, targets)
        ]
        for step in range(steps):
            planned = [
                (job, stages)
                for ride, job in zip(rides, jobs)
                for at, stages in ride.before(steps).items()
                if at == step
            ]
            if planned:

                @pl.when(pl.program_id(0) == step)
                def _(planned=planned, step=step):
                    if step == 0:
                        greet()
                    for job, stages in planned:
                        run_stages([job], stages)

        body(*own)

        @pl.when(pl.program_id(0) == steps - 1)
        def _():
            for ride, job in zip(rides, jobs):
                run_stages([job], ride.after)

    return kernel


def block_call(
    body, grid, in_specs, operands, out_specs, out_shape, scratch, name,
    cost=None, rides=(), collective_id=None,
):
    plain = []
    if rides and not with_kernels():
        plain, rides = [ride.plain() for ride in rides], ()
    transfer = {}
    kernel = body
    if rides:
        transfer = {"collective_id": collective_id, "has_side_effects": True}
        kernel = riding(body, (len(operands), len(out_shape), len(scratch)), rides, grid)
    count = len(out_shape)
    for ride in rides:
        operands = [*operands, *ride.operands]
        in_specs = [*in_specs, *[fixed(*operand.shape) for operand in ride.operands]]
        out_specs, out_shape = [*out_specs, *ride.out_specs], [*out_shape, *ride.out_shapes]
        scratch = [*scratch, *ride.scratch]
    outs = pl.pallas_call(
        kernel,
        grid=(grid,),
        in_specs=in_specs,
        out_specs=out_specs,
        out_shape=out_shape,
        scratch_shapes=scratch,
        compiler_params=pltpu.CompilerParams(vmem_limit_bytes=VMEM_LIMIT, **transfer),
        cost_estimate=cost or NO_COST,
        name=name,
    )(*operands)
    brought, outs = list(outs[count:]), list(outs[:count])
    for ride in rides:
        plain.append(ride.result(brought[: len(ride.out_shapes)]))
        brought = brought[len(ride.out_shapes) :]
    return outs + plain


def work(flops, size):
    return pl.CostEstimate(flops=flops, bytes_accessed=size, transcendentals=0)


def position_weights(seg_col, patch_row, nodes):
    rows = seg_col.shape[0]
    slot = lax.broadcasted_iota(jnp.int32, (rows, IMGS), 1)
    member = seg_col == slot
    counts = jnp.sum(member.astype(jnp.float32), 0, keepdims=True)
    start = jnp.sum(jnp.where(slot < seg_col, counts, 0.0), 1, keepdims=True)
    token = lax.broadcasted_iota(jnp.int32, (rows, 1), 0).astype(jnp.float32)
    inside = seg_col < IMGS
    offset = jnp.where(inside, token - start, 0.0)
    patch = jnp.sum(jnp.where(member, patch_row.astype(jnp.float32), 0.0), 1, keepdims=True)
    side = jnp.where(inside, jnp.floor(IMG / jnp.where(inside, patch, 1.0) + 0.5), 1.0)
    line = jnp.floor((offset + 0.5) / side)
    column = offset - line * side

    def spot(coord):
        return jnp.clip((2.0 * coord + 1.0) * GRID / (2.0 * side) - 0.5, 0.0, GRID - 1.0)

    node = lax.broadcasted_iota(jnp.int32, (rows, LANES), 1).astype(jnp.float32)
    across = jnp.floor((node + 0.5) / GRID)
    along = node - across * GRID
    weights = jnp.maximum(1.0 - jnp.abs(spot(line) - across), 0.0)
    weights = weights * jnp.maximum(1.0 - jnp.abs(spot(column) - along), 0.0)
    return jnp.where(node < nodes, weights, 0.0)


def first_kernel(*refs, spots):
    kernel, vectors, inputs, outputs, head, pixels, seg_col, patch_row, table, biases = refs[:10]
    stream, pos_t, vector_zero, vector_one = refs[10:14]
    qkv_full, up_level, up_zero, qkv_one, up_one, output_one, head_low = refs[14:21]
    wide_kernel, wide_inputs, wide_outputs, wide_head, pixel_rows, table_low = refs[21:27]
    kernel_full, qkv_zero, vectors_full, qkv_landing, up_landing, load_sems, sems = refs[27:]
    _, level, core = place()
    mine = 2 * level + core
    pairs = [
        (kernel, wide_kernel),
        (inputs.at[0], wide_inputs.at[0]),
        (pixels, pixel_rows),
        (inputs.at[1], wide_inputs.at[1]),
        (outputs.at[1], wide_outputs),
        (head, wide_head),
    ]
    copies = [
        pltpu.make_async_copy(source, target, load_sems.at[index])
        for index, (source, target) in enumerate(pairs)
    ]
    for copy in copies:
        copy.start()
    patch_job = Gather(kernel_full.at[mine], kernel_full, sems.at[0], True, in_place=True)
    vector_job = Gather(vectors, vectors_full, sems.at[1], False)
    qkv_job = Gather(qkv_zero, qkv_landing, sems.at[2], True)
    up_job = LevelGather(up_zero, up_landing, sems.at[3])
    up_job.target = up_level
    copies[0].wait()
    kernel_full[mine] = wide_kernel[...].astype(LOW)
    greet()
    patch_job.first()
    vector_job.first()
    copies[1].wait()
    qkv_zero[...] = wide_inputs[0, :, : 3 * D].astype(LOW)
    qkv_job.first()
    up_zero[...] = wide_inputs[0, :, 3 * D :].astype(LOW)
    up_job.first()

    weights = position_weights(seg_col[...], patch_row[...], table.shape[0])
    pos_t[...] = weights.T[: pos_t.shape[0], :]
    table_low[...] = jnp.zeros_like(table_low)
    table_low[: table.shape[0], :] = table[...].astype(LOW).astype(jnp.float32)
    bias = biases[:, :D].astype(LOW).astype(jnp.float32)
    stream[...] = bias + jnp.dot(
        weights, table_low[...], precision=HIGHEST, preferred_element_type=jnp.float32
    )
    copies[2].wait()
    depth = wide_kernel.shape[0]

    def add_block(slot):
        columns = pl.ds(pl.multiple_of(slot * depth, depth), depth)

        def add(step, carry):
            rows = pl.ds(pl.multiple_of(step * 256, 256), 256)
            stream[rows, :] += mul(pixel_rows[rows, columns], kernel_full[slot])
            return carry

        lax.fori_loop(0, stream.shape[0] // 256, add, 0)

    def use(turn, own_core):
        add_block(2 * partner(level, turn) + (core if own_core else 1 - core))

    add_block(mine)
    patch_job.second()
    vector_job.second()
    qkv_job.second()
    patch_job.core_copy(0).wait_recv()
    use(0, False)
    copies[3].wait()
    qkv_one[...] = wide_inputs[1, :, : 3 * D].astype(LOW)
    up_one[...] = wide_inputs[1, :, 3 * D :].astype(LOW)
    copies[4].wait()
    output_one[...] = wide_outputs[...].astype(LOW)
    copies[5].wait()
    head_low[...] = jnp.zeros_like(head_low)
    head_low[:, : head.shape[1]] = wide_head[...].astype(LOW)
    patch_job.third(use)
    qkv_job.third()
    patch_job.fourth(use)
    vector_job.third()
    vector_job.fourth()
    blocks = [vectors_full[slot].astype(jnp.float32) for slot in range(vectors_full.shape[0])]
    span = vectors.shape[0] // LAYERS
    for layer, out in enumerate((vector_zero, vector_one)):
        for row in range(out.shape[1] // LANES):
            parts = [
                block[layer * span + row - spot : layer * span + row - spot + 1, :]
                for block, spot in zip(blocks, spots)
                if 0 <= row - spot < span
            ]
            out[:, row * LANES : (row + 1) * LANES] = sum(parts)
    qkv_job.fourth()
    copy = pltpu.make_async_copy(qkv_landing, qkv_full, load_sems.at[0])
    copy.start()
    up_job.fourth()
    up_job.store()
    copy.wait()


def padded_vectors(shard):
    layers, width = shard.shape
    owners = lax.axis_size("fsdp")
    spots = [owner * width // LANES for owner in range(owners)]
    span = max(-(-(owner + 1) * width // LANES) - spot for owner, spot in enumerate(spots))
    span += -span % 16
    shift = lax.rem(lax.axis_index("fsdp") * width, LANES)
    padded = jnp.zeros((layers, span * LANES), LOW)
    padded = lax.dynamic_update_slice(padded, shard.astype(LOW), (0, shift))
    return padded.reshape(layers * span, LANES), spots


def begin(
    pixels, segment, patch_size, patch_kernel, layer_vector, input_proj, output_proj, head_weight,
    position_table, global_vector,
):
    classes = head_weight.shape[1] + -head_weight.shape[1] % LANES
    nodes = position_table.shape[0] + -position_table.shape[0] % 64
    if not with_kernels():
        inputs = [
            (input_proj[index, :, : 3 * D].astype(LOW), input_proj[index, :, 3 * D :].astype(LOW))
            for index in range(LAYERS)
        ]
        outputs = [output_proj[index].astype(LOW) for index in range(LAYERS)]
        gather = lambda shard, axis: lax.all_gather(shard, "fsdp", axis=axis, tiled=True)
        weights, _, _ = row_layout(segment, patch_size[0])
        weights = jnp.pad(weights, ((0, 0), (0, nodes - weights.shape[1])))
        table = jnp.pad(rounded(position_table), ((0, nodes - position_table.shape[0]), (0, 0)))
        bias = rounded(global_vector)[None, :D]
        stream = embed(pixels, gather(patch_kernel.astype(LOW), 0), weights, table, bias)
        vectors = gather(layer_vector.astype(LOW), 1).astype(jnp.float32)
        head = jnp.pad(head_weight.astype(LOW), ((0, 0), (0, classes - head_weight.shape[1])))
        return (
            stream,
            weights.T,
            [vectors[index : index + 1] for index in range(LAYERS)],
            gather(inputs[0][0], 0),
            [GatherRide(inputs[0][1], inputs[0][1]), LevelRide(inputs[1][0]), LevelRide(outputs[1])],
            [inputs[1][1], head],
        )
    rows = pixels.shape[0]
    owners = lax.axis_size("fsdp")
    vectors, spots = padded_vectors(layer_vector)
    depth = input_proj.shape[1]
    up_shape = (depth, input_proj.shape[2] - 3 * D)
    qkv_shape, out_shape = (depth, 3 * D), output_proj.shape[1:]
    low = lambda *shape: jax.ShapeDtypeStruct(shape, LOW)
    levels = lambda shape: low(4, *quarter_shape(*shape))
    width = layer_vector.shape[1] * owners
    shapes = [
        shape_of(rows, D),
        shape_of(nodes, rows),
        shape_of(1, width),
        shape_of(1, width),
        low(owners, *qkv_shape),
        levels(up_shape),
        low(*up_shape),
        low(*qkv_shape),
        low(*up_shape),
        low(*out_shape),
        low(head_weight.shape[0], classes),
    ]
    wide = (patch_kernel, input_proj, output_proj[0], head_weight, pixels)
    in_vmem = pl.BlockSpec(memory_space=pltpu.VMEM)
    results = pl.pallas_call(
        functools.partial(first_kernel, spots=spots),
        in_specs=[ANYWHERE] * 6 + [in_vmem] * 4,
        out_specs=[in_vmem] * 4 + [ANYWHERE] + [in_vmem] * 6,
        out_shape=shapes,
        scratch_shapes=[
            *[pltpu.VMEM(array.shape, array.dtype) for array in wide],
            pltpu.VMEM((LANES, D), jnp.float32),
            pltpu.VMEM((owners, *patch_kernel.shape), LOW),
            pltpu.VMEM(qkv_shape, LOW),
            pltpu.VMEM((owners, *vectors.shape), LOW),
            pltpu.VMEM((owners, *qkv_shape), LOW),
            pltpu.VMEM((4, *quarter_shape(*up_shape)), LOW),
            pltpu.SemaphoreType.DMA((6,)),
            pltpu.SemaphoreType.DMA((4, GATHER_SEMS)),
        ],
        compiler_params=pltpu.CompilerParams(
            collective_id=1, has_side_effects=True, vmem_limit_bytes=VMEM_LIMIT
        ),
        cost_estimate=NO_COST,
        name="begin",
    )(
        patch_kernel,
        vectors,
        input_proj,
        output_proj,
        head_weight,
        pixels,
        segment[:, None],
        patch_size,
        position_table,
        global_vector[None, :],
    )
    up_zero, qkv_one, up_one, output_one, head_low = results[6:]
    return (
        results[0],
        results[1],
        results[2:4],
        results[4].reshape(owners * depth, 3 * D),
        [GatherRide(up_zero, results[5]), LevelRide(qkv_one), LevelRide(output_one)],
        [up_one, head_low],
    )


REDUCE_SEMS = 48


class Reduce:
    def __init__(self, grad, out, scratch, sems):
        self.grad, self.out, self.sems = grad, out, sems
        self.own, self.got_core, self.got_group, self.part, self.got_level = scratch
        self.rows, self.columns = out.shape
        self.chunk = 16

    def load(self, level):
        _, _, core = place()
        return pltpu.make_async_copy(
            self.grad.at[2 * level + core], self.own.at[level], self.sems.at[level]
        )

    def core_copy(self, target_level):
        group, level, core = place()
        return remote(
            self.grad.at[2 * target_level + 1 - core],
            self.got_core.at[target_level],
            self.sems.at[4 + target_level],
            self.sems.at[8 + target_level],
            (group, 2 * level + 1 - core),
        )

    def group_copy(self, turn, other):
        group, level, core = place()
        target = partner(level, turn)
        peer = partner(group, other)
        part = quarter(peer, self.rows, self.columns)
        index = 3 * turn + other - 1
        return remote(
            self.own.at[target].at[part],
            self.got_group.at[other - 1, target],
            self.sems.at[12 + index],
            self.sems.at[24 + index],
            (peer, 2 * level + core),
        )

    def level_copy(self, turn):
        group, level, core = place()
        target = partner(level, turn)
        return remote(
            self.part.at[target],
            self.got_level.at[turn - 1],
            self.sems.at[35 + turn],
            self.sems.at[38 + turn],
            (group, 2 * target + core),
        )

    def share_copy(self, other):
        group, level, core = place()
        mine = self.out.at[quarter(group, self.rows, self.columns)]
        return remote(
            mine,
            mine,
            self.sems.at[41 + other],
            self.sems.at[44 + other],
            (partner(group, other), 2 * level + core),
        )

    def first(self):
        _, level, _ = place()
        for turn in (*TURNS, 0):
            self.core_copy(partner(level, turn)).start()
            self.load(partner(level, turn)).start()

    def second(self):
        _, level, _ = place()
        for turn in (*TURNS, 0):
            target = partner(level, turn)
            self.load(target).wait()
            self.core_copy(target).wait_recv()

            def add(step, carry):
                rows = pl.ds(pl.multiple_of(step * self.chunk, self.chunk), self.chunk)
                total = self.own[target, rows, :].astype(jnp.float32)
                total = total + self.got_core[target, rows, :].astype(jnp.float32)
                self.own[target, rows, :] = total.astype(self.own.dtype)
                return carry

            lax.fori_loop(0, self.rows // self.chunk, add, 0)
            for other in TURNS:
                self.group_copy(turn, other).start()

    def between(self):
        pass

    def third(self):
        group, level, _ = place()
        high, wide = quarter_shape(self.rows, self.columns)
        row_part, column_part = quarter(group, self.rows, self.columns)
        for turn in (*TURNS, 0):
            target = partner(level, turn)
            for other in TURNS:
                self.group_copy(turn, other).wait_recv()

            def add(step, carry):
                at = pl.multiple_of(step * self.chunk, self.chunk)
                rows = pl.ds(at, self.chunk)
                mine = pl.ds(pl.multiple_of(row_part.start + at, self.chunk), self.chunk)
                total = self.own[target, mine, column_part].astype(jnp.float32)
                for slot in range(3):
                    total = total + self.got_group[slot, target, rows, :].astype(jnp.float32)
                self.part[target, rows, :] = total.astype(self.part.dtype)
                return carry

            lax.fori_loop(0, high // self.chunk, add, 0)
            if turn:
                self.level_copy(turn).start()

    def fourth(self):
        group, level, _ = place()
        high, wide = quarter_shape(self.rows, self.columns)
        row_part, column_part = quarter(group, self.rows, self.columns)
        for turn in TURNS:
            self.level_copy(turn).wait_recv()

        def add(step, carry):
            at = pl.multiple_of(step * self.chunk, self.chunk)
            rows = pl.ds(at, self.chunk)
            mine = pl.ds(pl.multiple_of(row_part.start + at, self.chunk), self.chunk)
            total = self.part[level, rows, :].astype(jnp.float32)
            for slot in range(3):
                total = total + self.got_level[slot, rows, :].astype(jnp.float32)
            self.out[mine, column_part] = total.astype(self.out.dtype)
            return carry

        lax.fori_loop(0, high // self.chunk, add, 0)
        for other in TURNS:
            self.share_copy(other).start()

    def fifth(self):
        for other in TURNS:
            self.share_copy(other).wait_recv()

    def sixth(self):
        _, level, _ = place()
        for turn in (*TURNS, 0):
            self.core_copy(partner(level, turn)).wait_send()
            for other in TURNS:
                self.group_copy(turn, other).wait_send()
            if turn:
                self.level_copy(turn).wait_send()
                self.share_copy(turn).wait_send()


WHOLE_SEMS = 40


def add_rows(target, row, columns, source, count, wide):
    chunk = 16 if wide > 1536 else 48

    def add(step, carry):
        at = pl.multiple_of(step * chunk, chunk)
        mine = pl.ds(pl.multiple_of(row + at, 16), chunk)
        total = target[mine, columns].astype(jnp.float32)
        total = total + source[pl.ds(at, chunk), :].astype(jnp.float32)
        target[mine, columns] = total.astype(target.dtype)
        return carry

    lax.fori_loop(0, count // chunk, add, 0)


class Whole:
    FIRST_X = (1, 0)

    def __init__(self, grad, out, scratch, sems):
        self.grad, self.out, self.sems = grad, out, sems
        self.own, self.got_core, self.got_x, self.got_y, self.got_last, self.part, self.got_level = scratch
        self.rows, self.columns = out.shape
        self.high, self.wide = self.rows // 2, self.columns // 2

    def row_half(self, index):
        return pl.ds(pl.multiple_of(lax.div(index, 2) * self.high, self.high), self.high)

    def column_half(self, index):
        return pl.ds(pl.multiple_of(lax.rem(index, 2) * self.wide, self.wide), self.wide)

    def load(self, level):
        _, _, core = place()
        return pltpu.make_async_copy(
            self.grad.at[2 * level + core], self.own.at[level], self.sems.at[level]
        )

    def core_copy(self, target_level):
        group, level, core = place()
        return remote(
            self.grad.at[2 * target_level + 1 - core],
            self.got_core.at[target_level],
            self.sems.at[4 + target_level],
            self.sems.at[8 + target_level],
            (group, 2 * level + 1 - core),
        )

    def step_copy(self, turn):
        group, level, core = place()
        block = self.own.at[partner(level, turn)]
        if turn in self.FIRST_X:
            peer = partner(group, 1)
            source = block.at[:, self.column_half(peer)]
            target = self.got_x.at[self.FIRST_X.index(turn)]
        else:
            peer = partner(group, 2)
            source = block.at[self.row_half(peer), :]
            target = self.got_y.at[turn - 2]
        return remote(
            source, target, self.sems.at[12 + turn], self.sems.at[16 + turn], (peer, 2 * level + core)
        )

    def last_copy(self, turn):
        group, level, core = place()
        block = self.own.at[partner(level, turn)]
        peer = partner(group, 2 if turn in self.FIRST_X else 1)
        rows = self.row_half(peer)
        columns = self.column_half(peer)
        return remote(
            block.at[rows, columns],
            self.got_last.at[turn],
            self.sems.at[20 + turn],
            self.sems.at[24 + turn],
            (peer, 2 * level + core),
        )

    def level_copy(self, turn):
        group, level, core = place()
        target = partner(level, turn)
        return remote(
            self.part.at[target],
            self.got_level.at[turn - 1],
            self.sems.at[27 + turn],
            self.sems.at[30 + turn],
            (group, 2 * target + core),
        )

    def share_copy(self, other):
        group, level, core = place()
        mine = self.out.at[self.row_half(group), self.column_half(group)]
        return remote(
            mine,
            mine,
            self.sems.at[33 + other],
            self.sems.at[36 + other],
            (partner(group, other), 2 * level + core),
        )

    def first(self):
        _, level, _ = place()
        for turn in (*TURNS, 0):
            self.core_copy(partner(level, turn)).start()
            self.load(partner(level, turn)).start()

    def second(self):
        _, level, _ = place()
        for turn in (*TURNS, 0):
            target = partner(level, turn)
            self.load(target).wait()
            self.core_copy(target).wait_recv()
            add_rows(
                self.own.at[target], 0, slice(None), self.got_core.at[target], self.rows, self.columns
            )
            self.step_copy(turn).start()

    def between(self):
        group, level, _ = place()
        for turn in (*TURNS, 0):
            block = self.own.at[partner(level, turn)]
            self.step_copy(turn).wait_recv()
            if turn in self.FIRST_X:
                source = self.got_x.at[self.FIRST_X.index(turn)]
                add_rows(block, 0, self.column_half(group), source, self.rows, self.wide)
            else:
                source = self.got_y.at[turn - 2]
                start = lax.div(group, 2) * self.high
                add_rows(block, start, slice(None), source, self.high, self.columns)
            self.last_copy(turn).start()

    def third(self):
        group, level, _ = place()
        start = lax.div(group, 2) * self.high
        columns = self.column_half(group)
        chunk = 16 if self.wide > 1536 else 48
        for turn in (*TURNS, 0):
            target = partner(level, turn)
            self.last_copy(turn).wait_recv()

            def add(step, carry):
                at = pl.multiple_of(step * chunk, chunk)
                rows = pl.ds(at, chunk)
                mine = pl.ds(pl.multiple_of(start + at, 16), chunk)
                total = self.own[target, mine, columns].astype(jnp.float32)
                total = total + self.got_last[turn, rows, :].astype(jnp.float32)
                self.part[target, rows, :] = total.astype(self.part.dtype)
                return carry

            lax.fori_loop(0, self.high // chunk, add, 0)
            if turn:
                self.level_copy(turn).start()

    def fourth(self):
        group, level, _ = place()
        start = lax.div(group, 2) * self.high
        columns = self.column_half(group)
        chunk = 16 if self.wide > 1536 else 48
        for turn in TURNS:
            self.level_copy(turn).wait_recv()

        def add(step, carry):
            at = pl.multiple_of(step * chunk, chunk)
            rows = pl.ds(at, chunk)
            mine = pl.ds(pl.multiple_of(start + at, 16), chunk)
            total = self.part[level, rows, :].astype(jnp.float32)
            for slot in range(3):
                total = total + self.got_level[slot, rows, :].astype(jnp.float32)
            self.out[mine, columns] = total.astype(self.out.dtype)
            return carry

        lax.fori_loop(0, self.high // chunk, add, 0)
        for other in TURNS:
            self.share_copy(other).start()

    def fifth(self):
        for other in TURNS:
            self.share_copy(other).wait_recv()

    def sixth(self):
        _, level, _ = place()
        for turn in (*TURNS, 0):
            self.core_copy(partner(level, turn)).wait_send()
            self.step_copy(turn).wait_send()
            self.last_copy(turn).wait_send()
            if turn:
                self.level_copy(turn).wait_send()
                self.share_copy(turn).wait_send()


GROUP_SEMS = 13


class GroupReduce:
    def __init__(self, share, out, scratch, sems):
        self.share, self.out, self.sems = share, out, sems
        self.own, self.got = scratch
        self.rows, self.columns = out.shape
        self.chunk = 16

    def load(self):
        return pltpu.make_async_copy(self.share, self.own, self.sems.at[0])

    def group_copy(self, other):
        group, level, core = place()
        peer = partner(group, other)
        return remote(
            self.own.at[quarter(peer, self.rows, self.columns)],
            self.got.at[other - 1],
            self.sems.at[other],
            self.sems.at[3 + other],
            (peer, 2 * level + core),
        )

    def share_copy(self, other):
        group, level, core = place()
        mine = self.out.at[quarter(group, self.rows, self.columns)]
        return remote(
            mine,
            mine,
            self.sems.at[6 + other],
            self.sems.at[9 + other],
            (partner(group, other), 2 * level + core),
        )

    def first(self):
        self.load().start()

    def second(self):
        self.load().wait()
        for other in TURNS:
            self.group_copy(other).start()

    def between(self):
        pass

    def third(self):
        group, _, _ = place()
        high, wide = quarter_shape(self.rows, self.columns)
        row_part, column_part = quarter(group, self.rows, self.columns)
        for other in TURNS:
            self.group_copy(other).wait_recv()

        def add(step, carry):
            at = pl.multiple_of(step * self.chunk, self.chunk)
            rows = pl.ds(at, self.chunk)
            mine = pl.ds(pl.multiple_of(row_part.start + at, self.chunk), self.chunk)
            total = self.own[mine, column_part].astype(jnp.float32)
            for slot in range(3):
                total = total + self.got[slot, rows, :].astype(jnp.float32)
            self.out[mine, column_part] = total.astype(self.out.dtype)
            return carry

        lax.fori_loop(0, high // self.chunk, add, 0)
        for other in TURNS:
            self.share_copy(other).start()

    def fourth(self):
        pass

    def fifth(self):
        for other in TURNS:
            self.share_copy(other).wait_recv()

    def store(self):
        self.target[...] = self.out[...]

    def sixth(self):
        for other in TURNS:
            self.group_copy(other).wait_send()
            self.share_copy(other).wait_send()


class Spread:
    def __init__(self, full, sems):
        self.full, self.sems = full, sems

    def level_copy(self, turn):
        group, level, core = place()
        block = self.full.at[2 * level + core]
        peer = (group, 2 * partner(level, turn) + core)
        return remote(block, block, self.sems.at[turn - 1], self.sems.at[2 + turn], peer)

    def core_copy(self, turn):
        group, level, core = place()
        block = self.full.at[2 * partner(level, turn) + core]
        peer = (group, 2 * level + 1 - core)
        return remote(block, block, self.sems.at[6 + turn], self.sems.at[10 + turn], peer)

    def run(self):
        for turn in TURNS:
            self.level_copy(turn).start()
        self.core_copy(0).start()
        for turn in TURNS:
            self.level_copy(turn).wait_recv()
            self.core_copy(turn).start()
        for turn in (0, *TURNS):
            self.core_copy(turn).wait_recv()
        for turn in (0, *TURNS):
            self.core_copy(turn).wait_send()
            if turn:
                self.level_copy(turn).wait_send()


def squares_in(out):
    def add(step, total):
        piece = out[pl.ds(pl.multiple_of(step * 16, 16), 16), :].astype(jnp.float32)
        piece = piece * piece
        for lane in range(0, out.shape[1], LANES):
            total = total + piece[:, lane : lane + LANES]
        return total

    total = lax.fori_loop(0, out.shape[0] // 16, add, jnp.zeros((16, LANES), jnp.float32))
    return jnp.sum(total, 0, keepdims=True)


def run_stages(jobs, stages):
    for stage in stages:
        for job in jobs:
            getattr(job, stage)()


STAGES = ("first", "second", "between", "third", "fourth", "fifth", "sixth")


def whole_scratch(grad):
    _, rows, columns = grad.shape
    high, wide = quarter_shape(rows, columns)
    shapes = ((4, rows, columns), (4, rows, columns), (3, 4, high, wide), (4, high, wide))
    return [pltpu.VMEM(shape, grad.dtype) for shape in (*shapes, (3, high, wide))]


def stepped_scratch(grad):
    _, rows, columns = grad.shape
    high, wide = rows // 2, columns // 2
    shapes = (
        (4, rows, columns),
        (4, rows, columns),
        (2, rows, wide),
        (2, high, columns),
        (4, high, wide),
        (4, high, wide),
        (3, high, wide),
    )
    return [pltpu.VMEM(shape, grad.dtype) for shape in shapes]


def share_scratch(share):
    return [
        pltpu.VMEM(share.shape, share.dtype),
        pltpu.VMEM((3, *quarter_shape(*share.shape)), share.dtype),
    ]


def reduce_kernel(*refs, whole, partly):
    count = whole + partly
    grads, outs, refs = refs[:count], refs[count : 2 * count], refs[2 * count :]
    sems, group_sems, refs = refs[0], refs[1], refs[2:]
    jobs = [
        Whole(grads[i], outs[i], refs[7 * i : 7 * i + 7], sems.at[i]) for i in range(whole)
    ]
    refs = refs[7 * whole :]
    shares = [
        GroupReduce(grads[whole + i], outs[whole + i], refs[2 * i : 2 * i + 2], group_sems.at[i])
        for i in range(partly)
    ]
    greet()
    run_stages([*jobs, *shares], STAGES[:1])
    run_stages(shares, STAGES[1:2])
    run_stages(jobs, STAGES[1:3])
    run_stages(shares, STAGES[3:4])
    run_stages(jobs, STAGES[3:5])
    run_stages([*shares, *jobs], STAGES[5:])


def transfer_cost(size):
    return pl.CostEstimate(flops=4000 * size, bytes_accessed=2 * size, transcendentals=0)


def reduce_call(grads, shares, collective_id):
    in_vmem = pl.BlockSpec(memory_space=pltpu.VMEM)
    whole, partly = len(grads), len(shares)
    scratch = [
        pltpu.SemaphoreType.DMA((whole, WHOLE_SEMS)),
        pltpu.SemaphoreType.DMA((partly, GROUP_SEMS)),
    ]
    for grad in grads:
        scratch.extend(stepped_scratch(grad))
    for share in shares:
        scratch.extend(share_scratch(share))
    out_shape = [jax.ShapeDtypeStruct(g.shape[1:], g.dtype) for g in grads]
    out_shape += [jax.ShapeDtypeStruct(s.shape, s.dtype) for s in shares]
    return pl.pallas_call(
        functools.partial(reduce_kernel, whole=whole, partly=partly),
        in_specs=[ANYWHERE] * (whole + partly),
        out_specs=[in_vmem] * (whole + partly),
        out_shape=out_shape,
        scratch_shapes=scratch,
        compiler_params=pltpu.CompilerParams(
            collective_id=collective_id, has_side_effects=True, vmem_limit_bytes=VMEM_LIMIT
        ),
        cost_estimate=NO_COST,
        name="reduce_gradients",
    )(*grads, *shares)


def finish_kernel(*refs, done, partly):
    finished, refs = refs[:done], refs[done:]
    shares, small, refs = refs[:partly], refs[partly], refs[partly + 1 :]
    outs, small_out, full, refs = refs[:partly], refs[partly], refs[partly + 1], refs[partly + 2 :]
    sems, group_sems, spread_sems, refs = refs[0], refs[1], refs[2], refs[3:]
    job = Reduce(small, small_out, refs[:5], sems)
    refs = refs[5:]
    jobs = [
        GroupReduce(shares[i], outs[i], refs[2 * i : 2 * i + 2], group_sems.at[i])
        for i in range(partly)
    ]
    greet()
    run_stages([job, *jobs], STAGES[:3])
    total = sum(squares_in(out) for out in finished)
    run_stages([*jobs, job], STAGES[3:6])
    total = total + sum(squares_in(out) for out in outs)
    _, level, core = place()
    mine = 2 * level + core
    last = small_out.shape[0] - 1
    full[mine] = small_out[...]
    full[mine, last : last + 1, :] = total
    Spread(full, spread_sems).run()
    run_stages([job, *jobs], STAGES[6:])


def finish_call(finished, shares, small, collective_id):
    done, partly = len(finished), len(shares)
    in_vmem = pl.BlockSpec(memory_space=pltpu.VMEM)
    scratch = [
        pltpu.SemaphoreType.DMA((REDUCE_SEMS,)),
        pltpu.SemaphoreType.DMA((partly, GROUP_SEMS)),
        pltpu.SemaphoreType.DMA((14,)),
        *whole_scratch(small),
    ]
    for share in shares:
        scratch.extend(share_scratch(share))
    out_shape = [jax.ShapeDtypeStruct(s.shape, s.dtype) for s in shares]
    out_shape.append(jax.ShapeDtypeStruct(small.shape[1:], small.dtype))
    out_shape.append(jax.ShapeDtypeStruct(small.shape, small.dtype))
    return pl.pallas_call(
        functools.partial(finish_kernel, done=done, partly=partly),
        in_specs=[in_vmem] * done + [ANYWHERE] * (partly + 1),
        out_specs=[in_vmem] * len(out_shape),
        out_shape=out_shape,
        scratch_shapes=scratch,
        compiler_params=pltpu.CompilerParams(
            collective_id=collective_id, has_side_effects=True, vmem_limit_bytes=VMEM_LIMIT
        ),
        name="finish_gradients",
    )(*finished, *shares, small)


def with_kernels():
    return lax.axis_size("dp") == 4 and lax.axis_size("fsdp") == 8


def reduce_all(grads, shares, collective_id):
    if with_kernels():
        return reduce_call(grads, shares, collective_id)
    return [lax.psum(scatter(grad), "dp") for grad in grads] + sum_shares(shares)


def sum_shares(shares):
    return [lax.psum(share, "dp") for share in shares]


def finish_all(finished, shares, small, collective_id):
    if with_kernels():
        return finish_call(finished, shares, small, collective_id)
    outs = [lax.psum(share, "dp") for share in shares]
    own = lax.psum(scatter(small), "dp")
    total = sum(jnp.sum(jnp.square(out.astype(jnp.float32))) for out in (*finished, *outs))
    row = jnp.full((1, LANES), 1.0 / LANES, jnp.float32) * total
    return [*outs, own, lax.all_gather(own.at[-1:].set(row), "fsdp", axis=0)]


def take(items, *counts):
    cut = []
    for count in counts:
        cut.append(items[:count])
        items = items[count:]
    return cut


def scatter(grad):
    return lax.psum_scatter(grad, "fsdp", scatter_dimension=0)


def by_owner(grad, low=jnp.bfloat16):
    owners = lax.axis_size("fsdp")
    return grad.astype(low).reshape(owners, grad.shape[0] // owners, grad.shape[1])


def attention_forward_kernel(
    q_ref, k_ref, v_ref, seg_col_ref, seg_row_ref, out_ref, expo_ref, inv_ref, *, block
):
    rows = q_ref.shape[0]
    lower = lax.broadcasted_iota(jnp.int32, (block, PAIR), 1) < HD
    keys = k_ref[...]
    values = jnp.concatenate([v_ref[...], jnp.ones((rows, PAIR), v_ref.dtype)], 1)
    seg_row = seg_row_ref[...]
    tasks = [(step, head) for step in range(rows // block) for head in range(2)]

    def scores_of(step, head):
        query = q_ref[step * block : (step + 1) * block, :] * jnp.bfloat16(HD**-0.5)
        keep = lower if head == 0 else jnp.logical_not(lower)
        return mul_nt(jnp.where(keep, query, jnp.bfloat16(0)), keys)

    scores = scores_of(*tasks[0])
    outs = []
    for index, (step, head) in enumerate(tasks):
        following = scores_of(*tasks[index + 1]) if index + 1 < len(tasks) else None
        at = slice(step * block, (step + 1) * block)
        scores = jnp.where(seg_col_ref[at, :] == seg_row, scores, MASKED)
        highest = jnp.max(scores, -1, keepdims=True)
        low = jnp.exp(scores - highest).astype(jnp.bfloat16)
        expo_ref[head, at, :] = low
        outs.append(mul(low, values))
        if head:
            inverse = 1.0 / jnp.where(lower, outs[0][:, PAIR:], outs[1][:, PAIR:])
            sums = jnp.where(lower, outs[0][:, :PAIR], outs[1][:, :PAIR])
            out_ref[at, :] = (sums * inverse).astype(jnp.bfloat16)
            inv_ref[at, :] = inverse
            outs = []
        scores = following


def attention_forward(qkv_rows, segment, rides, collective_id):
    rows = qkv_rows.shape[0]
    pairs = HEADS // 2
    wide = lambda base: pl.BlockSpec((rows, PAIR), lambda j, base=base: (0, base + j))
    return block_call(
        functools.partial(attention_forward_kernel, block=min(256, rows)),
        pairs,
        [wide(0), wide(pairs), wide(2 * pairs), fixed(rows, 1), fixed(1, rows)],
        [qkv_rows, qkv_rows, qkv_rows, segment[:, None], segment[None, :]],
        [wide(0), pl.BlockSpec((2, rows, rows), lambda j: (j, 0, 0)), wide(0)],
        [
            shape_of(rows, D, dtype=LOW),
            shape_of(HEADS, rows, rows, dtype=LOW),
            shape_of(rows, D),
        ],
        [],
        "attention_forward",
        work(16 * HEADS * rows * rows * HD, 2 * HEADS * rows * rows + 12 * rows * D),
        rides,
        collective_id,
    )


def attention_backward_kernel(
    q_ref, k_ref, v_ref, expo_ref, inv_ref, out_ref, grad_ref, dqkv_ref, *, block
):
    rows = q_ref.shape[0]
    pair = pl.program_id(0)
    lower = lax.broadcasted_iota(jnp.int32, (block, PAIR), 1) < HD
    keys = k_ref[...]
    values = v_ref[...]
    scale = HD**-0.5
    scaled_grad = (grad_ref[...].astype(jnp.float32) * inv_ref[...]).astype(jnp.bfloat16)
    query = q_ref[...]
    query_t = query.T
    grad_t = scaled_grad.T
    product = scaled_grad.astype(jnp.float32) * out_ref[...].astype(jnp.float32)
    key_t = [None, None]
    value_t = [None, None]
    tasks = [(step, head) for step in range(rows // block) for head in range(2)]

    def probs_grad_of(step, head):
        keep = lower if head == 0 else jnp.logical_not(lower)
        mine = scaled_grad[step * block : (step + 1) * block]
        return mul_nt(jnp.where(keep, mine, jnp.bfloat16(0)), values)

    probs_grad = probs_grad_of(*tasks[0])
    query_parts = []
    for index, (step, head) in enumerate(tasks):
        following = probs_grad_of(*tasks[index + 1]) if index + 1 < len(tasks) else None
        at = slice(step * block, (step + 1) * block)
        lanes = slice(head * HD, (head + 1) * HD)
        keep = lower if head == 0 else jnp.logical_not(lower)
        inner = jnp.sum(jnp.where(keep, product[at], 0.0), -1, keepdims=True)
        low = expo_ref[head, at, :]
        value_part = mul(grad_t[lanes, at], low)
        scores_grad = (low.astype(jnp.float32) * (probs_grad - inner)).astype(jnp.bfloat16)
        query_parts.append(mul(scores_grad, keys))
        key_part = mul(query_t[lanes, at], scores_grad)
        key_t[head] = key_part if step == 0 else key_t[head] + key_part
        value_t[head] = value_part if step == 0 else value_t[head] + value_part
        if head:
            query_grad = jnp.where(lower, query_parts[0], query_parts[1]) * scale
            dqkv_ref[at, pl.ds(pl.multiple_of(pair * PAIR, PAIR), PAIR)] = query_grad.astype(
                jnp.bfloat16
            )
            query_parts = []
        probs_grad = following
    key_grad = (jnp.concatenate(key_t, 0) * scale).T
    value_grad = jnp.concatenate(value_t, 0).T
    dqkv_ref[:, pl.ds(pl.multiple_of(D + pair * PAIR, PAIR), PAIR)] = key_grad.astype(jnp.bfloat16)
    dqkv_ref[:, pl.ds(pl.multiple_of(2 * D + pair * PAIR, PAIR), PAIR)] = value_grad.astype(jnp.bfloat16)


def attention_backward(qkv_rows, expo, inverse, attended, attended_grad, rides, collective_id):
    rows = qkv_rows.shape[0]
    pairs = HEADS // 2
    wide = lambda base: pl.BlockSpec((rows, PAIR), lambda j, base=base: (0, base + j))
    return block_call(
        functools.partial(attention_backward_kernel, block=min(256, rows)),
        pairs,
        [
            wide(0),
            wide(pairs),
            wide(2 * pairs),
            pl.BlockSpec((2, rows, rows), lambda j: (j, 0, 0)),
            wide(0),
            wide(0),
            wide(0),
        ],
        [qkv_rows, qkv_rows, qkv_rows, expo, inverse, attended, attended_grad],
        [fixed(rows, 3 * D)],
        [shape_of(rows, 3 * D, dtype=LOW)],
        [],
        "attention_backward",
        None,
        rides,
        collective_id,
    )


def mul(left, right):
    return jnp.dot(left, right, preferred_element_type=jnp.float32)


def mul_nt(left, right):
    return lax.dot_general(left, right, NT, preferred_element_type=jnp.float32)


def normalized(values):
    center = values - jnp.mean(values, -1, keepdims=True)
    inverse = lax.rsqrt(jnp.mean(center * center, -1, keepdims=True) + NORM_EPS)
    return center * inverse, inverse


def norm_backward(grad, values, gain):
    unit, inverse = normalized(values)
    inner = grad * gain
    mean_inner = jnp.mean(inner, -1, keepdims=True)
    mean_cross = jnp.mean(inner * unit, -1, keepdims=True)
    value_grad = inverse * (inner - mean_inner - unit * mean_cross)
    return value_grad, column_sum(grad * unit), column_sum(grad)


def column_sum(rows):
    return jnp.sum(rows.astype(jnp.float32), 0, keepdims=True)


def at_first(action):
    pl.when(pl.program_id(0) == 0)(action)


def rows_of(block, columns):
    return pl.BlockSpec((block, columns), lambda i: (i, 0))


def fixed(*shape):
    return pl.BlockSpec(shape, lambda i: (0,) * len(shape), pipeline_mode=pl.Buffered(1))


def loads(sources, targets, sems):
    return [
        pltpu.make_async_copy(source, target, sems.at[index])
        for index, (source, target) in enumerate(zip(sources, targets))
    ]


def shape_of(*shape, dtype=jnp.float32):
    return jax.ShapeDtypeStruct(shape, dtype)


def embed_kernel(pixel_ref, weight_ref, pos_ref, table_ref, bias_ref, out_ref):
    position = jnp.dot(
        pos_ref[...], table_ref[...], precision=HIGHEST, preferred_element_type=jnp.float32
    )
    out_ref[...] = mul(pixel_ref[...], weight_ref[...]) + bias_ref[...] + position


def embed(pixels, weight, pos_weights, table, bias):
    rows, depth = pixels.shape
    block = 256
    nodes = pos_weights.shape[1]
    return block_call(
        embed_kernel,
        rows // block,
        [rows_of(block, depth), fixed(depth, D), rows_of(block, nodes), fixed(nodes, D), fixed(1, D)],
        [pixels, weight, pos_weights, table, bias],
        [rows_of(block, D)],
        [shape_of(rows, D)],
        [],
        "embed",
        work(2 * rows * depth * D, 2 * rows * depth + 2 * depth * D + 4 * rows * D),
    )[0]


def chunk_at(base):
    return pl.ds(pl.multiple_of(base + pl.program_id(0) * D, LANES), D)


def columns_of(rows):
    return pl.BlockSpec((rows, D), lambda i: (0, i))


def halves_of(rows):
    half = rows // 2
    return [slice(start, start + half) for start in range(0, rows, half)]


def at_last(action):
    pl.when(pl.program_id(0) == pl.num_programs(0) - 1)(action)


def qkv_kernel(stream_ref, weight_ref, vector_ref, normed_out, qkv_ref, normed_ref, sem):
    copy = pltpu.make_async_copy(normed_ref, normed_out, sem)

    @at_first
    def _():
        unit, _ = normalized(stream_ref[...])
        normed_ref[...] = (unit * vector_ref[:, :D] + vector_ref[:, D : 2 * D]).astype(LOW)
        copy.start()

    bias = vector_ref[:, chunk_at(4 * D)]
    for half in halves_of(stream_ref.shape[0]):
        qkv_ref[half, :] = (mul(normed_ref[half, :], weight_ref[...]) + bias).astype(LOW)
    at_last(copy.wait)


def qkv_forward(stream, weight, vector):
    rows = stream.shape[0]
    return block_call(
        qkv_kernel,
        3,
        [fixed(rows, D), columns_of(D), fixed(1, vector.shape[1])],
        [stream, weight, vector],
        [ANYWHERE, columns_of(rows)],
        [shape_of(rows, D, dtype=LOW), shape_of(rows, 3 * D, dtype=LOW)],
        [pltpu.VMEM((rows, D), LOW), pltpu.SemaphoreType.DMA],
        "qkv_forward",
        work(6 * rows * D * D, 14 * rows * D + 6 * D * D),
    )


def mlp_kernel(
    stream_ref, attended_ref, mix_ref, up_ref, down_ref, vector_ref,
    residual_out, normed_out, active_ref, slope_ref, out_ref,
    residual_ref, normed_ref, sems,
):
    rows = stream_ref.shape[0]
    copies = loads((residual_ref, normed_ref), (residual_out, normed_out), sems)

    @at_first
    def _():
        for half in halves_of(rows):
            residual = stream_ref[half, :] + mul(attended_ref[half, :], mix_ref[...])
            residual = residual + vector_ref[:, 7 * D : 8 * D]
            residual_ref[half, :] = residual
            unit, _ = normalized(residual)
            normed = unit * vector_ref[:, 2 * D : 3 * D] + vector_ref[:, 3 * D : 4 * D]
            normed_ref[half, :] = normed.astype(LOW)
            out_ref[half, :] = residual + vector_ref[:, 8 * D : 9 * D]
        for copy in copies:
            copy.start()

    bias = vector_ref[:, chunk_at(9 * D)]
    parts = halves_of(rows)
    hidden = mul(normed_ref[parts[0], :], up_ref[...]) + bias
    for index, half in enumerate(parts):
        following = None
        if index + 1 < len(parts):
            following = mul(normed_ref[parts[index + 1], :], up_ref[...]) + bias
        square = hidden * hidden
        rise = 0.5 + 0.5 * jnp.tanh(hidden * (ROOT + (ROOT * CUBE) * square))
        active = hidden * rise
        active_low = active.astype(LOW)
        active_ref[half, :] = active_low
        bend = (2.0 * ROOT) + (6.0 * ROOT * CUBE) * square
        slope_ref[half, :] = (rise + active * (1.0 - rise) * bend).astype(LOW)
        out_ref[half, :] += mul(active_low, down_ref[...])
        hidden = following

    @at_last
    def _():
        for copy in copies:
            copy.wait()


def mlp_specs(up, proj_out):
    return (
        [fixed(D, D), columns_of(D), pl.BlockSpec((D, D), lambda i: (i + 1, 0))],
        [proj_out, up, proj_out],
    )


def mlp_forward(stream, attended, up, proj_out, vector, rides, collective_id):
    rows = stream.shape[0]
    width = up.shape[1]
    weight_specs, weights = mlp_specs(up, proj_out)
    return block_call(
        mlp_kernel,
        width // D,
        [fixed(rows, D), fixed(rows, D), *weight_specs, fixed(1, vector.shape[1])],
        [stream, attended, *weights, vector],
        [ANYWHERE, ANYWHERE, columns_of(rows), columns_of(rows), fixed(rows, D)],
        [
            shape_of(rows, D),
            shape_of(rows, D, dtype=LOW),
            shape_of(rows, width, dtype=LOW),
            shape_of(rows, width, dtype=LOW),
            shape_of(rows, D),
        ],
        [
            pltpu.VMEM((rows, D), jnp.float32),
            pltpu.VMEM((rows, D), LOW),
            pltpu.SemaphoreType.DMA((2,)),
        ],
        "mlp_forward",
        work(2 * rows * D * (D + 2 * width), rows * (16 * D + 4 * width) + 2 * D * (D + 2 * width)),
        rides,
        collective_id,
    )


def mlp_back_kernel(
    grad_ref, slope_ref, residual_ref, mix_ref, up_ref, down_ref, vector_ref,
    low_out, hidden_ref, out_ref, out_low_ref, attended_ref, sums_ref,
    low_ref, second_ref, sem,
):
    rows = grad_ref.shape[0]
    copy = pltpu.make_async_copy(low_ref, low_out, sem)

    @at_first
    def _():
        low_ref[...] = grad_ref[...].astype(LOW)
        copy.start()
        second_ref[...] = jnp.zeros_like(second_ref)

    parts = halves_of(rows)
    active_grad = mul_nt(low_ref[parts[0], :], down_ref[...])
    hidden_sum = 0.0
    for index, half in enumerate(parts):
        following = None
        if index + 1 < len(parts):
            following = mul_nt(low_ref[parts[index + 1], :], down_ref[...])
        hidden_grad = (active_grad * slope_ref[half, :].astype(jnp.float32)).astype(LOW)
        hidden_ref[half, :] = hidden_grad
        hidden_sum = hidden_sum + column_sum(hidden_grad)
        second_ref[half, :] += mul_nt(hidden_grad, up_ref[...])
        active_grad = following
    sums_ref[:, chunk_at(4 * D)] = hidden_sum

    @at_last
    def _():
        gain = vector_ref[:, 2 * D : 3 * D]
        totals = [0.0] * 4
        for half in halves_of(rows):
            grad = grad_ref[half, :]
            value_grad, gain_grad, shift_grad = norm_backward(
                second_ref[half, :], residual_ref[half, :], gain
            )
            total = value_grad + grad
            out_ref[half, :] = total
            total_low = total.astype(LOW)
            out_low_ref[half, :] = total_low
            attended_ref[half, :] = mul_nt(total_low, mix_ref[...]).astype(LOW)
            new = (gain_grad, shift_grad, column_sum(total_low), column_sum(low_ref[half, :]))
            totals = [old + part for old, part in zip(totals, new)]
        sums_ref[:, : 4 * D] = jnp.concatenate(totals, 1)
        copy.wait()


def mlp_backward(grad, slope, residual, up, proj_out, vector):
    rows = grad.shape[0]
    width = up.shape[1]
    whole = fixed(rows, D)
    weight_specs, weights = mlp_specs(up, proj_out)
    return block_call(
        mlp_back_kernel,
        width // D,
        [whole, columns_of(rows), whole, *weight_specs, fixed(1, vector.shape[1])],
        [grad, slope, residual, *weights, vector],
        [ANYWHERE, columns_of(rows), whole, whole, whole, fixed(1, 4 * D + width)],
        [
            shape_of(rows, D, dtype=LOW),
            shape_of(rows, width, dtype=LOW),
            shape_of(rows, D),
            shape_of(rows, D, dtype=LOW),
            shape_of(rows, D, dtype=LOW),
            shape_of(1, 4 * D + width),
        ],
        [
            pltpu.VMEM((rows, D), LOW),
            pltpu.VMEM((rows, D), jnp.float32),
            pltpu.SemaphoreType.DMA,
        ],
        "mlp_backward",
    )


def qkv_back_kernel(
    grad_ref, residual_ref, stream_ref, weight_ref, vector_ref, out_ref, sums_ref, normed_ref
):
    rows = stream_ref.shape[0]

    @at_first
    def _():
        normed_ref[...] = jnp.zeros_like(normed_ref)

    for half in halves_of(rows):
        normed_ref[half, :] += mul_nt(grad_ref[half, :], weight_ref[...])
    sums_ref[:, chunk_at(2 * D)] = column_sum(grad_ref[...])

    @at_last
    def _():
        totals = [0.0] * 2
        for half in halves_of(rows):
            value_grad, gain_grad, shift_grad = norm_backward(
                normed_ref[half, :], stream_ref[half, :], vector_ref[:, :D]
            )
            out_ref[half, :] = residual_ref[half, :] + value_grad
            totals = [totals[0] + gain_grad, totals[1] + shift_grad]
        sums_ref[:, : 2 * D] = jnp.concatenate(totals, 1)


def qkv_backward(grad, residual_grad, stream, weight, vector):
    rows = stream.shape[0]
    whole = fixed(rows, D)
    return block_call(
        qkv_back_kernel,
        3,
        [columns_of(rows), whole, whole, columns_of(D), fixed(1, vector.shape[1])],
        [grad, residual_grad, stream, weight, vector],
        [whole, fixed(1, 5 * D)],
        [shape_of(rows, D), shape_of(1, 5 * D)],
        [pltpu.VMEM((rows, D), jnp.float32)],
        "qkv_backward",
    )


def input_grad_kernel(first_ref, second_ref, qkv_ref, hidden_ref, qkv_out, up_out, left_ref, *, cut):
    step = pl.program_id(0)

    @pl.when(step == 0)
    def _():
        left_ref[...] = first_ref[...].T

    @pl.when(step == cut)
    def _():
        left_ref[...] = second_ref[...].T

    @pl.when(step < cut)
    def _():
        qkv_out[...] = mul(left_ref[...], qkv_ref[...]).astype(jnp.bfloat16)

    @pl.when(step >= cut)
    def _():
        up_out[...] = mul(left_ref[...], hidden_ref[...]).astype(jnp.bfloat16)


def input_weight_grad(first, second, qkv_grad, hidden_grad):
    rows = first.shape[0]
    cut = qkv_grad.shape[1] // D
    steps = cut + hidden_grad.shape[1] // D
    before = lambda i: (0, jnp.minimum(i, cut - 1))
    after = lambda i: (0, jnp.maximum(i - cut, 0))
    return block_call(
        functools.partial(input_grad_kernel, cut=cut),
        steps,
        [
            fixed(rows, D),
            fixed(rows, D),
            pl.BlockSpec((rows, D), before),
            pl.BlockSpec((rows, D), after),
        ],
        [first, second, qkv_grad, hidden_grad],
        [pl.BlockSpec((D, D), before), pl.BlockSpec((D, D), after)],
        [
            shape_of(D, qkv_grad.shape[1], dtype=jnp.bfloat16),
            shape_of(D, hidden_grad.shape[1], dtype=jnp.bfloat16),
        ],
        [pltpu.VMEM((D, rows), jnp.bfloat16)],
        "input_weight_grad",
        None,
    )


def output_grad_kernel(attended_ref, active_ref, residual_ref, grad_ref, *outs, cut):
    step = pl.program_id(0)

    def store(product):
        base = 0
        for out in outs:
            out[...] = product[:, base : base + out.shape[1]].astype(jnp.bfloat16)
            base += out.shape[1]

    @pl.when(step < cut)
    def _():
        store(mul(attended_ref[...].T, residual_ref[...]))

    @pl.when(step >= cut)
    def _():
        store(mul(active_ref[...].T, grad_ref[...]))


def output_weight_grad(attended, active, residual_low, grad_low, parts):
    rows = attended.shape[0]
    block = 768
    cut = attended.shape[1] // block
    steps = cut + active.shape[1] // block
    return block_call(
        functools.partial(output_grad_kernel, cut=cut),
        steps,
        [
            pl.BlockSpec((rows, block), lambda i: (0, jnp.minimum(i, cut - 1))),
            pl.BlockSpec((rows, block), lambda i: (0, jnp.maximum(i - cut, 0))),
            fixed(rows, D),
            fixed(rows, D),
        ],
        [attended, active, residual_low, grad_low],
        [rows_of(block, part) for part in parts],
        [shape_of(steps * block, part, dtype=LOW) for part in parts],
        [],
        "output_weight_grad",
    )


def embed_back_kernel(pixel_ref, grad_ref, pos_ref, out_ref, table_ref, bias_ref, low_ref):
    @at_first
    def _():
        grad = grad_ref[...]
        low = grad.astype(jnp.bfloat16)
        low_ref[...] = low
        bias_ref[...] = column_sum(low)
        table_ref[...] = jnp.dot(
            pos_ref[...], grad, precision=HIGHEST, preferred_element_type=jnp.float32
        )

    out_ref[...] = mul(pixel_ref[...].T, low_ref[...]).astype(jnp.bfloat16)


def embed_backward(pixels, grad, pos_weights_t):
    rows, depth = pixels.shape
    block = 768
    nodes = pos_weights_t.shape[0]
    return block_call(
        embed_back_kernel,
        depth // block,
        [pl.BlockSpec((rows, block), lambda i: (0, i)), fixed(rows, D), fixed(nodes, rows)],
        [pixels, grad, pos_weights_t],
        [rows_of(block, D), fixed(nodes, D), fixed(1, D)],
        [shape_of(depth, D, dtype=jnp.bfloat16), shape_of(nodes, D), shape_of(1, D)],
        [pltpu.VMEM((rows, D), jnp.bfloat16)],
        "embed_backward",
        None,
    )


def head_kernel(
    stream_ref, seg_col_ref, seg_row_ref, label_ref, weight_ref, vector_ref,
    grad_ref, weight_grad_ref, sums_ref, bias_grad_ref, numbers_ref, *, classes,
):
    padded = weight_ref.shape[1]
    vector = vector_ref[...].astype(LOW).astype(jnp.float32)
    gain, shift = vector[:, D : 2 * D], vector[:, 2 * D : 3 * D]
    slots = lax.broadcasted_iota(jnp.int32, (IMGS, 1), 0)
    member = (seg_row_ref[...] == slots).astype(jnp.float32)
    counts = jnp.sum(member, 1, keepdims=True)
    sizes = jnp.maximum(counts, 1.0)
    unit, inverse = normalized(stream_ref[...])
    final = unit * gain + shift
    pooled = jnp.dot(member, final, precision=HIGHEST, preferred_element_type=jnp.float32)
    pooled = (pooled / sizes).astype(LOW)
    class_at = lax.broadcasted_iota(jnp.int32, (IMGS, padded), 1)
    logits = mul(pooled, weight_ref[...]) + vector[:, 3 * D :]
    logits = jnp.where(class_at < classes, logits, MASKED)
    highest = jnp.max(logits, -1, keepdims=True)
    exponent = jnp.exp(logits - highest)
    totals = jnp.sum(exponent, -1, keepdims=True)
    onehot = class_at == label_ref[...]
    picked = jnp.sum(jnp.where(onehot, logits, 0.0), 1, keepdims=True)
    loss = jnp.sum(counts * (highest + jnp.log(totals) - picked), 0, keepdims=True)
    numbers_ref[...] = jnp.concatenate([loss, jnp.sum(counts, 0, keepdims=True)], 1)
    logits_grad = ((exponent / totals - onehot.astype(jnp.float32)) * counts).astype(LOW)
    bias_grad_ref[...] = column_sum(logits_grad)
    weight_grad_ref[...] = lax.dot_general(
        pooled, logits_grad, (((0,), (0,)), ((), ())), preferred_element_type=jnp.float32
    ).astype(LOW)
    pooled_grad = mul_nt(logits_grad, weight_ref[...]) / sizes
    own = (seg_col_ref[...] == lax.broadcasted_iota(jnp.int32, (1, IMGS), 1)).astype(jnp.float32)
    final_grad = jnp.dot(own, pooled_grad, precision=HIGHEST, preferred_element_type=jnp.float32)
    inner = final_grad * gain
    mean_inner = jnp.mean(inner, -1, keepdims=True)
    mean_cross = jnp.mean(inner * unit, -1, keepdims=True)
    grad_ref[...] = inverse * (inner - mean_inner - unit * mean_cross)
    sums_ref[...] = jnp.concatenate([column_sum(final_grad * unit), column_sum(final_grad)], 1)


def head(stream, segment, labels, weight, global_vector, classes):
    rows = stream.shape[0]
    padded = weight.shape[1]
    vector = jnp.pad(global_vector, (0, padded - classes))[None, :]
    return pl.pallas_call(
        functools.partial(head_kernel, classes=classes),
        out_shape=[
            shape_of(rows, D),
            shape_of(D, padded, dtype=LOW),
            shape_of(1, 2 * D),
            shape_of(1, padded),
            shape_of(1, 2),
        ],
        compiler_params=pltpu.CompilerParams(vmem_limit_bytes=VMEM_LIMIT),
        cost_estimate=NO_COST,
        name="head",
    )(stream, segment[:, None], segment[None, :], labels.reshape(IMGS, 1), weight, vector)


def adam_update(gradient, moment, square, weight, factor, learn_rate):
    clipped = gradient * factor
    moment = BETA_ONE * moment + (1.0 - BETA_ONE) * clipped
    square = BETA_TWO * square + (1.0 - BETA_TWO) * clipped * clipped
    fixed_one = 1.0 - BETA_ONE**STEP
    fixed_two = 1.0 - BETA_TWO**STEP
    step_dir = (
        moment / fixed_one / (jnp.sqrt(square / fixed_two) + ADAM_EPS) + WEIGHT_DECAY * weight
    )
    return (moment, square, weight - learn_rate * step_dir)


def body(
    pixels,
    segment,
    patch_size,
    labels,
    patch_kernel,
    head_weight,
    input_proj,
    output_proj,
    layer_vector,
    position_table,
    global_vector,
    patch_moment,
    head_moment,
    input_moment,
    output_moment,
    layer_moment,
    position_moment,
    global_moment,
    patch_square,
    head_square,
    input_square,
    output_square,
    layer_square,
    position_square,
    global_square,
):
    owners = lax.axis_size("fsdp")
    nodes = position_table.shape[0]
    vector_size = layer_vector.size
    output_zero = lax.all_gather(output_proj[0].astype(LOW), "fsdp", axis=0, tiled=True)
    stream, pos_weights_t, vectors, qkv_weight, rides, rest_shards = begin(
        pixels,
        segment,
        patch_size,
        patch_kernel,
        layer_vector,
        input_proj,
        output_proj,
        head_weight,
        position_table,
        global_vector,
    )
    up_one, head_full = (
        lax.all_gather(shard, "fsdp", axis=0, tiled=True) for shard in rest_shards
    )
    up_ride, qkv_ride, output_ride = rides
    saved_layers = []
    for index in range(LAYERS):
        vector = vectors[index]
        normed, qkv_rows = qkv_forward(stream, qkv_weight, vector)
        if index == 0:
            attended, expo, inverse, up, qkv_ride = attention_forward(
                qkv_rows, segment, [up_ride, qkv_ride], 4
            )
            output, mlp_rides = output_zero, [qkv_ride, output_ride]
        else:
            attended, expo, inverse, output = attention_forward(qkv_rows, segment, [output_ride], 5)
            up, mlp_rides = up_one, ()
        residual, normed_second, active, slope, following, *fetched = mlp_forward(
            stream, attended, up, output, vector, mlp_rides, 7
        )
        saved_layers.append(
            (
                (qkv_weight, up, output, vector),
                (stream, normed, qkv_rows, attended, expo, inverse),
                (residual, normed_second, active, slope),
            )
        )
        stream = following
        if fetched:
            qkv_weight, output_ride = fetched
    stream_grad, head_grad, final_sums, head_bias_grad, numbers = head(
        stream, segment, labels, head_full, global_vector, head_weight.shape[1]
    )
    head_part = scatter(by_owner(head_grad))
    vector_grads = [None] * LAYERS
    early_parts, late_parts = [head_part], []
    for index in reversed(range(LAYERS)):
        (qkv_weight, up, output, vector), first, second = saved_layers[index]
        entering, normed, qkv_rows, attended, expo, inverse = first
        residual, normed_second, active, slope = second
        grad_low, hidden_grad, residual_grad, residual_low, attended_grad, mlp_sums = mlp_backward(
            stream_grad, slope, residual, up, output, vector
        )
        output_grads = output_weight_grad(
            attended, active, residual_low, grad_low, (D // 2,) * 2 if index else (D,)
        )
        attended_grad, *output_grads = lax.optimization_barrier((attended_grad, *output_grads))
        output_parts = [scatter(by_owner(grad)) for grad in output_grads]
        if index:
            early_parts.extend(output_parts)
        else:
            (last_part,) = output_parts
        qkv_grad, *early_sums = attention_backward(
            qkv_rows,
            expo,
            inverse,
            attended,
            attended_grad,
            () if index else [ShareRide(early_parts[0]), ShareRide(jnp.concatenate(early_parts[1:], 1))],
            6,
        )
        stream_grad, qkv_sums = qkv_backward(qkv_grad, residual_grad, entering, qkv_weight, vector)
        input_grads = input_weight_grad(normed, normed_second, qkv_grad, hidden_grad)
        if index:
            stream_grad, *input_grads = lax.optimization_barrier((stream_grad, *input_grads))
            late_parts.extend(scatter(by_owner(grad)) for grad in input_grads)
        vector_grads[index] = jnp.concatenate(
            [
                qkv_sums[0, : 2 * D],
                mlp_sums[0, : 2 * D],
                qkv_sums[0, 2 * D :],
                mlp_sums[0, 2 * D :],
            ]
        )
    kernel_grad, position_grad, bias_grad = embed_backward(pixels, stream_grad, pos_weights_t)
    position_grad = position_grad[:nodes]
    vector_part = jnp.stack(vector_grads).reshape(LAYERS, owners, -1)
    vector_part = jnp.swapaxes(vector_part, 0, 1).reshape(owners, vector_size)
    vector_rows = -(-vector_size // LANES)
    vector_part = jnp.pad(vector_part, ((0, 0), (0, vector_rows * LANES - vector_size)))
    rest = jnp.concatenate(
        [
            position_grad.reshape(-1),
            bias_grad[0],
            final_sums[0],
            head_bias_grad[0, :CLS],
            numbers[0],
        ]
    )
    rest_rows = -(-rest.shape[0] // (owners * LANES))
    rest_part = jnp.pad(rest, (0, rest_rows * owners * LANES - rest.shape[0]))
    small = jnp.concatenate([vector_part, rest_part.reshape(owners, -1)], 1)
    used = vector_rows + rest_rows
    block_rows = (used // 64 + 1) * 64
    small = jnp.pad(small.reshape(owners, used, LANES), ((0, 0), (0, block_rows - used), (0, 0)))
    input_zero_sums, kernel_sum, input_one_sums = take(
        reduce_all([by_owner(grad) for grad in (*input_grads, kernel_grad)], late_parts, 2), 2, 1, 2
    )
    output_zero_sum, small_share, small_full = finish_all(
        [*early_sums, *input_zero_sums, *kernel_sum, *input_one_sums], [last_part], small, 3
    )
    head_sum, output_one_sum = early_sums
    rest_sum = small_full[:, vector_rows:used].reshape(-1)
    position_sum = rest_sum[: position_grad.size].reshape(position_grad.shape)
    global_sum = rest_sum[position_grad.size :][: global_vector.shape[0]]
    loss_sum = rest_sum[rest.shape[0] - 2]
    token_total = rest_sum[rest.shape[0] - 1]
    kernel_sum = kernel_sum[0].astype(jnp.float32)
    head_sum = head_sum[:, :CLS].astype(jnp.float32)
    input_sum = jnp.stack(
        [jnp.concatenate(pair, 1) for pair in (input_zero_sums, input_one_sums)]
    ).astype(jnp.float32)
    output_sum = jnp.stack([output_zero_sum, output_one_sum]).astype(
        jnp.float32
    )
    vector_sum = small_share[:vector_rows].reshape(-1)[:vector_size].reshape(layer_vector.shape)
    grad_norm = (
        jnp.sqrt(
            jnp.sum(small_full[:, -1])
            + jnp.sum(jnp.square(small_full[:, :vector_rows]))
            + jnp.sum(position_sum * position_sum)
            + jnp.sum(global_sum * global_sum)
        )
        / token_total
    )
    factor = jnp.minimum(1.0, CLIP_NORM / grad_norm) / token_total
    patch_next = adam_update(
        kernel_sum, patch_moment, patch_square, patch_kernel, factor, LEARN_RATE
    )
    head_next = adam_update(head_sum, head_moment, head_square, head_weight, factor, LEARN_RATE)
    input_next = adam_update(input_sum, input_moment, input_square, input_proj, factor, LEARN_RATE)
    output_next = adam_update(
        output_sum, output_moment, output_square, output_proj, factor, LEARN_RATE
    )
    layer_next = adam_update(
        vector_sum, layer_moment, layer_square, layer_vector, factor, VECTOR_RATE
    )
    position_next = adam_update(
        position_sum, position_moment, position_square, position_table, factor, LEARN_RATE
    )
    global_next = adam_update(
        global_sum, global_moment, global_square, global_vector, factor, VECTOR_RATE
    )
    return (
        loss_sum,
        token_total,
        grad_norm,
        patch_next[0],
        head_next[0],
        input_next[0],
        output_next[0],
        layer_next[0],
        position_next[0],
        global_next[0],
        patch_next[1],
        head_next[1],
        input_next[1],
        output_next[1],
        layer_next[1],
        position_next[1],
        global_next[1],
        patch_next[2],
        head_next[2],
        input_next[2],
        output_next[2],
        layer_next[2],
        position_next[2],
        global_next[2],
    )


def solution(mesh):
    in_specs = (
        P(("dp", "fsdp"), None),
        P(("dp", "fsdp")),
        P(("dp", "fsdp"), None),
        P(("dp", "fsdp"), None),
        P("fsdp", None),
        P("fsdp", None),
        P(None, "fsdp", None),
        P(None, "fsdp", None),
        P(None, "fsdp"),
        P(),
        P(),
        P("fsdp", None),
        P("fsdp", None),
        P(None, "fsdp", None),
        P(None, "fsdp", None),
        P(None, "fsdp"),
        P(),
        P(),
        P("fsdp", None),
        P("fsdp", None),
        P(None, "fsdp", None),
        P(None, "fsdp", None),
        P(None, "fsdp"),
        P(),
        P(),
    )
    out_specs = (
        P(),
        P(),
        P(),
        P("fsdp", None),
        P("fsdp", None),
        P(None, "fsdp", None),
        P(None, "fsdp", None),
        P(None, "fsdp"),
        P(),
        P(),
        P("fsdp", None),
        P("fsdp", None),
        P(None, "fsdp", None),
        P(None, "fsdp", None),
        P(None, "fsdp"),
        P(),
        P(),
        P("fsdp", None),
        P("fsdp", None),
        P(None, "fsdp", None),
        P(None, "fsdp", None),
        P(None, "fsdp"),
        P(),
        P(),
    )
    return jax.shard_map(body, mesh=mesh, in_specs=in_specs, out_specs=out_specs, check_vma=False)
```

```python
import functools

import jax
import jax.numpy as jnp
from jax import lax
from jax.experimental import pallas as pl
from jax.experimental.pallas import tpu as pltpu
from jax.sharding import PartitionSpec as P

D = 768
HEADS = 12
HD = 64
CLS = 1000
GRID = 7
IMG = 240
IMGS = 8
LAYERS = 2
STEP = 3


NORM_EPS = 1e-06
CLIP_NORM = 0.01
LEARN_RATE = 0.05
VECTOR_RATE = 0.25
BETA_ONE = 0.5
BETA_TWO = 0.5
ADAM_EPS = 1e-08
WEIGHT_DECAY = 0.05
HIGHEST = lax.Precision.HIGHEST

PAIR = 2 * HD
MASKED = -1e30
MIB = 1024 * 1024
VMEM_LIMIT = 56 * MIB
MESH = pl.DeviceIdType.MESH
LANES = 128
LOW = jnp.bfloat16
ANYWHERE = pl.BlockSpec(memory_space=pl.ANY)
NO_COST = pl.CostEstimate(flops=0, bytes_accessed=0, transcendentals=0)
ROOT = 0.7978845608028654
CUBE = 0.044715
NT = (((1,), (1,)), ((), ()))


def layer_norm(values, gain, shift):
    center = values - jnp.mean(values, -1, keepdims=True)
    spread = jnp.mean(center * center, -1, keepdims=True)
    return center * lax.rsqrt(spread + NORM_EPS) * gain + shift


def rounded(values):
    return lax.optimization_barrier(values.astype(jnp.bfloat16)).astype(jnp.float32)


def matmul(left, right):
    return jnp.dot(left, right, preferred_element_type=jnp.float32)


def padded_rows(flat, multiple):
    extra = -flat.shape[0] % (multiple * LANES)
    return jnp.pad(flat, (0, extra)).reshape(-1, LANES)


def row_layout(seg_row, patch_row):
    row_count = seg_row.shape[0]
    slots = jnp.arange(IMGS, dtype=jnp.int32)
    member = seg_row[:, None] == slots[None, :]
    counts = jnp.sum(member.astype(jnp.int32), 0, dtype=jnp.int32)
    starts = jnp.cumsum(counts, dtype=jnp.int32) - counts
    inside = jnp.any(member, 1)
    offset = jnp.arange(row_count, dtype=jnp.int32) - jnp.sum(
        jnp.where(member, starts[None, :], 0), 1, dtype=jnp.int32
    )
    offset = jnp.where(inside, offset, 0)
    patch_tok = jnp.sum(jnp.where(member, patch_row[None, :], 0), 1, dtype=jnp.int32) + jnp.where(
        inside, 0, IMG
    )
    side = IMG // patch_tok
    nodes = jnp.arange(GRID, dtype=jnp.int32).astype(jnp.float32)

    def hat(coord):
        place = ((2 * coord + 1) * GRID).astype(jnp.float32) / (2 * side).astype(jnp.float32) - 0.5
        place = jnp.clip(place, 0.0, GRID - 1.0)
        return jnp.maximum(1.0 - jnp.abs(place[:, None] - nodes[None, :]), 0.0)

    weights = (hat(offset // side)[:, :, None] * hat(offset % side)[:, None, :]).reshape(
        row_count, GRID * GRID
    )
    return (weights, member.astype(jnp.float32), counts.astype(jnp.float32))


TURNS = (1, 2, 3)


def place():
    slot = lax.axis_index("fsdp")
    return lax.axis_index("dp"), lax.div(slot, 2), lax.rem(slot, 2)


def partner(index, turn):
    if turn == 0:
        return index
    if turn == 1:
        return index + 1 - 2 * lax.rem(index, 2)
    if turn == 2:
        return lax.rem(index + 2, 4)
    return 3 - index


def greet():
    group, level, core = place()
    barrier = pltpu.get_barrier_semaphore()
    peers = [(group, 2 * level + 1 - core)]
    for turn in TURNS:
        peers.append((group, 2 * partner(level, turn) + core))
        peers.append((partner(group, turn), 2 * level + core))
    for peer in peers:
        pl.semaphore_signal(barrier, inc=1, device_id=peer, device_id_type=MESH)
    pl.semaphore_wait(barrier, len(peers))


def quarter_shape(rows, columns):
    if columns % (2 * LANES) == 0:
        return rows // 2, columns // 2
    return rows // 4, columns


def quarter(index, rows, columns):
    high, wide = quarter_shape(rows, columns)
    if wide == columns:
        return pl.ds(pl.multiple_of(index * high, high), high), pl.ds(0, columns)
    return (
        pl.ds(pl.multiple_of(lax.div(index, 2) * high, high), high),
        pl.ds(pl.multiple_of(lax.rem(index, 2) * wide, wide), wide),
    )


def remote(source, target, send, receive, device):
    return pltpu.make_async_remote_copy(
        src_ref=source,
        dst_ref=target,
        send_sem=send,
        recv_sem=receive,
        device_id=device,
        device_id_type=MESH,
    )


GATHER_SEMS = 39


def relay_rows(part, rows):
    cut = -(-rows // 32) * 16
    return (0, cut) if part == 0 else (cut, rows - cut)


class Relay:
    def region(self, turn, index):
        _, level, core = place()
        block = self.out.at[2 * partner(level, turn) + core]
        return block.at[quarter(index, *self.shard.shape)]

    def group_copy(self, turn, other):
        group, level, core = place()
        index = self.group_at + 2 * (turn - 1) + other - 1
        peer = (partner(group, other), 2 * level + core)
        target = self.region(turn, group)
        source = self.quarter_source(turn, target)
        return remote(source, target, self.sems.at[index], self.sems.at[index + 6], peer)

    def relay_copy(self, turn, part):
        group, level, core = place()
        first, count = relay_rows(part, quarter_shape(*self.shard.shape)[0])
        block = self.region(turn, partner(group, 1 + part)).at[pl.ds(first, count)]
        index = self.relay_at + 2 * (turn - 1) + part
        peer = (partner(group, 2 - part), 2 * level + core)
        return remote(block, block, self.sems.at[index], self.sems.at[index + 6], peer)

    def relay(self):
        for turn in TURNS:
            for part in range(2):
                self.group_copy(turn, 1 + part).wait_recv()
                self.relay_copy(turn, part).start()

    def wait_quarters(self, turn):
        for part in range(2):
            self.relay_copy(turn, part).wait_recv()

    def wait_passed(self):
        for turn in TURNS:
            for part in range(2):
                self.group_copy(turn, 1 + part).wait_send()
                self.relay_copy(turn, part).wait_send()


class Gather(Relay):
    group_at, relay_at = 7, 19

    def __init__(self, shard, out, sems, split, in_place=False):
        self.shard, self.out, self.sems, self.split = shard, out, sems, split
        self.in_place = in_place
        self.rows, self.columns = shard.shape

    def quarter_source(self, turn, target):
        return target

    def level_copy(self, turn):
        group, level, core = place()
        block = self.out.at[2 * level + core]
        source = self.shard
        if self.split:
            part = quarter(group, self.rows, self.columns)
            source, block = source.at[part], block.at[part]
        peer = (group, 2 * partner(level, turn) + core)
        return remote(source, block, self.sems.at[turn], self.sems.at[3 + turn], peer)

    def core_copy(self, turn):
        group, level, core = place()
        slot = 2 * partner(level, turn) + core
        source = self.shard if turn == 0 else self.out.at[slot]
        peer = (group, 2 * level + 1 - core)
        return remote(source, self.out.at[slot], self.sems.at[31 + turn], self.sems.at[35 + turn], peer)

    def own_copy(self):
        _, level, core = place()
        return pltpu.make_async_copy(self.shard, self.out.at[2 * level + core], self.sems.at[0])

    def first(self):
        for turn in TURNS:
            self.level_copy(turn).start()
        self.core_copy(0).start()
        if not self.in_place:
            self.own_copy().start()

    def second(self):
        for turn in TURNS:
            self.level_copy(turn).wait_recv()
            if self.split:
                for other in (1, 2):
                    self.group_copy(turn, other).start()
            else:
                self.core_copy(turn).start()

    def third(self, use=None):
        for turn in TURNS if self.split else ():
            self.wait_quarters(turn)
            self.core_copy(turn).start()
            if use is not None:
                use(turn, True)

    def fourth(self, use=None):
        for turn in TURNS if use is not None else (0, *TURNS):
            self.core_copy(turn).wait_recv()
            if use is not None:
                use(turn, False)
        for turn in TURNS:
            self.level_copy(turn).wait_send()
        if self.split:
            self.wait_passed()
        for turn in (0, *TURNS):
            self.core_copy(turn).wait_send()
        if not self.in_place:
            self.own_copy().wait()


class LevelGather:
    def __init__(self, shard, out, sems):
        self.shard, self.out, self.sems = shard, out, sems

    def level_copy(self, turn):
        group, level, core = place()
        return remote(
            self.shard.at[quarter(group, *self.shard.shape)],
            self.out.at[level],
            self.sems.at[turn],
            self.sems.at[3 + turn],
            (group, 2 * partner(level, turn) + core),
        )

    def first(self):
        for turn in TURNS:
            self.level_copy(turn).start()

    def second(self):
        pass

    def third(self):
        pass

    def fourth(self):
        for turn in TURNS:
            self.level_copy(turn).wait_recv()
            self.level_copy(turn).wait_send()

    def store(self):
        _, level, _ = place()
        self.out[level] = jnp.zeros(self.out.shape[1:], self.out.dtype)
        self.target[...] = self.out[...]


GROUP_GATHER_SEMS = 36


class GroupGather(Relay):
    group_at, relay_at = 4, 16

    def __init__(self, shard, quarters, out, sems):
        self.shard, self.quarters, self.out, self.sems = shard, quarters, out, sems

    def quarter_source(self, turn, target):
        _, level, _ = place()
        return self.quarters.at[partner(level, turn)]

    def own_copy(self, turn):
        group, level, core = place()
        if turn == 0:
            source, target = self.shard, self.out.at[2 * level + core]
        else:
            source, target = self.quarters.at[partner(level, turn)], self.region(turn, group)
        return pltpu.make_async_copy(source, target, self.sems.at[turn])

    def core_copy(self, turn):
        group, level, core = place()
        slot = 2 * partner(level, turn) + core
        source = self.shard if turn == 0 else self.out.at[slot]
        peer = (group, 2 * level + 1 - core)
        return remote(source, self.out.at[slot], self.sems.at[28 + turn], self.sems.at[32 + turn], peer)

    def first(self):
        for turn in TURNS:
            for other in (1, 2):
                self.group_copy(turn, other).start()
        for turn in (0, *TURNS):
            self.own_copy(turn).start()
        self.core_copy(0).start()

    def third(self):
        for turn in TURNS:
            self.wait_quarters(turn)
            self.own_copy(turn).wait()
            self.core_copy(turn).start()

    def fourth(self):
        for turn in (0, *TURNS):
            self.core_copy(turn).wait_recv()
            self.core_copy(turn).wait_send()
        self.wait_passed()
        self.own_copy(0).wait()

    def store(self):
        copy = pltpu.make_async_copy(self.out, self.target, self.sems.at[0])
        copy.start()
        copy.wait()


class LevelRide:
    def __init__(self, shard):
        self.operands = [shard]
        self.in_specs = [fixed(*shard.shape)]
        shape = (4, *quarter_shape(*shard.shape))
        self.out_specs = [fixed(*shape)]
        self.out_shapes = [jax.ShapeDtypeStruct(shape, shard.dtype)]
        self.scratch = [pltpu.VMEM(shape, shard.dtype), pltpu.SemaphoreType.DMA((7,))]

    def job(self, sources, targets, scratch):
        job = LevelGather(sources[0], *scratch)
        job.target = targets[0]
        return job

    def before(self, steps):
        return {0: ("first",)}

    after = ("fourth", "store")

    def result(self, outs):
        return GatherRide(self.operands[0], outs[0])

    def plain(self):
        return GatherRide(self.operands[0], self.operands[0])


class GatherRide:
    def __init__(self, shard, quarters):
        owners = lax.axis_size("fsdp")
        full = (owners, *shard.shape)
        self.operands = [shard, quarters]
        self.in_specs = [fixed(*shard.shape), fixed(*quarters.shape)]
        self.out_specs = [ANYWHERE]
        self.out_shapes = [jax.ShapeDtypeStruct(full, shard.dtype)]
        self.scratch = [
            pltpu.VMEM(full, shard.dtype),
            pltpu.SemaphoreType.DMA((GROUP_GATHER_SEMS,)),
        ]

    def job(self, sources, targets, scratch):
        job = GroupGather(*sources, *scratch)
        job.target = targets[0]
        return job

    def before(self, steps):
        return {0: ("first",), steps // 2: ("relay",), steps - 1: ("third",)}

    after = ("fourth", "store")

    def result(self, outs):
        return outs[0].reshape(-1, outs[0].shape[2])

    def plain(self):
        return lax.all_gather(self.operands[0], "fsdp", axis=0, tiled=True)


class ShareRide:
    def __init__(self, share):
        self.operands = [share]
        self.in_specs = [ANYWHERE]
        self.out_specs = [fixed(*share.shape)]
        self.out_shapes = [jax.ShapeDtypeStruct(share.shape, share.dtype)]
        self.scratch = [
            pltpu.VMEM(share.shape, share.dtype),
            *share_scratch(share),
            pltpu.SemaphoreType.DMA((GROUP_SEMS,)),
        ]

    def job(self, sources, targets, scratch):
        job = GroupReduce(sources[0], scratch[0], scratch[1:3], scratch[3])
        job.target = targets[0]
        return job

    def before(self, steps):
        return {0: ("first", "second"), max(1, steps // 2): ("third",)}

    after = ("fifth", "sixth", "store")

    def result(self, outs):
        return outs[0]

    def plain(self):
        return lax.psum(self.operands[0], "dp")


class SumRide:
    def __init__(self, grad, large):
        block = grad.shape[1:]
        self.large = large
        self.operands = [grad]
        self.in_specs = [ANYWHERE]
        self.out_specs = [fixed(*block)]
        self.out_shapes = [jax.ShapeDtypeStruct(block, grad.dtype)]
        buffers = stepped_scratch(grad) if large else whole_scratch(grad)
        sems = WHOLE_SEMS if large else REDUCE_SEMS
        self.scratch = [pltpu.VMEM(block, grad.dtype), *buffers, pltpu.SemaphoreType.DMA((sems,))]

    def job(self, sources, targets, scratch):
        job = (Whole if self.large else Reduce)(sources[0], scratch[0], scratch[1:-1], scratch[-1])
        job.target = targets[0]
        return job

    def before(self, steps):
        if self.large:
            return {0: ("first",), 1: ("second",), steps - 2: ("between",), steps - 1: ("third",)}
        return {0: ("first",), 1: ("second",), steps // 2: ("third",), steps - 1: ("fourth",)}

    @property
    def after(self):
        return (("fourth",) if self.large else ()) + ("fifth", "sixth", "store")

    def result(self, outs):
        return outs[0]

    def plain(self):
        return lax.psum(scatter(self.operands[0]), "dp")


def riding(body, counts, rides, steps):
    def kernel(*refs):
        refs = list(refs)

        def pop(count):
            taken = refs[:count]
            del refs[:count]
            return taken

        own = pop(counts[0])
        sources = [pop(len(ride.operands)) for ride in rides]
        own += pop(counts[1])
        targets = [pop(len(ride.out_shapes)) for ride in rides]
        own += pop(counts[2])
        jobs = [
            ride.job(source, target, pop(len(ride.scratch)))
            for ride, source, target in zip(rides, sources, targets)
        ]
        for step in range(steps):
            planned = [
                (job, stages)
                for ride, job in zip(rides, jobs)
                for at, stages in ride.before(steps).items()
                if at == step
            ]
            if planned:

                @pl.when(pl.program_id(0) == step)
                def _(planned=planned, step=step):
                    if step == 0:
                        greet()
                    for job, stages in planned:
                        run_stages([job], stages)

        body(*own)

        @pl.when(pl.program_id(0) == steps - 1)
        def _():
            for ride, job in zip(rides, jobs):
                run_stages([job], ride.after)

    return kernel


def block_call(
    body, grid, in_specs, operands, out_specs, out_shape, scratch, name,
    cost=None, rides=(), collective_id=None,
):
    plain = []
    if rides and not with_kernels():
        plain, rides = [ride.plain() for ride in rides], ()
    transfer = {}
    kernel = body
    if rides:
        transfer = {"collective_id": collective_id, "has_side_effects": True}
        kernel = riding(body, (len(operands), len(out_shape), len(scratch)), rides, grid)
    count = len(out_shape)
    for ride in rides:
        operands = [*operands, *ride.operands]
        in_specs = [*in_specs, *ride.in_specs]
        out_specs, out_shape = [*out_specs, *ride.out_specs], [*out_shape, *ride.out_shapes]
        scratch = [*scratch, *ride.scratch]
    outs = pl.pallas_call(
        kernel,
        grid=(grid,),
        in_specs=in_specs,
        out_specs=out_specs,
        out_shape=out_shape,
        scratch_shapes=scratch,
        compiler_params=pltpu.CompilerParams(vmem_limit_bytes=VMEM_LIMIT, **transfer),
        cost_estimate=cost or NO_COST,
        name=name,
    )(*operands)
    brought, outs = list(outs[count:]), list(outs[:count])
    for ride in rides:
        plain.append(ride.result(brought[: len(ride.out_shapes)]))
        brought = brought[len(ride.out_shapes) :]
    return outs + plain


def work(flops, size):
    return pl.CostEstimate(flops=flops, bytes_accessed=size, transcendentals=0)


def position_weights(seg_col, patch_row, nodes):
    rows = seg_col.shape[0]
    slot = lax.broadcasted_iota(jnp.int32, (rows, IMGS), 1)
    member = seg_col == slot
    counts = jnp.sum(member.astype(jnp.float32), 0, keepdims=True)
    start = jnp.sum(jnp.where(slot < seg_col, counts, 0.0), 1, keepdims=True)
    token = lax.broadcasted_iota(jnp.int32, (rows, 1), 0).astype(jnp.float32)
    inside = seg_col < IMGS
    offset = jnp.where(inside, token - start, 0.0)
    patch = jnp.sum(jnp.where(member, patch_row.astype(jnp.float32), 0.0), 1, keepdims=True)
    side = jnp.where(inside, jnp.floor(IMG / jnp.where(inside, patch, 1.0) + 0.5), 1.0)
    line = jnp.floor((offset + 0.5) / side)
    column = offset - line * side

    def spot(coord):
        return jnp.clip((2.0 * coord + 1.0) * GRID / (2.0 * side) - 0.5, 0.0, GRID - 1.0)

    node = lax.broadcasted_iota(jnp.int32, (rows, LANES), 1).astype(jnp.float32)
    across = jnp.floor((node + 0.5) / GRID)
    along = node - across * GRID
    weights = jnp.maximum(1.0 - jnp.abs(spot(line) - across), 0.0)
    weights = weights * jnp.maximum(1.0 - jnp.abs(spot(column) - along), 0.0)
    return jnp.where(node < nodes, weights, 0.0)


def first_kernel(*refs, spots):
    kernel, vectors, inputs, outputs, head, pixels, seg_col, patch_row, table, biases = refs[:10]
    stream, pos_t, vector_zero, vector_one = refs[10:14]
    qkv_full, up_level, output_level = refs[14:17]
    up_zero, output_zero, qkv_one, up_one, output_one, head_low = refs[17:23]
    wide_kernel, wide_inputs, wide_outputs, wide_head, pixel_rows, table_low = refs[23:29]
    kernel_full, qkv_zero, vectors_full, qkv_landing, up_landing, output_landing = refs[29:35]
    load_sems, sems = refs[35:]
    _, level, core = place()
    mine = 2 * level + core
    pairs = [
        (kernel, wide_kernel),
        (inputs.at[0], wide_inputs.at[0]),
        (pixels, pixel_rows),
        (inputs.at[1], wide_inputs.at[1]),
        (outputs.at[0], wide_outputs.at[0]),
        (outputs.at[1], wide_outputs.at[1]),
        (head, wide_head),
    ]
    copies = [
        pltpu.make_async_copy(source, target, load_sems.at[index])
        for index, (source, target) in enumerate(pairs)
    ]
    for copy in copies:
        copy.start()
    patch_job = Gather(kernel_full.at[mine], kernel_full, sems.at[0], True, in_place=True)
    vector_job = Gather(vectors, vectors_full, sems.at[1], False)
    qkv_job = Gather(qkv_zero, qkv_landing, sems.at[2], True)
    up_job = LevelGather(up_zero, up_landing, sems.at[3])
    up_job.target = up_level
    output_job = LevelGather(output_zero, output_landing, sems.at[4])
    output_job.target = output_level
    copies[0].wait()
    kernel_full[mine] = wide_kernel[...].astype(LOW)
    greet()
    patch_job.first()
    vector_job.first()
    copies[1].wait()
    qkv_zero[...] = wide_inputs[0, :, : 3 * D].astype(LOW)
    qkv_job.first()
    up_zero[...] = wide_inputs[0, :, 3 * D :].astype(LOW)
    up_job.first()
    copies[4].wait()
    output_zero[...] = wide_outputs[0].astype(LOW)
    output_job.first()

    weights = position_weights(seg_col[...], patch_row[...], table.shape[0])
    pos_t[...] = weights.T[: pos_t.shape[0], :]
    table_low[...] = jnp.zeros_like(table_low)
    table_low[: table.shape[0], :] = table[...].astype(LOW).astype(jnp.float32)
    bias = biases[:, :D].astype(LOW).astype(jnp.float32)
    stream[...] = bias + jnp.dot(
        weights, table_low[...], precision=HIGHEST, preferred_element_type=jnp.float32
    )
    copies[2].wait()
    depth = wide_kernel.shape[0]

    def add_block(slot):
        columns = pl.ds(pl.multiple_of(slot * depth, depth), depth)

        def add(step, carry):
            rows = pl.ds(pl.multiple_of(step * 256, 256), 256)
            stream[rows, :] += mul(pixel_rows[rows, columns], kernel_full[slot])
            return carry

        lax.fori_loop(0, stream.shape[0] // 256, add, 0)

    def use(turn, own_core):
        add_block(2 * partner(level, turn) + (core if own_core else 1 - core))

    add_block(mine)
    patch_job.second()
    vector_job.second()
    qkv_job.second()
    patch_job.core_copy(0).wait_recv()
    use(0, False)
    copies[3].wait()
    qkv_one[...] = wide_inputs[1, :, : 3 * D].astype(LOW)
    up_one[...] = wide_inputs[1, :, 3 * D :].astype(LOW)
    copies[5].wait()
    output_one[...] = wide_outputs[1].astype(LOW)
    copies[6].wait()
    head_low[...] = jnp.zeros_like(head_low)
    head_low[:, : head.shape[1]] = wide_head[...].astype(LOW)
    patch_job.relay()
    qkv_job.relay()
    patch_job.third(use)
    qkv_job.third()
    patch_job.fourth(use)
    vector_job.third()
    vector_job.fourth()
    blocks = [vectors_full[slot].astype(jnp.float32) for slot in range(vectors_full.shape[0])]
    span = vectors.shape[0] // LAYERS
    for layer, out in enumerate((vector_zero, vector_one)):
        for row in range(out.shape[1] // LANES):
            parts = [
                block[layer * span + row - spot : layer * span + row - spot + 1, :]
                for block, spot in zip(blocks, spots)
                if 0 <= row - spot < span
            ]
            out[:, row * LANES : (row + 1) * LANES] = sum(parts)
    qkv_job.fourth()
    copy = pltpu.make_async_copy(qkv_landing, qkv_full, load_sems.at[0])
    copy.start()
    run_stages([up_job, output_job], ("fourth", "store"))
    copy.wait()


def padded_vectors(shard):
    layers, width = shard.shape
    owners = lax.axis_size("fsdp")
    spots = [owner * width // LANES for owner in range(owners)]
    span = max(-(-(owner + 1) * width // LANES) - spot for owner, spot in enumerate(spots))
    span += -span % 16
    shift = lax.rem(lax.axis_index("fsdp") * width, LANES)
    padded = jnp.zeros((layers, span * LANES), LOW)
    padded = lax.dynamic_update_slice(padded, shard.astype(LOW), (0, shift))
    return padded.reshape(layers * span, LANES), spots


def begin(
    pixels, segment, patch_size, patch_kernel, layer_vector, input_proj, output_proj, head_weight,
    position_table, global_vector,
):
    classes = head_weight.shape[1] + -head_weight.shape[1] % LANES
    nodes = position_table.shape[0] + -position_table.shape[0] % 64
    if not with_kernels():
        inputs = [
            (input_proj[index, :, : 3 * D].astype(LOW), input_proj[index, :, 3 * D :].astype(LOW))
            for index in range(LAYERS)
        ]
        outputs = [output_proj[index].astype(LOW) for index in range(LAYERS)]
        gather = lambda shard, axis: lax.all_gather(shard, "fsdp", axis=axis, tiled=True)
        weights, _, _ = row_layout(segment, patch_size[0])
        weights = jnp.pad(weights, ((0, 0), (0, nodes - weights.shape[1])))
        table = jnp.pad(rounded(position_table), ((0, nodes - position_table.shape[0]), (0, 0)))
        bias = rounded(global_vector)[None, :D]
        stream = embed(pixels, gather(patch_kernel.astype(LOW), 0), weights, table, bias)
        vectors = gather(layer_vector.astype(LOW), 1).astype(jnp.float32)
        head = jnp.pad(head_weight.astype(LOW), ((0, 0), (0, classes - head_weight.shape[1])))
        return (
            stream,
            weights.T,
            [vectors[index : index + 1] for index in range(LAYERS)],
            gather(inputs[0][0], 0),
            [*[GatherRide(shard, shard) for shard in (inputs[0][1], outputs[0])], LevelRide(outputs[1])],
            [*inputs[1], head],
        )
    rows = pixels.shape[0]
    owners = lax.axis_size("fsdp")
    vectors, spots = padded_vectors(layer_vector)
    depth = input_proj.shape[1]
    up_shape = (depth, input_proj.shape[2] - 3 * D)
    qkv_shape, out_shape = (depth, 3 * D), output_proj.shape[1:]
    low = lambda *shape: jax.ShapeDtypeStruct(shape, LOW)
    levels = lambda shape: low(4, *quarter_shape(*shape))
    width = layer_vector.shape[1] * owners
    shapes = [
        shape_of(rows, D),
        shape_of(nodes, rows),
        shape_of(1, width),
        shape_of(1, width),
        low(owners, *qkv_shape),
        levels(up_shape),
        levels(out_shape),
        low(*up_shape),
        low(*out_shape),
        low(*qkv_shape),
        low(*up_shape),
        low(*out_shape),
        low(head_weight.shape[0], classes),
    ]
    wide = (patch_kernel, input_proj, output_proj, head_weight, pixels)
    in_vmem = pl.BlockSpec(memory_space=pltpu.VMEM)
    results = pl.pallas_call(
        functools.partial(first_kernel, spots=spots),
        in_specs=[ANYWHERE] * 6 + [in_vmem] * 4,
        out_specs=[in_vmem] * 4 + [ANYWHERE] + [in_vmem] * 8,
        out_shape=shapes,
        scratch_shapes=[
            *[pltpu.VMEM(array.shape, array.dtype) for array in wide],
            pltpu.VMEM((LANES, D), jnp.float32),
            pltpu.VMEM((owners, *patch_kernel.shape), LOW),
            pltpu.VMEM(qkv_shape, LOW),
            pltpu.VMEM((owners, *vectors.shape), LOW),
            pltpu.VMEM((owners, *qkv_shape), LOW),
            pltpu.VMEM((4, *quarter_shape(*up_shape)), LOW),
            pltpu.VMEM((4, *quarter_shape(*out_shape)), LOW),
            pltpu.SemaphoreType.DMA((7,)),
            pltpu.SemaphoreType.DMA((5, GATHER_SEMS)),
        ],
        compiler_params=pltpu.CompilerParams(
            collective_id=1, has_side_effects=True, vmem_limit_bytes=VMEM_LIMIT
        ),
        cost_estimate=NO_COST,
        name="begin",
    )(
        patch_kernel,
        vectors,
        input_proj,
        output_proj,
        head_weight,
        pixels,
        segment[:, None],
        patch_size,
        position_table,
        global_vector[None, :],
    )
    up_zero, output_zero, qkv_one, up_one, output_one, head_low = results[7:]
    return (
        results[0],
        results[1],
        results[2:4],
        results[4].reshape(owners * depth, 3 * D),
        [GatherRide(up_zero, results[5]), GatherRide(output_zero, results[6]), LevelRide(output_one)],
        [qkv_one, up_one, head_low],
    )


REDUCE_SEMS = 48


class Reduce:
    def __init__(self, grad, out, scratch, sems):
        self.grad, self.out, self.sems = grad, out, sems
        self.own, self.got_core, self.got_group, self.part, self.got_level = scratch
        self.rows, self.columns = out.shape
        self.chunk = 16

    def load(self, level):
        _, _, core = place()
        return pltpu.make_async_copy(
            self.grad.at[2 * level + core], self.own.at[level], self.sems.at[level]
        )

    def core_copy(self, target_level):
        group, level, core = place()
        return remote(
            self.grad.at[2 * target_level + 1 - core],
            self.got_core.at[target_level],
            self.sems.at[4 + target_level],
            self.sems.at[8 + target_level],
            (group, 2 * level + 1 - core),
        )

    def group_copy(self, turn, other):
        group, level, core = place()
        target = partner(level, turn)
        peer = partner(group, other)
        part = quarter(peer, self.rows, self.columns)
        index = 3 * turn + other - 1
        return remote(
            self.own.at[target].at[part],
            self.got_group.at[other - 1, target],
            self.sems.at[12 + index],
            self.sems.at[24 + index],
            (peer, 2 * level + core),
        )

    def level_copy(self, turn):
        group, level, core = place()
        target = partner(level, turn)
        return remote(
            self.part.at[target],
            self.got_level.at[turn - 1],
            self.sems.at[35 + turn],
            self.sems.at[38 + turn],
            (group, 2 * target + core),
        )

    def share_copy(self, other):
        group, level, core = place()
        mine = self.out.at[quarter(group, self.rows, self.columns)]
        return remote(
            mine,
            mine,
            self.sems.at[41 + other],
            self.sems.at[44 + other],
            (partner(group, other), 2 * level + core),
        )

    def first(self):
        _, level, _ = place()
        for turn in (*TURNS, 0):
            self.core_copy(partner(level, turn)).start()
            self.load(partner(level, turn)).start()

    def second(self):
        _, level, _ = place()
        for turn in (*TURNS, 0):
            target = partner(level, turn)
            self.load(target).wait()
            self.core_copy(target).wait_recv()

            def add(step, carry):
                rows = pl.ds(pl.multiple_of(step * self.chunk, self.chunk), self.chunk)
                total = self.own[target, rows, :].astype(jnp.float32)
                total = total + self.got_core[target, rows, :].astype(jnp.float32)
                self.own[target, rows, :] = total.astype(self.own.dtype)
                return carry

            lax.fori_loop(0, self.rows // self.chunk, add, 0)
            for other in TURNS:
                self.group_copy(turn, other).start()

    def between(self):
        pass

    def third(self):
        group, level, _ = place()
        high, wide = quarter_shape(self.rows, self.columns)
        row_part, column_part = quarter(group, self.rows, self.columns)
        for turn in (*TURNS, 0):
            target = partner(level, turn)
            for other in TURNS:
                self.group_copy(turn, other).wait_recv()

            def add(step, carry):
                at = pl.multiple_of(step * self.chunk, self.chunk)
                rows = pl.ds(at, self.chunk)
                mine = pl.ds(pl.multiple_of(row_part.start + at, self.chunk), self.chunk)
                total = self.own[target, mine, column_part].astype(jnp.float32)
                for slot in range(3):
                    total = total + self.got_group[slot, target, rows, :].astype(jnp.float32)
                self.part[target, rows, :] = total.astype(self.part.dtype)
                return carry

            lax.fori_loop(0, high // self.chunk, add, 0)
            if turn:
                self.level_copy(turn).start()

    def fourth(self):
        group, level, _ = place()
        high, wide = quarter_shape(self.rows, self.columns)
        row_part, column_part = quarter(group, self.rows, self.columns)
        for turn in TURNS:
            self.level_copy(turn).wait_recv()

        def add(step, carry):
            at = pl.multiple_of(step * self.chunk, self.chunk)
            rows = pl.ds(at, self.chunk)
            mine = pl.ds(pl.multiple_of(row_part.start + at, self.chunk), self.chunk)
            total = self.part[level, rows, :].astype(jnp.float32)
            for slot in range(3):
                total = total + self.got_level[slot, rows, :].astype(jnp.float32)
            self.out[mine, column_part] = total.astype(self.out.dtype)
            return carry

        lax.fori_loop(0, high // self.chunk, add, 0)
        for other in TURNS:
            self.share_copy(other).start()

    def store(self):
        self.target[...] = self.out[...]

    def fifth(self):
        for other in TURNS:
            self.share_copy(other).wait_recv()

    def sixth(self):
        _, level, _ = place()
        for turn in (*TURNS, 0):
            self.core_copy(partner(level, turn)).wait_send()
            for other in TURNS:
                self.group_copy(turn, other).wait_send()
            if turn:
                self.level_copy(turn).wait_send()
                self.share_copy(turn).wait_send()


WHOLE_SEMS = 40


def add_rows(target, row, columns, source, count, wide):
    chunk = 16 if wide > 1536 else 48

    def add(step, carry):
        at = pl.multiple_of(step * chunk, chunk)
        mine = pl.ds(pl.multiple_of(row + at, 16), chunk)
        total = target[mine, columns].astype(jnp.float32)
        total = total + source[pl.ds(at, chunk), :].astype(jnp.float32)
        target[mine, columns] = total.astype(target.dtype)
        return carry

    lax.fori_loop(0, count // chunk, add, 0)


class Whole:
    FIRST_X = (1, 0)

    def __init__(self, grad, out, scratch, sems):
        self.grad, self.out, self.sems = grad, out, sems
        self.own, self.got_core, self.got_x, self.got_y, self.got_last, self.part, self.got_level = scratch
        self.rows, self.columns = out.shape
        self.high, self.wide = self.rows // 2, self.columns // 2

    def row_half(self, index):
        return pl.ds(pl.multiple_of(lax.div(index, 2) * self.high, self.high), self.high)

    def column_half(self, index):
        return pl.ds(pl.multiple_of(lax.rem(index, 2) * self.wide, self.wide), self.wide)

    def load(self, level):
        _, _, core = place()
        return pltpu.make_async_copy(
            self.grad.at[2 * level + core], self.own.at[level], self.sems.at[level]
        )

    def core_copy(self, target_level):
        group, level, core = place()
        return remote(
            self.grad.at[2 * target_level + 1 - core],
            self.got_core.at[target_level],
            self.sems.at[4 + target_level],
            self.sems.at[8 + target_level],
            (group, 2 * level + 1 - core),
        )

    def step_copy(self, turn):
        group, level, core = place()
        block = self.own.at[partner(level, turn)]
        if turn in self.FIRST_X:
            peer = partner(group, 1)
            source = block.at[:, self.column_half(peer)]
            target = self.got_x.at[self.FIRST_X.index(turn)]
        else:
            peer = partner(group, 2)
            source = block.at[self.row_half(peer), :]
            target = self.got_y.at[turn - 2]
        return remote(
            source, target, self.sems.at[12 + turn], self.sems.at[16 + turn], (peer, 2 * level + core)
        )

    def last_copy(self, turn):
        group, level, core = place()
        block = self.own.at[partner(level, turn)]
        peer = partner(group, 2 if turn in self.FIRST_X else 1)
        rows = self.row_half(peer)
        columns = self.column_half(peer)
        return remote(
            block.at[rows, columns],
            self.got_last.at[turn],
            self.sems.at[20 + turn],
            self.sems.at[24 + turn],
            (peer, 2 * level + core),
        )

    def level_copy(self, turn):
        group, level, core = place()
        target = partner(level, turn)
        return remote(
            self.part.at[target],
            self.got_level.at[turn - 1],
            self.sems.at[27 + turn],
            self.sems.at[30 + turn],
            (group, 2 * target + core),
        )

    def share_copy(self, other):
        group, level, core = place()
        mine = self.out.at[self.row_half(group), self.column_half(group)]
        return remote(
            mine,
            mine,
            self.sems.at[33 + other],
            self.sems.at[36 + other],
            (partner(group, other), 2 * level + core),
        )

    def first(self):
        _, level, _ = place()
        for turn in (*TURNS, 0):
            self.core_copy(partner(level, turn)).start()
            self.load(partner(level, turn)).start()

    def second(self):
        _, level, _ = place()
        for turn in (*TURNS, 0):
            target = partner(level, turn)
            self.load(target).wait()
            self.core_copy(target).wait_recv()
            add_rows(
                self.own.at[target], 0, slice(None), self.got_core.at[target], self.rows, self.columns
            )
            self.step_copy(turn).start()

    def between(self):
        group, level, _ = place()
        for turn in (*TURNS, 0):
            block = self.own.at[partner(level, turn)]
            self.step_copy(turn).wait_recv()
            if turn in self.FIRST_X:
                source = self.got_x.at[self.FIRST_X.index(turn)]
                add_rows(block, 0, self.column_half(group), source, self.rows, self.wide)
            else:
                source = self.got_y.at[turn - 2]
                start = lax.div(group, 2) * self.high
                add_rows(block, start, slice(None), source, self.high, self.columns)
            self.last_copy(turn).start()

    def third(self):
        group, level, _ = place()
        start = lax.div(group, 2) * self.high
        columns = self.column_half(group)
        chunk = 16 if self.wide > 1536 else 48
        for turn in (*TURNS, 0):
            target = partner(level, turn)
            self.last_copy(turn).wait_recv()

            def add(step, carry):
                at = pl.multiple_of(step * chunk, chunk)
                rows = pl.ds(at, chunk)
                mine = pl.ds(pl.multiple_of(start + at, 16), chunk)
                total = self.own[target, mine, columns].astype(jnp.float32)
                total = total + self.got_last[turn, rows, :].astype(jnp.float32)
                self.part[target, rows, :] = total.astype(self.part.dtype)
                return carry

            lax.fori_loop(0, self.high // chunk, add, 0)
            if turn:
                self.level_copy(turn).start()

    def fourth(self):
        group, level, _ = place()
        start = lax.div(group, 2) * self.high
        columns = self.column_half(group)
        chunk = 16 if self.wide > 1536 else 48
        for turn in TURNS:
            self.level_copy(turn).wait_recv()

        def add(step, carry):
            at = pl.multiple_of(step * chunk, chunk)
            rows = pl.ds(at, chunk)
            mine = pl.ds(pl.multiple_of(start + at, 16), chunk)
            total = self.part[level, rows, :].astype(jnp.float32)
            for slot in range(3):
                total = total + self.got_level[slot, rows, :].astype(jnp.float32)
            self.out[mine, columns] = total.astype(self.out.dtype)
            return carry

        lax.fori_loop(0, self.high // chunk, add, 0)
        for other in TURNS:
            self.share_copy(other).start()

    def store(self):
        self.target[...] = self.out[...]

    def fifth(self):
        for other in TURNS:
            self.share_copy(other).wait_recv()

    def sixth(self):
        _, level, _ = place()
        for turn in (*TURNS, 0):
            self.core_copy(partner(level, turn)).wait_send()
            self.step_copy(turn).wait_send()
            self.last_copy(turn).wait_send()
            if turn:
                self.level_copy(turn).wait_send()
                self.share_copy(turn).wait_send()


GROUP_SEMS = 13


class GroupReduce:
    def __init__(self, share, out, scratch, sems):
        self.share, self.out, self.sems = share, out, sems
        self.own, self.got = scratch
        self.rows, self.columns = out.shape
        self.chunk = 16

    def load(self):
        return pltpu.make_async_copy(self.share, self.own, self.sems.at[0])

    def group_copy(self, other):
        group, level, core = place()
        peer = partner(group, other)
        return remote(
            self.own.at[quarter(peer, self.rows, self.columns)],
            self.got.at[other - 1],
            self.sems.at[other],
            self.sems.at[3 + other],
            (peer, 2 * level + core),
        )

    def share_copy(self, other):
        group, level, core = place()
        mine = self.out.at[quarter(group, self.rows, self.columns)]
        return remote(
            mine,
            mine,
            self.sems.at[6 + other],
            self.sems.at[9 + other],
            (partner(group, other), 2 * level + core),
        )

    def first(self):
        self.load().start()

    def second(self):
        self.load().wait()
        for other in TURNS:
            self.group_copy(other).start()

    def between(self):
        pass

    def third(self):
        group, _, _ = place()
        high, wide = quarter_shape(self.rows, self.columns)
        row_part, column_part = quarter(group, self.rows, self.columns)
        for other in TURNS:
            self.group_copy(other).wait_recv()

        def add(step, carry):
            at = pl.multiple_of(step * self.chunk, self.chunk)
            rows = pl.ds(at, self.chunk)
            mine = pl.ds(pl.multiple_of(row_part.start + at, self.chunk), self.chunk)
            total = self.own[mine, column_part].astype(jnp.float32)
            for slot in range(3):
                total = total + self.got[slot, rows, :].astype(jnp.float32)
            self.out[mine, column_part] = total.astype(self.out.dtype)
            return carry

        lax.fori_loop(0, high // self.chunk, add, 0)
        for other in TURNS:
            self.share_copy(other).start()

    def fourth(self):
        pass

    def fifth(self):
        for other in TURNS:
            self.share_copy(other).wait_recv()

    def store(self):
        self.target[...] = self.out[...]

    def sixth(self):
        for other in TURNS:
            self.group_copy(other).wait_send()
            self.share_copy(other).wait_send()


class Spread:
    def __init__(self, full, sems):
        self.full, self.sems = full, sems

    def level_copy(self, turn):
        group, level, core = place()
        block = self.full.at[2 * level + core]
        peer = (group, 2 * partner(level, turn) + core)
        return remote(block, block, self.sems.at[turn - 1], self.sems.at[2 + turn], peer)

    def core_copy(self, turn):
        group, level, core = place()
        block = self.full.at[2 * partner(level, turn) + core]
        peer = (group, 2 * level + 1 - core)
        return remote(block, block, self.sems.at[6 + turn], self.sems.at[10 + turn], peer)

    def run(self):
        for turn in TURNS:
            self.level_copy(turn).start()
        self.core_copy(0).start()
        for turn in TURNS:
            self.level_copy(turn).wait_recv()
            self.core_copy(turn).start()
        for turn in (0, *TURNS):
            self.core_copy(turn).wait_recv()
        for turn in (0, *TURNS):
            self.core_copy(turn).wait_send()
            if turn:
                self.level_copy(turn).wait_send()


def squares_in(out):
    def add(step, total):
        piece = out[pl.ds(pl.multiple_of(step * 16, 16), 16), :].astype(jnp.float32)
        piece = piece * piece
        for lane in range(0, out.shape[1], LANES):
            total = total + piece[:, lane : lane + LANES]
        return total

    total = lax.fori_loop(0, out.shape[0] // 16, add, jnp.zeros((16, LANES), jnp.float32))
    return jnp.sum(total, 0, keepdims=True)


def run_stages(jobs, stages):
    for stage in stages:
        for job in jobs:
            getattr(job, stage)()


STAGES = ("first", "second", "between", "third", "fourth", "fifth", "sixth")


def whole_scratch(grad):
    _, rows, columns = grad.shape
    high, wide = quarter_shape(rows, columns)
    shapes = ((4, rows, columns), (4, rows, columns), (3, 4, high, wide), (4, high, wide))
    return [pltpu.VMEM(shape, grad.dtype) for shape in (*shapes, (3, high, wide))]


def stepped_scratch(grad):
    _, rows, columns = grad.shape
    high, wide = rows // 2, columns // 2
    shapes = (
        (4, rows, columns),
        (4, rows, columns),
        (2, rows, wide),
        (2, high, columns),
        (4, high, wide),
        (4, high, wide),
        (3, high, wide),
    )
    return [pltpu.VMEM(shape, grad.dtype) for shape in shapes]


def share_scratch(share):
    return [
        pltpu.VMEM(share.shape, share.dtype),
        pltpu.VMEM((3, *quarter_shape(*share.shape)), share.dtype),
    ]


def reduce_kernel(*refs, whole, partly):
    count = whole + partly
    grads, outs, refs = refs[:count], refs[count : 2 * count], refs[2 * count :]
    sems, group_sems, refs = refs[0], refs[1], refs[2:]
    jobs = [
        Whole(grads[i], outs[i], refs[7 * i : 7 * i + 7], sems.at[i]) for i in range(whole)
    ]
    refs = refs[7 * whole :]
    shares = [
        GroupReduce(grads[whole + i], outs[whole + i], refs[2 * i : 2 * i + 2], group_sems.at[i])
        for i in range(partly)
    ]
    greet()
    run_stages([*jobs, *shares], STAGES[:1])
    run_stages(shares, STAGES[1:2])
    run_stages(jobs, STAGES[1:3])
    run_stages(shares, STAGES[3:4])
    run_stages(jobs, STAGES[3:5])
    run_stages([*shares, *jobs], STAGES[5:])


def transfer_cost(size):
    return pl.CostEstimate(flops=4000 * size, bytes_accessed=2 * size, transcendentals=0)


def reduce_call(grads, shares, collective_id):
    in_vmem = pl.BlockSpec(memory_space=pltpu.VMEM)
    whole, partly = len(grads), len(shares)
    scratch = [
        pltpu.SemaphoreType.DMA((whole, WHOLE_SEMS)),
        pltpu.SemaphoreType.DMA((partly, GROUP_SEMS)),
    ]
    for grad in grads:
        scratch.extend(stepped_scratch(grad))
    for share in shares:
        scratch.extend(share_scratch(share))
    out_shape = [jax.ShapeDtypeStruct(g.shape[1:], g.dtype) for g in grads]
    out_shape += [jax.ShapeDtypeStruct(s.shape, s.dtype) for s in shares]
    return pl.pallas_call(
        functools.partial(reduce_kernel, whole=whole, partly=partly),
        in_specs=[ANYWHERE] * (whole + partly),
        out_specs=[in_vmem] * (whole + partly),
        out_shape=out_shape,
        scratch_shapes=scratch,
        compiler_params=pltpu.CompilerParams(
            collective_id=collective_id, has_side_effects=True, vmem_limit_bytes=VMEM_LIMIT
        ),
        cost_estimate=NO_COST,
        name="reduce_gradients",
    )(*grads, *shares)


def finish_kernel(*refs, done, partly):
    finished, refs = refs[:done], refs[done:]
    shares, small, refs = refs[:partly], refs[partly], refs[partly + 1 :]
    outs, small_out, full, refs = refs[:partly], refs[partly], refs[partly + 1], refs[partly + 2 :]
    sems, group_sems, spread_sems, refs = refs[0], refs[1], refs[2], refs[3:]
    job = Reduce(small, small_out, refs[:5], sems)
    refs = refs[5:]
    jobs = [
        GroupReduce(shares[i], outs[i], refs[2 * i : 2 * i + 2], group_sems.at[i])
        for i in range(partly)
    ]
    greet()
    run_stages([job, *jobs], STAGES[:3])
    total = sum(squares_in(out) for out in finished)
    run_stages([*jobs, job], STAGES[3:6])
    total = total + sum(squares_in(out) for out in outs)
    _, level, core = place()
    mine = 2 * level + core
    last = small_out.shape[0] - 1
    full[mine] = small_out[...]
    full[mine, last : last + 1, :] = total
    Spread(full, spread_sems).run()
    run_stages([job, *jobs], STAGES[6:])


def finish_call(finished, shares, small, collective_id):
    done, partly = len(finished), len(shares)
    in_vmem = pl.BlockSpec(memory_space=pltpu.VMEM)
    scratch = [
        pltpu.SemaphoreType.DMA((REDUCE_SEMS,)),
        pltpu.SemaphoreType.DMA((partly, GROUP_SEMS)),
        pltpu.SemaphoreType.DMA((14,)),
        *whole_scratch(small),
    ]
    for share in shares:
        scratch.extend(share_scratch(share))
    out_shape = [jax.ShapeDtypeStruct(s.shape, s.dtype) for s in shares]
    out_shape.append(jax.ShapeDtypeStruct(small.shape[1:], small.dtype))
    out_shape.append(jax.ShapeDtypeStruct(small.shape, small.dtype))
    return pl.pallas_call(
        functools.partial(finish_kernel, done=done, partly=partly),
        in_specs=[in_vmem] * done + [ANYWHERE] * (partly + 1),
        out_specs=[in_vmem] * len(out_shape),
        out_shape=out_shape,
        scratch_shapes=scratch,
        compiler_params=pltpu.CompilerParams(
            collective_id=collective_id, has_side_effects=True, vmem_limit_bytes=VMEM_LIMIT
        ),
        name="finish_gradients",
    )(*finished, *shares, small)


def with_kernels():
    return lax.axis_size("dp") == 4 and lax.axis_size("fsdp") == 8


def reduce_all(grads, shares, collective_id):
    if with_kernels():
        return reduce_call(grads, shares, collective_id)
    return [lax.psum(scatter(grad), "dp") for grad in grads] + sum_shares(shares)


def sum_shares(shares):
    return [lax.psum(share, "dp") for share in shares]


def finish_all(finished, shares, small, collective_id):
    if with_kernels():
        return finish_call(finished, shares, small, collective_id)
    outs = [lax.psum(share, "dp") for share in shares]
    own = lax.psum(scatter(small), "dp")
    total = sum(jnp.sum(jnp.square(out.astype(jnp.float32))) for out in (*finished, *outs))
    row = jnp.full((1, LANES), 1.0 / LANES, jnp.float32) * total
    return [*outs, own, lax.all_gather(own.at[-1:].set(row), "fsdp", axis=0)]


def scatter(grad):
    return lax.psum_scatter(grad, "fsdp", scatter_dimension=0)


def by_owner(grad, low=jnp.bfloat16):
    owners = lax.axis_size("fsdp")
    return grad.astype(low).reshape(owners, grad.shape[0] // owners, grad.shape[1])


def attention_forward_kernel(
    q_ref, k_ref, v_ref, seg_col_ref, seg_row_ref, out_ref, expo_ref, inv_ref, *, block
):
    rows = q_ref.shape[0]
    lower = lax.broadcasted_iota(jnp.int32, (block, PAIR), 1) < HD
    keys = k_ref[...]
    values = jnp.concatenate([v_ref[...], jnp.ones((rows, PAIR), v_ref.dtype)], 1)
    seg_row = seg_row_ref[...]
    tasks = [(step, head) for step in range(rows // block) for head in range(2)]

    def scores_of(step, head):
        query = q_ref[step * block : (step + 1) * block, :] * jnp.bfloat16(HD**-0.5)
        keep = lower if head == 0 else jnp.logical_not(lower)
        return mul_nt(jnp.where(keep, query, jnp.bfloat16(0)), keys)

    scores = scores_of(*tasks[0])
    outs = []
    for index, (step, head) in enumerate(tasks):
        following = scores_of(*tasks[index + 1]) if index + 1 < len(tasks) else None
        at = slice(step * block, (step + 1) * block)
        scores = jnp.where(seg_col_ref[at, :] == seg_row, scores, MASKED)
        highest = jnp.max(scores, -1, keepdims=True)
        low = jnp.exp(scores - highest).astype(jnp.bfloat16)
        expo_ref[head, at, :] = low
        outs.append(mul(low, values))
        if head:
            inverse = 1.0 / jnp.where(lower, outs[0][:, PAIR:], outs[1][:, PAIR:])
            sums = jnp.where(lower, outs[0][:, :PAIR], outs[1][:, :PAIR])
            out_ref[at, :] = (sums * inverse).astype(jnp.bfloat16)
            inv_ref[at, :] = inverse
            outs = []
        scores = following


def attention_forward(qkv_rows, segment, rides, collective_id):
    rows = qkv_rows.shape[0]
    pairs = HEADS // 2
    wide = lambda base: pl.BlockSpec((rows, PAIR), lambda j, base=base: (0, base + j))
    return block_call(
        functools.partial(attention_forward_kernel, block=min(256, rows)),
        pairs,
        [wide(0), wide(pairs), wide(2 * pairs), fixed(rows, 1), fixed(1, rows)],
        [qkv_rows, qkv_rows, qkv_rows, segment[:, None], segment[None, :]],
        [wide(0), pl.BlockSpec((2, rows, rows), lambda j: (j, 0, 0)), wide(0)],
        [
            shape_of(rows, D, dtype=LOW),
            shape_of(HEADS, rows, rows, dtype=LOW),
            shape_of(rows, D),
        ],
        [],
        "attention_forward",
        work(16 * HEADS * rows * rows * HD, 2 * HEADS * rows * rows + 12 * rows * D),
        rides,
        collective_id,
    )


def attention_backward_kernel(
    q_ref, k_ref, v_ref, expo_ref, inv_ref, out_ref, grad_ref, dqkv_ref, *, block
):
    rows = q_ref.shape[0]
    pair = pl.program_id(0)
    lower = lax.broadcasted_iota(jnp.int32, (block, PAIR), 1) < HD
    keys = k_ref[...]
    values = v_ref[...]
    scale = HD**-0.5
    scaled_grad = (grad_ref[...].astype(jnp.float32) * inv_ref[...]).astype(jnp.bfloat16)
    query = q_ref[...]
    query_t = query.T
    grad_t = scaled_grad.T
    product = scaled_grad.astype(jnp.float32) * out_ref[...].astype(jnp.float32)
    key_t = [None, None]
    value_t = [None, None]
    tasks = [(step, head) for step in range(rows // block) for head in range(2)]

    def probs_grad_of(step, head):
        keep = lower if head == 0 else jnp.logical_not(lower)
        mine = scaled_grad[step * block : (step + 1) * block]
        return mul_nt(jnp.where(keep, mine, jnp.bfloat16(0)), values)

    probs_grad = probs_grad_of(*tasks[0])
    query_parts = []
    for index, (step, head) in enumerate(tasks):
        following = probs_grad_of(*tasks[index + 1]) if index + 1 < len(tasks) else None
        at = slice(step * block, (step + 1) * block)
        lanes = slice(head * HD, (head + 1) * HD)
        keep = lower if head == 0 else jnp.logical_not(lower)
        inner = jnp.sum(jnp.where(keep, product[at], 0.0), -1, keepdims=True)
        low = expo_ref[head, at, :]
        value_part = mul(grad_t[lanes, at], low)
        scores_grad = (low.astype(jnp.float32) * (probs_grad - inner)).astype(jnp.bfloat16)
        query_parts.append(mul(scores_grad, keys))
        key_part = mul(query_t[lanes, at], scores_grad)
        key_t[head] = key_part if step == 0 else key_t[head] + key_part
        value_t[head] = value_part if step == 0 else value_t[head] + value_part
        if head:
            query_grad = jnp.where(lower, query_parts[0], query_parts[1]) * scale
            dqkv_ref[at, pl.ds(pl.multiple_of(pair * PAIR, PAIR), PAIR)] = query_grad.astype(
                jnp.bfloat16
            )
            query_parts = []
        probs_grad = following
    key_grad = (jnp.concatenate(key_t, 0) * scale).T
    value_grad = jnp.concatenate(value_t, 0).T
    dqkv_ref[:, pl.ds(pl.multiple_of(D + pair * PAIR, PAIR), PAIR)] = key_grad.astype(jnp.bfloat16)
    dqkv_ref[:, pl.ds(pl.multiple_of(2 * D + pair * PAIR, PAIR), PAIR)] = value_grad.astype(jnp.bfloat16)


def attention_backward(qkv_rows, expo, inverse, attended, attended_grad, rides, collective_id):
    rows = qkv_rows.shape[0]
    pairs = HEADS // 2
    wide = lambda base: pl.BlockSpec((rows, PAIR), lambda j, base=base: (0, base + j))
    return block_call(
        functools.partial(attention_backward_kernel, block=min(256, rows)),
        pairs,
        [
            wide(0),
            wide(pairs),
            wide(2 * pairs),
            pl.BlockSpec((2, rows, rows), lambda j: (j, 0, 0)),
            wide(0),
            wide(0),
            wide(0),
        ],
        [qkv_rows, qkv_rows, qkv_rows, expo, inverse, attended, attended_grad],
        [fixed(rows, 3 * D)],
        [shape_of(rows, 3 * D, dtype=LOW)],
        [],
        "attention_backward",
        None,
        rides,
        collective_id,
    )


def mul(left, right):
    return jnp.dot(left, right, preferred_element_type=jnp.float32)


def mul_nt(left, right):
    return lax.dot_general(left, right, NT, preferred_element_type=jnp.float32)


def normalized(values):
    center = values - jnp.mean(values, -1, keepdims=True)
    inverse = lax.rsqrt(jnp.mean(center * center, -1, keepdims=True) + NORM_EPS)
    return center * inverse, inverse


def norm_backward(grad, values, gain):
    unit, inverse = normalized(values)
    inner = grad * gain
    mean_inner = jnp.mean(inner, -1, keepdims=True)
    mean_cross = jnp.mean(inner * unit, -1, keepdims=True)
    value_grad = inverse * (inner - mean_inner - unit * mean_cross)
    return value_grad, column_sum(grad * unit), column_sum(grad)


def column_sum(rows):
    return jnp.sum(rows.astype(jnp.float32), 0, keepdims=True)


def at_first(action):
    pl.when(pl.program_id(0) == 0)(action)


def rows_of(block, columns):
    return pl.BlockSpec((block, columns), lambda i: (i, 0))


def fixed(*shape):
    return pl.BlockSpec(shape, lambda i: (0,) * len(shape), pipeline_mode=pl.Buffered(1))


def loads(sources, targets, sems):
    return [
        pltpu.make_async_copy(source, target, sems.at[index])
        for index, (source, target) in enumerate(zip(sources, targets))
    ]


def shape_of(*shape, dtype=jnp.float32):
    return jax.ShapeDtypeStruct(shape, dtype)


def embed_kernel(pixel_ref, weight_ref, pos_ref, table_ref, bias_ref, out_ref):
    position = jnp.dot(
        pos_ref[...], table_ref[...], precision=HIGHEST, preferred_element_type=jnp.float32
    )
    out_ref[...] = mul(pixel_ref[...], weight_ref[...]) + bias_ref[...] + position


def embed(pixels, weight, pos_weights, table, bias):
    rows, depth = pixels.shape
    block = 256
    nodes = pos_weights.shape[1]
    return block_call(
        embed_kernel,
        rows // block,
        [rows_of(block, depth), fixed(depth, D), rows_of(block, nodes), fixed(nodes, D), fixed(1, D)],
        [pixels, weight, pos_weights, table, bias],
        [rows_of(block, D)],
        [shape_of(rows, D)],
        [],
        "embed",
        work(2 * rows * depth * D, 2 * rows * depth + 2 * depth * D + 4 * rows * D),
    )[0]


def chunk_at(base):
    return pl.ds(pl.multiple_of(base + pl.program_id(0) * D, LANES), D)


def columns_of(rows):
    return pl.BlockSpec((rows, D), lambda i: (0, i))


def halves_of(rows):
    half = rows // 2
    return [slice(start, start + half) for start in range(0, rows, half)]


def at_last(action):
    pl.when(pl.program_id(0) == pl.num_programs(0) - 1)(action)


def qkv_kernel(stream_ref, weight_ref, vector_ref, normed_out, qkv_ref, normed_ref, sem):
    copy = pltpu.make_async_copy(normed_ref, normed_out, sem)

    @at_first
    def _():
        unit, _ = normalized(stream_ref[...])
        normed_ref[...] = (unit * vector_ref[:, :D] + vector_ref[:, D : 2 * D]).astype(LOW)
        copy.start()

    bias = vector_ref[:, chunk_at(4 * D)]
    for half in halves_of(stream_ref.shape[0]):
        qkv_ref[half, :] = (mul(normed_ref[half, :], weight_ref[...]) + bias).astype(LOW)
    at_last(copy.wait)


def qkv_forward(stream, weight, vector):
    rows = stream.shape[0]
    return block_call(
        qkv_kernel,
        3,
        [fixed(rows, D), columns_of(D), fixed(1, vector.shape[1])],
        [stream, weight, vector],
        [ANYWHERE, columns_of(rows)],
        [shape_of(rows, D, dtype=LOW), shape_of(rows, 3 * D, dtype=LOW)],
        [pltpu.VMEM((rows, D), LOW), pltpu.SemaphoreType.DMA],
        "qkv_forward",
        work(6 * rows * D * D, 14 * rows * D + 6 * D * D),
    )


def mlp_kernel(
    stream_ref, attended_ref, mix_ref, up_ref, down_ref, vector_ref,
    residual_out, normed_out, active_ref, slope_ref, out_ref,
    residual_ref, normed_ref, sems,
):
    rows = stream_ref.shape[0]
    copies = loads((residual_ref, normed_ref), (residual_out, normed_out), sems)

    @at_first
    def _():
        for half in halves_of(rows):
            residual = stream_ref[half, :] + mul(attended_ref[half, :], mix_ref[...])
            residual = residual + vector_ref[:, 7 * D : 8 * D]
            residual_ref[half, :] = residual
            unit, _ = normalized(residual)
            normed = unit * vector_ref[:, 2 * D : 3 * D] + vector_ref[:, 3 * D : 4 * D]
            normed_ref[half, :] = normed.astype(LOW)
            out_ref[half, :] = residual + vector_ref[:, 8 * D : 9 * D]
        for copy in copies:
            copy.start()

    bias = vector_ref[:, chunk_at(9 * D)]
    parts = halves_of(rows)
    hidden = mul(normed_ref[parts[0], :], up_ref[...]) + bias
    for index, half in enumerate(parts):
        following = None
        if index + 1 < len(parts):
            following = mul(normed_ref[parts[index + 1], :], up_ref[...]) + bias
        square = hidden * hidden
        rise = 0.5 + 0.5 * jnp.tanh(hidden * (ROOT + (ROOT * CUBE) * square))
        active = hidden * rise
        active_low = active.astype(LOW)
        active_ref[half, :] = active_low
        bend = (2.0 * ROOT) + (6.0 * ROOT * CUBE) * square
        slope_ref[half, :] = (rise + active * (1.0 - rise) * bend).astype(LOW)
        out_ref[half, :] += mul(active_low, down_ref[...])
        hidden = following

    @at_last
    def _():
        for copy in copies:
            copy.wait()


def mlp_specs(up, proj_out):
    return (
        [fixed(D, D), columns_of(D), pl.BlockSpec((D, D), lambda i: (i + 1, 0))],
        [proj_out, up, proj_out],
    )


def mlp_forward(stream, attended, up, proj_out, vector, rides, collective_id):
    rows = stream.shape[0]
    width = up.shape[1]
    weight_specs, weights = mlp_specs(up, proj_out)
    return block_call(
        mlp_kernel,
        width // D,
        [fixed(rows, D), fixed(rows, D), *weight_specs, fixed(1, vector.shape[1])],
        [stream, attended, *weights, vector],
        [ANYWHERE, ANYWHERE, columns_of(rows), columns_of(rows), fixed(rows, D)],
        [
            shape_of(rows, D),
            shape_of(rows, D, dtype=LOW),
            shape_of(rows, width, dtype=LOW),
            shape_of(rows, width, dtype=LOW),
            shape_of(rows, D),
        ],
        [
            pltpu.VMEM((rows, D), jnp.float32),
            pltpu.VMEM((rows, D), LOW),
            pltpu.SemaphoreType.DMA((2,)),
        ],
        "mlp_forward",
        work(2 * rows * D * (D + 2 * width), rows * (16 * D + 4 * width) + 2 * D * (D + 2 * width)),
        rides,
        collective_id,
    )


def mlp_back_kernel(
    grad_ref, slope_ref, residual_ref, mix_ref, up_ref, down_ref, vector_ref,
    low_out, hidden_ref, out_ref, out_low_ref, attended_ref, sums_ref,
    low_ref, second_ref, sem,
):
    rows = grad_ref.shape[0]
    copy = pltpu.make_async_copy(low_ref, low_out, sem)

    @at_first
    def _():
        low_ref[...] = grad_ref[...].astype(LOW)
        copy.start()
        second_ref[...] = jnp.zeros_like(second_ref)

    parts = halves_of(rows)
    active_grad = mul_nt(low_ref[parts[0], :], down_ref[...])
    hidden_sum = 0.0
    for index, half in enumerate(parts):
        following = None
        if index + 1 < len(parts):
            following = mul_nt(low_ref[parts[index + 1], :], down_ref[...])
        hidden_grad = (active_grad * slope_ref[half, :].astype(jnp.float32)).astype(LOW)
        hidden_ref[half, :] = hidden_grad
        hidden_sum = hidden_sum + column_sum(hidden_grad)
        second_ref[half, :] += mul_nt(hidden_grad, up_ref[...])
        active_grad = following
    sums_ref[:, chunk_at(4 * D)] = hidden_sum

    @at_last
    def _():
        gain = vector_ref[:, 2 * D : 3 * D]
        totals = [0.0] * 4
        for half in halves_of(rows):
            grad = grad_ref[half, :]
            value_grad, gain_grad, shift_grad = norm_backward(
                second_ref[half, :], residual_ref[half, :], gain
            )
            total = value_grad + grad
            out_ref[half, :] = total
            total_low = total.astype(LOW)
            out_low_ref[half, :] = total_low
            attended_ref[half, :] = mul_nt(total_low, mix_ref[...]).astype(LOW)
            new = (gain_grad, shift_grad, column_sum(total_low), column_sum(low_ref[half, :]))
            totals = [old + part for old, part in zip(totals, new)]
        sums_ref[:, : 4 * D] = jnp.concatenate(totals, 1)
        copy.wait()


def mlp_backward(grad, slope, residual, up, proj_out, vector):
    rows = grad.shape[0]
    width = up.shape[1]
    whole = fixed(rows, D)
    weight_specs, weights = mlp_specs(up, proj_out)
    return block_call(
        mlp_back_kernel,
        width // D,
        [whole, columns_of(rows), whole, *weight_specs, fixed(1, vector.shape[1])],
        [grad, slope, residual, *weights, vector],
        [ANYWHERE, columns_of(rows), whole, whole, whole, fixed(1, 4 * D + width)],
        [
            shape_of(rows, D, dtype=LOW),
            shape_of(rows, width, dtype=LOW),
            shape_of(rows, D),
            shape_of(rows, D, dtype=LOW),
            shape_of(rows, D, dtype=LOW),
            shape_of(1, 4 * D + width),
        ],
        [
            pltpu.VMEM((rows, D), LOW),
            pltpu.VMEM((rows, D), jnp.float32),
            pltpu.SemaphoreType.DMA,
        ],
        "mlp_backward",
    )


def qkv_back_kernel(grad_ref, residual_ref, stream_ref, weight_ref, vector_ref, out_ref, sums_ref):
    grad = grad_ref[...]
    normed_grad = mul_nt(grad, weight_ref[...])
    value_grad, gain_grad, shift_grad = norm_backward(normed_grad, stream_ref[...], vector_ref[:, :D])
    out_ref[...] = residual_ref[...] + value_grad
    sums = jnp.concatenate([gain_grad, shift_grad, column_sum(grad)], 1)

    @at_first
    def _():
        sums_ref[...] = jnp.zeros_like(sums_ref)

    sums_ref[...] += sums


def qkv_backward(grad, residual_grad, stream, weight, vector):
    rows = stream.shape[0]
    block = 256
    narrow = rows_of(block, D)
    return block_call(
        qkv_back_kernel,
        rows // block,
        [rows_of(block, 3 * D), narrow, narrow, fixed(D, 3 * D), fixed(1, vector.shape[1])],
        [grad, residual_grad, stream, weight, vector],
        [narrow, fixed(1, 5 * D)],
        [shape_of(rows, D), shape_of(1, 5 * D)],
        [],
        "qkv_backward",
    )


def input_grad_kernel(left_ref, right_ref, out_ref, turned_ref):
    @at_first
    def _():
        turned_ref[...] = left_ref[...].T

    out_ref[...] = mul(turned_ref[...], right_ref[...]).astype(LOW)


def input_weight_grad(left, right):
    rows, width = right.shape
    return block_call(
        input_grad_kernel,
        width // D,
        [fixed(rows, D), columns_of(rows)],
        [left, right],
        [columns_of(D)],
        [shape_of(D, width, dtype=LOW)],
        [pltpu.VMEM((D, rows), LOW)],
        "input_weight_grad",
    )[0]


def output_grad_kernel(attended_ref, active_ref, residual_ref, grad_ref, *outs, cut):
    step = pl.program_id(0)

    def store(product):
        base = 0
        for out in outs:
            out[...] = product[:, base : base + out.shape[1]].astype(jnp.bfloat16)
            base += out.shape[1]

    @pl.when(step < cut)
    def _():
        store(mul(attended_ref[...].T, residual_ref[...]))

    @pl.when(step >= cut)
    def _():
        store(mul(active_ref[...].T, grad_ref[...]))


def output_weight_grad(attended, active, residual_low, grad_low, parts):
    rows = attended.shape[0]
    block = 768
    cut = attended.shape[1] // block
    steps = cut + active.shape[1] // block
    return block_call(
        functools.partial(output_grad_kernel, cut=cut),
        steps,
        [
            pl.BlockSpec((rows, block), lambda i: (0, jnp.minimum(i, cut - 1))),
            pl.BlockSpec((rows, block), lambda i: (0, jnp.maximum(i - cut, 0))),
            fixed(rows, D),
            fixed(rows, D),
        ],
        [attended, active, residual_low, grad_low],
        [rows_of(block, part) for part in parts],
        [shape_of(steps * block, part, dtype=LOW) for part in parts],
        [],
        "output_weight_grad",
    )


def embed_back_kernel(pixel_ref, grad_ref, pos_ref, out_ref, table_ref, bias_ref, low_ref):
    @at_first
    def _():
        grad = grad_ref[...]
        low = grad.astype(jnp.bfloat16)
        low_ref[...] = low
        bias_ref[...] = column_sum(low)
        table_ref[...] = jnp.dot(
            pos_ref[...], grad, precision=HIGHEST, preferred_element_type=jnp.float32
        )

    out_ref[...] = mul(pixel_ref[...].T, low_ref[...]).astype(jnp.bfloat16)


def embed_backward(pixels, grad, pos_weights_t):
    rows, depth = pixels.shape
    block = 768
    nodes = pos_weights_t.shape[0]
    return block_call(
        embed_back_kernel,
        depth // block,
        [pl.BlockSpec((rows, block), lambda i: (0, i)), fixed(rows, D), fixed(nodes, rows)],
        [pixels, grad, pos_weights_t],
        [rows_of(block, D), fixed(nodes, D), fixed(1, D)],
        [shape_of(depth, D, dtype=jnp.bfloat16), shape_of(nodes, D), shape_of(1, D)],
        [pltpu.VMEM((rows, D), jnp.bfloat16)],
        "embed_backward",
        None,
    )


def head_kernel(
    stream_ref, seg_col_ref, seg_row_ref, label_ref, weight_ref, vector_ref,
    grad_ref, weight_grad_ref, sums_ref, bias_grad_ref, numbers_ref, *, classes,
):
    padded = weight_ref.shape[1]
    vector = vector_ref[...].astype(LOW).astype(jnp.float32)
    gain, shift = vector[:, D : 2 * D], vector[:, 2 * D : 3 * D]
    slots = lax.broadcasted_iota(jnp.int32, (IMGS, 1), 0)
    member = (seg_row_ref[...] == slots).astype(jnp.float32)
    counts = jnp.sum(member, 1, keepdims=True)
    sizes = jnp.maximum(counts, 1.0)
    unit, inverse = normalized(stream_ref[...])
    final = unit * gain + shift
    pooled = jnp.dot(member, final, precision=HIGHEST, preferred_element_type=jnp.float32)
    pooled = (pooled / sizes).astype(LOW)
    class_at = lax.broadcasted_iota(jnp.int32, (IMGS, padded), 1)
    logits = mul(pooled, weight_ref[...]) + vector[:, 3 * D :]
    logits = jnp.where(class_at < classes, logits, MASKED)
    highest = jnp.max(logits, -1, keepdims=True)
    exponent = jnp.exp(logits - highest)
    totals = jnp.sum(exponent, -1, keepdims=True)
    onehot = class_at == label_ref[...]
    picked = jnp.sum(jnp.where(onehot, logits, 0.0), 1, keepdims=True)
    loss = jnp.sum(counts * (highest + jnp.log(totals) - picked), 0, keepdims=True)
    numbers_ref[...] = jnp.concatenate([loss, jnp.sum(counts, 0, keepdims=True)], 1)
    logits_grad = ((exponent / totals - onehot.astype(jnp.float32)) * counts).astype(LOW)
    bias_grad_ref[...] = column_sum(logits_grad)
    weight_grad_ref[...] = lax.dot_general(
        pooled, logits_grad, (((0,), (0,)), ((), ())), preferred_element_type=jnp.float32
    ).astype(LOW)
    pooled_grad = mul_nt(logits_grad, weight_ref[...]) / sizes
    own = (seg_col_ref[...] == lax.broadcasted_iota(jnp.int32, (1, IMGS), 1)).astype(jnp.float32)
    final_grad = jnp.dot(own, pooled_grad, precision=HIGHEST, preferred_element_type=jnp.float32)
    inner = final_grad * gain
    mean_inner = jnp.mean(inner, -1, keepdims=True)
    mean_cross = jnp.mean(inner * unit, -1, keepdims=True)
    grad_ref[...] = inverse * (inner - mean_inner - unit * mean_cross)
    sums_ref[...] = jnp.concatenate([column_sum(final_grad * unit), column_sum(final_grad)], 1)


def head(stream, segment, labels, weight, global_vector, classes):
    rows = stream.shape[0]
    padded = weight.shape[1]
    vector = jnp.pad(global_vector, (0, padded - classes))[None, :]
    return pl.pallas_call(
        functools.partial(head_kernel, classes=classes),
        out_shape=[
            shape_of(rows, D),
            shape_of(D, padded, dtype=LOW),
            shape_of(1, 2 * D),
            shape_of(1, padded),
            shape_of(1, 2),
        ],
        compiler_params=pltpu.CompilerParams(vmem_limit_bytes=VMEM_LIMIT),
        cost_estimate=NO_COST,
        name="head",
    )(stream, segment[:, None], segment[None, :], labels.reshape(IMGS, 1), weight, vector)


def adam_update(gradient, moment, square, weight, factor, learn_rate):
    clipped = gradient * factor
    moment = BETA_ONE * moment + (1.0 - BETA_ONE) * clipped
    square = BETA_TWO * square + (1.0 - BETA_TWO) * clipped * clipped
    fixed_one = 1.0 - BETA_ONE**STEP
    fixed_two = 1.0 - BETA_TWO**STEP
    step_dir = (
        moment / fixed_one / (jnp.sqrt(square / fixed_two) + ADAM_EPS) + WEIGHT_DECAY * weight
    )
    return (moment, square, weight - learn_rate * step_dir)


def body(
    pixels,
    segment,
    patch_size,
    labels,
    patch_kernel,
    head_weight,
    input_proj,
    output_proj,
    layer_vector,
    position_table,
    global_vector,
    patch_moment,
    head_moment,
    input_moment,
    output_moment,
    layer_moment,
    position_moment,
    global_moment,
    patch_square,
    head_square,
    input_square,
    output_square,
    layer_square,
    position_square,
    global_square,
):
    owners = lax.axis_size("fsdp")
    nodes = position_table.shape[0]
    vector_size = layer_vector.size
    stream, pos_weights_t, vectors, qkv_weight, rides, rest_shards = begin(
        pixels,
        segment,
        patch_size,
        patch_kernel,
        layer_vector,
        input_proj,
        output_proj,
        head_weight,
        position_table,
        global_vector,
    )
    qkv_one, up_one, head_full = (
        lax.all_gather(shard, "fsdp", axis=0, tiled=True) for shard in rest_shards
    )
    saved_layers = []
    for index in range(LAYERS):
        vector = vectors[index]
        normed, qkv_rows = qkv_forward(stream, qkv_weight, vector)
        if index == 0:
            attended, expo, inverse, up, output = attention_forward(qkv_rows, segment, rides[:2], 4)
        else:
            attended, expo, inverse, output = attention_forward(qkv_rows, segment, [output_ride], 5)
            up = up_one
        residual, normed_second, active, slope, following, *fetched = mlp_forward(
            stream, attended, up, output, vector, () if index else rides[2:], 7
        )
        saved_layers.append(
            (
                (qkv_weight, up, output, vector),
                (stream, normed, qkv_rows, attended, expo, inverse),
                (residual, normed_second, active, slope),
            )
        )
        stream = following
        if fetched:
            qkv_weight, (output_ride,) = qkv_one, fetched
    stream_grad, head_grad, final_sums, head_bias_grad, numbers = head(
        stream, segment, labels, head_full, global_vector, head_weight.shape[1]
    )
    vector_grads = [None] * LAYERS
    early_parts, late_parts = [], []
    for index in reversed(range(LAYERS)):
        (qkv_weight, up, output, vector), first, second = saved_layers[index]
        entering, normed, qkv_rows, attended, expo, inverse = first
        residual, normed_second, active, slope = second
        grad_low, hidden_grad, residual_grad, residual_low, attended_grad, mlp_sums = mlp_backward(
            stream_grad, slope, residual, up, output, vector
        )
        output_grads = output_weight_grad(
            attended, active, residual_low, grad_low, (D // 2,) * 2 if index else (D,)
        )
        attended_grad, *output_grads = lax.optimization_barrier((attended_grad, *output_grads))
        up_grad = input_weight_grad(normed_second, hidden_grad)
        output_parts = [scatter(by_owner(grad)) for grad in output_grads]
        if index:
            early_parts.extend(output_parts)
            beside = [SumRide(by_owner(head_grad), False)]
        else:
            (last_part,) = output_parts
            beside = [ShareRide(jnp.concatenate(early_parts, 1)), SumRide(by_owner(up_grad), True)]
        qkv_grad, *beside_sums = attention_backward(
            qkv_rows, expo, inverse, attended, attended_grad, beside, 6 if index else 8
        )
        stream_grad, qkv_sums = qkv_backward(qkv_grad, residual_grad, entering, qkv_weight, vector)
        qkv_weight_grad = input_weight_grad(normed, qkv_grad)
        if index:
            (head_sum,) = beside_sums
            stream_grad, qkv_weight_grad, up_grad = lax.optimization_barrier(
                (stream_grad, qkv_weight_grad, up_grad)
            )
            late_parts.extend(scatter(by_owner(grad)) for grad in (qkv_weight_grad, up_grad))
        else:
            output_one_sum, up_zero_sum = beside_sums
        vector_grads[index] = jnp.concatenate(
            [
                qkv_sums[0, : 2 * D],
                mlp_sums[0, : 2 * D],
                qkv_sums[0, 2 * D :],
                mlp_sums[0, 2 * D :],
            ]
        )
    kernel_grad, position_grad, bias_grad = embed_backward(pixels, stream_grad, pos_weights_t)
    position_grad = position_grad[:nodes]
    vector_part = jnp.stack(vector_grads).reshape(LAYERS, owners, -1)
    vector_part = jnp.swapaxes(vector_part, 0, 1).reshape(owners, vector_size)
    vector_rows = -(-vector_size // LANES)
    vector_part = jnp.pad(vector_part, ((0, 0), (0, vector_rows * LANES - vector_size)))
    rest = jnp.concatenate(
        [
            position_grad.reshape(-1),
            bias_grad[0],
            final_sums[0],
            head_bias_grad[0, :CLS],
            numbers[0],
        ]
    )
    rest_rows = -(-rest.shape[0] // (owners * LANES))
    rest_part = jnp.pad(rest, (0, rest_rows * owners * LANES - rest.shape[0]))
    small = jnp.concatenate([vector_part, rest_part.reshape(owners, -1)], 1)
    used = vector_rows + rest_rows
    block_rows = (used // 64 + 1) * 64
    small = jnp.pad(small.reshape(owners, used, LANES), ((0, 0), (0, block_rows - used), (0, 0)))
    qkv_zero_sum, kernel_sum, *input_one_sums = reduce_all(
        [by_owner(qkv_weight_grad), by_owner(kernel_grad)], late_parts, 2
    )
    output_zero_sum, small_share, small_full = finish_all(
        [head_sum, output_one_sum, up_zero_sum, qkv_zero_sum, kernel_sum, *input_one_sums],
        [last_part],
        small,
        3,
    )
    rest_sum = small_full[:, vector_rows:used].reshape(-1)
    position_sum = rest_sum[: position_grad.size].reshape(position_grad.shape)
    global_sum = rest_sum[position_grad.size :][: global_vector.shape[0]]
    loss_sum = rest_sum[rest.shape[0] - 2]
    token_total = rest_sum[rest.shape[0] - 1]
    kernel_sum = kernel_sum.astype(jnp.float32)
    head_sum = head_sum[:, :CLS].astype(jnp.float32)
    input_sum = jnp.stack(
        [jnp.concatenate(pair, 1) for pair in ((qkv_zero_sum, up_zero_sum), input_one_sums)]
    ).astype(jnp.float32)
    output_sum = jnp.stack([output_zero_sum, output_one_sum]).astype(
        jnp.float32
    )
    vector_sum = small_share[:vector_rows].reshape(-1)[:vector_size].reshape(layer_vector.shape)
    grad_norm = (
        jnp.sqrt(
            jnp.sum(small_full[:, -1])
            + jnp.sum(jnp.square(small_full[:, :vector_rows]))
            + jnp.sum(position_sum * position_sum)
            + jnp.sum(global_sum * global_sum)
        )
        / token_total
    )
    factor = jnp.minimum(1.0, CLIP_NORM / grad_norm) / token_total
    patch_next = adam_update(
        kernel_sum, patch_moment, patch_square, patch_kernel, factor, LEARN_RATE
    )
    head_next = adam_update(head_sum, head_moment, head_square, head_weight, factor, LEARN_RATE)
    input_next = adam_update(input_sum, input_moment, input_square, input_proj, factor, LEARN_RATE)
    output_next = adam_update(
        output_sum, output_moment, output_square, output_proj, factor, LEARN_RATE
    )
    layer_next = adam_update(
        vector_sum, layer_moment, layer_square, layer_vector, factor, VECTOR_RATE
    )
    position_next = adam_update(
        position_sum, position_moment, position_square, position_table, factor, LEARN_RATE
    )
    global_next = adam_update(
        global_sum, global_moment, global_square, global_vector, factor, VECTOR_RATE
    )
    return (
        loss_sum,
        token_total,
        grad_norm,
        patch_next[0],
        head_next[0],
        input_next[0],
        output_next[0],
        layer_next[0],
        position_next[0],
        global_next[0],
        patch_next[1],
        head_next[1],
        input_next[1],
        output_next[1],
        layer_next[1],
        position_next[1],
        global_next[1],
        patch_next[2],
        head_next[2],
        input_next[2],
        output_next[2],
        layer_next[2],
        position_next[2],
        global_next[2],
    )


def solution(mesh):
    in_specs = (
        P(("dp", "fsdp"), None),
        P(("dp", "fsdp")),
        P(("dp", "fsdp"), None),
        P(("dp", "fsdp"), None),
        P("fsdp", None),
        P("fsdp", None),
        P(None, "fsdp", None),
        P(None, "fsdp", None),
        P(None, "fsdp"),
        P(),
        P(),
        P("fsdp", None),
        P("fsdp", None),
        P(None, "fsdp", None),
        P(None, "fsdp", None),
        P(None, "fsdp"),
        P(),
        P(),
        P("fsdp", None),
        P("fsdp", None),
        P(None, "fsdp", None),
        P(None, "fsdp", None),
        P(None, "fsdp"),
        P(),
        P(),
    )
    out_specs = (
        P(),
        P(),
        P(),
        P("fsdp", None),
        P("fsdp", None),
        P(None, "fsdp", None),
        P(None, "fsdp", None),
        P(None, "fsdp"),
        P(),
        P(),
        P("fsdp", None),
        P("fsdp", None),
        P(None, "fsdp", None),
        P(None, "fsdp", None),
        P(None, "fsdp"),
        P(),
        P(),
        P("fsdp", None),
        P("fsdp", None),
        P(None, "fsdp", None),
        P(None, "fsdp", None),
        P(None, "fsdp"),
        P(),
        P(),
    )
    return jax.shard_map(body, mesh=mesh, in_specs=in_specs, out_specs=out_specs, check_vma=False)
```

```python
import functools

import jax
import jax.numpy as jnp
from jax import lax
from jax.experimental import pallas as pl
from jax.experimental.pallas import tpu as pltpu
from jax.sharding import PartitionSpec as P

D = 768
HEADS = 12
HD = 64
CLS = 1000
GRID = 7
IMG = 240
IMGS = 8
LAYERS = 2
STEP = 3


NORM_EPS = 1e-06
CLIP_NORM = 0.01
LEARN_RATE = 0.05
VECTOR_RATE = 0.25
BETA_ONE = 0.5
BETA_TWO = 0.5
ADAM_EPS = 1e-08
WEIGHT_DECAY = 0.05
HIGHEST = lax.Precision.HIGHEST

PAIR = 2 * HD
MASKED = -1e30
MIB = 1024 * 1024
VMEM_LIMIT = 56 * MIB
MESH = pl.DeviceIdType.MESH
LANES = 128
LOW = jnp.bfloat16
ANYWHERE = pl.BlockSpec(memory_space=pl.ANY)
NO_COST = pl.CostEstimate(flops=0, bytes_accessed=0, transcendentals=0)
ROOT = 0.7978845608028654
CUBE = 0.044715
NT = (((1,), (1,)), ((), ()))


def layer_norm(values, gain, shift):
    center = values - jnp.mean(values, -1, keepdims=True)
    spread = jnp.mean(center * center, -1, keepdims=True)
    return center * lax.rsqrt(spread + NORM_EPS) * gain + shift


def rounded(values):
    return lax.optimization_barrier(values.astype(jnp.bfloat16)).astype(jnp.float32)


def matmul(left, right):
    return jnp.dot(left, right, preferred_element_type=jnp.float32)


def padded_rows(flat, multiple):
    extra = -flat.shape[0] % (multiple * LANES)
    return jnp.pad(flat, (0, extra)).reshape(-1, LANES)


def row_layout(seg_row, patch_row):
    row_count = seg_row.shape[0]
    slots = jnp.arange(IMGS, dtype=jnp.int32)
    member = seg_row[:, None] == slots[None, :]
    counts = jnp.sum(member.astype(jnp.int32), 0, dtype=jnp.int32)
    starts = jnp.cumsum(counts, dtype=jnp.int32) - counts
    inside = jnp.any(member, 1)
    offset = jnp.arange(row_count, dtype=jnp.int32) - jnp.sum(
        jnp.where(member, starts[None, :], 0), 1, dtype=jnp.int32
    )
    offset = jnp.where(inside, offset, 0)
    patch_tok = jnp.sum(jnp.where(member, patch_row[None, :], 0), 1, dtype=jnp.int32) + jnp.where(
        inside, 0, IMG
    )
    side = IMG // patch_tok
    nodes = jnp.arange(GRID, dtype=jnp.int32).astype(jnp.float32)

    def hat(coord):
        place = ((2 * coord + 1) * GRID).astype(jnp.float32) / (2 * side).astype(jnp.float32) - 0.5
        place = jnp.clip(place, 0.0, GRID - 1.0)
        return jnp.maximum(1.0 - jnp.abs(place[:, None] - nodes[None, :]), 0.0)

    weights = (hat(offset // side)[:, :, None] * hat(offset % side)[:, None, :]).reshape(
        row_count, GRID * GRID
    )
    return (weights, member.astype(jnp.float32), counts.astype(jnp.float32))


TURNS = (1, 2, 3)


def place():
    slot = lax.axis_index("fsdp")
    return lax.axis_index("dp"), lax.div(slot, 2), lax.rem(slot, 2)


def partner(index, turn):
    if turn == 0:
        return index
    if turn == 1:
        return index + 1 - 2 * lax.rem(index, 2)
    if turn == 2:
        return lax.rem(index + 2, 4)
    return 3 - index


def greet():
    group, level, core = place()
    barrier = pltpu.get_barrier_semaphore()
    peers = [(group, 2 * level + 1 - core)]
    for turn in TURNS:
        peers.append((group, 2 * partner(level, turn) + core))
        peers.append((partner(group, turn), 2 * level + core))
    for peer in peers:
        pl.semaphore_signal(barrier, inc=1, device_id=peer, device_id_type=MESH)
    pl.semaphore_wait(barrier, len(peers))


def quarter_shape(rows, columns):
    if columns % (2 * LANES) == 0:
        return rows // 2, columns // 2
    return rows // 4, columns


def quarter(index, rows, columns):
    high, wide = quarter_shape(rows, columns)
    if wide == columns:
        return pl.ds(pl.multiple_of(index * high, high), high), pl.ds(0, columns)
    return (
        pl.ds(pl.multiple_of(lax.div(index, 2) * high, high), high),
        pl.ds(pl.multiple_of(lax.rem(index, 2) * wide, wide), wide),
    )


def remote(source, target, send, receive, device):
    return pltpu.make_async_remote_copy(
        src_ref=source,
        dst_ref=target,
        send_sem=send,
        recv_sem=receive,
        device_id=device,
        device_id_type=MESH,
    )


GATHER_SEMS = 39


def relay_rows(part, rows):
    cut = -(-rows // 32) * 16
    return (0, cut) if part == 0 else (cut, rows - cut)


class Relay:
    def region(self, turn, index):
        _, level, core = place()
        block = self.out.at[2 * partner(level, turn) + core]
        return block.at[quarter(index, *self.shard.shape)]

    def group_copy(self, turn, other):
        group, level, core = place()
        index = self.group_at + 2 * (turn - 1) + other - 1
        peer = (partner(group, other), 2 * level + core)
        target = self.region(turn, group)
        source = self.quarter_source(turn, target)
        return remote(source, target, self.sems.at[index], self.sems.at[index + 6], peer)

    def relay_copy(self, turn, part):
        group, level, core = place()
        first, count = relay_rows(part, quarter_shape(*self.shard.shape)[0])
        block = self.region(turn, partner(group, 1 + part)).at[pl.ds(first, count)]
        index = self.relay_at + 2 * (turn - 1) + part
        peer = (partner(group, 2 - part), 2 * level + core)
        return remote(block, block, self.sems.at[index], self.sems.at[index + 6], peer)

    def relay(self):
        for turn in TURNS:
            for part in range(2):
                self.group_copy(turn, 1 + part).wait_recv()
                self.relay_copy(turn, part).start()

    def wait_quarters(self, turn):
        for part in range(2):
            self.relay_copy(turn, part).wait_recv()

    def wait_passed(self):
        for turn in TURNS:
            for part in range(2):
                self.group_copy(turn, 1 + part).wait_send()
                self.relay_copy(turn, part).wait_send()


class Gather(Relay):
    group_at, relay_at = 7, 19

    def __init__(self, shard, out, sems, split, in_place=False):
        self.shard, self.out, self.sems, self.split = shard, out, sems, split
        self.in_place = in_place
        self.rows, self.columns = shard.shape

    def quarter_source(self, turn, target):
        return target

    def level_copy(self, turn):
        group, level, core = place()
        block = self.out.at[2 * level + core]
        source = self.shard
        if self.split:
            part = quarter(group, self.rows, self.columns)
            source, block = source.at[part], block.at[part]
        peer = (group, 2 * partner(level, turn) + core)
        return remote(source, block, self.sems.at[turn], self.sems.at[3 + turn], peer)

    def core_copy(self, turn):
        group, level, core = place()
        slot = 2 * partner(level, turn) + core
        source = self.shard if turn == 0 else self.out.at[slot]
        peer = (group, 2 * level + 1 - core)
        return remote(source, self.out.at[slot], self.sems.at[31 + turn], self.sems.at[35 + turn], peer)

    def own_copy(self):
        _, level, core = place()
        return pltpu.make_async_copy(self.shard, self.out.at[2 * level + core], self.sems.at[0])

    def first(self):
        for turn in TURNS:
            self.level_copy(turn).start()
        self.core_copy(0).start()
        if not self.in_place:
            self.own_copy().start()

    def second(self):
        for turn in TURNS:
            self.level_copy(turn).wait_recv()
            if self.split:
                for other in (1, 2):
                    self.group_copy(turn, other).start()
            else:
                self.core_copy(turn).start()

    def third(self, use=None):
        for turn in TURNS if self.split else ():
            self.wait_quarters(turn)
            self.core_copy(turn).start()
            if use is not None:
                use(turn, True)

    def fourth(self, use=None):
        for turn in TURNS if use is not None else (0, *TURNS):
            self.core_copy(turn).wait_recv()
            if use is not None:
                use(turn, False)
        for turn in TURNS:
            self.level_copy(turn).wait_send()
        if self.split:
            self.wait_passed()
        for turn in (0, *TURNS):
            self.core_copy(turn).wait_send()
        if not self.in_place:
            self.own_copy().wait()


class LevelGather:
    def __init__(self, shard, out, sems):
        self.shard, self.out, self.sems = shard, out, sems

    def level_copy(self, turn):
        group, level, core = place()
        return remote(
            self.shard.at[quarter(group, *self.shard.shape)],
            self.out.at[level],
            self.sems.at[turn],
            self.sems.at[3 + turn],
            (group, 2 * partner(level, turn) + core),
        )

    def first(self):
        for turn in TURNS:
            self.level_copy(turn).start()

    def second(self):
        pass

    def third(self):
        pass

    def fourth(self):
        for turn in TURNS:
            self.level_copy(turn).wait_recv()
            self.level_copy(turn).wait_send()

    def store(self):
        _, level, _ = place()
        self.out[level] = jnp.zeros(self.out.shape[1:], self.out.dtype)
        self.target[...] = self.out[...]


GROUP_GATHER_SEMS = 36


class GroupGather(Relay):
    group_at, relay_at = 4, 16

    def __init__(self, shard, quarters, out, sems):
        self.shard, self.quarters, self.out, self.sems = shard, quarters, out, sems

    def quarter_source(self, turn, target):
        _, level, _ = place()
        return self.quarters.at[partner(level, turn)]

    def own_copy(self, turn):
        group, level, core = place()
        if turn == 0:
            source, target = self.shard, self.out.at[2 * level + core]
        else:
            source, target = self.quarters.at[partner(level, turn)], self.region(turn, group)
        return pltpu.make_async_copy(source, target, self.sems.at[turn])

    def core_copy(self, turn):
        group, level, core = place()
        slot = 2 * partner(level, turn) + core
        source = self.shard if turn == 0 else self.out.at[slot]
        peer = (group, 2 * level + 1 - core)
        return remote(source, self.out.at[slot], self.sems.at[28 + turn], self.sems.at[32 + turn], peer)

    def first(self):
        for turn in TURNS:
            for other in (1, 2):
                self.group_copy(turn, other).start()
        for turn in (0, *TURNS):
            self.own_copy(turn).start()
        self.core_copy(0).start()

    def third(self):
        for turn in TURNS:
            self.wait_quarters(turn)
            self.own_copy(turn).wait()
            self.core_copy(turn).start()

    def fourth(self):
        for turn in (0, *TURNS):
            self.core_copy(turn).wait_recv()
            self.core_copy(turn).wait_send()
        self.wait_passed()
        self.own_copy(0).wait()

    def store(self):
        copy = pltpu.make_async_copy(self.out, self.target, self.sems.at[0])
        copy.start()
        copy.wait()


class LevelRide:
    def __init__(self, shard):
        self.operands = [shard]
        self.in_specs = [fixed(*shard.shape)]
        shape = (4, *quarter_shape(*shard.shape))
        self.out_specs = [fixed(*shape)]
        self.out_shapes = [jax.ShapeDtypeStruct(shape, shard.dtype)]
        self.scratch = [pltpu.VMEM(shape, shard.dtype), pltpu.SemaphoreType.DMA((7,))]

    def job(self, sources, targets, scratch):
        job = LevelGather(sources[0], *scratch)
        job.target = targets[0]
        return job

    def before(self, steps):
        return {0: ("first",)}

    after = ("fourth", "store")

    def result(self, outs):
        return GatherRide(self.operands[0], outs[0])

    def plain(self):
        return GatherRide(self.operands[0], self.operands[0])


class GatherRide:
    def __init__(self, shard, quarters):
        owners = lax.axis_size("fsdp")
        full = (owners, *shard.shape)
        self.operands = [shard, quarters]
        self.in_specs = [fixed(*shard.shape), fixed(*quarters.shape)]
        self.out_specs = [ANYWHERE]
        self.out_shapes = [jax.ShapeDtypeStruct(full, shard.dtype)]
        self.scratch = [
            pltpu.VMEM(full, shard.dtype),
            pltpu.SemaphoreType.DMA((GROUP_GATHER_SEMS,)),
        ]

    def job(self, sources, targets, scratch):
        job = GroupGather(*sources, *scratch)
        job.target = targets[0]
        return job

    def before(self, steps):
        return {0: ("first",), steps // 2: ("relay",), steps - 1: ("third",)}

    after = ("fourth", "store")

    def result(self, outs):
        return outs[0].reshape(-1, outs[0].shape[2])

    def plain(self):
        return lax.all_gather(self.operands[0], "fsdp", axis=0, tiled=True)


class ShareRide:
    def __init__(self, share):
        self.operands = [share]
        self.in_specs = [ANYWHERE]
        self.out_specs = [fixed(*share.shape)]
        self.out_shapes = [jax.ShapeDtypeStruct(share.shape, share.dtype)]
        self.scratch = [
            pltpu.VMEM(share.shape, share.dtype),
            *share_scratch(share),
            pltpu.SemaphoreType.DMA((GROUP_SEMS,)),
        ]

    def job(self, sources, targets, scratch):
        job = GroupReduce(sources[0], scratch[0], scratch[1:3], scratch[3])
        job.target = targets[0]
        return job

    def before(self, steps):
        return {0: ("first", "second"), max(1, steps // 2): ("third",)}

    after = ("fifth", "sixth", "store")

    def result(self, outs):
        return outs[0]

    def plain(self):
        return lax.psum(self.operands[0], "dp")


class SumRide:
    def __init__(self, grad, large):
        block = grad.shape[1:]
        self.large = large
        self.operands = [grad]
        self.in_specs = [ANYWHERE]
        self.out_specs = [fixed(*block)]
        self.out_shapes = [jax.ShapeDtypeStruct(block, grad.dtype)]
        buffers = stepped_scratch(grad) if large else whole_scratch(grad)
        sems = WHOLE_SEMS if large else REDUCE_SEMS
        self.scratch = [pltpu.VMEM(block, grad.dtype), *buffers, pltpu.SemaphoreType.DMA((sems,))]

    def job(self, sources, targets, scratch):
        job = (Whole if self.large else Reduce)(sources[0], scratch[0], scratch[1:-1], scratch[-1])
        job.target = targets[0]
        return job

    def before(self, steps):
        if self.large:
            return {0: ("first",), 1: ("second",), steps - 2: ("between",), steps - 1: ("third",)}
        return {0: ("first",), 1: ("second",), steps // 2: ("third",), steps - 1: ("fourth",)}

    @property
    def after(self):
        return (("fourth",) if self.large else ()) + ("fifth", "sixth", "store")

    def result(self, outs):
        return outs[0]

    def plain(self):
        return lax.psum(scatter(self.operands[0]), "dp")


def riding(body, counts, rides, steps):
    def kernel(*refs):
        refs = list(refs)

        def pop(count):
            taken = refs[:count]
            del refs[:count]
            return taken

        own = pop(counts[0])
        sources = [pop(len(ride.operands)) for ride in rides]
        own += pop(counts[1])
        targets = [pop(len(ride.out_shapes)) for ride in rides]
        own += pop(counts[2])
        jobs = [
            ride.job(source, target, pop(len(ride.scratch)))
            for ride, source, target in zip(rides, sources, targets)
        ]
        for step in range(steps):
            planned = [
                (job, stages)
                for ride, job in zip(rides, jobs)
                for at, stages in ride.before(steps).items()
                if at == step
            ]
            if planned:

                @pl.when(pl.program_id(0) == step)
                def _(planned=planned, step=step):
                    if step == 0:
                        greet()
                    for job, stages in planned:
                        run_stages([job], stages)

        body(*own)

        @pl.when(pl.program_id(0) == steps - 1)
        def _():
            for ride, job in zip(rides, jobs):
                run_stages([job], ride.after)

    return kernel


def block_call(
    body, grid, in_specs, operands, out_specs, out_shape, scratch, name,
    cost=None, rides=(), collective_id=None,
):
    plain = []
    if rides and not with_kernels():
        plain, rides = [ride.plain() for ride in rides], ()
    transfer = {}
    kernel = body
    if rides:
        transfer = {"collective_id": collective_id, "has_side_effects": True}
        kernel = riding(body, (len(operands), len(out_shape), len(scratch)), rides, grid)
    count = len(out_shape)
    for ride in rides:
        operands = [*operands, *ride.operands]
        in_specs = [*in_specs, *ride.in_specs]
        out_specs, out_shape = [*out_specs, *ride.out_specs], [*out_shape, *ride.out_shapes]
        scratch = [*scratch, *ride.scratch]
    outs = pl.pallas_call(
        kernel,
        grid=(grid,),
        in_specs=in_specs,
        out_specs=out_specs,
        out_shape=out_shape,
        scratch_shapes=scratch,
        compiler_params=pltpu.CompilerParams(vmem_limit_bytes=VMEM_LIMIT, **transfer),
        cost_estimate=cost or NO_COST,
        name=name,
    )(*operands)
    brought, outs = list(outs[count:]), list(outs[:count])
    for ride in rides:
        plain.append(ride.result(brought[: len(ride.out_shapes)]))
        brought = brought[len(ride.out_shapes) :]
    return outs + plain


def work(flops, size):
    return pl.CostEstimate(flops=flops, bytes_accessed=size, transcendentals=0)


def position_weights(seg_col, patch_row, nodes):
    rows = seg_col.shape[0]
    slot = lax.broadcasted_iota(jnp.int32, (rows, IMGS), 1)
    member = seg_col == slot
    counts = jnp.sum(member.astype(jnp.float32), 0, keepdims=True)
    start = jnp.sum(jnp.where(slot < seg_col, counts, 0.0), 1, keepdims=True)
    token = lax.broadcasted_iota(jnp.int32, (rows, 1), 0).astype(jnp.float32)
    inside = seg_col < IMGS
    offset = jnp.where(inside, token - start, 0.0)
    patch = jnp.sum(jnp.where(member, patch_row.astype(jnp.float32), 0.0), 1, keepdims=True)
    side = jnp.where(inside, jnp.floor(IMG / jnp.where(inside, patch, 1.0) + 0.5), 1.0)
    line = jnp.floor((offset + 0.5) / side)
    column = offset - line * side

    def spot(coord):
        return jnp.clip((2.0 * coord + 1.0) * GRID / (2.0 * side) - 0.5, 0.0, GRID - 1.0)

    node = lax.broadcasted_iota(jnp.int32, (rows, LANES), 1).astype(jnp.float32)
    across = jnp.floor((node + 0.5) / GRID)
    along = node - across * GRID
    weights = jnp.maximum(1.0 - jnp.abs(spot(line) - across), 0.0)
    weights = weights * jnp.maximum(1.0 - jnp.abs(spot(column) - along), 0.0)
    return jnp.where(node < nodes, weights, 0.0)


def first_kernel(*refs, spots):
    kernel, vectors, inputs, outputs, head, pixels, seg_col, patch_row, table, biases = refs[:10]
    stream, pos_t, vector_zero, vector_one = refs[10:14]
    qkv_full, up_level, output_level = refs[14:17]
    up_zero, output_zero, qkv_one, up_one, output_one, head_low = refs[17:23]
    wide_kernel, wide_inputs, wide_outputs, wide_head, pixel_rows, table_low = refs[23:29]
    kernel_full, qkv_zero, vectors_full, qkv_landing, up_landing, output_landing = refs[29:35]
    load_sems, sems = refs[35:]
    _, level, core = place()
    mine = 2 * level + core
    pairs = [
        (kernel, wide_kernel),
        (inputs.at[0], wide_inputs.at[0]),
        (pixels, pixel_rows),
        (inputs.at[1], wide_inputs.at[1]),
        (outputs.at[0], wide_outputs.at[0]),
        (outputs.at[1], wide_outputs.at[1]),
        (head, wide_head),
    ]
    copies = [
        pltpu.make_async_copy(source, target, load_sems.at[index])
        for index, (source, target) in enumerate(pairs)
    ]
    for copy in copies:
        copy.start()
    patch_job = Gather(kernel_full.at[mine], kernel_full, sems.at[0], True, in_place=True)
    vector_job = Gather(vectors, vectors_full, sems.at[1], False)
    qkv_job = Gather(qkv_zero, qkv_landing, sems.at[2], True)
    up_job = LevelGather(up_zero, up_landing, sems.at[3])
    up_job.target = up_level
    output_job = LevelGather(output_zero, output_landing, sems.at[4])
    output_job.target = output_level
    copies[0].wait()
    kernel_full[mine] = wide_kernel[...].astype(LOW)
    greet()
    patch_job.first()
    vector_job.first()
    copies[1].wait()
    qkv_zero[...] = wide_inputs[0, :, : 3 * D].astype(LOW)
    qkv_job.first()
    up_zero[...] = wide_inputs[0, :, 3 * D :].astype(LOW)
    up_job.first()
    copies[4].wait()
    output_zero[...] = wide_outputs[0].astype(LOW)
    output_job.first()

    weights = position_weights(seg_col[...], patch_row[...], table.shape[0])
    pos_t[...] = weights.T[: pos_t.shape[0], :]
    table_low[...] = jnp.zeros_like(table_low)
    table_low[: table.shape[0], :] = table[...].astype(LOW).astype(jnp.float32)
    bias = biases[:, :D].astype(LOW).astype(jnp.float32)
    stream[...] = bias + jnp.dot(
        weights, table_low[...], precision=HIGHEST, preferred_element_type=jnp.float32
    )
    copies[2].wait()
    depth = wide_kernel.shape[0]

    def add_block(slot):
        columns = pl.ds(pl.multiple_of(slot * depth, depth), depth)

        def add(step, carry):
            rows = pl.ds(pl.multiple_of(step * 256, 256), 256)
            stream[rows, :] += mul(pixel_rows[rows, columns], kernel_full[slot])
            return carry

        lax.fori_loop(0, stream.shape[0] // 256, add, 0)

    def use(turn, own_core):
        add_block(2 * partner(level, turn) + (core if own_core else 1 - core))

    add_block(mine)
    patch_job.second()
    vector_job.second()
    qkv_job.second()
    patch_job.core_copy(0).wait_recv()
    use(0, False)
    copies[3].wait()
    qkv_one[...] = wide_inputs[1, :, : 3 * D].astype(LOW)
    up_one[...] = wide_inputs[1, :, 3 * D :].astype(LOW)
    copies[5].wait()
    output_one[...] = wide_outputs[1].astype(LOW)
    copies[6].wait()
    head_low[...] = jnp.zeros_like(head_low)
    head_low[:, : head.shape[1]] = wide_head[...].astype(LOW)
    patch_job.relay()
    qkv_job.relay()
    patch_job.third(use)
    qkv_job.third()
    patch_job.fourth(use)
    vector_job.third()
    vector_job.fourth()
    blocks = [vectors_full[slot].astype(jnp.float32) for slot in range(vectors_full.shape[0])]
    span = vectors.shape[0] // LAYERS
    for layer, out in enumerate((vector_zero, vector_one)):
        for row in range(out.shape[1] // LANES):
            parts = [
                block[layer * span + row - spot : layer * span + row - spot + 1, :]
                for block, spot in zip(blocks, spots)
                if 0 <= row - spot < span
            ]
            out[:, row * LANES : (row + 1) * LANES] = sum(parts)
    qkv_job.fourth()
    copy = pltpu.make_async_copy(qkv_landing, qkv_full, load_sems.at[0])
    copy.start()
    run_stages([up_job, output_job], ("fourth", "store"))
    copy.wait()


def padded_vectors(shard):
    layers, width = shard.shape
    owners = lax.axis_size("fsdp")
    spots = [owner * width // LANES for owner in range(owners)]
    span = max(-(-(owner + 1) * width // LANES) - spot for owner, spot in enumerate(spots))
    span += -span % 16
    shift = lax.rem(lax.axis_index("fsdp") * width, LANES)
    padded = jnp.zeros((layers, span * LANES), LOW)
    padded = lax.dynamic_update_slice(padded, shard.astype(LOW), (0, shift))
    return padded.reshape(layers * span, LANES), spots


def begin(
    pixels, segment, patch_size, patch_kernel, layer_vector, input_proj, output_proj, head_weight,
    position_table, global_vector,
):
    classes = head_weight.shape[1] + -head_weight.shape[1] % LANES
    nodes = position_table.shape[0] + -position_table.shape[0] % 64
    if not with_kernels():
        inputs = [
            (input_proj[index, :, : 3 * D].astype(LOW), input_proj[index, :, 3 * D :].astype(LOW))
            for index in range(LAYERS)
        ]
        outputs = [output_proj[index].astype(LOW) for index in range(LAYERS)]
        gather = lambda shard, axis: lax.all_gather(shard, "fsdp", axis=axis, tiled=True)
        weights, _, _ = row_layout(segment, patch_size[0])
        weights = jnp.pad(weights, ((0, 0), (0, nodes - weights.shape[1])))
        table = jnp.pad(rounded(position_table), ((0, nodes - position_table.shape[0]), (0, 0)))
        bias = rounded(global_vector)[None, :D]
        stream = embed(pixels, gather(patch_kernel.astype(LOW), 0), weights, table, bias)
        vectors = gather(layer_vector.astype(LOW), 1).astype(jnp.float32)
        head = jnp.pad(head_weight.astype(LOW), ((0, 0), (0, classes - head_weight.shape[1])))
        return (
            stream,
            weights.T,
            [vectors[index : index + 1] for index in range(LAYERS)],
            gather(inputs[0][0], 0),
            [*[GatherRide(shard, shard) for shard in (inputs[0][1], outputs[0])], LevelRide(outputs[1])],
            [*inputs[1], head],
        )
    rows = pixels.shape[0]
    owners = lax.axis_size("fsdp")
    vectors, spots = padded_vectors(layer_vector)
    depth = input_proj.shape[1]
    up_shape = (depth, input_proj.shape[2] - 3 * D)
    qkv_shape, out_shape = (depth, 3 * D), output_proj.shape[1:]
    low = lambda *shape: jax.ShapeDtypeStruct(shape, LOW)
    levels = lambda shape: low(4, *quarter_shape(*shape))
    width = layer_vector.shape[1] * owners
    shapes = [
        shape_of(rows, D),
        shape_of(nodes, rows),
        shape_of(1, width),
        shape_of(1, width),
        low(owners, *qkv_shape),
        levels(up_shape),
        levels(out_shape),
        low(*up_shape),
        low(*out_shape),
        low(*qkv_shape),
        low(*up_shape),
        low(*out_shape),
        low(head_weight.shape[0], classes),
    ]
    wide = (patch_kernel, input_proj, output_proj, head_weight, pixels)
    in_vmem = pl.BlockSpec(memory_space=pltpu.VMEM)
    results = pl.pallas_call(
        functools.partial(first_kernel, spots=spots),
        in_specs=[ANYWHERE] * 6 + [in_vmem] * 4,
        out_specs=[in_vmem] * 4 + [ANYWHERE] + [in_vmem] * 8,
        out_shape=shapes,
        scratch_shapes=[
            *[pltpu.VMEM(array.shape, array.dtype) for array in wide],
            pltpu.VMEM((LANES, D), jnp.float32),
            pltpu.VMEM((owners, *patch_kernel.shape), LOW),
            pltpu.VMEM(qkv_shape, LOW),
            pltpu.VMEM((owners, *vectors.shape), LOW),
            pltpu.VMEM((owners, *qkv_shape), LOW),
            pltpu.VMEM((4, *quarter_shape(*up_shape)), LOW),
            pltpu.VMEM((4, *quarter_shape(*out_shape)), LOW),
            pltpu.SemaphoreType.DMA((7,)),
            pltpu.SemaphoreType.DMA((5, GATHER_SEMS)),
        ],
        compiler_params=pltpu.CompilerParams(
            collective_id=1, has_side_effects=True, vmem_limit_bytes=VMEM_LIMIT
        ),
        cost_estimate=NO_COST,
        name="begin",
    )(
        patch_kernel,
        vectors,
        input_proj,
        output_proj,
        head_weight,
        pixels,
        segment[:, None],
        patch_size,
        position_table,
        global_vector[None, :],
    )
    up_zero, output_zero, qkv_one, up_one, output_one, head_low = results[7:]
    return (
        results[0],
        results[1],
        results[2:4],
        results[4].reshape(owners * depth, 3 * D),
        [GatherRide(up_zero, results[5]), GatherRide(output_zero, results[6]), LevelRide(output_one)],
        [qkv_one, up_one, head_low],
    )


REDUCE_SEMS = 52


class Reduce:
    def __init__(self, grad, out, scratch, sems):
        self.grad, self.out, self.sems = grad, out, sems
        self.own, self.away, self.got_core, self.got_group, self.part, self.got_level = scratch
        self.rows, self.columns = out.shape
        self.chunk = 16

    def load(self, level):
        _, _, core = place()
        return pltpu.make_async_copy(
            self.grad.at[2 * level + core], self.own.at[level], self.sems.at[level]
        )

    def load_away(self, level):
        _, _, core = place()
        return pltpu.make_async_copy(
            self.grad.at[2 * level + 1 - core], self.away.at[level], self.sems.at[48 + level]
        )

    def core_copy(self, target_level):
        group, level, core = place()
        return remote(
            self.away.at[target_level],
            self.got_core.at[target_level],
            self.sems.at[4 + target_level],
            self.sems.at[8 + target_level],
            (group, 2 * level + 1 - core),
        )

    def group_copy(self, turn, other):
        group, level, core = place()
        target = partner(level, turn)
        peer = partner(group, other)
        part = quarter(peer, self.rows, self.columns)
        index = 3 * turn + other - 1
        return remote(
            self.own.at[target].at[part],
            self.got_group.at[other - 1, target],
            self.sems.at[12 + index],
            self.sems.at[24 + index],
            (peer, 2 * level + core),
        )

    def level_copy(self, turn):
        group, level, core = place()
        target = partner(level, turn)
        return remote(
            self.part.at[target],
            self.got_level.at[turn - 1],
            self.sems.at[35 + turn],
            self.sems.at[38 + turn],
            (group, 2 * target + core),
        )

    def share_copy(self, other):
        group, level, core = place()
        mine = self.out.at[quarter(group, self.rows, self.columns)]
        return remote(
            mine,
            mine,
            self.sems.at[41 + other],
            self.sems.at[44 + other],
            (partner(group, other), 2 * level + core),
        )

    def first(self):
        _, level, _ = place()
        for turn in (*TURNS, 0):
            self.load_away(partner(level, turn)).start()
        for turn in (*TURNS, 0):
            self.load(partner(level, turn)).start()
        for turn in (*TURNS, 0):
            self.load_away(partner(level, turn)).wait()
            self.core_copy(partner(level, turn)).start()

    def second(self):
        _, level, _ = place()
        for turn in (*TURNS, 0):
            target = partner(level, turn)
            self.load(target).wait()
            self.core_copy(target).wait_recv()

            def add(step, carry):
                rows = pl.ds(pl.multiple_of(step * self.chunk, self.chunk), self.chunk)
                total = self.own[target, rows, :].astype(jnp.float32)
                total = total + self.got_core[target, rows, :].astype(jnp.float32)
                self.own[target, rows, :] = total.astype(self.own.dtype)
                return carry

            lax.fori_loop(0, self.rows // self.chunk, add, 0)
            for other in TURNS:
                self.group_copy(turn, other).start()

    def between(self):
        pass

    def third(self):
        group, level, _ = place()
        high, wide = quarter_shape(self.rows, self.columns)
        row_part, column_part = quarter(group, self.rows, self.columns)
        for turn in (*TURNS, 0):
            target = partner(level, turn)
            for other in TURNS:
                self.group_copy(turn, other).wait_recv()

            def add(step, carry):
                at = pl.multiple_of(step * self.chunk, self.chunk)
                rows = pl.ds(at, self.chunk)
                mine = pl.ds(pl.multiple_of(row_part.start + at, self.chunk), self.chunk)
                total = self.own[target, mine, column_part].astype(jnp.float32)
                for slot in range(3):
                    total = total + self.got_group[slot, target, rows, :].astype(jnp.float32)
                self.part[target, rows, :] = total.astype(self.part.dtype)
                return carry

            lax.fori_loop(0, high // self.chunk, add, 0)
            if turn:
                self.level_copy(turn).start()

    def fourth(self):
        group, level, _ = place()
        high, wide = quarter_shape(self.rows, self.columns)
        row_part, column_part = quarter(group, self.rows, self.columns)
        for turn in TURNS:
            self.level_copy(turn).wait_recv()

        def add(step, carry):
            at = pl.multiple_of(step * self.chunk, self.chunk)
            rows = pl.ds(at, self.chunk)
            mine = pl.ds(pl.multiple_of(row_part.start + at, self.chunk), self.chunk)
            total = self.part[level, rows, :].astype(jnp.float32)
            for slot in range(3):
                total = total + self.got_level[slot, rows, :].astype(jnp.float32)
            self.out[mine, column_part] = total.astype(self.out.dtype)
            return carry

        lax.fori_loop(0, high // self.chunk, add, 0)
        for other in TURNS:
            self.share_copy(other).start()

    def store(self):
        self.target[...] = self.out[...]

    def fifth(self):
        for other in TURNS:
            self.share_copy(other).wait_recv()

    def sixth(self):
        _, level, _ = place()
        for turn in (*TURNS, 0):
            self.core_copy(partner(level, turn)).wait_send()
            for other in TURNS:
                self.group_copy(turn, other).wait_send()
            if turn:
                self.level_copy(turn).wait_send()
                self.share_copy(turn).wait_send()


WHOLE_SEMS = 44


def add_rows(target, row, columns, source, count, wide):
    chunk = 16 if wide > 1536 else 48

    def add(step, carry):
        at = pl.multiple_of(step * chunk, chunk)
        mine = pl.ds(pl.multiple_of(row + at, 16), chunk)
        total = target[mine, columns].astype(jnp.float32)
        total = total + source[pl.ds(at, chunk), :].astype(jnp.float32)
        target[mine, columns] = total.astype(target.dtype)
        return carry

    lax.fori_loop(0, count // chunk, add, 0)


class Whole:
    FIRST_X = (1, 0)

    def __init__(self, grad, out, scratch, sems):
        self.grad, self.out, self.sems = grad, out, sems
        self.own, self.away, self.got_core, self.got_x, self.got_y, self.got_last, self.part, self.got_level = scratch
        self.rows, self.columns = out.shape
        self.high, self.wide = self.rows // 2, self.columns // 2

    def row_half(self, index):
        return pl.ds(pl.multiple_of(lax.div(index, 2) * self.high, self.high), self.high)

    def column_half(self, index):
        return pl.ds(pl.multiple_of(lax.rem(index, 2) * self.wide, self.wide), self.wide)

    def load(self, level):
        _, _, core = place()
        return pltpu.make_async_copy(
            self.grad.at[2 * level + core], self.own.at[level], self.sems.at[level]
        )

    def load_away(self, level):
        _, _, core = place()
        return pltpu.make_async_copy(
            self.grad.at[2 * level + 1 - core], self.away.at[level], self.sems.at[40 + level]
        )

    def core_copy(self, target_level):
        group, level, core = place()
        return remote(
            self.away.at[target_level],
            self.got_core.at[target_level],
            self.sems.at[4 + target_level],
            self.sems.at[8 + target_level],
            (group, 2 * level + 1 - core),
        )

    def step_copy(self, turn):
        group, level, core = place()
        block = self.own.at[partner(level, turn)]
        if turn in self.FIRST_X:
            peer = partner(group, 1)
            source = block.at[:, self.column_half(peer)]
            target = self.got_x.at[self.FIRST_X.index(turn)]
        else:
            peer = partner(group, 2)
            source = block.at[self.row_half(peer), :]
            target = self.got_y.at[turn - 2]
        return remote(
            source, target, self.sems.at[12 + turn], self.sems.at[16 + turn], (peer, 2 * level + core)
        )

    def last_copy(self, turn):
        group, level, core = place()
        block = self.own.at[partner(level, turn)]
        peer = partner(group, 2 if turn in self.FIRST_X else 1)
        rows = self.row_half(peer)
        columns = self.column_half(peer)
        return remote(
            block.at[rows, columns],
            self.got_last.at[turn],
            self.sems.at[20 + turn],
            self.sems.at[24 + turn],
            (peer, 2 * level + core),
        )

    def level_copy(self, turn):
        group, level, core = place()
        target = partner(level, turn)
        return remote(
            self.part.at[target],
            self.got_level.at[turn - 1],
            self.sems.at[27 + turn],
            self.sems.at[30 + turn],
            (group, 2 * target + core),
        )

    def share_copy(self, other):
        group, level, core = place()
        mine = self.out.at[self.row_half(group), self.column_half(group)]
        return remote(
            mine,
            mine,
            self.sems.at[33 + other],
            self.sems.at[36 + other],
            (partner(group, other), 2 * level + core),
        )

    def first(self):
        _, level, _ = place()
        for turn in (*TURNS, 0):
            self.load_away(partner(level, turn)).start()
        for turn in (*TURNS, 0):
            self.load(partner(level, turn)).start()
        for turn in (*TURNS, 0):
            self.load_away(partner(level, turn)).wait()
            self.core_copy(partner(level, turn)).start()

    def second(self):
        _, level, _ = place()
        for turn in (*TURNS, 0):
            target = partner(level, turn)
            self.load(target).wait()
            self.core_copy(target).wait_recv()
            add_rows(
                self.own.at[target], 0, slice(None), self.got_core.at[target], self.rows, self.columns
            )
            self.step_copy(turn).start()

    def between(self):
        group, level, _ = place()
        for turn in (*TURNS, 0):
            block = self.own.at[partner(level, turn)]
            self.step_copy(turn).wait_recv()
            if turn in self.FIRST_X:
                source = self.got_x.at[self.FIRST_X.index(turn)]
                add_rows(block, 0, self.column_half(group), source, self.rows, self.wide)
            else:
                source = self.got_y.at[turn - 2]
                start = lax.div(group, 2) * self.high
                add_rows(block, start, slice(None), source, self.high, self.columns)
            self.last_copy(turn).start()

    def third(self):
        group, level, _ = place()
        start = lax.div(group, 2) * self.high
        columns = self.column_half(group)
        chunk = 16 if self.wide > 1536 else 48
        for turn in (*TURNS, 0):
            target = partner(level, turn)
            self.last_copy(turn).wait_recv()

            def add(step, carry):
                at = pl.multiple_of(step * chunk, chunk)
                rows = pl.ds(at, chunk)
                mine = pl.ds(pl.multiple_of(start + at, 16), chunk)
                total = self.own[target, mine, columns].astype(jnp.float32)
                total = total + self.got_last[turn, rows, :].astype(jnp.float32)
                self.part[target, rows, :] = total.astype(self.part.dtype)
                return carry

            lax.fori_loop(0, self.high // chunk, add, 0)
            if turn:
                self.level_copy(turn).start()

    def fourth(self):
        group, level, _ = place()
        start = lax.div(group, 2) * self.high
        columns = self.column_half(group)
        chunk = 16 if self.wide > 1536 else 48
        for turn in TURNS:
            self.level_copy(turn).wait_recv()

        def add(step, carry):
            at = pl.multiple_of(step * chunk, chunk)
            rows = pl.ds(at, chunk)
            mine = pl.ds(pl.multiple_of(start + at, 16), chunk)
            total = self.part[level, rows, :].astype(jnp.float32)
            for slot in range(3):
                total = total + self.got_level[slot, rows, :].astype(jnp.float32)
            self.out[mine, columns] = total.astype(self.out.dtype)
            return carry

        lax.fori_loop(0, self.high // chunk, add, 0)
        for other in TURNS:
            self.share_copy(other).start()

    def store(self):
        self.target[...] = self.out[...]

    def fifth(self):
        for other in TURNS:
            self.share_copy(other).wait_recv()

    def sixth(self):
        _, level, _ = place()
        for turn in (*TURNS, 0):
            self.core_copy(partner(level, turn)).wait_send()
            self.step_copy(turn).wait_send()
            self.last_copy(turn).wait_send()
            if turn:
                self.level_copy(turn).wait_send()
                self.share_copy(turn).wait_send()


GROUP_SEMS = 13


class GroupReduce:
    def __init__(self, share, out, scratch, sems):
        self.share, self.out, self.sems = share, out, sems
        self.own, self.got = scratch
        self.rows, self.columns = out.shape
        self.chunk = 16

    def load(self):
        return pltpu.make_async_copy(self.share, self.own, self.sems.at[0])

    def group_copy(self, other):
        group, level, core = place()
        peer = partner(group, other)
        return remote(
            self.own.at[quarter(peer, self.rows, self.columns)],
            self.got.at[other - 1],
            self.sems.at[other],
            self.sems.at[3 + other],
            (peer, 2 * level + core),
        )

    def share_copy(self, other):
        group, level, core = place()
        mine = self.out.at[quarter(group, self.rows, self.columns)]
        return remote(
            mine,
            mine,
            self.sems.at[6 + other],
            self.sems.at[9 + other],
            (partner(group, other), 2 * level + core),
        )

    def first(self):
        self.load().start()

    def second(self):
        self.load().wait()
        for other in TURNS:
            self.group_copy(other).start()

    def between(self):
        pass

    def third(self):
        group, _, _ = place()
        high, wide = quarter_shape(self.rows, self.columns)
        row_part, column_part = quarter(group, self.rows, self.columns)
        for other in TURNS:
            self.group_copy(other).wait_recv()

        def add(step, carry):
            at = pl.multiple_of(step * self.chunk, self.chunk)
            rows = pl.ds(at, self.chunk)
            mine = pl.ds(pl.multiple_of(row_part.start + at, self.chunk), self.chunk)
            total = self.own[mine, column_part].astype(jnp.float32)
            for slot in range(3):
                total = total + self.got[slot, rows, :].astype(jnp.float32)
            self.out[mine, column_part] = total.astype(self.out.dtype)
            return carry

        lax.fori_loop(0, high // self.chunk, add, 0)
        for other in TURNS:
            self.share_copy(other).start()

    def fourth(self):
        pass

    def fifth(self):
        for other in TURNS:
            self.share_copy(other).wait_recv()

    def store(self):
        self.target[...] = self.out[...]

    def sixth(self):
        for other in TURNS:
            self.group_copy(other).wait_send()
            self.share_copy(other).wait_send()


class Spread:
    def __init__(self, full, sems):
        self.full, self.sems = full, sems

    def level_copy(self, turn):
        group, level, core = place()
        block = self.full.at[2 * level + core]
        peer = (group, 2 * partner(level, turn) + core)
        return remote(block, block, self.sems.at[turn - 1], self.sems.at[2 + turn], peer)

    def core_copy(self, turn):
        group, level, core = place()
        block = self.full.at[2 * partner(level, turn) + core]
        peer = (group, 2 * level + 1 - core)
        return remote(block, block, self.sems.at[6 + turn], self.sems.at[10 + turn], peer)

    def run(self):
        for turn in TURNS:
            self.level_copy(turn).start()
        self.core_copy(0).start()
        for turn in TURNS:
            self.level_copy(turn).wait_recv()
            self.core_copy(turn).start()
        for turn in (0, *TURNS):
            self.core_copy(turn).wait_recv()
        for turn in (0, *TURNS):
            self.core_copy(turn).wait_send()
            if turn:
                self.level_copy(turn).wait_send()


def squares_in(out):
    def add(step, total):
        piece = out[pl.ds(pl.multiple_of(step * 16, 16), 16), :].astype(jnp.float32)
        piece = piece * piece
        for lane in range(0, out.shape[1], LANES):
            total = total + piece[:, lane : lane + LANES]
        return total

    total = lax.fori_loop(0, out.shape[0] // 16, add, jnp.zeros((16, LANES), jnp.float32))
    return jnp.sum(total, 0, keepdims=True)


def run_stages(jobs, stages):
    for stage in stages:
        for job in jobs:
            getattr(job, stage)()


STAGES = ("first", "second", "between", "third", "fourth", "fifth", "sixth")


def whole_scratch(grad):
    _, rows, columns = grad.shape
    high, wide = quarter_shape(rows, columns)
    shapes = (*[(4, rows, columns)] * 3, (3, 4, high, wide), (4, high, wide))
    return [pltpu.VMEM(shape, grad.dtype) for shape in (*shapes, (3, high, wide))]


def stepped_scratch(grad):
    _, rows, columns = grad.shape
    high, wide = rows // 2, columns // 2
    shapes = (
        *[(4, rows, columns)] * 3,
        (2, rows, wide),
        (2, high, columns),
        (4, high, wide),
        (4, high, wide),
        (3, high, wide),
    )
    return [pltpu.VMEM(shape, grad.dtype) for shape in shapes]


def share_scratch(share):
    return [
        pltpu.VMEM(share.shape, share.dtype),
        pltpu.VMEM((3, *quarter_shape(*share.shape)), share.dtype),
    ]


def reduce_kernel(*refs, whole, partly):
    count = whole + 1 + partly
    grads, outs, refs = refs[:count], refs[count : 2 * count], refs[2 * count :]
    sems, small_sems, group_sems, refs = refs[0], refs[1], refs[2], refs[3:]
    jobs = [
        Whole(grads[i], outs[i], refs[8 * i : 8 * i + 8], sems.at[i]) for i in range(whole)
    ]
    refs = refs[8 * whole :]
    small = Reduce(grads[whole], outs[whole], refs[:6], small_sems)
    refs = refs[6:]
    shares = [
        GroupReduce(
            grads[whole + 1 + i], outs[whole + 1 + i], refs[2 * i : 2 * i + 2], group_sems.at[i]
        )
        for i in range(partly)
    ]
    greet()
    run_stages([*jobs, small, *shares], STAGES[:1])
    run_stages([small, *shares], STAGES[1:2])
    run_stages(jobs, STAGES[1:3])
    run_stages([small, *shares], STAGES[3:4])
    run_stages(jobs, STAGES[3:4])
    run_stages([small, *jobs], STAGES[4:5])
    run_stages([*shares, small, *jobs], STAGES[5:])


def transfer_outs(arrays):
    return [jax.ShapeDtypeStruct(array.shape[-2:], array.dtype) for array in arrays]


def reduce_call(grads, small, shares, collective_id):
    in_vmem = pl.BlockSpec(memory_space=pltpu.VMEM)
    whole, partly = len(grads), len(shares)
    operands = [*grads, small, *shares]
    scratch = [
        pltpu.SemaphoreType.DMA((whole, WHOLE_SEMS)),
        pltpu.SemaphoreType.DMA((REDUCE_SEMS,)),
        pltpu.SemaphoreType.DMA((partly, GROUP_SEMS)),
    ]
    for grad in grads:
        scratch.extend(stepped_scratch(grad))
    scratch.extend(whole_scratch(small))
    for share in shares:
        scratch.extend(share_scratch(share))
    return pl.pallas_call(
        functools.partial(reduce_kernel, whole=whole, partly=partly),
        in_specs=[ANYWHERE] * len(operands),
        out_specs=[in_vmem] * len(operands),
        out_shape=transfer_outs(operands),
        scratch_shapes=scratch,
        compiler_params=pltpu.CompilerParams(
            collective_id=collective_id, has_side_effects=True, vmem_limit_bytes=VMEM_LIMIT
        ),
        cost_estimate=NO_COST,
        name="reduce_gradients",
    )(*operands)


def totals(full, vector_rows, rest_size):
    owners, rows, _ = full.shape
    rest_rows = -(-rest_size // (owners * LANES))
    row = lax.broadcasted_iota(jnp.int32, full.shape, 1)
    spot = row - vector_rows + rest_rows * lax.broadcasted_iota(jnp.int32, full.shape, 0)
    spot = spot * LANES + lax.broadcasted_iota(jnp.int32, full.shape, 2)
    in_rest = (row >= vector_rows) & (row < vector_rows + rest_rows)

    def summed(values):
        return jnp.sum(jnp.sum(jnp.sum(values, 0), 0, keepdims=True), 1, keepdims=True)

    tokens = summed(jnp.where(in_rest & (spot == rest_size - 1), full, 0.0))
    loss = summed(jnp.where(in_rest & (spot == rest_size - 2), full, 0.0))
    kept = (row < vector_rows) | (in_rest & (spot < rest_size - 2))
    squares = jnp.where(kept, full * full, jnp.where(row == rows - 1, full, 0.0))
    norm = jnp.sqrt(summed(squares)) / tokens
    factor = jnp.minimum(1.0, CLIP_NORM / norm) / tokens
    lane = lax.broadcasted_iota(jnp.int32, (1, LANES), 1)
    return jnp.where(
        lane == 0, factor, jnp.where(lane == 1, norm, jnp.where(lane == 2, loss, tokens))
    )


def finish_kernel(*refs, done, partly, vector_rows, rest_size):
    finished, small, refs = refs[:done], refs[done], refs[done + 1 :]
    shares, refs = refs[:partly], refs[partly:]
    outs, full, numbers, refs = refs[:partly], refs[partly], refs[partly + 1], refs[partly + 2 :]
    group_sems, spread_sems, refs = refs[0], refs[1], refs[2:]
    jobs = [
        GroupReduce(shares[i], outs[i], refs[2 * i : 2 * i + 2], group_sems.at[i])
        for i in range(partly)
    ]
    greet()
    run_stages(jobs, STAGES[:2])
    total = sum(squares_in(out) for out in finished)
    run_stages(jobs, STAGES[3:6])
    total = total + sum(squares_in(out) for out in outs)
    _, level, core = place()
    mine = 2 * level + core
    last = small.shape[0] - 1
    full[mine] = small[...]
    full[mine, last : last + 1, :] = total
    Spread(full, spread_sems).run()
    numbers[...] = totals(full[...], vector_rows, rest_size)
    run_stages(jobs, STAGES[6:])


def finish_call(finished, small, shares, vector_rows, rest_size, collective_id):
    done, partly = len(finished), len(shares)
    in_vmem = pl.BlockSpec(memory_space=pltpu.VMEM)
    scratch = [
        pltpu.SemaphoreType.DMA((partly, GROUP_SEMS)),
        pltpu.SemaphoreType.DMA((14,)),
    ]
    for share in shares:
        scratch.extend(share_scratch(share))
    full = (lax.axis_size("fsdp"), *small.shape)
    out_shape = [*transfer_outs(shares), jax.ShapeDtypeStruct(full, small.dtype), shape_of(1, LANES)]
    return pl.pallas_call(
        functools.partial(
            finish_kernel, done=done, partly=partly, vector_rows=vector_rows, rest_size=rest_size
        ),
        in_specs=[in_vmem] * (done + 1) + [ANYWHERE] * partly,
        out_specs=[in_vmem] * len(out_shape),
        out_shape=out_shape,
        scratch_shapes=scratch,
        compiler_params=pltpu.CompilerParams(
            collective_id=collective_id, has_side_effects=True, vmem_limit_bytes=VMEM_LIMIT
        ),
        name="finish_gradients",
    )(*finished, small, *shares)


def with_kernels():
    return lax.axis_size("dp") == 4 and lax.axis_size("fsdp") == 8


def reduce_all(grads, small, shares, collective_id):
    if with_kernels():
        return reduce_call(grads, small, shares, collective_id)
    return [lax.psum(scatter(grad), "dp") for grad in (*grads, small)] + [
        lax.psum(share, "dp") for share in shares
    ]


def finish_all(finished, small, shares, vector_rows, rest_size, collective_id):
    if with_kernels():
        return finish_call(finished, small, shares, vector_rows, rest_size, collective_id)
    outs = [lax.psum(share, "dp") for share in shares]
    total = sum(jnp.sum(jnp.square(out.astype(jnp.float32))) for out in (*finished, *outs))
    row = jnp.full((1, LANES), 1.0 / LANES, jnp.float32) * total
    full = lax.all_gather(small.at[-1:].set(row), "fsdp", axis=0)
    return [*outs, full, totals(full, vector_rows, rest_size)]


def scatter(grad):
    return lax.psum_scatter(grad, "fsdp", scatter_dimension=0)


def by_owner(grad, low=jnp.bfloat16):
    owners = lax.axis_size("fsdp")
    return grad.astype(low).reshape(owners, grad.shape[0] // owners, grad.shape[1])


def attention_forward_kernel(
    q_ref, k_ref, v_ref, seg_col_ref, seg_row_ref, out_ref, expo_ref, inv_ref, *, block
):
    rows = q_ref.shape[0]
    lower = lax.broadcasted_iota(jnp.int32, (block, PAIR), 1) < HD
    keys = k_ref[...]
    values = jnp.concatenate([v_ref[...], jnp.ones((rows, PAIR), v_ref.dtype)], 1)
    seg_row = seg_row_ref[...]
    tasks = [(step, head) for step in range(rows // block) for head in range(2)]

    def scores_of(step, head):
        query = q_ref[step * block : (step + 1) * block, :] * jnp.bfloat16(HD**-0.5)
        keep = lower if head == 0 else jnp.logical_not(lower)
        return mul_nt(jnp.where(keep, query, jnp.bfloat16(0)), keys)

    scores = scores_of(*tasks[0])
    outs = []
    for index, (step, head) in enumerate(tasks):
        following = scores_of(*tasks[index + 1]) if index + 1 < len(tasks) else None
        at = slice(step * block, (step + 1) * block)
        scores = jnp.where(seg_col_ref[at, :] == seg_row, scores, MASKED)
        highest = jnp.max(scores, -1, keepdims=True)
        low = jnp.exp(scores - highest).astype(jnp.bfloat16)
        expo_ref[head, at, :] = low
        outs.append(mul(low, values))
        if head:
            inverse = 1.0 / jnp.where(lower, outs[0][:, PAIR:], outs[1][:, PAIR:])
            sums = jnp.where(lower, outs[0][:, :PAIR], outs[1][:, :PAIR])
            out_ref[at, :] = (sums * inverse).astype(jnp.bfloat16)
            inv_ref[at, :] = inverse
            outs = []
        scores = following


def attention_forward(qkv_rows, segment, rides, collective_id):
    rows = qkv_rows.shape[0]
    pairs = HEADS // 2
    wide = lambda base: pl.BlockSpec((rows, PAIR), lambda j, base=base: (0, base + j))
    return block_call(
        functools.partial(attention_forward_kernel, block=min(256, rows)),
        pairs,
        [wide(0), wide(pairs), wide(2 * pairs), fixed(rows, 1), fixed(1, rows)],
        [qkv_rows, qkv_rows, qkv_rows, segment[:, None], segment[None, :]],
        [wide(0), pl.BlockSpec((2, rows, rows), lambda j: (j, 0, 0)), wide(0)],
        [
            shape_of(rows, D, dtype=LOW),
            shape_of(HEADS, rows, rows, dtype=LOW),
            shape_of(rows, D),
        ],
        [],
        "attention_forward",
        work(16 * HEADS * rows * rows * HD, 2 * HEADS * rows * rows + 12 * rows * D),
        rides,
        collective_id,
    )


def attention_backward_kernel(
    q_ref, k_ref, v_ref, expo_ref, inv_ref, out_ref, grad_ref, dqkv_ref, *, block
):
    rows = q_ref.shape[0]
    pair = pl.program_id(0)
    lower = lax.broadcasted_iota(jnp.int32, (block, PAIR), 1) < HD
    keys = k_ref[...]
    values = v_ref[...]
    scale = HD**-0.5
    scaled_grad = (grad_ref[...].astype(jnp.float32) * inv_ref[...]).astype(jnp.bfloat16)
    query = q_ref[...]
    query_t = query.T
    grad_t = scaled_grad.T
    product = scaled_grad.astype(jnp.float32) * out_ref[...].astype(jnp.float32)
    key_t = [None, None]
    value_t = [None, None]
    tasks = [(step, head) for step in range(rows // block) for head in range(2)]

    def probs_grad_of(step, head):
        keep = lower if head == 0 else jnp.logical_not(lower)
        mine = scaled_grad[step * block : (step + 1) * block]
        return mul_nt(jnp.where(keep, mine, jnp.bfloat16(0)), values)

    probs_grad = probs_grad_of(*tasks[0])
    query_parts = []
    for index, (step, head) in enumerate(tasks):
        following = probs_grad_of(*tasks[index + 1]) if index + 1 < len(tasks) else None
        at = slice(step * block, (step + 1) * block)
        lanes = slice(head * HD, (head + 1) * HD)
        keep = lower if head == 0 else jnp.logical_not(lower)
        inner = jnp.sum(jnp.where(keep, product[at], 0.0), -1, keepdims=True)
        low = expo_ref[head, at, :]
        value_part = mul(grad_t[lanes, at], low)
        scores_grad = (low.astype(jnp.float32) * (probs_grad - inner)).astype(jnp.bfloat16)
        query_parts.append(mul(scores_grad, keys))
        key_part = mul(query_t[lanes, at], scores_grad)
        key_t[head] = key_part if step == 0 else key_t[head] + key_part
        value_t[head] = value_part if step == 0 else value_t[head] + value_part
        if head:
            query_grad = jnp.where(lower, query_parts[0], query_parts[1]) * scale
            dqkv_ref[at, pl.ds(pl.multiple_of(pair * PAIR, PAIR), PAIR)] = query_grad.astype(
                jnp.bfloat16
            )
            query_parts = []
        probs_grad = following
    key_grad = (jnp.concatenate(key_t, 0) * scale).T
    value_grad = jnp.concatenate(value_t, 0).T
    dqkv_ref[:, pl.ds(pl.multiple_of(D + pair * PAIR, PAIR), PAIR)] = key_grad.astype(jnp.bfloat16)
    dqkv_ref[:, pl.ds(pl.multiple_of(2 * D + pair * PAIR, PAIR), PAIR)] = value_grad.astype(jnp.bfloat16)


def attention_backward(qkv_rows, expo, inverse, attended, attended_grad, rides, collective_id):
    rows = qkv_rows.shape[0]
    pairs = HEADS // 2
    wide = lambda base: pl.BlockSpec((rows, PAIR), lambda j, base=base: (0, base + j))
    return block_call(
        functools.partial(attention_backward_kernel, block=min(256, rows)),
        pairs,
        [
            wide(0),
            wide(pairs),
            wide(2 * pairs),
            pl.BlockSpec((2, rows, rows), lambda j: (j, 0, 0)),
            wide(0),
            wide(0),
            wide(0),
        ],
        [qkv_rows, qkv_rows, qkv_rows, expo, inverse, attended, attended_grad],
        [fixed(rows, 3 * D)],
        [shape_of(rows, 3 * D, dtype=LOW)],
        [],
        "attention_backward",
        None,
        rides,
        collective_id,
    )


def mul(left, right):
    return jnp.dot(left, right, preferred_element_type=jnp.float32)


def mul_nt(left, right):
    return lax.dot_general(left, right, NT, preferred_element_type=jnp.float32)


def normalized(values):
    center = values - jnp.mean(values, -1, keepdims=True)
    inverse = lax.rsqrt(jnp.mean(center * center, -1, keepdims=True) + NORM_EPS)
    return center * inverse, inverse


def norm_backward(grad, values, gain):
    unit, inverse = normalized(values)
    inner = grad * gain
    mean_inner = jnp.mean(inner, -1, keepdims=True)
    mean_cross = jnp.mean(inner * unit, -1, keepdims=True)
    value_grad = inverse * (inner - mean_inner - unit * mean_cross)
    return value_grad, column_sum(grad * unit), column_sum(grad)


def column_sum(rows):
    return jnp.sum(rows.astype(jnp.float32), 0, keepdims=True)


def at_first(action):
    pl.when(pl.program_id(0) == 0)(action)


def rows_of(block, columns):
    return pl.BlockSpec((block, columns), lambda i: (i, 0))


def fixed(*shape):
    return pl.BlockSpec(shape, lambda i: (0,) * len(shape), pipeline_mode=pl.Buffered(1))


def loads(sources, targets, sems):
    return [
        pltpu.make_async_copy(source, target, sems.at[index])
        for index, (source, target) in enumerate(zip(sources, targets))
    ]


def shape_of(*shape, dtype=jnp.float32):
    return jax.ShapeDtypeStruct(shape, dtype)


def embed_kernel(pixel_ref, weight_ref, pos_ref, table_ref, bias_ref, out_ref):
    position = jnp.dot(
        pos_ref[...], table_ref[...], precision=HIGHEST, preferred_element_type=jnp.float32
    )
    out_ref[...] = mul(pixel_ref[...], weight_ref[...]) + bias_ref[...] + position


def embed(pixels, weight, pos_weights, table, bias):
    rows, depth = pixels.shape
    block = 256
    nodes = pos_weights.shape[1]
    return block_call(
        embed_kernel,
        rows // block,
        [rows_of(block, depth), fixed(depth, D), rows_of(block, nodes), fixed(nodes, D), fixed(1, D)],
        [pixels, weight, pos_weights, table, bias],
        [rows_of(block, D)],
        [shape_of(rows, D)],
        [],
        "embed",
        work(2 * rows * depth * D, 2 * rows * depth + 2 * depth * D + 4 * rows * D),
    )[0]


def chunk_at(base):
    return pl.ds(pl.multiple_of(base + pl.program_id(0) * D, LANES), D)


def columns_of(rows):
    return pl.BlockSpec((rows, D), lambda i: (0, i))


def halves_of(rows):
    half = rows // 2
    return [slice(start, start + half) for start in range(0, rows, half)]


def at_last(action):
    pl.when(pl.program_id(0) == pl.num_programs(0) - 1)(action)


def qkv_kernel(stream_ref, weight_ref, vector_ref, normed_out, qkv_ref, normed_ref, sem):
    copy = pltpu.make_async_copy(normed_ref, normed_out, sem)

    @at_first
    def _():
        unit, _ = normalized(stream_ref[...])
        normed_ref[...] = (unit * vector_ref[:, :D] + vector_ref[:, D : 2 * D]).astype(LOW)
        copy.start()

    bias = vector_ref[:, chunk_at(4 * D)]
    for half in halves_of(stream_ref.shape[0]):
        qkv_ref[half, :] = (mul(normed_ref[half, :], weight_ref[...]) + bias).astype(LOW)
    at_last(copy.wait)


def qkv_forward(stream, weight, vector):
    rows = stream.shape[0]
    return block_call(
        qkv_kernel,
        3,
        [fixed(rows, D), columns_of(D), fixed(1, vector.shape[1])],
        [stream, weight, vector],
        [ANYWHERE, columns_of(rows)],
        [shape_of(rows, D, dtype=LOW), shape_of(rows, 3 * D, dtype=LOW)],
        [pltpu.VMEM((rows, D), LOW), pltpu.SemaphoreType.DMA],
        "qkv_forward",
        work(6 * rows * D * D, 14 * rows * D + 6 * D * D),
    )


def mlp_kernel(
    stream_ref, attended_ref, mix_ref, up_ref, down_ref, vector_ref,
    residual_out, normed_out, active_ref, slope_ref, out_ref,
    residual_ref, normed_ref, sems,
):
    rows = stream_ref.shape[0]
    copies = loads((residual_ref, normed_ref), (residual_out, normed_out), sems)

    @at_first
    def _():
        for half in halves_of(rows):
            residual = stream_ref[half, :] + mul(attended_ref[half, :], mix_ref[...])
            residual = residual + vector_ref[:, 7 * D : 8 * D]
            residual_ref[half, :] = residual
            unit, _ = normalized(residual)
            normed = unit * vector_ref[:, 2 * D : 3 * D] + vector_ref[:, 3 * D : 4 * D]
            normed_ref[half, :] = normed.astype(LOW)
            out_ref[half, :] = residual + vector_ref[:, 8 * D : 9 * D]
        for copy in copies:
            copy.start()

    bias = vector_ref[:, chunk_at(9 * D)]
    parts = halves_of(rows)
    hidden = mul(normed_ref[parts[0], :], up_ref[...]) + bias
    for index, half in enumerate(parts):
        following = None
        if index + 1 < len(parts):
            following = mul(normed_ref[parts[index + 1], :], up_ref[...]) + bias
        square = hidden * hidden
        rise = 0.5 + 0.5 * jnp.tanh(hidden * (ROOT + (ROOT * CUBE) * square))
        active = hidden * rise
        active_low = active.astype(LOW)
        active_ref[half, :] = active_low
        bend = (2.0 * ROOT) + (6.0 * ROOT * CUBE) * square
        slope_ref[half, :] = (rise + active * (1.0 - rise) * bend).astype(LOW)
        out_ref[half, :] += mul(active_low, down_ref[...])
        hidden = following

    @at_last
    def _():
        for copy in copies:
            copy.wait()


def mlp_specs(up, proj_out):
    return (
        [fixed(D, D), columns_of(D), pl.BlockSpec((D, D), lambda i: (i + 1, 0))],
        [proj_out, up, proj_out],
    )


def mlp_forward(stream, attended, up, proj_out, vector):
    rows = stream.shape[0]
    width = up.shape[1]
    weight_specs, weights = mlp_specs(up, proj_out)
    return block_call(
        mlp_kernel,
        width // D,
        [fixed(rows, D), fixed(rows, D), *weight_specs, fixed(1, vector.shape[1])],
        [stream, attended, *weights, vector],
        [ANYWHERE, ANYWHERE, columns_of(rows), columns_of(rows), fixed(rows, D)],
        [
            shape_of(rows, D),
            shape_of(rows, D, dtype=LOW),
            shape_of(rows, width, dtype=LOW),
            shape_of(rows, width, dtype=LOW),
            shape_of(rows, D),
        ],
        [
            pltpu.VMEM((rows, D), jnp.float32),
            pltpu.VMEM((rows, D), LOW),
            pltpu.SemaphoreType.DMA((2,)),
        ],
        "mlp_forward",
        work(2 * rows * D * (D + 2 * width), rows * (16 * D + 4 * width) + 2 * D * (D + 2 * width)),
    )


def mlp_back_kernel(
    grad_ref, slope_ref, residual_ref, mix_ref, up_ref, down_ref, vector_ref,
    low_out, hidden_ref, out_ref, out_low_ref, attended_ref, sums_ref,
    low_ref, second_ref, sem,
):
    rows = grad_ref.shape[0]
    copy = pltpu.make_async_copy(low_ref, low_out, sem)

    @at_first
    def _():
        low_ref[...] = grad_ref[...].astype(LOW)
        copy.start()
        second_ref[...] = jnp.zeros_like(second_ref)

    parts = halves_of(rows)
    active_grad = mul_nt(low_ref[parts[0], :], down_ref[...])
    hidden_sum = 0.0
    for index, half in enumerate(parts):
        following = None
        if index + 1 < len(parts):
            following = mul_nt(low_ref[parts[index + 1], :], down_ref[...])
        hidden_grad = (active_grad * slope_ref[half, :].astype(jnp.float32)).astype(LOW)
        hidden_ref[half, :] = hidden_grad
        hidden_sum = hidden_sum + column_sum(hidden_grad)
        second_ref[half, :] += mul_nt(hidden_grad, up_ref[...])
        active_grad = following
    sums_ref[:, chunk_at(4 * D)] = hidden_sum

    @at_last
    def _():
        gain = vector_ref[:, 2 * D : 3 * D]
        totals = [0.0] * 4
        for half in halves_of(rows):
            grad = grad_ref[half, :]
            value_grad, gain_grad, shift_grad = norm_backward(
                second_ref[half, :], residual_ref[half, :], gain
            )
            total = value_grad + grad
            out_ref[half, :] = total
            total_low = total.astype(LOW)
            out_low_ref[half, :] = total_low
            attended_ref[half, :] = mul_nt(total_low, mix_ref[...]).astype(LOW)
            new = (gain_grad, shift_grad, column_sum(total_low), column_sum(low_ref[half, :]))
            totals = [old + part for old, part in zip(totals, new)]
        sums_ref[:, : 4 * D] = jnp.concatenate(totals, 1)
        copy.wait()


def mlp_backward(grad, slope, residual, up, proj_out, vector):
    rows = grad.shape[0]
    width = up.shape[1]
    whole = fixed(rows, D)
    weight_specs, weights = mlp_specs(up, proj_out)
    return block_call(
        mlp_back_kernel,
        width // D,
        [whole, columns_of(rows), whole, *weight_specs, fixed(1, vector.shape[1])],
        [grad, slope, residual, *weights, vector],
        [ANYWHERE, columns_of(rows), whole, whole, whole, fixed(1, 4 * D + width)],
        [
            shape_of(rows, D, dtype=LOW),
            shape_of(rows, width, dtype=LOW),
            shape_of(rows, D),
            shape_of(rows, D, dtype=LOW),
            shape_of(rows, D, dtype=LOW),
            shape_of(1, 4 * D + width),
        ],
        [
            pltpu.VMEM((rows, D), LOW),
            pltpu.VMEM((rows, D), jnp.float32),
            pltpu.SemaphoreType.DMA,
        ],
        "mlp_backward",
    )


def qkv_back_kernel(grad_ref, residual_ref, stream_ref, weight_ref, vector_ref, out_ref, sums_ref):
    grad = grad_ref[...]
    normed_grad = mul_nt(grad, weight_ref[...])
    value_grad, gain_grad, shift_grad = norm_backward(normed_grad, stream_ref[...], vector_ref[:, :D])
    out_ref[...] = residual_ref[...] + value_grad
    sums = jnp.concatenate([gain_grad, shift_grad, column_sum(grad)], 1)

    @at_first
    def _():
        sums_ref[...] = jnp.zeros_like(sums_ref)

    sums_ref[...] += sums


def qkv_backward(grad, residual_grad, stream, weight, vector):
    rows = stream.shape[0]
    block = 256
    narrow = rows_of(block, D)
    return block_call(
        qkv_back_kernel,
        rows // block,
        [rows_of(block, 3 * D), narrow, narrow, fixed(D, 3 * D), fixed(1, vector.shape[1])],
        [grad, residual_grad, stream, weight, vector],
        [narrow, fixed(1, 5 * D)],
        [shape_of(rows, D), shape_of(1, 5 * D)],
        [],
        "qkv_backward",
    )


def input_grad_kernel(left_ref, right_ref, out_ref, turned_ref):
    @at_first
    def _():
        turned_ref[...] = left_ref[...].T

    out_ref[...] = mul(turned_ref[...], right_ref[...]).astype(LOW)


def input_weight_grad(left, right):
    rows, width = right.shape
    return block_call(
        input_grad_kernel,
        width // D,
        [fixed(rows, D), columns_of(rows)],
        [left, right],
        [columns_of(D)],
        [shape_of(D, width, dtype=LOW)],
        [pltpu.VMEM((D, rows), LOW)],
        "input_weight_grad",
    )[0]


def output_grad_kernel(attended_ref, active_ref, residual_ref, grad_ref, *outs, cut):
    step = pl.program_id(0)

    def store(product):
        base = 0
        for out in outs:
            out[...] = product[:, base : base + out.shape[1]].astype(jnp.bfloat16)
            base += out.shape[1]

    @pl.when(step < cut)
    def _():
        store(mul(attended_ref[...].T, residual_ref[...]))

    @pl.when(step >= cut)
    def _():
        store(mul(active_ref[...].T, grad_ref[...]))


def output_weight_grad(attended, active, residual_low, grad_low, parts):
    rows = attended.shape[0]
    block = 768
    cut = attended.shape[1] // block
    steps = cut + active.shape[1] // block
    return block_call(
        functools.partial(output_grad_kernel, cut=cut),
        steps,
        [
            pl.BlockSpec((rows, block), lambda i: (0, jnp.minimum(i, cut - 1))),
            pl.BlockSpec((rows, block), lambda i: (0, jnp.maximum(i - cut, 0))),
            fixed(rows, D),
            fixed(rows, D),
        ],
        [attended, active, residual_low, grad_low],
        [rows_of(block, part) for part in parts],
        [shape_of(steps * block, part, dtype=LOW) for part in parts],
        [],
        "output_weight_grad",
    )


def embed_back_kernel(pixel_ref, grad_ref, pos_ref, out_ref, table_ref, bias_ref, low_ref):
    @at_first
    def _():
        grad = grad_ref[...]
        low = grad.astype(jnp.bfloat16)
        low_ref[...] = low
        bias_ref[...] = column_sum(low)
        table_ref[...] = jnp.dot(
            pos_ref[...], grad, precision=HIGHEST, preferred_element_type=jnp.float32
        )

    out_ref[...] = mul(pixel_ref[...].T, low_ref[...]).astype(jnp.bfloat16)


def embed_backward(pixels, grad, pos_weights_t):
    rows, depth = pixels.shape
    block = 768
    nodes = pos_weights_t.shape[0]
    return block_call(
        embed_back_kernel,
        depth // block,
        [pl.BlockSpec((rows, block), lambda i: (0, i)), fixed(rows, D), fixed(nodes, rows)],
        [pixels, grad, pos_weights_t],
        [rows_of(block, D), fixed(nodes, D), fixed(1, D)],
        [shape_of(depth, D, dtype=jnp.bfloat16), shape_of(nodes, D), shape_of(1, D)],
        [pltpu.VMEM((rows, D), jnp.bfloat16)],
        "embed_backward",
        None,
    )


def head_kernel(
    stream_ref, seg_col_ref, seg_row_ref, label_ref, weight_ref, vector_ref,
    grad_ref, weight_grad_ref, sums_ref, bias_grad_ref, numbers_ref, *, classes,
):
    padded = weight_ref.shape[1]
    vector = vector_ref[...].astype(LOW).astype(jnp.float32)
    gain, shift = vector[:, D : 2 * D], vector[:, 2 * D : 3 * D]
    slots = lax.broadcasted_iota(jnp.int32, (IMGS, 1), 0)
    member = (seg_row_ref[...] == slots).astype(jnp.float32)
    counts = jnp.sum(member, 1, keepdims=True)
    sizes = jnp.maximum(counts, 1.0)
    unit, inverse = normalized(stream_ref[...])
    final = unit * gain + shift
    owner = jnp.broadcast_to(seg_col_ref[...], final.shape)
    pooled = [jnp.sum(jnp.where(owner == k, final, 0.0), 0, keepdims=True) for k in range(IMGS)]
    pooled = (jnp.concatenate(pooled, 0) / sizes).astype(LOW)
    class_at = lax.broadcasted_iota(jnp.int32, (IMGS, padded), 1)
    logits = mul(pooled, weight_ref[...]) + vector[:, 3 * D :]
    logits = jnp.where(class_at < classes, logits, MASKED)
    highest = jnp.max(logits, -1, keepdims=True)
    exponent = jnp.exp(logits - highest)
    totals = jnp.sum(exponent, -1, keepdims=True)
    onehot = class_at == label_ref[...]
    picked = jnp.sum(jnp.where(onehot, logits, 0.0), 1, keepdims=True)
    loss = jnp.sum(counts * (highest + jnp.log(totals) - picked), 0, keepdims=True)
    numbers_ref[...] = jnp.concatenate([loss, jnp.sum(counts, 0, keepdims=True)], 1)
    logits_grad = ((exponent / totals - onehot.astype(jnp.float32)) * counts).astype(LOW)
    bias_grad_ref[...] = column_sum(logits_grad)
    weight_grad_ref[...] = lax.dot_general(
        pooled, logits_grad, (((0,), (0,)), ((), ())), preferred_element_type=jnp.float32
    ).astype(LOW)
    pooled_grad = mul_nt(logits_grad, weight_ref[...]) / sizes
    own = (seg_col_ref[...] == lax.broadcasted_iota(jnp.int32, (1, IMGS), 1)).astype(LOW)
    final_grad, left = 0.0, pooled_grad
    for _ in range(3):
        term = left.astype(LOW)
        final_grad = final_grad + mul(own, term)
        left = left - term.astype(jnp.float32)
    inner = final_grad * gain
    mean_inner = jnp.mean(inner, -1, keepdims=True)
    mean_cross = jnp.mean(inner * unit, -1, keepdims=True)
    grad_ref[...] = inverse * (inner - mean_inner - unit * mean_cross)
    sums_ref[...] = jnp.concatenate([column_sum(final_grad * unit), column_sum(final_grad)], 1)


def head(stream, segment, labels, weight, global_vector, classes):
    rows = stream.shape[0]
    padded = weight.shape[1]
    vector = jnp.pad(global_vector, (0, padded - classes))[None, :]
    return pl.pallas_call(
        functools.partial(head_kernel, classes=classes),
        out_shape=[
            shape_of(rows, D),
            shape_of(D, padded, dtype=LOW),
            shape_of(1, 2 * D),
            shape_of(1, padded),
            shape_of(1, 2),
        ],
        compiler_params=pltpu.CompilerParams(vmem_limit_bytes=VMEM_LIMIT),
        cost_estimate=NO_COST,
        name="head",
    )(stream, segment[:, None], segment[None, :], labels.reshape(IMGS, 1), weight, vector)


def adam_update(gradient, moment, square, weight, factor, learn_rate):
    clipped = gradient * factor
    moment = BETA_ONE * moment + (1.0 - BETA_ONE) * clipped
    square = BETA_TWO * square + (1.0 - BETA_TWO) * clipped * clipped
    fixed_one = 1.0 - BETA_ONE**STEP
    fixed_two = 1.0 - BETA_TWO**STEP
    step_dir = (
        moment / fixed_one / (jnp.sqrt(square / fixed_two) + ADAM_EPS) + WEIGHT_DECAY * weight
    )
    return (moment, square, weight - learn_rate * step_dir)


def body(
    pixels,
    segment,
    patch_size,
    labels,
    patch_kernel,
    head_weight,
    input_proj,
    output_proj,
    layer_vector,
    position_table,
    global_vector,
    patch_moment,
    head_moment,
    input_moment,
    output_moment,
    layer_moment,
    position_moment,
    global_moment,
    patch_square,
    head_square,
    input_square,
    output_square,
    layer_square,
    position_square,
    global_square,
):
    owners = lax.axis_size("fsdp")
    nodes = position_table.shape[0]
    vector_size = layer_vector.size
    stream, pos_weights_t, vectors, qkv_weight, rides, rest_shards = begin(
        pixels,
        segment,
        patch_size,
        patch_kernel,
        layer_vector,
        input_proj,
        output_proj,
        head_weight,
        position_table,
        global_vector,
    )
    qkv_one, up_one, head_full = (
        lax.all_gather(shard, "fsdp", axis=0, tiled=True) for shard in rest_shards
    )
    saved_layers = []
    for index in range(LAYERS):
        vector = vectors[index]
        normed, qkv_rows = qkv_forward(stream, qkv_weight, vector)
        if index == 0:
            attended, expo, inverse, up, output, output_ride = attention_forward(
                qkv_rows, segment, rides, 4
            )
        else:
            attended, expo, inverse, output = attention_forward(qkv_rows, segment, [output_ride], 5)
            up = up_one
        residual, normed_second, active, slope, following = mlp_forward(
            stream, attended, up, output, vector
        )
        saved_layers.append(
            (
                (qkv_weight, up, output, vector),
                (stream, normed, qkv_rows, attended, expo, inverse),
                (residual, normed_second, active, slope),
            )
        )
        stream, qkv_weight = following, qkv_one
    stream_grad, head_grad, final_sums, head_bias_grad, numbers = head(
        stream, segment, labels, head_full, global_vector, head_weight.shape[1]
    )
    vector_grads = [None] * LAYERS
    early_parts, late_parts = [], []
    for index in reversed(range(LAYERS)):
        (qkv_weight, up, output, vector), first, second = saved_layers[index]
        entering, normed, qkv_rows, attended, expo, inverse = first
        residual, normed_second, active, slope = second
        grad_low, hidden_grad, residual_grad, residual_low, attended_grad, mlp_sums = mlp_backward(
            stream_grad, slope, residual, up, output, vector
        )
        output_grads = output_weight_grad(
            attended, active, residual_low, grad_low, (D // 2,) * 2 if index else (D,)
        )
        attended_grad, *output_grads = lax.optimization_barrier((attended_grad, *output_grads))
        up_grad = input_weight_grad(normed_second, hidden_grad)
        output_parts = [scatter(by_owner(grad)) for grad in output_grads]
        if index:
            early_parts.extend(output_parts)
            beside = [SumRide(by_owner(head_grad), False)]
        else:
            (last_part,) = output_parts
            beside = [ShareRide(jnp.concatenate(early_parts, 1)), SumRide(by_owner(up_grad), True)]
        qkv_grad, *beside_sums = attention_backward(
            qkv_rows, expo, inverse, attended, attended_grad, beside, 6 if index else 8
        )
        stream_grad, qkv_sums = qkv_backward(qkv_grad, residual_grad, entering, qkv_weight, vector)
        qkv_weight_grad = input_weight_grad(normed, qkv_grad)
        if index:
            (head_sum,) = beside_sums
            stream_grad, qkv_weight_grad, up_grad = lax.optimization_barrier(
                (stream_grad, qkv_weight_grad, up_grad)
            )
            late_parts.extend(scatter(by_owner(grad)) for grad in (qkv_weight_grad, up_grad))
        else:
            output_one_sum, up_zero_sum = beside_sums
        vector_grads[index] = jnp.concatenate(
            [
                qkv_sums[0, : 2 * D],
                mlp_sums[0, : 2 * D],
                qkv_sums[0, 2 * D :],
                mlp_sums[0, 2 * D :],
            ]
        )
    kernel_grad, position_grad, bias_grad = embed_backward(pixels, stream_grad, pos_weights_t)
    position_grad = position_grad[:nodes]
    vector_part = jnp.stack(vector_grads).reshape(LAYERS, owners, -1)
    vector_part = jnp.swapaxes(vector_part, 0, 1).reshape(owners, vector_size)
    vector_rows = -(-vector_size // LANES)
    vector_part = jnp.pad(vector_part, ((0, 0), (0, vector_rows * LANES - vector_size)))
    rest = jnp.concatenate(
        [
            position_grad.reshape(-1),
            bias_grad[0],
            final_sums[0],
            head_bias_grad[0, :CLS],
            numbers[0],
        ]
    )
    rest_rows = -(-rest.shape[0] // (owners * LANES))
    rest_part = jnp.pad(rest, (0, rest_rows * owners * LANES - rest.shape[0]))
    small = jnp.concatenate([vector_part, rest_part.reshape(owners, -1)], 1)
    used = vector_rows + rest_rows
    block_rows = (used // 64 + 1) * 64
    small = jnp.pad(small.reshape(owners, used, LANES), ((0, 0), (0, block_rows - used), (0, 0)))
    qkv_zero_sum, kernel_sum, small_share, *input_one_sums = reduce_all(
        [by_owner(qkv_weight_grad), by_owner(kernel_grad)], small, late_parts, 2
    )
    output_zero_sum, small_full, numbers = finish_all(
        [head_sum, output_one_sum, up_zero_sum, qkv_zero_sum, kernel_sum, *input_one_sums],
        small_share,
        [last_part],
        vector_rows,
        rest.shape[0],
        3,
    )
    factor, grad_norm, loss_sum, token_total = (numbers[0, index] for index in range(4))
    rest_sum = small_full[:, vector_rows:used].reshape(-1)
    position_sum = rest_sum[: position_grad.size].reshape(position_grad.shape)
    global_sum = rest_sum[position_grad.size :][: global_vector.shape[0]]
    kernel_sum = kernel_sum.astype(jnp.float32)
    head_sum = head_sum[:, :CLS].astype(jnp.float32)
    input_sum = jnp.stack(
        [jnp.concatenate(pair, 1) for pair in ((qkv_zero_sum, up_zero_sum), input_one_sums)]
    ).astype(jnp.float32)
    output_sum = jnp.stack([output_zero_sum, output_one_sum]).astype(
        jnp.float32
    )
    vector_sum = small_share[:vector_rows].reshape(-1)[:vector_size].reshape(layer_vector.shape)
    patch_next = adam_update(
        kernel_sum, patch_moment, patch_square, patch_kernel, factor, LEARN_RATE
    )
    head_next = adam_update(head_sum, head_moment, head_square, head_weight, factor, LEARN_RATE)
    input_next = adam_update(input_sum, input_moment, input_square, input_proj, factor, LEARN_RATE)
    output_next = adam_update(
        output_sum, output_moment, output_square, output_proj, factor, LEARN_RATE
    )
    layer_next = adam_update(
        vector_sum, layer_moment, layer_square, layer_vector, factor, VECTOR_RATE
    )
    position_next = adam_update(
        position_sum, position_moment, position_square, position_table, factor, LEARN_RATE
    )
    global_next = adam_update(
        global_sum, global_moment, global_square, global_vector, factor, VECTOR_RATE
    )
    return (
        loss_sum,
        token_total,
        grad_norm,
        patch_next[0],
        head_next[0],
        input_next[0],
        output_next[0],
        layer_next[0],
        position_next[0],
        global_next[0],
        patch_next[1],
        head_next[1],
        input_next[1],
        output_next[1],
        layer_next[1],
        position_next[1],
        global_next[1],
        patch_next[2],
        head_next[2],
        input_next[2],
        output_next[2],
        layer_next[2],
        position_next[2],
        global_next[2],
    )


def solution(mesh):
    in_specs = (
        P(("dp", "fsdp"), None),
        P(("dp", "fsdp")),
        P(("dp", "fsdp"), None),
        P(("dp", "fsdp"), None),
        P("fsdp", None),
        P("fsdp", None),
        P(None, "fsdp", None),
        P(None, "fsdp", None),
        P(None, "fsdp"),
        P(),
        P(),
        P("fsdp", None),
        P("fsdp", None),
        P(None, "fsdp", None),
        P(None, "fsdp", None),
        P(None, "fsdp"),
        P(),
        P(),
        P("fsdp", None),
        P("fsdp", None),
        P(None, "fsdp", None),
        P(None, "fsdp", None),
        P(None, "fsdp"),
        P(),
        P(),
    )
    out_specs = (
        P(),
        P(),
        P(),
        P("fsdp", None),
        P("fsdp", None),
        P(None, "fsdp", None),
        P(None, "fsdp", None),
        P(None, "fsdp"),
        P(),
        P(),
        P("fsdp", None),
        P("fsdp", None),
        P(None, "fsdp", None),
        P(None, "fsdp", None),
        P(None, "fsdp"),
        P(),
        P(),
        P("fsdp", None),
        P("fsdp", None),
        P(None, "fsdp", None),
        P(None, "fsdp", None),
        P(None, "fsdp"),
        P(),
        P(),
    )
    return jax.shard_map(body, mesh=mesh, in_specs=in_specs, out_specs=out_specs, check_vma=False)
```

```python
import functools

import jax
import jax.numpy as jnp
from jax import lax
from jax.experimental import pallas as pl
from jax.experimental.pallas import tpu as pltpu
from jax.sharding import PartitionSpec as P

D = 768
HEADS = 12
HD = 64
CLS = 1000
GRID = 7
IMG = 240
IMGS = 8
LAYERS = 2
STEP = 3


NORM_EPS = 1e-06
CLIP_NORM = 0.01
LEARN_RATE = 0.05
VECTOR_RATE = 0.25
BETA_ONE = 0.5
BETA_TWO = 0.5
ADAM_EPS = 1e-08
WEIGHT_DECAY = 0.05
HIGHEST = lax.Precision.HIGHEST

PAIR = 2 * HD
MASKED = -1e30
MIB = 1024 * 1024
VMEM_LIMIT = 56 * MIB
MESH = pl.DeviceIdType.MESH
LANES = 128
LOW = jnp.bfloat16
ANYWHERE = pl.BlockSpec(memory_space=pl.ANY)
NO_COST = pl.CostEstimate(flops=0, bytes_accessed=0, transcendentals=0)
ROOT = 0.7978845608028654
CUBE = 0.044715
NT = (((1,), (1,)), ((), ()))


def layer_norm(values, gain, shift):
    center = values - jnp.mean(values, -1, keepdims=True)
    spread = jnp.mean(center * center, -1, keepdims=True)
    return center * lax.rsqrt(spread + NORM_EPS) * gain + shift


def rounded(values):
    return lax.optimization_barrier(values.astype(jnp.bfloat16)).astype(jnp.float32)


def matmul(left, right):
    return jnp.dot(left, right, preferred_element_type=jnp.float32)


def padded_rows(flat, multiple):
    extra = -flat.shape[0] % (multiple * LANES)
    return jnp.pad(flat, (0, extra)).reshape(-1, LANES)


def row_layout(seg_row, patch_row):
    row_count = seg_row.shape[0]
    slots = jnp.arange(IMGS, dtype=jnp.int32)
    member = seg_row[:, None] == slots[None, :]
    counts = jnp.sum(member.astype(jnp.int32), 0, dtype=jnp.int32)
    starts = jnp.cumsum(counts, dtype=jnp.int32) - counts
    inside = jnp.any(member, 1)
    offset = jnp.arange(row_count, dtype=jnp.int32) - jnp.sum(
        jnp.where(member, starts[None, :], 0), 1, dtype=jnp.int32
    )
    offset = jnp.where(inside, offset, 0)
    patch_tok = jnp.sum(jnp.where(member, patch_row[None, :], 0), 1, dtype=jnp.int32) + jnp.where(
        inside, 0, IMG
    )
    side = IMG // patch_tok
    nodes = jnp.arange(GRID, dtype=jnp.int32).astype(jnp.float32)

    def hat(coord):
        place = ((2 * coord + 1) * GRID).astype(jnp.float32) / (2 * side).astype(jnp.float32) - 0.5
        place = jnp.clip(place, 0.0, GRID - 1.0)
        return jnp.maximum(1.0 - jnp.abs(place[:, None] - nodes[None, :]), 0.0)

    weights = (hat(offset // side)[:, :, None] * hat(offset % side)[:, None, :]).reshape(
        row_count, GRID * GRID
    )
    return (weights, member.astype(jnp.float32), counts.astype(jnp.float32))


TURNS = (1, 2, 3)


def place():
    slot = lax.axis_index("fsdp")
    return lax.axis_index("dp"), lax.div(slot, 2), lax.rem(slot, 2)


def partner(index, turn):
    if turn == 0:
        return index
    if turn == 1:
        return index + 1 - 2 * lax.rem(index, 2)
    if turn == 2:
        return lax.rem(index + 2, 4)
    return 3 - index


def greet():
    group, level, core = place()
    barrier = pltpu.get_barrier_semaphore()
    peers = [(group, 2 * level + 1 - core)]
    for turn in TURNS:
        peers.append((group, 2 * partner(level, turn) + core))
        peers.append((partner(group, turn), 2 * level + core))
    for peer in peers:
        pl.semaphore_signal(barrier, inc=1, device_id=peer, device_id_type=MESH)
    pl.semaphore_wait(barrier, len(peers))


def quarter_shape(rows, columns):
    if columns % (2 * LANES) == 0:
        return rows // 2, columns // 2
    return rows // 4, columns


def quarter(index, rows, columns):
    high, wide = quarter_shape(rows, columns)
    if wide == columns:
        return pl.ds(pl.multiple_of(index * high, high), high), pl.ds(0, columns)
    return (
        pl.ds(pl.multiple_of(lax.div(index, 2) * high, high), high),
        pl.ds(pl.multiple_of(lax.rem(index, 2) * wide, wide), wide),
    )


def remote(source, target, send, receive, device):
    return pltpu.make_async_remote_copy(
        src_ref=source,
        dst_ref=target,
        send_sem=send,
        recv_sem=receive,
        device_id=device,
        device_id_type=MESH,
    )


GATHER_SEMS = 39


def relay_rows(part, rows):
    cut = -(-rows // 32) * 16
    return (0, cut) if part == 0 else (cut, rows - cut)


class Relay:
    def region(self, turn, index):
        _, level, core = place()
        block = self.out.at[2 * partner(level, turn) + core]
        return block.at[quarter(index, *self.shard.shape)]

    def group_copy(self, turn, other):
        group, level, core = place()
        index = self.group_at + 2 * (turn - 1) + other - 1
        peer = (partner(group, other), 2 * level + core)
        target = self.region(turn, group)
        source = self.quarter_source(turn, target)
        return remote(source, target, self.sems.at[index], self.sems.at[index + 6], peer)

    def relay_copy(self, turn, part):
        group, level, core = place()
        first, count = relay_rows(part, quarter_shape(*self.shard.shape)[0])
        block = self.region(turn, partner(group, 1 + part)).at[pl.ds(first, count)]
        index = self.relay_at + 2 * (turn - 1) + part
        peer = (partner(group, 2 - part), 2 * level + core)
        return remote(block, block, self.sems.at[index], self.sems.at[index + 6], peer)

    def relay(self):
        for turn in TURNS:
            for part in range(2):
                self.group_copy(turn, 1 + part).wait_recv()
                self.relay_copy(turn, part).start()

    def wait_quarters(self, turn):
        for part in range(2):
            self.relay_copy(turn, part).wait_recv()

    def wait_passed(self):
        for turn in TURNS:
            for part in range(2):
                self.group_copy(turn, 1 + part).wait_send()
                self.relay_copy(turn, part).wait_send()


class Gather(Relay):
    group_at, relay_at = 7, 19

    def __init__(self, shard, out, sems, split, in_place=False):
        self.shard, self.out, self.sems, self.split = shard, out, sems, split
        self.in_place = in_place
        self.rows, self.columns = shard.shape

    def quarter_source(self, turn, target):
        return target

    def level_copy(self, turn):
        group, level, core = place()
        block = self.out.at[2 * level + core]
        source = self.shard
        if self.split:
            part = quarter(group, self.rows, self.columns)
            source, block = source.at[part], block.at[part]
        peer = (group, 2 * partner(level, turn) + core)
        return remote(source, block, self.sems.at[turn], self.sems.at[3 + turn], peer)

    def core_copy(self, turn):
        group, level, core = place()
        slot = 2 * partner(level, turn) + core
        source = self.shard if turn == 0 else self.out.at[slot]
        peer = (group, 2 * level + 1 - core)
        return remote(source, self.out.at[slot], self.sems.at[31 + turn], self.sems.at[35 + turn], peer)

    def own_copy(self):
        _, level, core = place()
        return pltpu.make_async_copy(self.shard, self.out.at[2 * level + core], self.sems.at[0])

    def first(self):
        for turn in TURNS:
            self.level_copy(turn).start()
        self.core_copy(0).start()
        if not self.in_place:
            self.own_copy().start()

    def second(self):
        for turn in TURNS:
            self.level_copy(turn).wait_recv()
            if self.split:
                for other in (1, 2):
                    self.group_copy(turn, other).start()
            else:
                self.core_copy(turn).start()

    def third(self, use=None):
        for turn in TURNS if self.split else ():
            self.wait_quarters(turn)
            self.core_copy(turn).start()
            if use is not None:
                use(turn, True)

    def fourth(self, use=None):
        for turn in TURNS if use is not None else (0, *TURNS):
            self.core_copy(turn).wait_recv()
            if use is not None:
                use(turn, False)
        for turn in TURNS:
            self.level_copy(turn).wait_send()
        if self.split:
            self.wait_passed()
        for turn in (0, *TURNS):
            self.core_copy(turn).wait_send()
        if not self.in_place:
            self.own_copy().wait()


class LevelGather:
    def __init__(self, shard, out, sems):
        self.shard, self.out, self.sems = shard, out, sems

    def level_copy(self, turn):
        group, level, core = place()
        return remote(
            self.shard.at[quarter(group, *self.shard.shape)],
            self.out.at[level],
            self.sems.at[turn],
            self.sems.at[3 + turn],
            (group, 2 * partner(level, turn) + core),
        )

    def first(self):
        for turn in TURNS:
            self.level_copy(turn).start()

    def second(self):
        pass

    def third(self):
        pass

    def fourth(self):
        for turn in TURNS:
            self.level_copy(turn).wait_recv()
            self.level_copy(turn).wait_send()

    def store(self):
        _, level, _ = place()
        self.out[level] = jnp.zeros(self.out.shape[1:], self.out.dtype)
        self.target[...] = self.out[...]


GROUP_GATHER_SEMS = 36


class GroupGather(Relay):
    group_at, relay_at = 4, 16

    def __init__(self, shard, quarters, out, sems):
        self.shard, self.quarters, self.out, self.sems = shard, quarters, out, sems

    def quarter_source(self, turn, target):
        _, level, _ = place()
        return self.quarters.at[partner(level, turn)]

    def own_copy(self, turn):
        group, level, core = place()
        if turn == 0:
            source, target = self.shard, self.out.at[2 * level + core]
        else:
            source, target = self.quarters.at[partner(level, turn)], self.region(turn, group)
        return pltpu.make_async_copy(source, target, self.sems.at[turn])

    def core_copy(self, turn):
        group, level, core = place()
        slot = 2 * partner(level, turn) + core
        source = self.shard if turn == 0 else self.out.at[slot]
        peer = (group, 2 * level + 1 - core)
        return remote(source, self.out.at[slot], self.sems.at[28 + turn], self.sems.at[32 + turn], peer)

    def first(self):
        for turn in TURNS:
            for other in (1, 2):
                self.group_copy(turn, other).start()
        for turn in (0, *TURNS):
            self.own_copy(turn).start()
        self.core_copy(0).start()

    def third(self):
        for turn in TURNS:
            self.wait_quarters(turn)
            self.own_copy(turn).wait()
            self.core_copy(turn).start()

    def fourth(self):
        for turn in (0, *TURNS):
            self.core_copy(turn).wait_recv()
            self.core_copy(turn).wait_send()
        self.wait_passed()
        self.own_copy(0).wait()

    def store(self):
        copy = pltpu.make_async_copy(self.out, self.target, self.sems.at[0])
        copy.start()
        copy.wait()


class LevelRide:
    def __init__(self, shard):
        self.operands = [shard]
        self.in_specs = [fixed(*shard.shape)]
        shape = (4, *quarter_shape(*shard.shape))
        self.out_specs = [fixed(*shape)]
        self.out_shapes = [jax.ShapeDtypeStruct(shape, shard.dtype)]
        self.scratch = [pltpu.VMEM(shape, shard.dtype), pltpu.SemaphoreType.DMA((7,))]

    def job(self, sources, targets, scratch):
        job = LevelGather(sources[0], *scratch)
        job.target = targets[0]
        return job

    def before(self, steps):
        return {0: ("first",)}

    after = ("fourth", "store")

    def result(self, outs):
        return GatherRide(self.operands[0], outs[0])

    def plain(self):
        return GatherRide(self.operands[0], self.operands[0])


class GatherRide:
    def __init__(self, shard, quarters):
        owners = lax.axis_size("fsdp")
        full = (owners, *shard.shape)
        self.operands = [shard, quarters]
        self.in_specs = [fixed(*shard.shape), fixed(*quarters.shape)]
        self.out_specs = [ANYWHERE]
        self.out_shapes = [jax.ShapeDtypeStruct(full, shard.dtype)]
        self.scratch = [
            pltpu.VMEM(full, shard.dtype),
            pltpu.SemaphoreType.DMA((GROUP_GATHER_SEMS,)),
        ]

    def job(self, sources, targets, scratch):
        job = GroupGather(*sources, *scratch)
        job.target = targets[0]
        return job

    def before(self, steps):
        return {0: ("first",), steps // 2: ("relay",), steps - 1: ("third",)}

    after = ("fourth", "store")

    def result(self, outs):
        return outs[0].reshape(-1, outs[0].shape[2])

    def plain(self):
        return lax.all_gather(self.operands[0], "fsdp", axis=0, tiled=True)


class ShareRide:
    def __init__(self, share):
        self.operands = [share]
        self.in_specs = [ANYWHERE]
        self.out_specs = [fixed(*share.shape)]
        self.out_shapes = [jax.ShapeDtypeStruct(share.shape, share.dtype)]
        self.scratch = [
            pltpu.VMEM(share.shape, share.dtype),
            *share_scratch(share),
            pltpu.SemaphoreType.DMA((GROUP_SEMS,)),
        ]

    def job(self, sources, targets, scratch):
        job = GroupReduce(sources[0], scratch[0], scratch[1:3], scratch[3])
        job.target = targets[0]
        return job

    def before(self, steps):
        return {0: ("first", "second"), max(1, steps // 2): ("third",)}

    after = ("fifth", "sixth", "store")

    def result(self, outs):
        return outs[0]

    def plain(self):
        return lax.psum(self.operands[0], "dp")


class SumRide:
    def __init__(self, grad, large):
        block = grad.shape[1:]
        self.large = large
        self.operands = [grad]
        self.in_specs = [ANYWHERE]
        self.out_specs = [fixed(*block)]
        self.out_shapes = [jax.ShapeDtypeStruct(block, grad.dtype)]
        buffers = stepped_scratch(grad) if large else whole_scratch(grad)
        sems = WHOLE_SEMS if large else REDUCE_SEMS
        self.scratch = [pltpu.VMEM(block, grad.dtype), *buffers, pltpu.SemaphoreType.DMA((sems,))]

    def job(self, sources, targets, scratch):
        job = (Whole if self.large else Reduce)(sources[0], scratch[0], scratch[1:-1], scratch[-1])
        job.target = targets[0]
        return job

    def before(self, steps):
        if self.large:
            return {0: ("first",), 1: ("second",), steps - 2: ("between",), steps - 1: ("third",)}
        return {0: ("first",), 1: ("second",), steps // 2: ("third",), steps - 1: ("fourth",)}

    @property
    def after(self):
        return (("fourth",) if self.large else ()) + ("fifth", "sixth", "store")

    def result(self, outs):
        return outs[0]

    def plain(self):
        return lax.psum(scatter(self.operands[0]), "dp")


def riding(body, counts, rides, steps):
    def kernel(*refs):
        refs = list(refs)

        def pop(count):
            taken = refs[:count]
            del refs[:count]
            return taken

        own = pop(counts[0])
        sources = [pop(len(ride.operands)) for ride in rides]
        own += pop(counts[1])
        targets = [pop(len(ride.out_shapes)) for ride in rides]
        own += pop(counts[2])
        jobs = [
            ride.job(source, target, pop(len(ride.scratch)))
            for ride, source, target in zip(rides, sources, targets)
        ]
        for step in range(steps):
            planned = [
                (job, stages)
                for ride, job in zip(rides, jobs)
                for at, stages in ride.before(steps).items()
                if at == step
            ]
            if planned:

                @pl.when(pl.program_id(0) == step)
                def _(planned=planned, step=step):
                    if step == 0:
                        greet()
                    for job, stages in planned:
                        run_stages([job], stages)

        body(*own)

        @pl.when(pl.program_id(0) == steps - 1)
        def _():
            for ride, job in zip(rides, jobs):
                run_stages([job], ride.after)

    return kernel


def block_call(
    body, grid, in_specs, operands, out_specs, out_shape, scratch, name,
    cost=None, rides=(), collective_id=None,
):
    plain = []
    if rides and not with_kernels():
        plain, rides = [ride.plain() for ride in rides], ()
    transfer = {}
    kernel = body
    if rides:
        transfer = {"collective_id": collective_id, "has_side_effects": True}
        kernel = riding(body, (len(operands), len(out_shape), len(scratch)), rides, grid)
    count = len(out_shape)
    for ride in rides:
        operands = [*operands, *ride.operands]
        in_specs = [*in_specs, *ride.in_specs]
        out_specs, out_shape = [*out_specs, *ride.out_specs], [*out_shape, *ride.out_shapes]
        scratch = [*scratch, *ride.scratch]
    outs = pl.pallas_call(
        kernel,
        grid=(grid,),
        in_specs=in_specs,
        out_specs=out_specs,
        out_shape=out_shape,
        scratch_shapes=scratch,
        compiler_params=pltpu.CompilerParams(vmem_limit_bytes=VMEM_LIMIT, **transfer),
        cost_estimate=cost or NO_COST,
        name=name,
    )(*operands)
    brought, outs = list(outs[count:]), list(outs[:count])
    for ride in rides:
        plain.append(ride.result(brought[: len(ride.out_shapes)]))
        brought = brought[len(ride.out_shapes) :]
    return outs + plain


def work(flops, size):
    return pl.CostEstimate(flops=flops, bytes_accessed=size, transcendentals=0)


def position_weights(seg_col, patch_row, nodes):
    rows = seg_col.shape[0]
    slot = lax.broadcasted_iota(jnp.int32, (rows, IMGS), 1)
    member = seg_col == slot
    counts = jnp.sum(member.astype(jnp.float32), 0, keepdims=True)
    start = jnp.sum(jnp.where(slot < seg_col, counts, 0.0), 1, keepdims=True)
    token = lax.broadcasted_iota(jnp.int32, (rows, 1), 0).astype(jnp.float32)
    inside = seg_col < IMGS
    offset = jnp.where(inside, token - start, 0.0)
    patch = jnp.sum(jnp.where(member, patch_row.astype(jnp.float32), 0.0), 1, keepdims=True)
    side = jnp.where(inside, jnp.floor(IMG / jnp.where(inside, patch, 1.0) + 0.5), 1.0)
    line = jnp.floor((offset + 0.5) / side)
    column = offset - line * side

    def spot(coord):
        return jnp.clip((2.0 * coord + 1.0) * GRID / (2.0 * side) - 0.5, 0.0, GRID - 1.0)

    node = lax.broadcasted_iota(jnp.int32, (rows, LANES), 1).astype(jnp.float32)
    across = jnp.floor((node + 0.5) / GRID)
    along = node - across * GRID
    weights = jnp.maximum(1.0 - jnp.abs(spot(line) - across), 0.0)
    weights = weights * jnp.maximum(1.0 - jnp.abs(spot(column) - along), 0.0)
    return jnp.where(node < nodes, weights, 0.0)


def first_kernel(*refs, spots):
    kernel, vectors, inputs, outputs, head, pixels, seg_col, patch_row, table, biases = refs[:10]
    stream, pos_t, vector_zero, vector_one = refs[10:14]
    qkv_full, up_full, output_level = refs[14:17]
    output_zero, qkv_one, up_one, output_one, head_low = refs[17:22]
    wide_kernel, wide_inputs, wide_outputs, wide_head, pixel_rows, table_low = refs[22:28]
    kernel_full, qkv_zero, vectors_full, qkv_landing, up_landing, output_landing = refs[28:34]
    up_zero, load_sems, sems = refs[34:]
    _, level, core = place()
    mine = 2 * level + core
    pairs = [
        (kernel, wide_kernel),
        (inputs.at[0], wide_inputs.at[0]),
        (pixels, pixel_rows),
        (inputs.at[1], wide_inputs.at[1]),
        (outputs.at[0], wide_outputs.at[0]),
        (outputs.at[1], wide_outputs.at[1]),
        (head, wide_head),
    ]
    copies = [
        pltpu.make_async_copy(source, target, load_sems.at[index])
        for index, (source, target) in enumerate(pairs)
    ]
    for copy in copies:
        copy.start()
    patch_job = Gather(kernel_full.at[mine], kernel_full, sems.at[0], True, in_place=True)
    vector_job = Gather(vectors, vectors_full, sems.at[1], False)
    qkv_job = Gather(qkv_zero, qkv_landing, sems.at[2], True)
    up_job = Gather(up_zero, up_landing, sems.at[3], True)
    output_job = LevelGather(output_zero, output_landing, sems.at[4])
    output_job.target = output_level
    copies[0].wait()
    kernel_full[mine] = wide_kernel[...].astype(LOW)
    greet()
    patch_job.first()
    vector_job.first()
    copies[1].wait()
    qkv_zero[...] = wide_inputs[0, :, : 3 * D].astype(LOW)
    qkv_job.first()
    up_zero[...] = wide_inputs[0, :, 3 * D :].astype(LOW)
    up_job.first()
    copies[4].wait()
    output_zero[...] = wide_outputs[0].astype(LOW)
    output_job.first()

    weights = position_weights(seg_col[...], patch_row[...], table.shape[0])
    pos_t[...] = weights.T[: pos_t.shape[0], :]
    table_low[...] = jnp.zeros_like(table_low)
    table_low[: table.shape[0], :] = table[...].astype(LOW).astype(jnp.float32)
    bias = biases[:, :D].astype(LOW).astype(jnp.float32)
    stream[...] = bias + jnp.dot(
        weights, table_low[...], precision=HIGHEST, preferred_element_type=jnp.float32
    )
    copies[2].wait()
    depth = wide_kernel.shape[0]

    def add_block(slot):
        columns = pl.ds(pl.multiple_of(slot * depth, depth), depth)

        def add(step, carry):
            rows = pl.ds(pl.multiple_of(step * 256, 256), 256)
            stream[rows, :] += mul(pixel_rows[rows, columns], kernel_full[slot])
            return carry

        lax.fori_loop(0, stream.shape[0] // 256, add, 0)

    def use(turn, own_core):
        add_block(2 * partner(level, turn) + (core if own_core else 1 - core))

    add_block(mine)
    patch_job.second()
    vector_job.second()
    qkv_job.second()
    up_job.second()
    patch_job.core_copy(0).wait_recv()
    use(0, False)
    copies[3].wait()
    qkv_one[...] = wide_inputs[1, :, : 3 * D].astype(LOW)
    up_one[...] = wide_inputs[1, :, 3 * D :].astype(LOW)
    copies[5].wait()
    output_one[...] = wide_outputs[1].astype(LOW)
    copies[6].wait()
    head_low[...] = jnp.zeros_like(head_low)
    head_low[:, : head.shape[1]] = wide_head[...].astype(LOW)
    patch_job.relay()
    qkv_job.relay()
    patch_job.third(use)
    up_job.relay()
    qkv_job.third()
    patch_job.fourth(use)
    vector_job.third()
    vector_job.fourth()
    blocks = [vectors_full[slot].astype(jnp.float32) for slot in range(vectors_full.shape[0])]
    span = vectors.shape[0] // LAYERS
    for layer, out in enumerate((vector_zero, vector_one)):
        for row in range(out.shape[1] // LANES):
            parts = [
                block[layer * span + row - spot : layer * span + row - spot + 1, :]
                for block, spot in zip(blocks, spots)
                if 0 <= row - spot < span
            ]
            out[:, row * LANES : (row + 1) * LANES] = sum(parts)
    up_job.third()
    qkv_job.fourth()
    copy = pltpu.make_async_copy(qkv_landing, qkv_full, load_sems.at[0])
    copy.start()
    up_job.fourth()
    up_copy = pltpu.make_async_copy(up_landing, up_full, load_sems.at[1])
    up_copy.start()
    run_stages([output_job], ("fourth", "store"))
    copy.wait()
    up_copy.wait()


def padded_vectors(shard):
    layers, width = shard.shape
    owners = lax.axis_size("fsdp")
    spots = [owner * width // LANES for owner in range(owners)]
    span = max(-(-(owner + 1) * width // LANES) - spot for owner, spot in enumerate(spots))
    span += -span % 16
    shift = lax.rem(lax.axis_index("fsdp") * width, LANES)
    padded = jnp.zeros((layers, span * LANES), LOW)
    padded = lax.dynamic_update_slice(padded, shard.astype(LOW), (0, shift))
    return padded.reshape(layers * span, LANES), spots


def begin(
    pixels, segment, patch_size, patch_kernel, layer_vector, input_proj, output_proj, head_weight,
    position_table, global_vector,
):
    classes = head_weight.shape[1] + -head_weight.shape[1] % LANES
    nodes = position_table.shape[0] + -position_table.shape[0] % 64
    if not with_kernels():
        inputs = [
            (input_proj[index, :, : 3 * D].astype(LOW), input_proj[index, :, 3 * D :].astype(LOW))
            for index in range(LAYERS)
        ]
        outputs = [output_proj[index].astype(LOW) for index in range(LAYERS)]
        gather = lambda shard, axis: lax.all_gather(shard, "fsdp", axis=axis, tiled=True)
        weights, _, _ = row_layout(segment, patch_size[0])
        weights = jnp.pad(weights, ((0, 0), (0, nodes - weights.shape[1])))
        table = jnp.pad(rounded(position_table), ((0, nodes - position_table.shape[0]), (0, 0)))
        bias = rounded(global_vector)[None, :D]
        stream = embed(pixels, gather(patch_kernel.astype(LOW), 0), weights, table, bias)
        vectors = gather(layer_vector.astype(LOW), 1).astype(jnp.float32)
        head = jnp.pad(head_weight.astype(LOW), ((0, 0), (0, classes - head_weight.shape[1])))
        return (
            stream,
            weights.T,
            [vectors[index : index + 1] for index in range(LAYERS)],
            gather(inputs[0][0], 0),
            gather(inputs[0][1], 0),
            [GatherRide(outputs[0], outputs[0]), LevelRide(outputs[1])],
            [*inputs[1], head],
        )
    rows = pixels.shape[0]
    owners = lax.axis_size("fsdp")
    vectors, spots = padded_vectors(layer_vector)
    depth = input_proj.shape[1]
    up_shape = (depth, input_proj.shape[2] - 3 * D)
    qkv_shape, out_shape = (depth, 3 * D), output_proj.shape[1:]
    low = lambda *shape: jax.ShapeDtypeStruct(shape, LOW)
    levels = lambda shape: low(4, *quarter_shape(*shape))
    width = layer_vector.shape[1] * owners
    shapes = [
        shape_of(rows, D),
        shape_of(nodes, rows),
        shape_of(1, width),
        shape_of(1, width),
        low(owners, *qkv_shape),
        low(owners, *up_shape),
        levels(out_shape),
        low(*out_shape),
        low(*qkv_shape),
        low(*up_shape),
        low(*out_shape),
        low(head_weight.shape[0], classes),
    ]
    wide = (patch_kernel, input_proj, output_proj, head_weight, pixels)
    in_vmem = pl.BlockSpec(memory_space=pltpu.VMEM)
    results = pl.pallas_call(
        functools.partial(first_kernel, spots=spots),
        in_specs=[ANYWHERE] * 6 + [in_vmem] * 4,
        out_specs=[in_vmem] * 4 + [ANYWHERE] * 2 + [in_vmem] * 6,
        out_shape=shapes,
        scratch_shapes=[
            *[pltpu.VMEM(array.shape, array.dtype) for array in wide],
            pltpu.VMEM((LANES, D), jnp.float32),
            pltpu.VMEM((owners, *patch_kernel.shape), LOW),
            pltpu.VMEM(qkv_shape, LOW),
            pltpu.VMEM((owners, *vectors.shape), LOW),
            pltpu.VMEM((owners, *qkv_shape), LOW),
            pltpu.VMEM((owners, *up_shape), LOW),
            pltpu.VMEM((4, *quarter_shape(*out_shape)), LOW),
            pltpu.VMEM(up_shape, LOW),
            pltpu.SemaphoreType.DMA((7,)),
            pltpu.SemaphoreType.DMA((5, GATHER_SEMS)),
        ],
        compiler_params=pltpu.CompilerParams(
            collective_id=1, has_side_effects=True, vmem_limit_bytes=VMEM_LIMIT
        ),
        cost_estimate=NO_COST,
        name="begin",
    )(
        patch_kernel,
        vectors,
        input_proj,
        output_proj,
        head_weight,
        pixels,
        segment[:, None],
        patch_size,
        position_table,
        global_vector[None, :],
    )
    output_zero, qkv_one, up_one, output_one, head_low = results[7:]
    return (
        results[0],
        results[1],
        results[2:4],
        results[4].reshape(owners * depth, 3 * D),
        results[5].reshape(owners * depth, up_shape[1]),
        [GatherRide(output_zero, results[6]), LevelRide(output_one)],
        [qkv_one, up_one, head_low],
    )


REDUCE_SEMS = 52


class Reduce:
    def __init__(self, grad, out, scratch, sems):
        self.grad, self.out, self.sems = grad, out, sems
        self.own, self.away, self.got_core, self.got_group, self.part, self.got_level = scratch
        self.rows, self.columns = out.shape
        self.chunk = 16

    def load(self, level):
        _, _, core = place()
        return pltpu.make_async_copy(
            self.grad.at[2 * level + core], self.own.at[level], self.sems.at[level]
        )

    def load_away(self, level):
        _, _, core = place()
        return pltpu.make_async_copy(
            self.grad.at[2 * level + 1 - core], self.away.at[level], self.sems.at[48 + level]
        )

    def core_copy(self, target_level):
        group, level, core = place()
        return remote(
            self.away.at[target_level],
            self.got_core.at[target_level],
            self.sems.at[4 + target_level],
            self.sems.at[8 + target_level],
            (group, 2 * level + 1 - core),
        )

    def group_copy(self, turn, other):
        group, level, core = place()
        target = partner(level, turn)
        peer = partner(group, other)
        part = quarter(peer, self.rows, self.columns)
        index = 3 * turn + other - 1
        return remote(
            self.own.at[target].at[part],
            self.got_group.at[other - 1, target],
            self.sems.at[12 + index],
            self.sems.at[24 + index],
            (peer, 2 * level + core),
        )

    def level_copy(self, turn):
        group, level, core = place()
        target = partner(level, turn)
        return remote(
            self.part.at[target],
            self.got_level.at[turn - 1],
            self.sems.at[35 + turn],
            self.sems.at[38 + turn],
            (group, 2 * target + core),
        )

    def share_copy(self, other):
        group, level, core = place()
        mine = self.out.at[quarter(group, self.rows, self.columns)]
        return remote(
            mine,
            mine,
            self.sems.at[41 + other],
            self.sems.at[44 + other],
            (partner(group, other), 2 * level + core),
        )

    def first(self):
        _, level, _ = place()
        for turn in (*TURNS, 0):
            self.load_away(partner(level, turn)).start()
        for turn in (*TURNS, 0):
            self.load(partner(level, turn)).start()
        for turn in (*TURNS, 0):
            self.load_away(partner(level, turn)).wait()
            self.core_copy(partner(level, turn)).start()

    def second(self):
        _, level, _ = place()
        for turn in (*TURNS, 0):
            target = partner(level, turn)
            self.load(target).wait()
            self.core_copy(target).wait_recv()

            def add(step, carry):
                rows = pl.ds(pl.multiple_of(step * self.chunk, self.chunk), self.chunk)
                total = self.own[target, rows, :].astype(jnp.float32)
                total = total + self.got_core[target, rows, :].astype(jnp.float32)
                self.own[target, rows, :] = total.astype(self.own.dtype)
                return carry

            lax.fori_loop(0, self.rows // self.chunk, add, 0)
            for other in TURNS:
                self.group_copy(turn, other).start()

    def between(self):
        pass

    def third(self):
        group, level, _ = place()
        high, wide = quarter_shape(self.rows, self.columns)
        row_part, column_part = quarter(group, self.rows, self.columns)
        for turn in (*TURNS, 0):
            target = partner(level, turn)
            for other in TURNS:
                self.group_copy(turn, other).wait_recv()

            def add(step, carry):
                at = pl.multiple_of(step * self.chunk, self.chunk)
                rows = pl.ds(at, self.chunk)
                mine = pl.ds(pl.multiple_of(row_part.start + at, self.chunk), self.chunk)
                total = self.own[target, mine, column_part].astype(jnp.float32)
                for slot in range(3):
                    total = total + self.got_group[slot, target, rows, :].astype(jnp.float32)
                self.part[target, rows, :] = total.astype(self.part.dtype)
                return carry

            lax.fori_loop(0, high // self.chunk, add, 0)
            if turn:
                self.level_copy(turn).start()

    def fourth(self):
        group, level, _ = place()
        high, wide = quarter_shape(self.rows, self.columns)
        row_part, column_part = quarter(group, self.rows, self.columns)
        for turn in TURNS:
            self.level_copy(turn).wait_recv()

        def add(step, carry):
            at = pl.multiple_of(step * self.chunk, self.chunk)
            rows = pl.ds(at, self.chunk)
            mine = pl.ds(pl.multiple_of(row_part.start + at, self.chunk), self.chunk)
            total = self.part[level, rows, :].astype(jnp.float32)
            for slot in range(3):
                total = total + self.got_level[slot, rows, :].astype(jnp.float32)
            self.out[mine, column_part] = total.astype(self.out.dtype)
            return carry

        lax.fori_loop(0, high // self.chunk, add, 0)
        for other in TURNS:
            self.share_copy(other).start()

    def store(self):
        self.target[...] = self.out[...]

    def fifth(self):
        for other in TURNS:
            self.share_copy(other).wait_recv()

    def sixth(self):
        _, level, _ = place()
        for turn in (*TURNS, 0):
            self.core_copy(partner(level, turn)).wait_send()
            for other in TURNS:
                self.group_copy(turn, other).wait_send()
            if turn:
                self.level_copy(turn).wait_send()
                self.share_copy(turn).wait_send()


WHOLE_SEMS = 44


def add_rows(target, row, columns, source, count, wide):
    chunk = 16 if wide > 1536 else 48

    def add(step, carry):
        at = pl.multiple_of(step * chunk, chunk)
        mine = pl.ds(pl.multiple_of(row + at, 16), chunk)
        total = target[mine, columns].astype(jnp.float32)
        total = total + source[pl.ds(at, chunk), :].astype(jnp.float32)
        target[mine, columns] = total.astype(target.dtype)
        return carry

    lax.fori_loop(0, count // chunk, add, 0)


class Whole:
    FIRST_X = (1, 0)

    def __init__(self, grad, out, scratch, sems):
        self.grad, self.out, self.sems = grad, out, sems
        self.own, self.away, self.got_core, self.got_x, self.got_y, self.got_last, self.part, self.got_level = scratch
        self.rows, self.columns = out.shape
        self.high, self.wide = self.rows // 2, self.columns // 2

    def row_half(self, index):
        return pl.ds(pl.multiple_of(lax.div(index, 2) * self.high, self.high), self.high)

    def column_half(self, index):
        return pl.ds(pl.multiple_of(lax.rem(index, 2) * self.wide, self.wide), self.wide)

    def load(self, level):
        _, _, core = place()
        return pltpu.make_async_copy(
            self.grad.at[2 * level + core], self.own.at[level], self.sems.at[level]
        )

    def load_away(self, level):
        _, _, core = place()
        return pltpu.make_async_copy(
            self.grad.at[2 * level + 1 - core], self.away.at[level], self.sems.at[40 + level]
        )

    def core_copy(self, target_level):
        group, level, core = place()
        return remote(
            self.away.at[target_level],
            self.got_core.at[target_level],
            self.sems.at[4 + target_level],
            self.sems.at[8 + target_level],
            (group, 2 * level + 1 - core),
        )

    def step_copy(self, turn):
        group, level, core = place()
        block = self.own.at[partner(level, turn)]
        if turn in self.FIRST_X:
            peer = partner(group, 1)
            source = block.at[:, self.column_half(peer)]
            target = self.got_x.at[self.FIRST_X.index(turn)]
        else:
            peer = partner(group, 2)
            source = block.at[self.row_half(peer), :]
            target = self.got_y.at[turn - 2]
        return remote(
            source, target, self.sems.at[12 + turn], self.sems.at[16 + turn], (peer, 2 * level + core)
        )

    def last_copy(self, turn):
        group, level, core = place()
        block = self.own.at[partner(level, turn)]
        peer = partner(group, 2 if turn in self.FIRST_X else 1)
        rows = self.row_half(peer)
        columns = self.column_half(peer)
        return remote(
            block.at[rows, columns],
            self.got_last.at[turn],
            self.sems.at[20 + turn],
            self.sems.at[24 + turn],
            (peer, 2 * level + core),
        )

    def level_copy(self, turn):
        group, level, core = place()
        target = partner(level, turn)
        return remote(
            self.part.at[target],
            self.got_level.at[turn - 1],
            self.sems.at[27 + turn],
            self.sems.at[30 + turn],
            (group, 2 * target + core),
        )

    def share_copy(self, other):
        group, level, core = place()
        mine = self.out.at[self.row_half(group), self.column_half(group)]
        return remote(
            mine,
            mine,
            self.sems.at[33 + other],
            self.sems.at[36 + other],
            (partner(group, other), 2 * level + core),
        )

    def first(self):
        _, level, _ = place()
        for turn in (*TURNS, 0):
            self.load_away(partner(level, turn)).start()
        for turn in (*TURNS, 0):
            self.load(partner(level, turn)).start()
        for turn in (*TURNS, 0):
            self.load_away(partner(level, turn)).wait()
            self.core_copy(partner(level, turn)).start()

    def second(self):
        _, level, _ = place()
        for turn in (*TURNS, 0):
            target = partner(level, turn)
            self.load(target).wait()
            self.core_copy(target).wait_recv()
            add_rows(
                self.own.at[target], 0, slice(None), self.got_core.at[target], self.rows, self.columns
            )
            self.step_copy(turn).start()

    def between(self):
        group, level, _ = place()
        for turn in (*TURNS, 0):
            block = self.own.at[partner(level, turn)]
            self.step_copy(turn).wait_recv()
            if turn in self.FIRST_X:
                source = self.got_x.at[self.FIRST_X.index(turn)]
                add_rows(block, 0, self.column_half(group), source, self.rows, self.wide)
            else:
                source = self.got_y.at[turn - 2]
                start = lax.div(group, 2) * self.high
                add_rows(block, start, slice(None), source, self.high, self.columns)
            self.last_copy(turn).start()

    def third(self):
        group, level, _ = place()
        start = lax.div(group, 2) * self.high
        columns = self.column_half(group)
        chunk = 16 if self.wide > 1536 else 48
        for turn in (*TURNS, 0):
            target = partner(level, turn)
            self.last_copy(turn).wait_recv()

            def add(step, carry):
                at = pl.multiple_of(step * chunk, chunk)
                rows = pl.ds(at, chunk)
                mine = pl.ds(pl.multiple_of(start + at, 16), chunk)
                total = self.own[target, mine, columns].astype(jnp.float32)
                total = total + self.got_last[turn, rows, :].astype(jnp.float32)
                self.part[target, rows, :] = total.astype(self.part.dtype)
                return carry

            lax.fori_loop(0, self.high // chunk, add, 0)
            if turn:
                self.level_copy(turn).start()

    def fourth(self):
        group, level, _ = place()
        start = lax.div(group, 2) * self.high
        columns = self.column_half(group)
        chunk = 16 if self.wide > 1536 else 48
        for turn in TURNS:
            self.level_copy(turn).wait_recv()

        def add(step, carry):
            at = pl.multiple_of(step * chunk, chunk)
            rows = pl.ds(at, chunk)
            mine = pl.ds(pl.multiple_of(start + at, 16), chunk)
            total = self.part[level, rows, :].astype(jnp.float32)
            for slot in range(3):
                total = total + self.got_level[slot, rows, :].astype(jnp.float32)
            self.out[mine, columns] = total.astype(self.out.dtype)
            return carry

        lax.fori_loop(0, self.high // chunk, add, 0)
        for other in TURNS:
            self.share_copy(other).start()

    def store(self):
        self.target[...] = self.out[...]

    def fifth(self):
        for other in TURNS:
            self.share_copy(other).wait_recv()

    def sixth(self):
        _, level, _ = place()
        for turn in (*TURNS, 0):
            self.core_copy(partner(level, turn)).wait_send()
            self.step_copy(turn).wait_send()
            self.last_copy(turn).wait_send()
            if turn:
                self.level_copy(turn).wait_send()
                self.share_copy(turn).wait_send()


GROUP_SEMS = 13


class GroupReduce:
    def __init__(self, share, out, scratch, sems):
        self.share, self.out, self.sems = share, out, sems
        self.own, self.got = scratch
        self.rows, self.columns = out.shape
        self.chunk = 16

    def load(self):
        return pltpu.make_async_copy(self.share, self.own, self.sems.at[0])

    def group_copy(self, other):
        group, level, core = place()
        peer = partner(group, other)
        return remote(
            self.own.at[quarter(peer, self.rows, self.columns)],
            self.got.at[other - 1],
            self.sems.at[other],
            self.sems.at[3 + other],
            (peer, 2 * level + core),
        )

    def share_copy(self, other):
        group, level, core = place()
        mine = self.out.at[quarter(group, self.rows, self.columns)]
        return remote(
            mine,
            mine,
            self.sems.at[6 + other],
            self.sems.at[9 + other],
            (partner(group, other), 2 * level + core),
        )

    def first(self):
        self.load().start()

    def second(self):
        self.load().wait()
        for other in TURNS:
            self.group_copy(other).start()

    def between(self):
        pass

    def third(self):
        group, _, _ = place()
        high, wide = quarter_shape(self.rows, self.columns)
        row_part, column_part = quarter(group, self.rows, self.columns)
        for other in TURNS:
            self.group_copy(other).wait_recv()

        def add(step, carry):
            at = pl.multiple_of(step * self.chunk, self.chunk)
            rows = pl.ds(at, self.chunk)
            mine = pl.ds(pl.multiple_of(row_part.start + at, self.chunk), self.chunk)
            total = self.own[mine, column_part].astype(jnp.float32)
            for slot in range(3):
                total = total + self.got[slot, rows, :].astype(jnp.float32)
            self.out[mine, column_part] = total.astype(self.out.dtype)
            return carry

        lax.fori_loop(0, high // self.chunk, add, 0)
        for other in TURNS:
            self.share_copy(other).start()

    def fourth(self):
        pass

    def fifth(self):
        for other in TURNS:
            self.share_copy(other).wait_recv()

    def store(self):
        self.target[...] = self.out[...]

    def sixth(self):
        for other in TURNS:
            self.group_copy(other).wait_send()
            self.share_copy(other).wait_send()


class Spread:
    def __init__(self, full, sems):
        self.full, self.sems = full, sems

    def level_copy(self, turn):
        group, level, core = place()
        block = self.full.at[2 * level + core]
        peer = (group, 2 * partner(level, turn) + core)
        return remote(block, block, self.sems.at[turn - 1], self.sems.at[2 + turn], peer)

    def core_copy(self, turn):
        group, level, core = place()
        block = self.full.at[2 * partner(level, turn) + core]
        peer = (group, 2 * level + 1 - core)
        return remote(block, block, self.sems.at[6 + turn], self.sems.at[10 + turn], peer)

    def run(self):
        for turn in TURNS:
            self.level_copy(turn).start()
        self.core_copy(0).start()
        for turn in TURNS:
            self.level_copy(turn).wait_recv()
            self.core_copy(turn).start()
        for turn in (0, *TURNS):
            self.core_copy(turn).wait_recv()
        for turn in (0, *TURNS):
            self.core_copy(turn).wait_send()
            if turn:
                self.level_copy(turn).wait_send()


def squares_in(out):
    def add(step, total):
        piece = out[pl.ds(pl.multiple_of(step * 16, 16), 16), :].astype(jnp.float32)
        piece = piece * piece
        for lane in range(0, out.shape[1], LANES):
            total = total + piece[:, lane : lane + LANES]
        return total

    total = lax.fori_loop(0, out.shape[0] // 16, add, jnp.zeros((16, LANES), jnp.float32))
    return jnp.sum(total, 0, keepdims=True)


def run_stages(jobs, stages):
    for stage in stages:
        for job in jobs:
            getattr(job, stage)()


STAGES = ("first", "second", "between", "third", "fourth", "fifth", "sixth")


def whole_scratch(grad):
    _, rows, columns = grad.shape
    high, wide = quarter_shape(rows, columns)
    shapes = (*[(4, rows, columns)] * 3, (3, 4, high, wide), (4, high, wide))
    return [pltpu.VMEM(shape, grad.dtype) for shape in (*shapes, (3, high, wide))]


def stepped_scratch(grad):
    _, rows, columns = grad.shape
    high, wide = rows // 2, columns // 2
    shapes = (
        *[(4, rows, columns)] * 3,
        (2, rows, wide),
        (2, high, columns),
        (4, high, wide),
        (4, high, wide),
        (3, high, wide),
    )
    return [pltpu.VMEM(shape, grad.dtype) for shape in shapes]


def share_scratch(share):
    return [
        pltpu.VMEM(share.shape, share.dtype),
        pltpu.VMEM((3, *quarter_shape(*share.shape)), share.dtype),
    ]


def reduce_kernel(*refs, whole, partly):
    count = whole + 1 + partly
    grads, outs, refs = refs[:count], refs[count : 2 * count], refs[2 * count :]
    sems, small_sems, group_sems, refs = refs[0], refs[1], refs[2], refs[3:]
    jobs = [
        Whole(grads[i], outs[i], refs[8 * i : 8 * i + 8], sems.at[i]) for i in range(whole)
    ]
    refs = refs[8 * whole :]
    small = Reduce(grads[whole], outs[whole], refs[:6], small_sems)
    refs = refs[6:]
    shares = [
        GroupReduce(
            grads[whole + 1 + i], outs[whole + 1 + i], refs[2 * i : 2 * i + 2], group_sems.at[i]
        )
        for i in range(partly)
    ]
    greet()
    run_stages([*jobs, small, *shares], STAGES[:1])
    run_stages([small, *shares], STAGES[1:2])
    run_stages(jobs, STAGES[1:3])
    run_stages([small, *shares], STAGES[3:4])
    run_stages(jobs, STAGES[3:4])
    run_stages([small, *jobs], STAGES[4:5])
    run_stages([*shares, small, *jobs], STAGES[5:])


def transfer_outs(arrays):
    return [jax.ShapeDtypeStruct(array.shape[-2:], array.dtype) for array in arrays]


def reduce_call(grads, small, shares, collective_id):
    in_vmem = pl.BlockSpec(memory_space=pltpu.VMEM)
    whole, partly = len(grads), len(shares)
    operands = [*grads, small, *shares]
    scratch = [
        pltpu.SemaphoreType.DMA((whole, WHOLE_SEMS)),
        pltpu.SemaphoreType.DMA((REDUCE_SEMS,)),
        pltpu.SemaphoreType.DMA((partly, GROUP_SEMS)),
    ]
    for grad in grads:
        scratch.extend(stepped_scratch(grad))
    scratch.extend(whole_scratch(small))
    for share in shares:
        scratch.extend(share_scratch(share))
    return pl.pallas_call(
        functools.partial(reduce_kernel, whole=whole, partly=partly),
        in_specs=[ANYWHERE] * len(operands),
        out_specs=[in_vmem] * len(operands),
        out_shape=transfer_outs(operands),
        scratch_shapes=scratch,
        compiler_params=pltpu.CompilerParams(
            collective_id=collective_id, has_side_effects=True, vmem_limit_bytes=VMEM_LIMIT
        ),
        cost_estimate=NO_COST,
        name="reduce_gradients",
    )(*operands)


def totals(full, vector_rows, rest_size):
    owners, rows, _ = full.shape
    rest_rows = -(-rest_size // (owners * LANES))
    row = lax.broadcasted_iota(jnp.int32, full.shape, 1)
    spot = row - vector_rows + rest_rows * lax.broadcasted_iota(jnp.int32, full.shape, 0)
    spot = spot * LANES + lax.broadcasted_iota(jnp.int32, full.shape, 2)
    in_rest = (row >= vector_rows) & (row < vector_rows + rest_rows)

    def summed(values):
        return jnp.sum(jnp.sum(jnp.sum(values, 0), 0, keepdims=True), 1, keepdims=True)

    tokens = summed(jnp.where(in_rest & (spot == rest_size - 1), full, 0.0))
    loss = summed(jnp.where(in_rest & (spot == rest_size - 2), full, 0.0))
    kept = (row < vector_rows) | (in_rest & (spot < rest_size - 2))
    squares = jnp.where(kept, full * full, jnp.where(row == rows - 1, full, 0.0))
    norm = jnp.sqrt(summed(squares)) / tokens
    factor = jnp.minimum(1.0, CLIP_NORM / norm) / tokens
    lane = lax.broadcasted_iota(jnp.int32, (1, LANES), 1)
    return jnp.where(
        lane == 0, factor, jnp.where(lane == 1, norm, jnp.where(lane == 2, loss, tokens))
    )


def finish_kernel(*refs, done, partly, vector_rows, rest_size):
    finished, small, refs = refs[:done], refs[done], refs[done + 1 :]
    shares, refs = refs[:partly], refs[partly:]
    outs, full, numbers, refs = refs[:partly], refs[partly], refs[partly + 1], refs[partly + 2 :]
    group_sems, spread_sems, refs = refs[0], refs[1], refs[2:]
    jobs = [
        GroupReduce(shares[i], outs[i], refs[2 * i : 2 * i + 2], group_sems.at[i])
        for i in range(partly)
    ]
    greet()
    run_stages(jobs, STAGES[:2])
    total = sum(squares_in(out) for out in finished)
    run_stages(jobs, STAGES[3:6])
    total = total + sum(squares_in(out) for out in outs)
    _, level, core = place()
    mine = 2 * level + core
    last = small.shape[0] - 1
    full[mine] = small[...]
    full[mine, last : last + 1, :] = total
    Spread(full, spread_sems).run()
    numbers[...] = totals(full[...], vector_rows, rest_size)
    run_stages(jobs, STAGES[6:])


def finish_call(finished, small, shares, vector_rows, rest_size, collective_id):
    done, partly = len(finished), len(shares)
    in_vmem = pl.BlockSpec(memory_space=pltpu.VMEM)
    scratch = [
        pltpu.SemaphoreType.DMA((partly, GROUP_SEMS)),
        pltpu.SemaphoreType.DMA((14,)),
    ]
    for share in shares:
        scratch.extend(share_scratch(share))
    full = (lax.axis_size("fsdp"), *small.shape)
    out_shape = [*transfer_outs(shares), jax.ShapeDtypeStruct(full, small.dtype), shape_of(1, LANES)]
    return pl.pallas_call(
        functools.partial(
            finish_kernel, done=done, partly=partly, vector_rows=vector_rows, rest_size=rest_size
        ),
        in_specs=[in_vmem] * (done + 1) + [ANYWHERE] * partly,
        out_specs=[in_vmem] * len(out_shape),
        out_shape=out_shape,
        scratch_shapes=scratch,
        compiler_params=pltpu.CompilerParams(
            collective_id=collective_id, has_side_effects=True, vmem_limit_bytes=VMEM_LIMIT
        ),
        name="finish_gradients",
    )(*finished, small, *shares)


def with_kernels():
    return lax.axis_size("dp") == 4 and lax.axis_size("fsdp") == 8


def reduce_all(grads, small, shares, collective_id):
    if with_kernels():
        return reduce_call(grads, small, shares, collective_id)
    return [lax.psum(scatter(grad), "dp") for grad in (*grads, small)] + [
        lax.psum(share, "dp") for share in shares
    ]


def finish_all(finished, small, shares, vector_rows, rest_size, collective_id):
    if with_kernels():
        return finish_call(finished, small, shares, vector_rows, rest_size, collective_id)
    outs = [lax.psum(share, "dp") for share in shares]
    total = sum(jnp.sum(jnp.square(out.astype(jnp.float32))) for out in (*finished, *outs))
    row = jnp.full((1, LANES), 1.0 / LANES, jnp.float32) * total
    full = lax.all_gather(small.at[-1:].set(row), "fsdp", axis=0)
    return [*outs, full, totals(full, vector_rows, rest_size)]


def scatter(grad):
    return lax.psum_scatter(grad, "fsdp", scatter_dimension=0)


def by_owner(grad, low=jnp.bfloat16):
    owners = lax.axis_size("fsdp")
    return grad.astype(low).reshape(owners, grad.shape[0] // owners, grad.shape[1])


def attention_forward_kernel(
    q_ref, k_ref, v_ref, seg_col_ref, seg_row_ref, out_ref, expo_ref, inv_ref, *, block
):
    rows = q_ref.shape[0]
    lower = lax.broadcasted_iota(jnp.int32, (block, PAIR), 1) < HD
    keys = k_ref[...]
    values = jnp.concatenate([v_ref[...], jnp.ones((rows, PAIR), v_ref.dtype)], 1)
    seg_row = seg_row_ref[...]
    tasks = [(step, head) for step in range(rows // block) for head in range(2)]

    def scores_of(step, head):
        query = q_ref[step * block : (step + 1) * block, :] * jnp.bfloat16(HD**-0.5)
        keep = lower if head == 0 else jnp.logical_not(lower)
        return mul_nt(jnp.where(keep, query, jnp.bfloat16(0)), keys)

    scores = scores_of(*tasks[0])
    outs = []
    for index, (step, head) in enumerate(tasks):
        following = scores_of(*tasks[index + 1]) if index + 1 < len(tasks) else None
        at = slice(step * block, (step + 1) * block)
        scores = jnp.where(seg_col_ref[at, :] == seg_row, scores, MASKED)
        highest = jnp.max(scores, -1, keepdims=True)
        low = jnp.exp(scores - highest).astype(jnp.bfloat16)
        expo_ref[head, at, :] = low
        outs.append(mul(low, values))
        if head:
            inverse = 1.0 / jnp.where(lower, outs[0][:, PAIR:], outs[1][:, PAIR:])
            sums = jnp.where(lower, outs[0][:, :PAIR], outs[1][:, :PAIR])
            out_ref[at, :] = (sums * inverse).astype(jnp.bfloat16)
            inv_ref[at, :] = inverse
            outs = []
        scores = following


def attention_forward(qkv_rows, segment, rides, collective_id):
    rows = qkv_rows.shape[0]
    pairs = HEADS // 2
    wide = lambda base: pl.BlockSpec((rows, PAIR), lambda j, base=base: (0, base + j))
    return block_call(
        functools.partial(attention_forward_kernel, block=min(256, rows)),
        pairs,
        [wide(0), wide(pairs), wide(2 * pairs), fixed(rows, 1), fixed(1, rows)],
        [qkv_rows, qkv_rows, qkv_rows, segment[:, None], segment[None, :]],
        [wide(0), pl.BlockSpec((2, rows, rows), lambda j: (j, 0, 0)), wide(0)],
        [
            shape_of(rows, D, dtype=LOW),
            shape_of(HEADS, rows, rows, dtype=LOW),
            shape_of(rows, D),
        ],
        [],
        "attention_forward",
        work(16 * HEADS * rows * rows * HD, 2 * HEADS * rows * rows + 12 * rows * D),
        rides,
        collective_id,
    )


def attention_backward_kernel(
    q_ref, k_ref, v_ref, expo_ref, inv_ref, out_ref, grad_ref, dqkv_ref, *, block
):
    rows = q_ref.shape[0]
    pair = pl.program_id(0)
    lower = lax.broadcasted_iota(jnp.int32, (block, PAIR), 1) < HD
    keys = k_ref[...]
    values = v_ref[...]
    scale = HD**-0.5
    scaled_grad = (grad_ref[...].astype(jnp.float32) * inv_ref[...]).astype(jnp.bfloat16)
    query = q_ref[...]
    query_t = query.T
    grad_t = scaled_grad.T
    product = scaled_grad.astype(jnp.float32) * out_ref[...].astype(jnp.float32)
    key_t = [None, None]
    value_t = [None, None]
    tasks = [(step, head) for step in range(rows // block) for head in range(2)]

    def probs_grad_of(step, head):
        keep = lower if head == 0 else jnp.logical_not(lower)
        mine = scaled_grad[step * block : (step + 1) * block]
        return mul_nt(jnp.where(keep, mine, jnp.bfloat16(0)), values)

    probs_grad = probs_grad_of(*tasks[0])
    query_parts = []
    for index, (step, head) in enumerate(tasks):
        following = probs_grad_of(*tasks[index + 1]) if index + 1 < len(tasks) else None
        at = slice(step * block, (step + 1) * block)
        lanes = slice(head * HD, (head + 1) * HD)
        keep = lower if head == 0 else jnp.logical_not(lower)
        inner = jnp.sum(jnp.where(keep, product[at], 0.0), -1, keepdims=True)
        low = expo_ref[head, at, :]
        value_part = mul(grad_t[lanes, at], low)
        scores_grad = (low.astype(jnp.float32) * (probs_grad - inner)).astype(jnp.bfloat16)
        query_parts.append(mul(scores_grad, keys))
        key_part = mul(query_t[lanes, at], scores_grad)
        key_t[head] = key_part if step == 0 else key_t[head] + key_part
        value_t[head] = value_part if step == 0 else value_t[head] + value_part
        if head:
            query_grad = jnp.where(lower, query_parts[0], query_parts[1]) * scale
            dqkv_ref[at, pl.ds(pl.multiple_of(pair * PAIR, PAIR), PAIR)] = query_grad.astype(
                jnp.bfloat16
            )
            query_parts = []
        probs_grad = following
    key_grad = (jnp.concatenate(key_t, 0) * scale).T
    value_grad = jnp.concatenate(value_t, 0).T
    dqkv_ref[:, pl.ds(pl.multiple_of(D + pair * PAIR, PAIR), PAIR)] = key_grad.astype(jnp.bfloat16)
    dqkv_ref[:, pl.ds(pl.multiple_of(2 * D + pair * PAIR, PAIR), PAIR)] = value_grad.astype(jnp.bfloat16)


def attention_backward(qkv_rows, expo, inverse, attended, attended_grad, rides, collective_id):
    rows = qkv_rows.shape[0]
    pairs = HEADS // 2
    wide = lambda base: pl.BlockSpec((rows, PAIR), lambda j, base=base: (0, base + j))
    return block_call(
        functools.partial(attention_backward_kernel, block=min(256, rows)),
        pairs,
        [
            wide(0),
            wide(pairs),
            wide(2 * pairs),
            pl.BlockSpec((2, rows, rows), lambda j: (j, 0, 0)),
            wide(0),
            wide(0),
            wide(0),
        ],
        [qkv_rows, qkv_rows, qkv_rows, expo, inverse, attended, attended_grad],
        [fixed(rows, 3 * D)],
        [shape_of(rows, 3 * D, dtype=LOW)],
        [],
        "attention_backward",
        None,
        rides,
        collective_id,
    )


def mul(left, right):
    return jnp.dot(left, right, preferred_element_type=jnp.float32)


def mul_nt(left, right):
    return lax.dot_general(left, right, NT, preferred_element_type=jnp.float32)


def normalized(values):
    center = values - jnp.mean(values, -1, keepdims=True)
    inverse = lax.rsqrt(jnp.mean(center * center, -1, keepdims=True) + NORM_EPS)
    return center * inverse, inverse


def norm_backward(grad, values, gain):
    unit, inverse = normalized(values)
    inner = grad * gain
    mean_inner = jnp.mean(inner, -1, keepdims=True)
    mean_cross = jnp.mean(inner * unit, -1, keepdims=True)
    value_grad = inverse * (inner - mean_inner - unit * mean_cross)
    return value_grad, column_sum(grad * unit), column_sum(grad)


def column_sum(rows):
    return jnp.sum(rows.astype(jnp.float32), 0, keepdims=True)


def at_first(action):
    pl.when(pl.program_id(0) == 0)(action)


def rows_of(block, columns):
    return pl.BlockSpec((block, columns), lambda i: (i, 0))


def fixed(*shape):
    return pl.BlockSpec(shape, lambda i: (0,) * len(shape), pipeline_mode=pl.Buffered(1))


def loads(sources, targets, sems):
    return [
        pltpu.make_async_copy(source, target, sems.at[index])
        for index, (source, target) in enumerate(zip(sources, targets))
    ]


def shape_of(*shape, dtype=jnp.float32):
    return jax.ShapeDtypeStruct(shape, dtype)


def embed_kernel(pixel_ref, weight_ref, pos_ref, table_ref, bias_ref, out_ref):
    position = jnp.dot(
        pos_ref[...], table_ref[...], precision=HIGHEST, preferred_element_type=jnp.float32
    )
    out_ref[...] = mul(pixel_ref[...], weight_ref[...]) + bias_ref[...] + position


def embed(pixels, weight, pos_weights, table, bias):
    rows, depth = pixels.shape
    block = 256
    nodes = pos_weights.shape[1]
    return block_call(
        embed_kernel,
        rows // block,
        [rows_of(block, depth), fixed(depth, D), rows_of(block, nodes), fixed(nodes, D), fixed(1, D)],
        [pixels, weight, pos_weights, table, bias],
        [rows_of(block, D)],
        [shape_of(rows, D)],
        [],
        "embed",
        work(2 * rows * depth * D, 2 * rows * depth + 2 * depth * D + 4 * rows * D),
    )[0]


def chunk_at(base):
    return pl.ds(pl.multiple_of(base + pl.program_id(0) * D, LANES), D)


def columns_of(rows):
    return pl.BlockSpec((rows, D), lambda i: (0, i))


def halves_of(rows):
    half = rows // 2
    return [slice(start, start + half) for start in range(0, rows, half)]


def at_last(action):
    pl.when(pl.program_id(0) == pl.num_programs(0) - 1)(action)


def qkv_kernel(stream_ref, weight_ref, vector_ref, normed_out, qkv_ref, normed_ref, sem):
    copy = pltpu.make_async_copy(normed_ref, normed_out, sem)

    @at_first
    def _():
        unit, _ = normalized(stream_ref[...])
        normed_ref[...] = (unit * vector_ref[:, :D] + vector_ref[:, D : 2 * D]).astype(LOW)
        copy.start()

    bias = vector_ref[:, chunk_at(4 * D)]
    for half in halves_of(stream_ref.shape[0]):
        qkv_ref[half, :] = (mul(normed_ref[half, :], weight_ref[...]) + bias).astype(LOW)
    at_last(copy.wait)


def qkv_forward(stream, weight, vector):
    rows = stream.shape[0]
    return block_call(
        qkv_kernel,
        3,
        [fixed(rows, D), columns_of(D), fixed(1, vector.shape[1])],
        [stream, weight, vector],
        [ANYWHERE, columns_of(rows)],
        [shape_of(rows, D, dtype=LOW), shape_of(rows, 3 * D, dtype=LOW)],
        [pltpu.VMEM((rows, D), LOW), pltpu.SemaphoreType.DMA],
        "qkv_forward",
        work(6 * rows * D * D, 14 * rows * D + 6 * D * D),
    )


def mlp_kernel(
    stream_ref, attended_ref, mix_ref, up_ref, down_ref, vector_ref,
    residual_out, normed_out, active_ref, slope_ref, out_ref,
    residual_ref, normed_ref, sems,
):
    rows = stream_ref.shape[0]
    copies = loads((residual_ref, normed_ref), (residual_out, normed_out), sems)

    @at_first
    def _():
        for half in halves_of(rows):
            residual = stream_ref[half, :] + mul(attended_ref[half, :], mix_ref[...])
            residual = residual + vector_ref[:, 7 * D : 8 * D]
            residual_ref[half, :] = residual
            unit, _ = normalized(residual)
            normed = unit * vector_ref[:, 2 * D : 3 * D] + vector_ref[:, 3 * D : 4 * D]
            normed_ref[half, :] = normed.astype(LOW)
            out_ref[half, :] = residual + vector_ref[:, 8 * D : 9 * D]
        for copy in copies:
            copy.start()

    bias = vector_ref[:, chunk_at(9 * D)]
    parts = halves_of(rows)
    hidden = mul(normed_ref[parts[0], :], up_ref[...]) + bias
    for index, half in enumerate(parts):
        following = None
        if index + 1 < len(parts):
            following = mul(normed_ref[parts[index + 1], :], up_ref[...]) + bias
        square = hidden * hidden
        rise = 0.5 + 0.5 * jnp.tanh(hidden * (ROOT + (ROOT * CUBE) * square))
        active = hidden * rise
        active_low = active.astype(LOW)
        active_ref[half, :] = active_low
        bend = (2.0 * ROOT) + (6.0 * ROOT * CUBE) * square
        slope_ref[half, :] = (rise + active * (1.0 - rise) * bend).astype(LOW)
        out_ref[half, :] += mul(active_low, down_ref[...])
        hidden = following

    @at_last
    def _():
        for copy in copies:
            copy.wait()


def mlp_specs(up, proj_out):
    return (
        [fixed(D, D), columns_of(D), pl.BlockSpec((D, D), lambda i: (i + 1, 0))],
        [proj_out, up, proj_out],
    )


def mlp_forward(stream, attended, up, proj_out, vector):
    rows = stream.shape[0]
    width = up.shape[1]
    weight_specs, weights = mlp_specs(up, proj_out)
    return block_call(
        mlp_kernel,
        width // D,
        [fixed(rows, D), fixed(rows, D), *weight_specs, fixed(1, vector.shape[1])],
        [stream, attended, *weights, vector],
        [ANYWHERE, ANYWHERE, columns_of(rows), columns_of(rows), fixed(rows, D)],
        [
            shape_of(rows, D),
            shape_of(rows, D, dtype=LOW),
            shape_of(rows, width, dtype=LOW),
            shape_of(rows, width, dtype=LOW),
            shape_of(rows, D),
        ],
        [
            pltpu.VMEM((rows, D), jnp.float32),
            pltpu.VMEM((rows, D), LOW),
            pltpu.SemaphoreType.DMA((2,)),
        ],
        "mlp_forward",
        work(2 * rows * D * (D + 2 * width), rows * (16 * D + 4 * width) + 2 * D * (D + 2 * width)),
    )


def mlp_back_kernel(
    grad_ref, slope_ref, residual_in, normed_ref, active_ref, attended_ref, mix_ref, up_ref, down_ref, vector_ref,
    out_ref, attended_grad_ref, sums_ref, up_grad_ref, *refs,
):
    outs, scratch = refs[:-7], refs[-7:]
    residual_ref, low_ref, second_ref, turned_ref, hidden_ref, product_ref, sems = scratch
    rows = grad_ref.shape[0]
    step = pl.program_id(0)
    load = pltpu.make_async_copy(residual_in, residual_ref, sems.at[0, 0])

    def stores(slot):
        copies, base = [], 0
        for index, out in enumerate(outs):
            width = out.shape[1]
            source = product_ref.at[slot, :, pl.ds(base, width)]
            target = out.at[pl.ds(pl.multiple_of(slot * D, D), D)]
            copies.append(pltpu.make_async_copy(source, target, sems.at[1 + index, slot]))
            base += width
        return copies

    def store(slot, product):
        product_ref[slot] = product.astype(LOW)
        for copy in stores(slot):
            copy.start()

    @at_first
    def _():
        load.start()
        low_ref[...] = grad_ref[...].astype(LOW)
        turned_ref[...] = normed_ref[...].T
        second_ref[...] = jnp.zeros_like(second_ref)

    parts = halves_of(rows)
    active_grad = mul_nt(low_ref[parts[0], :], down_ref[...])
    hidden_sum = 0.0
    for index, half in enumerate(parts):
        following = None
        if index + 1 < len(parts):
            following = mul_nt(low_ref[parts[index + 1], :], down_ref[...])
        hidden_grad = (active_grad * slope_ref[half, :].astype(jnp.float32)).astype(LOW)
        hidden_ref[half, :] = hidden_grad
        hidden_sum = hidden_sum + column_sum(hidden_grad)
        second_ref[half, :] += mul_nt(hidden_grad, up_ref[...])
        active_grad = following
    sums_ref[:, chunk_at(4 * D)] = hidden_sum
    store(step + 1, mul(active_ref[...].T, low_ref[...]))
    up_grad_ref[...] = mul(turned_ref[...], hidden_ref[...]).astype(LOW)

    @at_last
    def _():
        load.wait()
        gain = vector_ref[:, 2 * D : 3 * D]
        totals = [0.0] * 4
        for half in halves_of(rows):
            grad = grad_ref[half, :]
            value_grad, gain_grad, shift_grad = norm_backward(
                second_ref[half, :], residual_ref[half, :], gain
            )
            total = value_grad + grad
            out_ref[half, :] = total
            total_low = total.astype(LOW)
            hidden_ref[half, :] = total_low
            attended_grad_ref[half, :] = mul_nt(total_low, mix_ref[...]).astype(LOW)
            new = (gain_grad, shift_grad, column_sum(total_low), column_sum(low_ref[half, :]))
            totals = [old + part for old, part in zip(totals, new)]
        sums_ref[:, : 4 * D] = jnp.concatenate(totals, 1)
        store(0, mul(attended_ref[...].T, hidden_ref[...]))
        for slot in range(product_ref.shape[0]):
            for copy in stores(slot):
                copy.wait()


def mlp_backward(grad, slope, residual, normed, active, attended, up, proj_out, vector, parts):
    rows = grad.shape[0]
    width = up.shape[1]
    steps = width // D
    whole = fixed(rows, D)
    weight_specs, weights = mlp_specs(up, proj_out)
    return block_call(
        mlp_back_kernel,
        steps,
        [
            whole,
            columns_of(rows),
            ANYWHERE,
            whole,
            columns_of(rows),
            whole,
            *weight_specs,
            fixed(1, vector.shape[1]),
        ],
        [grad, slope, residual, normed, active, attended, *weights, vector],
        [whole, whole, fixed(1, 4 * D + width), columns_of(D), *[ANYWHERE] * len(parts)],
        [
            shape_of(rows, D),
            shape_of(rows, D, dtype=LOW),
            shape_of(1, 4 * D + width),
            shape_of(D, width, dtype=LOW),
            *[shape_of(D + width, part, dtype=LOW) for part in parts],
        ],
        [
            pltpu.VMEM((rows, D), jnp.float32),
            pltpu.VMEM((rows, D), LOW),
            pltpu.VMEM((rows, D), jnp.float32),
            pltpu.VMEM((D, rows), LOW),
            pltpu.VMEM((rows, D), LOW),
            pltpu.VMEM((steps + 1, D, D), LOW),
            pltpu.SemaphoreType.DMA((1 + len(parts), steps + 1)),
        ],
        "mlp_backward",
    )


def qkv_back_kernel(
    grad_ref, residual_in, stream_in, normed_ref, weight_ref, vector_ref,
    out_ref, sums_ref, weight_grad_ref,
    residual_ref, stream_ref, sum_ref, turned_ref, sems,
):
    rows = out_ref.shape[0]
    copies = loads((residual_in, stream_in), (residual_ref, stream_ref), sems)

    @at_first
    def _():
        for copy in copies:
            copy.start()
        turned_ref[...] = normed_ref[...].T
        sum_ref[...] = jnp.zeros_like(sum_ref)

    for half in halves_of(rows):
        sum_ref[half, :] += mul_nt(grad_ref[half, :], weight_ref[...])
    sums_ref[:, chunk_at(2 * D)] = column_sum(grad_ref[...])
    weight_grad_ref[...] = mul(turned_ref[...], grad_ref[...]).astype(LOW)

    @at_last
    def _():
        for copy in copies:
            copy.wait()
        totals = [0.0] * 2
        for half in halves_of(rows):
            value_grad, gain_grad, shift_grad = norm_backward(
                sum_ref[half, :], stream_ref[half, :], vector_ref[:, :D]
            )
            out_ref[half, :] = residual_ref[half, :] + value_grad
            totals = [totals[0] + gain_grad, totals[1] + shift_grad]
        sums_ref[:, : 2 * D] = jnp.concatenate(totals, 1)


def qkv_backward(grad, residual_grad, stream, normed, weight, vector, rides, collective_id):
    rows = stream.shape[0]
    whole = fixed(rows, D)
    return block_call(
        qkv_back_kernel,
        3,
        [columns_of(rows), ANYWHERE, ANYWHERE, whole, columns_of(D), fixed(1, vector.shape[1])],
        [grad, residual_grad, stream, normed, weight, vector],
        [whole, fixed(1, 5 * D), columns_of(D)],
        [shape_of(rows, D), shape_of(1, 5 * D), shape_of(D, 3 * D, dtype=LOW)],
        [
            pltpu.VMEM((rows, D), jnp.float32),
            pltpu.VMEM((rows, D), jnp.float32),
            pltpu.VMEM((rows, D), jnp.float32),
            pltpu.VMEM((D, rows), LOW),
            pltpu.SemaphoreType.DMA((2,)),
        ],
        "qkv_backward",
        None,
        rides,
        collective_id,
    )


def embed_back_kernel(pixel_ref, grad_ref, pos_ref, out_ref, table_ref, bias_ref, low_ref):
    @at_first
    def _():
        grad = grad_ref[...]
        low = grad.astype(jnp.bfloat16)
        low_ref[...] = low
        bias_ref[...] = column_sum(low)
        table_ref[...] = jnp.dot(
            pos_ref[...], grad, precision=HIGHEST, preferred_element_type=jnp.float32
        )

    out_ref[...] = mul(pixel_ref[...].T, low_ref[...]).astype(jnp.bfloat16)


def embed_backward(pixels, grad, pos_weights_t):
    rows, depth = pixels.shape
    block = 768
    nodes = pos_weights_t.shape[0]
    return block_call(
        embed_back_kernel,
        depth // block,
        [pl.BlockSpec((rows, block), lambda i: (0, i)), fixed(rows, D), fixed(nodes, rows)],
        [pixels, grad, pos_weights_t],
        [rows_of(block, D), fixed(nodes, D), fixed(1, D)],
        [shape_of(depth, D, dtype=jnp.bfloat16), shape_of(nodes, D), shape_of(1, D)],
        [pltpu.VMEM((rows, D), jnp.bfloat16)],
        "embed_backward",
        None,
    )


def head_kernel(
    stream_ref, seg_col_ref, seg_row_ref, label_ref, weight_ref, vector_ref,
    grad_ref, weight_grad_ref, sums_ref, bias_grad_ref, numbers_ref, *, classes,
):
    padded = weight_ref.shape[1]
    vector = vector_ref[...].astype(LOW).astype(jnp.float32)
    gain, shift = vector[:, D : 2 * D], vector[:, 2 * D : 3 * D]
    slots = lax.broadcasted_iota(jnp.int32, (IMGS, 1), 0)
    member = (seg_row_ref[...] == slots).astype(jnp.float32)
    counts = jnp.sum(member, 1, keepdims=True)
    sizes = jnp.maximum(counts, 1.0)
    unit, inverse = normalized(stream_ref[...])
    final = unit * gain + shift
    owner = jnp.broadcast_to(seg_col_ref[...], final.shape)
    pooled = [jnp.sum(jnp.where(owner == k, final, 0.0), 0, keepdims=True) for k in range(IMGS)]
    pooled = (jnp.concatenate(pooled, 0) / sizes).astype(LOW)
    class_at = lax.broadcasted_iota(jnp.int32, (IMGS, padded), 1)
    logits = mul(pooled, weight_ref[...]) + vector[:, 3 * D :]
    logits = jnp.where(class_at < classes, logits, MASKED)
    highest = jnp.max(logits, -1, keepdims=True)
    exponent = jnp.exp(logits - highest)
    totals = jnp.sum(exponent, -1, keepdims=True)
    onehot = class_at == label_ref[...]
    picked = jnp.sum(jnp.where(onehot, logits, 0.0), 1, keepdims=True)
    loss = jnp.sum(counts * (highest + jnp.log(totals) - picked), 0, keepdims=True)
    numbers_ref[...] = jnp.concatenate([loss, jnp.sum(counts, 0, keepdims=True)], 1)
    logits_grad = ((exponent / totals - onehot.astype(jnp.float32)) * counts).astype(LOW)
    bias_grad_ref[...] = column_sum(logits_grad)
    weight_grad_ref[...] = lax.dot_general(
        pooled, logits_grad, (((0,), (0,)), ((), ())), preferred_element_type=jnp.float32
    ).astype(LOW)
    pooled_grad = mul_nt(logits_grad, weight_ref[...]) / sizes
    own = (seg_col_ref[...] == lax.broadcasted_iota(jnp.int32, (1, IMGS), 1)).astype(LOW)
    final_grad, left = 0.0, pooled_grad
    for _ in range(3):
        term = left.astype(LOW)
        final_grad = final_grad + mul(own, term)
        left = left - term.astype(jnp.float32)
    inner = final_grad * gain
    mean_inner = jnp.mean(inner, -1, keepdims=True)
    mean_cross = jnp.mean(inner * unit, -1, keepdims=True)
    grad_ref[...] = inverse * (inner - mean_inner - unit * mean_cross)
    sums_ref[...] = jnp.concatenate([column_sum(final_grad * unit), column_sum(final_grad)], 1)


def head(stream, segment, labels, weight, global_vector, classes):
    rows = stream.shape[0]
    padded = weight.shape[1]
    vector = jnp.pad(global_vector, (0, padded - classes))[None, :]
    return pl.pallas_call(
        functools.partial(head_kernel, classes=classes),
        out_shape=[
            shape_of(rows, D),
            shape_of(D, padded, dtype=LOW),
            shape_of(1, 2 * D),
            shape_of(1, padded),
            shape_of(1, 2),
        ],
        compiler_params=pltpu.CompilerParams(vmem_limit_bytes=VMEM_LIMIT),
        cost_estimate=NO_COST,
        name="head",
    )(stream, segment[:, None], segment[None, :], labels.reshape(IMGS, 1), weight, vector)


def adam_update(gradient, moment, square, weight, factor, learn_rate):
    clipped = gradient * factor
    moment = BETA_ONE * moment + (1.0 - BETA_ONE) * clipped
    square = BETA_TWO * square + (1.0 - BETA_TWO) * clipped * clipped
    fixed_one = 1.0 - BETA_ONE**STEP
    fixed_two = 1.0 - BETA_TWO**STEP
    step_dir = (
        moment / fixed_one / (jnp.sqrt(square / fixed_two) + ADAM_EPS) + WEIGHT_DECAY * weight
    )
    return (moment, square, weight - learn_rate * step_dir)


def body(
    pixels,
    segment,
    patch_size,
    labels,
    patch_kernel,
    head_weight,
    input_proj,
    output_proj,
    layer_vector,
    position_table,
    global_vector,
    patch_moment,
    head_moment,
    input_moment,
    output_moment,
    layer_moment,
    position_moment,
    global_moment,
    patch_square,
    head_square,
    input_square,
    output_square,
    layer_square,
    position_square,
    global_square,
):
    owners = lax.axis_size("fsdp")
    nodes = position_table.shape[0]
    vector_size = layer_vector.size
    stream, pos_weights_t, vectors, qkv_weight, up_zero, rides, rest_shards = begin(
        pixels,
        segment,
        patch_size,
        patch_kernel,
        layer_vector,
        input_proj,
        output_proj,
        head_weight,
        position_table,
        global_vector,
    )
    qkv_one, up_one, head_full = (
        lax.all_gather(shard, "fsdp", axis=0, tiled=True) for shard in rest_shards
    )
    saved_layers = []
    for index in range(LAYERS):
        vector = vectors[index]
        normed, qkv_rows = qkv_forward(stream, qkv_weight, vector)
        if index == 0:
            attended, expo, inverse, output, output_ride = attention_forward(
                qkv_rows, segment, rides, 4
            )
            up = up_zero
        else:
            attended, expo, inverse, output = attention_forward(qkv_rows, segment, [output_ride], 5)
            up = up_one
        residual, normed_second, active, slope, following = mlp_forward(
            stream, attended, up, output, vector
        )
        saved_layers.append(
            (
                (qkv_weight, up, output, vector),
                (stream, normed, qkv_rows, attended, expo, inverse),
                (residual, normed_second, active, slope),
            )
        )
        stream, qkv_weight = following, qkv_one
    stream_grad, head_grad, final_sums, head_bias_grad, numbers = head(
        stream, segment, labels, head_full, global_vector, head_weight.shape[1]
    )
    vector_grads = [None] * LAYERS
    for index in reversed(range(LAYERS)):
        (qkv_weight, up, output, vector), first, second = saved_layers[index]
        entering, normed, qkv_rows, attended, expo, inverse = first
        residual, normed_second, active, slope = second
        residual_grad, attended_grad, mlp_sums, up_grad, *output_grads = mlp_backward(
            stream_grad,
            slope,
            residual,
            normed_second,
            active,
            attended,
            up,
            output,
            vector,
            (D // 2,) * 2 if index else (D,),
        )
        attended_grad, *output_grads = lax.optimization_barrier((attended_grad, *output_grads))
        output_parts = [scatter(by_owner(grad)) for grad in output_grads]
        qkv_grad, beside_sum = attention_backward(
            qkv_rows,
            expo,
            inverse,
            attended,
            attended_grad,
            [SumRide(by_owner(head_grad), False) if index else SumRide(by_owner(up_grad), True)],
            6 if index else 8,
        )
        stream_grad, qkv_sums, qkv_weight_grad, *output_one_sum = qkv_backward(
            qkv_grad,
            residual_grad,
            entering,
            normed,
            qkv_weight,
            vector,
            () if index else [ShareRide(jnp.concatenate(early_parts, 1))],
            7,
        )
        if index:
            head_sum = beside_sum
            early_parts = output_parts
            stream_grad, qkv_weight_grad, up_grad = lax.optimization_barrier(
                (stream_grad, qkv_weight_grad, up_grad)
            )
            late_parts = [scatter(by_owner(grad)) for grad in (qkv_weight_grad, up_grad)]
        else:
            up_zero_sum, (output_one_sum,), (last_part,) = beside_sum, output_one_sum, output_parts
        vector_grads[index] = jnp.concatenate(
            [
                qkv_sums[0, : 2 * D],
                mlp_sums[0, : 2 * D],
                qkv_sums[0, 2 * D :],
                mlp_sums[0, 2 * D :],
            ]
        )
    kernel_grad, position_grad, bias_grad = embed_backward(pixels, stream_grad, pos_weights_t)
    position_grad = position_grad[:nodes]
    vector_part = jnp.stack(vector_grads).reshape(LAYERS, owners, -1)
    vector_part = jnp.swapaxes(vector_part, 0, 1).reshape(owners, vector_size)
    vector_rows = -(-vector_size // LANES)
    vector_part = jnp.pad(vector_part, ((0, 0), (0, vector_rows * LANES - vector_size)))
    rest = jnp.concatenate(
        [
            position_grad.reshape(-1),
            bias_grad[0],
            final_sums[0],
            head_bias_grad[0, :CLS],
            numbers[0],
        ]
    )
    rest_rows = -(-rest.shape[0] // (owners * LANES))
    rest_part = jnp.pad(rest, (0, rest_rows * owners * LANES - rest.shape[0]))
    small = jnp.concatenate([vector_part, rest_part.reshape(owners, -1)], 1)
    used = vector_rows + rest_rows
    block_rows = (used // 64 + 1) * 64
    small = jnp.pad(small.reshape(owners, used, LANES), ((0, 0), (0, block_rows - used), (0, 0)))
    qkv_zero_sum, kernel_sum, small_share, *input_one_sums = reduce_all(
        [by_owner(qkv_weight_grad), by_owner(kernel_grad)], small, late_parts, 2
    )
    output_zero_sum, small_full, numbers = finish_all(
        [head_sum, output_one_sum, up_zero_sum, qkv_zero_sum, kernel_sum, *input_one_sums],
        small_share,
        [last_part],
        vector_rows,
        rest.shape[0],
        3,
    )
    factor, grad_norm, loss_sum, token_total = (numbers[0, index] for index in range(4))
    rest_sum = small_full[:, vector_rows:used].reshape(-1)
    position_sum = rest_sum[: position_grad.size].reshape(position_grad.shape)
    global_sum = rest_sum[position_grad.size :][: global_vector.shape[0]]
    kernel_sum = kernel_sum.astype(jnp.float32)
    head_sum = head_sum[:, :CLS].astype(jnp.float32)
    input_sum = jnp.stack(
        [jnp.concatenate(pair, 1) for pair in ((qkv_zero_sum, up_zero_sum), input_one_sums)]
    ).astype(jnp.float32)
    output_sum = jnp.stack([output_zero_sum, output_one_sum]).astype(
        jnp.float32
    )
    vector_sum = small_share[:vector_rows].reshape(-1)[:vector_size].reshape(layer_vector.shape)
    patch_next = adam_update(
        kernel_sum, patch_moment, patch_square, patch_kernel, factor, LEARN_RATE
    )
    head_next = adam_update(head_sum, head_moment, head_square, head_weight, factor, LEARN_RATE)
    input_next = adam_update(input_sum, input_moment, input_square, input_proj, factor, LEARN_RATE)
    output_next = adam_update(
        output_sum, output_moment, output_square, output_proj, factor, LEARN_RATE
    )
    layer_next = adam_update(
        vector_sum, layer_moment, layer_square, layer_vector, factor, VECTOR_RATE
    )
    position_next = adam_update(
        position_sum, position_moment, position_square, position_table, factor, LEARN_RATE
    )
    global_next = adam_update(
        global_sum, global_moment, global_square, global_vector, factor, VECTOR_RATE
    )
    return (
        loss_sum,
        token_total,
        grad_norm,
        patch_next[0],
        head_next[0],
        input_next[0],
        output_next[0],
        layer_next[0],
        position_next[0],
        global_next[0],
        patch_next[1],
        head_next[1],
        input_next[1],
        output_next[1],
        layer_next[1],
        position_next[1],
        global_next[1],
        patch_next[2],
        head_next[2],
        input_next[2],
        output_next[2],
        layer_next[2],
        position_next[2],
        global_next[2],
    )


def solution(mesh):
    in_specs = (
        P(("dp", "fsdp"), None),
        P(("dp", "fsdp")),
        P(("dp", "fsdp"), None),
        P(("dp", "fsdp"), None),
        P("fsdp", None),
        P("fsdp", None),
        P(None, "fsdp", None),
        P(None, "fsdp", None),
        P(None, "fsdp"),
        P(),
        P(),
        P("fsdp", None),
        P("fsdp", None),
        P(None, "fsdp", None),
        P(None, "fsdp", None),
        P(None, "fsdp"),
        P(),
        P(),
        P("fsdp", None),
        P("fsdp", None),
        P(None, "fsdp", None),
        P(None, "fsdp", None),
        P(None, "fsdp"),
        P(),
        P(),
    )
    out_specs = (
        P(),
        P(),
        P(),
        P("fsdp", None),
        P("fsdp", None),
        P(None, "fsdp", None),
        P(None, "fsdp", None),
        P(None, "fsdp"),
        P(),
        P(),
        P("fsdp", None),
        P("fsdp", None),
        P(None, "fsdp", None),
        P(None, "fsdp", None),
        P(None, "fsdp"),
        P(),
        P(),
        P("fsdp", None),
        P("fsdp", None),
        P(None, "fsdp", None),
        P(None, "fsdp", None),
        P(None, "fsdp"),
        P(),
        P(),
    )
    return jax.shard_map(body, mesh=mesh, in_specs=in_specs, out_specs=out_specs, check_vma=False)
```

```python
import functools

import jax
import jax.numpy as jnp
from jax import lax
from jax.experimental import pallas as pl
from jax.experimental.pallas import tpu as pltpu
from jax.sharding import PartitionSpec as P

D = 768
HEADS = 12
HD = 64
CLS = 1000
GRID = 7
IMG = 240
IMGS = 8
LAYERS = 2
STEP = 3


NORM_EPS = 1e-06
CLIP_NORM = 0.01
LEARN_RATE = 0.05
VECTOR_RATE = 0.25
BETA_ONE = 0.5
BETA_TWO = 0.5
ADAM_EPS = 1e-08
WEIGHT_DECAY = 0.05
HIGHEST = lax.Precision.HIGHEST

PAIR = 2 * HD
MASKED = -1e30
MIB = 1024 * 1024
VMEM_LIMIT = 56 * MIB
MESH = pl.DeviceIdType.MESH
LANES = 128
LOW = jnp.bfloat16
ANYWHERE = pl.BlockSpec(memory_space=pl.ANY)
NO_COST = pl.CostEstimate(flops=0, bytes_accessed=0, transcendentals=0)
ROOT = 0.7978845608028654
CUBE = 0.044715
NT = (((1,), (1,)), ((), ()))


def layer_norm(values, gain, shift):
    center = values - jnp.mean(values, -1, keepdims=True)
    spread = jnp.mean(center * center, -1, keepdims=True)
    return center * lax.rsqrt(spread + NORM_EPS) * gain + shift


def rounded(values):
    return lax.optimization_barrier(values.astype(jnp.bfloat16)).astype(jnp.float32)


def matmul(left, right):
    return jnp.dot(left, right, preferred_element_type=jnp.float32)


def padded_rows(flat, multiple):
    extra = -flat.shape[0] % (multiple * LANES)
    return jnp.pad(flat, (0, extra)).reshape(-1, LANES)


def row_layout(seg_row, patch_row):
    row_count = seg_row.shape[0]
    slots = jnp.arange(IMGS, dtype=jnp.int32)
    member = seg_row[:, None] == slots[None, :]
    counts = jnp.sum(member.astype(jnp.int32), 0, dtype=jnp.int32)
    starts = jnp.cumsum(counts, dtype=jnp.int32) - counts
    inside = jnp.any(member, 1)
    offset = jnp.arange(row_count, dtype=jnp.int32) - jnp.sum(
        jnp.where(member, starts[None, :], 0), 1, dtype=jnp.int32
    )
    offset = jnp.where(inside, offset, 0)
    patch_tok = jnp.sum(jnp.where(member, patch_row[None, :], 0), 1, dtype=jnp.int32) + jnp.where(
        inside, 0, IMG
    )
    side = IMG // patch_tok
    nodes = jnp.arange(GRID, dtype=jnp.int32).astype(jnp.float32)

    def hat(coord):
        place = ((2 * coord + 1) * GRID).astype(jnp.float32) / (2 * side).astype(jnp.float32) - 0.5
        place = jnp.clip(place, 0.0, GRID - 1.0)
        return jnp.maximum(1.0 - jnp.abs(place[:, None] - nodes[None, :]), 0.0)

    weights = (hat(offset // side)[:, :, None] * hat(offset % side)[:, None, :]).reshape(
        row_count, GRID * GRID
    )
    return (weights, member.astype(jnp.float32), counts.astype(jnp.float32))


TURNS = (1, 2, 3)


def place():
    slot = lax.axis_index("fsdp")
    return lax.axis_index("dp"), lax.div(slot, 2), lax.rem(slot, 2)


def partner(index, turn):
    if turn == 0:
        return index
    if turn == 1:
        return index + 1 - 2 * lax.rem(index, 2)
    if turn == 2:
        return lax.rem(index + 2, 4)
    return 3 - index


def greet():
    group, level, core = place()
    barrier = pltpu.get_barrier_semaphore()
    peers = [(group, 2 * level + 1 - core)]
    for turn in TURNS:
        peers.append((group, 2 * partner(level, turn) + core))
        peers.append((partner(group, turn), 2 * level + core))
    for peer in peers:
        pl.semaphore_signal(barrier, inc=1, device_id=peer, device_id_type=MESH)
    pl.semaphore_wait(barrier, len(peers))


def quarter_shape(rows, columns):
    if columns % (2 * LANES) == 0:
        return rows // 2, columns // 2
    return rows // 4, columns


def quarter(index, rows, columns):
    high, wide = quarter_shape(rows, columns)
    if wide == columns:
        return pl.ds(pl.multiple_of(index * high, high), high), pl.ds(0, columns)
    return (
        pl.ds(pl.multiple_of(lax.div(index, 2) * high, high), high),
        pl.ds(pl.multiple_of(lax.rem(index, 2) * wide, wide), wide),
    )


def remote(source, target, send, receive, device):
    return pltpu.make_async_remote_copy(
        src_ref=source,
        dst_ref=target,
        send_sem=send,
        recv_sem=receive,
        device_id=device,
        device_id_type=MESH,
    )


GATHER_SEMS = 39


def relay_rows(part, rows):
    cut = -(-rows // 32) * 16
    return (0, cut) if part == 0 else (cut, rows - cut)


class Relay:
    def region(self, turn, index):
        _, level, core = place()
        block = self.out.at[2 * partner(level, turn) + core]
        return block.at[quarter(index, *self.shard.shape)]

    def group_copy(self, turn, other):
        group, level, core = place()
        index = self.group_at + 2 * (turn - 1) + other - 1
        peer = (partner(group, other), 2 * level + core)
        target = self.region(turn, group)
        source = self.quarter_source(turn, target)
        return remote(source, target, self.sems.at[index], self.sems.at[index + 6], peer)

    def relay_copy(self, turn, part):
        group, level, core = place()
        first, count = relay_rows(part, quarter_shape(*self.shard.shape)[0])
        block = self.region(turn, partner(group, 1 + part)).at[pl.ds(first, count)]
        index = self.relay_at + 2 * (turn - 1) + part
        peer = (partner(group, 2 - part), 2 * level + core)
        return remote(block, block, self.sems.at[index], self.sems.at[index + 6], peer)

    def relay(self):
        for turn in TURNS:
            for part in range(2):
                self.group_copy(turn, 1 + part).wait_recv()
                self.relay_copy(turn, part).start()

    def wait_quarters(self, turn):
        for part in range(2):
            self.relay_copy(turn, part).wait_recv()

    def wait_passed(self):
        for turn in TURNS:
            for part in range(2):
                self.group_copy(turn, 1 + part).wait_send()
                self.relay_copy(turn, part).wait_send()


class Gather(Relay):
    group_at, relay_at = 7, 19

    def __init__(self, shard, out, sems, split, in_place=False):
        self.shard, self.out, self.sems, self.split = shard, out, sems, split
        self.in_place = in_place
        self.rows, self.columns = shard.shape

    def quarter_source(self, turn, target):
        return target

    def level_copy(self, turn):
        group, level, core = place()
        block = self.out.at[2 * level + core]
        source = self.shard
        if self.split:
            part = quarter(group, self.rows, self.columns)
            source, block = source.at[part], block.at[part]
        peer = (group, 2 * partner(level, turn) + core)
        return remote(source, block, self.sems.at[turn], self.sems.at[3 + turn], peer)

    def core_copy(self, turn):
        group, level, core = place()
        slot = 2 * partner(level, turn) + core
        source = self.shard if turn == 0 else self.out.at[slot]
        peer = (group, 2 * level + 1 - core)
        return remote(source, self.out.at[slot], self.sems.at[31 + turn], self.sems.at[35 + turn], peer)

    def own_copy(self):
        _, level, core = place()
        return pltpu.make_async_copy(self.shard, self.out.at[2 * level + core], self.sems.at[0])

    def first(self):
        for turn in TURNS:
            self.level_copy(turn).start()
        self.core_copy(0).start()
        if not self.in_place:
            self.own_copy().start()

    def second(self):
        for turn in TURNS:
            self.level_copy(turn).wait_recv()
            if self.split:
                for other in (1, 2):
                    self.group_copy(turn, other).start()
            else:
                self.core_copy(turn).start()

    def third(self, use=None):
        for turn in TURNS if self.split else ():
            self.wait_quarters(turn)
            self.core_copy(turn).start()
            if use is not None:
                use(turn, True)

    def fourth(self, use=None):
        for turn in TURNS if use is not None else (0, *TURNS):
            self.core_copy(turn).wait_recv()
            if use is not None:
                use(turn, False)
        for turn in TURNS:
            self.level_copy(turn).wait_send()
        if self.split:
            self.wait_passed()
        for turn in (0, *TURNS):
            self.core_copy(turn).wait_send()
        if not self.in_place:
            self.own_copy().wait()


class LevelGather:
    def __init__(self, shard, out, sems):
        self.shard, self.out, self.sems = shard, out, sems

    def level_copy(self, turn):
        group, level, core = place()
        return remote(
            self.shard.at[quarter(group, *self.shard.shape)],
            self.out.at[level],
            self.sems.at[turn],
            self.sems.at[3 + turn],
            (group, 2 * partner(level, turn) + core),
        )

    def first(self):
        for turn in TURNS:
            self.level_copy(turn).start()

    def second(self):
        pass

    def third(self):
        pass

    def fourth(self):
        for turn in TURNS:
            self.level_copy(turn).wait_recv()
            self.level_copy(turn).wait_send()

    def store(self):
        _, level, _ = place()
        self.out[level] = jnp.zeros(self.out.shape[1:], self.out.dtype)
        self.target[...] = self.out[...]


GROUP_GATHER_SEMS = 36


class GroupGather(Relay):
    group_at, relay_at = 4, 16

    def __init__(self, shard, quarters, out, sems):
        self.shard, self.quarters, self.out, self.sems = shard, quarters, out, sems

    def quarter_source(self, turn, target):
        _, level, _ = place()
        return self.quarters.at[partner(level, turn)]

    def own_copy(self, turn):
        group, level, core = place()
        if turn == 0:
            source, target = self.shard, self.out.at[2 * level + core]
        else:
            source, target = self.quarters.at[partner(level, turn)], self.region(turn, group)
        return pltpu.make_async_copy(source, target, self.sems.at[turn])

    def core_copy(self, turn):
        group, level, core = place()
        slot = 2 * partner(level, turn) + core
        source = self.shard if turn == 0 else self.out.at[slot]
        peer = (group, 2 * level + 1 - core)
        return remote(source, self.out.at[slot], self.sems.at[28 + turn], self.sems.at[32 + turn], peer)

    def first(self):
        for turn in TURNS:
            for other in (1, 2):
                self.group_copy(turn, other).start()
        for turn in (0, *TURNS):
            self.own_copy(turn).start()
        self.core_copy(0).start()

    def third(self):
        for turn in TURNS:
            self.wait_quarters(turn)
            self.own_copy(turn).wait()
            self.core_copy(turn).start()

    def fourth(self):
        for turn in (0, *TURNS):
            self.core_copy(turn).wait_recv()
            self.core_copy(turn).wait_send()
        self.wait_passed()
        self.own_copy(0).wait()

    def store(self):
        copy = pltpu.make_async_copy(self.out, self.target, self.sems.at[0])
        copy.start()
        copy.wait()


class LevelRide:
    def __init__(self, shard):
        self.operands = [shard]
        self.in_specs = [fixed(*shard.shape)]
        shape = (4, *quarter_shape(*shard.shape))
        self.out_specs = [fixed(*shape)]
        self.out_shapes = [jax.ShapeDtypeStruct(shape, shard.dtype)]
        self.scratch = [pltpu.VMEM(shape, shard.dtype), pltpu.SemaphoreType.DMA((7,))]

    def job(self, sources, targets, scratch):
        job = LevelGather(sources[0], *scratch)
        job.target = targets[0]
        return job

    def before(self, steps):
        return {0: ("first",)}

    after = ("fourth", "store")

    def result(self, outs):
        return GatherRide(self.operands[0], outs[0])

    def plain(self):
        return GatherRide(self.operands[0], self.operands[0])


class GatherRide:
    def __init__(self, shard, quarters):
        owners = lax.axis_size("fsdp")
        full = (owners, *shard.shape)
        self.operands = [shard, quarters]
        self.in_specs = [fixed(*shard.shape), fixed(*quarters.shape)]
        self.out_specs = [ANYWHERE]
        self.out_shapes = [jax.ShapeDtypeStruct(full, shard.dtype)]
        self.scratch = [
            pltpu.VMEM(full, shard.dtype),
            pltpu.SemaphoreType.DMA((GROUP_GATHER_SEMS,)),
        ]

    def job(self, sources, targets, scratch):
        job = GroupGather(*sources, *scratch)
        job.target = targets[0]
        return job

    def before(self, steps):
        return {0: ("first",), steps // 2: ("relay",), steps - 1: ("third",)}

    after = ("fourth", "store")

    def result(self, outs):
        return outs[0].reshape(-1, outs[0].shape[2])

    def plain(self):
        return lax.all_gather(self.operands[0], "fsdp", axis=0, tiled=True)


class ShareRide:
    def __init__(self, share):
        self.operands = [share]
        self.in_specs = [ANYWHERE]
        self.out_specs = [fixed(*share.shape)]
        self.out_shapes = [jax.ShapeDtypeStruct(share.shape, share.dtype)]
        self.scratch = [
            pltpu.VMEM(share.shape, share.dtype),
            *share_scratch(share),
            pltpu.SemaphoreType.DMA((GROUP_SEMS,)),
        ]

    def job(self, sources, targets, scratch):
        job = GroupReduce(sources[0], scratch[0], scratch[1:3], scratch[3])
        job.target = targets[0]
        return job

    def before(self, steps):
        return {0: ("first", "second"), max(1, steps // 2): ("third",)}

    after = ("fifth", "sixth", "store")

    def result(self, outs):
        return outs[0]

    def plain(self):
        return lax.psum(self.operands[0], "dp")


class SumRide:
    def __init__(self, grad, large):
        block = grad.shape[1:]
        self.large = large
        self.operands = [grad]
        self.in_specs = [ANYWHERE]
        self.out_specs = [fixed(*block)]
        self.out_shapes = [jax.ShapeDtypeStruct(block, grad.dtype)]
        buffers = stepped_scratch(grad) if large else whole_scratch(grad)
        sems = WHOLE_SEMS if large else REDUCE_SEMS
        self.scratch = [pltpu.VMEM(block, grad.dtype), *buffers, pltpu.SemaphoreType.DMA((sems,))]

    def job(self, sources, targets, scratch):
        job = (Whole if self.large else Reduce)(sources[0], scratch[0], scratch[1:-1], scratch[-1])
        job.target = targets[0]
        return job

    def before(self, steps):
        if self.large:
            return {0: ("first",), 1: ("second",), steps - 2: ("between",), steps - 1: ("third",)}
        return {0: ("first",), 1: ("second",), steps // 2: ("third",), steps - 1: ("fourth",)}

    @property
    def after(self):
        return (("fourth",) if self.large else ()) + ("fifth", "sixth", "store")

    def result(self, outs):
        return outs[0]

    def plain(self):
        return lax.psum(scatter(self.operands[0]), "dp")


class LeadRide:
    after = ("third", "sixth", "store")

    def __init__(self, grad):
        _, rows, columns = grad.shape
        shape = (4, rows // 2, columns // 2)
        self.operands = [grad]
        self.in_specs = [ANYWHERE]
        self.out_specs = [fixed(*shape)]
        self.out_shapes = [jax.ShapeDtypeStruct(shape, grad.dtype)]
        self.scratch = [*stepped_scratch(grad), pltpu.SemaphoreType.DMA((WHOLE_SEMS,))]

    def job(self, sources, targets, scratch):
        job = Lead(sources[0], None, scratch[:-1], scratch[-1])
        job.target = targets[0]
        return job

    def before(self, steps):
        return {0: ("first",), 1: ("second",), steps - 2: ("between",)}

    def result(self, outs):
        return RestRide(outs[0])

    def plain(self):
        return RestRide(self.operands[0])


class RestRide:
    after = ("fifth", "sixth", "store")

    def __init__(self, part):
        _, high, wide = part.shape
        block = (2 * high, 2 * wide)
        self.operands = [part]
        self.in_specs = [fixed(*part.shape)]
        self.out_specs = [fixed(*block)]
        self.out_shapes = [jax.ShapeDtypeStruct(block, part.dtype)]
        self.scratch = [
            pltpu.VMEM(block, part.dtype),
            pltpu.VMEM((3, high, wide), part.dtype),
            pltpu.SemaphoreType.DMA((WHOLE_SEMS,)),
        ]

    def job(self, sources, targets, scratch):
        job = Rest(sources[0], *scratch)
        job.target = targets[0]
        return job

    def before(self, steps):
        return {0: ("first",), steps - 1: ("fourth",)}

    def result(self, outs):
        return outs[0]

    def plain(self):
        return lax.psum(scatter(self.operands[0]), "dp")


def riding(body, counts, rides, steps):
    def kernel(*refs):
        refs = list(refs)

        def pop(count):
            taken = refs[:count]
            del refs[:count]
            return taken

        own = pop(counts[0])
        sources = [pop(len(ride.operands)) for ride in rides]
        own += pop(counts[1])
        targets = [pop(len(ride.out_shapes)) for ride in rides]
        own += pop(counts[2])
        jobs = [
            ride.job(source, target, pop(len(ride.scratch)))
            for ride, source, target in zip(rides, sources, targets)
        ]
        for step in range(steps):
            planned = [
                (job, stages)
                for ride, job in zip(rides, jobs)
                for at, stages in ride.before(steps).items()
                if at == step
            ]
            if planned:

                @pl.when(pl.program_id(0) == step)
                def _(planned=planned, step=step):
                    if step == 0:
                        greet()
                    for job, stages in planned:
                        run_stages([job], stages)

        body(*own)

        @pl.when(pl.program_id(0) == steps - 1)
        def _():
            for ride, job in zip(rides, jobs):
                run_stages([job], ride.after)

    return kernel


def block_call(
    body, grid, in_specs, operands, out_specs, out_shape, scratch, name,
    cost=None, rides=(), collective_id=None,
):
    plain = []
    if rides and not with_kernels():
        plain, rides = [ride.plain() for ride in rides], ()
    transfer = {}
    kernel = body
    if rides:
        transfer = {"collective_id": collective_id, "has_side_effects": True}
        kernel = riding(body, (len(operands), len(out_shape), len(scratch)), rides, grid)
    count = len(out_shape)
    for ride in rides:
        operands = [*operands, *ride.operands]
        in_specs = [*in_specs, *ride.in_specs]
        out_specs, out_shape = [*out_specs, *ride.out_specs], [*out_shape, *ride.out_shapes]
        scratch = [*scratch, *ride.scratch]
    outs = pl.pallas_call(
        kernel,
        grid=(grid,),
        in_specs=in_specs,
        out_specs=out_specs,
        out_shape=out_shape,
        scratch_shapes=scratch,
        compiler_params=pltpu.CompilerParams(vmem_limit_bytes=VMEM_LIMIT, **transfer),
        cost_estimate=cost or NO_COST,
        name=name,
    )(*operands)
    brought, outs = list(outs[count:]), list(outs[:count])
    for ride in rides:
        plain.append(ride.result(brought[: len(ride.out_shapes)]))
        brought = brought[len(ride.out_shapes) :]
    return outs + plain


def work(flops, size):
    return pl.CostEstimate(flops=flops, bytes_accessed=size, transcendentals=0)


def position_weights(seg_col, patch_row, nodes):
    rows = seg_col.shape[0]
    slot = lax.broadcasted_iota(jnp.int32, (rows, IMGS), 1)
    member = seg_col == slot
    counts = jnp.sum(member.astype(jnp.float32), 0, keepdims=True)
    start = jnp.sum(jnp.where(slot < seg_col, counts, 0.0), 1, keepdims=True)
    token = lax.broadcasted_iota(jnp.int32, (rows, 1), 0).astype(jnp.float32)
    inside = seg_col < IMGS
    offset = jnp.where(inside, token - start, 0.0)
    patch = jnp.sum(jnp.where(member, patch_row.astype(jnp.float32), 0.0), 1, keepdims=True)
    side = jnp.where(inside, jnp.floor(IMG / jnp.where(inside, patch, 1.0) + 0.5), 1.0)
    line = jnp.floor((offset + 0.5) / side)
    column = offset - line * side

    def spot(coord):
        return jnp.clip((2.0 * coord + 1.0) * GRID / (2.0 * side) - 0.5, 0.0, GRID - 1.0)

    node = lax.broadcasted_iota(jnp.int32, (rows, LANES), 1).astype(jnp.float32)
    across = jnp.floor((node + 0.5) / GRID)
    along = node - across * GRID
    weights = jnp.maximum(1.0 - jnp.abs(spot(line) - across), 0.0)
    weights = weights * jnp.maximum(1.0 - jnp.abs(spot(column) - along), 0.0)
    return jnp.where(node < nodes, weights, 0.0)


def first_kernel(*refs, spots):
    kernel, vectors, inputs, outputs, head, pixels, seg_col, patch_row, table, biases = refs[:10]
    stream, pos_t, vector_zero, vector_one = refs[10:14]
    qkv_full, up_full, output_level = refs[14:17]
    output_zero, qkv_one, up_one, output_one, head_low, normed, qkv_rows = refs[17:24]
    wide_kernel, wide_inputs, wide_outputs, wide_head, pixel_rows, table_low = refs[24:30]
    kernel_full, qkv_zero, vectors_full, qkv_landing, up_landing, output_landing = refs[30:36]
    up_zero, load_sems, sems = refs[36:]
    _, level, core = place()
    mine = 2 * level + core
    pairs = [
        (kernel, wide_kernel),
        (inputs.at[0], wide_inputs.at[0]),
        (pixels, pixel_rows),
        (inputs.at[1], wide_inputs.at[1]),
        (outputs.at[0], wide_outputs.at[0]),
        (outputs.at[1], wide_outputs.at[1]),
        (head, wide_head),
    ]
    copies = [
        pltpu.make_async_copy(source, target, load_sems.at[index])
        for index, (source, target) in enumerate(pairs)
    ]
    for copy in copies:
        copy.start()
    patch_job = Gather(kernel_full.at[mine], kernel_full, sems.at[0], True, in_place=True)
    vector_job = Gather(vectors, vectors_full, sems.at[1], False)
    qkv_job = Gather(qkv_zero, qkv_landing, sems.at[2], True)
    up_job = Gather(up_zero, up_landing, sems.at[3], True)
    output_job = LevelGather(output_zero, output_landing, sems.at[4])
    output_job.target = output_level
    copies[0].wait()
    kernel_full[mine] = wide_kernel[...].astype(LOW)
    greet()
    patch_job.first()
    vector_job.first()
    copies[1].wait()
    qkv_zero[...] = wide_inputs[0, :, : 3 * D].astype(LOW)
    qkv_job.first()
    up_zero[...] = wide_inputs[0, :, 3 * D :].astype(LOW)
    up_job.first()
    copies[4].wait()
    output_zero[...] = wide_outputs[0].astype(LOW)
    output_job.first()

    weights = position_weights(seg_col[...], patch_row[...], table.shape[0])
    pos_t[...] = weights.T[: pos_t.shape[0], :]
    table_low[...] = jnp.zeros_like(table_low)
    table_low[: table.shape[0], :] = table[...].astype(LOW).astype(jnp.float32)
    bias = biases[:, :D].astype(LOW).astype(jnp.float32)
    stream[...] = bias + jnp.dot(
        weights, table_low[...], precision=HIGHEST, preferred_element_type=jnp.float32
    )
    copies[2].wait()
    depth = wide_kernel.shape[0]

    def add_block(slot):
        columns = pl.ds(pl.multiple_of(slot * depth, depth), depth)

        def add(step, carry):
            rows = pl.ds(pl.multiple_of(step * 256, 256), 256)
            stream[rows, :] += mul(pixel_rows[rows, columns], kernel_full[slot])
            return carry

        lax.fori_loop(0, stream.shape[0] // 256, add, 0)

    def use(turn, own_core):
        add_block(2 * partner(level, turn) + (core if own_core else 1 - core))

    add_block(mine)
    patch_job.second()
    vector_job.second()
    qkv_job.second()
    up_job.second()
    patch_job.core_copy(0).wait_recv()
    use(0, False)
    copies[3].wait()
    qkv_one[...] = wide_inputs[1, :, : 3 * D].astype(LOW)
    up_one[...] = wide_inputs[1, :, 3 * D :].astype(LOW)
    copies[5].wait()
    output_one[...] = wide_outputs[1].astype(LOW)
    copies[6].wait()
    head_low[...] = jnp.zeros_like(head_low)
    head_low[:, : head.shape[1]] = wide_head[...].astype(LOW)
    patch_job.relay()
    qkv_job.relay()
    patch_job.third(use)
    up_job.relay()
    qkv_job.third()
    patch_job.fourth(use)
    vector_job.third()
    vector_job.fourth()
    blocks = [vectors_full[slot].astype(jnp.float32) for slot in range(vectors_full.shape[0])]
    span = vectors.shape[0] // LAYERS
    for layer, out in enumerate((vector_zero, vector_one)):
        for row in range(out.shape[1] // LANES):
            parts = [
                block[layer * span + row - spot : layer * span + row - spot + 1, :]
                for block, spot in zip(blocks, spots)
                if 0 <= row - spot < span
            ]
            out[:, row * LANES : (row + 1) * LANES] = sum(parts)
    up_job.third()
    qkv_job.fourth()
    copy = pltpu.make_async_copy(qkv_landing, qkv_full, load_sems.at[0])
    copy.start()
    weight = qkv_landing[...].reshape(-1, qkv_landing.shape[2])
    for half in halves_of(stream.shape[0]):
        unit, _ = normalized(stream[half, :])
        low = (unit * vector_zero[:, :D] + vector_zero[:, D : 2 * D]).astype(LOW)
        normed[half, :] = low
        for base in range(0, 3 * D, D):
            bias = vector_zero[:, 4 * D + base : 5 * D + base]
            qkv_rows[half, base : base + D] = (mul(low, weight[:, base : base + D]) + bias).astype(LOW)
    up_job.fourth()
    up_copy = pltpu.make_async_copy(up_landing, up_full, load_sems.at[1])
    up_copy.start()
    run_stages([output_job], ("fourth", "store"))
    copy.wait()
    up_copy.wait()


def padded_vectors(shard):
    layers, width = shard.shape
    owners = lax.axis_size("fsdp")
    spots = [owner * width // LANES for owner in range(owners)]
    span = max(-(-(owner + 1) * width // LANES) - spot for owner, spot in enumerate(spots))
    span += -span % 16
    shift = lax.rem(lax.axis_index("fsdp") * width, LANES)
    padded = jnp.zeros((layers, span * LANES), LOW)
    padded = lax.dynamic_update_slice(padded, shard.astype(LOW), (0, shift))
    return padded.reshape(layers * span, LANES), spots


def begin(
    pixels, segment, patch_size, patch_kernel, layer_vector, input_proj, output_proj, head_weight,
    position_table, global_vector,
):
    classes = head_weight.shape[1] + -head_weight.shape[1] % LANES
    nodes = position_table.shape[0] + -position_table.shape[0] % 64
    if not with_kernels():
        inputs = [
            (input_proj[index, :, : 3 * D].astype(LOW), input_proj[index, :, 3 * D :].astype(LOW))
            for index in range(LAYERS)
        ]
        outputs = [output_proj[index].astype(LOW) for index in range(LAYERS)]
        gather = lambda shard, axis: lax.all_gather(shard, "fsdp", axis=axis, tiled=True)
        weights, _, _ = row_layout(segment, patch_size[0])
        weights = jnp.pad(weights, ((0, 0), (0, nodes - weights.shape[1])))
        table = jnp.pad(rounded(position_table), ((0, nodes - position_table.shape[0]), (0, 0)))
        bias = rounded(global_vector)[None, :D]
        stream = embed(pixels, gather(patch_kernel.astype(LOW), 0), weights, table, bias)
        vectors = gather(layer_vector.astype(LOW), 1).astype(jnp.float32)
        head = jnp.pad(head_weight.astype(LOW), ((0, 0), (0, classes - head_weight.shape[1])))
        return (
            stream,
            weights.T,
            [vectors[index : index + 1] for index in range(LAYERS)],
            gather(inputs[0][0], 0),
            gather(inputs[0][1], 0),
            [GatherRide(outputs[0], outputs[0]), LevelRide(outputs[1])],
            [*inputs[1], head],
            qkv_forward(stream, gather(inputs[0][0], 0), vectors[:1]),
        )
    rows = pixels.shape[0]
    owners = lax.axis_size("fsdp")
    vectors, spots = padded_vectors(layer_vector)
    depth = input_proj.shape[1]
    up_shape = (depth, input_proj.shape[2] - 3 * D)
    qkv_shape, out_shape = (depth, 3 * D), output_proj.shape[1:]
    low = lambda *shape: jax.ShapeDtypeStruct(shape, LOW)
    levels = lambda shape: low(4, *quarter_shape(*shape))
    width = layer_vector.shape[1] * owners
    shapes = [
        shape_of(rows, D),
        shape_of(nodes, rows),
        shape_of(1, width),
        shape_of(1, width),
        low(owners, *qkv_shape),
        low(owners, *up_shape),
        levels(out_shape),
        low(*out_shape),
        low(*qkv_shape),
        low(*up_shape),
        low(*out_shape),
        low(head_weight.shape[0], classes),
        low(rows, D),
        low(rows, 3 * D),
    ]
    wide = (patch_kernel, input_proj, output_proj, head_weight, pixels)
    in_vmem = pl.BlockSpec(memory_space=pltpu.VMEM)
    results = pl.pallas_call(
        functools.partial(first_kernel, spots=spots),
        in_specs=[ANYWHERE] * 6 + [in_vmem] * 4,
        out_specs=[in_vmem] * 4 + [ANYWHERE] * 2 + [in_vmem] * 8,
        out_shape=shapes,
        scratch_shapes=[
            *[pltpu.VMEM(array.shape, array.dtype) for array in wide],
            pltpu.VMEM((LANES, D), jnp.float32),
            pltpu.VMEM((owners, *patch_kernel.shape), LOW),
            pltpu.VMEM(qkv_shape, LOW),
            pltpu.VMEM((owners, *vectors.shape), LOW),
            pltpu.VMEM((owners, *qkv_shape), LOW),
            pltpu.VMEM((owners, *up_shape), LOW),
            pltpu.VMEM((4, *quarter_shape(*out_shape)), LOW),
            pltpu.VMEM(up_shape, LOW),
            pltpu.SemaphoreType.DMA((7,)),
            pltpu.SemaphoreType.DMA((5, GATHER_SEMS)),
        ],
        compiler_params=pltpu.CompilerParams(
            collective_id=1, has_side_effects=True, vmem_limit_bytes=VMEM_LIMIT
        ),
        cost_estimate=NO_COST,
        name="begin",
    )(
        patch_kernel,
        vectors,
        input_proj,
        output_proj,
        head_weight,
        pixels,
        segment[:, None],
        patch_size,
        position_table,
        global_vector[None, :],
    )
    output_zero, qkv_one, up_one, output_one, head_low, normed, qkv_rows = results[7:]
    return (
        results[0],
        results[1],
        results[2:4],
        results[4].reshape(owners * depth, 3 * D),
        results[5].reshape(owners * depth, up_shape[1]),
        [GatherRide(output_zero, results[6]), LevelRide(output_one)],
        [qkv_one, up_one, head_low],
        (normed, qkv_rows),
    )


REDUCE_SEMS = 52


class Reduce:
    def __init__(self, grad, out, scratch, sems):
        self.grad, self.out, self.sems = grad, out, sems
        self.own, self.away, self.got_core, self.got_group, self.part, self.got_level = scratch
        self.rows, self.columns = out.shape
        self.chunk = 16

    def load(self, level):
        _, _, core = place()
        return pltpu.make_async_copy(
            self.grad.at[2 * level + core], self.own.at[level], self.sems.at[level]
        )

    def load_away(self, level):
        _, _, core = place()
        return pltpu.make_async_copy(
            self.grad.at[2 * level + 1 - core], self.away.at[level], self.sems.at[48 + level]
        )

    def core_copy(self, target_level):
        group, level, core = place()
        return remote(
            self.away.at[target_level],
            self.got_core.at[target_level],
            self.sems.at[4 + target_level],
            self.sems.at[8 + target_level],
            (group, 2 * level + 1 - core),
        )

    def group_copy(self, turn, other):
        group, level, core = place()
        target = partner(level, turn)
        peer = partner(group, other)
        part = quarter(peer, self.rows, self.columns)
        index = 3 * turn + other - 1
        return remote(
            self.own.at[target].at[part],
            self.got_group.at[other - 1, target],
            self.sems.at[12 + index],
            self.sems.at[24 + index],
            (peer, 2 * level + core),
        )

    def level_copy(self, turn):
        group, level, core = place()
        target = partner(level, turn)
        return remote(
            self.part.at[target],
            self.got_level.at[turn - 1],
            self.sems.at[35 + turn],
            self.sems.at[38 + turn],
            (group, 2 * target + core),
        )

    def share_copy(self, other):
        group, level, core = place()
        mine = self.out.at[quarter(group, self.rows, self.columns)]
        return remote(
            mine,
            mine,
            self.sems.at[41 + other],
            self.sems.at[44 + other],
            (partner(group, other), 2 * level + core),
        )

    def first(self):
        _, level, _ = place()
        for turn in (*TURNS, 0):
            self.load_away(partner(level, turn)).start()
        for turn in (*TURNS, 0):
            self.load(partner(level, turn)).start()
        for turn in (*TURNS, 0):
            self.load_away(partner(level, turn)).wait()
            self.core_copy(partner(level, turn)).start()

    def second(self):
        _, level, _ = place()
        for turn in (*TURNS, 0):
            target = partner(level, turn)
            self.load(target).wait()
            self.core_copy(target).wait_recv()

            def add(step, carry):
                rows = pl.ds(pl.multiple_of(step * self.chunk, self.chunk), self.chunk)
                total = self.own[target, rows, :].astype(jnp.float32)
                total = total + self.got_core[target, rows, :].astype(jnp.float32)
                self.own[target, rows, :] = total.astype(self.own.dtype)
                return carry

            lax.fori_loop(0, self.rows // self.chunk, add, 0)
            for other in TURNS:
                self.group_copy(turn, other).start()

    def between(self):
        pass

    def third(self):
        group, level, _ = place()
        high, wide = quarter_shape(self.rows, self.columns)
        row_part, column_part = quarter(group, self.rows, self.columns)
        for turn in (*TURNS, 0):
            target = partner(level, turn)
            for other in TURNS:
                self.group_copy(turn, other).wait_recv()

            def add(step, carry):
                at = pl.multiple_of(step * self.chunk, self.chunk)
                rows = pl.ds(at, self.chunk)
                mine = pl.ds(pl.multiple_of(row_part.start + at, self.chunk), self.chunk)
                total = self.own[target, mine, column_part].astype(jnp.float32)
                for slot in range(3):
                    total = total + self.got_group[slot, target, rows, :].astype(jnp.float32)
                self.part[target, rows, :] = total.astype(self.part.dtype)
                return carry

            lax.fori_loop(0, high // self.chunk, add, 0)
            if turn:
                self.level_copy(turn).start()

    def fourth(self):
        group, level, _ = place()
        high, wide = quarter_shape(self.rows, self.columns)
        row_part, column_part = quarter(group, self.rows, self.columns)
        for turn in TURNS:
            self.level_copy(turn).wait_recv()

        def add(step, carry):
            at = pl.multiple_of(step * self.chunk, self.chunk)
            rows = pl.ds(at, self.chunk)
            mine = pl.ds(pl.multiple_of(row_part.start + at, self.chunk), self.chunk)
            total = self.part[level, rows, :].astype(jnp.float32)
            for slot in range(3):
                total = total + self.got_level[slot, rows, :].astype(jnp.float32)
            self.out[mine, column_part] = total.astype(self.out.dtype)
            return carry

        lax.fori_loop(0, high // self.chunk, add, 0)
        for other in TURNS:
            self.share_copy(other).start()

    def store(self):
        self.target[...] = self.out[...]

    def fifth(self):
        for other in TURNS:
            self.share_copy(other).wait_recv()

    def sixth(self):
        _, level, _ = place()
        for turn in (*TURNS, 0):
            self.core_copy(partner(level, turn)).wait_send()
            for other in TURNS:
                self.group_copy(turn, other).wait_send()
            if turn:
                self.level_copy(turn).wait_send()
                self.share_copy(turn).wait_send()


WHOLE_SEMS = 44


def add_rows(target, row, columns, source, count, wide):
    chunk = 16 if wide > 1536 else 48

    def add(step, carry):
        at = pl.multiple_of(step * chunk, chunk)
        mine = pl.ds(pl.multiple_of(row + at, 16), chunk)
        total = target[mine, columns].astype(jnp.float32)
        total = total + source[pl.ds(at, chunk), :].astype(jnp.float32)
        target[mine, columns] = total.astype(target.dtype)
        return carry

    lax.fori_loop(0, count // chunk, add, 0)


class Whole:
    FIRST_X = (1, 0)

    lead = False

    def __init__(self, grad, out, scratch, sems):
        self.grad, self.out, self.sems = grad, out, sems
        self.own, self.away, self.got_core, self.got_x, self.got_y, self.got_last, self.part, self.got_level = scratch
        self.rows, self.columns = grad.shape[1:]
        self.high, self.wide = self.rows // 2, self.columns // 2

    def row_half(self, index):
        return pl.ds(pl.multiple_of(lax.div(index, 2) * self.high, self.high), self.high)

    def column_half(self, index):
        return pl.ds(pl.multiple_of(lax.rem(index, 2) * self.wide, self.wide), self.wide)

    def load(self, level):
        _, _, core = place()
        return pltpu.make_async_copy(
            self.grad.at[2 * level + core], self.own.at[level], self.sems.at[level]
        )

    def load_away(self, level):
        _, _, core = place()
        return pltpu.make_async_copy(
            self.grad.at[2 * level + 1 - core], self.away.at[level], self.sems.at[40 + level]
        )

    def core_copy(self, target_level):
        group, level, core = place()
        return remote(
            self.away.at[target_level],
            self.got_core.at[target_level],
            self.sems.at[4 + target_level],
            self.sems.at[8 + target_level],
            (group, 2 * level + 1 - core),
        )

    def step_copy(self, turn):
        group, level, core = place()
        block = self.own.at[partner(level, turn)]
        if turn in self.FIRST_X:
            peer = partner(group, 1)
            source = block.at[:, self.column_half(peer)]
            target = self.got_x.at[self.FIRST_X.index(turn)]
        else:
            peer = partner(group, 2)
            source = block.at[self.row_half(peer), :]
            target = self.got_y.at[turn - 2]
        return remote(
            source, target, self.sems.at[12 + turn], self.sems.at[16 + turn], (peer, 2 * level + core)
        )

    def last_copy(self, turn):
        group, level, core = place()
        block = self.own.at[partner(level, turn)]
        peer = partner(group, 2 if turn in self.FIRST_X else 1)
        rows = self.row_half(peer)
        columns = self.column_half(peer)
        return remote(
            block.at[rows, columns],
            self.got_last.at[turn],
            self.sems.at[20 + turn],
            self.sems.at[24 + turn],
            (peer, 2 * level + core),
        )

    def level_copy(self, turn):
        group, level, core = place()
        target = partner(level, turn)
        return remote(
            self.part.at[target],
            self.got_level.at[turn - 1],
            self.sems.at[27 + turn],
            self.sems.at[30 + turn],
            (group, 2 * target + core),
        )

    def share_copy(self, other):
        group, level, core = place()
        mine = self.out.at[self.row_half(group), self.column_half(group)]
        return remote(
            mine,
            mine,
            self.sems.at[33 + other],
            self.sems.at[36 + other],
            (partner(group, other), 2 * level + core),
        )

    def first(self):
        _, level, _ = place()
        for turn in (*TURNS, 0):
            self.load_away(partner(level, turn)).start()
        for turn in (*TURNS, 0):
            self.load(partner(level, turn)).start()
        for turn in (*TURNS, 0):
            self.load_away(partner(level, turn)).wait()
            self.core_copy(partner(level, turn)).start()

    def second(self):
        _, level, _ = place()
        for turn in (*TURNS, 0):
            target = partner(level, turn)
            self.load(target).wait()
            self.core_copy(target).wait_recv()
            add_rows(
                self.own.at[target], 0, slice(None), self.got_core.at[target], self.rows, self.columns
            )
            self.step_copy(turn).start()

    def between(self):
        group, level, _ = place()
        for turn in (*TURNS, 0):
            block = self.own.at[partner(level, turn)]
            self.step_copy(turn).wait_recv()
            if turn in self.FIRST_X:
                source = self.got_x.at[self.FIRST_X.index(turn)]
                add_rows(block, 0, self.column_half(group), source, self.rows, self.wide)
            else:
                source = self.got_y.at[turn - 2]
                start = lax.div(group, 2) * self.high
                add_rows(block, start, slice(None), source, self.high, self.columns)
            self.last_copy(turn).start()

    def third(self):
        group, level, _ = place()
        start = lax.div(group, 2) * self.high
        columns = self.column_half(group)
        chunk = 16 if self.wide > 1536 else 48
        for turn in (*TURNS, 0):
            target = partner(level, turn)
            self.last_copy(turn).wait_recv()

            def add(step, carry):
                at = pl.multiple_of(step * chunk, chunk)
                rows = pl.ds(at, chunk)
                mine = pl.ds(pl.multiple_of(start + at, 16), chunk)
                total = self.own[target, mine, columns].astype(jnp.float32)
                total = total + self.got_last[turn, rows, :].astype(jnp.float32)
                self.part[target, rows, :] = total.astype(self.part.dtype)
                return carry

            lax.fori_loop(0, self.high // chunk, add, 0)
            if turn and not self.lead:
                self.level_copy(turn).start()

    def fourth(self):
        group, level, _ = place()
        start = lax.div(group, 2) * self.high
        columns = self.column_half(group)
        chunk = 16 if self.wide > 1536 else 48
        for turn in TURNS:
            self.level_copy(turn).wait_recv()

        def add(step, carry):
            at = pl.multiple_of(step * chunk, chunk)
            rows = pl.ds(at, chunk)
            mine = pl.ds(pl.multiple_of(start + at, 16), chunk)
            total = self.part[level, rows, :].astype(jnp.float32)
            for slot in range(3):
                total = total + self.got_level[slot, rows, :].astype(jnp.float32)
            self.out[mine, columns] = total.astype(self.out.dtype)
            return carry

        lax.fori_loop(0, self.high // chunk, add, 0)
        for other in TURNS:
            self.share_copy(other).start()

    def store(self):
        self.target[...] = self.out[...]

    def fifth(self):
        for other in TURNS:
            self.share_copy(other).wait_recv()

    def sixth(self):
        _, level, _ = place()
        for turn in (*TURNS, 0):
            self.core_copy(partner(level, turn)).wait_send()
            self.step_copy(turn).wait_send()
            self.last_copy(turn).wait_send()
            if turn and not self.lead:
                self.level_copy(turn).wait_send()
                self.share_copy(turn).wait_send()


class Lead(Whole):
    lead = True

    def store(self):
        self.target[...] = self.part[...]


class Rest(Whole):
    def __init__(self, part, out, got_level, sems):
        self.part, self.out, self.got_level, self.sems = part, out, got_level, sems
        self.rows, self.columns = out.shape
        self.high, self.wide = self.rows // 2, self.columns // 2

    def first(self):
        for turn in TURNS:
            self.level_copy(turn).start()

    def sixth(self):
        for turn in TURNS:
            self.level_copy(turn).wait_send()
            self.share_copy(turn).wait_send()


GROUP_SEMS = 13


class GroupReduce:
    def __init__(self, share, out, scratch, sems):
        self.share, self.out, self.sems = share, out, sems
        self.own, self.got = scratch
        self.rows, self.columns = out.shape
        self.chunk = 16

    def load(self):
        return pltpu.make_async_copy(self.share, self.own, self.sems.at[0])

    def group_copy(self, other):
        group, level, core = place()
        peer = partner(group, other)
        return remote(
            self.own.at[quarter(peer, self.rows, self.columns)],
            self.got.at[other - 1],
            self.sems.at[other],
            self.sems.at[3 + other],
            (peer, 2 * level + core),
        )

    def share_copy(self, other):
        group, level, core = place()
        mine = self.out.at[quarter(group, self.rows, self.columns)]
        return remote(
            mine,
            mine,
            self.sems.at[6 + other],
            self.sems.at[9 + other],
            (partner(group, other), 2 * level + core),
        )

    def first(self):
        self.load().start()

    def second(self):
        self.load().wait()
        for other in TURNS:
            self.group_copy(other).start()

    def between(self):
        pass

    def third(self):
        group, _, _ = place()
        high, wide = quarter_shape(self.rows, self.columns)
        row_part, column_part = quarter(group, self.rows, self.columns)
        for other in TURNS:
            self.group_copy(other).wait_recv()

        def add(step, carry):
            at = pl.multiple_of(step * self.chunk, self.chunk)
            rows = pl.ds(at, self.chunk)
            mine = pl.ds(pl.multiple_of(row_part.start + at, self.chunk), self.chunk)
            total = self.own[mine, column_part].astype(jnp.float32)
            for slot in range(3):
                total = total + self.got[slot, rows, :].astype(jnp.float32)
            self.out[mine, column_part] = total.astype(self.out.dtype)
            return carry

        lax.fori_loop(0, high // self.chunk, add, 0)
        for other in TURNS:
            self.share_copy(other).start()

    def fourth(self):
        pass

    def fifth(self):
        for other in TURNS:
            self.share_copy(other).wait_recv()

    def store(self):
        self.target[...] = self.out[...]

    def sixth(self):
        for other in TURNS:
            self.group_copy(other).wait_send()
            self.share_copy(other).wait_send()


class Spread:
    def __init__(self, full, sems):
        self.full, self.sems = full, sems

    def level_copy(self, turn):
        group, level, core = place()
        block = self.full.at[2 * level + core]
        peer = (group, 2 * partner(level, turn) + core)
        return remote(block, block, self.sems.at[turn - 1], self.sems.at[2 + turn], peer)

    def core_copy(self, turn):
        group, level, core = place()
        block = self.full.at[2 * partner(level, turn) + core]
        peer = (group, 2 * level + 1 - core)
        return remote(block, block, self.sems.at[6 + turn], self.sems.at[10 + turn], peer)

    def run(self):
        for turn in TURNS:
            self.level_copy(turn).start()
        self.core_copy(0).start()
        for turn in TURNS:
            self.level_copy(turn).wait_recv()
            self.core_copy(turn).start()
        for turn in (0, *TURNS):
            self.core_copy(turn).wait_recv()
        for turn in (0, *TURNS):
            self.core_copy(turn).wait_send()
            if turn:
                self.level_copy(turn).wait_send()


def squares_in(out):
    def add(step, total):
        piece = out[pl.ds(pl.multiple_of(step * 16, 16), 16), :].astype(jnp.float32)
        piece = piece * piece
        for lane in range(0, out.shape[1], LANES):
            total = total + piece[:, lane : lane + LANES]
        return total

    total = lax.fori_loop(0, out.shape[0] // 16, add, jnp.zeros((16, LANES), jnp.float32))
    return jnp.sum(total, 0, keepdims=True)


def run_stages(jobs, stages):
    for stage in stages:
        for job in jobs:
            getattr(job, stage)()


STAGES = ("first", "second", "between", "third", "fourth", "fifth", "sixth")


def whole_scratch(grad):
    _, rows, columns = grad.shape
    high, wide = quarter_shape(rows, columns)
    shapes = (*[(4, rows, columns)] * 3, (3, 4, high, wide), (4, high, wide))
    return [pltpu.VMEM(shape, grad.dtype) for shape in (*shapes, (3, high, wide))]


def stepped_scratch(grad):
    _, rows, columns = grad.shape
    high, wide = rows // 2, columns // 2
    shapes = (
        *[(4, rows, columns)] * 3,
        (2, rows, wide),
        (2, high, columns),
        (4, high, wide),
        (4, high, wide),
        (3, high, wide),
    )
    return [pltpu.VMEM(shape, grad.dtype) for shape in shapes]


def share_scratch(share):
    return [
        pltpu.VMEM(share.shape, share.dtype),
        pltpu.VMEM((3, *quarter_shape(*share.shape)), share.dtype),
    ]


def reduce_kernel(*refs, whole, partly):
    count = whole + 1 + partly
    grads, outs, refs = refs[:count], refs[count : 2 * count], refs[2 * count :]
    sems, small_sems, group_sems, refs = refs[0], refs[1], refs[2], refs[3:]
    jobs = [
        Whole(grads[i], outs[i], refs[8 * i : 8 * i + 8], sems.at[i]) for i in range(whole)
    ]
    refs = refs[8 * whole :]
    small = Reduce(grads[whole], outs[whole], refs[:6], small_sems)
    refs = refs[6:]
    shares = [
        GroupReduce(
            grads[whole + 1 + i], outs[whole + 1 + i], refs[2 * i : 2 * i + 2], group_sems.at[i]
        )
        for i in range(partly)
    ]
    greet()
    run_stages([*jobs, small, *shares], STAGES[:1])
    run_stages([small, *shares], STAGES[1:2])
    run_stages(jobs, STAGES[1:3])
    run_stages([small, *shares], STAGES[3:4])
    run_stages(jobs, STAGES[3:4])
    run_stages([small, *jobs], STAGES[4:5])
    run_stages([*shares, small, *jobs], STAGES[5:])


def transfer_outs(arrays):
    return [jax.ShapeDtypeStruct(array.shape[-2:], array.dtype) for array in arrays]


def reduce_call(grads, small, shares, collective_id):
    in_vmem = pl.BlockSpec(memory_space=pltpu.VMEM)
    whole, partly = len(grads), len(shares)
    operands = [*grads, small, *shares]
    scratch = [
        pltpu.SemaphoreType.DMA((whole, WHOLE_SEMS)),
        pltpu.SemaphoreType.DMA((REDUCE_SEMS,)),
        pltpu.SemaphoreType.DMA((partly, GROUP_SEMS)),
    ]
    for grad in grads:
        scratch.extend(stepped_scratch(grad))
    scratch.extend(whole_scratch(small))
    for share in shares:
        scratch.extend(share_scratch(share))
    return pl.pallas_call(
        functools.partial(reduce_kernel, whole=whole, partly=partly),
        in_specs=[ANYWHERE] * len(operands),
        out_specs=[in_vmem] * len(operands),
        out_shape=transfer_outs(operands),
        scratch_shapes=scratch,
        compiler_params=pltpu.CompilerParams(
            collective_id=collective_id, has_side_effects=True, vmem_limit_bytes=VMEM_LIMIT
        ),
        cost_estimate=NO_COST,
        name="reduce_gradients",
    )(*operands)


def totals(full, vector_rows, rest_size):
    owners, rows, _ = full.shape
    rest_rows = -(-rest_size // (owners * LANES))
    row = lax.broadcasted_iota(jnp.int32, full.shape, 1)
    spot = row - vector_rows + rest_rows * lax.broadcasted_iota(jnp.int32, full.shape, 0)
    spot = spot * LANES + lax.broadcasted_iota(jnp.int32, full.shape, 2)
    in_rest = (row >= vector_rows) & (row < vector_rows + rest_rows)

    def summed(values):
        return jnp.sum(jnp.sum(jnp.sum(values, 0), 0, keepdims=True), 1, keepdims=True)

    tokens = summed(jnp.where(in_rest & (spot == rest_size - 1), full, 0.0))
    loss = summed(jnp.where(in_rest & (spot == rest_size - 2), full, 0.0))
    kept = (row < vector_rows) | (in_rest & (spot < rest_size - 2))
    squares = jnp.where(kept, full * full, jnp.where(row == rows - 1, full, 0.0))
    norm = jnp.sqrt(summed(squares)) / tokens
    factor = jnp.minimum(1.0, CLIP_NORM / norm) / tokens
    lane = lax.broadcasted_iota(jnp.int32, (1, LANES), 1)
    return jnp.where(
        lane == 0, factor, jnp.where(lane == 1, norm, jnp.where(lane == 2, loss, tokens))
    )


def finish_kernel(*refs, done, partly, vector_rows, rest_size):
    finished, small, refs = refs[:done], refs[done], refs[done + 1 :]
    shares, refs = refs[:partly], refs[partly:]
    outs, full, numbers, refs = refs[:partly], refs[partly], refs[partly + 1], refs[partly + 2 :]
    group_sems, spread_sems, refs = refs[0], refs[1], refs[2:]
    jobs = [
        GroupReduce(shares[i], outs[i], refs[2 * i : 2 * i + 2], group_sems.at[i])
        for i in range(partly)
    ]
    greet()
    run_stages(jobs, STAGES[:2])
    total = sum(squares_in(out) for out in finished)
    run_stages(jobs, STAGES[3:6])
    total = total + sum(squares_in(out) for out in outs)
    _, level, core = place()
    mine = 2 * level + core
    last = small.shape[0] - 1
    full[mine] = small[...]
    full[mine, last : last + 1, :] = total
    Spread(full, spread_sems).run()
    numbers[...] = totals(full[...], vector_rows, rest_size)
    run_stages(jobs, STAGES[6:])


def finish_call(finished, small, shares, vector_rows, rest_size, collective_id):
    done, partly = len(finished), len(shares)
    in_vmem = pl.BlockSpec(memory_space=pltpu.VMEM)
    scratch = [
        pltpu.SemaphoreType.DMA((partly, GROUP_SEMS)),
        pltpu.SemaphoreType.DMA((14,)),
    ]
    for share in shares:
        scratch.extend(share_scratch(share))
    full = (lax.axis_size("fsdp"), *small.shape)
    out_shape = [*transfer_outs(shares), jax.ShapeDtypeStruct(full, small.dtype), shape_of(1, LANES)]
    return pl.pallas_call(
        functools.partial(
            finish_kernel, done=done, partly=partly, vector_rows=vector_rows, rest_size=rest_size
        ),
        in_specs=[in_vmem] * (done + 1) + [ANYWHERE] * partly,
        out_specs=[in_vmem] * len(out_shape),
        out_shape=out_shape,
        scratch_shapes=scratch,
        compiler_params=pltpu.CompilerParams(
            collective_id=collective_id, has_side_effects=True, vmem_limit_bytes=VMEM_LIMIT
        ),
        name="finish_gradients",
    )(*finished, small, *shares)


def with_kernels():
    return lax.axis_size("dp") == 4 and lax.axis_size("fsdp") == 8


def reduce_all(grads, small, shares, collective_id):
    if with_kernels():
        return reduce_call(grads, small, shares, collective_id)
    return [lax.psum(scatter(grad), "dp") for grad in (*grads, small)] + [
        lax.psum(share, "dp") for share in shares
    ]


def finish_all(finished, small, shares, vector_rows, rest_size, collective_id):
    if with_kernels():
        return finish_call(finished, small, shares, vector_rows, rest_size, collective_id)
    outs = [lax.psum(share, "dp") for share in shares]
    total = sum(jnp.sum(jnp.square(out.astype(jnp.float32))) for out in (*finished, *outs))
    row = jnp.full((1, LANES), 1.0 / LANES, jnp.float32) * total
    full = lax.all_gather(small.at[-1:].set(row), "fsdp", axis=0)
    return [*outs, full, totals(full, vector_rows, rest_size)]


def scatter(grad):
    return lax.psum_scatter(grad, "fsdp", scatter_dimension=0)


def by_owner(grad, low=jnp.bfloat16):
    owners = lax.axis_size("fsdp")
    return grad.astype(low).reshape(owners, grad.shape[0] // owners, grad.shape[1])


def attention_forward_kernel(
    q_ref, k_ref, v_ref, seg_col_ref, seg_row_ref, out_ref, expo_ref, inv_ref, *, block
):
    rows = q_ref.shape[0]
    lower = lax.broadcasted_iota(jnp.int32, (block, PAIR), 1) < HD
    keys = k_ref[...]
    values = jnp.concatenate([v_ref[...], jnp.ones((rows, PAIR), v_ref.dtype)], 1)
    seg_row = seg_row_ref[...]
    tasks = [(step, head) for step in range(rows // block) for head in range(2)]

    def scores_of(step, head):
        query = q_ref[step * block : (step + 1) * block, :] * jnp.bfloat16(HD**-0.5)
        keep = lower if head == 0 else jnp.logical_not(lower)
        return mul_nt(jnp.where(keep, query, jnp.bfloat16(0)), keys)

    scores = scores_of(*tasks[0])
    outs = []
    for index, (step, head) in enumerate(tasks):
        following = scores_of(*tasks[index + 1]) if index + 1 < len(tasks) else None
        at = slice(step * block, (step + 1) * block)
        scores = jnp.where(seg_col_ref[at, :] == seg_row, scores, MASKED)
        highest = jnp.max(scores, -1, keepdims=True)
        low = jnp.exp(scores - highest).astype(jnp.bfloat16)
        expo_ref[head, at, :] = low
        outs.append(mul(low, values))
        if head:
            inverse = 1.0 / jnp.where(lower, outs[0][:, PAIR:], outs[1][:, PAIR:])
            sums = jnp.where(lower, outs[0][:, :PAIR], outs[1][:, :PAIR])
            out_ref[at, :] = (sums * inverse).astype(jnp.bfloat16)
            inv_ref[at, :] = inverse
            outs = []
        scores = following


def attention_forward(qkv_rows, segment, rides, collective_id):
    rows = qkv_rows.shape[0]
    pairs = HEADS // 2
    wide = lambda base: pl.BlockSpec((rows, PAIR), lambda j, base=base: (0, base + j))
    return block_call(
        functools.partial(attention_forward_kernel, block=min(256, rows)),
        pairs,
        [wide(0), wide(pairs), wide(2 * pairs), fixed(rows, 1), fixed(1, rows)],
        [qkv_rows, qkv_rows, qkv_rows, segment[:, None], segment[None, :]],
        [wide(0), pl.BlockSpec((2, rows, rows), lambda j: (j, 0, 0)), wide(0)],
        [
            shape_of(rows, D, dtype=LOW),
            shape_of(HEADS, rows, rows, dtype=LOW),
            shape_of(rows, D),
        ],
        [],
        "attention_forward",
        work(16 * HEADS * rows * rows * HD, 2 * HEADS * rows * rows + 12 * rows * D),
        rides,
        collective_id,
    )


def attention_backward_kernel(
    q_ref, k_ref, v_ref, expo_ref, inv_ref, out_ref, grad_ref, dqkv_ref, *, block
):
    rows = q_ref.shape[0]
    pair = pl.program_id(0)
    lower = lax.broadcasted_iota(jnp.int32, (block, PAIR), 1) < HD
    keys = k_ref[...]
    values = v_ref[...]
    scale = HD**-0.5
    scaled_grad = (grad_ref[...].astype(jnp.float32) * inv_ref[...]).astype(jnp.bfloat16)
    query = q_ref[...]
    query_t = query.T
    grad_t = scaled_grad.T
    product = scaled_grad.astype(jnp.float32) * out_ref[...].astype(jnp.float32)
    key_t = [None, None]
    value_t = [None, None]
    tasks = [(step, head) for step in range(rows // block) for head in range(2)]

    def probs_grad_of(step, head):
        keep = lower if head == 0 else jnp.logical_not(lower)
        mine = scaled_grad[step * block : (step + 1) * block]
        return mul_nt(jnp.where(keep, mine, jnp.bfloat16(0)), values)

    probs_grad = probs_grad_of(*tasks[0])
    query_parts = []
    for index, (step, head) in enumerate(tasks):
        following = probs_grad_of(*tasks[index + 1]) if index + 1 < len(tasks) else None
        at = slice(step * block, (step + 1) * block)
        lanes = slice(head * HD, (head + 1) * HD)
        keep = lower if head == 0 else jnp.logical_not(lower)
        inner = jnp.sum(jnp.where(keep, product[at], 0.0), -1, keepdims=True)
        low = expo_ref[head, at, :]
        value_part = mul(grad_t[lanes, at], low)
        scores_grad = (low.astype(jnp.float32) * (probs_grad - inner)).astype(jnp.bfloat16)
        query_parts.append(mul(scores_grad, keys))
        key_part = mul(query_t[lanes, at], scores_grad)
        key_t[head] = key_part if step == 0 else key_t[head] + key_part
        value_t[head] = value_part if step == 0 else value_t[head] + value_part
        if head:
            query_grad = jnp.where(lower, query_parts[0], query_parts[1]) * scale
            dqkv_ref[at, pl.ds(pl.multiple_of(pair * PAIR, PAIR), PAIR)] = query_grad.astype(
                jnp.bfloat16
            )
            query_parts = []
        probs_grad = following
    key_grad = (jnp.concatenate(key_t, 0) * scale).T
    value_grad = jnp.concatenate(value_t, 0).T
    dqkv_ref[:, pl.ds(pl.multiple_of(D + pair * PAIR, PAIR), PAIR)] = key_grad.astype(jnp.bfloat16)
    dqkv_ref[:, pl.ds(pl.multiple_of(2 * D + pair * PAIR, PAIR), PAIR)] = value_grad.astype(jnp.bfloat16)


def attention_backward(qkv_rows, expo, inverse, attended, attended_grad, rides, collective_id):
    rows = qkv_rows.shape[0]
    pairs = HEADS // 2
    wide = lambda base: pl.BlockSpec((rows, PAIR), lambda j, base=base: (0, base + j))
    return block_call(
        functools.partial(attention_backward_kernel, block=min(256, rows)),
        pairs,
        [
            wide(0),
            wide(pairs),
            wide(2 * pairs),
            pl.BlockSpec((2, rows, rows), lambda j: (j, 0, 0)),
            wide(0),
            wide(0),
            wide(0),
        ],
        [qkv_rows, qkv_rows, qkv_rows, expo, inverse, attended, attended_grad],
        [fixed(rows, 3 * D)],
        [shape_of(rows, 3 * D, dtype=LOW)],
        [],
        "attention_backward",
        None,
        rides,
        collective_id,
    )


def mul(left, right):
    return jnp.dot(left, right, preferred_element_type=jnp.float32)


def mul_nt(left, right):
    return lax.dot_general(left, right, NT, preferred_element_type=jnp.float32)


def normalized(values):
    center = values - jnp.mean(values, -1, keepdims=True)
    inverse = lax.rsqrt(jnp.mean(center * center, -1, keepdims=True) + NORM_EPS)
    return center * inverse, inverse


def norm_backward(grad, values, gain):
    unit, inverse = normalized(values)
    inner = grad * gain
    mean_inner = jnp.mean(inner, -1, keepdims=True)
    mean_cross = jnp.mean(inner * unit, -1, keepdims=True)
    value_grad = inverse * (inner - mean_inner - unit * mean_cross)
    return value_grad, column_sum(grad * unit), column_sum(grad)


def column_sum(rows):
    return jnp.sum(rows.astype(jnp.float32), 0, keepdims=True)


def at_first(action):
    pl.when(pl.program_id(0) == 0)(action)


def rows_of(block, columns):
    return pl.BlockSpec((block, columns), lambda i: (i, 0))


def fixed(*shape):
    return pl.BlockSpec(shape, lambda i: (0,) * len(shape), pipeline_mode=pl.Buffered(1))


def loads(sources, targets, sems):
    return [
        pltpu.make_async_copy(source, target, sems.at[index])
        for index, (source, target) in enumerate(zip(sources, targets))
    ]


def shape_of(*shape, dtype=jnp.float32):
    return jax.ShapeDtypeStruct(shape, dtype)


def embed_kernel(pixel_ref, weight_ref, pos_ref, table_ref, bias_ref, out_ref):
    position = jnp.dot(
        pos_ref[...], table_ref[...], precision=HIGHEST, preferred_element_type=jnp.float32
    )
    out_ref[...] = mul(pixel_ref[...], weight_ref[...]) + bias_ref[...] + position


def embed(pixels, weight, pos_weights, table, bias):
    rows, depth = pixels.shape
    block = 256
    nodes = pos_weights.shape[1]
    return block_call(
        embed_kernel,
        rows // block,
        [rows_of(block, depth), fixed(depth, D), rows_of(block, nodes), fixed(nodes, D), fixed(1, D)],
        [pixels, weight, pos_weights, table, bias],
        [rows_of(block, D)],
        [shape_of(rows, D)],
        [],
        "embed",
        work(2 * rows * depth * D, 2 * rows * depth + 2 * depth * D + 4 * rows * D),
    )[0]


def chunk_at(base):
    return pl.ds(pl.multiple_of(base + pl.program_id(0) * D, LANES), D)


def columns_of(rows):
    return pl.BlockSpec((rows, D), lambda i: (0, i))


def halves_of(rows):
    half = rows // 2
    return [slice(start, start + half) for start in range(0, rows, half)]


def at_last(action):
    pl.when(pl.program_id(0) == pl.num_programs(0) - 1)(action)


def qkv_kernel(stream_ref, weight_ref, vector_ref, normed_out, qkv_ref, normed_ref, sem):
    copy = pltpu.make_async_copy(normed_ref, normed_out, sem)

    @at_first
    def _():
        unit, _ = normalized(stream_ref[...])
        normed_ref[...] = (unit * vector_ref[:, :D] + vector_ref[:, D : 2 * D]).astype(LOW)
        copy.start()

    bias = vector_ref[:, chunk_at(4 * D)]
    for half in halves_of(stream_ref.shape[0]):
        qkv_ref[half, :] = (mul(normed_ref[half, :], weight_ref[...]) + bias).astype(LOW)
    at_last(copy.wait)


def qkv_forward(stream, weight, vector):
    rows = stream.shape[0]
    return block_call(
        qkv_kernel,
        3,
        [fixed(rows, D), columns_of(D), fixed(1, vector.shape[1])],
        [stream, weight, vector],
        [ANYWHERE, columns_of(rows)],
        [shape_of(rows, D, dtype=LOW), shape_of(rows, 3 * D, dtype=LOW)],
        [pltpu.VMEM((rows, D), LOW), pltpu.SemaphoreType.DMA],
        "qkv_forward",
        work(6 * rows * D * D, 14 * rows * D + 6 * D * D),
    )


def mlp_kernel(
    stream_ref, attended_ref, mix_ref, up_ref, down_ref, vector_ref,
    residual_out, normed_out, active_ref, slope_ref, out_ref,
    residual_ref, normed_ref, sems,
):
    rows = stream_ref.shape[0]
    copies = loads((residual_ref, normed_ref), (residual_out, normed_out), sems)

    @at_first
    def _():
        for half in halves_of(rows):
            residual = stream_ref[half, :] + mul(attended_ref[half, :], mix_ref[...])
            residual = residual + vector_ref[:, 7 * D : 8 * D]
            residual_ref[half, :] = residual
            unit, _ = normalized(residual)
            normed = unit * vector_ref[:, 2 * D : 3 * D] + vector_ref[:, 3 * D : 4 * D]
            normed_ref[half, :] = normed.astype(LOW)
            out_ref[half, :] = residual + vector_ref[:, 8 * D : 9 * D]
        for copy in copies:
            copy.start()

    bias = vector_ref[:, chunk_at(9 * D)]
    parts = halves_of(rows)
    hidden = mul(normed_ref[parts[0], :], up_ref[...]) + bias
    for index, half in enumerate(parts):
        following = None
        if index + 1 < len(parts):
            following = mul(normed_ref[parts[index + 1], :], up_ref[...]) + bias
        square = hidden * hidden
        rise = 0.5 + 0.5 * jnp.tanh(hidden * (ROOT + (ROOT * CUBE) * square))
        active = hidden * rise
        active_low = active.astype(LOW)
        active_ref[half, :] = active_low
        bend = (2.0 * ROOT) + (6.0 * ROOT * CUBE) * square
        slope_ref[half, :] = (rise + active * (1.0 - rise) * bend).astype(LOW)
        out_ref[half, :] += mul(active_low, down_ref[...])
        hidden = following

    @at_last
    def _():
        for copy in copies:
            copy.wait()


def mlp_specs(up, proj_out):
    return (
        [fixed(D, D), columns_of(D), pl.BlockSpec((D, D), lambda i: (i + 1, 0))],
        [proj_out, up, proj_out],
    )


def mlp_forward(stream, attended, up, proj_out, vector):
    rows = stream.shape[0]
    width = up.shape[1]
    weight_specs, weights = mlp_specs(up, proj_out)
    return block_call(
        mlp_kernel,
        width // D,
        [fixed(rows, D), fixed(rows, D), *weight_specs, fixed(1, vector.shape[1])],
        [stream, attended, *weights, vector],
        [ANYWHERE, ANYWHERE, columns_of(rows), columns_of(rows), fixed(rows, D)],
        [
            shape_of(rows, D),
            shape_of(rows, D, dtype=LOW),
            shape_of(rows, width, dtype=LOW),
            shape_of(rows, width, dtype=LOW),
            shape_of(rows, D),
        ],
        [
            pltpu.VMEM((rows, D), jnp.float32),
            pltpu.VMEM((rows, D), LOW),
            pltpu.SemaphoreType.DMA((2,)),
        ],
        "mlp_forward",
        work(2 * rows * D * (D + 2 * width), rows * (16 * D + 4 * width) + 2 * D * (D + 2 * width)),
    )


def mlp_back_kernel(
    grad_ref, slope_ref, residual_in, normed_ref, active_ref, attended_ref, mix_ref, up_ref, down_ref, vector_ref,
    out_ref, attended_grad_ref, sums_ref, up_grad_ref, output_grad,
    residual_ref, low_ref, second_ref, turned_ref, hidden_ref, product_ref, sems,
):
    rows = grad_ref.shape[0]
    step = pl.program_id(0)
    load = pltpu.make_async_copy(residual_in, residual_ref, sems.at[0])

    def store_copy(slot):
        rows_at = pl.ds(pl.multiple_of(slot * D, D), D)
        return pltpu.make_async_copy(
            product_ref.at[slot], output_grad.at[rows_at], sems.at[1 + slot]
        )

    def store(slot, product):
        product_ref[slot] = product.astype(LOW)
        store_copy(slot).start()

    @at_first
    def _():
        load.start()
        low_ref[...] = grad_ref[...].astype(LOW)
        turned_ref[...] = normed_ref[...].T
        second_ref[...] = jnp.zeros_like(second_ref)

    parts = halves_of(rows)
    active_grad = mul_nt(low_ref[parts[0], :], down_ref[...])
    hidden_sum = 0.0
    for index, half in enumerate(parts):
        following = None
        if index + 1 < len(parts):
            following = mul_nt(low_ref[parts[index + 1], :], down_ref[...])
        hidden_grad = (active_grad * slope_ref[half, :].astype(jnp.float32)).astype(LOW)
        hidden_ref[half, :] = hidden_grad
        hidden_sum = hidden_sum + column_sum(hidden_grad)
        second_ref[half, :] += mul_nt(hidden_grad, up_ref[...])
        active_grad = following
    sums_ref[:, chunk_at(4 * D)] = hidden_sum
    store(step + 1, mul(active_ref[...].T, low_ref[...]))
    up_grad_ref[...] = mul(turned_ref[...], hidden_ref[...]).astype(LOW)

    @at_last
    def _():
        load.wait()
        gain = vector_ref[:, 2 * D : 3 * D]
        totals = [0.0] * 4
        for half in halves_of(rows):
            grad = grad_ref[half, :]
            value_grad, gain_grad, shift_grad = norm_backward(
                second_ref[half, :], residual_ref[half, :], gain
            )
            total = value_grad + grad
            out_ref[half, :] = total
            total_low = total.astype(LOW)
            hidden_ref[half, :] = total_low
            attended_grad_ref[half, :] = mul_nt(total_low, mix_ref[...]).astype(LOW)
            new = (gain_grad, shift_grad, column_sum(total_low), column_sum(low_ref[half, :]))
            totals = [old + part for old, part in zip(totals, new)]
        sums_ref[:, : 4 * D] = jnp.concatenate(totals, 1)
        store(0, mul(attended_ref[...].T, hidden_ref[...]))
        for slot in range(product_ref.shape[0]):
            store_copy(slot).wait()


def mlp_backward(
    grad, slope, residual, normed, active, attended, up, proj_out, vector, rides, collective_id
):
    rows = grad.shape[0]
    width = up.shape[1]
    steps = width // D
    whole = fixed(rows, D)
    weight_specs, weights = mlp_specs(up, proj_out)
    return block_call(
        mlp_back_kernel,
        steps,
        [
            whole,
            columns_of(rows),
            ANYWHERE,
            whole,
            columns_of(rows),
            whole,
            *weight_specs,
            fixed(1, vector.shape[1]),
        ],
        [grad, slope, residual, normed, active, attended, *weights, vector],
        [whole, whole, fixed(1, 4 * D + width), columns_of(D), ANYWHERE],
        [
            shape_of(rows, D),
            shape_of(rows, D, dtype=LOW),
            shape_of(1, 4 * D + width),
            shape_of(D, width, dtype=LOW),
            shape_of(D + width, D, dtype=LOW),
        ],
        [
            pltpu.VMEM((rows, D), jnp.float32),
            pltpu.VMEM((rows, D), LOW),
            pltpu.VMEM((rows, D), jnp.float32),
            pltpu.VMEM((D, rows), LOW),
            pltpu.VMEM((rows, D), LOW),
            pltpu.VMEM((steps + 1, D, D), LOW),
            pltpu.SemaphoreType.DMA((steps + 2,)),
        ],
        "mlp_backward",
        None,
        rides,
        collective_id,
    )


def qkv_back_kernel(
    grad_ref, residual_in, stream_in, normed_ref, weight_ref, vector_ref,
    out_ref, sums_ref, weight_grad_ref,
    residual_ref, stream_ref, sum_ref, turned_ref, sems,
):
    rows = out_ref.shape[0]
    copies = loads((residual_in, stream_in), (residual_ref, stream_ref), sems)

    @at_first
    def _():
        for copy in copies:
            copy.start()
        turned_ref[...] = normed_ref[...].T
        sum_ref[...] = jnp.zeros_like(sum_ref)

    for half in halves_of(rows):
        sum_ref[half, :] += mul_nt(grad_ref[half, :], weight_ref[...])
    sums_ref[:, chunk_at(2 * D)] = column_sum(grad_ref[...])
    weight_grad_ref[...] = mul(turned_ref[...], grad_ref[...]).astype(LOW)

    @at_last
    def _():
        for copy in copies:
            copy.wait()
        totals = [0.0] * 2
        for half in halves_of(rows):
            value_grad, gain_grad, shift_grad = norm_backward(
                sum_ref[half, :], stream_ref[half, :], vector_ref[:, :D]
            )
            out_ref[half, :] = residual_ref[half, :] + value_grad
            totals = [totals[0] + gain_grad, totals[1] + shift_grad]
        sums_ref[:, : 2 * D] = jnp.concatenate(totals, 1)


def qkv_backward(grad, residual_grad, stream, normed, weight, vector, rides, collective_id):
    rows = stream.shape[0]
    whole = fixed(rows, D)
    return block_call(
        qkv_back_kernel,
        3,
        [columns_of(rows), ANYWHERE, ANYWHERE, whole, columns_of(D), fixed(1, vector.shape[1])],
        [grad, residual_grad, stream, normed, weight, vector],
        [whole, fixed(1, 5 * D), columns_of(D)],
        [shape_of(rows, D), shape_of(1, 5 * D), shape_of(D, 3 * D, dtype=LOW)],
        [
            pltpu.VMEM((rows, D), jnp.float32),
            pltpu.VMEM((rows, D), jnp.float32),
            pltpu.VMEM((rows, D), jnp.float32),
            pltpu.VMEM((D, rows), LOW),
            pltpu.SemaphoreType.DMA((2,)),
        ],
        "qkv_backward",
        None,
        rides,
        collective_id,
    )


def embed_back_kernel(pixel_ref, grad_ref, pos_ref, out_ref, table_ref, bias_ref, low_ref):
    @at_first
    def _():
        grad = grad_ref[...]
        low = grad.astype(jnp.bfloat16)
        low_ref[...] = low
        bias_ref[...] = column_sum(low)
        table_ref[...] = jnp.dot(
            pos_ref[...], grad, precision=HIGHEST, preferred_element_type=jnp.float32
        )

    out_ref[...] = mul(pixel_ref[...].T, low_ref[...]).astype(jnp.bfloat16)


def embed_backward(pixels, grad, pos_weights_t):
    rows, depth = pixels.shape
    block = 768
    nodes = pos_weights_t.shape[0]
    return block_call(
        embed_back_kernel,
        depth // block,
        [pl.BlockSpec((rows, block), lambda i: (0, i)), fixed(rows, D), fixed(nodes, rows)],
        [pixels, grad, pos_weights_t],
        [rows_of(block, D), fixed(nodes, D), fixed(1, D)],
        [shape_of(depth, D, dtype=jnp.bfloat16), shape_of(nodes, D), shape_of(1, D)],
        [pltpu.VMEM((rows, D), jnp.bfloat16)],
        "embed_backward",
        None,
    )


def head_kernel(
    stream_ref, seg_col_ref, seg_row_ref, label_ref, weight_ref, vector_ref,
    grad_ref, weight_grad_ref, sums_ref, bias_grad_ref, numbers_ref, *, classes,
):
    padded = weight_ref.shape[1]
    vector = vector_ref[...].astype(LOW).astype(jnp.float32)
    gain, shift = vector[:, D : 2 * D], vector[:, 2 * D : 3 * D]
    slots = lax.broadcasted_iota(jnp.int32, (IMGS, 1), 0)
    member = (seg_row_ref[...] == slots).astype(jnp.float32)
    counts = jnp.sum(member, 1, keepdims=True)
    sizes = jnp.maximum(counts, 1.0)
    unit, inverse = normalized(stream_ref[...])
    final = unit * gain + shift
    owner = jnp.broadcast_to(seg_col_ref[...], final.shape)
    pooled = [jnp.sum(jnp.where(owner == k, final, 0.0), 0, keepdims=True) for k in range(IMGS)]
    pooled = (jnp.concatenate(pooled, 0) / sizes).astype(LOW)
    class_at = lax.broadcasted_iota(jnp.int32, (IMGS, padded), 1)
    logits = mul(pooled, weight_ref[...]) + vector[:, 3 * D :]
    logits = jnp.where(class_at < classes, logits, MASKED)
    highest = jnp.max(logits, -1, keepdims=True)
    exponent = jnp.exp(logits - highest)
    totals = jnp.sum(exponent, -1, keepdims=True)
    onehot = class_at == label_ref[...]
    picked = jnp.sum(jnp.where(onehot, logits, 0.0), 1, keepdims=True)
    loss = jnp.sum(counts * (highest + jnp.log(totals) - picked), 0, keepdims=True)
    numbers_ref[...] = jnp.concatenate([loss, jnp.sum(counts, 0, keepdims=True)], 1)
    logits_grad = ((exponent / totals - onehot.astype(jnp.float32)) * counts).astype(LOW)
    bias_grad_ref[...] = column_sum(logits_grad)
    weight_grad_ref[...] = lax.dot_general(
        pooled, logits_grad, (((0,), (0,)), ((), ())), preferred_element_type=jnp.float32
    ).astype(LOW)
    pooled_grad = mul_nt(logits_grad, weight_ref[...]) / sizes
    own = (seg_col_ref[...] == lax.broadcasted_iota(jnp.int32, (1, IMGS), 1)).astype(LOW)
    final_grad, left = 0.0, pooled_grad
    for _ in range(3):
        term = left.astype(LOW)
        final_grad = final_grad + mul(own, term)
        left = left - term.astype(jnp.float32)
    inner = final_grad * gain
    mean_inner = jnp.mean(inner, -1, keepdims=True)
    mean_cross = jnp.mean(inner * unit, -1, keepdims=True)
    grad_ref[...] = inverse * (inner - mean_inner - unit * mean_cross)
    sums_ref[...] = jnp.concatenate([column_sum(final_grad * unit), column_sum(final_grad)], 1)


def head(stream, segment, labels, weight, global_vector, classes):
    rows = stream.shape[0]
    padded = weight.shape[1]
    vector = jnp.pad(global_vector, (0, padded - classes))[None, :]
    return pl.pallas_call(
        functools.partial(head_kernel, classes=classes),
        out_shape=[
            shape_of(rows, D),
            shape_of(D, padded, dtype=LOW),
            shape_of(1, 2 * D),
            shape_of(1, padded),
            shape_of(1, 2),
        ],
        compiler_params=pltpu.CompilerParams(vmem_limit_bytes=VMEM_LIMIT),
        cost_estimate=NO_COST,
        name="head",
    )(stream, segment[:, None], segment[None, :], labels.reshape(IMGS, 1), weight, vector)


def adam_update(gradient, moment, square, weight, factor, learn_rate):
    clipped = gradient * factor
    moment = BETA_ONE * moment + (1.0 - BETA_ONE) * clipped
    square = BETA_TWO * square + (1.0 - BETA_TWO) * clipped * clipped
    fixed_one = 1.0 - BETA_ONE**STEP
    fixed_two = 1.0 - BETA_TWO**STEP
    step_dir = (
        moment / fixed_one / (jnp.sqrt(square / fixed_two) + ADAM_EPS) + WEIGHT_DECAY * weight
    )
    return (moment, square, weight - learn_rate * step_dir)


def body(
    pixels,
    segment,
    patch_size,
    labels,
    patch_kernel,
    head_weight,
    input_proj,
    output_proj,
    layer_vector,
    position_table,
    global_vector,
    patch_moment,
    head_moment,
    input_moment,
    output_moment,
    layer_moment,
    position_moment,
    global_moment,
    patch_square,
    head_square,
    input_square,
    output_square,
    layer_square,
    position_square,
    global_square,
):
    owners = lax.axis_size("fsdp")
    nodes = position_table.shape[0]
    vector_size = layer_vector.size
    stream, pos_weights_t, vectors, qkv_weight, up_zero, rides, rest_shards, first_rows = begin(
        pixels,
        segment,
        patch_size,
        patch_kernel,
        layer_vector,
        input_proj,
        output_proj,
        head_weight,
        position_table,
        global_vector,
    )
    qkv_one, up_one, head_full = (
        lax.all_gather(shard, "fsdp", axis=0, tiled=True) for shard in rest_shards
    )
    saved_layers = []
    for index in range(LAYERS):
        vector = vectors[index]
        if index:
            normed, qkv_rows = qkv_forward(stream, qkv_weight, vector)
        else:
            normed, qkv_rows = first_rows
        if index == 0:
            attended, expo, inverse, output, output_ride = attention_forward(
                qkv_rows, segment, rides, 4
            )
            up = up_zero
        else:
            attended, expo, inverse, output = attention_forward(qkv_rows, segment, [output_ride], 5)
            up = up_one
        residual, normed_second, active, slope, following = mlp_forward(
            stream, attended, up, output, vector
        )
        saved_layers.append(
            (
                (qkv_weight, up, output, vector),
                (stream, normed, qkv_rows, attended, expo, inverse),
                (residual, normed_second, active, slope),
            )
        )
        stream, qkv_weight = following, qkv_one
    stream_grad, head_grad, final_sums, head_bias_grad, numbers = head(
        stream, segment, labels, head_full, global_vector, head_weight.shape[1]
    )
    vector_grads = [None] * LAYERS
    for index in reversed(range(LAYERS)):
        (qkv_weight, up, output, vector), first, second = saved_layers[index]
        entering, normed, qkv_rows, attended, expo, inverse = first
        residual, normed_second, active, slope = second
        residual_grad, attended_grad, mlp_sums, up_grad, output_grad, *brought = mlp_backward(
            stream_grad,
            slope,
            residual,
            normed_second,
            active,
            attended,
            up,
            output,
            vector,
            () if index else [output_rest, SumRide(by_owner(head_grad), False)],
            9,
        )
        if index == 0:
            output_one_sum, head_sum = brought
            attended_grad, output_grad = lax.optimization_barrier((attended_grad, output_grad))
            last_part = scatter(by_owner(output_grad))
        qkv_grad, rest = attention_backward(
            qkv_rows,
            expo,
            inverse,
            attended,
            attended_grad,
            [LeadRide(by_owner(output_grad if index else up_grad))],
            6 if index else 8,
        )
        stream_grad, qkv_sums, qkv_weight_grad, *brought = qkv_backward(
            qkv_grad,
            residual_grad,
            entering,
            normed,
            qkv_weight,
            vector,
            () if index else [rest],
            7,
        )
        if index:
            output_rest = rest
            stream_grad, qkv_weight_grad, up_grad = lax.optimization_barrier(
                (stream_grad, qkv_weight_grad, up_grad)
            )
            late_parts = [scatter(by_owner(grad)) for grad in (qkv_weight_grad, up_grad)]
        else:
            (up_zero_sum,) = brought
        vector_grads[index] = jnp.concatenate(
            [
                qkv_sums[0, : 2 * D],
                mlp_sums[0, : 2 * D],
                qkv_sums[0, 2 * D :],
                mlp_sums[0, 2 * D :],
            ]
        )
    kernel_grad, position_grad, bias_grad = embed_backward(pixels, stream_grad, pos_weights_t)
    position_grad = position_grad[:nodes]
    vector_part = jnp.stack(vector_grads).reshape(LAYERS, owners, -1)
    vector_part = jnp.swapaxes(vector_part, 0, 1).reshape(owners, vector_size)
    vector_rows = -(-vector_size // LANES)
    vector_part = jnp.pad(vector_part, ((0, 0), (0, vector_rows * LANES - vector_size)))
    rest = jnp.concatenate(
        [
            position_grad.reshape(-1),
            bias_grad[0],
            final_sums[0],
            head_bias_grad[0, :CLS],
            numbers[0],
        ]
    )
    rest_rows = -(-rest.shape[0] // (owners * LANES))
    rest_part = jnp.pad(rest, (0, rest_rows * owners * LANES - rest.shape[0]))
    small = jnp.concatenate([vector_part, rest_part.reshape(owners, -1)], 1)
    used = vector_rows + rest_rows
    block_rows = (used // 64 + 1) * 64
    small = jnp.pad(small.reshape(owners, used, LANES), ((0, 0), (0, block_rows - used), (0, 0)))
    qkv_zero_sum, kernel_sum, small_share, *input_one_sums = reduce_all(
        [by_owner(qkv_weight_grad), by_owner(kernel_grad)], small, late_parts, 2
    )
    output_zero_sum, small_full, numbers = finish_all(
        [head_sum, output_one_sum, up_zero_sum, qkv_zero_sum, kernel_sum, *input_one_sums],
        small_share,
        [last_part],
        vector_rows,
        rest.shape[0],
        3,
    )
    factor, grad_norm, loss_sum, token_total = (numbers[0, index] for index in range(4))
    rest_sum = small_full[:, vector_rows:used].reshape(-1)
    position_sum = rest_sum[: position_grad.size].reshape(position_grad.shape)
    global_sum = rest_sum[position_grad.size :][: global_vector.shape[0]]
    kernel_sum = kernel_sum.astype(jnp.float32)
    head_sum = head_sum[:, :CLS].astype(jnp.float32)
    input_sum = jnp.stack(
        [jnp.concatenate(pair, 1) for pair in ((qkv_zero_sum, up_zero_sum), input_one_sums)]
    ).astype(jnp.float32)
    output_sum = jnp.stack([output_zero_sum, output_one_sum]).astype(
        jnp.float32
    )
    vector_sum = small_share[:vector_rows].reshape(-1)[:vector_size].reshape(layer_vector.shape)
    patch_next = adam_update(
        kernel_sum, patch_moment, patch_square, patch_kernel, factor, LEARN_RATE
    )
    head_next = adam_update(head_sum, head_moment, head_square, head_weight, factor, LEARN_RATE)
    input_next = adam_update(input_sum, input_moment, input_square, input_proj, factor, LEARN_RATE)
    output_next = adam_update(
        output_sum, output_moment, output_square, output_proj, factor, LEARN_RATE
    )
    layer_next = adam_update(
        vector_sum, layer_moment, layer_square, layer_vector, factor, VECTOR_RATE
    )
    position_next = adam_update(
        position_sum, position_moment, position_square, position_table, factor, LEARN_RATE
    )
    global_next = adam_update(
        global_sum, global_moment, global_square, global_vector, factor, VECTOR_RATE
    )
    return (
        loss_sum,
        token_total,
        grad_norm,
        patch_next[0],
        head_next[0],
        input_next[0],
        output_next[0],
        layer_next[0],
        position_next[0],
        global_next[0],
        patch_next[1],
        head_next[1],
        input_next[1],
        output_next[1],
        layer_next[1],
        position_next[1],
        global_next[1],
        patch_next[2],
        head_next[2],
        input_next[2],
        output_next[2],
        layer_next[2],
        position_next[2],
        global_next[2],
    )


def solution(mesh):
    in_specs = (
        P(("dp", "fsdp"), None),
        P(("dp", "fsdp")),
        P(("dp", "fsdp"), None),
        P(("dp", "fsdp"), None),
        P("fsdp", None),
        P("fsdp", None),
        P(None, "fsdp", None),
        P(None, "fsdp", None),
        P(None, "fsdp"),
        P(),
        P(),
        P("fsdp", None),
        P("fsdp", None),
        P(None, "fsdp", None),
        P(None, "fsdp", None),
        P(None, "fsdp"),
        P(),
        P(),
        P("fsdp", None),
        P("fsdp", None),
        P(None, "fsdp", None),
        P(None, "fsdp", None),
        P(None, "fsdp"),
        P(),
        P(),
    )
    out_specs = (
        P(),
        P(),
        P(),
        P("fsdp", None),
        P("fsdp", None),
        P(None, "fsdp", None),
        P(None, "fsdp", None),
        P(None, "fsdp"),
        P(),
        P(),
        P("fsdp", None),
        P("fsdp", None),
        P(None, "fsdp", None),
        P(None, "fsdp", None),
        P(None, "fsdp"),
        P(),
        P(),
        P("fsdp", None),
        P("fsdp", None),
        P(None, "fsdp", None),
        P(None, "fsdp", None),
        P(None, "fsdp"),
        P(),
        P(),
    )
    return jax.shard_map(body, mesh=mesh, in_specs=in_specs, out_specs=out_specs, check_vma=False)
```

```python
import functools

import jax
import jax.numpy as jnp
from jax import lax
from jax.experimental import pallas as pl
from jax.experimental.pallas import tpu as pltpu
from jax.sharding import PartitionSpec as P

D = 768
HEADS = 12
HD = 64
CLS = 1000
GRID = 7
IMG = 240
IMGS = 8
LAYERS = 2
STEP = 3


NORM_EPS = 1e-06
CLIP_NORM = 0.01
LEARN_RATE = 0.05
VECTOR_RATE = 0.25
BETA_ONE = 0.5
BETA_TWO = 0.5
ADAM_EPS = 1e-08
WEIGHT_DECAY = 0.05
HIGHEST = lax.Precision.HIGHEST

PAIR = 2 * HD
MASKED = -1e30
MIB = 1024 * 1024
VMEM_LIMIT = 56 * MIB
MESH = pl.DeviceIdType.MESH
LANES = 128
LOW = jnp.bfloat16
ANYWHERE = pl.BlockSpec(memory_space=pl.ANY)
NO_COST = pl.CostEstimate(flops=0, bytes_accessed=0, transcendentals=0)
ROOT = 0.7978845608028654
CUBE = 0.044715
NT = (((1,), (1,)), ((), ()))


def layer_norm(values, gain, shift):
    center = values - jnp.mean(values, -1, keepdims=True)
    spread = jnp.mean(center * center, -1, keepdims=True)
    return center * lax.rsqrt(spread + NORM_EPS) * gain + shift


def rounded(values):
    return lax.optimization_barrier(values.astype(jnp.bfloat16)).astype(jnp.float32)


def matmul(left, right):
    return jnp.dot(left, right, preferred_element_type=jnp.float32)


def padded_rows(flat, multiple):
    extra = -flat.shape[0] % (multiple * LANES)
    return jnp.pad(flat, (0, extra)).reshape(-1, LANES)


def row_layout(seg_row, patch_row):
    row_count = seg_row.shape[0]
    slots = jnp.arange(IMGS, dtype=jnp.int32)
    member = seg_row[:, None] == slots[None, :]
    counts = jnp.sum(member.astype(jnp.int32), 0, dtype=jnp.int32)
    starts = jnp.cumsum(counts, dtype=jnp.int32) - counts
    inside = jnp.any(member, 1)
    offset = jnp.arange(row_count, dtype=jnp.int32) - jnp.sum(
        jnp.where(member, starts[None, :], 0), 1, dtype=jnp.int32
    )
    offset = jnp.where(inside, offset, 0)
    patch_tok = jnp.sum(jnp.where(member, patch_row[None, :], 0), 1, dtype=jnp.int32) + jnp.where(
        inside, 0, IMG
    )
    side = IMG // patch_tok
    nodes = jnp.arange(GRID, dtype=jnp.int32).astype(jnp.float32)

    def hat(coord):
        place = ((2 * coord + 1) * GRID).astype(jnp.float32) / (2 * side).astype(jnp.float32) - 0.5
        place = jnp.clip(place, 0.0, GRID - 1.0)
        return jnp.maximum(1.0 - jnp.abs(place[:, None] - nodes[None, :]), 0.0)

    weights = (hat(offset // side)[:, :, None] * hat(offset % side)[:, None, :]).reshape(
        row_count, GRID * GRID
    )
    return (weights, member.astype(jnp.float32), counts.astype(jnp.float32))


TURNS = (1, 2, 3)


def place():
    slot = lax.axis_index("fsdp")
    return lax.axis_index("dp"), lax.div(slot, 2), lax.rem(slot, 2)


def partner(index, turn):
    if turn == 0:
        return index
    if turn == 1:
        return index + 1 - 2 * lax.rem(index, 2)
    if turn == 2:
        return lax.rem(index + 2, 4)
    return 3 - index


def greet():
    group, level, core = place()
    barrier = pltpu.get_barrier_semaphore()
    peers = [(group, 2 * level + 1 - core)]
    for turn in TURNS:
        peers.append((group, 2 * partner(level, turn) + core))
        peers.append((partner(group, turn), 2 * level + core))
    for peer in peers:
        pl.semaphore_signal(barrier, inc=1, device_id=peer, device_id_type=MESH)
    pl.semaphore_wait(barrier, len(peers))


def quarter_shape(rows, columns):
    if columns % (2 * LANES) == 0:
        return rows // 2, columns // 2
    return rows // 4, columns


def quarter(index, rows, columns):
    high, wide = quarter_shape(rows, columns)
    if wide == columns:
        return pl.ds(pl.multiple_of(index * high, high), high), pl.ds(0, columns)
    return (
        pl.ds(pl.multiple_of(lax.div(index, 2) * high, high), high),
        pl.ds(pl.multiple_of(lax.rem(index, 2) * wide, wide), wide),
    )


def remote(source, target, send, receive, device):
    return pltpu.make_async_remote_copy(
        src_ref=source,
        dst_ref=target,
        send_sem=send,
        recv_sem=receive,
        device_id=device,
        device_id_type=MESH,
    )


GATHER_SEMS = 39


def relay_rows(part, rows):
    cut = -(-rows // 32) * 16
    return (0, cut) if part == 0 else (cut, rows - cut)


class Relay:
    def region(self, turn, index):
        _, level, core = place()
        block = self.out.at[2 * partner(level, turn) + core]
        return block.at[quarter(index, *self.shard.shape)]

    def group_copy(self, turn, other):
        group, level, core = place()
        index = self.group_at + 2 * (turn - 1) + other - 1
        peer = (partner(group, other), 2 * level + core)
        target = self.region(turn, group)
        source = self.quarter_source(turn, target)
        return remote(source, target, self.sems.at[index], self.sems.at[index + 6], peer)

    def relay_copy(self, turn, part):
        group, level, core = place()
        first, count = relay_rows(part, quarter_shape(*self.shard.shape)[0])
        block = self.region(turn, partner(group, 1 + part)).at[pl.ds(first, count)]
        index = self.relay_at + 2 * (turn - 1) + part
        peer = (partner(group, 2 - part), 2 * level + core)
        return remote(block, block, self.sems.at[index], self.sems.at[index + 6], peer)

    def relay(self):
        for turn in TURNS:
            for part in range(2):
                self.group_copy(turn, 1 + part).wait_recv()
                self.relay_copy(turn, part).start()

    def wait_quarters(self, turn):
        for part in range(2):
            self.relay_copy(turn, part).wait_recv()

    def wait_passed(self):
        for turn in TURNS:
            for part in range(2):
                self.group_copy(turn, 1 + part).wait_send()
                self.relay_copy(turn, part).wait_send()


class Gather(Relay):
    group_at, relay_at = 7, 19

    def __init__(self, shard, out, sems, split, in_place=False):
        self.shard, self.out, self.sems, self.split = shard, out, sems, split
        self.in_place = in_place
        self.rows, self.columns = shard.shape

    def quarter_source(self, turn, target):
        return target

    def level_copy(self, turn):
        group, level, core = place()
        block = self.out.at[2 * level + core]
        source = self.shard
        if self.split:
            part = quarter(group, self.rows, self.columns)
            source, block = source.at[part], block.at[part]
        peer = (group, 2 * partner(level, turn) + core)
        return remote(source, block, self.sems.at[turn], self.sems.at[3 + turn], peer)

    def core_copy(self, turn):
        group, level, core = place()
        slot = 2 * partner(level, turn) + core
        source = self.shard if turn == 0 else self.out.at[slot]
        peer = (group, 2 * level + 1 - core)
        return remote(source, self.out.at[slot], self.sems.at[31 + turn], self.sems.at[35 + turn], peer)

    def own_copy(self):
        _, level, core = place()
        return pltpu.make_async_copy(self.shard, self.out.at[2 * level + core], self.sems.at[0])

    def first(self):
        for turn in TURNS:
            self.level_copy(turn).start()
        self.core_copy(0).start()
        if not self.in_place:
            self.own_copy().start()

    def second(self):
        for turn in TURNS:
            self.level_copy(turn).wait_recv()
            if self.split:
                for other in (1, 2):
                    self.group_copy(turn, other).start()
            else:
                self.core_copy(turn).start()

    def third(self, use=None):
        for turn in TURNS if self.split else ():
            self.wait_quarters(turn)
            self.core_copy(turn).start()
            if use is not None:
                use(turn, True)

    def fourth(self, use=None):
        for turn in TURNS if use is not None else (0, *TURNS):
            self.core_copy(turn).wait_recv()
            if use is not None:
                use(turn, False)
        for turn in TURNS:
            self.level_copy(turn).wait_send()
        if self.split:
            self.wait_passed()
        for turn in (0, *TURNS):
            self.core_copy(turn).wait_send()
        if not self.in_place:
            self.own_copy().wait()


class LevelGather:
    def __init__(self, shard, out, sems):
        self.shard, self.out, self.sems = shard, out, sems

    def level_copy(self, turn):
        group, level, core = place()
        return remote(
            self.shard.at[quarter(group, *self.shard.shape)],
            self.out.at[level],
            self.sems.at[turn],
            self.sems.at[3 + turn],
            (group, 2 * partner(level, turn) + core),
        )

    def first(self):
        for turn in TURNS:
            self.level_copy(turn).start()

    def second(self):
        pass

    def third(self):
        pass

    def fourth(self):
        for turn in TURNS:
            self.level_copy(turn).wait_recv()
            self.level_copy(turn).wait_send()

    def store(self):
        _, level, _ = place()
        self.out[level] = jnp.zeros(self.out.shape[1:], self.out.dtype)
        self.target[...] = self.out[...]


GROUP_GATHER_SEMS = 36


class GroupGather(Relay):
    group_at, relay_at = 4, 16

    def __init__(self, shard, quarters, out, sems):
        self.shard, self.quarters, self.out, self.sems = shard, quarters, out, sems

    def quarter_source(self, turn, target):
        _, level, _ = place()
        return self.quarters.at[partner(level, turn)]

    def own_copy(self, turn):
        group, level, core = place()
        if turn == 0:
            source, target = self.shard, self.out.at[2 * level + core]
        else:
            source, target = self.quarters.at[partner(level, turn)], self.region(turn, group)
        return pltpu.make_async_copy(source, target, self.sems.at[turn])

    def core_copy(self, turn):
        group, level, core = place()
        slot = 2 * partner(level, turn) + core
        source = self.shard if turn == 0 else self.out.at[slot]
        peer = (group, 2 * level + 1 - core)
        return remote(source, self.out.at[slot], self.sems.at[28 + turn], self.sems.at[32 + turn], peer)

    def first(self):
        for turn in TURNS:
            for other in (1, 2):
                self.group_copy(turn, other).start()
        for turn in (0, *TURNS):
            self.own_copy(turn).start()
        self.core_copy(0).start()

    def third(self):
        for turn in TURNS:
            self.wait_quarters(turn)
            self.own_copy(turn).wait()
            self.core_copy(turn).start()

    def fourth(self):
        for turn in (0, *TURNS):
            self.core_copy(turn).wait_recv()
            self.core_copy(turn).wait_send()
        self.wait_passed()
        self.own_copy(0).wait()

    def store(self):
        copy = pltpu.make_async_copy(self.out, self.target, self.sems.at[0])
        copy.start()
        copy.wait()


class LevelRide:
    def __init__(self, shard):
        self.operands = [shard]
        self.in_specs = [fixed(*shard.shape)]
        shape = (4, *quarter_shape(*shard.shape))
        self.out_specs = [fixed(*shape)]
        self.out_shapes = [jax.ShapeDtypeStruct(shape, shard.dtype)]
        self.scratch = [pltpu.VMEM(shape, shard.dtype), pltpu.SemaphoreType.DMA((7,))]

    def job(self, sources, targets, scratch):
        job = LevelGather(sources[0], *scratch)
        job.target = targets[0]
        return job

    def before(self, steps):
        return {0: ("first",)}

    after = ("fourth", "store")

    def result(self, outs):
        return GatherRide(self.operands[0], outs[0])

    def plain(self):
        return GatherRide(self.operands[0], self.operands[0])


class GatherRide:
    def __init__(self, shard, quarters):
        owners = lax.axis_size("fsdp")
        full = (owners, *shard.shape)
        self.operands = [shard, quarters]
        self.in_specs = [fixed(*shard.shape), fixed(*quarters.shape)]
        self.out_specs = [ANYWHERE]
        self.out_shapes = [jax.ShapeDtypeStruct(full, shard.dtype)]
        self.scratch = [
            pltpu.VMEM(full, shard.dtype),
            pltpu.SemaphoreType.DMA((GROUP_GATHER_SEMS,)),
        ]

    def job(self, sources, targets, scratch):
        job = GroupGather(*sources, *scratch)
        job.target = targets[0]
        return job

    def before(self, steps):
        return {0: ("first",), steps // 2: ("relay",), steps - 1: ("third",)}

    after = ("fourth", "store")

    def result(self, outs):
        return outs[0].reshape(-1, outs[0].shape[2])

    def plain(self):
        return lax.all_gather(self.operands[0], "fsdp", axis=0, tiled=True)


class ShareRide:
    def __init__(self, share):
        self.operands = [share]
        self.in_specs = [ANYWHERE]
        self.out_specs = [fixed(*share.shape)]
        self.out_shapes = [jax.ShapeDtypeStruct(share.shape, share.dtype)]
        self.scratch = [
            pltpu.VMEM(share.shape, share.dtype),
            *share_scratch(share),
            pltpu.SemaphoreType.DMA((GROUP_SEMS,)),
        ]

    def job(self, sources, targets, scratch):
        job = GroupReduce(sources[0], scratch[0], scratch[1:3], scratch[3])
        job.target = targets[0]
        return job

    def before(self, steps):
        return {0: ("first", "second"), max(1, steps // 2): ("third",)}

    after = ("fifth", "sixth", "store")

    def result(self, outs):
        return outs[0]

    def plain(self):
        return lax.psum(self.operands[0], "dp")


class SumRide:
    def __init__(self, grad, large):
        block = grad.shape[1:]
        self.large = large
        self.operands = [grad]
        self.in_specs = [ANYWHERE]
        self.out_specs = [fixed(*block)]
        self.out_shapes = [jax.ShapeDtypeStruct(block, grad.dtype)]
        buffers = stepped_scratch(grad) if large else whole_scratch(grad)
        sems = WHOLE_SEMS if large else REDUCE_SEMS
        self.scratch = [pltpu.VMEM(block, grad.dtype), *buffers, pltpu.SemaphoreType.DMA((sems,))]

    def job(self, sources, targets, scratch):
        job = (Whole if self.large else Reduce)(sources[0], scratch[0], scratch[1:-1], scratch[-1])
        job.target = targets[0]
        return job

    def before(self, steps):
        if self.large:
            return {0: ("first",), 1: ("second",), steps - 2: ("between",), steps - 1: ("third",)}
        return {0: ("first",), 1: ("second",), steps // 2: ("third",), steps - 1: ("fourth",)}

    @property
    def after(self):
        return (("fourth",) if self.large else ()) + ("fifth", "sixth", "store")

    def result(self, outs):
        return outs[0]

    def plain(self):
        return lax.psum(scatter(self.operands[0]), "dp")


class LeadRide:
    after = ("third", "sixth", "store")

    def __init__(self, grad):
        _, rows, columns = grad.shape
        shape = (4, rows // 2, columns // 2)
        self.operands = [grad]
        self.in_specs = [ANYWHERE]
        self.out_specs = [fixed(*shape)]
        self.out_shapes = [jax.ShapeDtypeStruct(shape, grad.dtype)]
        self.scratch = [*stepped_scratch(grad), pltpu.SemaphoreType.DMA((WHOLE_SEMS,))]

    def job(self, sources, targets, scratch):
        job = Lead(sources[0], None, scratch[:-1], scratch[-1])
        job.target = targets[0]
        return job

    def before(self, steps):
        return {0: ("first",), 1: ("second",), steps - 2: ("between",)}

    def result(self, outs):
        return RestRide(outs[0])

    def plain(self):
        return RestRide(self.operands[0])


class RestRide:
    after = ("fifth", "sixth", "store")

    def __init__(self, part):
        _, high, wide = part.shape
        block = (2 * high, 2 * wide)
        self.operands = [part]
        self.in_specs = [fixed(*part.shape)]
        self.out_specs = [fixed(*block)]
        self.out_shapes = [jax.ShapeDtypeStruct(block, part.dtype)]
        self.scratch = [
            pltpu.VMEM(block, part.dtype),
            pltpu.VMEM((3, high, wide), part.dtype),
            pltpu.SemaphoreType.DMA((WHOLE_SEMS,)),
        ]

    def job(self, sources, targets, scratch):
        job = Rest(sources[0], *scratch)
        job.target = targets[0]
        return job

    def before(self, steps):
        return {0: ("first",), steps - 1: ("fourth",)}

    def result(self, outs):
        return outs[0]

    def plain(self):
        return lax.psum(scatter(self.operands[0]), "dp")


def riding(body, counts, rides, steps):
    def kernel(*refs):
        refs = list(refs)

        def pop(count):
            taken = refs[:count]
            del refs[:count]
            return taken

        own = pop(counts[0])
        sources = [pop(len(ride.operands)) for ride in rides]
        own += pop(counts[1])
        targets = [pop(len(ride.out_shapes)) for ride in rides]
        own += pop(counts[2])
        jobs = [
            ride.job(source, target, pop(len(ride.scratch)))
            for ride, source, target in zip(rides, sources, targets)
        ]
        for step in range(steps):
            planned = [
                (job, stages)
                for ride, job in zip(rides, jobs)
                for at, stages in ride.before(steps).items()
                if at == step
            ]
            if planned:

                @pl.when(pl.program_id(0) == step)
                def _(planned=planned, step=step):
                    if step == 0:
                        greet()
                    for job, stages in planned:
                        run_stages([job], stages)

        body(*own)

        @pl.when(pl.program_id(0) == steps - 1)
        def _():
            for ride, job in zip(rides, jobs):
                run_stages([job], ride.after)

    return kernel


def block_call(
    body, grid, in_specs, operands, out_specs, out_shape, scratch, name,
    cost=None, rides=(), collective_id=None,
):
    plain = []
    if rides and not with_kernels():
        plain, rides = [ride.plain() for ride in rides], ()
    transfer = {}
    kernel = body
    if rides:
        transfer = {"collective_id": collective_id, "has_side_effects": True}
        kernel = riding(body, (len(operands), len(out_shape), len(scratch)), rides, grid)
    count = len(out_shape)
    for ride in rides:
        operands = [*operands, *ride.operands]
        in_specs = [*in_specs, *ride.in_specs]
        out_specs, out_shape = [*out_specs, *ride.out_specs], [*out_shape, *ride.out_shapes]
        scratch = [*scratch, *ride.scratch]
    outs = pl.pallas_call(
        kernel,
        grid=(grid,),
        in_specs=in_specs,
        out_specs=out_specs,
        out_shape=out_shape,
        scratch_shapes=scratch,
        compiler_params=pltpu.CompilerParams(vmem_limit_bytes=VMEM_LIMIT, **transfer),
        cost_estimate=cost or NO_COST,
        name=name,
    )(*operands)
    brought, outs = list(outs[count:]), list(outs[:count])
    for ride in rides:
        plain.append(ride.result(brought[: len(ride.out_shapes)]))
        brought = brought[len(ride.out_shapes) :]
    return outs + plain


def work(flops, size):
    return pl.CostEstimate(flops=flops, bytes_accessed=size, transcendentals=0)


def position_weights(seg_col, patch_row, nodes):
    rows = seg_col.shape[0]
    slot = lax.broadcasted_iota(jnp.int32, (rows, IMGS), 1)
    member = seg_col == slot
    counts = jnp.sum(member.astype(jnp.float32), 0, keepdims=True)
    start = jnp.sum(jnp.where(slot < seg_col, counts, 0.0), 1, keepdims=True)
    token = lax.broadcasted_iota(jnp.int32, (rows, 1), 0).astype(jnp.float32)
    inside = seg_col < IMGS
    offset = jnp.where(inside, token - start, 0.0)
    patch = jnp.sum(jnp.where(member, patch_row.astype(jnp.float32), 0.0), 1, keepdims=True)
    side = jnp.where(inside, jnp.floor(IMG / jnp.where(inside, patch, 1.0) + 0.5), 1.0)
    line = jnp.floor((offset + 0.5) / side)
    column = offset - line * side

    def spot(coord):
        return jnp.clip((2.0 * coord + 1.0) * GRID / (2.0 * side) - 0.5, 0.0, GRID - 1.0)

    node = lax.broadcasted_iota(jnp.int32, (rows, LANES), 1).astype(jnp.float32)
    across = jnp.floor((node + 0.5) / GRID)
    along = node - across * GRID
    weights = jnp.maximum(1.0 - jnp.abs(spot(line) - across), 0.0)
    weights = weights * jnp.maximum(1.0 - jnp.abs(spot(column) - along), 0.0)
    return jnp.where(node < nodes, weights, 0.0)


def first_kernel(*refs, spots):
    kernel, vectors, inputs, outputs, head, pixels, seg_col, patch_row, table, biases = refs[:10]
    stream, pos_t, vector_zero, vector_one = refs[10:14]
    qkv_full, up_full, output_level = refs[14:17]
    output_zero, qkv_one, up_one, output_one, head_low, normed, qkv_rows = refs[17:24]
    wide_kernel, wide_inputs, wide_outputs, wide_head, pixel_rows, table_low = refs[24:30]
    kernel_full, qkv_zero, vectors_full, qkv_landing, up_landing, output_landing = refs[30:36]
    up_zero, load_sems, sems = refs[36:]
    _, level, core = place()
    mine = 2 * level + core
    pairs = [
        (kernel, wide_kernel),
        (inputs.at[0], wide_inputs.at[0]),
        (pixels, pixel_rows),
        (inputs.at[1], wide_inputs.at[1]),
        (outputs.at[0], wide_outputs.at[0]),
        (outputs.at[1], wide_outputs.at[1]),
        (head, wide_head),
    ]
    copies = [
        pltpu.make_async_copy(source, target, load_sems.at[index])
        for index, (source, target) in enumerate(pairs)
    ]
    for copy in copies:
        copy.start()
    patch_job = Gather(kernel_full.at[mine], kernel_full, sems.at[0], True, in_place=True)
    vector_job = Gather(vectors, vectors_full, sems.at[1], False)
    qkv_job = Gather(qkv_zero, qkv_landing, sems.at[2], True)
    up_job = Gather(up_zero, up_landing, sems.at[3], True)
    output_job = LevelGather(output_zero, output_landing, sems.at[4])
    output_job.target = output_level
    copies[0].wait()
    kernel_full[mine] = wide_kernel[...].astype(LOW)
    greet()
    patch_job.first()
    vector_job.first()
    copies[1].wait()
    qkv_zero[...] = wide_inputs[0, :, : 3 * D].astype(LOW)
    qkv_job.first()
    up_zero[...] = wide_inputs[0, :, 3 * D :].astype(LOW)
    up_job.first()
    copies[4].wait()
    output_zero[...] = wide_outputs[0].astype(LOW)
    output_job.first()

    weights = position_weights(seg_col[...], patch_row[...], table.shape[0])
    pos_t[...] = weights.T[: pos_t.shape[0], :]
    table_low[...] = jnp.zeros_like(table_low)
    table_low[: table.shape[0], :] = table[...].astype(LOW).astype(jnp.float32)
    bias = biases[:, :D].astype(LOW).astype(jnp.float32)
    stream[...] = bias + jnp.dot(
        weights, table_low[...], precision=HIGHEST, preferred_element_type=jnp.float32
    )
    copies[2].wait()
    depth = wide_kernel.shape[0]

    def add_block(slot):
        columns = pl.ds(pl.multiple_of(slot * depth, depth), depth)

        def add(step, carry):
            rows = pl.ds(pl.multiple_of(step * 256, 256), 256)
            stream[rows, :] += mul(pixel_rows[rows, columns], kernel_full[slot])
            return carry

        lax.fori_loop(0, stream.shape[0] // 256, add, 0)

    def use(turn, own_core):
        add_block(2 * partner(level, turn) + (core if own_core else 1 - core))

    add_block(mine)
    patch_job.second()
    qkv_job.second()
    vector_job.second()
    patch_job.core_copy(0).wait_recv()
    use(0, False)
    copies[3].wait()
    qkv_one[...] = wide_inputs[1, :, : 3 * D].astype(LOW)
    up_one[...] = wide_inputs[1, :, 3 * D :].astype(LOW)
    patch_job.relay()
    copies[5].wait()
    output_one[...] = wide_outputs[1].astype(LOW)
    copies[6].wait()
    head_low[...] = jnp.zeros_like(head_low)
    head_low[:, : head.shape[1]] = wide_head[...].astype(LOW)
    patch_job.third(use)
    qkv_job.relay()
    up_job.second()
    patch_job.fourth(use)
    qkv_job.third()
    vector_job.third()
    vector_job.fourth()
    blocks = [vectors_full[slot].astype(jnp.float32) for slot in range(vectors_full.shape[0])]
    span = vectors.shape[0] // LAYERS
    for layer, out in enumerate((vector_zero, vector_one)):
        for row in range(out.shape[1] // LANES):
            parts = [
                block[layer * span + row - spot : layer * span + row - spot + 1, :]
                for block, spot in zip(blocks, spots)
                if 0 <= row - spot < span
            ]
            out[:, row * LANES : (row + 1) * LANES] = sum(parts)
    up_job.relay()
    up_job.third()
    qkv_job.fourth()
    copy = pltpu.make_async_copy(qkv_landing, qkv_full, load_sems.at[0])
    copy.start()
    weight = qkv_landing[...].reshape(-1, qkv_landing.shape[2])
    for half in halves_of(stream.shape[0]):
        unit, _ = normalized(stream[half, :])
        low = (unit * vector_zero[:, :D] + vector_zero[:, D : 2 * D]).astype(LOW)
        normed[half, :] = low
        for base in range(0, 3 * D, D):
            bias = vector_zero[:, 4 * D + base : 5 * D + base]
            qkv_rows[half, base : base + D] = (mul(low, weight[:, base : base + D]) + bias).astype(LOW)
    up_job.fourth()
    up_copy = pltpu.make_async_copy(up_landing, up_full, load_sems.at[1])
    up_copy.start()
    run_stages([output_job], ("fourth", "store"))
    copy.wait()
    up_copy.wait()


def padded_vectors(shard):
    layers, width = shard.shape
    owners = lax.axis_size("fsdp")
    spots = [owner * width // LANES for owner in range(owners)]
    span = max(-(-(owner + 1) * width // LANES) - spot for owner, spot in enumerate(spots))
    span += -span % 16
    shift = lax.rem(lax.axis_index("fsdp") * width, LANES)
    padded = jnp.zeros((layers, span * LANES), LOW)
    padded = lax.dynamic_update_slice(padded, shard.astype(LOW), (0, shift))
    return padded.reshape(layers * span, LANES), spots


def begin(
    pixels, segment, patch_size, patch_kernel, layer_vector, input_proj, output_proj, head_weight,
    position_table, global_vector,
):
    classes = head_weight.shape[1] + -head_weight.shape[1] % LANES
    nodes = position_table.shape[0] + -position_table.shape[0] % 64
    if not with_kernels():
        inputs = [
            (input_proj[index, :, : 3 * D].astype(LOW), input_proj[index, :, 3 * D :].astype(LOW))
            for index in range(LAYERS)
        ]
        outputs = [output_proj[index].astype(LOW) for index in range(LAYERS)]
        gather = lambda shard, axis: lax.all_gather(shard, "fsdp", axis=axis, tiled=True)
        weights, _, _ = row_layout(segment, patch_size[0])
        weights = jnp.pad(weights, ((0, 0), (0, nodes - weights.shape[1])))
        table = jnp.pad(rounded(position_table), ((0, nodes - position_table.shape[0]), (0, 0)))
        bias = rounded(global_vector)[None, :D]
        stream = embed(pixels, gather(patch_kernel.astype(LOW), 0), weights, table, bias)
        vectors = gather(layer_vector.astype(LOW), 1).astype(jnp.float32)
        head = jnp.pad(head_weight.astype(LOW), ((0, 0), (0, classes - head_weight.shape[1])))
        return (
            stream,
            weights.T,
            [vectors[index : index + 1] for index in range(LAYERS)],
            gather(inputs[0][0], 0),
            gather(inputs[0][1], 0),
            [GatherRide(outputs[0], outputs[0]), LevelRide(outputs[1])],
            [*inputs[1], head],
            qkv_forward(stream, gather(inputs[0][0], 0), vectors[:1]),
        )
    rows = pixels.shape[0]
    owners = lax.axis_size("fsdp")
    vectors, spots = padded_vectors(layer_vector)
    depth = input_proj.shape[1]
    up_shape = (depth, input_proj.shape[2] - 3 * D)
    qkv_shape, out_shape = (depth, 3 * D), output_proj.shape[1:]
    low = lambda *shape: jax.ShapeDtypeStruct(shape, LOW)
    levels = lambda shape: low(4, *quarter_shape(*shape))
    width = layer_vector.shape[1] * owners
    shapes = [
        shape_of(rows, D),
        shape_of(nodes, rows),
        shape_of(1, width),
        shape_of(1, width),
        low(owners, *qkv_shape),
        low(owners, *up_shape),
        levels(out_shape),
        low(*out_shape),
        low(*qkv_shape),
        low(*up_shape),
        low(*out_shape),
        low(head_weight.shape[0], classes),
        low(rows, D),
        low(rows, 3 * D),
    ]
    wide = (patch_kernel, input_proj, output_proj, head_weight, pixels)
    in_vmem = pl.BlockSpec(memory_space=pltpu.VMEM)
    results = pl.pallas_call(
        functools.partial(first_kernel, spots=spots),
        in_specs=[ANYWHERE] * 6 + [in_vmem] * 4,
        out_specs=[in_vmem] * 4 + [ANYWHERE] * 2 + [in_vmem] * 8,
        out_shape=shapes,
        scratch_shapes=[
            *[pltpu.VMEM(array.shape, array.dtype) for array in wide],
            pltpu.VMEM((LANES, D), jnp.float32),
            pltpu.VMEM((owners, *patch_kernel.shape), LOW),
            pltpu.VMEM(qkv_shape, LOW),
            pltpu.VMEM((owners, *vectors.shape), LOW),
            pltpu.VMEM((owners, *qkv_shape), LOW),
            pltpu.VMEM((owners, *up_shape), LOW),
            pltpu.VMEM((4, *quarter_shape(*out_shape)), LOW),
            pltpu.VMEM(up_shape, LOW),
            pltpu.SemaphoreType.DMA((7,)),
            pltpu.SemaphoreType.DMA((5, GATHER_SEMS)),
        ],
        compiler_params=pltpu.CompilerParams(
            collective_id=1, has_side_effects=True, vmem_limit_bytes=VMEM_LIMIT
        ),
        cost_estimate=NO_COST,
        name="begin",
    )(
        patch_kernel,
        vectors,
        input_proj,
        output_proj,
        head_weight,
        pixels,
        segment[:, None],
        patch_size,
        position_table,
        global_vector[None, :],
    )
    output_zero, qkv_one, up_one, output_one, head_low, normed, qkv_rows = results[7:]
    return (
        results[0],
        results[1],
        results[2:4],
        results[4].reshape(owners * depth, 3 * D),
        results[5].reshape(owners * depth, up_shape[1]),
        [GatherRide(output_zero, results[6]), LevelRide(output_one)],
        [qkv_one, up_one, head_low],
        (normed, qkv_rows),
    )


REDUCE_SEMS = 52


class Reduce:
    def __init__(self, grad, out, scratch, sems):
        self.grad, self.out, self.sems = grad, out, sems
        self.own, self.away, self.got_core, self.got_group, self.part, self.got_level = scratch
        self.rows, self.columns = out.shape
        self.chunk = 16

    def load(self, level):
        _, _, core = place()
        return pltpu.make_async_copy(
            self.grad.at[2 * level + core], self.own.at[level], self.sems.at[level]
        )

    def load_away(self, level):
        _, _, core = place()
        return pltpu.make_async_copy(
            self.grad.at[2 * level + 1 - core], self.away.at[level], self.sems.at[48 + level]
        )

    def core_copy(self, target_level):
        group, level, core = place()
        return remote(
            self.away.at[target_level],
            self.got_core.at[target_level],
            self.sems.at[4 + target_level],
            self.sems.at[8 + target_level],
            (group, 2 * level + 1 - core),
        )

    def group_copy(self, turn, other):
        group, level, core = place()
        target = partner(level, turn)
        peer = partner(group, other)
        part = quarter(peer, self.rows, self.columns)
        index = 3 * turn + other - 1
        return remote(
            self.own.at[target].at[part],
            self.got_group.at[other - 1, target],
            self.sems.at[12 + index],
            self.sems.at[24 + index],
            (peer, 2 * level + core),
        )

    def level_copy(self, turn):
        group, level, core = place()
        target = partner(level, turn)
        return remote(
            self.part.at[target],
            self.got_level.at[turn - 1],
            self.sems.at[35 + turn],
            self.sems.at[38 + turn],
            (group, 2 * target + core),
        )

    def share_copy(self, other):
        group, level, core = place()
        mine = self.out.at[quarter(group, self.rows, self.columns)]
        return remote(
            mine,
            mine,
            self.sems.at[41 + other],
            self.sems.at[44 + other],
            (partner(group, other), 2 * level + core),
        )

    def first(self):
        _, level, _ = place()
        for turn in (*TURNS, 0):
            self.load_away(partner(level, turn)).start()
        for turn in (*TURNS, 0):
            self.load(partner(level, turn)).start()
        for turn in (*TURNS, 0):
            self.load_away(partner(level, turn)).wait()
            self.core_copy(partner(level, turn)).start()

    def second(self):
        _, level, _ = place()
        for turn in (*TURNS, 0):
            target = partner(level, turn)
            self.load(target).wait()
            self.core_copy(target).wait_recv()

            def add(step, carry):
                rows = pl.ds(pl.multiple_of(step * self.chunk, self.chunk), self.chunk)
                total = self.own[target, rows, :].astype(jnp.float32)
                total = total + self.got_core[target, rows, :].astype(jnp.float32)
                self.own[target, rows, :] = total.astype(self.own.dtype)
                return carry

            lax.fori_loop(0, self.rows // self.chunk, add, 0)
            for other in TURNS:
                self.group_copy(turn, other).start()

    def between(self):
        pass

    def third(self):
        group, level, _ = place()
        high, wide = quarter_shape(self.rows, self.columns)
        row_part, column_part = quarter(group, self.rows, self.columns)
        for turn in (*TURNS, 0):
            target = partner(level, turn)
            for other in TURNS:
                self.group_copy(turn, other).wait_recv()

            def add(step, carry):
                at = pl.multiple_of(step * self.chunk, self.chunk)
                rows = pl.ds(at, self.chunk)
                mine = pl.ds(pl.multiple_of(row_part.start + at, self.chunk), self.chunk)
                total = self.own[target, mine, column_part].astype(jnp.float32)
                for slot in range(3):
                    total = total + self.got_group[slot, target, rows, :].astype(jnp.float32)
                self.part[target, rows, :] = total.astype(self.part.dtype)
                return carry

            lax.fori_loop(0, high // self.chunk, add, 0)
            if turn:
                self.level_copy(turn).start()

    def fourth(self):
        group, level, _ = place()
        high, wide = quarter_shape(self.rows, self.columns)
        row_part, column_part = quarter(group, self.rows, self.columns)
        for turn in TURNS:
            self.level_copy(turn).wait_recv()

        def add(step, carry):
            at = pl.multiple_of(step * self.chunk, self.chunk)
            rows = pl.ds(at, self.chunk)
            mine = pl.ds(pl.multiple_of(row_part.start + at, self.chunk), self.chunk)
            total = self.part[level, rows, :].astype(jnp.float32)
            for slot in range(3):
                total = total + self.got_level[slot, rows, :].astype(jnp.float32)
            self.out[mine, column_part] = total.astype(self.out.dtype)
            return carry

        lax.fori_loop(0, high // self.chunk, add, 0)
        for other in TURNS:
            self.share_copy(other).start()

    def store(self):
        self.target[...] = self.out[...]

    def fifth(self):
        for other in TURNS:
            self.share_copy(other).wait_recv()

    def sixth(self):
        _, level, _ = place()
        for turn in (*TURNS, 0):
            self.core_copy(partner(level, turn)).wait_send()
            for other in TURNS:
                self.group_copy(turn, other).wait_send()
            if turn:
                self.level_copy(turn).wait_send()
                self.share_copy(turn).wait_send()


WHOLE_SEMS = 44


def add_rows(target, row, columns, source, count, wide):
    chunk = 16 if wide > 1536 else 48

    def add(step, carry):
        at = pl.multiple_of(step * chunk, chunk)
        mine = pl.ds(pl.multiple_of(row + at, 16), chunk)
        total = target[mine, columns].astype(jnp.float32)
        total = total + source[pl.ds(at, chunk), :].astype(jnp.float32)
        target[mine, columns] = total.astype(target.dtype)
        return carry

    lax.fori_loop(0, count // chunk, add, 0)


class Whole:
    FIRST_X = (1, 0)

    lead = False

    def __init__(self, grad, out, scratch, sems):
        self.grad, self.out, self.sems = grad, out, sems
        self.own, self.away, self.got_core, self.got_x, self.got_y, self.got_last, self.part, self.got_level = scratch
        self.rows, self.columns = grad.shape[1:]
        self.high, self.wide = self.rows // 2, self.columns // 2

    def row_half(self, index):
        return pl.ds(pl.multiple_of(lax.div(index, 2) * self.high, self.high), self.high)

    def column_half(self, index):
        return pl.ds(pl.multiple_of(lax.rem(index, 2) * self.wide, self.wide), self.wide)

    def load(self, level):
        _, _, core = place()
        return pltpu.make_async_copy(
            self.grad.at[2 * level + core], self.own.at[level], self.sems.at[level]
        )

    def load_away(self, level):
        _, _, core = place()
        return pltpu.make_async_copy(
            self.grad.at[2 * level + 1 - core], self.away.at[level], self.sems.at[40 + level]
        )

    def core_copy(self, target_level):
        group, level, core = place()
        return remote(
            self.away.at[target_level],
            self.got_core.at[target_level],
            self.sems.at[4 + target_level],
            self.sems.at[8 + target_level],
            (group, 2 * level + 1 - core),
        )

    def step_copy(self, turn):
        group, level, core = place()
        block = self.own.at[partner(level, turn)]
        if turn in self.FIRST_X:
            peer = partner(group, 1)
            source = block.at[:, self.column_half(peer)]
            target = self.got_x.at[self.FIRST_X.index(turn)]
        else:
            peer = partner(group, 2)
            source = block.at[self.row_half(peer), :]
            target = self.got_y.at[turn - 2]
        return remote(
            source, target, self.sems.at[12 + turn], self.sems.at[16 + turn], (peer, 2 * level + core)
        )

    def last_copy(self, turn):
        group, level, core = place()
        block = self.own.at[partner(level, turn)]
        peer = partner(group, 2 if turn in self.FIRST_X else 1)
        rows = self.row_half(peer)
        columns = self.column_half(peer)
        return remote(
            block.at[rows, columns],
            self.got_last.at[turn],
            self.sems.at[20 + turn],
            self.sems.at[24 + turn],
            (peer, 2 * level + core),
        )

    def level_copy(self, turn):
        group, level, core = place()
        target = partner(level, turn)
        return remote(
            self.part.at[target],
            self.got_level.at[turn - 1],
            self.sems.at[27 + turn],
            self.sems.at[30 + turn],
            (group, 2 * target + core),
        )

    def share_copy(self, other):
        group, level, core = place()
        mine = self.out.at[self.row_half(group), self.column_half(group)]
        return remote(
            mine,
            mine,
            self.sems.at[33 + other],
            self.sems.at[36 + other],
            (partner(group, other), 2 * level + core),
        )

    def first(self):
        _, level, _ = place()
        for turn in (*TURNS, 0):
            self.load_away(partner(level, turn)).start()
        for turn in (*TURNS, 0):
            self.load(partner(level, turn)).start()
        for turn in (*TURNS, 0):
            self.load_away(partner(level, turn)).wait()
            self.core_copy(partner(level, turn)).start()

    def second(self):
        _, level, _ = place()
        for turn in (*TURNS, 0):
            target = partner(level, turn)
            self.load(target).wait()
            self.core_copy(target).wait_recv()
            add_rows(
                self.own.at[target], 0, slice(None), self.got_core.at[target], self.rows, self.columns
            )
            self.step_copy(turn).start()

    def between(self):
        group, level, _ = place()
        for turn in (*TURNS, 0):
            block = self.own.at[partner(level, turn)]
            self.step_copy(turn).wait_recv()
            if turn in self.FIRST_X:
                source = self.got_x.at[self.FIRST_X.index(turn)]
                add_rows(block, 0, self.column_half(group), source, self.rows, self.wide)
            else:
                source = self.got_y.at[turn - 2]
                start = lax.div(group, 2) * self.high
                add_rows(block, start, slice(None), source, self.high, self.columns)
            self.last_copy(turn).start()

    def third(self):
        group, level, _ = place()
        start = lax.div(group, 2) * self.high
        columns = self.column_half(group)
        chunk = 16 if self.wide > 1536 else 48
        for turn in (*TURNS, 0):
            target = partner(level, turn)
            self.last_copy(turn).wait_recv()

            def add(step, carry):
                at = pl.multiple_of(step * chunk, chunk)
                rows = pl.ds(at, chunk)
                mine = pl.ds(pl.multiple_of(start + at, 16), chunk)
                total = self.own[target, mine, columns].astype(jnp.float32)
                total = total + self.got_last[turn, rows, :].astype(jnp.float32)
                self.part[target, rows, :] = total.astype(self.part.dtype)
                return carry

            lax.fori_loop(0, self.high // chunk, add, 0)
            if turn and not self.lead:
                self.level_copy(turn).start()

    def fourth(self):
        group, level, _ = place()
        start = lax.div(group, 2) * self.high
        columns = self.column_half(group)
        chunk = 16 if self.wide > 1536 else 48
        for turn in TURNS:
            self.level_copy(turn).wait_recv()

        def add(step, carry):
            at = pl.multiple_of(step * chunk, chunk)
            rows = pl.ds(at, chunk)
            mine = pl.ds(pl.multiple_of(start + at, 16), chunk)
            total = self.part[level, rows, :].astype(jnp.float32)
            for slot in range(3):
                total = total + self.got_level[slot, rows, :].astype(jnp.float32)
            self.out[mine, columns] = total.astype(self.out.dtype)
            return carry

        lax.fori_loop(0, self.high // chunk, add, 0)
        for other in TURNS:
            self.share_copy(other).start()

    def store(self):
        self.target[...] = self.out[...]

    def fifth(self):
        for other in TURNS:
            self.share_copy(other).wait_recv()

    def sixth(self):
        _, level, _ = place()
        for turn in (*TURNS, 0):
            self.core_copy(partner(level, turn)).wait_send()
            self.step_copy(turn).wait_send()
            self.last_copy(turn).wait_send()
            if turn and not self.lead:
                self.level_copy(turn).wait_send()
                self.share_copy(turn).wait_send()


class Lead(Whole):
    lead = True

    def store(self):
        self.target[...] = self.part[...]


class Rest(Whole):
    def __init__(self, part, out, got_level, sems):
        self.part, self.out, self.got_level, self.sems = part, out, got_level, sems
        self.rows, self.columns = out.shape
        self.high, self.wide = self.rows // 2, self.columns // 2

    def first(self):
        for turn in TURNS:
            self.level_copy(turn).start()

    def sixth(self):
        for turn in TURNS:
            self.level_copy(turn).wait_send()
            self.share_copy(turn).wait_send()


GROUP_SEMS = 13


class GroupReduce:
    def __init__(self, share, out, scratch, sems):
        self.share, self.out, self.sems = share, out, sems
        self.own, self.got = scratch
        self.rows, self.columns = out.shape
        self.chunk = 16

    def load(self):
        return pltpu.make_async_copy(self.share, self.own, self.sems.at[0])

    def group_copy(self, other):
        group, level, core = place()
        peer = partner(group, other)
        return remote(
            self.own.at[quarter(peer, self.rows, self.columns)],
            self.got.at[other - 1],
            self.sems.at[other],
            self.sems.at[3 + other],
            (peer, 2 * level + core),
        )

    def share_copy(self, other):
        group, level, core = place()
        mine = self.out.at[quarter(group, self.rows, self.columns)]
        return remote(
            mine,
            mine,
            self.sems.at[6 + other],
            self.sems.at[9 + other],
            (partner(group, other), 2 * level + core),
        )

    def first(self):
        self.load().start()

    def second(self):
        self.load().wait()
        for other in TURNS:
            self.group_copy(other).start()

    def between(self):
        pass

    def third(self):
        group, _, _ = place()
        high, wide = quarter_shape(self.rows, self.columns)
        row_part, column_part = quarter(group, self.rows, self.columns)
        for other in TURNS:
            self.group_copy(other).wait_recv()

        def add(step, carry):
            at = pl.multiple_of(step * self.chunk, self.chunk)
            rows = pl.ds(at, self.chunk)
            mine = pl.ds(pl.multiple_of(row_part.start + at, self.chunk), self.chunk)
            total = self.own[mine, column_part].astype(jnp.float32)
            for slot in range(3):
                total = total + self.got[slot, rows, :].astype(jnp.float32)
            self.out[mine, column_part] = total.astype(self.out.dtype)
            return carry

        lax.fori_loop(0, high // self.chunk, add, 0)
        for other in TURNS:
            self.share_copy(other).start()

    def fourth(self):
        pass

    def fifth(self):
        for other in TURNS:
            self.share_copy(other).wait_recv()

    def store(self):
        self.target[...] = self.out[...]

    def sixth(self):
        for other in TURNS:
            self.group_copy(other).wait_send()
            self.share_copy(other).wait_send()


class Spread:
    def __init__(self, full, sems):
        self.full, self.sems = full, sems

    def level_copy(self, turn):
        group, level, core = place()
        block = self.full.at[2 * level + core]
        peer = (group, 2 * partner(level, turn) + core)
        return remote(block, block, self.sems.at[turn - 1], self.sems.at[2 + turn], peer)

    def core_copy(self, turn):
        group, level, core = place()
        block = self.full.at[2 * partner(level, turn) + core]
        peer = (group, 2 * level + 1 - core)
        return remote(block, block, self.sems.at[6 + turn], self.sems.at[10 + turn], peer)

    def run(self):
        for turn in TURNS:
            self.level_copy(turn).start()
        self.core_copy(0).start()
        for turn in TURNS:
            self.level_copy(turn).wait_recv()
            self.core_copy(turn).start()
        for turn in (0, *TURNS):
            self.core_copy(turn).wait_recv()
        for turn in (0, *TURNS):
            self.core_copy(turn).wait_send()
            if turn:
                self.level_copy(turn).wait_send()


def squares_in(out):
    def add(step, total):
        piece = out[pl.ds(pl.multiple_of(step * 16, 16), 16), :].astype(jnp.float32)
        piece = piece * piece
        for lane in range(0, out.shape[1], LANES):
            total = total + piece[:, lane : lane + LANES]
        return total

    total = lax.fori_loop(0, out.shape[0] // 16, add, jnp.zeros((16, LANES), jnp.float32))
    return jnp.sum(total, 0, keepdims=True)


def run_stages(jobs, stages):
    for stage in stages:
        for job in jobs:
            getattr(job, stage)()


STAGES = ("first", "second", "between", "third", "fourth", "fifth", "sixth")


def whole_scratch(grad):
    _, rows, columns = grad.shape
    high, wide = quarter_shape(rows, columns)
    shapes = (*[(4, rows, columns)] * 3, (3, 4, high, wide), (4, high, wide))
    return [pltpu.VMEM(shape, grad.dtype) for shape in (*shapes, (3, high, wide))]


def stepped_scratch(grad):
    _, rows, columns = grad.shape
    high, wide = rows // 2, columns // 2
    shapes = (
        *[(4, rows, columns)] * 3,
        (2, rows, wide),
        (2, high, columns),
        (4, high, wide),
        (4, high, wide),
        (3, high, wide),
    )
    return [pltpu.VMEM(shape, grad.dtype) for shape in shapes]


def share_scratch(share):
    return [
        pltpu.VMEM(share.shape, share.dtype),
        pltpu.VMEM((3, *quarter_shape(*share.shape)), share.dtype),
    ]


def reduce_kernel(*refs, whole, partly, done, vector_rows, rest_size):
    count = whole + 1 + partly
    finished, grads, refs = refs[:done], refs[done : done + count], refs[done + count :]
    outs, full, numbers, refs = refs[:count], refs[count], refs[count + 1], refs[count + 2 :]
    sems, small_sems, group_sems, spread_sems, refs = *refs[:4], refs[4:]
    jobs = [
        Whole(grads[i], outs[i], refs[8 * i : 8 * i + 8], sems.at[i]) for i in range(whole)
    ]
    refs = refs[8 * whole :]
    small = Reduce(grads[whole], outs[whole], refs[:6], small_sems)
    refs = refs[6:]
    shares = [
        GroupReduce(
            grads[whole + 1 + i], outs[whole + 1 + i], refs[2 * i : 2 * i + 2], group_sems.at[i]
        )
        for i in range(partly)
    ]
    greet()
    run_stages([*jobs, small, *shares], STAGES[:1])
    run_stages([small, *shares], STAGES[1:2])
    run_stages(jobs, STAGES[1:3])
    run_stages([small, *shares], STAGES[3:4])
    run_stages(jobs, STAGES[3:4])
    run_stages([small, *jobs], STAGES[4:5])
    run_stages([*shares, small, *jobs], STAGES[5:6])
    total = sum(squares_in(out) for out in (*finished, *outs[:whole], *outs[whole + 1 :]))
    _, level, core = place()
    mine = 2 * level + core
    block = outs[whole]
    last = block.shape[0] - 1
    full[mine] = block[...]
    full[mine, last : last + 1, :] = total
    Spread(full, spread_sems).run()
    numbers[...] = totals(full[...], vector_rows, rest_size)
    run_stages([*shares, small, *jobs], STAGES[6:])


def transfer_outs(arrays):
    return [jax.ShapeDtypeStruct(array.shape[-2:], array.dtype) for array in arrays]


def reduce_call(grads, small, shares, finished, vector_rows, rest_size, collective_id):
    in_vmem = pl.BlockSpec(memory_space=pltpu.VMEM)
    whole, partly, done = len(grads), len(shares), len(finished)
    operands = [*grads, small, *shares]
    scratch = [
        pltpu.SemaphoreType.DMA((whole, WHOLE_SEMS)),
        pltpu.SemaphoreType.DMA((REDUCE_SEMS,)),
        pltpu.SemaphoreType.DMA((partly, GROUP_SEMS)),
        pltpu.SemaphoreType.DMA((14,)),
    ]
    for grad in grads:
        scratch.extend(stepped_scratch(grad))
    scratch.extend(whole_scratch(small))
    for share in shares:
        scratch.extend(share_scratch(share))
    out_shape = [*transfer_outs(operands), shape_of(*small.shape), shape_of(1, LANES)]
    return pl.pallas_call(
        functools.partial(
            reduce_kernel,
            whole=whole,
            partly=partly,
            done=done,
            vector_rows=vector_rows,
            rest_size=rest_size,
        ),
        in_specs=[in_vmem] * done + [ANYWHERE] * len(operands),
        out_specs=[in_vmem] * len(out_shape),
        out_shape=out_shape,
        scratch_shapes=scratch,
        compiler_params=pltpu.CompilerParams(
            collective_id=collective_id, has_side_effects=True, vmem_limit_bytes=VMEM_LIMIT
        ),
        cost_estimate=NO_COST,
        name="reduce_gradients",
    )(*finished, *operands)


def totals(full, vector_rows, rest_size):
    owners, rows, _ = full.shape
    rest_rows = -(-rest_size // (owners * LANES))
    row = lax.broadcasted_iota(jnp.int32, full.shape, 1)
    spot = row - vector_rows + rest_rows * lax.broadcasted_iota(jnp.int32, full.shape, 0)
    spot = spot * LANES + lax.broadcasted_iota(jnp.int32, full.shape, 2)
    in_rest = (row >= vector_rows) & (row < vector_rows + rest_rows)

    def summed(values):
        return jnp.sum(jnp.sum(jnp.sum(values, 0), 0, keepdims=True), 1, keepdims=True)

    tokens = summed(jnp.where(in_rest & (spot == rest_size - 1), full, 0.0))
    loss = summed(jnp.where(in_rest & (spot == rest_size - 2), full, 0.0))
    kept = (row < vector_rows) | (in_rest & (spot < rest_size - 2))
    squares = jnp.where(kept, full * full, jnp.where(row == rows - 1, full, 0.0))
    norm = jnp.sqrt(summed(squares)) / tokens
    factor = jnp.minimum(1.0, CLIP_NORM / norm) / tokens
    lane = lax.broadcasted_iota(jnp.int32, (1, LANES), 1)
    return jnp.where(
        lane == 0, factor, jnp.where(lane == 1, norm, jnp.where(lane == 2, loss, tokens))
    )


def with_kernels():
    return lax.axis_size("dp") == 4 and lax.axis_size("fsdp") == 8


def reduce_all(grads, small, shares, finished, vector_rows, rest_size, collective_id):
    if with_kernels():
        return reduce_call(grads, small, shares, finished, vector_rows, rest_size, collective_id)
    sums = [lax.psum(scatter(grad), "dp") for grad in grads]
    block = lax.psum(scatter(small), "dp")
    outs = [lax.psum(share, "dp") for share in shares]
    total = sum(jnp.sum(jnp.square(out.astype(jnp.float32))) for out in (*finished, *sums, *outs))
    row = jnp.full((1, LANES), 1.0 / LANES, jnp.float32) * total
    full = lax.all_gather(block.at[-1:].set(row), "fsdp", axis=0)
    return [*sums, block, *outs, full, totals(full, vector_rows, rest_size)]


def scatter(grad):
    return lax.psum_scatter(grad, "fsdp", scatter_dimension=0)


def by_owner(grad, low=jnp.bfloat16):
    owners = lax.axis_size("fsdp")
    return grad.astype(low).reshape(owners, grad.shape[0] // owners, grad.shape[1])


def attention_forward_kernel(
    q_ref, k_ref, v_ref, seg_col_ref, seg_row_ref, out_ref, expo_ref, inv_ref, *, block
):
    rows = q_ref.shape[0]
    lower = lax.broadcasted_iota(jnp.int32, (block, PAIR), 1) < HD
    keys = k_ref[...]
    values = jnp.concatenate([v_ref[...], jnp.ones((rows, PAIR), v_ref.dtype)], 1)
    seg_row = seg_row_ref[...]
    tasks = [(step, head) for step in range(rows // block) for head in range(2)]

    def scores_of(step, head):
        query = q_ref[step * block : (step + 1) * block, :] * jnp.bfloat16(HD**-0.5)
        keep = lower if head == 0 else jnp.logical_not(lower)
        return mul_nt(jnp.where(keep, query, jnp.bfloat16(0)), keys)

    scores = scores_of(*tasks[0])
    outs = []
    for index, (step, head) in enumerate(tasks):
        following = scores_of(*tasks[index + 1]) if index + 1 < len(tasks) else None
        at = slice(step * block, (step + 1) * block)
        scores = jnp.where(seg_col_ref[at, :] == seg_row, scores, MASKED)
        highest = jnp.max(scores, -1, keepdims=True)
        low = jnp.exp(scores - highest).astype(jnp.bfloat16)
        expo_ref[head, at, :] = low
        outs.append(mul(low, values))
        if head:
            inverse = 1.0 / jnp.where(lower, outs[0][:, PAIR:], outs[1][:, PAIR:])
            sums = jnp.where(lower, outs[0][:, :PAIR], outs[1][:, :PAIR])
            out_ref[at, :] = (sums * inverse).astype(jnp.bfloat16)
            inv_ref[at, :] = inverse
            outs = []
        scores = following


def attention_forward(qkv_rows, segment, rides, collective_id):
    rows = qkv_rows.shape[0]
    pairs = HEADS // 2
    wide = lambda base: pl.BlockSpec((rows, PAIR), lambda j, base=base: (0, base + j))
    return block_call(
        functools.partial(attention_forward_kernel, block=min(256, rows)),
        pairs,
        [wide(0), wide(pairs), wide(2 * pairs), fixed(rows, 1), fixed(1, rows)],
        [qkv_rows, qkv_rows, qkv_rows, segment[:, None], segment[None, :]],
        [wide(0), pl.BlockSpec((2, rows, rows), lambda j: (j, 0, 0)), wide(0)],
        [
            shape_of(rows, D, dtype=LOW),
            shape_of(HEADS, rows, rows, dtype=LOW),
            shape_of(rows, D),
        ],
        [],
        "attention_forward",
        work(16 * HEADS * rows * rows * HD, 2 * HEADS * rows * rows + 12 * rows * D),
        rides,
        collective_id,
    )


def attention_backward_kernel(
    q_ref, k_ref, v_ref, expo_ref, inv_ref, out_ref, grad_ref, dqkv_ref, *, block
):
    rows = q_ref.shape[0]
    pair = pl.program_id(0)
    lower = lax.broadcasted_iota(jnp.int32, (block, PAIR), 1) < HD
    keys = k_ref[...]
    values = v_ref[...]
    scale = HD**-0.5
    scaled_grad = (grad_ref[...].astype(jnp.float32) * inv_ref[...]).astype(jnp.bfloat16)
    query = q_ref[...]
    query_t = query.T
    grad_t = scaled_grad.T
    product = scaled_grad.astype(jnp.float32) * out_ref[...].astype(jnp.float32)
    key_t = [None, None]
    value_t = [None, None]
    tasks = [(step, head) for step in range(rows // block) for head in range(2)]

    def probs_grad_of(step, head):
        keep = lower if head == 0 else jnp.logical_not(lower)
        mine = scaled_grad[step * block : (step + 1) * block]
        return mul_nt(jnp.where(keep, mine, jnp.bfloat16(0)), values)

    probs_grad = probs_grad_of(*tasks[0])
    query_parts = []
    for index, (step, head) in enumerate(tasks):
        following = probs_grad_of(*tasks[index + 1]) if index + 1 < len(tasks) else None
        at = slice(step * block, (step + 1) * block)
        lanes = slice(head * HD, (head + 1) * HD)
        keep = lower if head == 0 else jnp.logical_not(lower)
        inner = jnp.sum(jnp.where(keep, product[at], 0.0), -1, keepdims=True)
        low = expo_ref[head, at, :]
        value_part = mul(grad_t[lanes, at], low)
        scores_grad = (low.astype(jnp.float32) * (probs_grad - inner)).astype(jnp.bfloat16)
        query_parts.append(mul(scores_grad, keys))
        key_part = mul(query_t[lanes, at], scores_grad)
        key_t[head] = key_part if step == 0 else key_t[head] + key_part
        value_t[head] = value_part if step == 0 else value_t[head] + value_part
        if head:
            query_grad = jnp.where(lower, query_parts[0], query_parts[1]) * scale
            dqkv_ref[at, pl.ds(pl.multiple_of(pair * PAIR, PAIR), PAIR)] = query_grad.astype(
                jnp.bfloat16
            )
            query_parts = []
        probs_grad = following
    key_grad = (jnp.concatenate(key_t, 0) * scale).T
    value_grad = jnp.concatenate(value_t, 0).T
    dqkv_ref[:, pl.ds(pl.multiple_of(D + pair * PAIR, PAIR), PAIR)] = key_grad.astype(jnp.bfloat16)
    dqkv_ref[:, pl.ds(pl.multiple_of(2 * D + pair * PAIR, PAIR), PAIR)] = value_grad.astype(jnp.bfloat16)


def attention_backward(qkv_rows, expo, inverse, attended, attended_grad, rides, collective_id):
    rows = qkv_rows.shape[0]
    pairs = HEADS // 2
    wide = lambda base: pl.BlockSpec((rows, PAIR), lambda j, base=base: (0, base + j))
    return block_call(
        functools.partial(attention_backward_kernel, block=min(256, rows)),
        pairs,
        [
            wide(0),
            wide(pairs),
            wide(2 * pairs),
            pl.BlockSpec((2, rows, rows), lambda j: (j, 0, 0)),
            wide(0),
            wide(0),
            wide(0),
        ],
        [qkv_rows, qkv_rows, qkv_rows, expo, inverse, attended, attended_grad],
        [fixed(rows, 3 * D)],
        [shape_of(rows, 3 * D, dtype=LOW)],
        [],
        "attention_backward",
        None,
        rides,
        collective_id,
    )


def mul(left, right):
    return jnp.dot(left, right, preferred_element_type=jnp.float32)


def mul_nt(left, right):
    return lax.dot_general(left, right, NT, preferred_element_type=jnp.float32)


def normalized(values):
    center = values - jnp.mean(values, -1, keepdims=True)
    inverse = lax.rsqrt(jnp.mean(center * center, -1, keepdims=True) + NORM_EPS)
    return center * inverse, inverse


def norm_backward(grad, values, gain):
    unit, inverse = normalized(values)
    inner = grad * gain
    mean_inner = jnp.mean(inner, -1, keepdims=True)
    mean_cross = jnp.mean(inner * unit, -1, keepdims=True)
    value_grad = inverse * (inner - mean_inner - unit * mean_cross)
    return value_grad, column_sum(grad * unit), column_sum(grad)


def column_sum(rows):
    return jnp.sum(rows.astype(jnp.float32), 0, keepdims=True)


def at_first(action):
    pl.when(pl.program_id(0) == 0)(action)


def rows_of(block, columns):
    return pl.BlockSpec((block, columns), lambda i: (i, 0))


def fixed(*shape):
    return pl.BlockSpec(shape, lambda i: (0,) * len(shape), pipeline_mode=pl.Buffered(1))


def loads(sources, targets, sems):
    return [
        pltpu.make_async_copy(source, target, sems.at[index])
        for index, (source, target) in enumerate(zip(sources, targets))
    ]


def shape_of(*shape, dtype=jnp.float32):
    return jax.ShapeDtypeStruct(shape, dtype)


def embed_kernel(pixel_ref, weight_ref, pos_ref, table_ref, bias_ref, out_ref):
    position = jnp.dot(
        pos_ref[...], table_ref[...], precision=HIGHEST, preferred_element_type=jnp.float32
    )
    out_ref[...] = mul(pixel_ref[...], weight_ref[...]) + bias_ref[...] + position


def embed(pixels, weight, pos_weights, table, bias):
    rows, depth = pixels.shape
    block = 256
    nodes = pos_weights.shape[1]
    return block_call(
        embed_kernel,
        rows // block,
        [rows_of(block, depth), fixed(depth, D), rows_of(block, nodes), fixed(nodes, D), fixed(1, D)],
        [pixels, weight, pos_weights, table, bias],
        [rows_of(block, D)],
        [shape_of(rows, D)],
        [],
        "embed",
        work(2 * rows * depth * D, 2 * rows * depth + 2 * depth * D + 4 * rows * D),
    )[0]


def chunk_at(base):
    return pl.ds(pl.multiple_of(base + pl.program_id(0) * D, LANES), D)


def columns_of(rows):
    return pl.BlockSpec((rows, D), lambda i: (0, i))


def halves_of(rows):
    half = rows // 2
    return [slice(start, start + half) for start in range(0, rows, half)]


def at_last(action):
    pl.when(pl.program_id(0) == pl.num_programs(0) - 1)(action)


def qkv_kernel(stream_ref, weight_ref, vector_ref, normed_out, qkv_ref, normed_ref, sem):
    copy = pltpu.make_async_copy(normed_ref, normed_out, sem)

    @at_first
    def _():
        unit, _ = normalized(stream_ref[...])
        normed_ref[...] = (unit * vector_ref[:, :D] + vector_ref[:, D : 2 * D]).astype(LOW)
        copy.start()

    bias = vector_ref[:, chunk_at(4 * D)]
    for half in halves_of(stream_ref.shape[0]):
        qkv_ref[half, :] = (mul(normed_ref[half, :], weight_ref[...]) + bias).astype(LOW)
    at_last(copy.wait)


def qkv_forward(stream, weight, vector):
    rows = stream.shape[0]
    return block_call(
        qkv_kernel,
        3,
        [fixed(rows, D), columns_of(D), fixed(1, vector.shape[1])],
        [stream, weight, vector],
        [ANYWHERE, columns_of(rows)],
        [shape_of(rows, D, dtype=LOW), shape_of(rows, 3 * D, dtype=LOW)],
        [pltpu.VMEM((rows, D), LOW), pltpu.SemaphoreType.DMA],
        "qkv_forward",
        work(6 * rows * D * D, 14 * rows * D + 6 * D * D),
    )


def mlp_kernel(
    stream_ref, attended_ref, mix_ref, up_ref, down_ref, vector_ref,
    residual_out, normed_out, active_ref, slope_ref, out_ref,
    residual_ref, normed_ref, sems,
):
    rows = stream_ref.shape[0]
    copies = loads((residual_ref, normed_ref), (residual_out, normed_out), sems)

    @at_first
    def _():
        for half in halves_of(rows):
            residual = stream_ref[half, :] + mul(attended_ref[half, :], mix_ref[...])
            residual = residual + vector_ref[:, 7 * D : 8 * D]
            residual_ref[half, :] = residual
            unit, _ = normalized(residual)
            normed = unit * vector_ref[:, 2 * D : 3 * D] + vector_ref[:, 3 * D : 4 * D]
            normed_ref[half, :] = normed.astype(LOW)
            out_ref[half, :] = residual + vector_ref[:, 8 * D : 9 * D]
        for copy in copies:
            copy.start()

    bias = vector_ref[:, chunk_at(9 * D)]
    parts = halves_of(rows)
    hidden = mul(normed_ref[parts[0], :], up_ref[...]) + bias
    for index, half in enumerate(parts):
        following = None
        if index + 1 < len(parts):
            following = mul(normed_ref[parts[index + 1], :], up_ref[...]) + bias
        square = hidden * hidden
        rise = 0.5 + 0.5 * jnp.tanh(hidden * (ROOT + (ROOT * CUBE) * square))
        active = hidden * rise
        active_low = active.astype(LOW)
        active_ref[half, :] = active_low
        bend = (2.0 * ROOT) + (6.0 * ROOT * CUBE) * square
        slope_ref[half, :] = (rise + active * (1.0 - rise) * bend).astype(LOW)
        out_ref[half, :] += mul(active_low, down_ref[...])
        hidden = following

    @at_last
    def _():
        for copy in copies:
            copy.wait()


def mlp_specs(up, proj_out):
    return (
        [fixed(D, D), columns_of(D), pl.BlockSpec((D, D), lambda i: (i + 1, 0))],
        [proj_out, up, proj_out],
    )


def mlp_forward(stream, attended, up, proj_out, vector):
    rows = stream.shape[0]
    width = up.shape[1]
    weight_specs, weights = mlp_specs(up, proj_out)
    return block_call(
        mlp_kernel,
        width // D,
        [fixed(rows, D), fixed(rows, D), *weight_specs, fixed(1, vector.shape[1])],
        [stream, attended, *weights, vector],
        [ANYWHERE, ANYWHERE, columns_of(rows), columns_of(rows), fixed(rows, D)],
        [
            shape_of(rows, D),
            shape_of(rows, D, dtype=LOW),
            shape_of(rows, width, dtype=LOW),
            shape_of(rows, width, dtype=LOW),
            shape_of(rows, D),
        ],
        [
            pltpu.VMEM((rows, D), jnp.float32),
            pltpu.VMEM((rows, D), LOW),
            pltpu.SemaphoreType.DMA((2,)),
        ],
        "mlp_forward",
        work(2 * rows * D * (D + 2 * width), rows * (16 * D + 4 * width) + 2 * D * (D + 2 * width)),
    )


def mlp_back_kernel(
    grad_ref, slope_ref, residual_in, normed_ref, active_ref, attended_ref, mix_ref, up_ref, down_ref, vector_ref,
    out_ref, attended_grad_ref, sums_ref, output_grad, *refs,
):
    up_grads, scratch = refs[:-7], refs[-7:]
    residual_ref, low_ref, second_ref, turned_ref, hidden_ref, product_ref, sems = scratch
    rows = grad_ref.shape[0]
    step = pl.program_id(0)
    load = pltpu.make_async_copy(residual_in, residual_ref, sems.at[0])

    def store_copy(slot):
        rows_at = pl.ds(pl.multiple_of(slot * D, D), D)
        return pltpu.make_async_copy(
            product_ref.at[slot], output_grad.at[rows_at], sems.at[1 + slot]
        )

    def store(slot, product):
        product_ref[slot] = product.astype(LOW)
        store_copy(slot).start()

    @at_first
    def _():
        load.start()
        low_ref[...] = grad_ref[...].astype(LOW)
        turned_ref[...] = normed_ref[...].T
        second_ref[...] = jnp.zeros_like(second_ref)

    parts = halves_of(rows)
    active_grad = mul_nt(low_ref[parts[0], :], down_ref[...])
    hidden_sum = 0.0
    for index, half in enumerate(parts):
        following = None
        if index + 1 < len(parts):
            following = mul_nt(low_ref[parts[index + 1], :], down_ref[...])
        hidden_grad = (active_grad * slope_ref[half, :].astype(jnp.float32)).astype(LOW)
        hidden_ref[half, :] = hidden_grad
        hidden_sum = hidden_sum + column_sum(hidden_grad)
        second_ref[half, :] += mul_nt(hidden_grad, up_ref[...])
        active_grad = following
    sums_ref[:, chunk_at(4 * D)] = hidden_sum
    store(step + 1, mul(active_ref[...].T, low_ref[...]))
    up_grad = mul(turned_ref[...], hidden_ref[...]).astype(LOW)
    share = pl.num_programs(0) // len(up_grads)
    for index, part in enumerate(up_grads):

        @pl.when(lax.div(step, share) == index)
        def _(part=part):
            part[...] = up_grad

    @at_last
    def _():
        load.wait()
        gain = vector_ref[:, 2 * D : 3 * D]
        totals = [0.0] * 4
        for half in halves_of(rows):
            grad = grad_ref[half, :]
            value_grad, gain_grad, shift_grad = norm_backward(
                second_ref[half, :], residual_ref[half, :], gain
            )
            total = value_grad + grad
            out_ref[half, :] = total
            total_low = total.astype(LOW)
            hidden_ref[half, :] = total_low
            attended_grad_ref[half, :] = mul_nt(total_low, mix_ref[...]).astype(LOW)
            new = (gain_grad, shift_grad, column_sum(total_low), column_sum(low_ref[half, :]))
            totals = [old + part for old, part in zip(totals, new)]
        sums_ref[:, : 4 * D] = jnp.concatenate(totals, 1)
        store(0, mul(attended_ref[...].T, hidden_ref[...]))
        for slot in range(product_ref.shape[0]):
            store_copy(slot).wait()


def mlp_backward(
    grad, slope, residual, normed, active, attended, up, proj_out, vector, parts, rides, collective_id
):
    rows = grad.shape[0]
    width = up.shape[1]
    steps = width // D
    share = steps // parts
    part_of = lambda index: lambda i: (0, jnp.clip(i - index * share, 0, share - 1))
    whole = fixed(rows, D)
    weight_specs, weights = mlp_specs(up, proj_out)
    return block_call(
        mlp_back_kernel,
        steps,
        [
            whole,
            columns_of(rows),
            ANYWHERE,
            whole,
            columns_of(rows),
            whole,
            *weight_specs,
            fixed(1, vector.shape[1]),
        ],
        [grad, slope, residual, normed, active, attended, *weights, vector],
        [whole, whole, fixed(1, 4 * D + width), ANYWHERE, *[pl.BlockSpec((D, D), part_of(index)) for index in range(parts)]],
        [
            shape_of(rows, D),
            shape_of(rows, D, dtype=LOW),
            shape_of(1, 4 * D + width),
            shape_of(D + width, D, dtype=LOW),
            *[shape_of(D, width // parts, dtype=LOW)] * parts,
        ],
        [
            pltpu.VMEM((rows, D), jnp.float32),
            pltpu.VMEM((rows, D), LOW),
            pltpu.VMEM((rows, D), jnp.float32),
            pltpu.VMEM((D, rows), LOW),
            pltpu.VMEM((rows, D), LOW),
            pltpu.VMEM((steps + 1, D, D), LOW),
            pltpu.SemaphoreType.DMA((steps + 2,)),
        ],
        "mlp_backward",
        None,
        rides,
        collective_id,
    )


def qkv_back_kernel(
    grad_ref, residual_in, stream_in, normed_ref, weight_ref, vector_ref,
    out_ref, sums_ref, weight_grad_ref,
    residual_ref, stream_ref, sum_ref, turned_ref, sems,
):
    rows = out_ref.shape[0]
    copies = loads((residual_in, stream_in), (residual_ref, stream_ref), sems)

    @at_first
    def _():
        for copy in copies:
            copy.start()
        turned_ref[...] = normed_ref[...].T
        sum_ref[...] = jnp.zeros_like(sum_ref)

    for half in halves_of(rows):
        sum_ref[half, :] += mul_nt(grad_ref[half, :], weight_ref[...])
    sums_ref[:, chunk_at(2 * D)] = column_sum(grad_ref[...])
    weight_grad_ref[...] = mul(turned_ref[...], grad_ref[...]).astype(LOW)

    @at_last
    def _():
        for copy in copies:
            copy.wait()
        totals = [0.0] * 2
        for half in halves_of(rows):
            value_grad, gain_grad, shift_grad = norm_backward(
                sum_ref[half, :], stream_ref[half, :], vector_ref[:, :D]
            )
            out_ref[half, :] = residual_ref[half, :] + value_grad
            totals = [totals[0] + gain_grad, totals[1] + shift_grad]
        sums_ref[:, : 2 * D] = jnp.concatenate(totals, 1)


def qkv_backward(grad, residual_grad, stream, normed, weight, vector, rides, collective_id):
    rows = stream.shape[0]
    whole = fixed(rows, D)
    return block_call(
        qkv_back_kernel,
        3,
        [columns_of(rows), ANYWHERE, ANYWHERE, whole, columns_of(D), fixed(1, vector.shape[1])],
        [grad, residual_grad, stream, normed, weight, vector],
        [whole, fixed(1, 5 * D), columns_of(D)],
        [shape_of(rows, D), shape_of(1, 5 * D), shape_of(D, 3 * D, dtype=LOW)],
        [
            pltpu.VMEM((rows, D), jnp.float32),
            pltpu.VMEM((rows, D), jnp.float32),
            pltpu.VMEM((rows, D), jnp.float32),
            pltpu.VMEM((D, rows), LOW),
            pltpu.SemaphoreType.DMA((2,)),
        ],
        "qkv_backward",
        None,
        rides,
        collective_id,
    )


def embed_back_kernel(pixel_ref, grad_ref, pos_ref, out_ref, table_ref, bias_ref, low_ref):
    @at_first
    def _():
        grad = grad_ref[...]
        low = grad.astype(jnp.bfloat16)
        low_ref[...] = low
        bias_ref[...] = column_sum(low)
        table_ref[...] = jnp.dot(
            pos_ref[...], grad, precision=HIGHEST, preferred_element_type=jnp.float32
        )

    out_ref[...] = mul(pixel_ref[...].T, low_ref[...]).astype(jnp.bfloat16)


def embed_backward(pixels, grad, pos_weights_t):
    rows, depth = pixels.shape
    block = 768
    nodes = pos_weights_t.shape[0]
    return block_call(
        embed_back_kernel,
        depth // block,
        [pl.BlockSpec((rows, block), lambda i: (0, i)), fixed(rows, D), fixed(nodes, rows)],
        [pixels, grad, pos_weights_t],
        [rows_of(block, D), fixed(nodes, D), fixed(1, D)],
        [shape_of(depth, D, dtype=jnp.bfloat16), shape_of(nodes, D), shape_of(1, D)],
        [pltpu.VMEM((rows, D), jnp.bfloat16)],
        "embed_backward",
        None,
    )


def head_kernel(
    stream_ref, seg_col_ref, seg_row_ref, label_ref, weight_ref, vector_ref,
    grad_ref, weight_grad_ref, sums_ref, bias_grad_ref, numbers_ref, *, classes,
):
    padded = weight_ref.shape[1]
    vector = vector_ref[...].astype(LOW).astype(jnp.float32)
    gain, shift = vector[:, D : 2 * D], vector[:, 2 * D : 3 * D]
    slots = lax.broadcasted_iota(jnp.int32, (IMGS, 1), 0)
    member = (seg_row_ref[...] == slots).astype(jnp.float32)
    counts = jnp.sum(member, 1, keepdims=True)
    sizes = jnp.maximum(counts, 1.0)
    unit, inverse = normalized(stream_ref[...])
    final = unit * gain + shift
    owner = jnp.broadcast_to(seg_col_ref[...], final.shape)
    pooled = [jnp.sum(jnp.where(owner == k, final, 0.0), 0, keepdims=True) for k in range(IMGS)]
    pooled = (jnp.concatenate(pooled, 0) / sizes).astype(LOW)
    class_at = lax.broadcasted_iota(jnp.int32, (IMGS, padded), 1)
    logits = mul(pooled, weight_ref[...]) + vector[:, 3 * D :]
    logits = jnp.where(class_at < classes, logits, MASKED)
    highest = jnp.max(logits, -1, keepdims=True)
    exponent = jnp.exp(logits - highest)
    totals = jnp.sum(exponent, -1, keepdims=True)
    onehot = class_at == label_ref[...]
    picked = jnp.sum(jnp.where(onehot, logits, 0.0), 1, keepdims=True)
    loss = jnp.sum(counts * (highest + jnp.log(totals) - picked), 0, keepdims=True)
    numbers_ref[...] = jnp.concatenate([loss, jnp.sum(counts, 0, keepdims=True)], 1)
    logits_grad = ((exponent / totals - onehot.astype(jnp.float32)) * counts).astype(LOW)
    bias_grad_ref[...] = column_sum(logits_grad)
    weight_grad_ref[...] = lax.dot_general(
        pooled, logits_grad, (((0,), (0,)), ((), ())), preferred_element_type=jnp.float32
    ).astype(LOW)
    pooled_grad = mul_nt(logits_grad, weight_ref[...]) / sizes
    own = (seg_col_ref[...] == lax.broadcasted_iota(jnp.int32, (1, IMGS), 1)).astype(LOW)
    final_grad, left = 0.0, pooled_grad
    for _ in range(3):
        term = left.astype(LOW)
        final_grad = final_grad + mul(own, term)
        left = left - term.astype(jnp.float32)
    inner = final_grad * gain
    mean_inner = jnp.mean(inner, -1, keepdims=True)
    mean_cross = jnp.mean(inner * unit, -1, keepdims=True)
    grad_ref[...] = inverse * (inner - mean_inner - unit * mean_cross)
    sums_ref[...] = jnp.concatenate([column_sum(final_grad * unit), column_sum(final_grad)], 1)


def head(stream, segment, labels, weight, global_vector, classes):
    rows = stream.shape[0]
    padded = weight.shape[1]
    vector = jnp.pad(global_vector, (0, padded - classes))[None, :]
    return pl.pallas_call(
        functools.partial(head_kernel, classes=classes),
        out_shape=[
            shape_of(rows, D),
            shape_of(D, padded, dtype=LOW),
            shape_of(1, 2 * D),
            shape_of(1, padded),
            shape_of(1, 2),
        ],
        compiler_params=pltpu.CompilerParams(vmem_limit_bytes=VMEM_LIMIT),
        cost_estimate=NO_COST,
        name="head",
    )(stream, segment[:, None], segment[None, :], labels.reshape(IMGS, 1), weight, vector)


def adam_update(gradient, moment, square, weight, factor, learn_rate):
    clipped = gradient * factor
    moment = BETA_ONE * moment + (1.0 - BETA_ONE) * clipped
    square = BETA_TWO * square + (1.0 - BETA_TWO) * clipped * clipped
    fixed_one = 1.0 - BETA_ONE**STEP
    fixed_two = 1.0 - BETA_TWO**STEP
    step_dir = (
        moment / fixed_one / (jnp.sqrt(square / fixed_two) + ADAM_EPS) + WEIGHT_DECAY * weight
    )
    return (moment, square, weight - learn_rate * step_dir)


def body(
    pixels,
    segment,
    patch_size,
    labels,
    patch_kernel,
    head_weight,
    input_proj,
    output_proj,
    layer_vector,
    position_table,
    global_vector,
    patch_moment,
    head_moment,
    input_moment,
    output_moment,
    layer_moment,
    position_moment,
    global_moment,
    patch_square,
    head_square,
    input_square,
    output_square,
    layer_square,
    position_square,
    global_square,
):
    owners = lax.axis_size("fsdp")
    nodes = position_table.shape[0]
    vector_size = layer_vector.size
    stream, pos_weights_t, vectors, qkv_weight, up_zero, rides, rest_shards, first_rows = begin(
        pixels,
        segment,
        patch_size,
        patch_kernel,
        layer_vector,
        input_proj,
        output_proj,
        head_weight,
        position_table,
        global_vector,
    )
    qkv_one, up_one, head_full = (
        lax.all_gather(shard, "fsdp", axis=0, tiled=True) for shard in rest_shards
    )
    saved_layers = []
    for index in range(LAYERS):
        vector = vectors[index]
        if index:
            normed, qkv_rows = qkv_forward(stream, qkv_weight, vector)
        else:
            normed, qkv_rows = first_rows
        if index == 0:
            attended, expo, inverse, output, output_ride = attention_forward(
                qkv_rows, segment, rides, 4
            )
            up = up_zero
        else:
            attended, expo, inverse, output = attention_forward(qkv_rows, segment, [output_ride], 5)
            up = up_one
        residual, normed_second, active, slope, following = mlp_forward(
            stream, attended, up, output, vector
        )
        saved_layers.append(
            (
                (qkv_weight, up, output, vector),
                (stream, normed, qkv_rows, attended, expo, inverse),
                (residual, normed_second, active, slope),
            )
        )
        stream, qkv_weight = following, qkv_one
    stream_grad, head_grad, final_sums, head_bias_grad, numbers = head(
        stream, segment, labels, head_full, global_vector, head_weight.shape[1]
    )
    vector_grads = [None] * LAYERS
    for index in reversed(range(LAYERS)):
        (qkv_weight, up, output, vector), first, second = saved_layers[index]
        entering, normed, qkv_rows, attended, expo, inverse = first
        residual, normed_second, active, slope = second
        residual_grad, attended_grad, mlp_sums, output_grad, *brought = mlp_backward(
            stream_grad,
            slope,
            residual,
            normed_second,
            active,
            attended,
            up,
            output,
            vector,
            2 if index else 1,
            () if index else [output_rest, SumRide(by_owner(head_grad), False)],
            9,
        )
        if index:
            attended_grad, *up_parts = lax.optimization_barrier((attended_grad, *brought))
            late_parts = [scatter(by_owner(part)) for part in up_parts]
        else:
            up_grad, output_one_sum, head_sum = brought
            attended_grad, output_grad = lax.optimization_barrier((attended_grad, output_grad))
            late_parts.append(scatter(by_owner(output_grad)))
        qkv_grad, rest = attention_backward(
            qkv_rows,
            expo,
            inverse,
            attended,
            attended_grad,
            [LeadRide(by_owner(output_grad if index else up_grad))],
            6 if index else 8,
        )
        stream_grad, qkv_sums, qkv_weight_grad, *brought = qkv_backward(
            qkv_grad,
            residual_grad,
            entering,
            normed,
            qkv_weight,
            vector,
            () if index else [rest],
            7,
        )
        if index:
            output_rest = rest
            stream_grad, qkv_weight_grad = lax.optimization_barrier((stream_grad, qkv_weight_grad))
            late_parts.append(scatter(by_owner(qkv_weight_grad)))
        else:
            (up_zero_sum,) = brought
        vector_grads[index] = jnp.concatenate(
            [
                qkv_sums[0, : 2 * D],
                mlp_sums[0, : 2 * D],
                qkv_sums[0, 2 * D :],
                mlp_sums[0, 2 * D :],
            ]
        )
    kernel_grad, position_grad, bias_grad = embed_backward(pixels, stream_grad, pos_weights_t)
    position_grad = position_grad[:nodes]
    vector_part = jnp.stack(vector_grads).reshape(LAYERS, owners, -1)
    vector_part = jnp.swapaxes(vector_part, 0, 1).reshape(owners, vector_size)
    vector_rows = -(-vector_size // LANES)
    vector_part = jnp.pad(vector_part, ((0, 0), (0, vector_rows * LANES - vector_size)))
    rest = jnp.concatenate(
        [
            position_grad.reshape(-1),
            bias_grad[0],
            final_sums[0],
            head_bias_grad[0, :CLS],
            numbers[0],
        ]
    )
    rest_rows = -(-rest.shape[0] // (owners * LANES))
    rest_part = jnp.pad(rest, (0, rest_rows * owners * LANES - rest.shape[0]))
    small = jnp.concatenate([vector_part, rest_part.reshape(owners, -1)], 1)
    used = vector_rows + rest_rows
    block_rows = (used // 64 + 1) * 64
    small = jnp.pad(small.reshape(owners, used, LANES), ((0, 0), (0, block_rows - used), (0, 0)))
    (
        qkv_zero_sum,
        kernel_sum,
        small_share,
        *up_one_sums,
        qkv_one_sum,
        output_zero_sum,
        small_full,
        numbers,
    ) = reduce_all(
        [by_owner(qkv_weight_grad), by_owner(kernel_grad)],
        small,
        late_parts,
        [head_sum, output_one_sum, up_zero_sum],
        vector_rows,
        rest.shape[0],
        2,
    )
    factor, grad_norm, loss_sum, token_total = (numbers[0, index] for index in range(4))
    rest_sum = small_full[:, vector_rows:used].reshape(-1)
    position_sum = rest_sum[: position_grad.size].reshape(position_grad.shape)
    global_sum = rest_sum[position_grad.size :][: global_vector.shape[0]]
    kernel_sum = kernel_sum.astype(jnp.float32)
    head_sum = head_sum[:, :CLS].astype(jnp.float32)
    input_sum = jnp.stack(
        [
            jnp.concatenate(parts, 1)
            for parts in ((qkv_zero_sum, up_zero_sum), (qkv_one_sum, *up_one_sums))
        ]
    ).astype(jnp.float32)
    output_sum = jnp.stack([output_zero_sum, output_one_sum]).astype(
        jnp.float32
    )
    vector_sum = small_share[:vector_rows].reshape(-1)[:vector_size].reshape(layer_vector.shape)
    patch_next = adam_update(
        kernel_sum, patch_moment, patch_square, patch_kernel, factor, LEARN_RATE
    )
    head_next = adam_update(head_sum, head_moment, head_square, head_weight, factor, LEARN_RATE)
    input_next = adam_update(input_sum, input_moment, input_square, input_proj, factor, LEARN_RATE)
    output_next = adam_update(
        output_sum, output_moment, output_square, output_proj, factor, LEARN_RATE
    )
    layer_next = adam_update(
        vector_sum, layer_moment, layer_square, layer_vector, factor, VECTOR_RATE
    )
    position_next = adam_update(
        position_sum, position_moment, position_square, position_table, factor, LEARN_RATE
    )
    global_next = adam_update(
        global_sum, global_moment, global_square, global_vector, factor, VECTOR_RATE
    )
    return (
        loss_sum,
        token_total,
        grad_norm,
        patch_next[0],
        head_next[0],
        input_next[0],
        output_next[0],
        layer_next[0],
        position_next[0],
        global_next[0],
        patch_next[1],
        head_next[1],
        input_next[1],
        output_next[1],
        layer_next[1],
        position_next[1],
        global_next[1],
        patch_next[2],
        head_next[2],
        input_next[2],
        output_next[2],
        layer_next[2],
        position_next[2],
        global_next[2],
    )


def solution(mesh):
    in_specs = (
        P(("dp", "fsdp"), None),
        P(("dp", "fsdp")),
        P(("dp", "fsdp"), None),
        P(("dp", "fsdp"), None),
        P("fsdp", None),
        P("fsdp", None),
        P(None, "fsdp", None),
        P(None, "fsdp", None),
        P(None, "fsdp"),
        P(),
        P(),
        P("fsdp", None),
        P("fsdp", None),
        P(None, "fsdp", None),
        P(None, "fsdp", None),
        P(None, "fsdp"),
        P(),
        P(),
        P("fsdp", None),
        P("fsdp", None),
        P(None, "fsdp", None),
        P(None, "fsdp", None),
        P(None, "fsdp"),
        P(),
        P(),
    )
    out_specs = (
        P(),
        P(),
        P(),
        P("fsdp", None),
        P("fsdp", None),
        P(None, "fsdp", None),
        P(None, "fsdp", None),
        P(None, "fsdp"),
        P(),
        P(),
        P("fsdp", None),
        P("fsdp", None),
        P(None, "fsdp", None),
        P(None, "fsdp", None),
        P(None, "fsdp"),
        P(),
        P(),
        P("fsdp", None),
        P("fsdp", None),
        P(None, "fsdp", None),
        P(None, "fsdp", None),
        P(None, "fsdp"),
        P(),
        P(),
    )
    return jax.shard_map(body, mesh=mesh, in_specs=in_specs, out_specs=out_specs, check_vma=False)
```

```python
import functools

import jax
import jax.numpy as jnp
from jax import lax
from jax.experimental import pallas as pl
from jax.experimental.pallas import tpu as pltpu
from jax.sharding import PartitionSpec as P

D = 768
HEADS = 12
HD = 64
CLS = 1000
GRID = 7
IMG = 240
IMGS = 8
LAYERS = 2
STEP = 3


NORM_EPS = 1e-06
CLIP_NORM = 0.01
LEARN_RATE = 0.05
VECTOR_RATE = 0.25
BETA_ONE = 0.5
BETA_TWO = 0.5
ADAM_EPS = 1e-08
WEIGHT_DECAY = 0.05
HIGHEST = lax.Precision.HIGHEST

PAIR = 2 * HD
MASKED = -1e30
MIB = 1024 * 1024
VMEM_LIMIT = 56 * MIB
MESH = pl.DeviceIdType.MESH
LANES = 128
LOW = jnp.bfloat16
ANYWHERE = pl.BlockSpec(memory_space=pl.ANY)
NO_COST = pl.CostEstimate(flops=0, bytes_accessed=0, transcendentals=0)
ROOT = 0.7978845608028654
CUBE = 0.044715
NT = (((1,), (1,)), ((), ()))


def layer_norm(values, gain, shift):
    center = values - jnp.mean(values, -1, keepdims=True)
    spread = jnp.mean(center * center, -1, keepdims=True)
    return center * lax.rsqrt(spread + NORM_EPS) * gain + shift


def rounded(values):
    return lax.optimization_barrier(values.astype(jnp.bfloat16)).astype(jnp.float32)


def matmul(left, right):
    return jnp.dot(left, right, preferred_element_type=jnp.float32)


def padded_rows(flat, multiple):
    extra = -flat.shape[0] % (multiple * LANES)
    return jnp.pad(flat, (0, extra)).reshape(-1, LANES)


def row_layout(seg_row, patch_row):
    row_count = seg_row.shape[0]
    slots = jnp.arange(IMGS, dtype=jnp.int32)
    member = seg_row[:, None] == slots[None, :]
    counts = jnp.sum(member.astype(jnp.int32), 0, dtype=jnp.int32)
    starts = jnp.cumsum(counts, dtype=jnp.int32) - counts
    inside = jnp.any(member, 1)
    offset = jnp.arange(row_count, dtype=jnp.int32) - jnp.sum(
        jnp.where(member, starts[None, :], 0), 1, dtype=jnp.int32
    )
    offset = jnp.where(inside, offset, 0)
    patch_tok = jnp.sum(jnp.where(member, patch_row[None, :], 0), 1, dtype=jnp.int32) + jnp.where(
        inside, 0, IMG
    )
    side = IMG // patch_tok
    nodes = jnp.arange(GRID, dtype=jnp.int32).astype(jnp.float32)

    def hat(coord):
        place = ((2 * coord + 1) * GRID).astype(jnp.float32) / (2 * side).astype(jnp.float32) - 0.5
        place = jnp.clip(place, 0.0, GRID - 1.0)
        return jnp.maximum(1.0 - jnp.abs(place[:, None] - nodes[None, :]), 0.0)

    weights = (hat(offset // side)[:, :, None] * hat(offset % side)[:, None, :]).reshape(
        row_count, GRID * GRID
    )
    return (weights, member.astype(jnp.float32), counts.astype(jnp.float32))


TURNS = (1, 2, 3)


def place():
    slot = lax.axis_index("fsdp")
    return lax.axis_index("dp"), lax.div(slot, 2), lax.rem(slot, 2)


def partner(index, turn):
    if turn == 0:
        return index
    if turn == 1:
        return index + 1 - 2 * lax.rem(index, 2)
    if turn == 2:
        return lax.rem(index + 2, 4)
    return 3 - index


def greet():
    group, level, core = place()
    barrier = pltpu.get_barrier_semaphore()
    peers = [(group, 2 * level + 1 - core)]
    for turn in TURNS:
        peers.append((group, 2 * partner(level, turn) + core))
        peers.append((partner(group, turn), 2 * level + core))
    for peer in peers:
        pl.semaphore_signal(barrier, inc=1, device_id=peer, device_id_type=MESH)
    pl.semaphore_wait(barrier, len(peers))


def quarter_shape(rows, columns):
    if columns % (2 * LANES) == 0:
        return rows // 2, columns // 2
    return rows // 4, columns


def quarter(index, rows, columns):
    high, wide = quarter_shape(rows, columns)
    if wide == columns:
        return pl.ds(pl.multiple_of(index * high, high), high), pl.ds(0, columns)
    return (
        pl.ds(pl.multiple_of(lax.div(index, 2) * high, high), high),
        pl.ds(pl.multiple_of(lax.rem(index, 2) * wide, wide), wide),
    )


def remote(source, target, send, receive, device):
    return pltpu.make_async_remote_copy(
        src_ref=source,
        dst_ref=target,
        send_sem=send,
        recv_sem=receive,
        device_id=device,
        device_id_type=MESH,
    )


GATHER_SEMS = 39


def relay_rows(part, rows):
    cut = -(-rows // 32) * 16
    return (0, cut) if part == 0 else (cut, rows - cut)


class Relay:
    def region(self, turn, index):
        _, level, core = place()
        block = self.out.at[2 * partner(level, turn) + core]
        return block.at[quarter(index, *self.shard.shape)]

    def group_copy(self, turn, other):
        group, level, core = place()
        index = self.group_at + 2 * (turn - 1) + other - 1
        peer = (partner(group, other), 2 * level + core)
        target = self.region(turn, group)
        source = self.quarter_source(turn, target)
        return remote(source, target, self.sems.at[index], self.sems.at[index + 6], peer)

    def relay_copy(self, turn, part):
        group, level, core = place()
        first, count = relay_rows(part, quarter_shape(*self.shard.shape)[0])
        block = self.region(turn, partner(group, 1 + part)).at[pl.ds(first, count)]
        index = self.relay_at + 2 * (turn - 1) + part
        peer = (partner(group, 2 - part), 2 * level + core)
        return remote(block, block, self.sems.at[index], self.sems.at[index + 6], peer)

    def relay(self):
        for turn in TURNS:
            for part in range(2):
                self.group_copy(turn, 1 + part).wait_recv()
                self.relay_copy(turn, part).start()

    def wait_quarters(self, turn):
        for part in range(2):
            self.relay_copy(turn, part).wait_recv()

    def wait_passed(self):
        for turn in TURNS:
            for part in range(2):
                self.group_copy(turn, 1 + part).wait_send()
                self.relay_copy(turn, part).wait_send()


class Gather(Relay):
    group_at, relay_at = 7, 19

    def __init__(self, shard, out, sems, split, in_place=False):
        self.shard, self.out, self.sems, self.split = shard, out, sems, split
        self.in_place = in_place
        self.rows, self.columns = shard.shape

    def quarter_source(self, turn, target):
        return target

    def level_copy(self, turn):
        group, level, core = place()
        block = self.out.at[2 * level + core]
        source = self.shard
        if self.split:
            part = quarter(group, self.rows, self.columns)
            source, block = source.at[part], block.at[part]
        peer = (group, 2 * partner(level, turn) + core)
        return remote(source, block, self.sems.at[turn], self.sems.at[3 + turn], peer)

    def core_copy(self, turn):
        group, level, core = place()
        slot = 2 * partner(level, turn) + core
        source = self.shard if turn == 0 else self.out.at[slot]
        peer = (group, 2 * level + 1 - core)
        return remote(source, self.out.at[slot], self.sems.at[31 + turn], self.sems.at[35 + turn], peer)

    def own_copy(self):
        _, level, core = place()
        return pltpu.make_async_copy(self.shard, self.out.at[2 * level + core], self.sems.at[0])

    def first(self):
        for turn in TURNS:
            self.level_copy(turn).start()
        self.core_copy(0).start()
        if not self.in_place:
            self.own_copy().start()

    def second(self):
        for turn in TURNS:
            self.level_copy(turn).wait_recv()
            if self.split:
                for other in (1, 2):
                    self.group_copy(turn, other).start()
            else:
                self.core_copy(turn).start()

    def third(self, use=None):
        for turn in TURNS if self.split else ():
            self.wait_quarters(turn)
            self.core_copy(turn).start()
            if use is not None:
                use(turn, True)

    def fourth(self, use=None):
        for turn in TURNS if use is not None else (0, *TURNS):
            self.core_copy(turn).wait_recv()
            if use is not None:
                use(turn, False)
        for turn in TURNS:
            self.level_copy(turn).wait_send()
        if self.split:
            self.wait_passed()
        for turn in (0, *TURNS):
            self.core_copy(turn).wait_send()
        if not self.in_place:
            self.own_copy().wait()


class LevelGather:
    def __init__(self, shard, out, sems):
        self.shard, self.out, self.sems = shard, out, sems

    def level_copy(self, turn):
        group, level, core = place()
        return remote(
            self.shard.at[quarter(group, *self.shard.shape)],
            self.out.at[level],
            self.sems.at[turn],
            self.sems.at[3 + turn],
            (group, 2 * partner(level, turn) + core),
        )

    def first(self):
        for turn in TURNS:
            self.level_copy(turn).start()

    def second(self):
        pass

    def third(self):
        pass

    def fourth(self):
        for turn in TURNS:
            self.level_copy(turn).wait_recv()
            self.level_copy(turn).wait_send()

    def store(self):
        _, level, _ = place()
        self.out[level] = jnp.zeros(self.out.shape[1:], self.out.dtype)
        self.target[...] = self.out[...]


GROUP_GATHER_SEMS = 36


class GroupGather(Relay):
    group_at, relay_at = 4, 16

    def __init__(self, shard, quarters, out, sems):
        self.shard, self.quarters, self.out, self.sems = shard, quarters, out, sems

    def quarter_source(self, turn, target):
        _, level, _ = place()
        return self.quarters.at[partner(level, turn)]

    def own_copy(self, turn):
        group, level, core = place()
        if turn == 0:
            source, target = self.shard, self.out.at[2 * level + core]
        else:
            source, target = self.quarters.at[partner(level, turn)], self.region(turn, group)
        return pltpu.make_async_copy(source, target, self.sems.at[turn])

    def core_copy(self, turn):
        group, level, core = place()
        slot = 2 * partner(level, turn) + core
        source = self.shard if turn == 0 else self.out.at[slot]
        peer = (group, 2 * level + 1 - core)
        return remote(source, self.out.at[slot], self.sems.at[28 + turn], self.sems.at[32 + turn], peer)

    def first(self):
        for turn in TURNS:
            for other in (1, 2):
                self.group_copy(turn, other).start()
        for turn in (0, *TURNS):
            self.own_copy(turn).start()
        self.core_copy(0).start()

    def third(self):
        for turn in TURNS:
            self.wait_quarters(turn)
            self.own_copy(turn).wait()
            self.core_copy(turn).start()

    def fourth(self):
        for turn in (0, *TURNS):
            self.core_copy(turn).wait_recv()
            self.core_copy(turn).wait_send()
        self.wait_passed()
        self.own_copy(0).wait()

    def store(self):
        copy = pltpu.make_async_copy(self.out, self.target, self.sems.at[0])
        copy.start()
        copy.wait()


class LevelRide:
    def __init__(self, shard):
        self.operands = [shard]
        self.in_specs = [fixed(*shard.shape)]
        shape = (4, *quarter_shape(*shard.shape))
        self.out_specs = [fixed(*shape)]
        self.out_shapes = [jax.ShapeDtypeStruct(shape, shard.dtype)]
        self.scratch = [pltpu.VMEM(shape, shard.dtype), pltpu.SemaphoreType.DMA((7,))]

    def job(self, sources, targets, scratch):
        job = LevelGather(sources[0], *scratch)
        job.target = targets[0]
        return job

    def before(self, steps):
        return {0: ("first",)}

    after = ("fourth", "store")

    def result(self, outs):
        return GatherRide(self.operands[0], outs[0])

    def plain(self):
        return GatherRide(self.operands[0], self.operands[0])


class GatherRide:
    def __init__(self, shard, quarters):
        owners = lax.axis_size("fsdp")
        full = (owners, *shard.shape)
        self.operands = [shard, quarters]
        self.in_specs = [fixed(*shard.shape), fixed(*quarters.shape)]
        self.out_specs = [ANYWHERE]
        self.out_shapes = [jax.ShapeDtypeStruct(full, shard.dtype)]
        self.scratch = [
            pltpu.VMEM(full, shard.dtype),
            pltpu.SemaphoreType.DMA((GROUP_GATHER_SEMS,)),
        ]

    def job(self, sources, targets, scratch):
        job = GroupGather(*sources, *scratch)
        job.target = targets[0]
        return job

    def before(self, steps):
        return {0: ("first",), steps // 2: ("relay",), steps - 1: ("third",)}

    after = ("fourth", "store")

    def result(self, outs):
        return outs[0].reshape(-1, outs[0].shape[2])

    def plain(self):
        return lax.all_gather(self.operands[0], "fsdp", axis=0, tiled=True)


class ShareRide:
    def __init__(self, share):
        self.operands = [share]
        self.in_specs = [ANYWHERE]
        self.out_specs = [fixed(*share.shape)]
        self.out_shapes = [jax.ShapeDtypeStruct(share.shape, share.dtype)]
        self.scratch = [
            pltpu.VMEM(share.shape, share.dtype),
            *share_scratch(share),
            pltpu.SemaphoreType.DMA((GROUP_SEMS,)),
        ]

    def job(self, sources, targets, scratch):
        job = GroupReduce(sources[0], scratch[0], scratch[1:3], scratch[3])
        job.target = targets[0]
        return job

    def before(self, steps):
        return {0: ("first", "second"), max(1, steps // 2): ("third",)}

    after = ("fifth", "sixth", "store")

    def result(self, outs):
        return outs[0]

    def plain(self):
        return lax.psum(self.operands[0], "dp")


class SumRide:
    def __init__(self, grad, large):
        block = grad.shape[1:]
        self.large = large
        self.operands = [grad]
        self.in_specs = [ANYWHERE]
        self.out_specs = [fixed(*block)]
        self.out_shapes = [jax.ShapeDtypeStruct(block, grad.dtype)]
        buffers = stepped_scratch(grad) if large else whole_scratch(grad)
        sems = WHOLE_SEMS if large else REDUCE_SEMS
        self.scratch = [pltpu.VMEM(block, grad.dtype), *buffers, pltpu.SemaphoreType.DMA((sems,))]

    def job(self, sources, targets, scratch):
        job = (Whole if self.large else Reduce)(sources[0], scratch[0], scratch[1:-1], scratch[-1])
        job.target = targets[0]
        return job

    def before(self, steps):
        if self.large:
            return {0: ("first",), 1: ("second",), steps - 2: ("between",), steps - 1: ("third",)}
        return {0: ("first",), 1: ("second",), steps // 2: ("third",), steps - 1: ("fourth",)}

    @property
    def after(self):
        return (("fourth",) if self.large else ()) + ("fifth", "sixth", "store")

    def result(self, outs):
        return outs[0]

    def plain(self):
        return lax.psum(scatter(self.operands[0]), "dp")


class LeadRide:
    after = ("third", "sixth", "store")

    def __init__(self, grad):
        _, rows, columns = grad.shape
        shape = (4, rows // 2, columns // 2)
        self.operands = [grad]
        self.in_specs = [ANYWHERE]
        self.out_specs = [fixed(*shape)]
        self.out_shapes = [jax.ShapeDtypeStruct(shape, grad.dtype)]
        self.scratch = [*stepped_scratch(grad), pltpu.SemaphoreType.DMA((WHOLE_SEMS,))]

    def job(self, sources, targets, scratch):
        job = Lead(sources[0], None, scratch[:-1], scratch[-1])
        job.target = targets[0]
        return job

    def before(self, steps):
        return {0: ("first",), 1: ("second",), steps - 2: ("between",)}

    def result(self, outs):
        return RestRide(outs[0])

    def plain(self):
        return RestRide(self.operands[0])


class RestRide:
    after = ("fifth", "sixth", "store")

    def __init__(self, part):
        _, high, wide = part.shape
        block = (2 * high, 2 * wide)
        self.operands = [part]
        self.in_specs = [fixed(*part.shape)]
        self.out_specs = [fixed(*block)]
        self.out_shapes = [jax.ShapeDtypeStruct(block, part.dtype)]
        self.scratch = [
            pltpu.VMEM(block, part.dtype),
            pltpu.VMEM((3, high, wide), part.dtype),
            pltpu.SemaphoreType.DMA((WHOLE_SEMS,)),
        ]

    def job(self, sources, targets, scratch):
        job = Rest(sources[0], *scratch)
        job.target = targets[0]
        return job

    def before(self, steps):
        return {0: ("first",), steps - 1: ("fourth",)}

    def result(self, outs):
        return outs[0]

    def plain(self):
        return lax.psum(scatter(self.operands[0]), "dp")


def riding(body, counts, rides, steps):
    def kernel(*refs):
        refs = list(refs)

        def pop(count):
            taken = refs[:count]
            del refs[:count]
            return taken

        own = pop(counts[0])
        sources = [pop(len(ride.operands)) for ride in rides]
        own += pop(counts[1])
        targets = [pop(len(ride.out_shapes)) for ride in rides]
        own += pop(counts[2])
        jobs = [
            ride.job(source, target, pop(len(ride.scratch)))
            for ride, source, target in zip(rides, sources, targets)
        ]
        for step in range(steps):
            planned = [
                (job, stages)
                for ride, job in zip(rides, jobs)
                for at, stages in ride.before(steps).items()
                if at == step
            ]
            if planned:

                @pl.when(pl.program_id(0) == step)
                def _(planned=planned, step=step):
                    if step == 0:
                        greet()
                    for job, stages in planned:
                        run_stages([job], stages)

        body(*own)

        @pl.when(pl.program_id(0) == steps - 1)
        def _():
            for ride, job in zip(rides, jobs):
                run_stages([job], ride.after)

    return kernel


def block_call(
    body, grid, in_specs, operands, out_specs, out_shape, scratch, name,
    cost=None, rides=(), collective_id=None,
):
    plain = []
    if rides and not with_kernels():
        plain, rides = [ride.plain() for ride in rides], ()
    transfer = {}
    kernel = body
    if rides:
        transfer = {"collective_id": collective_id, "has_side_effects": True}
        kernel = riding(body, (len(operands), len(out_shape), len(scratch)), rides, grid)
    count = len(out_shape)
    for ride in rides:
        operands = [*operands, *ride.operands]
        in_specs = [*in_specs, *ride.in_specs]
        out_specs, out_shape = [*out_specs, *ride.out_specs], [*out_shape, *ride.out_shapes]
        scratch = [*scratch, *ride.scratch]
    outs = pl.pallas_call(
        kernel,
        grid=(grid,),
        in_specs=in_specs,
        out_specs=out_specs,
        out_shape=out_shape,
        scratch_shapes=scratch,
        compiler_params=pltpu.CompilerParams(vmem_limit_bytes=VMEM_LIMIT, **transfer),
        cost_estimate=cost or NO_COST,
        name=name,
    )(*operands)
    brought, outs = list(outs[count:]), list(outs[:count])
    for ride in rides:
        plain.append(ride.result(brought[: len(ride.out_shapes)]))
        brought = brought[len(ride.out_shapes) :]
    return outs + plain


def work(flops, size):
    return pl.CostEstimate(flops=flops, bytes_accessed=size, transcendentals=0)


def position_weights(seg_col, patch_row, nodes):
    rows = seg_col.shape[0]
    slot = lax.broadcasted_iota(jnp.int32, (rows, IMGS), 1)
    member = seg_col == slot
    counts = jnp.sum(member.astype(jnp.float32), 0, keepdims=True)
    start = jnp.sum(jnp.where(slot < seg_col, counts, 0.0), 1, keepdims=True)
    token = lax.broadcasted_iota(jnp.int32, (rows, 1), 0).astype(jnp.float32)
    inside = seg_col < IMGS
    offset = jnp.where(inside, token - start, 0.0)
    patch = jnp.sum(jnp.where(member, patch_row.astype(jnp.float32), 0.0), 1, keepdims=True)
    side = jnp.where(inside, jnp.floor(IMG / jnp.where(inside, patch, 1.0) + 0.5), 1.0)
    line = jnp.floor((offset + 0.5) / side)
    column = offset - line * side

    def spot(coord):
        return jnp.clip((2.0 * coord + 1.0) * GRID / (2.0 * side) - 0.5, 0.0, GRID - 1.0)

    node = lax.broadcasted_iota(jnp.int32, (rows, LANES), 1).astype(jnp.float32)
    across = jnp.floor((node + 0.5) / GRID)
    along = node - across * GRID
    weights = jnp.maximum(1.0 - jnp.abs(spot(line) - across), 0.0)
    weights = weights * jnp.maximum(1.0 - jnp.abs(spot(column) - along), 0.0)
    return jnp.where(node < nodes, weights, 0.0)


def first_kernel(*refs, spots):
    kernel, vectors, inputs, outputs, head, pixels, seg_col, patch_row, table, biases = refs[:10]
    stream, pos_t, vector_zero, vector_one = refs[10:14]
    qkv_full, up_full, output_level = refs[14:17]
    output_zero, qkv_one, up_one, output_one, head_low, normed, qkv_rows = refs[17:24]
    wide_kernel, wide_inputs, wide_outputs, wide_head, pixel_rows, table_low = refs[24:30]
    kernel_full, qkv_zero, vectors_full, qkv_landing, up_landing, output_landing = refs[30:36]
    up_zero, load_sems, sems = refs[36:]
    _, level, core = place()
    mine = 2 * level + core
    pairs = [
        (kernel, wide_kernel),
        (inputs.at[0], wide_inputs.at[0]),
        (pixels, pixel_rows),
        (inputs.at[1], wide_inputs.at[1]),
        (outputs.at[0], wide_outputs.at[0]),
        (outputs.at[1], wide_outputs.at[1]),
        (head, wide_head),
    ]
    copies = [
        pltpu.make_async_copy(source, target, load_sems.at[index])
        for index, (source, target) in enumerate(pairs)
    ]
    for copy in copies:
        copy.start()
    patch_job = Gather(kernel_full.at[mine], kernel_full, sems.at[0], True, in_place=True)
    vector_job = Gather(vectors, vectors_full, sems.at[1], False)
    qkv_job = Gather(qkv_zero, qkv_landing, sems.at[2], True)
    up_job = Gather(up_zero, up_landing, sems.at[3], True)
    output_job = LevelGather(output_zero, output_landing, sems.at[4])
    output_job.target = output_level
    copies[0].wait()
    kernel_full[mine] = wide_kernel[...].astype(LOW)
    greet()
    patch_job.first()
    vector_job.first()
    copies[1].wait()
    qkv_zero[...] = wide_inputs[0, :, : 3 * D].astype(LOW)
    qkv_job.first()
    up_zero[...] = wide_inputs[0, :, 3 * D :].astype(LOW)
    up_job.first()
    copies[4].wait()
    output_zero[...] = wide_outputs[0].astype(LOW)
    output_job.first()

    weights = position_weights(seg_col[...], patch_row[...], table.shape[0])
    pos_t[...] = weights.T[: pos_t.shape[0], :]
    table_low[...] = jnp.zeros_like(table_low)
    table_low[: table.shape[0], :] = table[...].astype(LOW).astype(jnp.float32)
    bias = biases[:, :D].astype(LOW).astype(jnp.float32)
    stream[...] = bias + jnp.dot(
        weights, table_low[...], precision=HIGHEST, preferred_element_type=jnp.float32
    )
    copies[2].wait()
    depth = wide_kernel.shape[0]

    def add_block(slot):
        columns = pl.ds(pl.multiple_of(slot * depth, depth), depth)

        def add(step, carry):
            rows = pl.ds(pl.multiple_of(step * 256, 256), 256)
            stream[rows, :] += mul(pixel_rows[rows, columns], kernel_full[slot])
            return carry

        lax.fori_loop(0, stream.shape[0] // 256, add, 0)

    def use(turn, own_core):
        add_block(2 * partner(level, turn) + (core if own_core else 1 - core))

    add_block(mine)
    patch_job.second()
    qkv_job.second()
    vector_job.second()
    patch_job.core_copy(0).wait_recv()
    use(0, False)
    copies[3].wait()
    qkv_one[...] = wide_inputs[1, :, : 3 * D].astype(LOW)
    up_one[...] = wide_inputs[1, :, 3 * D :].astype(LOW)
    patch_job.relay()
    copies[5].wait()
    output_one[...] = wide_outputs[1].astype(LOW)
    copies[6].wait()
    head_low[...] = jnp.zeros_like(head_low)
    head_low[:, : head.shape[1]] = wide_head[...].astype(LOW)
    patch_job.third(use)
    qkv_job.relay()
    up_job.second()
    patch_job.fourth(use)
    qkv_job.third()
    vector_job.third()
    vector_job.fourth()
    blocks = [vectors_full[slot].astype(jnp.float32) for slot in range(vectors_full.shape[0])]
    span = vectors.shape[0] // LAYERS
    for layer, out in enumerate((vector_zero, vector_one)):
        for row in range(out.shape[1] // LANES):
            parts = [
                block[layer * span + row - spot : layer * span + row - spot + 1, :]
                for block, spot in zip(blocks, spots)
                if 0 <= row - spot < span
            ]
            out[:, row * LANES : (row + 1) * LANES] = sum(parts)
    up_job.relay()
    up_job.third()
    qkv_job.fourth()
    copy = pltpu.make_async_copy(qkv_landing, qkv_full, load_sems.at[0])
    copy.start()
    weight = qkv_landing[...].reshape(-1, qkv_landing.shape[2])
    for half in halves_of(stream.shape[0]):
        unit, _ = normalized(stream[half, :])
        low = (unit * vector_zero[:, :D] + vector_zero[:, D : 2 * D]).astype(LOW)
        normed[half, :] = low
        for base in range(0, 3 * D, D):
            bias = vector_zero[:, 4 * D + base : 5 * D + base]
            qkv_rows[half, base : base + D] = (mul(low, weight[:, base : base + D]) + bias).astype(LOW)
    up_job.fourth()
    up_copy = pltpu.make_async_copy(up_landing, up_full, load_sems.at[1])
    up_copy.start()
    run_stages([output_job], ("fourth", "store"))
    copy.wait()
    up_copy.wait()


def padded_vectors(shard):
    layers, width = shard.shape
    owners = lax.axis_size("fsdp")
    spots = [owner * width // LANES for owner in range(owners)]
    span = max(-(-(owner + 1) * width // LANES) - spot for owner, spot in enumerate(spots))
    span += -span % 16
    shift = lax.rem(lax.axis_index("fsdp") * width, LANES)
    padded = jnp.zeros((layers, span * LANES), LOW)
    padded = lax.dynamic_update_slice(padded, shard.astype(LOW), (0, shift))
    return padded.reshape(layers * span, LANES), spots


def begin(
    pixels, segment, patch_size, patch_kernel, layer_vector, input_proj, output_proj, head_weight,
    position_table, global_vector,
):
    classes = head_weight.shape[1] + -head_weight.shape[1] % LANES
    nodes = position_table.shape[0] + -position_table.shape[0] % 64
    if not with_kernels():
        inputs = [
            (input_proj[index, :, : 3 * D].astype(LOW), input_proj[index, :, 3 * D :].astype(LOW))
            for index in range(LAYERS)
        ]
        outputs = [output_proj[index].astype(LOW) for index in range(LAYERS)]
        gather = lambda shard, axis: lax.all_gather(shard, "fsdp", axis=axis, tiled=True)
        weights, _, _ = row_layout(segment, patch_size[0])
        weights = jnp.pad(weights, ((0, 0), (0, nodes - weights.shape[1])))
        table = jnp.pad(rounded(position_table), ((0, nodes - position_table.shape[0]), (0, 0)))
        bias = rounded(global_vector)[None, :D]
        stream = embed(pixels, gather(patch_kernel.astype(LOW), 0), weights, table, bias)
        vectors = gather(layer_vector.astype(LOW), 1).astype(jnp.float32)
        head = jnp.pad(head_weight.astype(LOW), ((0, 0), (0, classes - head_weight.shape[1])))
        return (
            stream,
            weights.T,
            [vectors[index : index + 1] for index in range(LAYERS)],
            gather(inputs[0][0], 0),
            gather(inputs[0][1], 0),
            [GatherRide(outputs[0], outputs[0]), LevelRide(outputs[1])],
            [*inputs[1], head],
            qkv_forward(stream, gather(inputs[0][0], 0), vectors[:1]),
        )
    rows = pixels.shape[0]
    owners = lax.axis_size("fsdp")
    vectors, spots = padded_vectors(layer_vector)
    depth = input_proj.shape[1]
    up_shape = (depth, input_proj.shape[2] - 3 * D)
    qkv_shape, out_shape = (depth, 3 * D), output_proj.shape[1:]
    low = lambda *shape: jax.ShapeDtypeStruct(shape, LOW)
    levels = lambda shape: low(4, *quarter_shape(*shape))
    width = layer_vector.shape[1] * owners
    shapes = [
        shape_of(rows, D),
        shape_of(nodes, rows),
        shape_of(1, width),
        shape_of(1, width),
        low(owners, *qkv_shape),
        low(owners, *up_shape),
        levels(out_shape),
        low(*out_shape),
        low(*qkv_shape),
        low(*up_shape),
        low(*out_shape),
        low(head_weight.shape[0], classes),
        low(rows, D),
        low(rows, 3 * D),
    ]
    wide = (patch_kernel, input_proj, output_proj, head_weight, pixels)
    in_vmem = pl.BlockSpec(memory_space=pltpu.VMEM)
    results = pl.pallas_call(
        functools.partial(first_kernel, spots=spots),
        in_specs=[ANYWHERE] * 6 + [in_vmem] * 4,
        out_specs=[in_vmem] * 4 + [ANYWHERE] * 2 + [in_vmem] * 8,
        out_shape=shapes,
        scratch_shapes=[
            *[pltpu.VMEM(array.shape, array.dtype) for array in wide],
            pltpu.VMEM((LANES, D), jnp.float32),
            pltpu.VMEM((owners, *patch_kernel.shape), LOW),
            pltpu.VMEM(qkv_shape, LOW),
            pltpu.VMEM((owners, *vectors.shape), LOW),
            pltpu.VMEM((owners, *qkv_shape), LOW),
            pltpu.VMEM((owners, *up_shape), LOW),
            pltpu.VMEM((4, *quarter_shape(*out_shape)), LOW),
            pltpu.VMEM(up_shape, LOW),
            pltpu.SemaphoreType.DMA((7,)),
            pltpu.SemaphoreType.DMA((5, GATHER_SEMS)),
        ],
        compiler_params=pltpu.CompilerParams(
            collective_id=1, has_side_effects=True, vmem_limit_bytes=VMEM_LIMIT
        ),
        cost_estimate=NO_COST,
        name="begin",
    )(
        patch_kernel,
        vectors,
        input_proj,
        output_proj,
        head_weight,
        pixels,
        segment[:, None],
        patch_size,
        position_table,
        global_vector[None, :],
    )
    output_zero, qkv_one, up_one, output_one, head_low, normed, qkv_rows = results[7:]
    return (
        results[0],
        results[1],
        results[2:4],
        results[4].reshape(owners * depth, 3 * D),
        results[5].reshape(owners * depth, up_shape[1]),
        [GatherRide(output_zero, results[6]), LevelRide(output_one)],
        [qkv_one, up_one, head_low],
        (normed, qkv_rows),
    )


REDUCE_SEMS = 52


class Reduce:
    def __init__(self, grad, out, scratch, sems):
        self.grad, self.out, self.sems = grad, out, sems
        self.own, self.away, self.got_core, self.got_group, self.part, self.got_level = scratch
        self.rows, self.columns = out.shape
        self.chunk = 16

    def load(self, level):
        _, _, core = place()
        return pltpu.make_async_copy(
            self.grad.at[2 * level + core], self.own.at[level], self.sems.at[level]
        )

    def load_away(self, level):
        _, _, core = place()
        return pltpu.make_async_copy(
            self.grad.at[2 * level + 1 - core], self.away.at[level], self.sems.at[48 + level]
        )

    def core_copy(self, target_level):
        group, level, core = place()
        return remote(
            self.away.at[target_level],
            self.got_core.at[target_level],
            self.sems.at[4 + target_level],
            self.sems.at[8 + target_level],
            (group, 2 * level + 1 - core),
        )

    def group_copy(self, turn, other):
        group, level, core = place()
        target = partner(level, turn)
        peer = partner(group, other)
        part = quarter(peer, self.rows, self.columns)
        index = 3 * turn + other - 1
        return remote(
            self.own.at[target].at[part],
            self.got_group.at[other - 1, target],
            self.sems.at[12 + index],
            self.sems.at[24 + index],
            (peer, 2 * level + core),
        )

    def level_copy(self, turn):
        group, level, core = place()
        target = partner(level, turn)
        return remote(
            self.part.at[target],
            self.got_level.at[turn - 1],
            self.sems.at[35 + turn],
            self.sems.at[38 + turn],
            (group, 2 * target + core),
        )

    def share_copy(self, other):
        group, level, core = place()
        mine = self.out.at[quarter(group, self.rows, self.columns)]
        return remote(
            mine,
            mine,
            self.sems.at[41 + other],
            self.sems.at[44 + other],
            (partner(group, other), 2 * level + core),
        )

    def first(self):
        _, level, _ = place()
        for turn in (*TURNS, 0):
            self.load_away(partner(level, turn)).start()
        for turn in (*TURNS, 0):
            self.load(partner(level, turn)).start()
        for turn in (*TURNS, 0):
            self.load_away(partner(level, turn)).wait()
            self.core_copy(partner(level, turn)).start()

    def second(self):
        _, level, _ = place()
        for turn in (*TURNS, 0):
            target = partner(level, turn)
            self.load(target).wait()
            self.core_copy(target).wait_recv()

            def add(step, carry):
                rows = pl.ds(pl.multiple_of(step * self.chunk, self.chunk), self.chunk)
                total = self.own[target, rows, :].astype(jnp.float32)
                total = total + self.got_core[target, rows, :].astype(jnp.float32)
                self.own[target, rows, :] = total.astype(self.own.dtype)
                return carry

            lax.fori_loop(0, self.rows // self.chunk, add, 0)
            for other in TURNS:
                self.group_copy(turn, other).start()

    def between(self):
        pass

    def third(self):
        group, level, _ = place()
        high, wide = quarter_shape(self.rows, self.columns)
        row_part, column_part = quarter(group, self.rows, self.columns)
        for turn in (*TURNS, 0):
            target = partner(level, turn)
            for other in TURNS:
                self.group_copy(turn, other).wait_recv()

            def add(step, carry):
                at = pl.multiple_of(step * self.chunk, self.chunk)
                rows = pl.ds(at, self.chunk)
                mine = pl.ds(pl.multiple_of(row_part.start + at, self.chunk), self.chunk)
                total = self.own[target, mine, column_part].astype(jnp.float32)
                for slot in range(3):
                    total = total + self.got_group[slot, target, rows, :].astype(jnp.float32)
                self.part[target, rows, :] = total.astype(self.part.dtype)
                return carry

            lax.fori_loop(0, high // self.chunk, add, 0)
            if turn:
                self.level_copy(turn).start()

    def fourth(self):
        group, level, _ = place()
        high, wide = quarter_shape(self.rows, self.columns)
        row_part, column_part = quarter(group, self.rows, self.columns)
        for turn in TURNS:
            self.level_copy(turn).wait_recv()

        def add(step, carry):
            at = pl.multiple_of(step * self.chunk, self.chunk)
            rows = pl.ds(at, self.chunk)
            mine = pl.ds(pl.multiple_of(row_part.start + at, self.chunk), self.chunk)
            total = self.part[level, rows, :].astype(jnp.float32)
            for slot in range(3):
                total = total + self.got_level[slot, rows, :].astype(jnp.float32)
            self.out[mine, column_part] = total.astype(self.out.dtype)
            return carry

        lax.fori_loop(0, high // self.chunk, add, 0)
        for other in TURNS:
            self.share_copy(other).start()

    def store(self):
        self.target[...] = self.out[...]

    def fifth(self):
        for other in TURNS:
            self.share_copy(other).wait_recv()

    def sixth(self):
        _, level, _ = place()
        for turn in (*TURNS, 0):
            self.core_copy(partner(level, turn)).wait_send()
            for other in TURNS:
                self.group_copy(turn, other).wait_send()
            if turn:
                self.level_copy(turn).wait_send()
                self.share_copy(turn).wait_send()


WHOLE_SEMS = 44


def add_rows(target, row, columns, source, count, wide):
    chunk = 16 if wide > 1536 else 48

    def add(step, carry):
        at = pl.multiple_of(step * chunk, chunk)
        mine = pl.ds(pl.multiple_of(row + at, 16), chunk)
        total = target[mine, columns].astype(jnp.float32)
        total = total + source[pl.ds(at, chunk), :].astype(jnp.float32)
        target[mine, columns] = total.astype(target.dtype)
        return carry

    lax.fori_loop(0, count // chunk, add, 0)


class Whole:
    FIRST_X = (1, 0)

    lead = False

    def __init__(self, grad, out, scratch, sems):
        self.grad, self.out, self.sems = grad, out, sems
        self.own, self.away, self.got_core, self.got_x, self.got_y, self.got_last, self.part, self.got_level = scratch
        self.rows, self.columns = grad.shape[1:]
        self.high, self.wide = self.rows // 2, self.columns // 2

    def row_half(self, index):
        return pl.ds(pl.multiple_of(lax.div(index, 2) * self.high, self.high), self.high)

    def column_half(self, index):
        return pl.ds(pl.multiple_of(lax.rem(index, 2) * self.wide, self.wide), self.wide)

    def load(self, level):
        _, _, core = place()
        return pltpu.make_async_copy(
            self.grad.at[2 * level + core], self.own.at[level], self.sems.at[level]
        )

    def load_away(self, level):
        _, _, core = place()
        return pltpu.make_async_copy(
            self.grad.at[2 * level + 1 - core], self.away.at[level], self.sems.at[40 + level]
        )

    def core_copy(self, target_level):
        group, level, core = place()
        return remote(
            self.away.at[target_level],
            self.got_core.at[target_level],
            self.sems.at[4 + target_level],
            self.sems.at[8 + target_level],
            (group, 2 * level + 1 - core),
        )

    def step_copy(self, turn):
        group, level, core = place()
        block = self.own.at[partner(level, turn)]
        if turn in self.FIRST_X:
            peer = partner(group, 1)
            source = block.at[:, self.column_half(peer)]
            target = self.got_x.at[self.FIRST_X.index(turn)]
        else:
            peer = partner(group, 2)
            source = block.at[self.row_half(peer), :]
            target = self.got_y.at[turn - 2]
        return remote(
            source, target, self.sems.at[12 + turn], self.sems.at[16 + turn], (peer, 2 * level + core)
        )

    def last_copy(self, turn):
        group, level, core = place()
        block = self.own.at[partner(level, turn)]
        peer = partner(group, 2 if turn in self.FIRST_X else 1)
        rows = self.row_half(peer)
        columns = self.column_half(peer)
        return remote(
            block.at[rows, columns],
            self.got_last.at[turn],
            self.sems.at[20 + turn],
            self.sems.at[24 + turn],
            (peer, 2 * level + core),
        )

    def level_copy(self, turn):
        group, level, core = place()
        target = partner(level, turn)
        return remote(
            self.part.at[target],
            self.got_level.at[turn - 1],
            self.sems.at[27 + turn],
            self.sems.at[30 + turn],
            (group, 2 * target + core),
        )

    def share_copy(self, other):
        group, level, core = place()
        mine = self.out.at[self.row_half(group), self.column_half(group)]
        return remote(
            mine,
            mine,
            self.sems.at[33 + other],
            self.sems.at[36 + other],
            (partner(group, other), 2 * level + core),
        )

    def first(self):
        _, level, _ = place()
        for turn in (*TURNS, 0):
            self.load_away(partner(level, turn)).start()
        for turn in (*TURNS, 0):
            self.load(partner(level, turn)).start()
        for turn in (*TURNS, 0):
            self.load_away(partner(level, turn)).wait()
            self.core_copy(partner(level, turn)).start()

    def second(self):
        _, level, _ = place()
        for turn in (*TURNS, 0):
            target = partner(level, turn)
            self.load(target).wait()
            self.core_copy(target).wait_recv()
            add_rows(
                self.own.at[target], 0, slice(None), self.got_core.at[target], self.rows, self.columns
            )
            self.step_copy(turn).start()

    def between(self):
        group, level, _ = place()
        for turn in (*TURNS, 0):
            block = self.own.at[partner(level, turn)]
            self.step_copy(turn).wait_recv()
            if turn in self.FIRST_X:
                source = self.got_x.at[self.FIRST_X.index(turn)]
                add_rows(block, 0, self.column_half(group), source, self.rows, self.wide)
            else:
                source = self.got_y.at[turn - 2]
                start = lax.div(group, 2) * self.high
                add_rows(block, start, slice(None), source, self.high, self.columns)
            self.last_copy(turn).start()

    def third(self):
        group, level, _ = place()
        start = lax.div(group, 2) * self.high
        columns = self.column_half(group)
        chunk = 16 if self.wide > 1536 else 48
        for turn in (*TURNS, 0):
            target = partner(level, turn)
            self.last_copy(turn).wait_recv()

            def add(step, carry):
                at = pl.multiple_of(step * chunk, chunk)
                rows = pl.ds(at, chunk)
                mine = pl.ds(pl.multiple_of(start + at, 16), chunk)
                total = self.own[target, mine, columns].astype(jnp.float32)
                total = total + self.got_last[turn, rows, :].astype(jnp.float32)
                self.part[target, rows, :] = total.astype(self.part.dtype)
                return carry

            lax.fori_loop(0, self.high // chunk, add, 0)
            if turn and not self.lead:
                self.level_copy(turn).start()

    def fourth(self):
        group, level, _ = place()
        start = lax.div(group, 2) * self.high
        columns = self.column_half(group)
        chunk = 16 if self.wide > 1536 else 48
        for turn in TURNS:
            self.level_copy(turn).wait_recv()

        def add(step, carry):
            at = pl.multiple_of(step * chunk, chunk)
            rows = pl.ds(at, chunk)
            mine = pl.ds(pl.multiple_of(start + at, 16), chunk)
            total = self.part[level, rows, :].astype(jnp.float32)
            for slot in range(3):
                total = total + self.got_level[slot, rows, :].astype(jnp.float32)
            self.out[mine, columns] = total.astype(self.out.dtype)
            return carry

        lax.fori_loop(0, self.high // chunk, add, 0)
        for other in TURNS:
            self.share_copy(other).start()

    def store(self):
        self.target[...] = self.out[...]

    def fifth(self):
        for other in TURNS:
            self.share_copy(other).wait_recv()

    def sixth(self):
        _, level, _ = place()
        for turn in (*TURNS, 0):
            self.core_copy(partner(level, turn)).wait_send()
            self.step_copy(turn).wait_send()
            self.last_copy(turn).wait_send()
            if turn and not self.lead:
                self.level_copy(turn).wait_send()
                self.share_copy(turn).wait_send()


class Lead(Whole):
    lead = True

    def store(self):
        self.target[...] = self.part[...]


class Rest(Whole):
    def __init__(self, part, out, got_level, sems):
        self.part, self.out, self.got_level, self.sems = part, out, got_level, sems
        self.rows, self.columns = out.shape
        self.high, self.wide = self.rows // 2, self.columns // 2

    def first(self):
        for turn in TURNS:
            self.level_copy(turn).start()

    def sixth(self):
        for turn in TURNS:
            self.level_copy(turn).wait_send()
            self.share_copy(turn).wait_send()


GROUP_SEMS = 13


class GroupReduce:
    def __init__(self, share, out, scratch, sems):
        self.share, self.out, self.sems = share, out, sems
        self.own, self.got = scratch
        self.rows, self.columns = out.shape
        self.chunk = 16

    def load(self):
        return pltpu.make_async_copy(self.share, self.own, self.sems.at[0])

    def group_copy(self, other):
        group, level, core = place()
        peer = partner(group, other)
        return remote(
            self.own.at[quarter(peer, self.rows, self.columns)],
            self.got.at[other - 1],
            self.sems.at[other],
            self.sems.at[3 + other],
            (peer, 2 * level + core),
        )

    def share_copy(self, other):
        group, level, core = place()
        mine = self.out.at[quarter(group, self.rows, self.columns)]
        return remote(
            mine,
            mine,
            self.sems.at[6 + other],
            self.sems.at[9 + other],
            (partner(group, other), 2 * level + core),
        )

    def first(self):
        self.load().start()

    def second(self):
        self.load().wait()
        for other in TURNS:
            self.group_copy(other).start()

    def between(self):
        pass

    def third(self):
        group, _, _ = place()
        high, wide = quarter_shape(self.rows, self.columns)
        row_part, column_part = quarter(group, self.rows, self.columns)
        for other in TURNS:
            self.group_copy(other).wait_recv()

        def add(step, carry):
            at = pl.multiple_of(step * self.chunk, self.chunk)
            rows = pl.ds(at, self.chunk)
            mine = pl.ds(pl.multiple_of(row_part.start + at, self.chunk), self.chunk)
            total = self.own[mine, column_part].astype(jnp.float32)
            for slot in range(3):
                total = total + self.got[slot, rows, :].astype(jnp.float32)
            self.out[mine, column_part] = total.astype(self.out.dtype)
            return carry

        lax.fori_loop(0, high // self.chunk, add, 0)
        for other in TURNS:
            self.share_copy(other).start()

    def fourth(self):
        pass

    def fifth(self):
        for other in TURNS:
            self.share_copy(other).wait_recv()

    def store(self):
        self.target[...] = self.out[...]

    def sixth(self):
        for other in TURNS:
            self.group_copy(other).wait_send()
            self.share_copy(other).wait_send()


class Spread:
    def __init__(self, full, sems):
        self.full, self.sems = full, sems

    def level_copy(self, turn):
        group, level, core = place()
        block = self.full.at[2 * level + core]
        peer = (group, 2 * partner(level, turn) + core)
        return remote(block, block, self.sems.at[turn - 1], self.sems.at[2 + turn], peer)

    def core_copy(self, turn):
        group, level, core = place()
        block = self.full.at[2 * partner(level, turn) + core]
        peer = (group, 2 * level + 1 - core)
        return remote(block, block, self.sems.at[6 + turn], self.sems.at[10 + turn], peer)

    def run(self):
        for turn in TURNS:
            self.level_copy(turn).start()
        self.core_copy(0).start()
        for turn in TURNS:
            self.level_copy(turn).wait_recv()
            self.core_copy(turn).start()
        for turn in (0, *TURNS):
            self.core_copy(turn).wait_recv()
        for turn in (0, *TURNS):
            self.core_copy(turn).wait_send()
            if turn:
                self.level_copy(turn).wait_send()


def squares_in(out):
    def add(step, total):
        piece = out[pl.ds(pl.multiple_of(step * 16, 16), 16), :].astype(jnp.float32)
        piece = piece * piece
        for lane in range(0, out.shape[1], LANES):
            total = total + piece[:, lane : lane + LANES]
        return total

    total = lax.fori_loop(0, out.shape[0] // 16, add, jnp.zeros((16, LANES), jnp.float32))
    return jnp.sum(total, 0, keepdims=True)


def run_stages(jobs, stages):
    for stage in stages:
        for job in jobs:
            getattr(job, stage)()


STAGES = ("first", "second", "between", "third", "fourth", "fifth", "sixth")


def whole_scratch(grad):
    _, rows, columns = grad.shape
    high, wide = quarter_shape(rows, columns)
    shapes = (*[(4, rows, columns)] * 3, (3, 4, high, wide), (4, high, wide))
    return [pltpu.VMEM(shape, grad.dtype) for shape in (*shapes, (3, high, wide))]


def stepped_scratch(grad):
    _, rows, columns = grad.shape
    high, wide = rows // 2, columns // 2
    shapes = (
        *[(4, rows, columns)] * 3,
        (2, rows, wide),
        (2, high, columns),
        (4, high, wide),
        (4, high, wide),
        (3, high, wide),
    )
    return [pltpu.VMEM(shape, grad.dtype) for shape in shapes]


def share_scratch(share):
    return [
        pltpu.VMEM(share.shape, share.dtype),
        pltpu.VMEM((3, *quarter_shape(*share.shape)), share.dtype),
    ]


def reduce_kernel(*refs, whole, partly, done, vector_rows, rest_size):
    count = whole + 1 + partly
    finished, grads, refs = refs[:done], refs[done : done + count], refs[done + count :]
    outs, full, numbers, refs = refs[:count], refs[count], refs[count + 1], refs[count + 2 :]
    sems, small_sems, group_sems, spread_sems, refs = *refs[:4], refs[4:]
    jobs = [
        Whole(grads[i], outs[i], refs[8 * i : 8 * i + 8], sems.at[i]) for i in range(whole)
    ]
    refs = refs[8 * whole :]
    small = Reduce(grads[whole], outs[whole], refs[:6], small_sems)
    refs = refs[6:]
    shares = [
        GroupReduce(
            grads[whole + 1 + i], outs[whole + 1 + i], refs[2 * i : 2 * i + 2], group_sems.at[i]
        )
        for i in range(partly)
    ]
    greet()
    run_stages([*jobs, small, *shares], STAGES[:1])
    run_stages([small, *shares], STAGES[1:2])
    run_stages(jobs, STAGES[1:3])
    run_stages([small, *shares], STAGES[3:4])
    run_stages(jobs, STAGES[3:4])
    run_stages([small, *jobs], STAGES[4:5])
    run_stages([*shares, small, *jobs], STAGES[5:6])
    total = sum(squares_in(out) for out in (*finished, *outs[:whole], *outs[whole + 1 :]))
    _, level, core = place()
    mine = 2 * level + core
    block = outs[whole]
    last = block.shape[0] - 1
    full[mine] = block[...]
    full[mine, last : last + 1, :] = total
    Spread(full, spread_sems).run()
    numbers[...] = totals(full[...], vector_rows, rest_size)
    run_stages([*shares, small, *jobs], STAGES[6:])


def transfer_outs(arrays):
    return [jax.ShapeDtypeStruct(array.shape[-2:], array.dtype) for array in arrays]


def reduce_call(grads, small, shares, finished, vector_rows, rest_size, collective_id):
    in_vmem = pl.BlockSpec(memory_space=pltpu.VMEM)
    whole, partly, done = len(grads), len(shares), len(finished)
    operands = [*grads, small, *shares]
    scratch = [
        pltpu.SemaphoreType.DMA((whole, WHOLE_SEMS)),
        pltpu.SemaphoreType.DMA((REDUCE_SEMS,)),
        pltpu.SemaphoreType.DMA((partly, GROUP_SEMS)),
        pltpu.SemaphoreType.DMA((14,)),
    ]
    for grad in grads:
        scratch.extend(stepped_scratch(grad))
    scratch.extend(whole_scratch(small))
    for share in shares:
        scratch.extend(share_scratch(share))
    out_shape = [*transfer_outs(operands), shape_of(*small.shape), shape_of(1, LANES)]
    return pl.pallas_call(
        functools.partial(
            reduce_kernel,
            whole=whole,
            partly=partly,
            done=done,
            vector_rows=vector_rows,
            rest_size=rest_size,
        ),
        in_specs=[in_vmem] * done + [ANYWHERE] * len(operands),
        out_specs=[in_vmem] * len(out_shape),
        out_shape=out_shape,
        scratch_shapes=scratch,
        compiler_params=pltpu.CompilerParams(
            collective_id=collective_id, has_side_effects=True, vmem_limit_bytes=VMEM_LIMIT
        ),
        cost_estimate=NO_COST,
        name="reduce_gradients",
    )(*finished, *operands)


def totals(full, vector_rows, rest_size):
    owners, rows, _ = full.shape
    rest_rows = -(-rest_size // (owners * LANES))
    row = lax.broadcasted_iota(jnp.int32, full.shape, 1)
    spot = row - vector_rows + rest_rows * lax.broadcasted_iota(jnp.int32, full.shape, 0)
    spot = spot * LANES + lax.broadcasted_iota(jnp.int32, full.shape, 2)
    in_rest = (row >= vector_rows) & (row < vector_rows + rest_rows)

    def summed(values):
        return jnp.sum(jnp.sum(jnp.sum(values, 0), 0, keepdims=True), 1, keepdims=True)

    tokens = summed(jnp.where(in_rest & (spot == rest_size - 1), full, 0.0))
    loss = summed(jnp.where(in_rest & (spot == rest_size - 2), full, 0.0))
    kept = (row < vector_rows) | (in_rest & (spot < rest_size - 2))
    squares = jnp.where(kept, full * full, jnp.where(row == rows - 1, full, 0.0))
    norm = jnp.sqrt(summed(squares)) / tokens
    factor = jnp.minimum(1.0, CLIP_NORM / norm) / tokens
    lane = lax.broadcasted_iota(jnp.int32, (1, LANES), 1)
    return jnp.where(
        lane == 0, factor, jnp.where(lane == 1, norm, jnp.where(lane == 2, loss, tokens))
    )


def with_kernels():
    return lax.axis_size("dp") == 4 and lax.axis_size("fsdp") == 8


def reduce_all(grads, small, shares, finished, vector_rows, rest_size, collective_id):
    if with_kernels():
        return reduce_call(grads, small, shares, finished, vector_rows, rest_size, collective_id)
    sums = [lax.psum(scatter(grad), "dp") for grad in grads]
    block = lax.psum(scatter(small), "dp")
    outs = [lax.psum(share, "dp") for share in shares]
    total = sum(jnp.sum(jnp.square(out.astype(jnp.float32))) for out in (*finished, *sums, *outs))
    row = jnp.full((1, LANES), 1.0 / LANES, jnp.float32) * total
    full = lax.all_gather(block.at[-1:].set(row), "fsdp", axis=0)
    return [*sums, block, *outs, full, totals(full, vector_rows, rest_size)]


def scatter(grad):
    return lax.psum_scatter(grad, "fsdp", scatter_dimension=0)


def by_owner(grad, low=jnp.bfloat16):
    owners = lax.axis_size("fsdp")
    return grad.astype(low).reshape(owners, grad.shape[0] // owners, grad.shape[1])


def attention_forward_kernel(
    q_ref, k_ref, v_ref, seg_col_ref, seg_row_ref, out_ref, expo_ref, inv_ref, *, block
):
    rows = q_ref.shape[0]
    lower = lax.broadcasted_iota(jnp.int32, (block, PAIR), 1) < HD
    keys = k_ref[...]
    values = jnp.concatenate([v_ref[...], jnp.ones((rows, PAIR), v_ref.dtype)], 1)
    seg_row = seg_row_ref[...]
    tasks = [(step, head) for step in range(rows // block) for head in range(2)]

    def scores_of(step, head):
        query = q_ref[step * block : (step + 1) * block, :] * jnp.bfloat16(HD**-0.5)
        keep = lower if head == 0 else jnp.logical_not(lower)
        return mul_nt(jnp.where(keep, query, jnp.bfloat16(0)), keys)

    scores = scores_of(*tasks[0])
    outs = []
    for index, (step, head) in enumerate(tasks):
        following = scores_of(*tasks[index + 1]) if index + 1 < len(tasks) else None
        at = slice(step * block, (step + 1) * block)
        scores = jnp.where(seg_col_ref[at, :] == seg_row, scores, MASKED)
        highest = jnp.max(scores, -1, keepdims=True)
        low = jnp.exp(scores - highest).astype(jnp.bfloat16)
        expo_ref[head, at, :] = low
        outs.append(mul(low, values))
        if head:
            inverse = 1.0 / jnp.where(lower, outs[0][:, PAIR:], outs[1][:, PAIR:])
            sums = jnp.where(lower, outs[0][:, :PAIR], outs[1][:, :PAIR])
            out_ref[at, :] = (sums * inverse).astype(jnp.bfloat16)
            inv_ref[at, :] = inverse
            outs = []
        scores = following


def attention_forward(qkv_rows, segment, rides, collective_id):
    rows = qkv_rows.shape[0]
    pairs = HEADS // 2
    wide = lambda base: pl.BlockSpec((rows, PAIR), lambda j, base=base: (0, base + j))
    return block_call(
        functools.partial(attention_forward_kernel, block=min(256, rows)),
        pairs,
        [wide(0), wide(pairs), wide(2 * pairs), fixed(rows, 1), fixed(1, rows)],
        [qkv_rows, qkv_rows, qkv_rows, segment[:, None], segment[None, :]],
        [wide(0), pl.BlockSpec((2, rows, rows), lambda j: (j, 0, 0)), wide(0)],
        [
            shape_of(rows, D, dtype=LOW),
            shape_of(HEADS, rows, rows, dtype=LOW),
            shape_of(rows, D),
        ],
        [],
        "attention_forward",
        work(16 * HEADS * rows * rows * HD, 2 * HEADS * rows * rows + 12 * rows * D),
        rides,
        collective_id,
    )


def attention_backward_kernel(
    q_ref, k_ref, v_ref, expo_ref, inv_ref, out_ref, grad_ref, dqkv_ref, *, block
):
    rows = q_ref.shape[0]
    pair = pl.program_id(0)
    lower = lax.broadcasted_iota(jnp.int32, (block, PAIR), 1) < HD
    keys = k_ref[...]
    values = v_ref[...]
    scale = HD**-0.5
    scaled_grad = (grad_ref[...].astype(jnp.float32) * inv_ref[...]).astype(jnp.bfloat16)
    query = q_ref[...]
    query_t = query.T
    grad_t = scaled_grad.T
    product = scaled_grad.astype(jnp.float32) * out_ref[...].astype(jnp.float32)
    key_t = [None, None]
    value_t = [None, None]
    tasks = [(step, head) for step in range(rows // block) for head in range(2)]

    def probs_grad_of(step, head):
        keep = lower if head == 0 else jnp.logical_not(lower)
        mine = scaled_grad[step * block : (step + 1) * block]
        return mul_nt(jnp.where(keep, mine, jnp.bfloat16(0)), values)

    probs_grad = probs_grad_of(*tasks[0])
    query_parts = []
    for index, (step, head) in enumerate(tasks):
        following = probs_grad_of(*tasks[index + 1]) if index + 1 < len(tasks) else None
        at = slice(step * block, (step + 1) * block)
        lanes = slice(head * HD, (head + 1) * HD)
        keep = lower if head == 0 else jnp.logical_not(lower)
        inner = jnp.sum(jnp.where(keep, product[at], 0.0), -1, keepdims=True)
        low = expo_ref[head, at, :]
        value_part = mul(grad_t[lanes, at], low)
        scores_grad = (low.astype(jnp.float32) * (probs_grad - inner)).astype(jnp.bfloat16)
        query_parts.append(mul(scores_grad, keys))
        key_part = mul(query_t[lanes, at], scores_grad)
        key_t[head] = key_part if step == 0 else key_t[head] + key_part
        value_t[head] = value_part if step == 0 else value_t[head] + value_part
        if head:
            query_grad = jnp.where(lower, query_parts[0], query_parts[1]) * scale
            dqkv_ref[at, pl.ds(pl.multiple_of(pair * PAIR, PAIR), PAIR)] = query_grad.astype(
                jnp.bfloat16
            )
            query_parts = []
        probs_grad = following
    key_grad = (jnp.concatenate(key_t, 0) * scale).T
    value_grad = jnp.concatenate(value_t, 0).T
    dqkv_ref[:, pl.ds(pl.multiple_of(D + pair * PAIR, PAIR), PAIR)] = key_grad.astype(jnp.bfloat16)
    dqkv_ref[:, pl.ds(pl.multiple_of(2 * D + pair * PAIR, PAIR), PAIR)] = value_grad.astype(jnp.bfloat16)


def attention_backward(qkv_rows, expo, inverse, attended, attended_grad, rides, collective_id):
    rows = qkv_rows.shape[0]
    pairs = HEADS // 2
    wide = lambda base: pl.BlockSpec((rows, PAIR), lambda j, base=base: (0, base + j))
    return block_call(
        functools.partial(attention_backward_kernel, block=min(256, rows)),
        pairs,
        [
            wide(0),
            wide(pairs),
            wide(2 * pairs),
            pl.BlockSpec((2, rows, rows), lambda j: (j, 0, 0)),
            wide(0),
            wide(0),
            wide(0),
        ],
        [qkv_rows, qkv_rows, qkv_rows, expo, inverse, attended, attended_grad],
        [fixed(rows, 3 * D)],
        [shape_of(rows, 3 * D, dtype=LOW)],
        [],
        "attention_backward",
        None,
        rides,
        collective_id,
    )


def mul(left, right):
    return jnp.dot(left, right, preferred_element_type=jnp.float32)


def mul_nt(left, right):
    return lax.dot_general(left, right, NT, preferred_element_type=jnp.float32)


def normalized(values):
    center = values - jnp.mean(values, -1, keepdims=True)
    inverse = lax.rsqrt(jnp.mean(center * center, -1, keepdims=True) + NORM_EPS)
    return center * inverse, inverse


def norm_backward(grad, values, gain):
    unit, inverse = normalized(values)
    inner = grad * gain
    mean_inner = jnp.mean(inner, -1, keepdims=True)
    mean_cross = jnp.mean(inner * unit, -1, keepdims=True)
    value_grad = inverse * (inner - mean_inner - unit * mean_cross)
    return value_grad, column_sum(grad * unit), column_sum(grad)


def column_sum(rows):
    return jnp.sum(rows.astype(jnp.float32), 0, keepdims=True)


def at_first(action):
    pl.when(pl.program_id(0) == 0)(action)


def rows_of(block, columns):
    return pl.BlockSpec((block, columns), lambda i: (i, 0))


def fixed(*shape):
    return pl.BlockSpec(shape, lambda i: (0,) * len(shape), pipeline_mode=pl.Buffered(1))


def loads(sources, targets, sems):
    return [
        pltpu.make_async_copy(source, target, sems.at[index])
        for index, (source, target) in enumerate(zip(sources, targets))
    ]


def shape_of(*shape, dtype=jnp.float32):
    return jax.ShapeDtypeStruct(shape, dtype)


def embed_kernel(pixel_ref, weight_ref, pos_ref, table_ref, bias_ref, out_ref):
    position = jnp.dot(
        pos_ref[...], table_ref[...], precision=HIGHEST, preferred_element_type=jnp.float32
    )
    out_ref[...] = mul(pixel_ref[...], weight_ref[...]) + bias_ref[...] + position


def embed(pixels, weight, pos_weights, table, bias):
    rows, depth = pixels.shape
    block = 256
    nodes = pos_weights.shape[1]
    return block_call(
        embed_kernel,
        rows // block,
        [rows_of(block, depth), fixed(depth, D), rows_of(block, nodes), fixed(nodes, D), fixed(1, D)],
        [pixels, weight, pos_weights, table, bias],
        [rows_of(block, D)],
        [shape_of(rows, D)],
        [],
        "embed",
        work(2 * rows * depth * D, 2 * rows * depth + 2 * depth * D + 4 * rows * D),
    )[0]


def chunk_at(base):
    return pl.ds(pl.multiple_of(base + pl.program_id(0) * D, LANES), D)


def columns_of(rows):
    return pl.BlockSpec((rows, D), lambda i: (0, i))


def halves_of(rows):
    half = rows // 2
    return [slice(start, start + half) for start in range(0, rows, half)]


def at_last(action):
    pl.when(pl.program_id(0) == pl.num_programs(0) - 1)(action)


def qkv_kernel(stream_ref, weight_ref, vector_ref, normed_out, qkv_ref, normed_ref, sem):
    copy = pltpu.make_async_copy(normed_ref, normed_out, sem)

    @at_first
    def _():
        unit, _ = normalized(stream_ref[...])
        normed_ref[...] = (unit * vector_ref[:, :D] + vector_ref[:, D : 2 * D]).astype(LOW)
        copy.start()

    bias = vector_ref[:, chunk_at(4 * D)]
    for half in halves_of(stream_ref.shape[0]):
        qkv_ref[half, :] = (mul(normed_ref[half, :], weight_ref[...]) + bias).astype(LOW)
    at_last(copy.wait)


def qkv_forward(stream, weight, vector):
    rows = stream.shape[0]
    return block_call(
        qkv_kernel,
        3,
        [fixed(rows, D), columns_of(D), fixed(1, vector.shape[1])],
        [stream, weight, vector],
        [ANYWHERE, columns_of(rows)],
        [shape_of(rows, D, dtype=LOW), shape_of(rows, 3 * D, dtype=LOW)],
        [pltpu.VMEM((rows, D), LOW), pltpu.SemaphoreType.DMA],
        "qkv_forward",
        work(6 * rows * D * D, 14 * rows * D + 6 * D * D),
    )


def mlp_kernel(
    stream_ref, attended_ref, mix_ref, up_ref, down_ref, vector_ref,
    residual_out, normed_out, active_ref, slope_ref, out_ref,
    residual_ref, normed_ref, sems,
):
    rows = stream_ref.shape[0]
    copies = loads((residual_ref, normed_ref), (residual_out, normed_out), sems)

    @at_first
    def _():
        for half in halves_of(rows):
            residual = stream_ref[half, :] + mul(attended_ref[half, :], mix_ref[...])
            residual = residual + vector_ref[:, 7 * D : 8 * D]
            residual_ref[half, :] = residual
            unit, _ = normalized(residual)
            normed = unit * vector_ref[:, 2 * D : 3 * D] + vector_ref[:, 3 * D : 4 * D]
            normed_ref[half, :] = normed.astype(LOW)
            out_ref[half, :] = residual + vector_ref[:, 8 * D : 9 * D]
        for copy in copies:
            copy.start()

    bias = vector_ref[:, chunk_at(9 * D)]
    parts = halves_of(rows)
    hidden = mul(normed_ref[parts[0], :], up_ref[...]) + bias
    for index, half in enumerate(parts):
        following = None
        if index + 1 < len(parts):
            following = mul(normed_ref[parts[index + 1], :], up_ref[...]) + bias
        square = hidden * hidden
        rise = 0.5 + 0.5 * jnp.tanh(hidden * (ROOT + (ROOT * CUBE) * square))
        active = hidden * rise
        active_low = active.astype(LOW)
        active_ref[half, :] = active_low
        bend = (2.0 * ROOT) + (6.0 * ROOT * CUBE) * square
        slope_ref[half, :] = (rise + active * (1.0 - rise) * bend).astype(LOW)
        out_ref[half, :] += mul(active_low, down_ref[...])
        hidden = following

    @at_last
    def _():
        for copy in copies:
            copy.wait()


def mlp_specs(up, proj_out):
    return (
        [fixed(D, D), columns_of(D), pl.BlockSpec((D, D), lambda i: (i + 1, 0))],
        [proj_out, up, proj_out],
    )


def mlp_forward(stream, attended, up, proj_out, vector):
    rows = stream.shape[0]
    width = up.shape[1]
    weight_specs, weights = mlp_specs(up, proj_out)
    return block_call(
        mlp_kernel,
        width // D,
        [fixed(rows, D), fixed(rows, D), *weight_specs, fixed(1, vector.shape[1])],
        [stream, attended, *weights, vector],
        [ANYWHERE, ANYWHERE, columns_of(rows), columns_of(rows), fixed(rows, D)],
        [
            shape_of(rows, D),
            shape_of(rows, D, dtype=LOW),
            shape_of(rows, width, dtype=LOW),
            shape_of(rows, width, dtype=LOW),
            shape_of(rows, D),
        ],
        [
            pltpu.VMEM((rows, D), jnp.float32),
            pltpu.VMEM((rows, D), LOW),
            pltpu.SemaphoreType.DMA((2,)),
        ],
        "mlp_forward",
        work(2 * rows * D * (D + 2 * width), rows * (16 * D + 4 * width) + 2 * D * (D + 2 * width)),
    )


def mlp_back_kernel(
    grad_ref, slope_ref, residual_in, normed_ref, active_ref, attended_ref, mix_ref, up_ref, down_ref, vector_ref,
    out_ref, attended_grad_ref, sums_ref, output_grad, *refs,
):
    up_grads, scratch = refs[:-7], refs[-7:]
    residual_ref, low_ref, second_ref, turned_ref, hidden_ref, product_ref, sems = scratch
    rows = grad_ref.shape[0]
    step = pl.program_id(0)
    load = pltpu.make_async_copy(residual_in, residual_ref, sems.at[0])

    def store_copy(slot):
        rows_at = pl.ds(pl.multiple_of(slot * D, D), D)
        return pltpu.make_async_copy(
            product_ref.at[slot], output_grad.at[rows_at], sems.at[1 + slot]
        )

    def store(slot, product):
        product_ref[slot] = product.astype(LOW)
        store_copy(slot).start()

    @at_first
    def _():
        load.start()
        low_ref[...] = grad_ref[...].astype(LOW)
        turned_ref[...] = normed_ref[...].T
        second_ref[...] = jnp.zeros_like(second_ref)

    parts = halves_of(rows)
    active_grad = mul_nt(low_ref[parts[0], :], down_ref[...])
    hidden_sum = 0.0
    for index, half in enumerate(parts):
        following = None
        if index + 1 < len(parts):
            following = mul_nt(low_ref[parts[index + 1], :], down_ref[...])
        hidden_grad = (active_grad * slope_ref[half, :].astype(jnp.float32)).astype(LOW)
        hidden_ref[half, :] = hidden_grad
        hidden_sum = hidden_sum + column_sum(hidden_grad)
        second_ref[half, :] += mul_nt(hidden_grad, up_ref[...])
        active_grad = following
    sums_ref[:, chunk_at(4 * D)] = hidden_sum
    store(step + 1, mul(active_ref[...].T, low_ref[...]))
    up_grad = mul(turned_ref[...], hidden_ref[...]).astype(LOW)
    share = pl.num_programs(0) // len(up_grads)
    for index, part in enumerate(up_grads):

        @pl.when(lax.div(step, share) == index)
        def _(part=part):
            part[...] = up_grad

    @at_last
    def _():
        load.wait()
        gain = vector_ref[:, 2 * D : 3 * D]
        totals = [0.0] * 4
        for half in halves_of(rows):
            grad = grad_ref[half, :]
            value_grad, gain_grad, shift_grad = norm_backward(
                second_ref[half, :], residual_ref[half, :], gain
            )
            total = value_grad + grad
            out_ref[half, :] = total
            total_low = total.astype(LOW)
            hidden_ref[half, :] = total_low
            attended_grad_ref[half, :] = mul_nt(total_low, mix_ref[...]).astype(LOW)
            new = (gain_grad, shift_grad, column_sum(total_low), column_sum(low_ref[half, :]))
            totals = [old + part for old, part in zip(totals, new)]
        sums_ref[:, : 4 * D] = jnp.concatenate(totals, 1)
        store(0, mul(attended_ref[...].T, hidden_ref[...]))
        for slot in range(product_ref.shape[0]):
            store_copy(slot).wait()


def mlp_backward(
    grad, slope, residual, normed, active, attended, up, proj_out, vector, parts, rides, collective_id
):
    rows = grad.shape[0]
    width = up.shape[1]
    steps = width // D
    share = steps // parts
    part_of = lambda index: lambda i: (0, jnp.clip(i - index * share, 0, share - 1))
    whole = fixed(rows, D)
    weight_specs, weights = mlp_specs(up, proj_out)
    return block_call(
        mlp_back_kernel,
        steps,
        [
            whole,
            columns_of(rows),
            ANYWHERE,
            whole,
            columns_of(rows),
            whole,
            *weight_specs,
            fixed(1, vector.shape[1]),
        ],
        [grad, slope, residual, normed, active, attended, *weights, vector],
        [whole, whole, fixed(1, 4 * D + width), ANYWHERE, *[pl.BlockSpec((D, D), part_of(index)) for index in range(parts)]],
        [
            shape_of(rows, D),
            shape_of(rows, D, dtype=LOW),
            shape_of(1, 4 * D + width),
            shape_of(D + width, D, dtype=LOW),
            *[shape_of(D, width // parts, dtype=LOW)] * parts,
        ],
        [
            pltpu.VMEM((rows, D), jnp.float32),
            pltpu.VMEM((rows, D), LOW),
            pltpu.VMEM((rows, D), jnp.float32),
            pltpu.VMEM((D, rows), LOW),
            pltpu.VMEM((rows, D), LOW),
            pltpu.VMEM((steps + 1, D, D), LOW),
            pltpu.SemaphoreType.DMA((steps + 2,)),
        ],
        "mlp_backward",
        None,
        rides,
        collective_id,
    )


def qkv_back_kernel(
    grad_ref, residual_in, stream_in, normed_ref, weight_ref, vector_ref,
    out_ref, sums_ref, weight_grad_ref,
    residual_ref, stream_ref, sum_ref, turned_ref, sems,
):
    rows = out_ref.shape[0]
    copies = loads((residual_in, stream_in), (residual_ref, stream_ref), sems)

    @at_first
    def _():
        for copy in copies:
            copy.start()
        turned_ref[...] = normed_ref[...].T
        sum_ref[...] = jnp.zeros_like(sum_ref)

    for half in halves_of(rows):
        sum_ref[half, :] += mul_nt(grad_ref[half, :], weight_ref[...])
    sums_ref[:, chunk_at(2 * D)] = column_sum(grad_ref[...])
    weight_grad_ref[...] = mul(turned_ref[...], grad_ref[...]).astype(LOW)

    @at_last
    def _():
        for copy in copies:
            copy.wait()
        totals = [0.0] * 2
        for half in halves_of(rows):
            value_grad, gain_grad, shift_grad = norm_backward(
                sum_ref[half, :], stream_ref[half, :], vector_ref[:, :D]
            )
            out_ref[half, :] = residual_ref[half, :] + value_grad
            totals = [totals[0] + gain_grad, totals[1] + shift_grad]
        sums_ref[:, : 2 * D] = jnp.concatenate(totals, 1)


def qkv_backward(grad, residual_grad, stream, normed, weight, vector, rides, collective_id):
    rows = stream.shape[0]
    whole = fixed(rows, D)
    return block_call(
        qkv_back_kernel,
        3,
        [columns_of(rows), ANYWHERE, ANYWHERE, whole, columns_of(D), fixed(1, vector.shape[1])],
        [grad, residual_grad, stream, normed, weight, vector],
        [whole, fixed(1, 5 * D), columns_of(D)],
        [shape_of(rows, D), shape_of(1, 5 * D), shape_of(D, 3 * D, dtype=LOW)],
        [
            pltpu.VMEM((rows, D), jnp.float32),
            pltpu.VMEM((rows, D), jnp.float32),
            pltpu.VMEM((rows, D), jnp.float32),
            pltpu.VMEM((D, rows), LOW),
            pltpu.SemaphoreType.DMA((2,)),
        ],
        "qkv_backward",
        None,
        rides,
        collective_id,
    )


def embed_back_kernel(pixel_ref, grad_ref, pos_ref, out_ref, table_ref, bias_ref, low_ref):
    @at_first
    def _():
        grad = grad_ref[...]
        low = grad.astype(jnp.bfloat16)
        low_ref[...] = low
        bias_ref[...] = column_sum(low)
        table_ref[...] = jnp.dot(
            pos_ref[...], grad, precision=HIGHEST, preferred_element_type=jnp.float32
        )

    out_ref[...] = mul(pixel_ref[...].T, low_ref[...]).astype(jnp.bfloat16)


def embed_backward(pixels, grad, pos_weights_t):
    rows, depth = pixels.shape
    block = 768
    nodes = pos_weights_t.shape[0]
    return block_call(
        embed_back_kernel,
        depth // block,
        [pl.BlockSpec((rows, block), lambda i: (0, i)), fixed(rows, D), fixed(nodes, rows)],
        [pixels, grad, pos_weights_t],
        [rows_of(block, D), fixed(nodes, D), fixed(1, D)],
        [shape_of(depth, D, dtype=jnp.bfloat16), shape_of(nodes, D), shape_of(1, D)],
        [pltpu.VMEM((rows, D), jnp.bfloat16)],
        "embed_backward",
        None,
    )


def head_kernel(
    stream_ref, seg_col_ref, seg_row_ref, label_ref, weight_ref, vector_ref,
    grad_ref, weight_grad_ref, sums_ref, bias_grad_ref, numbers_ref, *, classes,
):
    padded = weight_ref.shape[1]
    vector = vector_ref[...].astype(LOW).astype(jnp.float32)
    gain, shift = vector[:, D : 2 * D], vector[:, 2 * D : 3 * D]
    slots = lax.broadcasted_iota(jnp.int32, (IMGS, 1), 0)
    member = (seg_row_ref[...] == slots).astype(jnp.float32)
    counts = jnp.sum(member, 1, keepdims=True)
    sizes = jnp.maximum(counts, 1.0)
    unit, inverse = normalized(stream_ref[...])
    final = unit * gain + shift
    owner = jnp.broadcast_to(seg_col_ref[...], final.shape)
    pooled = [jnp.sum(jnp.where(owner == k, final, 0.0), 0, keepdims=True) for k in range(IMGS)]
    pooled = (jnp.concatenate(pooled, 0) / sizes).astype(LOW)
    class_at = lax.broadcasted_iota(jnp.int32, (IMGS, padded), 1)
    logits = mul(pooled, weight_ref[...]) + vector[:, 3 * D :]
    logits = jnp.where(class_at < classes, logits, MASKED)
    highest = jnp.max(logits, -1, keepdims=True)
    exponent = jnp.exp(logits - highest)
    totals = jnp.sum(exponent, -1, keepdims=True)
    onehot = class_at == label_ref[...]
    picked = jnp.sum(jnp.where(onehot, logits, 0.0), 1, keepdims=True)
    loss = jnp.sum(counts * (highest + jnp.log(totals) - picked), 0, keepdims=True)
    numbers_ref[...] = jnp.concatenate([loss, jnp.sum(counts, 0, keepdims=True)], 1)
    logits_grad = ((exponent / totals - onehot.astype(jnp.float32)) * counts).astype(LOW)
    bias_grad_ref[...] = column_sum(logits_grad)
    weight_grad_ref[...] = lax.dot_general(
        pooled, logits_grad, (((0,), (0,)), ((), ())), preferred_element_type=jnp.float32
    ).astype(LOW)
    pooled_grad = mul_nt(logits_grad, weight_ref[...]) / sizes
    own = (seg_col_ref[...] == lax.broadcasted_iota(jnp.int32, (1, IMGS), 1)).astype(LOW)
    final_grad, left = 0.0, pooled_grad
    for _ in range(3):
        term = left.astype(LOW)
        final_grad = final_grad + mul(own, term)
        left = left - term.astype(jnp.float32)
    inner = final_grad * gain
    mean_inner = jnp.mean(inner, -1, keepdims=True)
    mean_cross = jnp.mean(inner * unit, -1, keepdims=True)
    grad_ref[...] = inverse * (inner - mean_inner - unit * mean_cross)
    sums_ref[...] = jnp.concatenate([column_sum(final_grad * unit), column_sum(final_grad)], 1)


def head(stream, segment, labels, weight, global_vector, classes):
    rows = stream.shape[0]
    padded = weight.shape[1]
    vector = jnp.pad(global_vector, (0, padded - classes))[None, :]
    return pl.pallas_call(
        functools.partial(head_kernel, classes=classes),
        out_shape=[
            shape_of(rows, D),
            shape_of(D, padded, dtype=LOW),
            shape_of(1, 2 * D),
            shape_of(1, padded),
            shape_of(1, 2),
        ],
        compiler_params=pltpu.CompilerParams(vmem_limit_bytes=VMEM_LIMIT),
        cost_estimate=NO_COST,
        name="head",
    )(stream, segment[:, None], segment[None, :], labels.reshape(IMGS, 1), weight, vector)


def adam_update(gradient, moment, square, weight, factor, learn_rate):
    clipped = gradient * factor
    moment = BETA_ONE * moment + (1.0 - BETA_ONE) * clipped
    square = BETA_TWO * square + (1.0 - BETA_TWO) * clipped * clipped
    fixed_one = 1.0 - BETA_ONE**STEP
    fixed_two = 1.0 - BETA_TWO**STEP
    step_dir = (
        moment / fixed_one / (jnp.sqrt(square / fixed_two) + ADAM_EPS) + WEIGHT_DECAY * weight
    )
    return (moment, square, weight - learn_rate * step_dir)


def body(
    pixels,
    segment,
    patch_size,
    labels,
    patch_kernel,
    head_weight,
    input_proj,
    output_proj,
    layer_vector,
    position_table,
    global_vector,
    patch_moment,
    head_moment,
    input_moment,
    output_moment,
    layer_moment,
    position_moment,
    global_moment,
    patch_square,
    head_square,
    input_square,
    output_square,
    layer_square,
    position_square,
    global_square,
):
    owners = lax.axis_size("fsdp")
    nodes = position_table.shape[0]
    vector_size = layer_vector.size
    stream, pos_weights_t, vectors, qkv_weight, up_zero, rides, rest_shards, first_rows = begin(
        pixels,
        segment,
        patch_size,
        patch_kernel,
        layer_vector,
        input_proj,
        output_proj,
        head_weight,
        position_table,
        global_vector,
    )
    qkv_one, up_one, head_full = (
        lax.all_gather(shard, "fsdp", axis=0, tiled=True) for shard in rest_shards
    )
    saved_layers = []
    for index in range(LAYERS):
        vector = vectors[index]
        if index:
            normed, qkv_rows = qkv_forward(stream, qkv_weight, vector)
        else:
            normed, qkv_rows = first_rows
        if index == 0:
            attended, expo, inverse, output, output_ride = attention_forward(
                qkv_rows, segment, rides, 4
            )
            up = up_zero
        else:
            attended, expo, inverse, output = attention_forward(qkv_rows, segment, [output_ride], 5)
            up = up_one
        residual, normed_second, active, slope, following = mlp_forward(
            stream, attended, up, output, vector
        )
        saved_layers.append(
            (
                (qkv_weight, up, output, vector),
                (stream, normed, qkv_rows, attended, expo, inverse),
                (residual, normed_second, active, slope),
            )
        )
        stream, qkv_weight = following, qkv_one
    stream_grad, head_grad, final_sums, head_bias_grad, numbers = head(
        stream, segment, labels, head_full, global_vector, head_weight.shape[1]
    )
    vector_grads = [None] * LAYERS
    for index in reversed(range(LAYERS)):
        (qkv_weight, up, output, vector), first, second = saved_layers[index]
        entering, normed, qkv_rows, attended, expo, inverse = first
        residual, normed_second, active, slope = second
        residual_grad, attended_grad, mlp_sums, output_grad, *brought = mlp_backward(
            stream_grad,
            slope,
            residual,
            normed_second,
            active,
            attended,
            up,
            output,
            vector,
            2 if index else 1,
            [SumRide(by_owner(head_grad), False) if index else output_rest],
            10 if index else 9,
        )
        if index:
            *up_parts, head_sum = brought
            attended_grad, *up_parts = lax.optimization_barrier((attended_grad, *up_parts))
            one_parts = [scatter(by_owner(part)) for part in up_parts]
        else:
            up_grad, output_one_sum = brought
            attended_grad, output_grad = lax.optimization_barrier((attended_grad, output_grad))
            output_zero_part = scatter(by_owner(output_grad))
        qkv_grad, rest = attention_backward(
            qkv_rows,
            expo,
            inverse,
            attended,
            attended_grad,
            [LeadRide(by_owner(output_grad if index else up_grad))],
            6 if index else 8,
        )
        stream_grad, qkv_sums, qkv_weight_grad, *brought = qkv_backward(
            qkv_grad,
            residual_grad,
            entering,
            normed,
            qkv_weight,
            vector,
            () if index else [rest, *[ShareRide(part) for part in one_parts]],
            7,
        )
        if index:
            output_rest = rest
            stream_grad, qkv_weight_grad = lax.optimization_barrier((stream_grad, qkv_weight_grad))
            one_parts.append(scatter(by_owner(qkv_weight_grad)))
        else:
            up_zero_sum, *up_one_sums, qkv_one_sum = brought
        vector_grads[index] = jnp.concatenate(
            [
                qkv_sums[0, : 2 * D],
                mlp_sums[0, : 2 * D],
                qkv_sums[0, 2 * D :],
                mlp_sums[0, 2 * D :],
            ]
        )
    kernel_grad, position_grad, bias_grad = embed_backward(pixels, stream_grad, pos_weights_t)
    position_grad = position_grad[:nodes]
    vector_part = jnp.stack(vector_grads).reshape(LAYERS, owners, -1)
    vector_part = jnp.swapaxes(vector_part, 0, 1).reshape(owners, vector_size)
    vector_rows = -(-vector_size // LANES)
    vector_part = jnp.pad(vector_part, ((0, 0), (0, vector_rows * LANES - vector_size)))
    rest = jnp.concatenate(
        [
            position_grad.reshape(-1),
            bias_grad[0],
            final_sums[0],
            head_bias_grad[0, :CLS],
            numbers[0],
        ]
    )
    rest_rows = -(-rest.shape[0] // (owners * LANES))
    rest_part = jnp.pad(rest, (0, rest_rows * owners * LANES - rest.shape[0]))
    small = jnp.concatenate([vector_part, rest_part.reshape(owners, -1)], 1)
    used = vector_rows + rest_rows
    block_rows = (used // 64 + 1) * 64
    small = jnp.pad(small.reshape(owners, used, LANES), ((0, 0), (0, block_rows - used), (0, 0)))
    (
        qkv_zero_sum,
        kernel_sum,
        small_share,
        output_zero_sum,
        small_full,
        numbers,
    ) = reduce_all(
        [by_owner(qkv_weight_grad), by_owner(kernel_grad)],
        small,
        [output_zero_part],
        [head_sum, output_one_sum, up_zero_sum, *up_one_sums, qkv_one_sum],
        vector_rows,
        rest.shape[0],
        2,
    )
    factor, grad_norm, loss_sum, token_total = (numbers[0, index] for index in range(4))
    rest_sum = small_full[:, vector_rows:used].reshape(-1)
    position_sum = rest_sum[: position_grad.size].reshape(position_grad.shape)
    global_sum = rest_sum[position_grad.size :][: global_vector.shape[0]]
    kernel_sum = kernel_sum.astype(jnp.float32)
    head_sum = head_sum[:, :CLS].astype(jnp.float32)
    input_sum = jnp.stack(
        [
            jnp.concatenate(parts, 1)
            for parts in ((qkv_zero_sum, up_zero_sum), (qkv_one_sum, *up_one_sums))
        ]
    ).astype(jnp.float32)
    output_sum = jnp.stack([output_zero_sum, output_one_sum]).astype(
        jnp.float32
    )
    vector_sum = small_share[:vector_rows].reshape(-1)[:vector_size].reshape(layer_vector.shape)
    patch_next = adam_update(
        kernel_sum, patch_moment, patch_square, patch_kernel, factor, LEARN_RATE
    )
    head_next = adam_update(head_sum, head_moment, head_square, head_weight, factor, LEARN_RATE)
    input_next = adam_update(input_sum, input_moment, input_square, input_proj, factor, LEARN_RATE)
    output_next = adam_update(
        output_sum, output_moment, output_square, output_proj, factor, LEARN_RATE
    )
    layer_next = adam_update(
        vector_sum, layer_moment, layer_square, layer_vector, factor, VECTOR_RATE
    )
    position_next = adam_update(
        position_sum, position_moment, position_square, position_table, factor, LEARN_RATE
    )
    global_next = adam_update(
        global_sum, global_moment, global_square, global_vector, factor, VECTOR_RATE
    )
    return (
        loss_sum,
        token_total,
        grad_norm,
        patch_next[0],
        head_next[0],
        input_next[0],
        output_next[0],
        layer_next[0],
        position_next[0],
        global_next[0],
        patch_next[1],
        head_next[1],
        input_next[1],
        output_next[1],
        layer_next[1],
        position_next[1],
        global_next[1],
        patch_next[2],
        head_next[2],
        input_next[2],
        output_next[2],
        layer_next[2],
        position_next[2],
        global_next[2],
    )


def solution(mesh):
    in_specs = (
        P(("dp", "fsdp"), None),
        P(("dp", "fsdp")),
        P(("dp", "fsdp"), None),
        P(("dp", "fsdp"), None),
        P("fsdp", None),
        P("fsdp", None),
        P(None, "fsdp", None),
        P(None, "fsdp", None),
        P(None, "fsdp"),
        P(),
        P(),
        P("fsdp", None),
        P("fsdp", None),
        P(None, "fsdp", None),
        P(None, "fsdp", None),
        P(None, "fsdp"),
        P(),
        P(),
        P("fsdp", None),
        P("fsdp", None),
        P(None, "fsdp", None),
        P(None, "fsdp", None),
        P(None, "fsdp"),
        P(),
        P(),
    )
    out_specs = (
        P(),
        P(),
        P(),
        P("fsdp", None),
        P("fsdp", None),
        P(None, "fsdp", None),
        P(None, "fsdp", None),
        P(None, "fsdp"),
        P(),
        P(),
        P("fsdp", None),
        P("fsdp", None),
        P(None, "fsdp", None),
        P(None, "fsdp", None),
        P(None, "fsdp"),
        P(),
        P(),
        P("fsdp", None),
        P("fsdp", None),
        P(None, "fsdp", None),
        P(None, "fsdp", None),
        P(None, "fsdp"),
        P(),
        P(),
    )
    return jax.shard_map(body, mesh=mesh, in_specs=in_specs, out_specs=out_specs, check_vma=False)
```

```python
import functools

import jax
import jax.numpy as jnp
from jax import lax
from jax.experimental import pallas as pl
from jax.experimental.pallas import tpu as pltpu
from jax.sharding import PartitionSpec as P

D = 768
HEADS = 12
HD = 64
CLS = 1000
GRID = 7
IMG = 240
IMGS = 8
LAYERS = 2
STEP = 3


NORM_EPS = 1e-06
CLIP_NORM = 0.01
LEARN_RATE = 0.05
VECTOR_RATE = 0.25
BETA_ONE = 0.5
BETA_TWO = 0.5
ADAM_EPS = 1e-08
WEIGHT_DECAY = 0.05
HIGHEST = lax.Precision.HIGHEST

PAIR = 2 * HD
MASKED = -1e30
MIB = 1024 * 1024
VMEM_LIMIT = 56 * MIB
MESH = pl.DeviceIdType.MESH
LANES = 128
LOW = jnp.bfloat16
ANYWHERE = pl.BlockSpec(memory_space=pl.ANY)
NO_COST = pl.CostEstimate(flops=0, bytes_accessed=0, transcendentals=0)
ROOT = 0.7978845608028654
CUBE = 0.044715
NT = (((1,), (1,)), ((), ()))


def layer_norm(values, gain, shift):
    center = values - jnp.mean(values, -1, keepdims=True)
    spread = jnp.mean(center * center, -1, keepdims=True)
    return center * lax.rsqrt(spread + NORM_EPS) * gain + shift


def rounded(values):
    return lax.optimization_barrier(values.astype(jnp.bfloat16)).astype(jnp.float32)


def matmul(left, right):
    return jnp.dot(left, right, preferred_element_type=jnp.float32)


def padded_rows(flat, multiple):
    extra = -flat.shape[0] % (multiple * LANES)
    return jnp.pad(flat, (0, extra)).reshape(-1, LANES)


def row_layout(seg_row, patch_row):
    row_count = seg_row.shape[0]
    slots = jnp.arange(IMGS, dtype=jnp.int32)
    member = seg_row[:, None] == slots[None, :]
    counts = jnp.sum(member.astype(jnp.int32), 0, dtype=jnp.int32)
    starts = jnp.cumsum(counts, dtype=jnp.int32) - counts
    inside = jnp.any(member, 1)
    offset = jnp.arange(row_count, dtype=jnp.int32) - jnp.sum(
        jnp.where(member, starts[None, :], 0), 1, dtype=jnp.int32
    )
    offset = jnp.where(inside, offset, 0)
    patch_tok = jnp.sum(jnp.where(member, patch_row[None, :], 0), 1, dtype=jnp.int32) + jnp.where(
        inside, 0, IMG
    )
    side = IMG // patch_tok
    nodes = jnp.arange(GRID, dtype=jnp.int32).astype(jnp.float32)

    def hat(coord):
        place = ((2 * coord + 1) * GRID).astype(jnp.float32) / (2 * side).astype(jnp.float32) - 0.5
        place = jnp.clip(place, 0.0, GRID - 1.0)
        return jnp.maximum(1.0 - jnp.abs(place[:, None] - nodes[None, :]), 0.0)

    weights = (hat(offset // side)[:, :, None] * hat(offset % side)[:, None, :]).reshape(
        row_count, GRID * GRID
    )
    return (weights, member.astype(jnp.float32), counts.astype(jnp.float32))


TURNS = (1, 2, 3)


def place():
    slot = lax.axis_index("fsdp")
    return lax.axis_index("dp"), lax.div(slot, 2), lax.rem(slot, 2)


def partner(index, turn):
    if turn == 0:
        return index
    if turn == 1:
        return index + 1 - 2 * lax.rem(index, 2)
    if turn == 2:
        return lax.rem(index + 2, 4)
    return 3 - index


def greet():
    group, level, core = place()
    barrier = pltpu.get_barrier_semaphore()
    peers = [(group, 2 * level + 1 - core)]
    for turn in TURNS:
        peers.append((group, 2 * partner(level, turn) + core))
        peers.append((partner(group, turn), 2 * level + core))
    for peer in peers:
        pl.semaphore_signal(barrier, inc=1, device_id=peer, device_id_type=MESH)
    pl.semaphore_wait(barrier, len(peers))


def quarter_shape(rows, columns):
    if columns % (2 * LANES) == 0:
        return rows // 2, columns // 2
    return rows // 4, columns


def quarter(index, rows, columns):
    high, wide = quarter_shape(rows, columns)
    if wide == columns:
        return pl.ds(pl.multiple_of(index * high, high), high), pl.ds(0, columns)
    return (
        pl.ds(pl.multiple_of(lax.div(index, 2) * high, high), high),
        pl.ds(pl.multiple_of(lax.rem(index, 2) * wide, wide), wide),
    )


def remote(source, target, send, receive, device):
    return pltpu.make_async_remote_copy(
        src_ref=source,
        dst_ref=target,
        send_sem=send,
        recv_sem=receive,
        device_id=device,
        device_id_type=MESH,
    )


GATHER_SEMS = 39


def relay_rows(part, rows):
    cut = -(-rows // 32) * 16
    return (0, cut) if part == 0 else (cut, rows - cut)


class Relay:
    def region(self, turn, index):
        _, level, core = place()
        block = self.out.at[2 * partner(level, turn) + core]
        return block.at[quarter(index, *self.shard.shape)]

    def group_copy(self, turn, other):
        group, level, core = place()
        index = self.group_at + 2 * (turn - 1) + other - 1
        peer = (partner(group, other), 2 * level + core)
        target = self.region(turn, group)
        source = self.quarter_source(turn, target)
        return remote(source, target, self.sems.at[index], self.sems.at[index + 6], peer)

    def relay_copy(self, turn, part):
        group, level, core = place()
        first, count = relay_rows(part, quarter_shape(*self.shard.shape)[0])
        block = self.region(turn, partner(group, 1 + part)).at[pl.ds(first, count)]
        index = self.relay_at + 2 * (turn - 1) + part
        peer = (partner(group, 2 - part), 2 * level + core)
        return remote(block, block, self.sems.at[index], self.sems.at[index + 6], peer)

    def relay(self):
        for turn in TURNS:
            for part in range(2):
                self.group_copy(turn, 1 + part).wait_recv()
                self.relay_copy(turn, part).start()

    def wait_quarters(self, turn):
        for part in range(2):
            self.relay_copy(turn, part).wait_recv()

    def wait_passed(self):
        for turn in TURNS:
            for part in range(2):
                self.group_copy(turn, 1 + part).wait_send()
                self.relay_copy(turn, part).wait_send()


class Gather(Relay):
    group_at, relay_at = 7, 19

    def __init__(self, shard, out, sems, split, in_place=False):
        self.shard, self.out, self.sems, self.split = shard, out, sems, split
        self.in_place = in_place
        self.rows, self.columns = shard.shape

    def quarter_source(self, turn, target):
        return target

    def level_copy(self, turn):
        group, level, core = place()
        block = self.out.at[2 * level + core]
        source = self.shard
        if self.split:
            part = quarter(group, self.rows, self.columns)
            source, block = source.at[part], block.at[part]
        peer = (group, 2 * partner(level, turn) + core)
        return remote(source, block, self.sems.at[turn], self.sems.at[3 + turn], peer)

    def core_copy(self, turn):
        group, level, core = place()
        slot = 2 * partner(level, turn) + core
        source = self.shard if turn == 0 else self.out.at[slot]
        peer = (group, 2 * level + 1 - core)
        return remote(source, self.out.at[slot], self.sems.at[31 + turn], self.sems.at[35 + turn], peer)

    def own_copy(self):
        _, level, core = place()
        return pltpu.make_async_copy(self.shard, self.out.at[2 * level + core], self.sems.at[0])

    def first(self):
        for turn in TURNS:
            self.level_copy(turn).start()
        self.core_copy(0).start()
        if not self.in_place:
            self.own_copy().start()

    def second(self):
        for turn in TURNS:
            self.level_copy(turn).wait_recv()
            if self.split:
                for other in (1, 2):
                    self.group_copy(turn, other).start()
            else:
                self.core_copy(turn).start()

    def third(self, use=None):
        for turn in TURNS if self.split else ():
            self.wait_quarters(turn)
            self.core_copy(turn).start()
            if use is not None:
                use(turn, True)

    def fourth(self, use=None):
        for turn in TURNS if use is not None else (0, *TURNS):
            self.core_copy(turn).wait_recv()
            if use is not None:
                use(turn, False)
        for turn in TURNS:
            self.level_copy(turn).wait_send()
        if self.split:
            self.wait_passed()
        for turn in (0, *TURNS):
            self.core_copy(turn).wait_send()
        if not self.in_place:
            self.own_copy().wait()


class LevelGather:
    def __init__(self, shard, out, sems):
        self.shard, self.out, self.sems = shard, out, sems

    def level_copy(self, turn):
        group, level, core = place()
        return remote(
            self.shard.at[quarter(group, *self.shard.shape)],
            self.out.at[level],
            self.sems.at[turn],
            self.sems.at[3 + turn],
            (group, 2 * partner(level, turn) + core),
        )

    def first(self):
        for turn in TURNS:
            self.level_copy(turn).start()

    def second(self):
        pass

    def third(self):
        pass

    def fourth(self):
        for turn in TURNS:
            self.level_copy(turn).wait_recv()
            self.level_copy(turn).wait_send()

    def store(self):
        _, level, _ = place()
        self.out[level] = jnp.zeros(self.out.shape[1:], self.out.dtype)
        self.target[...] = self.out[...]


GROUP_GATHER_SEMS = 36


class GroupGather(Relay):
    group_at, relay_at = 4, 16

    def __init__(self, shard, quarters, out, sems):
        self.shard, self.quarters, self.out, self.sems = shard, quarters, out, sems

    def quarter_source(self, turn, target):
        _, level, _ = place()
        return self.quarters.at[partner(level, turn)]

    def own_copy(self, turn):
        group, level, core = place()
        if turn == 0:
            source, target = self.shard, self.out.at[2 * level + core]
        else:
            source, target = self.quarters.at[partner(level, turn)], self.region(turn, group)
        return pltpu.make_async_copy(source, target, self.sems.at[turn])

    def core_copy(self, turn):
        group, level, core = place()
        slot = 2 * partner(level, turn) + core
        source = self.shard if turn == 0 else self.out.at[slot]
        peer = (group, 2 * level + 1 - core)
        return remote(source, self.out.at[slot], self.sems.at[28 + turn], self.sems.at[32 + turn], peer)

    def first(self):
        for turn in TURNS:
            for other in (1, 2):
                self.group_copy(turn, other).start()
        for turn in (0, *TURNS):
            self.own_copy(turn).start()
        self.core_copy(0).start()

    def third(self):
        for turn in TURNS:
            self.wait_quarters(turn)
            self.own_copy(turn).wait()
            self.core_copy(turn).start()

    def fourth(self):
        for turn in (0, *TURNS):
            self.core_copy(turn).wait_recv()
            self.core_copy(turn).wait_send()
        self.wait_passed()
        self.own_copy(0).wait()

    def store(self):
        copy = pltpu.make_async_copy(self.out, self.target, self.sems.at[0])
        copy.start()
        copy.wait()


class LevelRide:
    def __init__(self, shard):
        self.operands = [shard]
        self.in_specs = [fixed(*shard.shape)]
        shape = (4, *quarter_shape(*shard.shape))
        self.out_specs = [fixed(*shape)]
        self.out_shapes = [jax.ShapeDtypeStruct(shape, shard.dtype)]
        self.scratch = [pltpu.VMEM(shape, shard.dtype), pltpu.SemaphoreType.DMA((7,))]

    def job(self, sources, targets, scratch):
        job = LevelGather(sources[0], *scratch)
        job.target = targets[0]
        return job

    def before(self, steps):
        return {0: ("first",)}

    after = ("fourth", "store")

    def result(self, outs):
        return GatherRide(self.operands[0], outs[0])

    def plain(self):
        return GatherRide(self.operands[0], self.operands[0])


class GatherRide:
    def __init__(self, shard, quarters):
        owners = lax.axis_size("fsdp")
        full = (owners, *shard.shape)
        self.operands = [shard, quarters]
        self.in_specs = [fixed(*shard.shape), fixed(*quarters.shape)]
        self.out_specs = [ANYWHERE]
        self.out_shapes = [jax.ShapeDtypeStruct(full, shard.dtype)]
        self.scratch = [
            pltpu.VMEM(full, shard.dtype),
            pltpu.SemaphoreType.DMA((GROUP_GATHER_SEMS,)),
        ]

    def job(self, sources, targets, scratch):
        job = GroupGather(*sources, *scratch)
        job.target = targets[0]
        return job

    def before(self, steps):
        return {0: ("first",), steps // 2: ("relay",), steps - 1: ("third",)}

    after = ("fourth", "store")

    def result(self, outs):
        return outs[0].reshape(-1, outs[0].shape[2])

    def plain(self):
        return lax.all_gather(self.operands[0], "fsdp", axis=0, tiled=True)


class ShareRide:
    def __init__(self, share):
        self.operands = [share]
        self.in_specs = [ANYWHERE]
        self.out_specs = [fixed(*share.shape)]
        self.out_shapes = [jax.ShapeDtypeStruct(share.shape, share.dtype)]
        self.scratch = [
            pltpu.VMEM(share.shape, share.dtype),
            *share_scratch(share),
            pltpu.SemaphoreType.DMA((GROUP_SEMS,)),
        ]

    def job(self, sources, targets, scratch):
        job = GroupReduce(sources[0], scratch[0], scratch[1:3], scratch[3])
        job.target = targets[0]
        return job

    def before(self, steps):
        return {0: ("first", "second"), max(1, steps // 2): ("third",)}

    after = ("fifth", "sixth", "store")

    def result(self, outs):
        return outs[0]

    def plain(self):
        return lax.psum(self.operands[0], "dp")


class SumRide:
    def __init__(self, grad, large):
        block = grad.shape[1:]
        self.large = large
        self.operands = [grad]
        self.in_specs = [ANYWHERE]
        self.out_specs = [fixed(*block)]
        self.out_shapes = [jax.ShapeDtypeStruct(block, grad.dtype)]
        buffers = stepped_scratch(grad) if large else whole_scratch(grad)
        sems = WHOLE_SEMS if large else REDUCE_SEMS
        self.scratch = [pltpu.VMEM(block, grad.dtype), *buffers, pltpu.SemaphoreType.DMA((sems,))]

    def job(self, sources, targets, scratch):
        job = (Whole if self.large else Reduce)(sources[0], scratch[0], scratch[1:-1], scratch[-1])
        job.target = targets[0]
        return job

    def before(self, steps):
        if self.large:
            return {0: ("first",), 1: ("second",), steps - 2: ("between",), steps - 1: ("third",)}
        return {0: ("first",), 1: ("second",), steps // 2: ("third",), steps - 1: ("fourth",)}

    @property
    def after(self):
        return (("fourth",) if self.large else ()) + ("fifth", "sixth", "store")

    def result(self, outs):
        return outs[0]

    def plain(self):
        return lax.psum(scatter(self.operands[0]), "dp")


class LeadRide:
    after = ("third", "sixth", "store")

    def __init__(self, grad):
        _, rows, columns = grad.shape
        shape = (4, rows // 2, columns // 2)
        self.operands = [grad]
        self.in_specs = [ANYWHERE]
        self.out_specs = [fixed(*shape)]
        self.out_shapes = [jax.ShapeDtypeStruct(shape, grad.dtype)]
        self.scratch = [*stepped_scratch(grad), pltpu.SemaphoreType.DMA((WHOLE_SEMS,))]

    def job(self, sources, targets, scratch):
        job = Lead(sources[0], None, scratch[:-1], scratch[-1])
        job.target = targets[0]
        return job

    def before(self, steps):
        return {0: ("first",), 1: ("second",), steps - 2: ("between",)}

    def result(self, outs):
        return RestRide(outs[0])

    def plain(self):
        return RestRide(self.operands[0])


class RestRide:
    after = ("fifth", "sixth", "store")

    def __init__(self, part):
        _, high, wide = part.shape
        block = (2 * high, 2 * wide)
        self.operands = [part]
        self.in_specs = [fixed(*part.shape)]
        self.out_specs = [fixed(*block)]
        self.out_shapes = [jax.ShapeDtypeStruct(block, part.dtype)]
        self.scratch = [
            pltpu.VMEM(block, part.dtype),
            pltpu.VMEM((3, high, wide), part.dtype),
            pltpu.SemaphoreType.DMA((WHOLE_SEMS,)),
        ]

    def job(self, sources, targets, scratch):
        job = Rest(sources[0], *scratch)
        job.target = targets[0]
        return job

    def before(self, steps):
        return {0: ("first",), steps - 1: ("fourth",)}

    def result(self, outs):
        return outs[0]

    def plain(self):
        return lax.psum(scatter(self.operands[0]), "dp")


def riding(body, counts, rides, steps):
    def kernel(*refs):
        refs = list(refs)

        def pop(count):
            taken = refs[:count]
            del refs[:count]
            return taken

        own = pop(counts[0])
        sources = [pop(len(ride.operands)) for ride in rides]
        own += pop(counts[1])
        targets = [pop(len(ride.out_shapes)) for ride in rides]
        own += pop(counts[2])
        jobs = [
            ride.job(source, target, pop(len(ride.scratch)))
            for ride, source, target in zip(rides, sources, targets)
        ]
        for step in range(steps):
            planned = [
                (job, stages)
                for ride, job in zip(rides, jobs)
                for at, stages in ride.before(steps).items()
                if at == step
            ]
            if planned:

                @pl.when(pl.program_id(0) == step)
                def _(planned=planned, step=step):
                    if step == 0:
                        greet()
                    for job, stages in planned:
                        run_stages([job], stages)

        body(*own)

        @pl.when(pl.program_id(0) == steps - 1)
        def _():
            for ride, job in zip(rides, jobs):
                run_stages([job], ride.after)

    return kernel


def block_call(
    body, grid, in_specs, operands, out_specs, out_shape, scratch, name,
    cost=None, rides=(), collective_id=None,
):
    plain = []
    if rides and not with_kernels():
        plain, rides = [ride.plain() for ride in rides], ()
    transfer = {}
    kernel = body
    if rides:
        transfer = {"collective_id": collective_id, "has_side_effects": True}
        kernel = riding(body, (len(operands), len(out_shape), len(scratch)), rides, grid)
    count = len(out_shape)
    for ride in rides:
        operands = [*operands, *ride.operands]
        in_specs = [*in_specs, *ride.in_specs]
        out_specs, out_shape = [*out_specs, *ride.out_specs], [*out_shape, *ride.out_shapes]
        scratch = [*scratch, *ride.scratch]
    outs = pl.pallas_call(
        kernel,
        grid=(grid,),
        in_specs=in_specs,
        out_specs=out_specs,
        out_shape=out_shape,
        scratch_shapes=scratch,
        compiler_params=pltpu.CompilerParams(vmem_limit_bytes=VMEM_LIMIT, **transfer),
        cost_estimate=cost or NO_COST,
        name=name,
    )(*operands)
    brought, outs = list(outs[count:]), list(outs[:count])
    for ride in rides:
        plain.append(ride.result(brought[: len(ride.out_shapes)]))
        brought = brought[len(ride.out_shapes) :]
    return outs + plain


def work(flops, size):
    return pl.CostEstimate(flops=flops, bytes_accessed=size, transcendentals=0)


def position_weights(seg_col, patch_row, nodes):
    rows = seg_col.shape[0]
    slot = lax.broadcasted_iota(jnp.int32, (rows, IMGS), 1)
    member = seg_col == slot
    counts = jnp.sum(member.astype(jnp.float32), 0, keepdims=True)
    start = jnp.sum(jnp.where(slot < seg_col, counts, 0.0), 1, keepdims=True)
    token = lax.broadcasted_iota(jnp.int32, (rows, 1), 0).astype(jnp.float32)
    inside = seg_col < IMGS
    offset = jnp.where(inside, token - start, 0.0)
    patch = jnp.sum(jnp.where(member, patch_row.astype(jnp.float32), 0.0), 1, keepdims=True)
    side = jnp.where(inside, jnp.floor(IMG / jnp.where(inside, patch, 1.0) + 0.5), 1.0)
    line = jnp.floor((offset + 0.5) / side)
    column = offset - line * side

    def spot(coord):
        return jnp.clip((2.0 * coord + 1.0) * GRID / (2.0 * side) - 0.5, 0.0, GRID - 1.0)

    node = lax.broadcasted_iota(jnp.int32, (rows, LANES), 1).astype(jnp.float32)
    across = jnp.floor((node + 0.5) / GRID)
    along = node - across * GRID
    weights = jnp.maximum(1.0 - jnp.abs(spot(line) - across), 0.0)
    weights = weights * jnp.maximum(1.0 - jnp.abs(spot(column) - along), 0.0)
    return jnp.where(node < nodes, weights, 0.0)


def first_kernel(*refs, spots):
    kernel, vectors, inputs, outputs, head, pixels, seg_col, patch_row, table, biases = refs[:10]
    stream, pos_t, vector_zero, vector_one = refs[10:14]
    qkv_full, up_full, output_level = refs[14:17]
    output_zero, qkv_one, up_one, output_one, head_low, normed, qkv_rows = refs[17:24]
    wide_kernel, wide_inputs, wide_outputs, wide_head, pixel_rows, table_low = refs[24:30]
    kernel_full, qkv_zero, vectors_full, qkv_landing, up_landing, output_landing = refs[30:36]
    up_zero, load_sems, sems = refs[36:]
    _, level, core = place()
    mine = 2 * level + core
    pairs = [
        (kernel, wide_kernel),
        (inputs.at[0], wide_inputs.at[0]),
        (pixels, pixel_rows),
        (inputs.at[1], wide_inputs.at[1]),
        (outputs.at[0], wide_outputs.at[0]),
        (outputs.at[1], wide_outputs.at[1]),
        (head, wide_head),
    ]
    copies = [
        pltpu.make_async_copy(source, target, load_sems.at[index])
        for index, (source, target) in enumerate(pairs)
    ]
    for copy in copies:
        copy.start()
    patch_job = Gather(kernel_full.at[mine], kernel_full, sems.at[0], True, in_place=True)
    vector_job = Gather(vectors, vectors_full, sems.at[1], False)
    qkv_job = Gather(qkv_zero, qkv_landing, sems.at[2], True)
    up_job = Gather(up_zero, up_landing, sems.at[3], True)
    output_job = LevelGather(output_zero, output_landing, sems.at[4])
    output_job.target = output_level
    copies[0].wait()
    kernel_full[mine] = wide_kernel[...].astype(LOW)
    greet()
    patch_job.first()
    vector_job.first()
    copies[1].wait()
    qkv_zero[...] = wide_inputs[0, :, : 3 * D].astype(LOW)
    qkv_job.first()
    up_zero[...] = wide_inputs[0, :, 3 * D :].astype(LOW)
    up_job.first()
    copies[4].wait()
    output_zero[...] = wide_outputs[0].astype(LOW)
    output_job.first()

    weights = position_weights(seg_col[...], patch_row[...], table.shape[0])
    pos_t[...] = weights.T[: pos_t.shape[0], :]
    table_low[...] = jnp.zeros_like(table_low)
    table_low[: table.shape[0], :] = table[...].astype(LOW).astype(jnp.float32)
    bias = biases[:, :D].astype(LOW).astype(jnp.float32)
    stream[...] = bias + jnp.dot(
        weights, table_low[...], precision=HIGHEST, preferred_element_type=jnp.float32
    )
    copies[2].wait()
    depth = wide_kernel.shape[0]

    def add_block(slot):
        columns = pl.ds(pl.multiple_of(slot * depth, depth), depth)

        def add(step, carry):
            rows = pl.ds(pl.multiple_of(step * 256, 256), 256)
            stream[rows, :] += mul(pixel_rows[rows, columns], kernel_full[slot])
            return carry

        lax.fori_loop(0, stream.shape[0] // 256, add, 0)

    def use(turn, own_core):
        add_block(2 * partner(level, turn) + (core if own_core else 1 - core))

    add_block(mine)
    patch_job.second()
    qkv_job.second()
    vector_job.second()
    patch_job.core_copy(0).wait_recv()
    use(0, False)
    copies[3].wait()
    qkv_one[...] = wide_inputs[1, :, : 3 * D].astype(LOW)
    up_one[...] = wide_inputs[1, :, 3 * D :].astype(LOW)
    patch_job.relay()
    copies[5].wait()
    output_one[...] = wide_outputs[1].astype(LOW)
    copies[6].wait()
    head_low[...] = jnp.zeros_like(head_low)
    head_low[:, : head.shape[1]] = wide_head[...].astype(LOW)
    patch_job.third(use)
    qkv_job.relay()
    up_job.second()
    patch_job.fourth(use)
    qkv_job.third()
    vector_job.third()
    vector_job.fourth()
    blocks = [vectors_full[slot].astype(jnp.float32) for slot in range(vectors_full.shape[0])]
    span = vectors.shape[0] // LAYERS
    for layer, out in enumerate((vector_zero, vector_one)):
        for row in range(out.shape[1] // LANES):
            parts = [
                block[layer * span + row - spot : layer * span + row - spot + 1, :]
                for block, spot in zip(blocks, spots)
                if 0 <= row - spot < span
            ]
            out[:, row * LANES : (row + 1) * LANES] = sum(parts)
    up_job.relay()
    up_job.third()
    qkv_job.fourth()
    copy = pltpu.make_async_copy(qkv_landing, qkv_full, load_sems.at[0])
    copy.start()
    weight = qkv_landing[...].reshape(-1, qkv_landing.shape[2])
    for half in halves_of(stream.shape[0]):
        unit, _ = normalized(stream[half, :])
        low = (unit * vector_zero[:, :D] + vector_zero[:, D : 2 * D]).astype(LOW)
        normed[half, :] = low
        for base in range(0, 3 * D, D):
            bias = vector_zero[:, 4 * D + base : 5 * D + base]
            qkv_rows[half, base : base + D] = (mul(low, weight[:, base : base + D]) + bias).astype(LOW)
    up_job.fourth()
    up_copy = pltpu.make_async_copy(up_landing, up_full, load_sems.at[1])
    up_copy.start()
    run_stages([output_job], ("fourth", "store"))
    copy.wait()
    up_copy.wait()


def padded_vectors(shard):
    layers, width = shard.shape
    owners = lax.axis_size("fsdp")
    spots = [owner * width // LANES for owner in range(owners)]
    span = max(-(-(owner + 1) * width // LANES) - spot for owner, spot in enumerate(spots))
    span += -span % 16
    shift = lax.rem(lax.axis_index("fsdp") * width, LANES)
    padded = jnp.zeros((layers, span * LANES), LOW)
    padded = lax.dynamic_update_slice(padded, shard.astype(LOW), (0, shift))
    return padded.reshape(layers * span, LANES), spots


def begin(
    pixels, segment, patch_size, patch_kernel, layer_vector, input_proj, output_proj, head_weight,
    position_table, global_vector,
):
    classes = head_weight.shape[1] + -head_weight.shape[1] % LANES
    nodes = position_table.shape[0] + -position_table.shape[0] % 64
    if not with_kernels():
        inputs = [
            (input_proj[index, :, : 3 * D].astype(LOW), input_proj[index, :, 3 * D :].astype(LOW))
            for index in range(LAYERS)
        ]
        outputs = [output_proj[index].astype(LOW) for index in range(LAYERS)]
        gather = lambda shard, axis: lax.all_gather(shard, "fsdp", axis=axis, tiled=True)
        weights, _, _ = row_layout(segment, patch_size[0])
        weights = jnp.pad(weights, ((0, 0), (0, nodes - weights.shape[1])))
        table = jnp.pad(rounded(position_table), ((0, nodes - position_table.shape[0]), (0, 0)))
        bias = rounded(global_vector)[None, :D]
        stream = embed(pixels, gather(patch_kernel.astype(LOW), 0), weights, table, bias)
        vectors = gather(layer_vector.astype(LOW), 1).astype(jnp.float32)
        head = jnp.pad(head_weight.astype(LOW), ((0, 0), (0, classes - head_weight.shape[1])))
        return (
            stream,
            weights.T,
            [vectors[index : index + 1] for index in range(LAYERS)],
            gather(inputs[0][0], 0),
            gather(inputs[0][1], 0),
            [GatherRide(outputs[0], outputs[0]), LevelRide(outputs[1])],
            [*inputs[1], head],
            qkv_forward(stream, gather(inputs[0][0], 0), vectors[:1]),
        )
    rows = pixels.shape[0]
    owners = lax.axis_size("fsdp")
    vectors, spots = padded_vectors(layer_vector)
    depth = input_proj.shape[1]
    up_shape = (depth, input_proj.shape[2] - 3 * D)
    qkv_shape, out_shape = (depth, 3 * D), output_proj.shape[1:]
    low = lambda *shape: jax.ShapeDtypeStruct(shape, LOW)
    levels = lambda shape: low(4, *quarter_shape(*shape))
    width = layer_vector.shape[1] * owners
    shapes = [
        shape_of(rows, D),
        shape_of(nodes, rows),
        shape_of(1, width),
        shape_of(1, width),
        low(owners, *qkv_shape),
        low(owners, *up_shape),
        levels(out_shape),
        low(*out_shape),
        low(*qkv_shape),
        low(*up_shape),
        low(*out_shape),
        low(head_weight.shape[0], classes),
        low(rows, D),
        low(rows, 3 * D),
    ]
    wide = (patch_kernel, input_proj, output_proj, head_weight, pixels)
    in_vmem = pl.BlockSpec(memory_space=pltpu.VMEM)
    results = pl.pallas_call(
        functools.partial(first_kernel, spots=spots),
        in_specs=[ANYWHERE] * 6 + [in_vmem] * 4,
        out_specs=[in_vmem] * 4 + [ANYWHERE] * 2 + [in_vmem] * 8,
        out_shape=shapes,
        scratch_shapes=[
            *[pltpu.VMEM(array.shape, array.dtype) for array in wide],
            pltpu.VMEM((LANES, D), jnp.float32),
            pltpu.VMEM((owners, *patch_kernel.shape), LOW),
            pltpu.VMEM(qkv_shape, LOW),
            pltpu.VMEM((owners, *vectors.shape), LOW),
            pltpu.VMEM((owners, *qkv_shape), LOW),
            pltpu.VMEM((owners, *up_shape), LOW),
            pltpu.VMEM((4, *quarter_shape(*out_shape)), LOW),
            pltpu.VMEM(up_shape, LOW),
            pltpu.SemaphoreType.DMA((7,)),
            pltpu.SemaphoreType.DMA((5, GATHER_SEMS)),
        ],
        compiler_params=pltpu.CompilerParams(
            collective_id=1, has_side_effects=True, vmem_limit_bytes=VMEM_LIMIT
        ),
        cost_estimate=NO_COST,
        name="begin",
    )(
        patch_kernel,
        vectors,
        input_proj,
        output_proj,
        head_weight,
        pixels,
        segment[:, None],
        patch_size,
        position_table,
        global_vector[None, :],
    )
    output_zero, qkv_one, up_one, output_one, head_low, normed, qkv_rows = results[7:]
    return (
        results[0],
        results[1],
        results[2:4],
        results[4].reshape(owners * depth, 3 * D),
        results[5].reshape(owners * depth, up_shape[1]),
        [GatherRide(output_zero, results[6]), LevelRide(output_one)],
        [qkv_one, up_one, head_low],
        (normed, qkv_rows),
    )


REDUCE_SEMS = 52


class Reduce:
    def __init__(self, grad, out, scratch, sems):
        self.grad, self.out, self.sems = grad, out, sems
        self.own, self.away, self.got_core, self.got_group, self.part, self.got_level = scratch
        self.rows, self.columns = out.shape
        self.chunk = 16

    def load(self, level):
        _, _, core = place()
        return pltpu.make_async_copy(
            self.grad.at[2 * level + core], self.own.at[level], self.sems.at[level]
        )

    def load_away(self, level):
        _, _, core = place()
        return pltpu.make_async_copy(
            self.grad.at[2 * level + 1 - core], self.away.at[level], self.sems.at[48 + level]
        )

    def core_copy(self, target_level):
        group, level, core = place()
        return remote(
            self.away.at[target_level],
            self.got_core.at[target_level],
            self.sems.at[4 + target_level],
            self.sems.at[8 + target_level],
            (group, 2 * level + 1 - core),
        )

    def group_copy(self, turn, other):
        group, level, core = place()
        target = partner(level, turn)
        peer = partner(group, other)
        part = quarter(peer, self.rows, self.columns)
        index = 3 * turn + other - 1
        return remote(
            self.own.at[target].at[part],
            self.got_group.at[other - 1, target],
            self.sems.at[12 + index],
            self.sems.at[24 + index],
            (peer, 2 * level + core),
        )

    def level_copy(self, turn):
        group, level, core = place()
        target = partner(level, turn)
        return remote(
            self.part.at[target],
            self.got_level.at[turn - 1],
            self.sems.at[35 + turn],
            self.sems.at[38 + turn],
            (group, 2 * target + core),
        )

    def share_copy(self, other):
        group, level, core = place()
        mine = self.out.at[quarter(group, self.rows, self.columns)]
        return remote(
            mine,
            mine,
            self.sems.at[41 + other],
            self.sems.at[44 + other],
            (partner(group, other), 2 * level + core),
        )

    def first(self):
        _, level, _ = place()
        for turn in (*TURNS, 0):
            self.load_away(partner(level, turn)).start()
        for turn in (*TURNS, 0):
            self.load(partner(level, turn)).start()
        for turn in (*TURNS, 0):
            self.load_away(partner(level, turn)).wait()
            self.core_copy(partner(level, turn)).start()

    def second(self):
        _, level, _ = place()
        for turn in (*TURNS, 0):
            target = partner(level, turn)
            self.load(target).wait()
            self.core_copy(target).wait_recv()

            def add(step, carry):
                rows = pl.ds(pl.multiple_of(step * self.chunk, self.chunk), self.chunk)
                total = self.own[target, rows, :].astype(jnp.float32)
                total = total + self.got_core[target, rows, :].astype(jnp.float32)
                self.own[target, rows, :] = total.astype(self.own.dtype)
                return carry

            lax.fori_loop(0, self.rows // self.chunk, add, 0)
            for other in TURNS:
                self.group_copy(turn, other).start()

    def between(self):
        pass

    def third(self):
        group, level, _ = place()
        high, wide = quarter_shape(self.rows, self.columns)
        row_part, column_part = quarter(group, self.rows, self.columns)
        for turn in (*TURNS, 0):
            target = partner(level, turn)
            for other in TURNS:
                self.group_copy(turn, other).wait_recv()

            def add(step, carry):
                at = pl.multiple_of(step * self.chunk, self.chunk)
                rows = pl.ds(at, self.chunk)
                mine = pl.ds(pl.multiple_of(row_part.start + at, self.chunk), self.chunk)
                total = self.own[target, mine, column_part].astype(jnp.float32)
                for slot in range(3):
                    total = total + self.got_group[slot, target, rows, :].astype(jnp.float32)
                self.part[target, rows, :] = total.astype(self.part.dtype)
                return carry

            lax.fori_loop(0, high // self.chunk, add, 0)
            if turn:
                self.level_copy(turn).start()

    def fourth(self):
        group, level, _ = place()
        high, wide = quarter_shape(self.rows, self.columns)
        row_part, column_part = quarter(group, self.rows, self.columns)
        for turn in TURNS:
            self.level_copy(turn).wait_recv()

        def add(step, carry):
            at = pl.multiple_of(step * self.chunk, self.chunk)
            rows = pl.ds(at, self.chunk)
            mine = pl.ds(pl.multiple_of(row_part.start + at, self.chunk), self.chunk)
            total = self.part[level, rows, :].astype(jnp.float32)
            for slot in range(3):
                total = total + self.got_level[slot, rows, :].astype(jnp.float32)
            self.out[mine, column_part] = total.astype(self.out.dtype)
            return carry

        lax.fori_loop(0, high // self.chunk, add, 0)
        for other in TURNS:
            self.share_copy(other).start()

    def store(self):
        self.target[...] = self.out[...]

    def fifth(self):
        for other in TURNS:
            self.share_copy(other).wait_recv()

    def sixth(self):
        _, level, _ = place()
        for turn in (*TURNS, 0):
            self.core_copy(partner(level, turn)).wait_send()
            for other in TURNS:
                self.group_copy(turn, other).wait_send()
            if turn:
                self.level_copy(turn).wait_send()
                self.share_copy(turn).wait_send()


WHOLE_SEMS = 44


def add_rows(target, row, columns, source, count, wide):
    chunk = 16 if wide > 1536 else 48

    def add(step, carry):
        at = pl.multiple_of(step * chunk, chunk)
        mine = pl.ds(pl.multiple_of(row + at, 16), chunk)
        total = target[mine, columns].astype(jnp.float32)
        total = total + source[pl.ds(at, chunk), :].astype(jnp.float32)
        target[mine, columns] = total.astype(target.dtype)
        return carry

    lax.fori_loop(0, count // chunk, add, 0)


class Whole:
    FIRST_X = (1, 0)

    lead = False

    def __init__(self, grad, out, scratch, sems):
        self.grad, self.out, self.sems = grad, out, sems
        self.own, self.away, self.got_core, self.got_x, self.got_y, self.got_last, self.part, self.got_level = scratch
        self.rows, self.columns = grad.shape[1:]
        self.high, self.wide = self.rows // 2, self.columns // 2

    def row_half(self, index):
        return pl.ds(pl.multiple_of(lax.div(index, 2) * self.high, self.high), self.high)

    def column_half(self, index):
        return pl.ds(pl.multiple_of(lax.rem(index, 2) * self.wide, self.wide), self.wide)

    def load(self, level):
        _, _, core = place()
        return pltpu.make_async_copy(
            self.grad.at[2 * level + core], self.own.at[level], self.sems.at[level]
        )

    def load_away(self, level):
        _, _, core = place()
        return pltpu.make_async_copy(
            self.grad.at[2 * level + 1 - core], self.away.at[level], self.sems.at[40 + level]
        )

    def core_copy(self, target_level):
        group, level, core = place()
        return remote(
            self.away.at[target_level],
            self.got_core.at[target_level],
            self.sems.at[4 + target_level],
            self.sems.at[8 + target_level],
            (group, 2 * level + 1 - core),
        )

    def step_copy(self, turn):
        group, level, core = place()
        block = self.own.at[partner(level, turn)]
        if turn in self.FIRST_X:
            peer = partner(group, 1)
            source = block.at[:, self.column_half(peer)]
            target = self.got_x.at[self.FIRST_X.index(turn)]
        else:
            peer = partner(group, 2)
            source = block.at[self.row_half(peer), :]
            target = self.got_y.at[turn - 2]
        return remote(
            source, target, self.sems.at[12 + turn], self.sems.at[16 + turn], (peer, 2 * level + core)
        )

    def last_copy(self, turn):
        group, level, core = place()
        block = self.own.at[partner(level, turn)]
        peer = partner(group, 2 if turn in self.FIRST_X else 1)
        rows = self.row_half(peer)
        columns = self.column_half(peer)
        return remote(
            block.at[rows, columns],
            self.got_last.at[turn],
            self.sems.at[20 + turn],
            self.sems.at[24 + turn],
            (peer, 2 * level + core),
        )

    def level_copy(self, turn):
        group, level, core = place()
        target = partner(level, turn)
        return remote(
            self.part.at[target],
            self.got_level.at[turn - 1],
            self.sems.at[27 + turn],
            self.sems.at[30 + turn],
            (group, 2 * target + core),
        )

    def share_copy(self, other):
        group, level, core = place()
        mine = self.out.at[self.row_half(group), self.column_half(group)]
        return remote(
            mine,
            mine,
            self.sems.at[33 + other],
            self.sems.at[36 + other],
            (partner(group, other), 2 * level + core),
        )

    def first(self):
        _, level, _ = place()
        for turn in (*TURNS, 0):
            self.load_away(partner(level, turn)).start()
        for turn in (*TURNS, 0):
            self.load(partner(level, turn)).start()
        for turn in (*TURNS, 0):
            self.load_away(partner(level, turn)).wait()
            self.core_copy(partner(level, turn)).start()

    def second(self):
        _, level, _ = place()
        for turn in (*TURNS, 0):
            target = partner(level, turn)
            self.load(target).wait()
            self.core_copy(target).wait_recv()
            add_rows(
                self.own.at[target], 0, slice(None), self.got_core.at[target], self.rows, self.columns
            )
            self.step_copy(turn).start()

    def between(self):
        group, level, _ = place()
        for turn in (*TURNS, 0):
            block = self.own.at[partner(level, turn)]
            self.step_copy(turn).wait_recv()
            if turn in self.FIRST_X:
                source = self.got_x.at[self.FIRST_X.index(turn)]
                add_rows(block, 0, self.column_half(group), source, self.rows, self.wide)
            else:
                source = self.got_y.at[turn - 2]
                start = lax.div(group, 2) * self.high
                add_rows(block, start, slice(None), source, self.high, self.columns)
            self.last_copy(turn).start()

    def third(self):
        group, level, _ = place()
        start = lax.div(group, 2) * self.high
        columns = self.column_half(group)
        chunk = 16 if self.wide > 1536 else 48
        for turn in (*TURNS, 0):
            target = partner(level, turn)
            self.last_copy(turn).wait_recv()

            def add(step, carry):
                at = pl.multiple_of(step * chunk, chunk)
                rows = pl.ds(at, chunk)
                mine = pl.ds(pl.multiple_of(start + at, 16), chunk)
                total = self.own[target, mine, columns].astype(jnp.float32)
                total = total + self.got_last[turn, rows, :].astype(jnp.float32)
                self.part[target, rows, :] = total.astype(self.part.dtype)
                return carry

            lax.fori_loop(0, self.high // chunk, add, 0)
            if turn and not self.lead:
                self.level_copy(turn).start()

    def fourth(self):
        group, level, _ = place()
        start = lax.div(group, 2) * self.high
        columns = self.column_half(group)
        chunk = 16 if self.wide > 1536 else 48
        for turn in TURNS:
            self.level_copy(turn).wait_recv()

        def add(step, carry):
            at = pl.multiple_of(step * chunk, chunk)
            rows = pl.ds(at, chunk)
            mine = pl.ds(pl.multiple_of(start + at, 16), chunk)
            total = self.part[level, rows, :].astype(jnp.float32)
            for slot in range(3):
                total = total + self.got_level[slot, rows, :].astype(jnp.float32)
            self.out[mine, columns] = total.astype(self.out.dtype)
            return carry

        lax.fori_loop(0, self.high // chunk, add, 0)
        for other in TURNS:
            self.share_copy(other).start()

    def store(self):
        self.target[...] = self.out[...]

    def fifth(self):
        for other in TURNS:
            self.share_copy(other).wait_recv()

    def sixth(self):
        _, level, _ = place()
        for turn in (*TURNS, 0):
            self.core_copy(partner(level, turn)).wait_send()
            self.step_copy(turn).wait_send()
            self.last_copy(turn).wait_send()
            if turn and not self.lead:
                self.level_copy(turn).wait_send()
                self.share_copy(turn).wait_send()


class Lead(Whole):
    lead = True

    def store(self):
        self.target[...] = self.part[...]


class Rest(Whole):
    def __init__(self, part, out, got_level, sems):
        self.part, self.out, self.got_level, self.sems = part, out, got_level, sems
        self.rows, self.columns = out.shape
        self.high, self.wide = self.rows // 2, self.columns // 2

    def first(self):
        for turn in TURNS:
            self.level_copy(turn).start()

    def sixth(self):
        for turn in TURNS:
            self.level_copy(turn).wait_send()
            self.share_copy(turn).wait_send()


GROUP_SEMS = 13


class GroupReduce:
    def __init__(self, share, out, scratch, sems):
        self.share, self.out, self.sems = share, out, sems
        self.own, self.got = scratch
        self.rows, self.columns = out.shape
        self.chunk = 16

    def load(self):
        return pltpu.make_async_copy(self.share, self.own, self.sems.at[0])

    def group_copy(self, other):
        group, level, core = place()
        peer = partner(group, other)
        return remote(
            self.own.at[quarter(peer, self.rows, self.columns)],
            self.got.at[other - 1],
            self.sems.at[other],
            self.sems.at[3 + other],
            (peer, 2 * level + core),
        )

    def share_copy(self, other):
        group, level, core = place()
        mine = self.out.at[quarter(group, self.rows, self.columns)]
        return remote(
            mine,
            mine,
            self.sems.at[6 + other],
            self.sems.at[9 + other],
            (partner(group, other), 2 * level + core),
        )

    def first(self):
        self.load().start()

    def second(self):
        self.load().wait()
        for other in TURNS:
            self.group_copy(other).start()

    def between(self):
        pass

    def third(self):
        group, _, _ = place()
        high, wide = quarter_shape(self.rows, self.columns)
        row_part, column_part = quarter(group, self.rows, self.columns)
        for other in TURNS:
            self.group_copy(other).wait_recv()

        def add(step, carry):
            at = pl.multiple_of(step * self.chunk, self.chunk)
            rows = pl.ds(at, self.chunk)
            mine = pl.ds(pl.multiple_of(row_part.start + at, self.chunk), self.chunk)
            total = self.own[mine, column_part].astype(jnp.float32)
            for slot in range(3):
                total = total + self.got[slot, rows, :].astype(jnp.float32)
            self.out[mine, column_part] = total.astype(self.out.dtype)
            return carry

        lax.fori_loop(0, high // self.chunk, add, 0)
        for other in TURNS:
            self.share_copy(other).start()

    def fourth(self):
        pass

    def fifth(self):
        for other in TURNS:
            self.share_copy(other).wait_recv()

    def store(self):
        self.target[...] = self.out[...]

    def sixth(self):
        for other in TURNS:
            self.group_copy(other).wait_send()
            self.share_copy(other).wait_send()


class Spread:
    def __init__(self, full, sems):
        self.full, self.sems = full, sems

    def level_copy(self, turn):
        group, level, core = place()
        block = self.full.at[2 * level + core]
        peer = (group, 2 * partner(level, turn) + core)
        return remote(block, block, self.sems.at[turn - 1], self.sems.at[2 + turn], peer)

    def core_copy(self, turn):
        group, level, core = place()
        block = self.full.at[2 * partner(level, turn) + core]
        peer = (group, 2 * level + 1 - core)
        return remote(block, block, self.sems.at[6 + turn], self.sems.at[10 + turn], peer)

    def run(self):
        for turn in TURNS:
            self.level_copy(turn).start()
        self.core_copy(0).start()
        for turn in TURNS:
            self.level_copy(turn).wait_recv()
            self.core_copy(turn).start()
        for turn in (0, *TURNS):
            self.core_copy(turn).wait_recv()
        for turn in (0, *TURNS):
            self.core_copy(turn).wait_send()
            if turn:
                self.level_copy(turn).wait_send()


def squares_in(out):
    def add(step, total):
        piece = out[pl.ds(pl.multiple_of(step * 16, 16), 16), :].astype(jnp.float32)
        piece = piece * piece
        for lane in range(0, out.shape[1], LANES):
            total = total + piece[:, lane : lane + LANES]
        return total

    total = lax.fori_loop(0, out.shape[0] // 16, add, jnp.zeros((16, LANES), jnp.float32))
    return jnp.sum(total, 0, keepdims=True)


def run_stages(jobs, stages):
    for stage in stages:
        for job in jobs:
            getattr(job, stage)()


STAGES = ("first", "second", "between", "third", "fourth", "fifth", "sixth")


def whole_scratch(grad):
    _, rows, columns = grad.shape
    high, wide = quarter_shape(rows, columns)
    shapes = (*[(4, rows, columns)] * 3, (3, 4, high, wide), (4, high, wide))
    return [pltpu.VMEM(shape, grad.dtype) for shape in (*shapes, (3, high, wide))]


def stepped_scratch(grad):
    _, rows, columns = grad.shape
    high, wide = rows // 2, columns // 2
    shapes = (
        *[(4, rows, columns)] * 3,
        (2, rows, wide),
        (2, high, columns),
        (4, high, wide),
        (4, high, wide),
        (3, high, wide),
    )
    return [pltpu.VMEM(shape, grad.dtype) for shape in shapes]


def share_scratch(share):
    return [
        pltpu.VMEM(share.shape, share.dtype),
        pltpu.VMEM((3, *quarter_shape(*share.shape)), share.dtype),
    ]


def reduce_kernel(*refs, whole, partly, done, vector_rows, rest_size):
    count = whole + 1 + partly
    finished, grads, refs = refs[:done], refs[done : done + count], refs[done + count :]
    outs, full, numbers, refs = refs[:count], refs[count], refs[count + 1], refs[count + 2 :]
    sems, small_sems, group_sems, spread_sems, refs = *refs[:4], refs[4:]
    jobs = [
        Whole(grads[i], outs[i], refs[8 * i : 8 * i + 8], sems.at[i]) for i in range(whole)
    ]
    refs = refs[8 * whole :]
    small = Reduce(grads[whole], outs[whole], refs[:6], small_sems)
    refs = refs[6:]
    shares = [
        GroupReduce(
            grads[whole + 1 + i], outs[whole + 1 + i], refs[2 * i : 2 * i + 2], group_sems.at[i]
        )
        for i in range(partly)
    ]
    greet()
    run_stages([*jobs, small, *shares], STAGES[:1])
    run_stages([small, *shares], STAGES[1:2])
    run_stages(jobs, STAGES[1:3])
    run_stages([small, *shares], STAGES[3:4])
    run_stages(jobs, STAGES[3:4])
    run_stages([small, *jobs], STAGES[4:5])
    run_stages([*shares, small, *jobs], STAGES[5:6])
    total = sum(squares_in(out) for out in (*finished, *outs[:whole], *outs[whole + 1 :]))
    _, level, core = place()
    mine = 2 * level + core
    block = outs[whole]
    last = block.shape[0] - 1
    full[mine] = block[...]
    full[mine, last : last + 1, :] = total
    Spread(full, spread_sems).run()
    numbers[...] = totals(full[...], vector_rows, rest_size)
    run_stages([*shares, small, *jobs], STAGES[6:])


def transfer_outs(arrays):
    return [jax.ShapeDtypeStruct(array.shape[-2:], array.dtype) for array in arrays]


def reduce_call(grads, small, shares, finished, vector_rows, rest_size, collective_id):
    in_vmem = pl.BlockSpec(memory_space=pltpu.VMEM)
    whole, partly, done = len(grads), len(shares), len(finished)
    operands = [*grads, small, *shares]
    scratch = [
        pltpu.SemaphoreType.DMA((whole, WHOLE_SEMS)),
        pltpu.SemaphoreType.DMA((REDUCE_SEMS,)),
        pltpu.SemaphoreType.DMA((partly, GROUP_SEMS)),
        pltpu.SemaphoreType.DMA((14,)),
    ]
    for grad in grads:
        scratch.extend(stepped_scratch(grad))
    scratch.extend(whole_scratch(small))
    for share in shares:
        scratch.extend(share_scratch(share))
    out_shape = [*transfer_outs(operands), shape_of(*small.shape), shape_of(1, LANES)]
    return pl.pallas_call(
        functools.partial(
            reduce_kernel,
            whole=whole,
            partly=partly,
            done=done,
            vector_rows=vector_rows,
            rest_size=rest_size,
        ),
        in_specs=[in_vmem] * done + [ANYWHERE] * len(operands),
        out_specs=[in_vmem] * len(out_shape),
        out_shape=out_shape,
        scratch_shapes=scratch,
        compiler_params=pltpu.CompilerParams(
            collective_id=collective_id, has_side_effects=True, vmem_limit_bytes=VMEM_LIMIT
        ),
        cost_estimate=NO_COST,
        name="reduce_gradients",
    )(*finished, *operands)


def totals(full, vector_rows, rest_size):
    owners, rows, _ = full.shape
    rest_rows = -(-rest_size // (owners * LANES))
    row = lax.broadcasted_iota(jnp.int32, full.shape, 1)
    spot = row - vector_rows + rest_rows * lax.broadcasted_iota(jnp.int32, full.shape, 0)
    spot = spot * LANES + lax.broadcasted_iota(jnp.int32, full.shape, 2)
    in_rest = (row >= vector_rows) & (row < vector_rows + rest_rows)

    def summed(values):
        return jnp.sum(jnp.sum(jnp.sum(values, 0), 0, keepdims=True), 1, keepdims=True)

    tokens = summed(jnp.where(in_rest & (spot == rest_size - 1), full, 0.0))
    loss = summed(jnp.where(in_rest & (spot == rest_size - 2), full, 0.0))
    kept = (row < vector_rows) | (in_rest & (spot < rest_size - 2))
    squares = jnp.where(kept, full * full, jnp.where(row == rows - 1, full, 0.0))
    norm = jnp.sqrt(summed(squares)) / tokens
    factor = jnp.minimum(1.0, CLIP_NORM / norm) / tokens
    lane = lax.broadcasted_iota(jnp.int32, (1, LANES), 1)
    return jnp.where(
        lane == 0, factor, jnp.where(lane == 1, norm, jnp.where(lane == 2, loss, tokens))
    )


def with_kernels():
    return lax.axis_size("dp") == 4 and lax.axis_size("fsdp") == 8


def reduce_all(grads, small, shares, finished, vector_rows, rest_size, collective_id):
    if with_kernels():
        return reduce_call(grads, small, shares, finished, vector_rows, rest_size, collective_id)
    sums = [lax.psum(scatter(grad), "dp") for grad in grads]
    block = lax.psum(scatter(small), "dp")
    outs = [lax.psum(share, "dp") for share in shares]
    total = sum(jnp.sum(jnp.square(out.astype(jnp.float32))) for out in (*finished, *sums, *outs))
    row = jnp.full((1, LANES), 1.0 / LANES, jnp.float32) * total
    full = lax.all_gather(block.at[-1:].set(row), "fsdp", axis=0)
    return [*sums, block, *outs, full, totals(full, vector_rows, rest_size)]


def scatter(grad):
    return lax.psum_scatter(grad, "fsdp", scatter_dimension=0)


def by_owner(grad, low=jnp.bfloat16):
    owners = lax.axis_size("fsdp")
    return grad.astype(low).reshape(owners, grad.shape[0] // owners, grad.shape[1])


def attention_forward_kernel(
    q_ref, k_ref, v_ref, seg_col_ref, seg_row_ref, out_ref, expo_ref, inv_ref, *, block
):
    rows = q_ref.shape[0]
    lower = lax.broadcasted_iota(jnp.int32, (block, PAIR), 1) < HD
    keys = k_ref[...]
    values = jnp.concatenate([v_ref[...], jnp.ones((rows, PAIR), v_ref.dtype)], 1)
    seg_row = seg_row_ref[...]
    tasks = [(step, head) for step in range(rows // block) for head in range(2)]

    def scores_of(step, head):
        query = q_ref[step * block : (step + 1) * block, :] * jnp.bfloat16(HD**-0.5)
        keep = lower if head == 0 else jnp.logical_not(lower)
        return mul_nt(jnp.where(keep, query, jnp.bfloat16(0)), keys)

    scores = scores_of(*tasks[0])
    outs = []
    for index, (step, head) in enumerate(tasks):
        following = scores_of(*tasks[index + 1]) if index + 1 < len(tasks) else None
        at = slice(step * block, (step + 1) * block)
        scores = jnp.where(seg_col_ref[at, :] == seg_row, scores, MASKED)
        highest = jnp.max(scores, -1, keepdims=True)
        low = jnp.exp(scores - highest).astype(jnp.bfloat16)
        expo_ref[head, at, :] = low
        outs.append(mul(low, values))
        if head:
            inverse = 1.0 / jnp.where(lower, outs[0][:, PAIR:], outs[1][:, PAIR:])
            sums = jnp.where(lower, outs[0][:, :PAIR], outs[1][:, :PAIR])
            out_ref[at, :] = (sums * inverse).astype(jnp.bfloat16)
            inv_ref[at, :] = inverse
            outs = []
        scores = following


def attention_forward(qkv_rows, segment, rides, collective_id):
    rows = qkv_rows.shape[0]
    pairs = HEADS // 2
    wide = lambda base: pl.BlockSpec((rows, PAIR), lambda j, base=base: (0, base + j))
    return block_call(
        functools.partial(attention_forward_kernel, block=min(256, rows)),
        pairs,
        [wide(0), wide(pairs), wide(2 * pairs), fixed(rows, 1), fixed(1, rows)],
        [qkv_rows, qkv_rows, qkv_rows, segment[:, None], segment[None, :]],
        [wide(0), pl.BlockSpec((2, rows, rows), lambda j: (j, 0, 0)), wide(0)],
        [
            shape_of(rows, D, dtype=LOW),
            shape_of(HEADS, rows, rows, dtype=LOW),
            shape_of(rows, D),
        ],
        [],
        "attention_forward",
        work(16 * HEADS * rows * rows * HD, 2 * HEADS * rows * rows + 12 * rows * D),
        rides,
        collective_id,
    )


def attention_backward_kernel(
    q_ref, k_ref, v_ref, expo_ref, inv_ref, out_ref, grad_ref, dqkv_ref, *, block
):
    rows = q_ref.shape[0]
    pair = pl.program_id(0)
    lower = lax.broadcasted_iota(jnp.int32, (block, PAIR), 1) < HD
    keys = k_ref[...]
    values = v_ref[...]
    scale = HD**-0.5
    scaled_grad = (grad_ref[...].astype(jnp.float32) * inv_ref[...]).astype(jnp.bfloat16)
    query = q_ref[...]
    query_t = query.T
    grad_t = scaled_grad.T
    product = scaled_grad.astype(jnp.float32) * out_ref[...].astype(jnp.float32)
    key_t = [None, None]
    value_t = [None, None]
    tasks = [(step, head) for step in range(rows // block) for head in range(2)]

    def probs_grad_of(step, head):
        keep = lower if head == 0 else jnp.logical_not(lower)
        mine = scaled_grad[step * block : (step + 1) * block]
        return mul_nt(jnp.where(keep, mine, jnp.bfloat16(0)), values)

    probs_grad = probs_grad_of(*tasks[0])
    query_parts = []
    for index, (step, head) in enumerate(tasks):
        following = probs_grad_of(*tasks[index + 1]) if index + 1 < len(tasks) else None
        at = slice(step * block, (step + 1) * block)
        lanes = slice(head * HD, (head + 1) * HD)
        keep = lower if head == 0 else jnp.logical_not(lower)
        inner = jnp.sum(jnp.where(keep, product[at], 0.0), -1, keepdims=True)
        low = expo_ref[head, at, :]
        value_part = mul(grad_t[lanes, at], low)
        scores_grad = (low.astype(jnp.float32) * (probs_grad - inner)).astype(jnp.bfloat16)
        query_parts.append(mul(scores_grad, keys))
        key_part = mul(query_t[lanes, at], scores_grad)
        key_t[head] = key_part if step == 0 else key_t[head] + key_part
        value_t[head] = value_part if step == 0 else value_t[head] + value_part
        if head:
            query_grad = jnp.where(lower, query_parts[0], query_parts[1]) * scale
            dqkv_ref[at, pl.ds(pl.multiple_of(pair * PAIR, PAIR), PAIR)] = query_grad.astype(
                jnp.bfloat16
            )
            query_parts = []
        probs_grad = following
    key_grad = (jnp.concatenate(key_t, 0) * scale).T
    value_grad = jnp.concatenate(value_t, 0).T
    dqkv_ref[:, pl.ds(pl.multiple_of(D + pair * PAIR, PAIR), PAIR)] = key_grad.astype(jnp.bfloat16)
    dqkv_ref[:, pl.ds(pl.multiple_of(2 * D + pair * PAIR, PAIR), PAIR)] = value_grad.astype(jnp.bfloat16)


def attention_backward(qkv_rows, expo, inverse, attended, attended_grad, rides, collective_id):
    rows = qkv_rows.shape[0]
    pairs = HEADS // 2
    wide = lambda base: pl.BlockSpec((rows, PAIR), lambda j, base=base: (0, base + j))
    return block_call(
        functools.partial(attention_backward_kernel, block=min(256, rows)),
        pairs,
        [
            wide(0),
            wide(pairs),
            wide(2 * pairs),
            pl.BlockSpec((2, rows, rows), lambda j: (j, 0, 0)),
            wide(0),
            wide(0),
            wide(0),
        ],
        [qkv_rows, qkv_rows, qkv_rows, expo, inverse, attended, attended_grad],
        [fixed(rows, 3 * D)],
        [shape_of(rows, 3 * D, dtype=LOW)],
        [],
        "attention_backward",
        None,
        rides,
        collective_id,
    )


def mul(left, right):
    return jnp.dot(left, right, preferred_element_type=jnp.float32)


def mul_nt(left, right):
    return lax.dot_general(left, right, NT, preferred_element_type=jnp.float32)


def normalized(values):
    center = values - jnp.mean(values, -1, keepdims=True)
    inverse = lax.rsqrt(jnp.mean(center * center, -1, keepdims=True) + NORM_EPS)
    return center * inverse, inverse


def norm_backward(grad, values, gain):
    unit, inverse = normalized(values)
    inner = grad * gain
    mean_inner = jnp.mean(inner, -1, keepdims=True)
    mean_cross = jnp.mean(inner * unit, -1, keepdims=True)
    value_grad = inverse * (inner - mean_inner - unit * mean_cross)
    return value_grad, column_sum(grad * unit), column_sum(grad)


def column_sum(rows):
    return jnp.sum(rows.astype(jnp.float32), 0, keepdims=True)


def at_first(action):
    pl.when(pl.program_id(0) == 0)(action)


def rows_of(block, columns):
    return pl.BlockSpec((block, columns), lambda i: (i, 0))


def fixed(*shape):
    return pl.BlockSpec(shape, lambda i: (0,) * len(shape), pipeline_mode=pl.Buffered(1))


def loads(sources, targets, sems):
    return [
        pltpu.make_async_copy(source, target, sems.at[index])
        for index, (source, target) in enumerate(zip(sources, targets))
    ]


def shape_of(*shape, dtype=jnp.float32):
    return jax.ShapeDtypeStruct(shape, dtype)


def embed_kernel(pixel_ref, weight_ref, pos_ref, table_ref, bias_ref, out_ref):
    position = jnp.dot(
        pos_ref[...], table_ref[...], precision=HIGHEST, preferred_element_type=jnp.float32
    )
    out_ref[...] = mul(pixel_ref[...], weight_ref[...]) + bias_ref[...] + position


def embed(pixels, weight, pos_weights, table, bias):
    rows, depth = pixels.shape
    block = 256
    nodes = pos_weights.shape[1]
    return block_call(
        embed_kernel,
        rows // block,
        [rows_of(block, depth), fixed(depth, D), rows_of(block, nodes), fixed(nodes, D), fixed(1, D)],
        [pixels, weight, pos_weights, table, bias],
        [rows_of(block, D)],
        [shape_of(rows, D)],
        [],
        "embed",
        work(2 * rows * depth * D, 2 * rows * depth + 2 * depth * D + 4 * rows * D),
    )[0]


def chunk_at(base):
    return pl.ds(pl.multiple_of(base + pl.program_id(0) * D, LANES), D)


def columns_of(rows):
    return pl.BlockSpec((rows, D), lambda i: (0, i))


def halves_of(rows):
    half = rows // 2
    return [slice(start, start + half) for start in range(0, rows, half)]


def at_last(action):
    pl.when(pl.program_id(0) == pl.num_programs(0) - 1)(action)


def qkv_kernel(stream_ref, weight_ref, vector_ref, normed_out, qkv_ref, normed_ref, sem):
    copy = pltpu.make_async_copy(normed_ref, normed_out, sem)

    @at_first
    def _():
        unit, _ = normalized(stream_ref[...])
        normed_ref[...] = (unit * vector_ref[:, :D] + vector_ref[:, D : 2 * D]).astype(LOW)
        copy.start()

    bias = vector_ref[:, chunk_at(4 * D)]
    for half in halves_of(stream_ref.shape[0]):
        qkv_ref[half, :] = (mul(normed_ref[half, :], weight_ref[...]) + bias).astype(LOW)
    at_last(copy.wait)


def qkv_forward(stream, weight, vector):
    rows = stream.shape[0]
    return block_call(
        qkv_kernel,
        3,
        [fixed(rows, D), columns_of(D), fixed(1, vector.shape[1])],
        [stream, weight, vector],
        [ANYWHERE, columns_of(rows)],
        [shape_of(rows, D, dtype=LOW), shape_of(rows, 3 * D, dtype=LOW)],
        [pltpu.VMEM((rows, D), LOW), pltpu.SemaphoreType.DMA],
        "qkv_forward",
        work(6 * rows * D * D, 14 * rows * D + 6 * D * D),
    )


def mlp_kernel(
    stream_ref, attended_ref, mix_ref, up_ref, down_ref, vector_ref,
    residual_out, normed_out, active_ref, slope_ref, out_ref,
    residual_ref, normed_ref, sems,
):
    rows = stream_ref.shape[0]
    copies = loads((residual_ref, normed_ref), (residual_out, normed_out), sems)

    @at_first
    def _():
        for half in halves_of(rows):
            residual = stream_ref[half, :] + mul(attended_ref[half, :], mix_ref[...])
            residual = residual + vector_ref[:, 7 * D : 8 * D]
            residual_ref[half, :] = residual
            unit, _ = normalized(residual)
            normed = unit * vector_ref[:, 2 * D : 3 * D] + vector_ref[:, 3 * D : 4 * D]
            normed_ref[half, :] = normed.astype(LOW)
            out_ref[half, :] = residual + vector_ref[:, 8 * D : 9 * D]
        for copy in copies:
            copy.start()

    bias = vector_ref[:, chunk_at(9 * D)]
    parts = halves_of(rows)
    hidden = mul(normed_ref[parts[0], :], up_ref[...]) + bias
    for index, half in enumerate(parts):
        following = None
        if index + 1 < len(parts):
            following = mul(normed_ref[parts[index + 1], :], up_ref[...]) + bias
        square = hidden * hidden
        rise = 0.5 + 0.5 * jnp.tanh(hidden * (ROOT + (ROOT * CUBE) * square))
        active = hidden * rise
        active_low = active.astype(LOW)
        active_ref[half, :] = active_low
        bend = (2.0 * ROOT) + (6.0 * ROOT * CUBE) * square
        slope_ref[half, :] = (rise + active * (1.0 - rise) * bend).astype(LOW)
        out_ref[half, :] += mul(active_low, down_ref[...])
        hidden = following

    @at_last
    def _():
        for copy in copies:
            copy.wait()


def mlp_specs(up, proj_out):
    return (
        [fixed(D, D), columns_of(D), pl.BlockSpec((D, D), lambda i: (i + 1, 0))],
        [proj_out, up, proj_out],
    )


def mlp_forward(stream, attended, up, proj_out, vector, rides, collective_id):
    rows = stream.shape[0]
    width = up.shape[1]
    weight_specs, weights = mlp_specs(up, proj_out)
    return block_call(
        mlp_kernel,
        width // D,
        [fixed(rows, D), fixed(rows, D), *weight_specs, fixed(1, vector.shape[1])],
        [stream, attended, *weights, vector],
        [ANYWHERE, ANYWHERE, columns_of(rows), columns_of(rows), fixed(rows, D)],
        [
            shape_of(rows, D),
            shape_of(rows, D, dtype=LOW),
            shape_of(rows, width, dtype=LOW),
            shape_of(rows, width, dtype=LOW),
            shape_of(rows, D),
        ],
        [
            pltpu.VMEM((rows, D), jnp.float32),
            pltpu.VMEM((rows, D), LOW),
            pltpu.SemaphoreType.DMA((2,)),
        ],
        "mlp_forward",
        work(2 * rows * D * (D + 2 * width), rows * (16 * D + 4 * width) + 2 * D * (D + 2 * width)),
        rides,
        collective_id,
    )


def mlp_back_kernel(
    grad_ref, slope_ref, residual_in, normed_ref, active_ref, attended_ref, mix_ref, up_ref, down_ref, vector_ref,
    out_ref, attended_grad_ref, sums_ref, output_grad, *refs,
):
    up_grads, scratch = refs[:-7], refs[-7:]
    residual_ref, low_ref, second_ref, turned_ref, hidden_ref, product_ref, sems = scratch
    rows = grad_ref.shape[0]
    step = pl.program_id(0)
    load = pltpu.make_async_copy(residual_in, residual_ref, sems.at[0])

    def store_copy(slot):
        rows_at = pl.ds(pl.multiple_of(slot * D, D), D)
        return pltpu.make_async_copy(
            product_ref.at[slot], output_grad.at[rows_at], sems.at[1 + slot]
        )

    def store(slot, product):
        product_ref[slot] = product.astype(LOW)
        store_copy(slot).start()

    @at_first
    def _():
        load.start()
        low_ref[...] = grad_ref[...].astype(LOW)
        turned_ref[...] = normed_ref[...].T
        second_ref[...] = jnp.zeros_like(second_ref)

    parts = halves_of(rows)
    active_grad = mul_nt(low_ref[parts[0], :], down_ref[...])
    hidden_sum = 0.0
    for index, half in enumerate(parts):
        following = None
        if index + 1 < len(parts):
            following = mul_nt(low_ref[parts[index + 1], :], down_ref[...])
        hidden_grad = (active_grad * slope_ref[half, :].astype(jnp.float32)).astype(LOW)
        hidden_ref[half, :] = hidden_grad
        hidden_sum = hidden_sum + column_sum(hidden_grad)
        second_ref[half, :] += mul_nt(hidden_grad, up_ref[...])
        active_grad = following
    sums_ref[:, chunk_at(4 * D)] = hidden_sum
    store(step + 1, mul(active_ref[...].T, low_ref[...]))
    up_grad = mul(turned_ref[...], hidden_ref[...]).astype(LOW)
    share = pl.num_programs(0) // len(up_grads)
    for index, part in enumerate(up_grads):

        @pl.when(lax.div(step, share) == index)
        def _(part=part):
            part[...] = up_grad

    @at_last
    def _():
        load.wait()
        gain = vector_ref[:, 2 * D : 3 * D]
        totals = [0.0] * 4
        for half in halves_of(rows):
            grad = grad_ref[half, :]
            value_grad, gain_grad, shift_grad = norm_backward(
                second_ref[half, :], residual_ref[half, :], gain
            )
            total = value_grad + grad
            out_ref[half, :] = total
            total_low = total.astype(LOW)
            hidden_ref[half, :] = total_low
            attended_grad_ref[half, :] = mul_nt(total_low, mix_ref[...]).astype(LOW)
            new = (gain_grad, shift_grad, column_sum(total_low), column_sum(low_ref[half, :]))
            totals = [old + part for old, part in zip(totals, new)]
        sums_ref[:, : 4 * D] = jnp.concatenate(totals, 1)
        store(0, mul(attended_ref[...].T, hidden_ref[...]))
        for slot in range(product_ref.shape[0]):
            store_copy(slot).wait()


def mlp_backward(
    grad, slope, residual, normed, active, attended, up, proj_out, vector, parts, rides, collective_id
):
    rows = grad.shape[0]
    width = up.shape[1]
    steps = width // D
    share = steps // parts
    part_of = lambda index: lambda i: (0, jnp.clip(i - index * share, 0, share - 1))
    whole = fixed(rows, D)
    weight_specs, weights = mlp_specs(up, proj_out)
    return block_call(
        mlp_back_kernel,
        steps,
        [
            whole,
            columns_of(rows),
            ANYWHERE,
            whole,
            columns_of(rows),
            whole,
            *weight_specs,
            fixed(1, vector.shape[1]),
        ],
        [grad, slope, residual, normed, active, attended, *weights, vector],
        [whole, whole, fixed(1, 4 * D + width), ANYWHERE, *[pl.BlockSpec((D, D), part_of(index)) for index in range(parts)]],
        [
            shape_of(rows, D),
            shape_of(rows, D, dtype=LOW),
            shape_of(1, 4 * D + width),
            shape_of(D + width, D, dtype=LOW),
            *[shape_of(D, width // parts, dtype=LOW)] * parts,
        ],
        [
            pltpu.VMEM((rows, D), jnp.float32),
            pltpu.VMEM((rows, D), LOW),
            pltpu.VMEM((rows, D), jnp.float32),
            pltpu.VMEM((D, rows), LOW),
            pltpu.VMEM((rows, D), LOW),
            pltpu.VMEM((steps + 1, D, D), LOW),
            pltpu.SemaphoreType.DMA((steps + 2,)),
        ],
        "mlp_backward",
        None,
        rides,
        collective_id,
    )


def qkv_back_kernel(
    grad_ref, residual_in, stream_in, normed_ref, weight_ref, vector_ref,
    out_ref, sums_ref, weight_grad_ref,
    residual_ref, stream_ref, sum_ref, turned_ref, sems,
):
    rows = out_ref.shape[0]
    copies = loads((residual_in, stream_in), (residual_ref, stream_ref), sems)

    @at_first
    def _():
        for copy in copies:
            copy.start()
        turned_ref[...] = normed_ref[...].T
        sum_ref[...] = jnp.zeros_like(sum_ref)

    for half in halves_of(rows):
        sum_ref[half, :] += mul_nt(grad_ref[half, :], weight_ref[...])
    sums_ref[:, chunk_at(2 * D)] = column_sum(grad_ref[...])
    weight_grad_ref[...] = mul(turned_ref[...], grad_ref[...]).astype(LOW)

    @at_last
    def _():
        for copy in copies:
            copy.wait()
        totals = [0.0] * 2
        for half in halves_of(rows):
            value_grad, gain_grad, shift_grad = norm_backward(
                sum_ref[half, :], stream_ref[half, :], vector_ref[:, :D]
            )
            out_ref[half, :] = residual_ref[half, :] + value_grad
            totals = [totals[0] + gain_grad, totals[1] + shift_grad]
        sums_ref[:, : 2 * D] = jnp.concatenate(totals, 1)


def qkv_backward(grad, residual_grad, stream, normed, weight, vector, rides, collective_id):
    rows = stream.shape[0]
    whole = fixed(rows, D)
    return block_call(
        qkv_back_kernel,
        3,
        [columns_of(rows), ANYWHERE, ANYWHERE, whole, columns_of(D), fixed(1, vector.shape[1])],
        [grad, residual_grad, stream, normed, weight, vector],
        [whole, fixed(1, 5 * D), columns_of(D)],
        [shape_of(rows, D), shape_of(1, 5 * D), shape_of(D, 3 * D, dtype=LOW)],
        [
            pltpu.VMEM((rows, D), jnp.float32),
            pltpu.VMEM((rows, D), jnp.float32),
            pltpu.VMEM((rows, D), jnp.float32),
            pltpu.VMEM((D, rows), LOW),
            pltpu.SemaphoreType.DMA((2,)),
        ],
        "qkv_backward",
        None,
        rides,
        collective_id,
    )


def embed_back_kernel(pixel_ref, grad_ref, pos_ref, out_ref, table_ref, bias_ref, low_ref):
    @at_first
    def _():
        grad = grad_ref[...]
        low = grad.astype(jnp.bfloat16)
        low_ref[...] = low
        bias_ref[...] = column_sum(low)
        table_ref[...] = jnp.dot(
            pos_ref[...], grad, precision=HIGHEST, preferred_element_type=jnp.float32
        )

    out_ref[...] = mul(pixel_ref[...].T, low_ref[...]).astype(jnp.bfloat16)


def embed_backward(pixels, grad, pos_weights_t):
    rows, depth = pixels.shape
    block = 768
    nodes = pos_weights_t.shape[0]
    return block_call(
        embed_back_kernel,
        depth // block,
        [pl.BlockSpec((rows, block), lambda i: (0, i)), fixed(rows, D), fixed(nodes, rows)],
        [pixels, grad, pos_weights_t],
        [rows_of(block, D), fixed(nodes, D), fixed(1, D)],
        [shape_of(depth, D, dtype=jnp.bfloat16), shape_of(nodes, D), shape_of(1, D)],
        [pltpu.VMEM((rows, D), jnp.bfloat16)],
        "embed_backward",
        None,
    )


def head_kernel(
    stream_ref, seg_col_ref, seg_row_ref, label_ref, weight_ref, vector_ref,
    grad_ref, weight_grad_ref, sums_ref, bias_grad_ref, numbers_ref, *, classes,
):
    padded = weight_ref.shape[1]
    vector = vector_ref[...].astype(LOW).astype(jnp.float32)
    gain, shift = vector[:, D : 2 * D], vector[:, 2 * D : 3 * D]
    slots = lax.broadcasted_iota(jnp.int32, (IMGS, 1), 0)
    member = (seg_row_ref[...] == slots).astype(jnp.float32)
    counts = jnp.sum(member, 1, keepdims=True)
    sizes = jnp.maximum(counts, 1.0)
    unit, inverse = normalized(stream_ref[...])
    final = unit * gain + shift
    owner = jnp.broadcast_to(seg_col_ref[...], final.shape)
    pooled = [jnp.sum(jnp.where(owner == k, final, 0.0), 0, keepdims=True) for k in range(IMGS)]
    pooled = (jnp.concatenate(pooled, 0) / sizes).astype(LOW)
    class_at = lax.broadcasted_iota(jnp.int32, (IMGS, padded), 1)
    logits = mul(pooled, weight_ref[...]) + vector[:, 3 * D :]
    logits = jnp.where(class_at < classes, logits, MASKED)
    highest = jnp.max(logits, -1, keepdims=True)
    exponent = jnp.exp(logits - highest)
    totals = jnp.sum(exponent, -1, keepdims=True)
    onehot = class_at == label_ref[...]
    picked = jnp.sum(jnp.where(onehot, logits, 0.0), 1, keepdims=True)
    loss = jnp.sum(counts * (highest + jnp.log(totals) - picked), 0, keepdims=True)
    numbers_ref[...] = jnp.concatenate([loss, jnp.sum(counts, 0, keepdims=True)], 1)
    logits_grad = ((exponent / totals - onehot.astype(jnp.float32)) * counts).astype(LOW)
    bias_grad_ref[...] = column_sum(logits_grad)
    weight_grad_ref[...] = lax.dot_general(
        pooled, logits_grad, (((0,), (0,)), ((), ())), preferred_element_type=jnp.float32
    ).astype(LOW)
    pooled_grad = mul_nt(logits_grad, weight_ref[...]) / sizes
    own = (seg_col_ref[...] == lax.broadcasted_iota(jnp.int32, (1, IMGS), 1)).astype(LOW)
    final_grad, left = 0.0, pooled_grad
    for _ in range(3):
        term = left.astype(LOW)
        final_grad = final_grad + mul(own, term)
        left = left - term.astype(jnp.float32)
    inner = final_grad * gain
    mean_inner = jnp.mean(inner, -1, keepdims=True)
    mean_cross = jnp.mean(inner * unit, -1, keepdims=True)
    grad_ref[...] = inverse * (inner - mean_inner - unit * mean_cross)
    sums_ref[...] = jnp.concatenate([column_sum(final_grad * unit), column_sum(final_grad)], 1)


def head(stream, segment, labels, weight, global_vector, classes):
    rows = stream.shape[0]
    padded = weight.shape[1]
    vector = jnp.pad(global_vector, (0, padded - classes))[None, :]
    return pl.pallas_call(
        functools.partial(head_kernel, classes=classes),
        out_shape=[
            shape_of(rows, D),
            shape_of(D, padded, dtype=LOW),
            shape_of(1, 2 * D),
            shape_of(1, padded),
            shape_of(1, 2),
        ],
        compiler_params=pltpu.CompilerParams(vmem_limit_bytes=VMEM_LIMIT),
        cost_estimate=NO_COST,
        name="head",
    )(stream, segment[:, None], segment[None, :], labels.reshape(IMGS, 1), weight, vector)


def adam_update(gradient, moment, square, weight, factor, learn_rate):
    clipped = gradient * factor
    moment = BETA_ONE * moment + (1.0 - BETA_ONE) * clipped
    square = BETA_TWO * square + (1.0 - BETA_TWO) * clipped * clipped
    fixed_one = 1.0 - BETA_ONE**STEP
    fixed_two = 1.0 - BETA_TWO**STEP
    step_dir = (
        moment / fixed_one / (jnp.sqrt(square / fixed_two) + ADAM_EPS) + WEIGHT_DECAY * weight
    )
    return (moment, square, weight - learn_rate * step_dir)


def body(
    pixels,
    segment,
    patch_size,
    labels,
    patch_kernel,
    head_weight,
    input_proj,
    output_proj,
    layer_vector,
    position_table,
    global_vector,
    patch_moment,
    head_moment,
    input_moment,
    output_moment,
    layer_moment,
    position_moment,
    global_moment,
    patch_square,
    head_square,
    input_square,
    output_square,
    layer_square,
    position_square,
    global_square,
):
    owners = lax.axis_size("fsdp")
    nodes = position_table.shape[0]
    vector_size = layer_vector.size
    stream, pos_weights_t, vectors, qkv_weight, up_zero, rides, rest_shards, first_rows = begin(
        pixels,
        segment,
        patch_size,
        patch_kernel,
        layer_vector,
        input_proj,
        output_proj,
        head_weight,
        position_table,
        global_vector,
    )
    qkv_one, up_one, head_full = (
        lax.all_gather(shard, "fsdp", axis=0, tiled=True) for shard in rest_shards
    )
    saved_layers = []
    for index in range(LAYERS):
        vector = vectors[index]
        if index:
            normed, qkv_rows = qkv_forward(stream, qkv_weight, vector)
        else:
            normed, qkv_rows = first_rows
        if index == 0:
            attended, expo, inverse, output, output_ride = attention_forward(
                qkv_rows, segment, rides, 4
            )
            up = up_zero
        else:
            attended, expo, inverse = attention_forward(qkv_rows, segment, (), 5)
            up, output = up_one, output_one
        residual, normed_second, active, slope, following, *fetched = mlp_forward(
            stream, attended, up, output, vector, () if index else [output_ride], 5
        )
        saved_layers.append(
            (
                (qkv_weight, up, output, vector),
                (stream, normed, qkv_rows, attended, expo, inverse),
                (residual, normed_second, active, slope),
            )
        )
        stream, qkv_weight = following, qkv_one
        if fetched:
            (output_one,) = fetched
    stream_grad, head_grad, final_sums, head_bias_grad, numbers = head(
        stream, segment, labels, head_full, global_vector, head_weight.shape[1]
    )
    vector_grads = [None] * LAYERS
    for index in reversed(range(LAYERS)):
        (qkv_weight, up, output, vector), first, second = saved_layers[index]
        entering, normed, qkv_rows, attended, expo, inverse = first
        residual, normed_second, active, slope = second
        residual_grad, attended_grad, mlp_sums, output_grad, *brought = mlp_backward(
            stream_grad,
            slope,
            residual,
            normed_second,
            active,
            attended,
            up,
            output,
            vector,
            2 if index else 1,
            () if index else [output_rest],
            9,
        )
        if index:
            attended_grad, *up_parts = lax.optimization_barrier((attended_grad, *brought))
            one_parts = [scatter(by_owner(part)) for part in up_parts]
        else:
            up_grad, output_one_sum = brought
            attended_grad, output_grad = lax.optimization_barrier((attended_grad, output_grad))
            output_zero_part = scatter(by_owner(output_grad))
        qkv_grad, rest, *head_sums = attention_backward(
            qkv_rows,
            expo,
            inverse,
            attended,
            attended_grad,
            [
                LeadRide(by_owner(output_grad if index else up_grad)),
                *([SumRide(by_owner(head_grad), False)] if index else []),
            ],
            6 if index else 8,
        )
        stream_grad, qkv_sums, qkv_weight_grad, *brought = qkv_backward(
            qkv_grad,
            residual_grad,
            entering,
            normed,
            qkv_weight,
            vector,
            () if index else [rest, *[ShareRide(part) for part in one_parts]],
            7,
        )
        if index:
            output_rest, (head_sum,) = rest, head_sums
            stream_grad, qkv_weight_grad = lax.optimization_barrier((stream_grad, qkv_weight_grad))
            one_parts.append(scatter(by_owner(qkv_weight_grad)))
        else:
            up_zero_sum, *up_one_sums, qkv_one_sum = brought
        vector_grads[index] = jnp.concatenate(
            [
                qkv_sums[0, : 2 * D],
                mlp_sums[0, : 2 * D],
                qkv_sums[0, 2 * D :],
                mlp_sums[0, 2 * D :],
            ]
        )
    kernel_grad, position_grad, bias_grad = embed_backward(pixels, stream_grad, pos_weights_t)
    position_grad = position_grad[:nodes]
    vector_part = jnp.stack(vector_grads).reshape(LAYERS, owners, -1)
    vector_part = jnp.swapaxes(vector_part, 0, 1).reshape(owners, vector_size)
    vector_rows = -(-vector_size // LANES)
    vector_part = jnp.pad(vector_part, ((0, 0), (0, vector_rows * LANES - vector_size)))
    rest = jnp.concatenate(
        [
            position_grad.reshape(-1),
            bias_grad[0],
            final_sums[0],
            head_bias_grad[0, :CLS],
            numbers[0],
        ]
    )
    rest_rows = -(-rest.shape[0] // (owners * LANES))
    rest_part = jnp.pad(rest, (0, rest_rows * owners * LANES - rest.shape[0]))
    small = jnp.concatenate([vector_part, rest_part.reshape(owners, -1)], 1)
    used = vector_rows + rest_rows
    block_rows = (used // 64 + 1) * 64
    small = jnp.pad(small.reshape(owners, used, LANES), ((0, 0), (0, block_rows - used), (0, 0)))
    (
        qkv_zero_sum,
        kernel_sum,
        small_share,
        output_zero_sum,
        small_full,
        numbers,
    ) = reduce_all(
        [by_owner(qkv_weight_grad), by_owner(kernel_grad)],
        small,
        [output_zero_part],
        [head_sum, output_one_sum, up_zero_sum, *up_one_sums, qkv_one_sum],
        vector_rows,
        rest.shape[0],
        2,
    )
    factor, grad_norm, loss_sum, token_total = (numbers[0, index] for index in range(4))
    rest_sum = small_full[:, vector_rows:used].reshape(-1)
    position_sum = rest_sum[: position_grad.size].reshape(position_grad.shape)
    global_sum = rest_sum[position_grad.size :][: global_vector.shape[0]]
    kernel_sum = kernel_sum.astype(jnp.float32)
    head_sum = head_sum[:, :CLS].astype(jnp.float32)
    input_sum = jnp.stack(
        [
            jnp.concatenate(parts, 1)
            for parts in ((qkv_zero_sum, up_zero_sum), (qkv_one_sum, *up_one_sums))
        ]
    ).astype(jnp.float32)
    output_sum = jnp.stack([output_zero_sum, output_one_sum]).astype(
        jnp.float32
    )
    vector_sum = small_share[:vector_rows].reshape(-1)[:vector_size].reshape(layer_vector.shape)
    patch_next = adam_update(
        kernel_sum, patch_moment, patch_square, patch_kernel, factor, LEARN_RATE
    )
    head_next = adam_update(head_sum, head_moment, head_square, head_weight, factor, LEARN_RATE)
    input_next = adam_update(input_sum, input_moment, input_square, input_proj, factor, LEARN_RATE)
    output_next = adam_update(
        output_sum, output_moment, output_square, output_proj, factor, LEARN_RATE
    )
    layer_next = adam_update(
        vector_sum, layer_moment, layer_square, layer_vector, factor, VECTOR_RATE
    )
    position_next = adam_update(
        position_sum, position_moment, position_square, position_table, factor, LEARN_RATE
    )
    global_next = adam_update(
        global_sum, global_moment, global_square, global_vector, factor, VECTOR_RATE
    )
    return (
        loss_sum,
        token_total,
        grad_norm,
        patch_next[0],
        head_next[0],
        input_next[0],
        output_next[0],
        layer_next[0],
        position_next[0],
        global_next[0],
        patch_next[1],
        head_next[1],
        input_next[1],
        output_next[1],
        layer_next[1],
        position_next[1],
        global_next[1],
        patch_next[2],
        head_next[2],
        input_next[2],
        output_next[2],
        layer_next[2],
        position_next[2],
        global_next[2],
    )


def solution(mesh):
    in_specs = (
        P(("dp", "fsdp"), None),
        P(("dp", "fsdp")),
        P(("dp", "fsdp"), None),
        P(("dp", "fsdp"), None),
        P("fsdp", None),
        P("fsdp", None),
        P(None, "fsdp", None),
        P(None, "fsdp", None),
        P(None, "fsdp"),
        P(),
        P(),
        P("fsdp", None),
        P("fsdp", None),
        P(None, "fsdp", None),
        P(None, "fsdp", None),
        P(None, "fsdp"),
        P(),
        P(),
        P("fsdp", None),
        P("fsdp", None),
        P(None, "fsdp", None),
        P(None, "fsdp", None),
        P(None, "fsdp"),
        P(),
        P(),
    )
    out_specs = (
        P(),
        P(),
        P(),
        P("fsdp", None),
        P("fsdp", None),
        P(None, "fsdp", None),
        P(None, "fsdp", None),
        P(None, "fsdp"),
        P(),
        P(),
        P("fsdp", None),
        P("fsdp", None),
        P(None, "fsdp", None),
        P(None, "fsdp", None),
        P(None, "fsdp"),
        P(),
        P(),
        P("fsdp", None),
        P("fsdp", None),
        P(None, "fsdp", None),
        P(None, "fsdp", None),
        P(None, "fsdp"),
        P(),
        P(),
    )
    return jax.shard_map(body, mesh=mesh, in_specs=in_specs, out_specs=out_specs, check_vma=False)
```

```python
import functools

import jax
import jax.numpy as jnp
from jax import lax
from jax.experimental import pallas as pl
from jax.experimental.pallas import tpu as pltpu
from jax.sharding import PartitionSpec as P

D = 768
HEADS = 12
HD = 64
CLS = 1000
GRID = 7
IMG = 240
IMGS = 8
LAYERS = 2
STEP = 3


NORM_EPS = 1e-06
CLIP_NORM = 0.01
LEARN_RATE = 0.05
VECTOR_RATE = 0.25
BETA_ONE = 0.5
BETA_TWO = 0.5
ADAM_EPS = 1e-08
WEIGHT_DECAY = 0.05
HIGHEST = lax.Precision.HIGHEST

PAIR = 2 * HD
MASKED = -1e30
MIB = 1024 * 1024
VMEM_LIMIT = 56 * MIB
MESH = pl.DeviceIdType.MESH
LANES = 128
LOW = jnp.bfloat16
ANYWHERE = pl.BlockSpec(memory_space=pl.ANY)
NO_COST = pl.CostEstimate(flops=0, bytes_accessed=0, transcendentals=0)
ROOT = 0.7978845608028654
CUBE = 0.044715
NT = (((1,), (1,)), ((), ()))


def layer_norm(values, gain, shift):
    center = values - jnp.mean(values, -1, keepdims=True)
    spread = jnp.mean(center * center, -1, keepdims=True)
    return center * lax.rsqrt(spread + NORM_EPS) * gain + shift


def rounded(values):
    return lax.optimization_barrier(values.astype(jnp.bfloat16)).astype(jnp.float32)


def matmul(left, right):
    return jnp.dot(left, right, preferred_element_type=jnp.float32)


def padded_rows(flat, multiple):
    extra = -flat.shape[0] % (multiple * LANES)
    return jnp.pad(flat, (0, extra)).reshape(-1, LANES)


def row_layout(seg_row, patch_row):
    row_count = seg_row.shape[0]
    slots = jnp.arange(IMGS, dtype=jnp.int32)
    member = seg_row[:, None] == slots[None, :]
    counts = jnp.sum(member.astype(jnp.int32), 0, dtype=jnp.int32)
    starts = jnp.cumsum(counts, dtype=jnp.int32) - counts
    inside = jnp.any(member, 1)
    offset = jnp.arange(row_count, dtype=jnp.int32) - jnp.sum(
        jnp.where(member, starts[None, :], 0), 1, dtype=jnp.int32
    )
    offset = jnp.where(inside, offset, 0)
    patch_tok = jnp.sum(jnp.where(member, patch_row[None, :], 0), 1, dtype=jnp.int32) + jnp.where(
        inside, 0, IMG
    )
    side = IMG // patch_tok
    nodes = jnp.arange(GRID, dtype=jnp.int32).astype(jnp.float32)

    def hat(coord):
        place = ((2 * coord + 1) * GRID).astype(jnp.float32) / (2 * side).astype(jnp.float32) - 0.5
        place = jnp.clip(place, 0.0, GRID - 1.0)
        return jnp.maximum(1.0 - jnp.abs(place[:, None] - nodes[None, :]), 0.0)

    weights = (hat(offset // side)[:, :, None] * hat(offset % side)[:, None, :]).reshape(
        row_count, GRID * GRID
    )
    return (weights, member.astype(jnp.float32), counts.astype(jnp.float32))


TURNS = (1, 2, 3)


def place():
    slot = lax.axis_index("fsdp")
    return lax.axis_index("dp"), lax.div(slot, 2), lax.rem(slot, 2)


def partner(index, turn):
    if turn == 0:
        return index
    if turn == 1:
        return index + 1 - 2 * lax.rem(index, 2)
    if turn == 2:
        return lax.rem(index + 2, 4)
    return 3 - index


def greet():
    group, level, core = place()
    barrier = pltpu.get_barrier_semaphore()
    peers = [(group, 2 * level + 1 - core)]
    for turn in TURNS:
        peers.append((group, 2 * partner(level, turn) + core))
        peers.append((partner(group, turn), 2 * level + core))
    for peer in peers:
        pl.semaphore_signal(barrier, inc=1, device_id=peer, device_id_type=MESH)
    pl.semaphore_wait(barrier, len(peers))


def quarter_shape(rows, columns):
    if columns % (2 * LANES) == 0:
        return rows // 2, columns // 2
    return rows // 4, columns


def quarter(index, rows, columns):
    high, wide = quarter_shape(rows, columns)
    if wide == columns:
        return pl.ds(pl.multiple_of(index * high, high), high), pl.ds(0, columns)
    return (
        pl.ds(pl.multiple_of(lax.div(index, 2) * high, high), high),
        pl.ds(pl.multiple_of(lax.rem(index, 2) * wide, wide), wide),
    )


def remote(source, target, send, receive, device):
    return pltpu.make_async_remote_copy(
        src_ref=source,
        dst_ref=target,
        send_sem=send,
        recv_sem=receive,
        device_id=device,
        device_id_type=MESH,
    )


GATHER_SEMS = 39


def relay_rows(part, rows):
    cut = -(-rows // 32) * 16
    return (0, cut) if part == 0 else (cut, rows - cut)


class Relay:
    def region(self, turn, index):
        _, level, core = place()
        block = self.out.at[2 * partner(level, turn) + core]
        return block.at[quarter(index, *self.shard.shape)]

    def group_copy(self, turn, other):
        group, level, core = place()
        index = self.group_at + 2 * (turn - 1) + other - 1
        peer = (partner(group, other), 2 * level + core)
        target = self.region(turn, group)
        source = self.quarter_source(turn, target)
        return remote(source, target, self.sems.at[index], self.sems.at[index + 6], peer)

    def relay_copy(self, turn, part):
        group, level, core = place()
        first, count = relay_rows(part, quarter_shape(*self.shard.shape)[0])
        block = self.region(turn, partner(group, 1 + part)).at[pl.ds(first, count)]
        index = self.relay_at + 2 * (turn - 1) + part
        peer = (partner(group, 2 - part), 2 * level + core)
        return remote(block, block, self.sems.at[index], self.sems.at[index + 6], peer)

    def relay(self):
        for turn in TURNS:
            for part in range(2):
                self.group_copy(turn, 1 + part).wait_recv()
                self.relay_copy(turn, part).start()

    def wait_quarters(self, turn):
        for part in range(2):
            self.relay_copy(turn, part).wait_recv()

    def wait_passed(self):
        for turn in TURNS:
            for part in range(2):
                self.group_copy(turn, 1 + part).wait_send()
                self.relay_copy(turn, part).wait_send()


class Gather(Relay):
    group_at, relay_at = 7, 19

    def __init__(self, shard, out, sems, split, in_place=False):
        self.shard, self.out, self.sems, self.split = shard, out, sems, split
        self.in_place = in_place
        self.rows, self.columns = shard.shape

    def quarter_source(self, turn, target):
        return target

    def level_copy(self, turn):
        group, level, core = place()
        block = self.out.at[2 * level + core]
        source = self.shard
        if self.split:
            part = quarter(group, self.rows, self.columns)
            source, block = source.at[part], block.at[part]
        peer = (group, 2 * partner(level, turn) + core)
        return remote(source, block, self.sems.at[turn], self.sems.at[3 + turn], peer)

    def core_copy(self, turn):
        group, level, core = place()
        slot = 2 * partner(level, turn) + core
        source = self.shard if turn == 0 else self.out.at[slot]
        peer = (group, 2 * level + 1 - core)
        return remote(source, self.out.at[slot], self.sems.at[31 + turn], self.sems.at[35 + turn], peer)

    def own_copy(self):
        _, level, core = place()
        return pltpu.make_async_copy(self.shard, self.out.at[2 * level + core], self.sems.at[0])

    def first(self):
        for turn in TURNS:
            self.level_copy(turn).start()
        self.core_copy(0).start()
        if not self.in_place:
            self.own_copy().start()

    def second(self):
        for turn in TURNS:
            self.level_copy(turn).wait_recv()
            if self.split:
                for other in (1, 2):
                    self.group_copy(turn, other).start()
            else:
                self.core_copy(turn).start()

    def third(self, use=None):
        for turn in TURNS if self.split else ():
            self.wait_quarters(turn)
            self.core_copy(turn).start()
            if use is not None:
                use(turn, True)

    def fourth(self, use=None):
        for turn in TURNS if use is not None else (0, *TURNS):
            self.core_copy(turn).wait_recv()
            if use is not None:
                use(turn, False)
        for turn in TURNS:
            self.level_copy(turn).wait_send()
        if self.split:
            self.wait_passed()
        for turn in (0, *TURNS):
            self.core_copy(turn).wait_send()
        if not self.in_place:
            self.own_copy().wait()


class LevelGather:
    def __init__(self, shard, out, sems):
        self.shard, self.out, self.sems = shard, out, sems

    def level_copy(self, turn):
        group, level, core = place()
        return remote(
            self.shard.at[quarter(group, *self.shard.shape)],
            self.out.at[level],
            self.sems.at[turn],
            self.sems.at[3 + turn],
            (group, 2 * partner(level, turn) + core),
        )

    def first(self):
        for turn in TURNS:
            self.level_copy(turn).start()

    def second(self):
        pass

    def third(self):
        pass

    def fourth(self):
        for turn in TURNS:
            self.level_copy(turn).wait_recv()
            self.level_copy(turn).wait_send()

    def store(self):
        _, level, _ = place()
        self.out[level] = jnp.zeros(self.out.shape[1:], self.out.dtype)
        self.target[...] = self.out[...]


GROUP_GATHER_SEMS = 36


class GroupGather(Relay):
    group_at, relay_at = 4, 16

    def __init__(self, shard, quarters, out, sems):
        self.shard, self.quarters, self.out, self.sems = shard, quarters, out, sems

    def quarter_source(self, turn, target):
        _, level, _ = place()
        return self.quarters.at[partner(level, turn)]

    def own_copy(self, turn):
        group, level, core = place()
        if turn == 0:
            source, target = self.shard, self.out.at[2 * level + core]
        else:
            source, target = self.quarters.at[partner(level, turn)], self.region(turn, group)
        return pltpu.make_async_copy(source, target, self.sems.at[turn])

    def core_copy(self, turn):
        group, level, core = place()
        slot = 2 * partner(level, turn) + core
        source = self.shard if turn == 0 else self.out.at[slot]
        peer = (group, 2 * level + 1 - core)
        return remote(source, self.out.at[slot], self.sems.at[28 + turn], self.sems.at[32 + turn], peer)

    def first(self):
        for turn in TURNS:
            for other in (1, 2):
                self.group_copy(turn, other).start()
        for turn in (0, *TURNS):
            self.own_copy(turn).start()
        self.core_copy(0).start()

    def third(self):
        for turn in TURNS:
            self.wait_quarters(turn)
            self.own_copy(turn).wait()
            self.core_copy(turn).start()

    def fourth(self):
        for turn in (0, *TURNS):
            self.core_copy(turn).wait_recv()
            self.core_copy(turn).wait_send()
        self.wait_passed()
        self.own_copy(0).wait()

    def store(self):
        copy = pltpu.make_async_copy(self.out, self.target, self.sems.at[0])
        copy.start()
        copy.wait()


class LevelRide:
    def __init__(self, shard):
        self.operands = [shard]
        self.in_specs = [fixed(*shard.shape)]
        shape = (4, *quarter_shape(*shard.shape))
        self.out_specs = [fixed(*shape)]
        self.out_shapes = [jax.ShapeDtypeStruct(shape, shard.dtype)]
        self.scratch = [pltpu.VMEM(shape, shard.dtype), pltpu.SemaphoreType.DMA((7,))]

    def job(self, sources, targets, scratch):
        job = LevelGather(sources[0], *scratch)
        job.target = targets[0]
        return job

    def before(self, steps):
        return {0: ("first",)}

    after = ("fourth", "store")

    def result(self, outs):
        return GatherRide(self.operands[0], outs[0])

    def plain(self):
        return GatherRide(self.operands[0], self.operands[0])


class GatherRide:
    def __init__(self, shard, quarters):
        owners = lax.axis_size("fsdp")
        full = (owners, *shard.shape)
        self.operands = [shard, quarters]
        self.in_specs = [fixed(*shard.shape), fixed(*quarters.shape)]
        self.out_specs = [ANYWHERE]
        self.out_shapes = [jax.ShapeDtypeStruct(full, shard.dtype)]
        self.scratch = [
            pltpu.VMEM(full, shard.dtype),
            pltpu.SemaphoreType.DMA((GROUP_GATHER_SEMS,)),
        ]

    def job(self, sources, targets, scratch):
        job = GroupGather(*sources, *scratch)
        job.target = targets[0]
        return job

    def before(self, steps):
        return {0: ("first",), steps // 2: ("relay",), steps - 1: ("third",)}

    after = ("fourth", "store")

    def result(self, outs):
        return outs[0].reshape(-1, outs[0].shape[2])

    def plain(self):
        return lax.all_gather(self.operands[0], "fsdp", axis=0, tiled=True)


class ShareRide:
    def __init__(self, share):
        self.operands = [share]
        self.in_specs = [ANYWHERE]
        self.out_specs = [fixed(*share.shape)]
        self.out_shapes = [jax.ShapeDtypeStruct(share.shape, share.dtype)]
        self.scratch = [
            pltpu.VMEM(share.shape, share.dtype),
            *share_scratch(share),
            pltpu.SemaphoreType.DMA((GROUP_SEMS,)),
        ]

    def job(self, sources, targets, scratch):
        job = GroupReduce(sources[0], scratch[0], scratch[1:3], scratch[3])
        job.target = targets[0]
        return job

    def before(self, steps):
        return {0: ("first", "second"), max(1, steps // 2): ("third",)}

    after = ("fifth", "sixth", "store")

    def result(self, outs):
        return outs[0]

    def plain(self):
        return lax.psum(self.operands[0], "dp")


class SumRide:
    def __init__(self, grad, large):
        block = grad.shape[1:]
        self.large = large
        self.operands = [grad]
        self.in_specs = [ANYWHERE]
        self.out_specs = [fixed(*block)]
        self.out_shapes = [jax.ShapeDtypeStruct(block, grad.dtype)]
        buffers = stepped_scratch(grad) if large else whole_scratch(grad)
        sems = WHOLE_SEMS if large else REDUCE_SEMS
        self.scratch = [pltpu.VMEM(block, grad.dtype), *buffers, pltpu.SemaphoreType.DMA((sems,))]

    def job(self, sources, targets, scratch):
        job = (Whole if self.large else Reduce)(sources[0], scratch[0], scratch[1:-1], scratch[-1])
        job.target = targets[0]
        return job

    def before(self, steps):
        if self.large:
            return {0: ("first",), 1: ("second",), steps - 2: ("between",), steps - 1: ("third",)}
        return {0: ("first",), 1: ("second",), steps // 2: ("third",), steps - 1: ("fourth",)}

    @property
    def after(self):
        return (("fourth",) if self.large else ()) + ("fifth", "sixth", "store")

    def result(self, outs):
        return outs[0]

    def plain(self):
        return lax.psum(scatter(self.operands[0]), "dp")


class LeadRide:
    after = ("third", "sixth", "store")

    def __init__(self, grad):
        _, rows, columns = grad.shape
        shape = (4, rows // 2, columns // 2)
        self.operands = [grad]
        self.in_specs = [ANYWHERE]
        self.out_specs = [fixed(*shape)]
        self.out_shapes = [jax.ShapeDtypeStruct(shape, grad.dtype)]
        self.scratch = [*stepped_scratch(grad), pltpu.SemaphoreType.DMA((WHOLE_SEMS,))]

    def job(self, sources, targets, scratch):
        job = Lead(sources[0], None, scratch[:-1], scratch[-1])
        job.target = targets[0]
        return job

    def before(self, steps):
        return {0: ("first",), 1: ("second",), steps - 2: ("between",)}

    def result(self, outs):
        return RestRide(outs[0])

    def plain(self):
        return RestRide(self.operands[0])


class RestRide:
    after = ("fifth", "sixth", "store")

    def __init__(self, part):
        _, high, wide = part.shape
        block = (2 * high, 2 * wide)
        self.operands = [part]
        self.in_specs = [fixed(*part.shape)]
        self.out_specs = [fixed(*block)]
        self.out_shapes = [jax.ShapeDtypeStruct(block, part.dtype)]
        self.scratch = [
            pltpu.VMEM(block, part.dtype),
            pltpu.VMEM((3, high, wide), part.dtype),
            pltpu.SemaphoreType.DMA((WHOLE_SEMS,)),
        ]

    def job(self, sources, targets, scratch):
        job = Rest(sources[0], *scratch)
        job.target = targets[0]
        return job

    def before(self, steps):
        return {0: ("first",), steps - 1: ("fourth",)}

    def result(self, outs):
        return outs[0]

    def plain(self):
        return lax.psum(scatter(self.operands[0]), "dp")


def riding(body, counts, rides, steps):
    def kernel(*refs):
        refs = list(refs)

        def pop(count):
            taken = refs[:count]
            del refs[:count]
            return taken

        own = pop(counts[0])
        sources = [pop(len(ride.operands)) for ride in rides]
        own += pop(counts[1])
        targets = [pop(len(ride.out_shapes)) for ride in rides]
        own += pop(counts[2])
        jobs = [
            ride.job(source, target, pop(len(ride.scratch)))
            for ride, source, target in zip(rides, sources, targets)
        ]
        for step in range(steps):
            planned = [
                (job, stages)
                for ride, job in zip(rides, jobs)
                for at, stages in ride.before(steps).items()
                if at == step
            ]
            if planned:

                @pl.when(pl.program_id(0) == step)
                def _(planned=planned, step=step):
                    if step == 0:
                        greet()
                    for job, stages in planned:
                        run_stages([job], stages)

        body(*own)

        @pl.when(pl.program_id(0) == steps - 1)
        def _():
            for ride, job in zip(rides, jobs):
                run_stages([job], ride.after)

    return kernel


def block_call(
    body, grid, in_specs, operands, out_specs, out_shape, scratch, name,
    cost=None, rides=(), collective_id=None,
):
    plain = []
    if rides and not with_kernels():
        plain, rides = [ride.plain() for ride in rides], ()
    transfer = {}
    kernel = body
    if rides:
        transfer = {"collective_id": collective_id, "has_side_effects": True}
        kernel = riding(body, (len(operands), len(out_shape), len(scratch)), rides, grid)
    count = len(out_shape)
    for ride in rides:
        operands = [*operands, *ride.operands]
        in_specs = [*in_specs, *ride.in_specs]
        out_specs, out_shape = [*out_specs, *ride.out_specs], [*out_shape, *ride.out_shapes]
        scratch = [*scratch, *ride.scratch]
    outs = pl.pallas_call(
        kernel,
        grid=(grid,),
        in_specs=in_specs,
        out_specs=out_specs,
        out_shape=out_shape,
        scratch_shapes=scratch,
        compiler_params=pltpu.CompilerParams(vmem_limit_bytes=VMEM_LIMIT, **transfer),
        cost_estimate=cost or NO_COST,
        name=name,
    )(*operands)
    brought, outs = list(outs[count:]), list(outs[:count])
    for ride in rides:
        plain.append(ride.result(brought[: len(ride.out_shapes)]))
        brought = brought[len(ride.out_shapes) :]
    return outs + plain


def work(flops, size):
    return pl.CostEstimate(flops=flops, bytes_accessed=size, transcendentals=0)


def position_weights(seg_col, patch_row, nodes):
    rows = seg_col.shape[0]
    slot = lax.broadcasted_iota(jnp.int32, (rows, IMGS), 1)
    member = seg_col == slot
    counts = jnp.sum(member.astype(jnp.float32), 0, keepdims=True)
    start = jnp.sum(jnp.where(slot < seg_col, counts, 0.0), 1, keepdims=True)
    token = lax.broadcasted_iota(jnp.int32, (rows, 1), 0).astype(jnp.float32)
    inside = seg_col < IMGS
    offset = jnp.where(inside, token - start, 0.0)
    patch = jnp.sum(jnp.where(member, patch_row.astype(jnp.float32), 0.0), 1, keepdims=True)
    side = jnp.where(inside, jnp.floor(IMG / jnp.where(inside, patch, 1.0) + 0.5), 1.0)
    line = jnp.floor((offset + 0.5) / side)
    column = offset - line * side

    def spot(coord):
        return jnp.clip((2.0 * coord + 1.0) * GRID / (2.0 * side) - 0.5, 0.0, GRID - 1.0)

    node = lax.broadcasted_iota(jnp.int32, (rows, LANES), 1).astype(jnp.float32)
    across = jnp.floor((node + 0.5) / GRID)
    along = node - across * GRID
    weights = jnp.maximum(1.0 - jnp.abs(spot(line) - across), 0.0)
    weights = weights * jnp.maximum(1.0 - jnp.abs(spot(column) - along), 0.0)
    return jnp.where(node < nodes, weights, 0.0)


def first_kernel(*refs, spots):
    kernel, vectors, inputs, outputs, head, pixels, seg_col, patch_row, table, biases = refs[:10]
    stream, pos_t, vector_zero, vector_one = refs[10:14]
    qkv_full, up_full, output_level = refs[14:17]
    output_zero, qkv_one, up_one, output_one, head_low, normed, qkv_rows = refs[17:24]
    wide_kernel, wide_inputs, wide_outputs, wide_head, pixel_rows, table_low = refs[24:30]
    kernel_full, qkv_zero, vectors_full, qkv_landing, up_landing, output_landing = refs[30:36]
    up_zero, load_sems, sems = refs[36:]
    _, level, core = place()
    mine = 2 * level + core
    pairs = [
        (kernel, wide_kernel),
        (inputs.at[0], wide_inputs.at[0]),
        (pixels, pixel_rows),
        (inputs.at[1], wide_inputs.at[1]),
        (outputs.at[0], wide_outputs.at[0]),
        (outputs.at[1], wide_outputs.at[1]),
        (head, wide_head),
    ]
    copies = [
        pltpu.make_async_copy(source, target, load_sems.at[index])
        for index, (source, target) in enumerate(pairs)
    ]
    for copy in copies:
        copy.start()
    patch_job = Gather(kernel_full.at[mine], kernel_full, sems.at[0], True, in_place=True)
    vector_job = Gather(vectors, vectors_full, sems.at[1], False)
    qkv_job = Gather(qkv_zero, qkv_landing, sems.at[2], True)
    up_job = Gather(up_zero, up_landing, sems.at[3], True)
    output_job = LevelGather(output_zero, output_landing, sems.at[4])
    output_job.target = output_level
    copies[0].wait()
    kernel_full[mine] = wide_kernel[...].astype(LOW)
    greet()
    patch_job.first()
    vector_job.first()
    copies[1].wait()
    qkv_zero[...] = wide_inputs[0, :, : 3 * D].astype(LOW)
    qkv_job.first()
    up_zero[...] = wide_inputs[0, :, 3 * D :].astype(LOW)
    up_job.first()
    copies[4].wait()
    output_zero[...] = wide_outputs[0].astype(LOW)
    output_job.first()

    weights = position_weights(seg_col[...], patch_row[...], table.shape[0])
    pos_t[...] = weights.T[: pos_t.shape[0], :]
    table_low[...] = jnp.zeros_like(table_low)
    table_low[: table.shape[0], :] = table[...].astype(LOW).astype(jnp.float32)
    bias = biases[:, :D].astype(LOW).astype(jnp.float32)
    stream[...] = bias + jnp.dot(
        weights, table_low[...], precision=HIGHEST, preferred_element_type=jnp.float32
    )
    copies[2].wait()
    depth = wide_kernel.shape[0]

    def add_block(slot):
        columns = pl.ds(pl.multiple_of(slot * depth, depth), depth)

        def add(step, carry):
            rows = pl.ds(pl.multiple_of(step * 256, 256), 256)
            stream[rows, :] += mul(pixel_rows[rows, columns], kernel_full[slot])
            return carry

        lax.fori_loop(0, stream.shape[0] // 256, add, 0)

    def use(turn, own_core):
        add_block(2 * partner(level, turn) + (core if own_core else 1 - core))

    add_block(mine)
    patch_job.second()
    qkv_job.second()
    vector_job.second()
    patch_job.core_copy(0).wait_recv()
    use(0, False)
    copies[3].wait()
    qkv_one[...] = wide_inputs[1, :, : 3 * D].astype(LOW)
    up_one[...] = wide_inputs[1, :, 3 * D :].astype(LOW)
    patch_job.relay()
    copies[5].wait()
    output_one[...] = wide_outputs[1].astype(LOW)
    copies[6].wait()
    head_low[...] = jnp.zeros_like(head_low)
    head_low[:, : head.shape[1]] = wide_head[...].astype(LOW)
    patch_job.third(use)
    qkv_job.relay()
    up_job.second()
    patch_job.fourth(use)
    qkv_job.third()
    vector_job.third()
    vector_job.fourth()
    blocks = [vectors_full[slot].astype(jnp.float32) for slot in range(vectors_full.shape[0])]
    span = vectors.shape[0] // LAYERS
    for layer, out in enumerate((vector_zero, vector_one)):
        for row in range(out.shape[1] // LANES):
            parts = [
                block[layer * span + row - spot : layer * span + row - spot + 1, :]
                for block, spot in zip(blocks, spots)
                if 0 <= row - spot < span
            ]
            out[:, row * LANES : (row + 1) * LANES] = sum(parts)
    up_job.relay()
    up_job.third()
    qkv_job.fourth()
    copy = pltpu.make_async_copy(qkv_landing, qkv_full, load_sems.at[0])
    copy.start()
    weight = qkv_landing[...].reshape(-1, qkv_landing.shape[2])
    for half in halves_of(stream.shape[0]):
        unit, _ = normalized(stream[half, :])
        low = (unit * vector_zero[:, :D] + vector_zero[:, D : 2 * D]).astype(LOW)
        normed[half, :] = low
        for base in range(0, 3 * D, D):
            bias = vector_zero[:, 4 * D + base : 5 * D + base]
            qkv_rows[half, base : base + D] = (mul(low, weight[:, base : base + D]) + bias).astype(LOW)
    up_job.fourth()
    up_copy = pltpu.make_async_copy(up_landing, up_full, load_sems.at[1])
    up_copy.start()
    run_stages([output_job], ("fourth", "store"))
    copy.wait()
    up_copy.wait()


def padded_vectors(shard):
    layers, width = shard.shape
    owners = lax.axis_size("fsdp")
    spots = [owner * width // LANES for owner in range(owners)]
    span = max(-(-(owner + 1) * width // LANES) - spot for owner, spot in enumerate(spots))
    span += -span % 16
    shift = lax.rem(lax.axis_index("fsdp") * width, LANES)
    padded = jnp.zeros((layers, span * LANES), LOW)
    padded = lax.dynamic_update_slice(padded, shard.astype(LOW), (0, shift))
    return padded.reshape(layers * span, LANES), spots


def begin(
    pixels, segment, patch_size, patch_kernel, layer_vector, input_proj, output_proj, head_weight,
    position_table, global_vector,
):
    classes = head_weight.shape[1] + -head_weight.shape[1] % LANES
    nodes = position_table.shape[0] + -position_table.shape[0] % 64
    if not with_kernels():
        inputs = [
            (input_proj[index, :, : 3 * D].astype(LOW), input_proj[index, :, 3 * D :].astype(LOW))
            for index in range(LAYERS)
        ]
        outputs = [output_proj[index].astype(LOW) for index in range(LAYERS)]
        gather = lambda shard, axis: lax.all_gather(shard, "fsdp", axis=axis, tiled=True)
        weights, _, _ = row_layout(segment, patch_size[0])
        weights = jnp.pad(weights, ((0, 0), (0, nodes - weights.shape[1])))
        table = jnp.pad(rounded(position_table), ((0, nodes - position_table.shape[0]), (0, 0)))
        bias = rounded(global_vector)[None, :D]
        stream = embed(pixels, gather(patch_kernel.astype(LOW), 0), weights, table, bias)
        vectors = gather(layer_vector.astype(LOW), 1).astype(jnp.float32)
        head = jnp.pad(head_weight.astype(LOW), ((0, 0), (0, classes - head_weight.shape[1])))
        return (
            stream,
            weights.T,
            [vectors[index : index + 1] for index in range(LAYERS)],
            gather(inputs[0][0], 0),
            gather(inputs[0][1], 0),
            [GatherRide(outputs[0], outputs[0]), LevelRide(outputs[1])],
            [*inputs[1], head],
            qkv_forward(stream, gather(inputs[0][0], 0), vectors[:1]),
        )
    rows = pixels.shape[0]
    owners = lax.axis_size("fsdp")
    vectors, spots = padded_vectors(layer_vector)
    depth = input_proj.shape[1]
    up_shape = (depth, input_proj.shape[2] - 3 * D)
    qkv_shape, out_shape = (depth, 3 * D), output_proj.shape[1:]
    low = lambda *shape: jax.ShapeDtypeStruct(shape, LOW)
    levels = lambda shape: low(4, *quarter_shape(*shape))
    width = layer_vector.shape[1] * owners
    shapes = [
        shape_of(rows, D),
        shape_of(nodes, rows),
        shape_of(1, width),
        shape_of(1, width),
        low(owners, *qkv_shape),
        low(owners, *up_shape),
        levels(out_shape),
        low(*out_shape),
        low(*qkv_shape),
        low(*up_shape),
        low(*out_shape),
        low(head_weight.shape[0], classes),
        low(rows, D),
        low(rows, 3 * D),
    ]
    wide = (patch_kernel, input_proj, output_proj, head_weight, pixels)
    in_vmem = pl.BlockSpec(memory_space=pltpu.VMEM)
    results = pl.pallas_call(
        functools.partial(first_kernel, spots=spots),
        in_specs=[ANYWHERE] * 6 + [in_vmem] * 4,
        out_specs=[in_vmem] * 4 + [ANYWHERE] * 2 + [in_vmem] * 8,
        out_shape=shapes,
        scratch_shapes=[
            *[pltpu.VMEM(array.shape, array.dtype) for array in wide],
            pltpu.VMEM((LANES, D), jnp.float32),
            pltpu.VMEM((owners, *patch_kernel.shape), LOW),
            pltpu.VMEM(qkv_shape, LOW),
            pltpu.VMEM((owners, *vectors.shape), LOW),
            pltpu.VMEM((owners, *qkv_shape), LOW),
            pltpu.VMEM((owners, *up_shape), LOW),
            pltpu.VMEM((4, *quarter_shape(*out_shape)), LOW),
            pltpu.VMEM(up_shape, LOW),
            pltpu.SemaphoreType.DMA((7,)),
            pltpu.SemaphoreType.DMA((5, GATHER_SEMS)),
        ],
        compiler_params=pltpu.CompilerParams(
            collective_id=1, has_side_effects=True, vmem_limit_bytes=VMEM_LIMIT
        ),
        cost_estimate=NO_COST,
        name="begin",
    )(
        patch_kernel,
        vectors,
        input_proj,
        output_proj,
        head_weight,
        pixels,
        segment[:, None],
        patch_size,
        position_table,
        global_vector[None, :],
    )
    output_zero, qkv_one, up_one, output_one, head_low, normed, qkv_rows = results[7:]
    return (
        results[0],
        results[1],
        results[2:4],
        results[4].reshape(owners * depth, 3 * D),
        results[5].reshape(owners * depth, up_shape[1]),
        [GatherRide(output_zero, results[6]), LevelRide(output_one)],
        [qkv_one, up_one, head_low],
        (normed, qkv_rows),
    )


REDUCE_SEMS = 52


class Reduce:
    def __init__(self, grad, out, scratch, sems):
        self.grad, self.out, self.sems = grad, out, sems
        self.own, self.away, self.got_core, self.got_group, self.part, self.got_level = scratch
        self.rows, self.columns = out.shape
        self.chunk = 16

    def load(self, level):
        _, _, core = place()
        return pltpu.make_async_copy(
            self.grad.at[2 * level + core], self.own.at[level], self.sems.at[level]
        )

    def load_away(self, level):
        _, _, core = place()
        return pltpu.make_async_copy(
            self.grad.at[2 * level + 1 - core], self.away.at[level], self.sems.at[48 + level]
        )

    def core_copy(self, target_level):
        group, level, core = place()
        return remote(
            self.away.at[target_level],
            self.got_core.at[target_level],
            self.sems.at[4 + target_level],
            self.sems.at[8 + target_level],
            (group, 2 * level + 1 - core),
        )

    def group_copy(self, turn, other):
        group, level, core = place()
        target = partner(level, turn)
        peer = partner(group, other)
        part = quarter(peer, self.rows, self.columns)
        index = 3 * turn + other - 1
        return remote(
            self.own.at[target].at[part],
            self.got_group.at[other - 1, target],
            self.sems.at[12 + index],
            self.sems.at[24 + index],
            (peer, 2 * level + core),
        )

    def level_copy(self, turn):
        group, level, core = place()
        target = partner(level, turn)
        return remote(
            self.part.at[target],
            self.got_level.at[turn - 1],
            self.sems.at[35 + turn],
            self.sems.at[38 + turn],
            (group, 2 * target + core),
        )

    def share_copy(self, other):
        group, level, core = place()
        mine = self.out.at[quarter(group, self.rows, self.columns)]
        return remote(
            mine,
            mine,
            self.sems.at[41 + other],
            self.sems.at[44 + other],
            (partner(group, other), 2 * level + core),
        )

    def first(self):
        _, level, _ = place()
        for turn in (*TURNS, 0):
            self.load_away(partner(level, turn)).start()
        for turn in (*TURNS, 0):
            self.load(partner(level, turn)).start()
        for turn in (*TURNS, 0):
            self.load_away(partner(level, turn)).wait()
            self.core_copy(partner(level, turn)).start()

    def second(self):
        _, level, _ = place()
        for turn in (*TURNS, 0):
            target = partner(level, turn)
            self.load(target).wait()
            self.core_copy(target).wait_recv()

            def add(step, carry):
                rows = pl.ds(pl.multiple_of(step * self.chunk, self.chunk), self.chunk)
                total = self.own[target, rows, :].astype(jnp.float32)
                total = total + self.got_core[target, rows, :].astype(jnp.float32)
                self.own[target, rows, :] = total.astype(self.own.dtype)
                return carry

            lax.fori_loop(0, self.rows // self.chunk, add, 0)
            for other in TURNS:
                self.group_copy(turn, other).start()

    def between(self):
        pass

    def third(self):
        group, level, _ = place()
        high, wide = quarter_shape(self.rows, self.columns)
        row_part, column_part = quarter(group, self.rows, self.columns)
        for turn in (*TURNS, 0):
            target = partner(level, turn)
            for other in TURNS:
                self.group_copy(turn, other).wait_recv()

            def add(step, carry):
                at = pl.multiple_of(step * self.chunk, self.chunk)
                rows = pl.ds(at, self.chunk)
                mine = pl.ds(pl.multiple_of(row_part.start + at, self.chunk), self.chunk)
                total = self.own[target, mine, column_part].astype(jnp.float32)
                for slot in range(3):
                    total = total + self.got_group[slot, target, rows, :].astype(jnp.float32)
                self.part[target, rows, :] = total.astype(self.part.dtype)
                return carry

            lax.fori_loop(0, high // self.chunk, add, 0)
            if turn:
                self.level_copy(turn).start()

    def fourth(self):
        group, level, _ = place()
        high, wide = quarter_shape(self.rows, self.columns)
        row_part, column_part = quarter(group, self.rows, self.columns)
        for turn in TURNS:
            self.level_copy(turn).wait_recv()

        def add(step, carry):
            at = pl.multiple_of(step * self.chunk, self.chunk)
            rows = pl.ds(at, self.chunk)
            mine = pl.ds(pl.multiple_of(row_part.start + at, self.chunk), self.chunk)
            total = self.part[level, rows, :].astype(jnp.float32)
            for slot in range(3):
                total = total + self.got_level[slot, rows, :].astype(jnp.float32)
            self.out[mine, column_part] = total.astype(self.out.dtype)
            return carry

        lax.fori_loop(0, high // self.chunk, add, 0)
        for other in TURNS:
            self.share_copy(other).start()

    def store(self):
        self.target[...] = self.out[...]

    def fifth(self):
        for other in TURNS:
            self.share_copy(other).wait_recv()

    def sixth(self):
        _, level, _ = place()
        for turn in (*TURNS, 0):
            self.core_copy(partner(level, turn)).wait_send()
            for other in TURNS:
                self.group_copy(turn, other).wait_send()
            if turn:
                self.level_copy(turn).wait_send()
                self.share_copy(turn).wait_send()


WHOLE_SEMS = 44


def add_rows(target, row, columns, source, count, wide):
    chunk = 16 if wide > 1536 else 48

    def add(step, carry):
        at = pl.multiple_of(step * chunk, chunk)
        mine = pl.ds(pl.multiple_of(row + at, 16), chunk)
        total = target[mine, columns].astype(jnp.float32)
        total = total + source[pl.ds(at, chunk), :].astype(jnp.float32)
        target[mine, columns] = total.astype(target.dtype)
        return carry

    lax.fori_loop(0, count // chunk, add, 0)


class Whole:
    FIRST_X = (1, 0)

    lead = False

    def __init__(self, grad, out, scratch, sems):
        self.grad, self.out, self.sems = grad, out, sems
        self.own, self.away, self.got_core, self.got_x, self.got_y, self.got_last, self.part, self.got_level = scratch
        self.rows, self.columns = grad.shape[1:]
        self.high, self.wide = self.rows // 2, self.columns // 2

    def row_half(self, index):
        return pl.ds(pl.multiple_of(lax.div(index, 2) * self.high, self.high), self.high)

    def column_half(self, index):
        return pl.ds(pl.multiple_of(lax.rem(index, 2) * self.wide, self.wide), self.wide)

    def load(self, level):
        _, _, core = place()
        return pltpu.make_async_copy(
            self.grad.at[2 * level + core], self.own.at[level], self.sems.at[level]
        )

    def load_away(self, level):
        _, _, core = place()
        return pltpu.make_async_copy(
            self.grad.at[2 * level + 1 - core], self.away.at[level], self.sems.at[40 + level]
        )

    def core_copy(self, target_level):
        group, level, core = place()
        return remote(
            self.away.at[target_level],
            self.got_core.at[target_level],
            self.sems.at[4 + target_level],
            self.sems.at[8 + target_level],
            (group, 2 * level + 1 - core),
        )

    def step_copy(self, turn):
        group, level, core = place()
        block = self.own.at[partner(level, turn)]
        if turn in self.FIRST_X:
            peer = partner(group, 1)
            source = block.at[:, self.column_half(peer)]
            target = self.got_x.at[self.FIRST_X.index(turn)]
        else:
            peer = partner(group, 2)
            source = block.at[self.row_half(peer), :]
            target = self.got_y.at[turn - 2]
        return remote(
            source, target, self.sems.at[12 + turn], self.sems.at[16 + turn], (peer, 2 * level + core)
        )

    def last_copy(self, turn):
        group, level, core = place()
        block = self.own.at[partner(level, turn)]
        peer = partner(group, 2 if turn in self.FIRST_X else 1)
        rows = self.row_half(peer)
        columns = self.column_half(peer)
        return remote(
            block.at[rows, columns],
            self.got_last.at[turn],
            self.sems.at[20 + turn],
            self.sems.at[24 + turn],
            (peer, 2 * level + core),
        )

    def level_copy(self, turn):
        group, level, core = place()
        target = partner(level, turn)
        return remote(
            self.part.at[target],
            self.got_level.at[turn - 1],
            self.sems.at[27 + turn],
            self.sems.at[30 + turn],
            (group, 2 * target + core),
        )

    def share_copy(self, other):
        group, level, core = place()
        mine = self.out.at[self.row_half(group), self.column_half(group)]
        return remote(
            mine,
            mine,
            self.sems.at[33 + other],
            self.sems.at[36 + other],
            (partner(group, other), 2 * level + core),
        )

    def first(self):
        _, level, _ = place()
        for turn in (*TURNS, 0):
            self.load_away(partner(level, turn)).start()
        for turn in (*TURNS, 0):
            self.load(partner(level, turn)).start()
        for turn in (*TURNS, 0):
            self.load_away(partner(level, turn)).wait()
            self.core_copy(partner(level, turn)).start()

    def second(self):
        _, level, _ = place()
        for turn in (*TURNS, 0):
            target = partner(level, turn)
            self.load(target).wait()
            self.core_copy(target).wait_recv()
            add_rows(
                self.own.at[target], 0, slice(None), self.got_core.at[target], self.rows, self.columns
            )
            self.step_copy(turn).start()

    def between(self):
        group, level, _ = place()
        for turn in (*TURNS, 0):
            block = self.own.at[partner(level, turn)]
            self.step_copy(turn).wait_recv()
            if turn in self.FIRST_X:
                source = self.got_x.at[self.FIRST_X.index(turn)]
                add_rows(block, 0, self.column_half(group), source, self.rows, self.wide)
            else:
                source = self.got_y.at[turn - 2]
                start = lax.div(group, 2) * self.high
                add_rows(block, start, slice(None), source, self.high, self.columns)
            self.last_copy(turn).start()

    def third(self):
        group, level, _ = place()
        start = lax.div(group, 2) * self.high
        columns = self.column_half(group)
        chunk = 16 if self.wide > 1536 else 48
        for turn in (*TURNS, 0):
            target = partner(level, turn)
            self.last_copy(turn).wait_recv()

            def add(step, carry):
                at = pl.multiple_of(step * chunk, chunk)
                rows = pl.ds(at, chunk)
                mine = pl.ds(pl.multiple_of(start + at, 16), chunk)
                total = self.own[target, mine, columns].astype(jnp.float32)
                total = total + self.got_last[turn, rows, :].astype(jnp.float32)
                self.part[target, rows, :] = total.astype(self.part.dtype)
                return carry

            lax.fori_loop(0, self.high // chunk, add, 0)
            if turn and not self.lead:
                self.level_copy(turn).start()

    def fourth(self):
        group, level, _ = place()
        start = lax.div(group, 2) * self.high
        columns = self.column_half(group)
        chunk = 16 if self.wide > 1536 else 48
        for turn in TURNS:
            self.level_copy(turn).wait_recv()

        def add(step, carry):
            at = pl.multiple_of(step * chunk, chunk)
            rows = pl.ds(at, chunk)
            mine = pl.ds(pl.multiple_of(start + at, 16), chunk)
            total = self.part[level, rows, :].astype(jnp.float32)
            for slot in range(3):
                total = total + self.got_level[slot, rows, :].astype(jnp.float32)
            self.out[mine, columns] = total.astype(self.out.dtype)
            return carry

        lax.fori_loop(0, self.high // chunk, add, 0)
        for other in TURNS:
            self.share_copy(other).start()

    def store(self):
        self.target[...] = self.out[...]

    def fifth(self):
        for other in TURNS:
            self.share_copy(other).wait_recv()

    def sixth(self):
        _, level, _ = place()
        for turn in (*TURNS, 0):
            self.core_copy(partner(level, turn)).wait_send()
            self.step_copy(turn).wait_send()
            self.last_copy(turn).wait_send()
            if turn and not self.lead:
                self.level_copy(turn).wait_send()
                self.share_copy(turn).wait_send()


class Lead(Whole):
    lead = True

    def store(self):
        self.target[...] = self.part[...]


class Rest(Whole):
    def __init__(self, part, out, got_level, sems):
        self.part, self.out, self.got_level, self.sems = part, out, got_level, sems
        self.rows, self.columns = out.shape
        self.high, self.wide = self.rows // 2, self.columns // 2

    def first(self):
        for turn in TURNS:
            self.level_copy(turn).start()

    def sixth(self):
        for turn in TURNS:
            self.level_copy(turn).wait_send()
            self.share_copy(turn).wait_send()


GROUP_SEMS = 13


class GroupReduce:
    def __init__(self, share, out, scratch, sems):
        self.share, self.out, self.sems = share, out, sems
        self.own, self.got = scratch
        self.rows, self.columns = out.shape
        self.chunk = 16

    def load(self):
        return pltpu.make_async_copy(self.share, self.own, self.sems.at[0])

    def group_copy(self, other):
        group, level, core = place()
        peer = partner(group, other)
        return remote(
            self.own.at[quarter(peer, self.rows, self.columns)],
            self.got.at[other - 1],
            self.sems.at[other],
            self.sems.at[3 + other],
            (peer, 2 * level + core),
        )

    def share_copy(self, other):
        group, level, core = place()
        mine = self.out.at[quarter(group, self.rows, self.columns)]
        return remote(
            mine,
            mine,
            self.sems.at[6 + other],
            self.sems.at[9 + other],
            (partner(group, other), 2 * level + core),
        )

    def first(self):
        self.load().start()

    def second(self):
        self.load().wait()
        for other in TURNS:
            self.group_copy(other).start()

    def between(self):
        pass

    def third(self):
        group, _, _ = place()
        high, wide = quarter_shape(self.rows, self.columns)
        row_part, column_part = quarter(group, self.rows, self.columns)
        for other in TURNS:
            self.group_copy(other).wait_recv()

        def add(step, carry):
            at = pl.multiple_of(step * self.chunk, self.chunk)
            rows = pl.ds(at, self.chunk)
            mine = pl.ds(pl.multiple_of(row_part.start + at, self.chunk), self.chunk)
            total = self.own[mine, column_part].astype(jnp.float32)
            for slot in range(3):
                total = total + self.got[slot, rows, :].astype(jnp.float32)
            self.out[mine, column_part] = total.astype(self.out.dtype)
            return carry

        lax.fori_loop(0, high // self.chunk, add, 0)
        for other in TURNS:
            self.share_copy(other).start()

    def fourth(self):
        pass

    def fifth(self):
        for other in TURNS:
            self.share_copy(other).wait_recv()

    def store(self):
        self.target[...] = self.out[...]

    def sixth(self):
        for other in TURNS:
            self.group_copy(other).wait_send()
            self.share_copy(other).wait_send()


class Spread:
    def __init__(self, full, sems):
        self.full, self.sems = full, sems

    def level_copy(self, turn):
        group, level, core = place()
        block = self.full.at[2 * level + core]
        peer = (group, 2 * partner(level, turn) + core)
        return remote(block, block, self.sems.at[turn - 1], self.sems.at[2 + turn], peer)

    def core_copy(self, turn):
        group, level, core = place()
        block = self.full.at[2 * partner(level, turn) + core]
        peer = (group, 2 * level + 1 - core)
        return remote(block, block, self.sems.at[6 + turn], self.sems.at[10 + turn], peer)

    def run(self):
        for turn in TURNS:
            self.level_copy(turn).start()
        self.core_copy(0).start()
        for turn in TURNS:
            self.level_copy(turn).wait_recv()
            self.core_copy(turn).start()
        for turn in (0, *TURNS):
            self.core_copy(turn).wait_recv()
        for turn in (0, *TURNS):
            self.core_copy(turn).wait_send()
            if turn:
                self.level_copy(turn).wait_send()


def squares_in(out):
    def add(step, total):
        piece = out[pl.ds(pl.multiple_of(step * 16, 16), 16), :].astype(jnp.float32)
        piece = piece * piece
        for lane in range(0, out.shape[1], LANES):
            total = total + piece[:, lane : lane + LANES]
        return total

    total = lax.fori_loop(0, out.shape[0] // 16, add, jnp.zeros((16, LANES), jnp.float32))
    return jnp.sum(total, 0, keepdims=True)


def run_stages(jobs, stages):
    for stage in stages:
        for job in jobs:
            getattr(job, stage)()


STAGES = ("first", "second", "between", "third", "fourth", "fifth", "sixth")


def whole_scratch(grad):
    _, rows, columns = grad.shape
    high, wide = quarter_shape(rows, columns)
    shapes = (*[(4, rows, columns)] * 3, (3, 4, high, wide), (4, high, wide))
    return [pltpu.VMEM(shape, grad.dtype) for shape in (*shapes, (3, high, wide))]


def stepped_scratch(grad):
    _, rows, columns = grad.shape
    high, wide = rows // 2, columns // 2
    shapes = (
        *[(4, rows, columns)] * 3,
        (2, rows, wide),
        (2, high, columns),
        (4, high, wide),
        (4, high, wide),
        (3, high, wide),
    )
    return [pltpu.VMEM(shape, grad.dtype) for shape in shapes]


def share_scratch(share):
    return [
        pltpu.VMEM(share.shape, share.dtype),
        pltpu.VMEM((3, *quarter_shape(*share.shape)), share.dtype),
    ]


def reduce_kernel(*refs, whole, partly, done, vector_rows, rest_size):
    count = whole + 1 + partly
    finished, grads, refs = refs[:done], refs[done : done + count], refs[done + count :]
    outs, full, numbers, refs = refs[:count], refs[count], refs[count + 1], refs[count + 2 :]
    sems, small_sems, group_sems, spread_sems, refs = *refs[:4], refs[4:]
    jobs = [
        Whole(grads[i], outs[i], refs[8 * i : 8 * i + 8], sems.at[i]) for i in range(whole)
    ]
    refs = refs[8 * whole :]
    small = Reduce(grads[whole], outs[whole], refs[:6], small_sems)
    refs = refs[6:]
    shares = [
        GroupReduce(
            grads[whole + 1 + i], outs[whole + 1 + i], refs[2 * i : 2 * i + 2], group_sems.at[i]
        )
        for i in range(partly)
    ]
    greet()
    run_stages([*jobs, small, *shares], STAGES[:1])
    run_stages([small, *shares], STAGES[1:2])
    run_stages(jobs, STAGES[1:3])
    run_stages([small, *shares], STAGES[3:4])
    run_stages(jobs, STAGES[3:4])
    run_stages([small, *jobs], STAGES[4:5])
    run_stages([*shares, small, *jobs], STAGES[5:6])
    total = sum(squares_in(out) for out in (*finished, *outs[:whole], *outs[whole + 1 :]))
    _, level, core = place()
    mine = 2 * level + core
    block = outs[whole]
    last = block.shape[0] - 1
    full[mine] = block[...]
    full[mine, last : last + 1, :] = total
    Spread(full, spread_sems).run()
    numbers[...] = totals(full[...], vector_rows, rest_size)
    run_stages([*shares, small, *jobs], STAGES[6:])


def transfer_outs(arrays):
    return [jax.ShapeDtypeStruct(array.shape[-2:], array.dtype) for array in arrays]


def reduce_call(grads, small, shares, finished, vector_rows, rest_size, collective_id):
    in_vmem = pl.BlockSpec(memory_space=pltpu.VMEM)
    whole, partly, done = len(grads), len(shares), len(finished)
    operands = [*grads, small, *shares]
    scratch = [
        pltpu.SemaphoreType.DMA((whole, WHOLE_SEMS)),
        pltpu.SemaphoreType.DMA((REDUCE_SEMS,)),
        pltpu.SemaphoreType.DMA((partly, GROUP_SEMS)),
        pltpu.SemaphoreType.DMA((14,)),
    ]
    for grad in grads:
        scratch.extend(stepped_scratch(grad))
    scratch.extend(whole_scratch(small))
    for share in shares:
        scratch.extend(share_scratch(share))
    out_shape = [*transfer_outs(operands), shape_of(*small.shape), shape_of(1, LANES)]
    return pl.pallas_call(
        functools.partial(
            reduce_kernel,
            whole=whole,
            partly=partly,
            done=done,
            vector_rows=vector_rows,
            rest_size=rest_size,
        ),
        in_specs=[in_vmem] * done + [ANYWHERE] * len(operands),
        out_specs=[in_vmem] * len(out_shape),
        out_shape=out_shape,
        scratch_shapes=scratch,
        compiler_params=pltpu.CompilerParams(
            collective_id=collective_id, has_side_effects=True, vmem_limit_bytes=VMEM_LIMIT
        ),
        cost_estimate=NO_COST,
        name="reduce_gradients",
    )(*finished, *operands)


def totals(full, vector_rows, rest_size):
    owners, rows, _ = full.shape
    rest_rows = -(-rest_size // (owners * LANES))
    row = lax.broadcasted_iota(jnp.int32, full.shape, 1)
    spot = row - vector_rows + rest_rows * lax.broadcasted_iota(jnp.int32, full.shape, 0)
    spot = spot * LANES + lax.broadcasted_iota(jnp.int32, full.shape, 2)
    in_rest = (row >= vector_rows) & (row < vector_rows + rest_rows)

    def summed(values):
        return jnp.sum(jnp.sum(jnp.sum(values, 0), 0, keepdims=True), 1, keepdims=True)

    tokens = summed(jnp.where(in_rest & (spot == rest_size - 1), full, 0.0))
    loss = summed(jnp.where(in_rest & (spot == rest_size - 2), full, 0.0))
    kept = (row < vector_rows) | (in_rest & (spot < rest_size - 2))
    squares = jnp.where(kept, full * full, jnp.where(row == rows - 1, full, 0.0))
    norm = jnp.sqrt(summed(squares)) / tokens
    factor = jnp.minimum(1.0, CLIP_NORM / norm) / tokens
    lane = lax.broadcasted_iota(jnp.int32, (1, LANES), 1)
    return jnp.where(
        lane == 0, factor, jnp.where(lane == 1, norm, jnp.where(lane == 2, loss, tokens))
    )


def with_kernels():
    return lax.axis_size("dp") == 4 and lax.axis_size("fsdp") == 8


def reduce_all(grads, small, shares, finished, vector_rows, rest_size, collective_id):
    if with_kernels():
        return reduce_call(grads, small, shares, finished, vector_rows, rest_size, collective_id)
    sums = [lax.psum(scatter(grad), "dp") for grad in grads]
    block = lax.psum(scatter(small), "dp")
    outs = [lax.psum(share, "dp") for share in shares]
    total = sum(jnp.sum(jnp.square(out.astype(jnp.float32))) for out in (*finished, *sums, *outs))
    row = jnp.full((1, LANES), 1.0 / LANES, jnp.float32) * total
    full = lax.all_gather(block.at[-1:].set(row), "fsdp", axis=0)
    return [*sums, block, *outs, full, totals(full, vector_rows, rest_size)]


def scatter(grad):
    return lax.psum_scatter(grad, "fsdp", scatter_dimension=0)


def by_owner(grad, low=jnp.bfloat16):
    owners = lax.axis_size("fsdp")
    return grad.astype(low).reshape(owners, grad.shape[0] // owners, grad.shape[1])


def attention_forward_kernel(
    q_ref, k_ref, v_ref, seg_col_ref, seg_row_ref, out_ref, expo_ref, inv_ref, *, block
):
    rows = q_ref.shape[0]
    lower = lax.broadcasted_iota(jnp.int32, (block, PAIR), 1) < HD
    keys = k_ref[...]
    values = jnp.concatenate([v_ref[...], jnp.ones((rows, PAIR), v_ref.dtype)], 1)
    seg_row = seg_row_ref[...]
    tasks = [(step, head) for step in range(rows // block) for head in range(2)]

    def scores_of(step, head):
        query = q_ref[step * block : (step + 1) * block, :] * jnp.bfloat16(HD**-0.5)
        keep = lower if head == 0 else jnp.logical_not(lower)
        return mul_nt(jnp.where(keep, query, jnp.bfloat16(0)), keys)

    scores = scores_of(*tasks[0])
    outs = []
    for index, (step, head) in enumerate(tasks):
        following = scores_of(*tasks[index + 1]) if index + 1 < len(tasks) else None
        at = slice(step * block, (step + 1) * block)
        scores = jnp.where(seg_col_ref[at, :] == seg_row, scores, MASKED)
        highest = jnp.max(scores, -1, keepdims=True)
        low = jnp.exp(scores - highest).astype(jnp.bfloat16)
        expo_ref[head, at, :] = low
        outs.append(mul(low, values))
        if head:
            inverse = 1.0 / jnp.where(lower, outs[0][:, PAIR:], outs[1][:, PAIR:])
            sums = jnp.where(lower, outs[0][:, :PAIR], outs[1][:, :PAIR])
            out_ref[at, :] = (sums * inverse).astype(jnp.bfloat16)
            inv_ref[at, :] = inverse
            outs = []
        scores = following


def attention_forward(qkv_rows, segment, rides, collective_id):
    rows = qkv_rows.shape[0]
    pairs = HEADS // 2
    wide = lambda base: pl.BlockSpec((rows, PAIR), lambda j, base=base: (0, base + j))
    return block_call(
        functools.partial(attention_forward_kernel, block=min(256, rows)),
        pairs,
        [wide(0), wide(pairs), wide(2 * pairs), fixed(rows, 1), fixed(1, rows)],
        [qkv_rows, qkv_rows, qkv_rows, segment[:, None], segment[None, :]],
        [wide(0), pl.BlockSpec((2, rows, rows), lambda j: (j, 0, 0)), wide(0)],
        [
            shape_of(rows, D, dtype=LOW),
            shape_of(HEADS, rows, rows, dtype=LOW),
            shape_of(rows, D),
        ],
        [],
        "attention_forward",
        work(16 * HEADS * rows * rows * HD, 2 * HEADS * rows * rows + 12 * rows * D),
        rides,
        collective_id,
    )


def attention_backward_kernel(
    q_ref, k_ref, v_ref, expo_ref, inv_ref, out_ref, grad_ref, dqkv_ref, *, block
):
    rows = q_ref.shape[0]
    pair = pl.program_id(0)
    lower = lax.broadcasted_iota(jnp.int32, (block, PAIR), 1) < HD
    keys = k_ref[...]
    values = v_ref[...]
    scale = HD**-0.5
    scaled_grad = (grad_ref[...].astype(jnp.float32) * inv_ref[...]).astype(jnp.bfloat16)
    query = q_ref[...]
    query_t = query.T
    grad_t = scaled_grad.T
    product = scaled_grad.astype(jnp.float32) * out_ref[...].astype(jnp.float32)
    key_t = [None, None]
    value_t = [None, None]
    tasks = [(step, head) for step in range(rows // block) for head in range(2)]

    def probs_grad_of(step, head):
        keep = lower if head == 0 else jnp.logical_not(lower)
        mine = scaled_grad[step * block : (step + 1) * block]
        return mul_nt(jnp.where(keep, mine, jnp.bfloat16(0)), values)

    probs_grad = probs_grad_of(*tasks[0])
    query_parts = []
    for index, (step, head) in enumerate(tasks):
        following = probs_grad_of(*tasks[index + 1]) if index + 1 < len(tasks) else None
        at = slice(step * block, (step + 1) * block)
        lanes = slice(head * HD, (head + 1) * HD)
        keep = lower if head == 0 else jnp.logical_not(lower)
        inner = jnp.sum(jnp.where(keep, product[at], 0.0), -1, keepdims=True)
        low = expo_ref[head, at, :]
        value_part = mul(grad_t[lanes, at], low)
        scores_grad = (low.astype(jnp.float32) * (probs_grad - inner)).astype(jnp.bfloat16)
        query_parts.append(mul(scores_grad, keys))
        key_part = mul(query_t[lanes, at], scores_grad)
        key_t[head] = key_part if step == 0 else key_t[head] + key_part
        value_t[head] = value_part if step == 0 else value_t[head] + value_part
        if head:
            query_grad = jnp.where(lower, query_parts[0], query_parts[1]) * scale
            dqkv_ref[at, pl.ds(pl.multiple_of(pair * PAIR, PAIR), PAIR)] = query_grad.astype(
                jnp.bfloat16
            )
            query_parts = []
        probs_grad = following
    key_grad = (jnp.concatenate(key_t, 0) * scale).T
    value_grad = jnp.concatenate(value_t, 0).T
    dqkv_ref[:, pl.ds(pl.multiple_of(D + pair * PAIR, PAIR), PAIR)] = key_grad.astype(jnp.bfloat16)
    dqkv_ref[:, pl.ds(pl.multiple_of(2 * D + pair * PAIR, PAIR), PAIR)] = value_grad.astype(jnp.bfloat16)


def attention_backward(qkv_rows, expo, inverse, attended, attended_grad, rides, collective_id):
    rows = qkv_rows.shape[0]
    pairs = HEADS // 2
    wide = lambda base: pl.BlockSpec((rows, PAIR), lambda j, base=base: (0, base + j))
    return block_call(
        functools.partial(attention_backward_kernel, block=min(256, rows)),
        pairs,
        [
            wide(0),
            wide(pairs),
            wide(2 * pairs),
            pl.BlockSpec((2, rows, rows), lambda j: (j, 0, 0)),
            wide(0),
            wide(0),
            wide(0),
        ],
        [qkv_rows, qkv_rows, qkv_rows, expo, inverse, attended, attended_grad],
        [fixed(rows, 3 * D)],
        [shape_of(rows, 3 * D, dtype=LOW)],
        [],
        "attention_backward",
        None,
        rides,
        collective_id,
    )


def mul(left, right):
    return jnp.dot(left, right, preferred_element_type=jnp.float32)


def mul_nt(left, right):
    return lax.dot_general(left, right, NT, preferred_element_type=jnp.float32)


def normalized(values):
    center = values - jnp.mean(values, -1, keepdims=True)
    inverse = lax.rsqrt(jnp.mean(center * center, -1, keepdims=True) + NORM_EPS)
    return center * inverse, inverse


def norm_backward(grad, values, gain):
    unit, inverse = normalized(values)
    inner = grad * gain
    mean_inner = jnp.mean(inner, -1, keepdims=True)
    mean_cross = jnp.mean(inner * unit, -1, keepdims=True)
    value_grad = inverse * (inner - mean_inner - unit * mean_cross)
    return value_grad, column_sum(grad * unit), column_sum(grad)


def column_sum(rows):
    return jnp.sum(rows.astype(jnp.float32), 0, keepdims=True)


def at_first(action):
    pl.when(pl.program_id(0) == 0)(action)


def rows_of(block, columns):
    return pl.BlockSpec((block, columns), lambda i: (i, 0))


def fixed(*shape):
    return pl.BlockSpec(shape, lambda i: (0,) * len(shape), pipeline_mode=pl.Buffered(1))


def loads(sources, targets, sems):
    return [
        pltpu.make_async_copy(source, target, sems.at[index])
        for index, (source, target) in enumerate(zip(sources, targets))
    ]


def shape_of(*shape, dtype=jnp.float32):
    return jax.ShapeDtypeStruct(shape, dtype)


def embed_kernel(pixel_ref, weight_ref, pos_ref, table_ref, bias_ref, out_ref):
    position = jnp.dot(
        pos_ref[...], table_ref[...], precision=HIGHEST, preferred_element_type=jnp.float32
    )
    out_ref[...] = mul(pixel_ref[...], weight_ref[...]) + bias_ref[...] + position


def embed(pixels, weight, pos_weights, table, bias):
    rows, depth = pixels.shape
    block = 256
    nodes = pos_weights.shape[1]
    return block_call(
        embed_kernel,
        rows // block,
        [rows_of(block, depth), fixed(depth, D), rows_of(block, nodes), fixed(nodes, D), fixed(1, D)],
        [pixels, weight, pos_weights, table, bias],
        [rows_of(block, D)],
        [shape_of(rows, D)],
        [],
        "embed",
        work(2 * rows * depth * D, 2 * rows * depth + 2 * depth * D + 4 * rows * D),
    )[0]


def chunk_at(base):
    return pl.ds(pl.multiple_of(base + pl.program_id(0) * D, LANES), D)


def columns_of(rows):
    return pl.BlockSpec((rows, D), lambda i: (0, i))


def halves_of(rows):
    half = rows // 2
    return [slice(start, start + half) for start in range(0, rows, half)]


def at_last(action):
    pl.when(pl.program_id(0) == pl.num_programs(0) - 1)(action)


def qkv_kernel(stream_ref, weight_ref, vector_ref, normed_out, qkv_ref, normed_ref, sem):
    copy = pltpu.make_async_copy(normed_ref, normed_out, sem)

    @at_first
    def _():
        unit, _ = normalized(stream_ref[...])
        normed_ref[...] = (unit * vector_ref[:, :D] + vector_ref[:, D : 2 * D]).astype(LOW)
        copy.start()

    bias = vector_ref[:, chunk_at(4 * D)]
    for half in halves_of(stream_ref.shape[0]):
        qkv_ref[half, :] = (mul(normed_ref[half, :], weight_ref[...]) + bias).astype(LOW)
    at_last(copy.wait)


def qkv_forward(stream, weight, vector):
    rows = stream.shape[0]
    return block_call(
        qkv_kernel,
        3,
        [fixed(rows, D), columns_of(D), fixed(1, vector.shape[1])],
        [stream, weight, vector],
        [ANYWHERE, columns_of(rows)],
        [shape_of(rows, D, dtype=LOW), shape_of(rows, 3 * D, dtype=LOW)],
        [pltpu.VMEM((rows, D), LOW), pltpu.SemaphoreType.DMA],
        "qkv_forward",
        work(6 * rows * D * D, 14 * rows * D + 6 * D * D),
    )


def mlp_kernel(
    stream_ref, attended_ref, mix_ref, up_ref, down_ref, vector_ref,
    residual_out, normed_out, active_ref, slope_ref, out_ref,
    residual_ref, normed_ref, sems,
):
    rows = stream_ref.shape[0]
    copies = loads((residual_ref, normed_ref), (residual_out, normed_out), sems)

    @at_first
    def _():
        for half in halves_of(rows):
            residual = stream_ref[half, :] + mul(attended_ref[half, :], mix_ref[...])
            residual = residual + vector_ref[:, 7 * D : 8 * D]
            residual_ref[half, :] = residual
            unit, _ = normalized(residual)
            normed = unit * vector_ref[:, 2 * D : 3 * D] + vector_ref[:, 3 * D : 4 * D]
            normed_ref[half, :] = normed.astype(LOW)
            out_ref[half, :] = residual + vector_ref[:, 8 * D : 9 * D]
        for copy in copies:
            copy.start()

    bias = vector_ref[:, chunk_at(9 * D)]
    parts = halves_of(rows)
    hidden = mul(normed_ref[parts[0], :], up_ref[...]) + bias
    for index, half in enumerate(parts):
        following = None
        if index + 1 < len(parts):
            following = mul(normed_ref[parts[index + 1], :], up_ref[...]) + bias
        square = hidden * hidden
        rise = 0.5 + 0.5 * jnp.tanh(hidden * (ROOT + (ROOT * CUBE) * square))
        active = hidden * rise
        active_low = active.astype(LOW)
        active_ref[half, :] = active_low
        bend = (2.0 * ROOT) + (6.0 * ROOT * CUBE) * square
        slope_ref[half, :] = (rise + active * (1.0 - rise) * bend).astype(LOW)
        out_ref[half, :] += mul(active_low, down_ref[...])
        hidden = following

    @at_last
    def _():
        for copy in copies:
            copy.wait()


def mlp_specs(up, proj_out):
    return (
        [fixed(D, D), columns_of(D), pl.BlockSpec((D, D), lambda i: (i + 1, 0))],
        [proj_out, up, proj_out],
    )


def mlp_forward(stream, attended, up, proj_out, vector):
    rows = stream.shape[0]
    width = up.shape[1]
    weight_specs, weights = mlp_specs(up, proj_out)
    return block_call(
        mlp_kernel,
        width // D,
        [fixed(rows, D), fixed(rows, D), *weight_specs, fixed(1, vector.shape[1])],
        [stream, attended, *weights, vector],
        [ANYWHERE, ANYWHERE, columns_of(rows), columns_of(rows), fixed(rows, D)],
        [
            shape_of(rows, D),
            shape_of(rows, D, dtype=LOW),
            shape_of(rows, width, dtype=LOW),
            shape_of(rows, width, dtype=LOW),
            shape_of(rows, D),
        ],
        [
            pltpu.VMEM((rows, D), jnp.float32),
            pltpu.VMEM((rows, D), LOW),
            pltpu.SemaphoreType.DMA((2,)),
        ],
        "mlp_forward",
        work(2 * rows * D * (D + 2 * width), rows * (16 * D + 4 * width) + 2 * D * (D + 2 * width)),
    )


def mlp_back_kernel(
    grad_ref, slope_ref, residual_in, normed_ref, active_ref, attended_ref, mix_ref, up_ref, down_ref, vector_ref,
    out_ref, attended_grad_ref, sums_ref, output_grad, *refs,
):
    up_grads, scratch = refs[:-7], refs[-7:]
    residual_ref, low_ref, second_ref, turned_ref, hidden_ref, product_ref, sems = scratch
    rows = grad_ref.shape[0]
    step = pl.program_id(0)
    load = pltpu.make_async_copy(residual_in, residual_ref, sems.at[0])

    def store_copy(slot):
        rows_at = pl.ds(pl.multiple_of(slot * D, D), D)
        return pltpu.make_async_copy(
            product_ref.at[slot], output_grad.at[rows_at], sems.at[1 + slot]
        )

    def store(slot, product):
        product_ref[slot] = product.astype(LOW)
        store_copy(slot).start()

    @at_first
    def _():
        load.start()
        low_ref[...] = grad_ref[...].astype(LOW)
        turned_ref[...] = normed_ref[...].T
        second_ref[...] = jnp.zeros_like(second_ref)

    parts = halves_of(rows)
    active_grad = mul_nt(low_ref[parts[0], :], down_ref[...])
    hidden_sum = 0.0
    for index, half in enumerate(parts):
        following = None
        if index + 1 < len(parts):
            following = mul_nt(low_ref[parts[index + 1], :], down_ref[...])
        hidden_grad = (active_grad * slope_ref[half, :].astype(jnp.float32)).astype(LOW)
        hidden_ref[half, :] = hidden_grad
        hidden_sum = hidden_sum + column_sum(hidden_grad)
        second_ref[half, :] += mul_nt(hidden_grad, up_ref[...])
        active_grad = following
    sums_ref[:, chunk_at(4 * D)] = hidden_sum
    store(step + 1, mul(active_ref[...].T, low_ref[...]))
    up_grad = mul(turned_ref[...], hidden_ref[...]).astype(LOW)
    share = pl.num_programs(0) // len(up_grads)
    for index, part in enumerate(up_grads):

        @pl.when(lax.div(step, share) == index)
        def _(part=part):
            part[...] = up_grad

    @at_last
    def _():
        load.wait()
        gain = vector_ref[:, 2 * D : 3 * D]
        totals = [0.0] * 4
        for half in halves_of(rows):
            grad = grad_ref[half, :]
            value_grad, gain_grad, shift_grad = norm_backward(
                second_ref[half, :], residual_ref[half, :], gain
            )
            total = value_grad + grad
            out_ref[half, :] = total
            total_low = total.astype(LOW)
            hidden_ref[half, :] = total_low
            attended_grad_ref[half, :] = mul_nt(total_low, mix_ref[...]).astype(LOW)
            new = (gain_grad, shift_grad, column_sum(total_low), column_sum(low_ref[half, :]))
            totals = [old + part for old, part in zip(totals, new)]
        sums_ref[:, : 4 * D] = jnp.concatenate(totals, 1)
        store(0, mul(attended_ref[...].T, hidden_ref[...]))
        for slot in range(product_ref.shape[0]):
            store_copy(slot).wait()


def mlp_backward(
    grad, slope, residual, normed, active, attended, up, proj_out, vector, parts, rides, collective_id
):
    rows = grad.shape[0]
    width = up.shape[1]
    steps = width // D
    share = steps // parts
    part_of = lambda index: lambda i: (0, jnp.clip(i - index * share, 0, share - 1))
    whole = fixed(rows, D)
    weight_specs, weights = mlp_specs(up, proj_out)
    return block_call(
        mlp_back_kernel,
        steps,
        [
            whole,
            columns_of(rows),
            ANYWHERE,
            whole,
            columns_of(rows),
            whole,
            *weight_specs,
            fixed(1, vector.shape[1]),
        ],
        [grad, slope, residual, normed, active, attended, *weights, vector],
        [whole, whole, fixed(1, 4 * D + width), ANYWHERE, *[pl.BlockSpec((D, D), part_of(index)) for index in range(parts)]],
        [
            shape_of(rows, D),
            shape_of(rows, D, dtype=LOW),
            shape_of(1, 4 * D + width),
            shape_of(D + width, D, dtype=LOW),
            *[shape_of(D, width // parts, dtype=LOW)] * parts,
        ],
        [
            pltpu.VMEM((rows, D), jnp.float32),
            pltpu.VMEM((rows, D), LOW),
            pltpu.VMEM((rows, D), jnp.float32),
            pltpu.VMEM((D, rows), LOW),
            pltpu.VMEM((rows, D), LOW),
            pltpu.VMEM((steps + 1, D, D), LOW),
            pltpu.SemaphoreType.DMA((steps + 2,)),
        ],
        "mlp_backward",
        None,
        rides,
        collective_id,
    )


def qkv_back_kernel(
    grad_ref, residual_in, stream_in, normed_ref, weight_ref, vector_ref,
    out_ref, sums_ref, weight_grad_ref,
    residual_ref, stream_ref, sum_ref, turned_ref, sems,
):
    rows = out_ref.shape[0]
    copies = loads((residual_in, stream_in), (residual_ref, stream_ref), sems)

    @at_first
    def _():
        for copy in copies:
            copy.start()
        turned_ref[...] = normed_ref[...].T
        sum_ref[...] = jnp.zeros_like(sum_ref)

    for half in halves_of(rows):
        sum_ref[half, :] += mul_nt(grad_ref[half, :], weight_ref[...])
    sums_ref[:, chunk_at(2 * D)] = column_sum(grad_ref[...])
    weight_grad_ref[...] = mul(turned_ref[...], grad_ref[...]).astype(LOW)

    @at_last
    def _():
        for copy in copies:
            copy.wait()
        totals = [0.0] * 2
        for half in halves_of(rows):
            value_grad, gain_grad, shift_grad = norm_backward(
                sum_ref[half, :], stream_ref[half, :], vector_ref[:, :D]
            )
            out_ref[half, :] = residual_ref[half, :] + value_grad
            totals = [totals[0] + gain_grad, totals[1] + shift_grad]
        sums_ref[:, : 2 * D] = jnp.concatenate(totals, 1)


def qkv_backward(grad, residual_grad, stream, normed, weight, vector, rides, collective_id):
    rows = stream.shape[0]
    whole = fixed(rows, D)
    return block_call(
        qkv_back_kernel,
        3,
        [columns_of(rows), ANYWHERE, ANYWHERE, whole, columns_of(D), fixed(1, vector.shape[1])],
        [grad, residual_grad, stream, normed, weight, vector],
        [whole, fixed(1, 5 * D), columns_of(D)],
        [shape_of(rows, D), shape_of(1, 5 * D), shape_of(D, 3 * D, dtype=LOW)],
        [
            pltpu.VMEM((rows, D), jnp.float32),
            pltpu.VMEM((rows, D), jnp.float32),
            pltpu.VMEM((rows, D), jnp.float32),
            pltpu.VMEM((D, rows), LOW),
            pltpu.SemaphoreType.DMA((2,)),
        ],
        "qkv_backward",
        None,
        rides,
        collective_id,
    )


def embed_back_kernel(pixel_ref, grad_ref, pos_ref, out_ref, table_ref, bias_ref, low_ref):
    @at_first
    def _():
        grad = grad_ref[...]
        low = grad.astype(jnp.bfloat16)
        low_ref[...] = low
        bias_ref[...] = column_sum(low)
        table_ref[...] = jnp.dot(
            pos_ref[...], grad, precision=HIGHEST, preferred_element_type=jnp.float32
        )

    out_ref[...] = mul(pixel_ref[...].T, low_ref[...]).astype(jnp.bfloat16)


def embed_backward(pixels, grad, pos_weights_t):
    rows, depth = pixels.shape
    block = 768
    nodes = pos_weights_t.shape[0]
    return block_call(
        embed_back_kernel,
        depth // block,
        [pl.BlockSpec((rows, block), lambda i: (0, i)), fixed(rows, D), fixed(nodes, rows)],
        [pixels, grad, pos_weights_t],
        [rows_of(block, D), fixed(nodes, D), fixed(1, D)],
        [shape_of(depth, D, dtype=jnp.bfloat16), shape_of(nodes, D), shape_of(1, D)],
        [pltpu.VMEM((rows, D), jnp.bfloat16)],
        "embed_backward",
        None,
    )


def head_kernel(
    stream_ref, seg_col_ref, seg_row_ref, label_ref, weight_ref, vector_ref,
    grad_ref, weight_grad_ref, sums_ref, bias_grad_ref, numbers_ref, *, classes,
):
    padded = weight_ref.shape[1]
    vector = vector_ref[...].astype(LOW).astype(jnp.float32)
    gain, shift = vector[:, D : 2 * D], vector[:, 2 * D : 3 * D]
    slots = lax.broadcasted_iota(jnp.int32, (IMGS, 1), 0)
    member = (seg_row_ref[...] == slots).astype(jnp.float32)
    counts = jnp.sum(member, 1, keepdims=True)
    sizes = jnp.maximum(counts, 1.0)
    unit, inverse = normalized(stream_ref[...])
    final = unit * gain + shift
    owner = jnp.broadcast_to(seg_col_ref[...], final.shape)
    pooled = [jnp.sum(jnp.where(owner == k, final, 0.0), 0, keepdims=True) for k in range(IMGS)]
    pooled = (jnp.concatenate(pooled, 0) / sizes).astype(LOW)
    class_at = lax.broadcasted_iota(jnp.int32, (IMGS, padded), 1)
    logits = mul(pooled, weight_ref[...]) + vector[:, 3 * D :]
    logits = jnp.where(class_at < classes, logits, MASKED)
    highest = jnp.max(logits, -1, keepdims=True)
    exponent = jnp.exp(logits - highest)
    totals = jnp.sum(exponent, -1, keepdims=True)
    onehot = class_at == label_ref[...]
    picked = jnp.sum(jnp.where(onehot, logits, 0.0), 1, keepdims=True)
    loss = jnp.sum(counts * (highest + jnp.log(totals) - picked), 0, keepdims=True)
    numbers_ref[...] = jnp.concatenate([loss, jnp.sum(counts, 0, keepdims=True)], 1)
    logits_grad = ((exponent / totals - onehot.astype(jnp.float32)) * counts).astype(LOW)
    bias_grad_ref[...] = column_sum(logits_grad)
    weight_grad_ref[...] = lax.dot_general(
        pooled, logits_grad, (((0,), (0,)), ((), ())), preferred_element_type=jnp.float32
    ).astype(LOW)
    pooled_grad = mul_nt(logits_grad, weight_ref[...]) / sizes
    own = (seg_col_ref[...] == lax.broadcasted_iota(jnp.int32, (1, IMGS), 1)).astype(LOW)
    final_grad, left = 0.0, pooled_grad
    for _ in range(3):
        term = left.astype(LOW)
        final_grad = final_grad + mul(own, term)
        left = left - term.astype(jnp.float32)
    inner = final_grad * gain
    mean_inner = jnp.mean(inner, -1, keepdims=True)
    mean_cross = jnp.mean(inner * unit, -1, keepdims=True)
    grad_ref[...] = inverse * (inner - mean_inner - unit * mean_cross)
    sums_ref[...] = jnp.concatenate([column_sum(final_grad * unit), column_sum(final_grad)], 1)


def head(stream, segment, labels, weight, global_vector, classes):
    rows = stream.shape[0]
    padded = weight.shape[1]
    vector = jnp.pad(global_vector, (0, padded - classes))[None, :]
    return pl.pallas_call(
        functools.partial(head_kernel, classes=classes),
        out_shape=[
            shape_of(rows, D),
            shape_of(D, padded, dtype=LOW),
            shape_of(1, 2 * D),
            shape_of(1, padded),
            shape_of(1, 2),
        ],
        compiler_params=pltpu.CompilerParams(vmem_limit_bytes=VMEM_LIMIT),
        cost_estimate=NO_COST,
        name="head",
    )(stream, segment[:, None], segment[None, :], labels.reshape(IMGS, 1), weight, vector)


def adam_update(gradient, moment, square, weight, factor, learn_rate):
    clipped = gradient * factor
    moment = BETA_ONE * moment + (1.0 - BETA_ONE) * clipped
    square = BETA_TWO * square + (1.0 - BETA_TWO) * clipped * clipped
    fixed_one = 1.0 - BETA_ONE**STEP
    fixed_two = 1.0 - BETA_TWO**STEP
    step_dir = (
        moment / fixed_one / (jnp.sqrt(square / fixed_two) + ADAM_EPS) + WEIGHT_DECAY * weight
    )
    return (moment, square, weight - learn_rate * step_dir)


def body(
    pixels,
    segment,
    patch_size,
    labels,
    patch_kernel,
    head_weight,
    input_proj,
    output_proj,
    layer_vector,
    position_table,
    global_vector,
    patch_moment,
    head_moment,
    input_moment,
    output_moment,
    layer_moment,
    position_moment,
    global_moment,
    patch_square,
    head_square,
    input_square,
    output_square,
    layer_square,
    position_square,
    global_square,
):
    owners = lax.axis_size("fsdp")
    nodes = position_table.shape[0]
    vector_size = layer_vector.size
    stream, pos_weights_t, vectors, qkv_weight, up_zero, rides, rest_shards, first_rows = begin(
        pixels,
        segment,
        patch_size,
        patch_kernel,
        layer_vector,
        input_proj,
        output_proj,
        head_weight,
        position_table,
        global_vector,
    )
    qkv_one, up_one, head_full = (
        lax.all_gather(shard, "fsdp", axis=0, tiled=True) for shard in rest_shards
    )
    saved_layers = []
    for index in range(LAYERS):
        vector = vectors[index]
        if index:
            normed, qkv_rows = qkv_forward(stream, qkv_weight, vector)
        else:
            normed, qkv_rows = first_rows
        if index == 0:
            attended, expo, inverse, output, output_ride = attention_forward(
                qkv_rows, segment, rides, 4
            )
            up = up_zero
        else:
            attended, expo, inverse, output = attention_forward(qkv_rows, segment, [output_ride], 5)
            up = up_one
        residual, normed_second, active, slope, following = mlp_forward(
            stream, attended, up, output, vector
        )
        saved_layers.append(
            (
                (qkv_weight, up, output, vector),
                (stream, normed, qkv_rows, attended, expo, inverse),
                (residual, normed_second, active, slope),
            )
        )
        stream, qkv_weight = following, qkv_one
    stream_grad, head_grad, final_sums, head_bias_grad, numbers = head(
        stream, segment, labels, head_full, global_vector, head_weight.shape[1]
    )
    vector_grads = [None] * LAYERS
    for index in reversed(range(LAYERS)):
        (qkv_weight, up, output, vector), first, second = saved_layers[index]
        entering, normed, qkv_rows, attended, expo, inverse = first
        residual, normed_second, active, slope = second
        residual_grad, attended_grad, mlp_sums, output_grad, *brought = mlp_backward(
            stream_grad,
            slope,
            residual,
            normed_second,
            active,
            attended,
            up,
            output,
            vector,
            2 if index else 1,
            () if index else [output_rest, SumRide(by_owner(head_grad), False)],
            9,
        )
        if index:
            attended_grad, *up_parts = lax.optimization_barrier((attended_grad, *brought))
            one_parts = [scatter(by_owner(part)) for part in up_parts]
        else:
            up_grad, output_one_sum, head_sum = brought
            attended_grad, output_grad = lax.optimization_barrier((attended_grad, output_grad))
            output_zero_part = scatter(by_owner(output_grad))
        qkv_grad, rest = attention_backward(
            qkv_rows,
            expo,
            inverse,
            attended,
            attended_grad,
            [LeadRide(by_owner(output_grad if index else up_grad))],
            6 if index else 8,
        )
        stream_grad, qkv_sums, qkv_weight_grad, *brought = qkv_backward(
            qkv_grad,
            residual_grad,
            entering,
            normed,
            qkv_weight,
            vector,
            () if index else [rest, *[ShareRide(part) for part in one_parts]],
            7,
        )
        if index:
            output_rest = rest
            stream_grad, qkv_weight_grad = lax.optimization_barrier((stream_grad, qkv_weight_grad))
            one_parts.append(scatter(by_owner(qkv_weight_grad)))
        else:
            up_zero_sum, *up_one_sums, qkv_one_sum = brought
        vector_grads[index] = jnp.concatenate(
            [
                qkv_sums[0, : 2 * D],
                mlp_sums[0, : 2 * D],
                qkv_sums[0, 2 * D :],
                mlp_sums[0, 2 * D :],
            ]
        )
    kernel_grad, position_grad, bias_grad = embed_backward(pixels, stream_grad, pos_weights_t)
    position_grad = position_grad[:nodes]
    vector_part = jnp.stack(vector_grads).reshape(LAYERS, owners, -1)
    vector_part = jnp.swapaxes(vector_part, 0, 1).reshape(owners, vector_size)
    vector_rows = -(-vector_size // LANES)
    vector_part = jnp.pad(vector_part, ((0, 0), (0, vector_rows * LANES - vector_size)))
    rest = jnp.concatenate(
        [
            position_grad.reshape(-1),
            bias_grad[0],
            final_sums[0],
            head_bias_grad[0, :CLS],
            numbers[0],
        ]
    )
    rest_rows = -(-rest.shape[0] // (owners * LANES))
    rest_part = jnp.pad(rest, (0, rest_rows * owners * LANES - rest.shape[0]))
    small = jnp.concatenate([vector_part, rest_part.reshape(owners, -1)], 1)
    used = vector_rows + rest_rows
    block_rows = (used // 64 + 1) * 64
    small = jnp.pad(small.reshape(owners, used, LANES), ((0, 0), (0, block_rows - used), (0, 0)))
    (
        qkv_zero_sum,
        kernel_sum,
        small_share,
        output_zero_sum,
        small_full,
        numbers,
    ) = reduce_all(
        [by_owner(qkv_weight_grad), by_owner(kernel_grad)],
        small,
        [output_zero_part],
        [head_sum, output_one_sum, up_zero_sum, *up_one_sums, qkv_one_sum],
        vector_rows,
        rest.shape[0],
        2,
    )
    factor, grad_norm, loss_sum, token_total = (numbers[0, index] for index in range(4))
    rest_sum = small_full[:, vector_rows:used].reshape(-1)
    position_sum = rest_sum[: position_grad.size].reshape(position_grad.shape)
    global_sum = rest_sum[position_grad.size :][: global_vector.shape[0]]
    kernel_sum = kernel_sum.astype(jnp.float32)
    head_sum = head_sum[:, :CLS].astype(jnp.float32)
    input_sum = jnp.stack(
        [
            jnp.concatenate(parts, 1)
            for parts in ((qkv_zero_sum, up_zero_sum), (qkv_one_sum, *up_one_sums))
        ]
    ).astype(jnp.float32)
    output_sum = jnp.stack([output_zero_sum, output_one_sum]).astype(
        jnp.float32
    )
    vector_sum = small_share[:vector_rows].reshape(-1)[:vector_size].reshape(layer_vector.shape)
    patch_next = adam_update(
        kernel_sum, patch_moment, patch_square, patch_kernel, factor, LEARN_RATE
    )
    head_next = adam_update(head_sum, head_moment, head_square, head_weight, factor, LEARN_RATE)
    input_next = adam_update(input_sum, input_moment, input_square, input_proj, factor, LEARN_RATE)
    output_next = adam_update(
        output_sum, output_moment, output_square, output_proj, factor, LEARN_RATE
    )
    layer_next = adam_update(
        vector_sum, layer_moment, layer_square, layer_vector, factor, VECTOR_RATE
    )
    position_next = adam_update(
        position_sum, position_moment, position_square, position_table, factor, LEARN_RATE
    )
    global_next = adam_update(
        global_sum, global_moment, global_square, global_vector, factor, VECTOR_RATE
    )
    return (
        loss_sum,
        token_total,
        grad_norm,
        patch_next[0],
        head_next[0],
        input_next[0],
        output_next[0],
        layer_next[0],
        position_next[0],
        global_next[0],
        patch_next[1],
        head_next[1],
        input_next[1],
        output_next[1],
        layer_next[1],
        position_next[1],
        global_next[1],
        patch_next[2],
        head_next[2],
        input_next[2],
        output_next[2],
        layer_next[2],
        position_next[2],
        global_next[2],
    )


def solution(mesh):
    in_specs = (
        P(("dp", "fsdp"), None),
        P(("dp", "fsdp")),
        P(("dp", "fsdp"), None),
        P(("dp", "fsdp"), None),
        P("fsdp", None),
        P("fsdp", None),
        P(None, "fsdp", None),
        P(None, "fsdp", None),
        P(None, "fsdp"),
        P(),
        P(),
        P("fsdp", None),
        P("fsdp", None),
        P(None, "fsdp", None),
        P(None, "fsdp", None),
        P(None, "fsdp"),
        P(),
        P(),
        P("fsdp", None),
        P("fsdp", None),
        P(None, "fsdp", None),
        P(None, "fsdp", None),
        P(None, "fsdp"),
        P(),
        P(),
    )
    out_specs = (
        P(),
        P(),
        P(),
        P("fsdp", None),
        P("fsdp", None),
        P(None, "fsdp", None),
        P(None, "fsdp", None),
        P(None, "fsdp"),
        P(),
        P(),
        P("fsdp", None),
        P("fsdp", None),
        P(None, "fsdp", None),
        P(None, "fsdp", None),
        P(None, "fsdp"),
        P(),
        P(),
        P("fsdp", None),
        P("fsdp", None),
        P(None, "fsdp", None),
        P(None, "fsdp", None),
        P(None, "fsdp"),
        P(),
        P(),
    )
    return jax.shard_map(body, mesh=mesh, in_specs=in_specs, out_specs=out_specs, check_vma=False)
```
